32 devices in a mesh: dp: 2 (over x), fsdp: 16 (over z, y, core).
Axes of the slice: x: 2, y: 2, z: 4, core: 2. Of those that a mesh axis runs over, the one named last changes fastest.
Arguments:
- input_token_index: int32 [32, 1024], P(('dp', 'fsdp')), may hold values from 0 to 51199
- sentence_numbers: int32 [32, 1024], P(('dp', 'fsdp')), may hold values from 0 to 15, never falling along the last dimension, each value on 1 to 128 neighbouring positions
- label_positions: int32 [32, 128], P(('dp', 'fsdp')), may hold values from 0 to 1023
- label_target_token: int32 [32, 128], P(('dp', 'fsdp')), may hold values from 0 to 51199
- sequence_task_index: int32 [32], P(('dp', 'fsdp')), may hold values from 0 to 3
- task_loss_weight: float32 [4], replicated, may hold values from 0.5 to 2
- optimizer_step_count: int32 [1], replicated, may hold values from 2 to 20
- embed: bfloat16 [51200, 768], P('dp'), may hold values from -0.4375 to 0.4375
- position_embedding: bfloat16 [128, 768], replicated, may hold values from -0.4375 to 0.4375
- norm_gain_vector: float32 [6, 768], replicated, may hold values from 0.5 to 1.5
- norm_bias_vector: float32 [6, 768], replicated, may hold values from -2 to 2
- attention_in_weight: bfloat16 [2, 768, 2304], P(None, None, ('dp', 'fsdp')), may hold values from -0.21875 to 0.21875
- attention_out_weight: bfloat16 [2, 768, 768], P(None, None, ('dp', 'fsdp')), may hold values from -1.75 to 1.75
- feedforward_up: bfloat16 [2, 768, 3072], P(None, None, ('dp', 'fsdp')), may hold values from -0.21875 to 0.21875
- feedforward_down: bfloat16 [2, 3072, 768], P(None, ('dp', 'fsdp')), may hold values from -0.109375 to 0.109375
- layer_bias_vector: float32 [2, 6144], replicated, may hold values from -2 to 2
- head_dense_bias: float32 [768], replicated, may hold values from -2 to 2
- vocabulary_bias: float32 [51200], P(('dp', 'fsdp')), may hold values from -3 to 3
- adapter_down_matrix: bfloat16 [2, 2, 768, 8], replicated, may hold values from -0.21875 to 0.21875
- adapter_up_matrix: float32 [2, 2, 8, 768], P(None, None, None, ('dp', 'fsdp')), may hold values from -0.6 to 0.6
- adapter_moment_first: float32 [2, 2, 8, 768], P(None, None, None, ('dp', 'fsdp')), may hold values from -1.9073486e-05 to 1.9073486e-05
- adapter_moment_second: float32 [2, 2, 8, 768], P(None, None, None, ('dp', 'fsdp')), may hold values from 1.6276042e-13 to 6.5104167e-13
- head_projection: float32 [768, 768], P(('dp', 'fsdp')), may hold values from -0.21875 to 0.21875
- head_moment_first: float32 [768, 768], P(('dp', 'fsdp')), may hold values from -1.9073486e-05 to 1.9073486e-05
- head_moment_second: float32 [768, 768], P(('dp', 'fsdp')), may hold values from 1.6276042e-13 to 6.5104167e-13
Outputs:
- masked_task_loss: float32 [], replicated
- gradient_norm: float32 [], replicated
- lora_up_next: float32 [2, 2, 8, 768], P(None, None, None, ('dp', 'fsdp'))
- lora_first_next: float32 [2, 2, 8, 768], P(None, None, None, ('dp', 'fsdp'))
- lora_second_next: float32 [2, 2, 8, 768], P(None, None, None, ('dp', 'fsdp'))
- head_dense_next: float32 [768, 768], P(('dp', 'fsdp'))
- head_first_next: float32 [768, 768], P(('dp', 'fsdp'))
- head_second_next: float32 [768, 768], P(('dp', 'fsdp'))
The draws below stay inside these ranges and needn't reach their ends.
Inputs may be any that keep to these rules, and one draw needn't show every extreme that they name: `sentence_numbers`: segment numbers never fall along a sequence; each sentence holds 1 to 128 tokens.
All inputs are finite; a program needn't handle non-finite values.
Results may differ from the reference program's by a relative error of at most 0.0044.
Values may be sent and summed in bfloat16 or wider, within the bound.
A program may use at most 448 MiB of HBM per device.

```python
import math
import jax
import jax.numpy as jnp
import numpy as np
from jax import lax

MODEL_DIM = 768
HEADS = 12
HDIM = 64
FF = 3072
VOCAB = 51200
ADAPTER_RANK = 8
ENCODER_LAYERS = 2
SEQ = 1024
SENT_MAX = 128
SEGS = 16
LAB = 128
TASKS = 4
SEQS = 32


def touch_ends(entries, own_key, least, largest):
    place = [jax.random.randint(jax.random.fold_in(own_key, axis), (), 0, length) for axis, length in enumerate(entries.shape)]
    main_axis = entries.shape.index(max(entries.shape))
    next_to = place[:main_axis] + [(place[main_axis] + 1) % entries.shape[main_axis]] + place[main_axis + 1:]
    return entries.at[tuple(place)].set(least).at[tuple(next_to)].set(largest)


def level_of(rng, dims, split, smallest, high):
    factor_of = 1.0
    for dim, shards_of in split:
        draws = jax.random.uniform(jax.random.fold_in(jax.random.fold_in(rng, 6), dim), (shards_of,), jnp.float32, smallest / len(split), high / len(split))
        factor_of = factor_of * jnp.repeat(jnp.exp(draws), dims[dim] // shards_of).reshape((-1,) + (1,) * (len(dims) - 1 - dim))
    return factor_of


def cumulative_ranks(count, slope):
    portions = [(1 << 20) // math.isqrt(grade ** slope) + 1 for grade in range(1, count + 1)]
    deviation = 1 + sum(portions) // (1 << 30)
    return np.cumsum(np.array([max(1, weight // deviation) for weight in portions]))


def ranked(own_key, extent, number_of, lean):
    listing = cumulative_ranks(number_of, lean)
    pick = jax.random.randint(jax.random.fold_in(own_key, 1), extent, 0, int(listing[number_of - 1]))
    grade = jnp.searchsorted(jnp.asarray(listing, jnp.int32), pick, side="right")
    return jax.random.permutation(jax.random.fold_in(own_key, 2), number_of)[grade].astype(jnp.int32)


def profile(amount, total, limit, lean):
    loads = [(1 << 20) // math.isqrt(standing ** lean) + 1 for standing in range(2, amount + 1)]
    surplus, holding = total - limit - (amount - 1), [1] * (amount - 1)
    while surplus > 0:
        free = [i for i in range(amount - 1) if holding[i] < limit]
        mass, remaining = sum([loads[i] for i in free]), surplus
        for i in free:
            addition = min(limit - holding[i], max(1, remaining * loads[i] // mass), surplus)
            holding[i] = holding[i] + addition
            surplus = surplus - addition
    return np.array([limit] + holding)


def ragged_sizes(key, amount, total, reach, slope):
    if amount == 2:
        one = jax.random.randint(key, (), max(1, total - reach), min(reach, total - 1) + 1)
        return jnp.stack([one, total - one])
    tallies = jnp.asarray(profile(amount, total, reach, slope), jnp.int32)
    couples = (amount - 1) // 2
    source_of, sink = tallies[1:1 + 2 * couples:2], tallies[2:2 + 2 * couples:2]
    slack = jnp.minimum(source_of - 1, reach - sink)
    passed = jax.random.randint(jax.random.fold_in(key, 1), (couples,), 0, 1 << 20) % (slack + 1)
    tallies = tallies.at[1:1 + 2 * couples:2].set(source_of - passed).at[2:2 + 2 * couples:2].set(sink + passed)
    return tallies[jax.random.permutation(jax.random.fold_in(key, 2), amount)]


def scatter_about(own_key, dims, width, bound, pieces=(), kind=jnp.bfloat16):
    level = level_of(own_key, dims, pieces, -0.22, 0.18) if pieces else 1.0
    values = jax.random.normal(own_key, dims, jnp.float32) * width * level
    return jnp.minimum(jnp.maximum(values, -bound), bound).astype(kind)


def setup_inputs(seed: int = 0) -> dict:
    key_of = jax.random.split(jax.random.key(seed), 26)
    input_token_index = touch_ends(ranked(key_of[0], (SEQS, SEQ), VOCAB, 2), jax.random.fold_in(key_of[0], 3), 0, VOCAB - 1).astype(jnp.int32)
    sentence_numbers = jax.vmap(lambda own: jnp.searchsorted(jnp.cumsum(ragged_sizes(own, SEGS, SEQ, SENT_MAX, 1)), jnp.arange(SEQ), side="right"))(jax.random.split(key_of[1], SEQS)).reshape((SEQS, SEQ)).astype(jnp.int32)
    label_positions = touch_ends(jax.random.randint(key_of[2], (SEQS, LAB), 0, SEQ), jax.random.fold_in(key_of[2], 1), 0, SEQ - 1).astype(jnp.int32)
    label_target_token = touch_ends(ranked(key_of[3], (SEQS, LAB), VOCAB, 2), jax.random.fold_in(key_of[3], 3), 0, VOCAB - 1).astype(jnp.int32)
    sequence_task_index = touch_ends(jax.random.randint(key_of[4], (SEQS,), 0, TASKS), jax.random.fold_in(key_of[4], 1), 0, TASKS - 1).astype(jnp.int32)
    task_loss_weight = jnp.clip(jnp.exp(jax.random.uniform(key_of[5], (TASKS,), jnp.float32, math.log(0.5), math.log(2.0))), 0.5, 2.0)
    optimizer_step_count = jax.random.randint(key_of[6], (1,), 2, 21).astype(jnp.int32)
    embed = scatter_about(key_of[7], (VOCAB, MODEL_DIM), (MODEL_DIM // 4) ** -0.5, 0.4375, ((0, 2),))
    position_embedding = scatter_about(key_of[8], (SENT_MAX, MODEL_DIM), (MODEL_DIM // 4) ** -0.5, 0.4375)
    norm_gain_vector = jnp.clip(1.0 + 0.1 * jax.random.normal(key_of[9], (2 * ENCODER_LAYERS + 2, MODEL_DIM), jnp.float32), 0.5, 1.5)
    norm_bias_vector = scatter_about(key_of[10], (2 * ENCODER_LAYERS + 2, MODEL_DIM), 0.3, 2.0, (), jnp.float32)
    attention_in_weight = scatter_about(key_of[11], (ENCODER_LAYERS, MODEL_DIM, 3 * MODEL_DIM), MODEL_DIM ** -0.5, 0.21875, ((2, 32),))
    attention_out_weight = scatter_about(key_of[12], (ENCODER_LAYERS, MODEL_DIM, MODEL_DIM), (MODEL_DIM // 64) ** -0.5, 1.75, ((2, 32),))
    feedforward_up = scatter_about(key_of[13], (ENCODER_LAYERS, MODEL_DIM, FF), MODEL_DIM ** -0.5, 0.21875, ((2, 32),))
    feedforward_down = scatter_about(key_of[14], (ENCODER_LAYERS, FF, MODEL_DIM), FF ** -0.5, 0.109375, ((1, 32),))
    layer_bias_vector = scatter_about(key_of[15], (ENCODER_LAYERS, 4 * MODEL_DIM + FF), 0.3, 2.0, (), jnp.float32)
    head_dense_bias = scatter_about(key_of[16], (MODEL_DIM,), 0.3, 2.0, (), jnp.float32)
    vocabulary_bias = scatter_about(key_of[17], (VOCAB,), 0.5, 3.0, ((0, 32),), jnp.float32)
    adapter_down_matrix = scatter_about(key_of[18], (ENCODER_LAYERS, 2, MODEL_DIM, ADAPTER_RANK), MODEL_DIM ** -0.5, 0.21875)
    adapter_up_matrix = scatter_about(key_of[19], (ENCODER_LAYERS, 2, ADAPTER_RANK, MODEL_DIM), 0.1, 0.6, ((3, 32),), jnp.float32)
    adapter_moment_first = scatter_about(key_of[20], (ENCODER_LAYERS, 2, ADAPTER_RANK, MODEL_DIM), (0.11 * 0.01 / (MODEL_DIM * MODEL_DIM + ENCODER_LAYERS * 2 * ADAPTER_RANK * MODEL_DIM) ** 0.5), 1.9073486328125e-05, ((3, 32),), jnp.float32)
    adapter_moment_second = jnp.clip(jnp.exp(math.log(6.510416663239871e-13) - 1.3862944 * jax.random.uniform(key_of[21], (ENCODER_LAYERS, 2, ADAPTER_RANK, MODEL_DIM), jnp.float32) ** level_of(key_of[21], (ENCODER_LAYERS, 2, ADAPTER_RANK, MODEL_DIM), ((3, 32),), -0.2, 0.2)), 1.6276041658099677e-13, 6.510416663239871e-13)
    head_projection = scatter_about(key_of[22], (MODEL_DIM, MODEL_DIM), MODEL_DIM ** -0.5, 0.21875, ((0, 32),), jnp.float32)
    head_moment_first = scatter_about(key_of[23], (MODEL_DIM, MODEL_DIM), (0.11 * 0.01 / (MODEL_DIM * MODEL_DIM + ENCODER_LAYERS * 2 * ADAPTER_RANK * MODEL_DIM) ** 0.5), 1.9073486328125e-05, ((0, 32),), jnp.float32)
    head_moment_second = jnp.clip(jnp.exp(math.log(6.510416663239871e-13) - 1.3862944 * jax.random.uniform(key_of[24], (MODEL_DIM, MODEL_DIM), jnp.float32) ** level_of(key_of[24], (MODEL_DIM, MODEL_DIM), ((0, 32),), -0.2, 0.2)), 1.6276041658099677e-13, 6.510416663239871e-13)
    return {"input_token_index": input_token_index, "sentence_numbers": sentence_numbers, "label_positions": label_positions, "label_target_token": label_target_token, "sequence_task_index": sequence_task_index, "task_loss_weight": task_loss_weight, "optimizer_step_count": optimizer_step_count, "embed": embed, "position_embedding": position_embedding, "norm_gain_vector": norm_gain_vector, "norm_bias_vector": norm_bias_vector, "attention_in_weight": attention_in_weight, "attention_out_weight": attention_out_weight, "feedforward_up": feedforward_up, "feedforward_down": feedforward_down, "layer_bias_vector": layer_bias_vector, "head_dense_bias": head_dense_bias, "vocabulary_bias": vocabulary_bias, "adapter_down_matrix": adapter_down_matrix, "adapter_up_matrix": adapter_up_matrix, "adapter_moment_first": adapter_moment_first, "adapter_moment_second": adapter_moment_second, "head_projection": head_projection, "head_moment_first": head_moment_first, "head_moment_second": head_moment_second}


@jax.custom_vjp
def reduced_precision(v):
    return lax.optimization_barrier(v.astype(jnp.bfloat16)).astype(jnp.float32)

@jax.custom_vjp
def reduced_backward(v):
    return v

def low_keep(v):
    return (reduced_precision(v), None)

def low_pass(kept, grad):
    return (grad,)

def back_keep(v):
    return (v, None)

def back_low(kept, grad):
    return (reduced_precision(grad),)
reduced_precision.defvjp(low_keep, low_pass)
reduced_backward.defvjp(back_keep, back_low)
highest = lax.Precision.HIGHEST
norm_eps = 1e-05
adapter_scale = 2.0
clip_limit = 0.01
learn_rate = 0.05
beta_first = 0.9
beta_second = 0.999
adam_eps = 1e-08
decay_rate = 0.01
masked_score = -1e+30

def precise_product(left_side, right_side):
    return jnp.dot(left_side, right_side, precision=highest, preferred_element_type=jnp.float32)

def layer_norm(rows_in, gain, shift):
    center = rows_in - lax.optimization_barrier(jnp.mean(rows_in, -1, keepdims=True))
    spread = lax.optimization_barrier(jnp.mean(center * center, -1, keepdims=True))
    return center * lax.rsqrt(spread + norm_eps) * gain + shift

def gelu_exact(rows_in):
    return jax.nn.gelu(rows_in, approximate=False)

def seg_positions(segments):
    index = jnp.arange(segments.shape[-1], dtype=jnp.int32)
    fresh = jnp.concatenate([jnp.ones(segments.shape[:-1] + (1,), dtype=bool), segments[..., 1:] != segments[..., :-1]], -1)
    starts = lax.cummax(jnp.where(fresh, index, jnp.zeros_like(index)), axis=segments.ndim - 1)
    return index - starts

def layer_forward(hidden, same_seg, proj_w, output_w, up_w, down_w, biases, gains, down_weight_couple, up_weight_couple):
    hidden_width = hidden.shape[1]
    ff_width = up_w.shape[1]
    adapter_rank_size = down_weight_couple.shape[2]
    seq_len = hidden.shape[0]
    hidden_reduced = reduced_precision(hidden)
    down_weight_merged = jnp.concatenate([down_weight_couple[0], down_weight_couple[1]], 1)
    adapter_middle = reduced_backward(reduced_precision(precise_product(hidden_reduced, down_weight_merged)))
    bias_qkv = jnp.concatenate([biases[:hidden_width], jnp.zeros((hidden_width,), biases.dtype), biases[hidden_width:2 * hidden_width]])
    merged_parts = precise_product(hidden_reduced, proj_w) + bias_qkv
    query_rows = merged_parts[:, :hidden_width] + adapter_scale * precise_product(adapter_middle[:, :adapter_rank_size], up_weight_couple[0])
    key_rows = merged_parts[:, hidden_width:2 * hidden_width]
    value_rows = merged_parts[:, 2 * hidden_width:] + adapter_scale * precise_product(adapter_middle[:, adapter_rank_size:], up_weight_couple[1])
    query_rows, key_rows, value_rows = [reduced_backward(reduced_precision(member)).reshape(seq_len, HEADS, HDIM) for member in (query_rows, key_rows, value_rows)]
    scores = reduced_backward(jnp.einsum('qhd,khd->hqk', query_rows, key_rows, precision=highest) * HDIM ** (-0.5))
    scores = jnp.where(same_seg[None], scores, masked_score)
    weights = jax.nn.softmax(scores, -1)
    context = jnp.einsum('hqk,khd->qhd', reduced_precision(weights), value_rows, precision=highest).reshape(seq_len, hidden_width)
    context = reduced_backward(reduced_precision(context))
    attn_part = reduced_backward(precise_product(context, output_w) + biases[2 * hidden_width:3 * hidden_width])
    middle = layer_norm(hidden + attn_part, gains[0], gains[1])
    gate_preactivation = reduced_backward(precise_product(reduced_precision(middle), up_w) + biases[3 * hidden_width:3 * hidden_width + ff_width])
    branch = reduced_backward(precise_product(reduced_precision(gelu_exact(gate_preactivation)), down_w) + biases[3 * hidden_width + ff_width:])
    return layer_norm(middle + branch, gains[2], gains[3])

def optimizer_update(weight, gradient, moment_one, moment_two, step_as_real):
    moment_one = beta_first * moment_one + (1.0 - beta_first) * gradient
    moment_two = beta_second * moment_two + (1.0 - beta_second) * gradient * gradient
    one_hat = moment_one / (1.0 - beta_first ** step_as_real)
    two_hat = moment_two / (1.0 - beta_second ** step_as_real)
    weight = weight - learn_rate * (one_hat / (jnp.sqrt(two_hat) + adam_eps) + decay_rate * weight)
    return (weight, moment_one, moment_two)

def reference(input_token_index, sentence_numbers, label_positions, label_target_token, sequence_task_index, task_loss_weight, optimizer_step_count, embed, position_embedding, norm_gain_vector, norm_bias_vector, attention_in_weight, attention_out_weight, feedforward_up, feedforward_down, layer_bias_vector, head_dense_bias, vocabulary_bias, adapter_down_matrix, adapter_up_matrix, adapter_moment_first, adapter_moment_second, head_projection, head_moment_first, head_moment_second):
    task_hot = (sequence_task_index[:, None] == jnp.arange(TASKS, dtype=jnp.int32)[None, :]).astype(jnp.float32)
    counts = lax.optimization_barrier(jnp.sum(task_hot, 0)) * LAB
    task_table = task_loss_weight / jnp.maximum(counts, 1.0)
    seq_weight = lax.optimization_barrier(jnp.sum(task_hot * task_table[None, :], 1))
    embed_f = embed.astype(jnp.float32)
    place_f = position_embedding.astype(jnp.float32)
    proj_f = attention_in_weight.astype(jnp.float32)
    output_f = attention_out_weight.astype(jnp.float32)
    up_f = feedforward_up.astype(jnp.float32)
    down_f = feedforward_down.astype(jnp.float32)
    adapter_apply = adapter_down_matrix.astype(jnp.float32)

    def compute_loss(up_weights, dense):
        up_low = reduced_precision(up_weights)
        dense_low = reduced_precision(dense)

        def one_seq(running, seq_item):
            tokens, segments, places, targets, weight = seq_item
            hidden = embed_f[tokens] + place_f[seg_positions(segments)]
            hidden = layer_norm(hidden, norm_gain_vector[0], norm_bias_vector[0])
            same_seg = segments[:, None] == segments[None, :]
            for layer_position in range(ENCODER_LAYERS):
                gains = (norm_gain_vector[1 + 2 * layer_position], norm_bias_vector[1 + 2 * layer_position], norm_gain_vector[2 + 2 * layer_position], norm_bias_vector[2 + 2 * layer_position])
                hidden = layer_forward(hidden, same_seg, proj_f[layer_position], output_f[layer_position], up_f[layer_position], down_f[layer_position], layer_bias_vector[layer_position], gains, adapter_apply[layer_position], up_low[layer_position])
            picked = hidden[places]
            pre_act = reduced_backward(precise_product(reduced_precision(picked), dense_low) + head_dense_bias)
            feats = reduced_precision(layer_norm(gelu_exact(pre_act), norm_gain_vector[-1], norm_bias_vector[-1]))
            logits = reduced_backward(precise_product(feats, embed_f.T) + vocabulary_bias)
            log_total = jax.nn.logsumexp(logits, -1)
            target = jnp.take_along_axis(logits, targets[:, None], 1)[:, 0]
            return (running + weight * jnp.sum(log_total - target), None)
        loss_total, unused = lax.scan(jax.checkpoint(one_seq), jnp.zeros((), jnp.float32), (input_token_index, sentence_numbers, label_positions, label_target_token, seq_weight))
        return loss_total
    masked_task_loss, fetch_rows = jax.vjp(compute_loss, adapter_up_matrix, head_projection)
    adapter_gradient, dense_gradient = fetch_rows(jnp.ones((), jnp.float32))
    gradient_norm = jnp.sqrt(jnp.sum(adapter_gradient * adapter_gradient) + jnp.sum(dense_gradient * dense_gradient))
    scale_factor = jnp.minimum(1.0, clip_limit / (gradient_norm + 1e-06))
    step_as_real = optimizer_step_count[0].astype(jnp.float32)
    adapter_updated, adapter_first_part, adapter_second_part = optimizer_update(adapter_up_matrix, adapter_gradient * scale_factor, adapter_moment_first, adapter_moment_second, step_as_real)
    dense_updated, dense_moment_first, dense_moment_second = optimizer_update(head_projection, dense_gradient * scale_factor, head_moment_first, head_moment_second, step_as_real)
    return (masked_task_loss, gradient_norm, adapter_updated, adapter_first_part, adapter_second_part, dense_updated, dense_moment_first, dense_moment_second)
```

```python
import functools

import jax
import jax.numpy as jnp
from jax import lax
from jax.experimental import pallas as pl
from jax.experimental.pallas import tpu as pltpu
from jax.sharding import PartitionSpec as P

HEADS = 12
TASKS = 4
REACH = 128

norm_eps = 1e-05
adapter_scale = 2.0
clip_limit = 0.01
learn_rate = 0.05
beta_first = 0.9
beta_second = 0.999
adam_eps = 1e-08
decay_rate = 0.01
masked_score = -1e30

BF = jnp.bfloat16
F32 = jnp.float32
BOTH = ("dp", "fsdp")
VMEM_BYTES = 60 * 1024 * 1024


def mm(a, b):
    return lax.dot_general(a, b, (((1,), (0,)), ((), ())), preferred_element_type=F32)


def mm_nt(a, b):
    return lax.dot_general(a, b, (((1,), (1,)), ((), ())), preferred_element_type=F32)


def mm_tn(a, b):
    return lax.dot_general(a, b, (((0,), (0,)), ((), ())), preferred_element_type=F32)


def layer_norm(rows_in, gain, shift):
    center = rows_in - jnp.mean(rows_in, -1, keepdims=True)
    spread = jnp.mean(center * center, -1, keepdims=True)
    return center * lax.rsqrt(spread + norm_eps) * gain + shift


def norm_back(rows_in, gain, gradient):
    center = rows_in - jnp.mean(rows_in, -1, keepdims=True)
    inverse = lax.rsqrt(jnp.mean(center * center, -1, keepdims=True) + norm_eps)
    unit = center * inverse
    scaled = gradient * gain
    return inverse * (
        scaled
        - jnp.mean(scaled, -1, keepdims=True)
        - unit * jnp.mean(scaled * unit, -1, keepdims=True)
    )


def gelu_pair(v):
    size = jnp.abs(v) * 0.7071067811865476
    base = 1.0 + 0.3275911 * size
    t = pl.reciprocal(base, approx=True)
    t = t * (2.0 - base * t)
    bell = jnp.exp(-0.5 * v * v)
    poly = t * (
        0.127414796 + t * (-0.142248368 + t * (0.7107068705 + t * (-0.7265760135 + t * 0.5307027145)))
    )
    tail = poly * bell
    phi = jnp.where(v >= 0.0, 1.0 - tail, tail)
    return v * phi, phi + v * (bell * 0.3989422804014327)


def params(**more):
    return pltpu.CompilerParams(vmem_limit_bytes=VMEM_BYTES, **more)


def full(shape):
    return pl.BlockSpec(shape, lambda *_: (0,) * len(shape))


def split_of(total, most, step):
    size = (min(most, total) // step) * step
    while size > step and total % size:
        size -= step
    return size if size and total % size == 0 else total


def pair_rows(block, width):
    first = lax.broadcasted_iota(jnp.int32, block.shape, 1) < width
    return jnp.concatenate([jnp.where(first, block, 0.0), jnp.where(first, 0.0, block)], 0).astype(BF)


def pair_join(wide, width):
    rows = wide.shape[1] // 2
    return jnp.concatenate([wide[:width, :rows], wide[width:, rows:]], 0)


def masked(scores, same):
    rows = scores.shape[1] // 2
    return jnp.concatenate(
        [
            jnp.where(same, scores[:, :rows], masked_score),
            jnp.where(same, scores[:, rows:], masked_score),
        ],
        1,
    )


def project_body(x_ref, down_ref, w_ref, up_ref, bias_ref, out_ref, mid_ref):
    low = x_ref[...].astype(BF)
    mid = mm(low, down_ref[...]).astype(BF)
    mid_ref[...] = mid
    total = w_ref.shape[0]
    step = split_of(total, 768, 128)
    for start in range(0, total, step):
        part = slice(start, start + step)
        out_ref[:, part] = (
            mm_nt(low, w_ref[part, :]) + mm(mid, up_ref[:, part]) + bias_ref[:, part]
        ).astype(BF)


def project(x, down, w, up, bias):
    rows, width = x.shape
    tile = split_of(rows, 256, 16)
    total = w.shape[0]
    return pl.pallas_call(
        project_body,
        grid=(rows // tile,),
        in_specs=[
            pl.BlockSpec((tile, width), lambda i: (i, 0)),
            full(down.shape),
            full(w.shape),
            full(up.shape),
            full(bias.shape),
        ],
        out_specs=[
            pl.BlockSpec((tile, total), lambda i: (i, 0)),
            pl.BlockSpec((tile, down.shape[1]), lambda i: (i, 0)),
        ],
        out_shape=[
            jax.ShapeDtypeStruct((rows, total), BF),
            jax.ShapeDtypeStruct((rows, down.shape[1]), BF),
        ],
        compiler_params=params(),
        name="project",
    )(x, down, w, up, bias)


def attend_body(q_ref, k_ref, v_ref, seg_ref, seg_row_ref, ctx_ref, log_ref):
    rows = q_ref.shape[0]
    width = q_ref.shape[1] // 2
    scale = width**-0.5
    for start in range(0, rows, REACH):
        own = slice(start, start + REACH)
        near = slice(max(0, start - REACH), min(rows, start + 2 * REACH))
        queries = pair_rows(q_ref[own, :].astype(F32) * scale, width)
        same = seg_ref[near, :] == seg_row_ref[:, own]
        scores = masked(mm_nt(k_ref[near, :], queries), same)
        top = jnp.max(scores, 0, keepdims=True)
        weights = jnp.exp(scores - top)
        total = jnp.sum(weights, 0, keepdims=True)
        context = mm_tn(v_ref[near, :], weights.astype(BF)) * (1.0 / total)
        ctx_ref[own, :] = pair_join(context, width).T.astype(BF)
        log_ref[0, :, 2 * start : 2 * start + 2 * REACH] = top + jnp.log(total)


def attend(qkv, seg_wide, seg_row):
    rows, total = qkv.shape
    hidden = total // 3
    lanes = 2 * (hidden // HEADS)
    pairs = hidden // lanes
    column = lambda kind: pl.BlockSpec((rows, lanes), lambda p: (0, kind * pairs + p))
    return pl.pallas_call(
        attend_body,
        grid=(pairs,),
        in_specs=[column(0), column(1), column(2), full(seg_wide.shape), full(seg_row.shape)],
        out_specs=[
            pl.BlockSpec((rows, lanes), lambda p: (0, p)),
            pl.BlockSpec((1, 1, 2 * rows), lambda p: (p, 0, 0)),
        ],
        out_shape=[
            jax.ShapeDtypeStruct((rows, hidden), BF),
            jax.ShapeDtypeStruct((pairs, 1, 2 * rows), F32),
        ],
        compiler_params=params(),
        name="attend",
    )(qkv, qkv, qkv, seg_wide, seg_row)


def flat(ref):
    whole = ref[...]
    return whole.reshape(-1, whole.shape[-1])


def rows_of(ref, start, size):
    each = ref.shape[1]
    if size % each == 0 and start % each == 0 and each % 16 == 0:
        part = ref[start // each : (start + size) // each, :, :]
        return part.reshape(size, part.shape[-1])
    return flat(ref)[start : start + size, :]


def feed_step(ref):
    units = ref.shape[0] * ref.shape[1]
    step = ref.shape[1]
    while units % (2 * step) == 0 and 2 * step <= 768 and ref.shape[0] > 1:
        step *= 2
    return units, (step if ref.shape[0] > 1 else split_of(units, 768, 128))


def after_body(
    ctx_ref, x_ref, wo_ref, up_ref, down_ref, bo_ref, b1_ref, b2_ref, norm_ref,
    out_ref, one_ref, two_ref, slope_ref,
):
    one = x_ref[...] + (mm_nt(ctx_ref[...], wo_ref[...]) + bo_ref[...])
    one_ref[...] = one
    middle = layer_norm(one, norm_ref[0:1, :], norm_ref[1:2, :])
    low = middle.astype(BF)
    total = middle + b2_ref[...]
    units, step = feed_step(up_ref)
    for start in range(0, units, step):
        part = slice(start, start + step)
        act, slope = gelu_pair(mm_nt(low, rows_of(up_ref, start, step)) + b1_ref[:, part])
        slope_ref[:, part] = slope.astype(BF)
        total = total + mm(act.astype(BF), rows_of(down_ref, start, step))
    two_ref[...] = total
    out_ref[...] = layer_norm(total, norm_ref[2:3, :], norm_ref[3:4, :])


def slab_spec(slab):
    array, place, rows = slab
    return pl.BlockSpec((array.shape[0], rows, array.shape[2]), lambda *_: (0, place, 0))


def after(ctx, x, wo, up, down, bo, b1, b2, norms):
    rows, width = x.shape
    tile = split_of(rows, 256, 16)
    units = b1.shape[1]
    row = lambda n: pl.BlockSpec((tile, n), lambda i: (i, 0))
    return pl.pallas_call(
        after_body,
        grid=(rows // tile,),
        in_specs=[row(width), row(width), full(wo.shape), slab_spec(up), slab_spec(down)]
        + [full(a.shape) for a in (bo, b1, b2, norms)],
        out_specs=[row(width), row(width), row(width), row(units)],
        out_shape=[jax.ShapeDtypeStruct((rows, width), F32)] * 3
        + [jax.ShapeDtypeStruct((rows, units), BF)],
        compiler_params=params(),
        name="after",
    )(ctx, x, wo, up[0], down[0], bo, b1, b2, norms)


def exact_rows(choose, matrix):
    high = matrix.astype(BF)
    rest = matrix - high.astype(F32)
    middle = rest.astype(BF)
    low = (rest - middle.astype(F32)).astype(BF)
    return mm(choose, high) + mm(choose, middle) + mm(choose, low)


def last_forward_body(
    x_ref, place_ref, place_row_ref, seg_ref, down_ref, w_ref, adapt_ref, bias_ref, wo_ref, up_any, dn_any,
    bo_ref, b1_ref, b2_ref, norm_ref, hb_ref, hbias_ref,
    kv_ref, q_ref, mid_ref, log_ref, one_ref, slope_ref, two_ref, low_ref, act_ref, hslope_ref, feat_ref,
    up_ref, dn_ref, ctx_ref, sems, *, places,
):
    copies = []
    for k, (source, target, place) in enumerate(
        ((up_any, up_ref, places[0]), (dn_any, dn_ref, places[1]))
    ):
        rows = target.shape[1]
        copies.append(
            pltpu.make_async_copy(
                source.at[:, pl.ds(place * rows, rows), :], target, sems.at[k]
            )
        )
        copies[-1].start()
    rows, hidden = x_ref.shape
    labels = place_ref.shape[0]
    lanes = 2 * (hidden // HEADS)
    width = lanes // 2
    low = x_ref[...].astype(BF)
    mid = mm(low, down_ref[...]).astype(BF)
    mid_ref[...] = mid
    step = split_of(2 * hidden, 512, 128)
    for start in range(hidden, 3 * hidden, step):
        part = slice(start, start + step)
        kv_ref[:, start - hidden : start - hidden + step] = (
            mm_nt(low, w_ref[part, :]) + mm(mid, adapt_ref[:, part]) + bias_ref[:, part]
        ).astype(BF)
    choose = (
        lax.broadcasted_iota(jnp.int32, (labels, rows), 1) == place_ref[...][:, 0:1]
    ).astype(F32).astype(BF)
    own = exact_rows(choose, x_ref[...])
    own_low = own.astype(BF)
    own_mid = mm(choose, mid).astype(BF)
    q_ref[...] = (
        mm_nt(own_low, w_ref[:hidden, :]) + mm(own_mid, adapt_ref[:, :hidden]) + bias_ref[:, :hidden]
    ).astype(BF)
    seg = seg_ref[...]
    seg_own = jnp.sum(
        jnp.where(
            lax.broadcasted_iota(jnp.int32, (rows, labels), 0) == place_row_ref[...], seg, 0.0
        ),
        0,
        keepdims=True,
    )
    same = seg == seg_own
    for p in range(hidden // lanes):
        part = slice(p * lanes, (p + 1) * lanes)
        queries = pair_rows(q_ref[:, part].astype(F32) * width**-0.5, width)
        scores = masked(mm_nt(kv_ref[:, part], queries), same)
        top = jnp.max(scores, 0, keepdims=True)
        weights = jnp.exp(scores - top)
        total = jnp.sum(weights, 0, keepdims=True)
        context = mm_tn(
            kv_ref[:, hidden + p * lanes : hidden + (p + 1) * lanes], weights.astype(BF)
        ) * (1.0 / total)
        ctx_ref[:, part] = pair_join(context, width).T.astype(BF)
        log_ref[p : p + 1, :] = top + jnp.log(total)
    one = own + (mm_nt(ctx_ref[...], wo_ref[...]) + bo_ref[...])
    one_ref[...] = one
    middle = layer_norm(one, norm_ref[0:1, :], norm_ref[1:2, :])
    middle_low = middle.astype(BF)
    sum_two = middle + b2_ref[...]
    units, step = feed_step(up_ref)
    for copy in copies:
        copy.wait()
    for start in range(0, units, step):
        part = slice(start, start + step)
        act, slope = gelu_pair(mm_nt(middle_low, rows_of(up_ref, start, step)) + b1_ref[:, part])
        slope_ref[:, part] = slope.astype(BF)
        sum_two = sum_two + mm(act.astype(BF), rows_of(dn_ref, start, step))
    two_ref[...] = sum_two
    out_low = layer_norm(sum_two, norm_ref[2:3, :], norm_ref[3:4, :]).astype(BF)
    low_ref[...] = out_low
    act, slope = gelu_pair(mm(out_low, hb_ref[...]) + hbias_ref[...])
    act_ref[...] = act
    hslope_ref[...] = slope
    feat_ref[...] = layer_norm(act, norm_ref[4:5, :], norm_ref[5:6, :]).astype(BF)


def slab_scratch(slab):
    array, place, rows = slab
    return pltpu.VMEM((array.shape[0], rows, array.shape[2]), BF)


def last_forward(x, place_col, place_row, seg_wide, down, w, adapt, bias, wo, up, dn, bo, b1, b2, norms, hb, hbias):
    rows, hidden = x.shape
    labels = place_col.shape[0]
    units = b1.shape[1]
    whole = pl.BlockSpec(memory_space=pltpu.VMEM)
    anywhere = pl.BlockSpec(memory_space=pl.ANY)
    shape = jax.ShapeDtypeStruct
    pairs = HEADS // 2
    return pl.pallas_call(
        functools.partial(last_forward_body, places=(up[1], dn[1])),
        in_specs=[whole] * 9 + [anywhere] * 2 + [whole] * 6,
        out_specs=[whole] * 11,
        out_shape=[
            shape((rows, 2 * hidden), BF),
            shape((labels, hidden), BF),
            shape((rows, down.shape[1]), BF),
            shape((pairs, 2 * labels), F32),
            shape((labels, hidden), F32),
            shape((labels, units), BF),
            shape((labels, hidden), F32),
            shape((labels, hidden), BF),
            shape((labels, hidden), F32),
            shape((labels, hidden), F32),
            shape((labels, hidden), BF),
        ],
        scratch_shapes=[
            slab_scratch(up),
            slab_scratch(dn),
            pltpu.VMEM((labels, hidden), BF),
            pltpu.SemaphoreType.DMA((2,)),
        ],
        compiler_params=params(),
        name="last_forward",
    )(x, place_col, place_row, seg_wide, down, w, adapt, bias, wo, up[0], dn[0], bo, b1, b2, norms, hb, hbias)


def vocab_body(u_ref, e_ref, et_ref, bias_ref, num_ref, log_ref, scores, weights):
    count = e_ref.shape[0]
    step = split_of(count, 640, 16)
    u = u_ref[...]
    rows = u.shape[0]
    labels = num_ref.shape[2]
    top = jnp.full((1, rows), -jnp.inf, F32)
    for start in range(0, count, step):
        part = slice(start, start + step)
        bias = bias_ref[part, :]
        logits = mm_nt(e_ref[part, :], u) + jnp.concatenate([bias] * (rows // bias.shape[1]), 1)
        scores[part, :] = logits
        top = jnp.maximum(top, jnp.max(logits, 0, keepdims=True))
    total = jnp.zeros((1, rows), F32)
    for start in range(0, count, step):
        part = slice(start, start + step)
        grown = jnp.exp(scores[part, :] - top)
        total = total + jnp.sum(grown, 0, keepdims=True)
        weights[part, :] = grown.astype(BF)
    mean = mm(et_ref[...], weights[...]) * (1.0 / total)
    logs = top + jnp.log(total)
    for k in range(rows // labels):
        num_ref[k, :, :] = mean[:, k * labels : (k + 1) * labels]
        log_ref[k, :, :] = logs[:, k * labels : (k + 1) * labels]


def vocab(u, e, et, bias_wide, labels):
    rows, hidden = u.shape
    count = e.shape[0]
    tile = 2 * labels
    return pl.pallas_call(
        vocab_body,
        grid=(rows // tile,),
        in_specs=[
            pl.BlockSpec((tile, hidden), lambda i: (i, 0)),
            full(e.shape),
            full(et.shape),
            full(bias_wide.shape),
        ],
        out_specs=[
            pl.BlockSpec((2, hidden, labels), lambda i: (i, 0, 0)),
            pl.BlockSpec((2, 1, labels), lambda i: (i, 0, 0)),
        ],
        out_shape=[
            jax.ShapeDtypeStruct((rows // labels, hidden, labels), F32),
            jax.ShapeDtypeStruct((rows // labels, 1, labels), F32),
        ],
        scratch_shapes=[pltpu.VMEM((count, tile), F32), pltpu.VMEM((count, tile), BF)],
        compiler_params=params(),
        name="vocab",
    )(u, e, et, bias_wide)


def last_backward_body(
    du_ref, kv_ref, q_ref, mid_ref, log_ref, one_ref, slope_ref, two_ref, low_ref, act_ref, hslope_ref,
    place_ref, place_row_ref, seg_ref, down_ref, w_ref, adapt_ref, wo_ref, up_any, dn_any, norm_ref, hb_ref,
    dx_ref, gh_ref, gq_ref, gv_ref,
    up_ref, dn_ref, dkv_ref, dq_ref, sems, *, places, rank,
):
    copies = []
    for k, (source, target, place) in enumerate(
        ((up_any, up_ref, places[0]), (dn_any, dn_ref, places[1]))
    ):
        rows = target.shape[1]
        copies.append(
            pltpu.make_async_copy(
                source.at[:, pl.ds(place * rows, rows), :], target, sems.at[k]
            )
        )
        copies[-1].start()
    rows = kv_ref.shape[0]
    labels, hidden = du_ref.shape
    lanes = 2 * (hidden // HEADS)
    width = lanes // 2
    scale = width**-0.5
    dact = norm_back(act_ref[...], norm_ref[4:5, :], du_ref[...])
    dz = (hslope_ref[...] * dact).astype(BF)
    gh_ref[...] = mm_tn(low_ref[...], dz)
    dtwo = norm_back(two_ref[...], norm_ref[2:3, :], mm_nt(dz, hb_ref[...]))
    dtwo_low = dtwo.astype(BF)
    dmiddle = dtwo
    units, step = feed_step(up_ref)
    for copy in copies:
        copy.wait()
    for start in range(0, units, step):
        part = slice(start, start + step)
        dgate = (
            slope_ref[:, part].astype(F32) * mm_nt(dtwo_low, rows_of(dn_ref, start, step))
        ).astype(BF)
        dmiddle = dmiddle + mm(dgate, rows_of(up_ref, start, step))
    done = norm_back(one_ref[...], norm_ref[0:1, :], dmiddle)
    dctx = mm(done.astype(BF), wo_ref[...]).astype(BF)
    seg = seg_ref[...]
    choose_t = lax.broadcasted_iota(jnp.int32, (rows, labels), 0) == place_row_ref[...]
    same = seg == jnp.sum(jnp.where(choose_t, seg, 0.0), 0, keepdims=True)
    for p in range(hidden // lanes):
        part = slice(p * lanes, (p + 1) * lanes)
        later = slice(hidden + p * lanes, hidden + (p + 1) * lanes)
        queries = pair_rows(q_ref[:, part].astype(F32) * scale, width)
        outs = pair_rows(dctx[:, part].astype(F32), width)
        keys = kv_ref[:, part]
        weights = jnp.exp(masked(mm_nt(keys, queries), same) - log_ref[p : p + 1, :])
        dweights = mm_nt(kv_ref[:, later], outs)
        inner = jnp.sum(dweights * weights, 0, keepdims=True)
        dscores = (weights * (dweights - inner)).astype(BF)
        dkv_ref[:, part] = mm(dscores, queries).astype(BF)
        dkv_ref[:, later] = mm(weights.astype(BF), outs).astype(BF)
        dq_ref[:, part] = (pair_join(mm_tn(keys, dscores), width) * scale).T.astype(BF)
    dq = dq_ref[...]
    own_mid = mm(
        (lax.broadcasted_iota(jnp.int32, (labels, rows), 1) == place_ref[...][:, 0:1]).astype(F32).astype(BF),
        mid_ref[...],
    ).astype(BF)
    gq_ref[...] = adapter_scale * mm_tn(own_mid, dq)[:rank, :]
    gv_ref[...] = adapter_scale * mm_tn(mid_ref[...], dkv_ref[:, hidden:])[rank : 2 * rank, :]
    dmid_own = mm_nt(dq, adapt_ref[:, :hidden]).astype(BF)
    own = done + mm(dq, w_ref[:hidden, :]) + mm_nt(dmid_own, down_ref[...])
    spread = choose_t.astype(F32).astype(BF)
    own_high = own.astype(BF)
    own_rest = (own - own_high.astype(F32)).astype(BF)
    dmid = mm_nt(dkv_ref[:, hidden:], adapt_ref[:, 2 * hidden :]).astype(BF)
    step = split_of(hidden, 256, 128)
    for start in range(0, hidden, step):
        part = slice(start, start + step)
        dx_ref[:, part] = (
            mm(dkv_ref[...], w_ref[hidden:, part])
            + mm_nt(dmid, down_ref[part, :])
            + mm(spread, own_high[:, part])
            + mm(spread, own_rest[:, part])
        )


def last_backward(du, saved, place_col, place_row, seg_wide, down, w, adapt, wo, up, dn, norms, hb, rank):
    kv = saved[0]
    rows = kv.shape[0]
    labels, hidden = du.shape
    whole = pl.BlockSpec(memory_space=pltpu.VMEM)
    anywhere = pl.BlockSpec(memory_space=pl.ANY)
    shape = jax.ShapeDtypeStruct
    return pl.pallas_call(
        functools.partial(last_backward_body, places=(up[1], dn[1]), rank=rank),
        in_specs=[whole] * 18 + [anywhere] * 2 + [whole] * 2,
        out_specs=[whole] * 4,
        out_shape=[
            shape((rows, hidden), F32),
            shape((hidden, hidden), F32),
            shape((rank, hidden), F32),
            shape((rank, hidden), F32),
        ],
        scratch_shapes=[
            slab_scratch(up),
            slab_scratch(dn),
            pltpu.VMEM(kv.shape, BF),
            pltpu.VMEM((labels, hidden), BF),
            pltpu.SemaphoreType.DMA((2,)),
        ],
        compiler_params=params(),
        name="last_backward",
    )(du, *saved, place_col, place_row, seg_wide, down, w, adapt, wo, up[0], dn[0], norms, hb)


def after_back_body(dout_ref, one_ref, two_ref, slope_ref, wo_ref, up_ref, down_ref, norm_ref, dctx_ref):
    dtwo = norm_back(two_ref[...], norm_ref[2:3, :], dout_ref[...])
    low = dtwo.astype(BF)
    dmiddle = dtwo
    units, step = feed_step(up_ref)
    for start in range(0, units, step):
        part = slice(start, start + step)
        dgate = (
            slope_ref[:, part].astype(F32) * mm_nt(low, rows_of(down_ref, start, step))
        ).astype(BF)
        dmiddle = dmiddle + mm(dgate, rows_of(up_ref, start, step))
    done = norm_back(one_ref[...], norm_ref[0:1, :], dmiddle)
    dctx_ref[...] = mm(done.astype(BF), wo_ref[...]).astype(BF)


def after_back(dout, one, two, slope, wo, up, down, norms):
    rows, width = dout.shape
    tile = split_of(rows, 256, 16)
    row = lambda n: pl.BlockSpec((tile, n), lambda i: (i, 0))
    return pl.pallas_call(
        after_back_body,
        grid=(rows // tile,),
        in_specs=[row(width), row(width), row(width), row(slope.shape[1]), full(wo.shape)]
        + [slab_spec(up), slab_spec(down), full(norms.shape)],
        out_specs=row(width),
        out_shape=jax.ShapeDtypeStruct((rows, width), BF),
        compiler_params=params(),
        name="after_back",
    )(dout, one, two, slope, wo, up[0], down[0], norms)


def attend_back_body(
    q_ref, k_ref, v_ref, dctx_ref, log_ref, seg_ref, seg_row_ref, mid_ref, gq_ref, gv_ref, dv_ref
):
    rows = q_ref.shape[0]
    width = q_ref.shape[1] // 2
    scale = width**-0.5
    rank = gq_ref.shape[0]
    dv_ref[...] = jnp.zeros_like(dv_ref)
    gq = jnp.zeros((2 * width, mid_ref.shape[1]), F32)
    for start in range(0, rows, REACH):
        own = slice(start, start + REACH)
        near = slice(max(0, start - REACH), min(rows, start + 2 * REACH))
        queries = pair_rows(q_ref[own, :].astype(F32) * scale, width)
        outs = pair_rows(dctx_ref[own, :].astype(F32), width)
        same = seg_ref[near, :] == seg_row_ref[:, own]
        keys = k_ref[near, :]
        logs = log_ref[0, :, 2 * start : 2 * start + 2 * REACH]
        weights = jnp.exp(masked(mm_nt(keys, queries), same) - logs)
        dweights = mm_nt(v_ref[near, :], outs)
        inner = jnp.sum(dweights * weights, 0, keepdims=True)
        dscores = (weights * (dweights - inner)).astype(BF)
        dv_ref[near, :] += mm(weights.astype(BF), outs)
        dq = (pair_join(mm_tn(keys, dscores), width) * scale).astype(BF)
        gq = gq + mm(dq, mid_ref[own, :])
    gq_ref[...] = adapter_scale * gq.T[:rank, :]
    gv_ref[...] = adapter_scale * mm_tn(mid_ref[...], dv_ref[...].astype(BF))[rank : 2 * rank, :]


def attend_back(qkv, dctx, logs, seg_wide, seg_row, mid, rank):
    rows, total = qkv.shape
    hidden = total // 3
    lanes = 2 * (hidden // HEADS)
    pairs = hidden // lanes
    column = lambda kind: pl.BlockSpec((rows, lanes), lambda p: (0, kind * pairs + p))
    return pl.pallas_call(
        attend_back_body,
        grid=(pairs,),
        in_specs=[
            column(0),
            column(1),
            column(2),
            column(0),
            pl.BlockSpec((1, 1, 2 * rows), lambda p: (p, 0, 0)),
            full(seg_wide.shape),
            full(seg_row.shape),
            full(mid.shape),
        ],
        out_specs=[pl.BlockSpec((rank, lanes), lambda p: (0, p))] * 2,
        out_shape=[jax.ShapeDtypeStruct((rank, hidden), F32)] * 2,
        scratch_shapes=[pltpu.VMEM((rows, lanes), F32)],
        compiler_params=params(),
        name="attend_back",
    )(qkv, qkv, qkv, dctx, logs, seg_wide, seg_row, mid)


def seg_positions(segments):
    index = jnp.arange(segments.shape[-1], dtype=jnp.int32)
    fresh = jnp.concatenate([jnp.ones((1,), dtype=bool), segments[1:] != segments[:-1]], -1)
    starts = lax.cummax(jnp.where(fresh, index, jnp.zeros_like(index)), axis=0)
    return index - starts


def optimizer_update(weight, gradient, moment_one, moment_two, step_as_real):
    moment_one = beta_first * moment_one + (1.0 - beta_first) * gradient
    moment_two = beta_second * moment_two + (1.0 - beta_second) * gradient * gradient
    one_hat = moment_one / (1.0 - beta_first**step_as_real)
    two_hat = moment_two / (1.0 - beta_second**step_as_real)
    weight = weight - learn_rate * (one_hat / (jnp.sqrt(two_hat) + adam_eps) + decay_rate * weight)
    return (weight, moment_one, moment_two)


def pad_rows(matrix, multiple):
    return jnp.pad(matrix, ((0, -matrix.shape[0] % multiple), (0, 0)))


def slab_of(gathered, start, rows):
    if rows % 16 == 0 and start % rows == 0:
        return (gathered, start // rows, rows)
    part = gathered[:, start : start + rows].reshape(1, -1, gathered.shape[2])
    return (part, 0, part.shape[1])


def per_device(
    input_token_index,
    sentence_numbers,
    label_positions,
    label_target_token,
    sequence_task_index,
    task_loss_weight,
    optimizer_step_count,
    embed,
    position_embedding,
    norm_gain_vector,
    norm_bias_vector,
    attention_in_weight,
    attention_out_weight,
    feedforward_up,
    feedforward_down,
    layer_bias_vector,
    head_dense_bias,
    vocabulary_bias,
    adapter_down_matrix,
    adapter_up_matrix,
    adapter_moment_first,
    adapter_moment_second,
    head_projection,
    head_moment_first,
    head_moment_second,
):
    shards = lax.axis_size("dp") * lax.axis_size("fsdp")
    dp_index = lax.axis_index("dp")
    fsdp_index = lax.axis_index("fsdp")
    layers, unused, rank, up_part = adapter_up_matrix.shape
    hidden = embed.shape[1]
    tokens = input_token_index.shape[1]
    labels = label_positions.shape[1]
    qkv_rows = attention_in_weight.shape[2]
    out_rows = attention_out_weight.shape[2]
    ff_rows = feedforward_up.shape[2]
    head_rows = head_projection.shape[0]

    pieces = []
    for layer in range(layers):
        pieces += [feedforward_up[layer].T, feedforward_down[layer]]
    for layer in range(layers):
        pieces += [attention_in_weight[layer].T, attention_out_weight[layer].T]
    pieces += [head_projection.astype(BF)]
    ups = adapter_up_matrix.astype(BF).reshape(-1)
    up_rows = -(-ups.size // hidden)
    pieces += [jnp.pad(ups, (0, up_rows * hidden - ups.size)).reshape(up_rows, hidden)]
    chunk = pad_rows(jnp.concatenate(pieces, 0), 32)
    gathered = lax.all_gather(chunk, BOTH, axis=0, tiled=False)
    slabs = [
        (
            slab_of(gathered, 2 * layer * ff_rows, ff_rows),
            slab_of(gathered, (2 * layer + 1) * ff_rows, ff_rows),
        )
        for layer in range(layers)
    ]
    at = 2 * layers * ff_rows
    in_weights, out_weights = [], []
    for layer in range(layers):
        in_weights.append(gathered[:, at : at + qkv_rows].reshape(-1, hidden))
        at += qkv_rows
        out_weights.append(gathered[:, at : at + out_rows].reshape(-1, hidden))
        at += out_rows
    head_full = gathered[:, at : at + head_rows].reshape(-1, hidden)
    at += head_rows
    ups_full = (
        gathered[:, at : at + up_rows]
        .reshape(shards, -1)[:, : ups.size]
        .reshape(shards, layers, 2, rank, up_part)
        .transpose(1, 2, 3, 0, 4)
        .reshape(layers, 2, rank, hidden)
    )
    adapters = [
        jnp.zeros((128, 3 * hidden), BF)
        .at[:rank, :hidden]
        .set(2 * ups_full[layer, 0])
        .at[rank : 2 * rank, 2 * hidden :]
        .set(2 * ups_full[layer, 1])
        for layer in range(layers)
    ]
    downs = [
        jnp.zeros((hidden, 128), BF)
        .at[:, :rank]
        .set(adapter_down_matrix[layer, 0])
        .at[:, rank : 2 * rank]
        .set(adapter_down_matrix[layer, 1])
        for layer in range(layers)
    ]
    bias_of = []
    for layer in range(layers):
        b = layer_bias_vector[layer][None, :]
        ff = b.shape[1] - 4 * hidden
        bias_of.append(
            (
                jnp.concatenate(
                    [b[:, :hidden], jnp.zeros((1, hidden), F32), b[:, hidden : 2 * hidden]], 1
                ),
                b[:, 2 * hidden : 3 * hidden],
                b[:, 3 * hidden : 3 * hidden + ff],
                b[:, 3 * hidden + ff :],
            )
        )
    norms_of = [
        jnp.concatenate(
            [
                norm_gain_vector[1 + 2 * layer][None],
                norm_bias_vector[1 + 2 * layer][None],
                norm_gain_vector[2 + 2 * layer][None],
                norm_bias_vector[2 + 2 * layer][None],
                norm_gain_vector[-1][None],
                norm_bias_vector[-1][None],
            ],
            0,
        )
        for layer in range(layers)
    ]

    table_rows = embed.shape[0]
    wanted = jnp.concatenate([input_token_index[0], label_target_token[0]])
    group_ids = lax.all_gather(wanted, "dp", axis=0, tiled=True) - dp_index * table_rows
    inside = (group_ids >= 0) & (group_ids < table_rows)
    looked = jnp.where(
        inside[:, None], embed[jnp.clip(group_ids, 0, table_rows - 1)], jnp.zeros((), BF)
    )
    rows = lax.psum_scatter(looked, "dp", scatter_dimension=0, tiled=True)
    target_rows = rows[tokens:].astype(F32)
    segments = sentence_numbers[0]
    place_hot = (
        seg_positions(segments)[:, None]
        == jnp.arange(position_embedding.shape[0], dtype=jnp.int32)[None, :]
    ).astype(BF)
    hidden_rows = layer_norm(
        rows[:tokens].astype(F32)
        + jnp.dot(place_hot, position_embedding, preferred_element_type=F32),
        norm_gain_vector[0],
        norm_bias_vector[0],
    )
    seg_real = segments.astype(F32)
    seg_wide = jnp.broadcast_to(seg_real[:, None], (tokens, 128))
    seg_row = seg_real[None, :]
    place_row = label_positions
    place_col = jnp.broadcast_to(label_positions.reshape(labels, 1), (labels, 128))

    slice_rows = vocabulary_bias.shape[0]
    own_slice = lax.dynamic_slice_in_dim(embed, fsdp_index * slice_rows, slice_rows, 0)
    parts = [own_slice]
    dp_count = lax.axis_size("dp")
    for shift in range(1, dp_count):
        parts.append(
            lax.ppermute(own_slice, "dp", [(k, (k + shift) % dp_count) for k in range(dp_count)])
        )
    own_vocab = jnp.concatenate(parts, 0)
    all_bias = lax.all_gather(vocabulary_bias, BOTH, axis=0, tiled=True)
    own_bias = jnp.concatenate(
        [
            lax.dynamic_slice_in_dim(
                all_bias,
                ((dp_index - shift) % dp_count) * table_rows + fsdp_index * slice_rows,
                slice_rows,
                0,
            )
            for shift in range(dp_count)
        ]
    )
    bias_wide = jnp.broadcast_to(own_bias[:, None], (own_bias.shape[0], 128))
    target_bias = all_bias[label_target_token[0]]

    task_range = jnp.arange(TASKS, dtype=jnp.int32)
    task_hot = (sequence_task_index[:, None] == task_range[None, :]).astype(F32)
    counts = lax.psum(jnp.sum(task_hot, 0) * labels, BOTH)
    row_weight = jnp.sum(task_hot[0] * (task_loss_weight / jnp.maximum(counts, 1.0)))

    qkv, mid = project(hidden_rows, downs[0], in_weights[0], adapters[0], bias_of[0][0])
    context, logs = attend(qkv, seg_wide, seg_row)
    x_last, one, two, slope = after(
        context, hidden_rows, out_weights[0], *slabs[0], *bias_of[0][1:], norms_of[0]
    )
    *saved, features = last_forward(
        x_last, place_col, place_row, seg_wide, downs[1], in_weights[1], adapters[1], bias_of[1][0],
        out_weights[1], *slabs[1], *bias_of[1][1:], norms_of[1], head_full, head_dense_bias[None, :],
    )
    every = lax.all_gather(features, "fsdp", axis=0, tiled=True)
    means, local_logs = vocab(every, own_vocab, own_vocab.T, bias_wide, labels)
    local_logs = local_logs.reshape(-1, labels)
    all_logs = lax.all_gather(local_logs, "fsdp", axis=0, tiled=False)
    whole_logs = jax.nn.logsumexp(all_logs, axis=0)
    scaled = (means * jnp.exp(local_logs - whole_logs)[:, None, :]).astype(BF)
    mean_rows = lax.psum_scatter(scaled, "fsdp", scatter_dimension=0, tiled=True)[0]
    own_logs = lax.dynamic_index_in_dim(whole_logs, fsdp_index, 0, keepdims=False)
    targets = jnp.sum(features.astype(F32) * target_rows, 1) + target_bias
    own_loss = row_weight * jnp.sum(own_logs - targets)
    feat_grad = row_weight * (mean_rows.astype(F32).T - target_rows)

    hidden_grad, dense_gradient, gq_last, gv_last = last_backward(
        feat_grad, saved, place_col, place_row, seg_wide, downs[1], in_weights[1], adapters[1],
        out_weights[1], *slabs[1], norms_of[1], head_full, rank,
    )
    dctx = after_back(hidden_grad, one, two, slope, out_weights[0], *slabs[0], norms_of[0])
    gq_first, gv_first = attend_back(qkv, dctx, logs, seg_wide, seg_row, mid, rank)
    adapter_gradient = jnp.stack(
        [jnp.stack([gq_first, gv_first]), jnp.stack([gq_last, gv_last])]
    )
    adapter_portion, dense_portion = (
        lax.psum_scatter(adapter_gradient, BOTH, scatter_dimension=3, tiled=True),
        lax.psum_scatter(dense_gradient, BOTH, scatter_dimension=0, tiled=True),
    )
    squared_entries = jnp.sum(adapter_portion * adapter_portion) + jnp.sum(
        dense_portion * dense_portion
    )
    masked_task_loss, norm_square = lax.psum((own_loss, squared_entries), BOTH)
    gradient_norm = jnp.sqrt(norm_square)
    scale_factor = jnp.minimum(1.0, clip_limit / (gradient_norm + 1e-06))
    step_as_real = optimizer_step_count[0].astype(F32)
    adapter_new = optimizer_update(
        adapter_up_matrix,
        adapter_portion * scale_factor,
        adapter_moment_first,
        adapter_moment_second,
        step_as_real,
    )
    dense_new = optimizer_update(
        head_projection,
        dense_portion * scale_factor,
        head_moment_first,
        head_moment_second,
        step_as_real,
    )
    return (masked_task_loss, gradient_norm, *adapter_new, *dense_new)


def solution(mesh):
    rows = P(BOTH, None)
    in_specs = (
        rows,
        rows,
        rows,
        rows,
        P(BOTH),
        P(),
        P(),
        P("dp", None),
        P(),
        P(),
        P(),
        P(None, None, BOTH),
        P(None, None, BOTH),
        P(None, None, BOTH),
        P(None, BOTH, None),
        P(),
        P(),
        P(BOTH),
        P(),
        P(None, None, None, BOTH),
        P(None, None, None, BOTH),
        P(None, None, None, BOTH),
        rows,
        rows,
        rows,
    )
    adapter = P(None, None, None, BOTH)
    out_specs = (P(), P(), adapter, adapter, adapter, rows, rows, rows)
    return jax.shard_map(
        per_device, mesh=mesh, in_specs=in_specs, out_specs=out_specs, check_vma=False
    )
```

```python
import functools

import jax
import jax.numpy as jnp
from jax import lax
from jax.experimental import pallas as pl
from jax.experimental.pallas import tpu as pltpu
from jax.sharding import PartitionSpec as P

HEADS = 12
TASKS = 4
REACH = 128

norm_eps = 1e-05
adapter_scale = 2.0
clip_limit = 0.01
learn_rate = 0.05
beta_first = 0.9
beta_second = 0.999
adam_eps = 1e-08
decay_rate = 0.01
masked_score = -1e30

BF = jnp.bfloat16
F32 = jnp.float32
BOTH = ("dp", "fsdp")
VMEM_BYTES = 60 * 1024 * 1024


def mm(a, b):
    return lax.dot_general(a, b, (((1,), (0,)), ((), ())), preferred_element_type=F32)


def mm_nt(a, b):
    return lax.dot_general(a, b, (((1,), (1,)), ((), ())), preferred_element_type=F32)


def mm_tn(a, b):
    return lax.dot_general(a, b, (((0,), (0,)), ((), ())), preferred_element_type=F32)


def layer_norm(rows_in, gain, shift):
    center = rows_in - jnp.mean(rows_in, -1, keepdims=True)
    spread = jnp.mean(center * center, -1, keepdims=True)
    return center * lax.rsqrt(spread + norm_eps) * gain + shift


def norm_back(rows_in, gain, gradient):
    center = rows_in - jnp.mean(rows_in, -1, keepdims=True)
    inverse = lax.rsqrt(jnp.mean(center * center, -1, keepdims=True) + norm_eps)
    unit = center * inverse
    scaled = gradient * gain
    return inverse * (
        scaled
        - jnp.mean(scaled, -1, keepdims=True)
        - unit * jnp.mean(scaled * unit, -1, keepdims=True)
    )


def gelu_pair(v):
    size = jnp.abs(v) * 0.7071067811865476
    base = 1.0 + 0.3275911 * size
    t = pl.reciprocal(base, approx=True)
    t = t * (2.0 - base * t)
    bell = jnp.exp(-0.5 * v * v)
    poly = t * (
        0.127414796 + t * (-0.142248368 + t * (0.7107068705 + t * (-0.7265760135 + t * 0.5307027145)))
    )
    tail = poly * bell
    phi = jnp.where(v >= 0.0, 1.0 - tail, tail)
    return v * phi, phi + v * (bell * 0.3989422804014327)


def params(**more):
    return pltpu.CompilerParams(vmem_limit_bytes=VMEM_BYTES, **more)


def full(shape):
    return pl.BlockSpec(shape, lambda *_: (0,) * len(shape))


def split_of(total, most, step):
    size = (min(most, total) // step) * step
    while size > step and total % size:
        size -= step
    return size if size and total % size == 0 else total


def pair_rows(block, width):
    first = lax.broadcasted_iota(jnp.int32, block.shape, 1) < width
    return jnp.concatenate([jnp.where(first, block, 0.0), jnp.where(first, 0.0, block)], 0).astype(BF)


def pair_join(wide, width):
    rows = wide.shape[1] // 2
    return jnp.concatenate([wide[:width, :rows], wide[width:, rows:]], 0)


def masked(scores, same):
    rows = scores.shape[1] // 2
    return jnp.concatenate(
        [
            jnp.where(same, scores[:, :rows], masked_score),
            jnp.where(same, scores[:, rows:], masked_score),
        ],
        1,
    )


def project_body(x_ref, down_ref, w_ref, up_ref, bias_ref, out_ref, mid_ref):
    low = x_ref[...].astype(BF)
    mid = mm(low, down_ref[...]).astype(BF)
    mid_ref[...] = mid
    total = w_ref.shape[0]
    step = split_of(total, 768, 128)
    for start in range(0, total, step):
        part = slice(start, start + step)
        out_ref[:, part] = (
            mm_nt(low, w_ref[part, :]) + mm(mid, up_ref[:, part]) + bias_ref[:, part]
        ).astype(BF)


def project(x, down, w, up, bias):
    rows, width = x.shape
    tile = split_of(rows, 256, 16)
    total = w.shape[0]
    return pl.pallas_call(
        project_body,
        grid=(rows // tile,),
        in_specs=[
            pl.BlockSpec((tile, width), lambda i: (i, 0)),
            full(down.shape),
            full(w.shape),
            full(up.shape),
            full(bias.shape),
        ],
        out_specs=[
            pl.BlockSpec((tile, total), lambda i: (i, 0)),
            pl.BlockSpec((tile, down.shape[1]), lambda i: (i, 0)),
        ],
        out_shape=[
            jax.ShapeDtypeStruct((rows, total), BF),
            jax.ShapeDtypeStruct((rows, down.shape[1]), BF),
        ],
        compiler_params=params(),
        name="project",
    )(x, down, w, up, bias)


def attend_body(q_ref, k_ref, v_ref, seg_ref, seg_row_ref, ctx_ref, log_ref):
    rows = q_ref.shape[0]
    width = q_ref.shape[1] // 2
    scale = width**-0.5
    for start in range(0, rows, REACH):
        own = slice(start, start + REACH)
        near = slice(max(0, start - REACH), min(rows, start + 2 * REACH))
        queries = pair_rows(q_ref[own, :].astype(F32) * scale, width)
        same = seg_ref[near, :] == seg_row_ref[:, own]
        scores = masked(mm_nt(k_ref[near, :], queries), same)
        top = jnp.max(scores, 0, keepdims=True)
        weights = jnp.exp(scores - top)
        total = jnp.sum(weights, 0, keepdims=True)
        context = mm_tn(v_ref[near, :], weights.astype(BF)) * (1.0 / total)
        ctx_ref[own, :] = pair_join(context, width).T.astype(BF)
        log_ref[0, :, 2 * start : 2 * start + 2 * REACH] = top + jnp.log(total)


def attend(qkv, seg_wide, seg_row):
    rows, total = qkv.shape
    hidden = total // 3
    lanes = 2 * (hidden // HEADS)
    pairs = hidden // lanes
    column = lambda kind: pl.BlockSpec((rows, lanes), lambda p: (0, kind * pairs + p))
    return pl.pallas_call(
        attend_body,
        grid=(pairs,),
        in_specs=[column(0), column(1), column(2), full(seg_wide.shape), full(seg_row.shape)],
        out_specs=[
            pl.BlockSpec((rows, lanes), lambda p: (0, p)),
            pl.BlockSpec((1, 1, 2 * rows), lambda p: (p, 0, 0)),
        ],
        out_shape=[
            jax.ShapeDtypeStruct((rows, hidden), BF),
            jax.ShapeDtypeStruct((pairs, 1, 2 * rows), F32),
        ],
        compiler_params=params(),
        name="attend",
    )(qkv, qkv, qkv, seg_wide, seg_row)


def flat(ref):
    whole = ref[...]
    return whole.reshape(-1, whole.shape[-1])


def rows_of(ref, start, size):
    each = ref.shape[1]
    if size % each == 0 and start % each == 0 and each % 16 == 0:
        part = ref[start // each : (start + size) // each, :, :]
        return part.reshape(size, part.shape[-1])
    return flat(ref)[start : start + size, :]


def feed_step(ref):
    units = ref.shape[0] * ref.shape[1]
    step = ref.shape[1]
    while units % (2 * step) == 0 and 2 * step <= 768 and ref.shape[0] > 1:
        step *= 2
    return units, (step if ref.shape[0] > 1 else split_of(units, 768, 128))


def after_body(
    ctx_ref, x_ref, wo_ref, up_ref, down_ref, bo_ref, b1_ref, b2_ref, norm_ref,
    out_ref, one_ref, two_ref, slope_ref,
):
    one = x_ref[...] + (mm_nt(ctx_ref[...], wo_ref[...]) + bo_ref[...])
    one_ref[...] = one
    middle = layer_norm(one, norm_ref[0:1, :], norm_ref[1:2, :])
    low = middle.astype(BF)
    total = middle + b2_ref[...]
    units, step = feed_step(up_ref)
    for start in range(0, units, step):
        part = slice(start, start + step)
        act, slope = gelu_pair(mm_nt(low, rows_of(up_ref, start, step)) + b1_ref[:, part])
        slope_ref[:, part] = slope.astype(BF)
        total = total + mm(act.astype(BF), rows_of(down_ref, start, step))
    two_ref[...] = total
    out_ref[...] = layer_norm(total, norm_ref[2:3, :], norm_ref[3:4, :])


def slab_spec(slab):
    array, place, rows = slab
    return pl.BlockSpec((array.shape[0], rows, array.shape[2]), lambda *_: (0, place, 0))


def after(ctx, x, wo, up, down, bo, b1, b2, norms):
    rows, width = x.shape
    tile = split_of(rows, 256, 16)
    units = b1.shape[1]
    row = lambda n: pl.BlockSpec((tile, n), lambda i: (i, 0))
    return pl.pallas_call(
        after_body,
        grid=(rows // tile,),
        in_specs=[row(width), row(width), full(wo.shape), slab_spec(up), slab_spec(down)]
        + [full(a.shape) for a in (bo, b1, b2, norms)],
        out_specs=[row(width), row(width), row(width), row(units)],
        out_shape=[jax.ShapeDtypeStruct((rows, width), F32)] * 3
        + [jax.ShapeDtypeStruct((rows, units), BF)],
        compiler_params=params(),
        name="after",
    )(ctx, x, wo, up[0], down[0], bo, b1, b2, norms)


def exact_rows(choose, matrix):
    high = matrix.astype(BF)
    rest = matrix - high.astype(F32)
    middle = rest.astype(BF)
    low = (rest - middle.astype(F32)).astype(BF)
    return mm(choose, high) + mm(choose, middle) + mm(choose, low)


def last_forward_body(
    x_ref, place_ref, place_row_ref, seg_ref, down_ref, w_ref, adapt_ref, bias_ref, wo_ref, up_any, dn_any,
    bo_ref, b1_ref, b2_ref, norm_ref, hb_ref, hbias_ref,
    kv_ref, q_ref, mid_ref, log_ref, one_ref, slope_ref, two_ref, low_ref, act_ref, hslope_ref, feat_ref,
    up_ref, dn_ref, ctx_ref, sems, *, places,
):
    copies = []
    for k, (source, target, place) in enumerate(
        ((up_any, up_ref, places[0]), (dn_any, dn_ref, places[1]))
    ):
        rows = target.shape[1]
        copies.append(
            pltpu.make_async_copy(
                source.at[:, pl.ds(place * rows, rows), :], target, sems.at[k]
            )
        )
        copies[-1].start()
    rows, hidden = x_ref.shape
    labels = place_ref.shape[0]
    lanes = 2 * (hidden // HEADS)
    width = lanes // 2
    low = x_ref[...].astype(BF)
    mid = mm(low, down_ref[...]).astype(BF)
    mid_ref[...] = mid
    step = split_of(2 * hidden, 512, 128)
    for start in range(hidden, 3 * hidden, step):
        part = slice(start, start + step)
        kv_ref[:, start - hidden : start - hidden + step] = (
            mm_nt(low, w_ref[part, :]) + mm(mid, adapt_ref[:, part]) + bias_ref[:, part]
        ).astype(BF)
    choose = (
        lax.broadcasted_iota(jnp.int32, (labels, rows), 1) == place_ref[...][:, 0:1]
    ).astype(F32).astype(BF)
    own = exact_rows(choose, x_ref[...])
    own_low = own.astype(BF)
    own_mid = mm(choose, mid).astype(BF)
    q_ref[...] = (
        mm_nt(own_low, w_ref[:hidden, :]) + mm(own_mid, adapt_ref[:, :hidden]) + bias_ref[:, :hidden]
    ).astype(BF)
    seg = seg_ref[...]
    seg_own = jnp.sum(
        jnp.where(
            lax.broadcasted_iota(jnp.int32, (rows, labels), 0) == place_row_ref[...], seg, 0.0
        ),
        0,
        keepdims=True,
    )
    same = seg == seg_own
    for p in range(hidden // lanes):
        part = slice(p * lanes, (p + 1) * lanes)
        queries = pair_rows(q_ref[:, part].astype(F32) * width**-0.5, width)
        scores = masked(mm_nt(kv_ref[:, part], queries), same)
        top = jnp.max(scores, 0, keepdims=True)
        weights = jnp.exp(scores - top)
        total = jnp.sum(weights, 0, keepdims=True)
        context = mm_tn(
            kv_ref[:, hidden + p * lanes : hidden + (p + 1) * lanes], weights.astype(BF)
        ) * (1.0 / total)
        ctx_ref[:, part] = pair_join(context, width).T.astype(BF)
        log_ref[p : p + 1, :] = top + jnp.log(total)
    one = own + (mm_nt(ctx_ref[...], wo_ref[...]) + bo_ref[...])
    one_ref[...] = one
    middle = layer_norm(one, norm_ref[0:1, :], norm_ref[1:2, :])
    middle_low = middle.astype(BF)
    sum_two = middle + b2_ref[...]
    units, step = feed_step(up_ref)
    for copy in copies:
        copy.wait()
    for start in range(0, units, step):
        part = slice(start, start + step)
        act, slope = gelu_pair(mm_nt(middle_low, rows_of(up_ref, start, step)) + b1_ref[:, part])
        slope_ref[:, part] = slope.astype(BF)
        sum_two = sum_two + mm(act.astype(BF), rows_of(dn_ref, start, step))
    two_ref[...] = sum_two
    out_low = layer_norm(sum_two, norm_ref[2:3, :], norm_ref[3:4, :]).astype(BF)
    low_ref[...] = out_low
    act, slope = gelu_pair(mm(out_low, hb_ref[...]) + hbias_ref[...])
    act_ref[...] = act
    hslope_ref[...] = slope
    feat_ref[...] = layer_norm(act, norm_ref[4:5, :], norm_ref[5:6, :]).astype(BF)


def slab_scratch(slab):
    array, place, rows = slab
    return pltpu.VMEM((array.shape[0], rows, array.shape[2]), BF)


def last_forward(x, place_col, place_row, seg_wide, down, w, adapt, bias, wo, up, dn, bo, b1, b2, norms, hb, hbias):
    rows, hidden = x.shape
    labels = place_col.shape[0]
    units = b1.shape[1]
    whole = pl.BlockSpec(memory_space=pltpu.VMEM)
    anywhere = pl.BlockSpec(memory_space=pl.ANY)
    shape = jax.ShapeDtypeStruct
    pairs = HEADS // 2
    return pl.pallas_call(
        functools.partial(last_forward_body, places=(up[1], dn[1])),
        in_specs=[whole] * 9 + [anywhere] * 2 + [whole] * 6,
        out_specs=[whole] * 11,
        out_shape=[
            shape((rows, 2 * hidden), BF),
            shape((labels, hidden), BF),
            shape((rows, down.shape[1]), BF),
            shape((pairs, 2 * labels), F32),
            shape((labels, hidden), F32),
            shape((labels, units), BF),
            shape((labels, hidden), F32),
            shape((labels, hidden), BF),
            shape((labels, hidden), F32),
            shape((labels, hidden), F32),
            shape((labels, hidden), BF),
        ],
        scratch_shapes=[
            slab_scratch(up),
            slab_scratch(dn),
            pltpu.VMEM((labels, hidden), BF),
            pltpu.SemaphoreType.DMA((2,)),
        ],
        compiler_params=params(),
        name="last_forward",
    )(x, place_col, place_row, seg_wide, down, w, adapt, bias, wo, up[0], dn[0], bo, b1, b2, norms, hb, hbias)


def vocab_body(u_ref, e_ref, et_ref, bias_ref, num_ref, log_ref, scores, weights):
    count = e_ref.shape[0]
    step = split_of(count, 640, 16)
    u = u_ref[...]
    rows = u.shape[0]
    labels = num_ref.shape[2]
    top = jnp.full((1, rows), -jnp.inf, F32)
    for start in range(0, count, step):
        part = slice(start, start + step)
        bias = bias_ref[part, :]
        logits = mm_nt(e_ref[part, :], u) + jnp.concatenate([bias] * (rows // bias.shape[1]), 1)
        scores[part, :] = logits
        top = jnp.maximum(top, jnp.max(logits, 0, keepdims=True))
    total = jnp.zeros((1, rows), F32)
    for start in range(0, count, step):
        part = slice(start, start + step)
        grown = jnp.exp(scores[part, :] - top)
        total = total + jnp.sum(grown, 0, keepdims=True)
        weights[part, :] = grown.astype(BF)
    mean = mm(et_ref[...], weights[...]) * (1.0 / total)
    logs = top + jnp.log(total)
    for k in range(rows // labels):
        num_ref[k, :, :] = mean[:, k * labels : (k + 1) * labels]
        log_ref[k, :, :] = logs[:, k * labels : (k + 1) * labels]


def vocab(u, e, et, bias_wide, labels):
    rows, hidden = u.shape
    count = e.shape[0]
    tile = 2 * labels
    return pl.pallas_call(
        vocab_body,
        grid=(rows // tile,),
        in_specs=[
            pl.BlockSpec((tile, hidden), lambda i: (i, 0)),
            full(e.shape),
            full(et.shape),
            full(bias_wide.shape),
        ],
        out_specs=[
            pl.BlockSpec((2, hidden, labels), lambda i: (i, 0, 0)),
            pl.BlockSpec((2, 1, labels), lambda i: (i, 0, 0)),
        ],
        out_shape=[
            jax.ShapeDtypeStruct((rows // labels, hidden, labels), F32),
            jax.ShapeDtypeStruct((rows // labels, 1, labels), F32),
        ],
        scratch_shapes=[pltpu.VMEM((count, tile), F32), pltpu.VMEM((count, tile), BF)],
        compiler_params=params(),
        name="vocab",
    )(u, e, et, bias_wide)


def last_backward_body(
    du_ref, kv_ref, q_ref, mid_ref, log_ref, one_ref, slope_ref, two_ref, low_ref, act_ref, hslope_ref,
    place_ref, place_row_ref, seg_ref, down_ref, w_ref, adapt_ref, wo_ref, up_any, dn_any, norm_ref, hb_ref,
    dx_ref, gh_ref, gq_ref, gv_ref,
    up_ref, dn_ref, dkv_ref, dq_ref, sems, *, places, rank,
):
    copies = []
    for k, (source, target, place) in enumerate(
        ((up_any, up_ref, places[0]), (dn_any, dn_ref, places[1]))
    ):
        rows = target.shape[1]
        copies.append(
            pltpu.make_async_copy(
                source.at[:, pl.ds(place * rows, rows), :], target, sems.at[k]
            )
        )
        copies[-1].start()
    rows = kv_ref.shape[0]
    labels, hidden = du_ref.shape
    lanes = 2 * (hidden // HEADS)
    width = lanes // 2
    scale = width**-0.5
    dact = norm_back(act_ref[...], norm_ref[4:5, :], du_ref[...])
    dz = (hslope_ref[...] * dact).astype(BF)
    gh_ref[...] = mm_tn(low_ref[...], dz)
    dtwo = norm_back(two_ref[...], norm_ref[2:3, :], mm_nt(dz, hb_ref[...]))
    dtwo_low = dtwo.astype(BF)
    dmiddle = dtwo
    units, step = feed_step(up_ref)
    for copy in copies:
        copy.wait()
    for start in range(0, units, step):
        part = slice(start, start + step)
        dgate = (
            slope_ref[:, part].astype(F32) * mm_nt(dtwo_low, rows_of(dn_ref, start, step))
        ).astype(BF)
        dmiddle = dmiddle + mm(dgate, rows_of(up_ref, start, step))
    done = norm_back(one_ref[...], norm_ref[0:1, :], dmiddle)
    dctx = mm(done.astype(BF), wo_ref[...]).astype(BF)
    seg = seg_ref[...]
    choose_t = lax.broadcasted_iota(jnp.int32, (rows, labels), 0) == place_row_ref[...]
    same = seg == jnp.sum(jnp.where(choose_t, seg, 0.0), 0, keepdims=True)
    for p in range(hidden // lanes):
        part = slice(p * lanes, (p + 1) * lanes)
        later = slice(hidden + p * lanes, hidden + (p + 1) * lanes)
        queries = pair_rows(q_ref[:, part].astype(F32) * scale, width)
        outs = pair_rows(dctx[:, part].astype(F32), width)
        keys = kv_ref[:, part]
        weights = jnp.exp(masked(mm_nt(keys, queries), same) - log_ref[p : p + 1, :])
        dweights = mm_nt(kv_ref[:, later], outs)
        inner = jnp.sum(dweights * weights, 0, keepdims=True)
        dscores = (weights * (dweights - inner)).astype(BF)
        dkv_ref[:, part] = mm(dscores, queries).astype(BF)
        dkv_ref[:, later] = mm(weights.astype(BF), outs).astype(BF)
        dq_ref[:, part] = (pair_join(mm_tn(keys, dscores), width) * scale).T.astype(BF)
    dq = dq_ref[...]
    own_mid = mm(
        (lax.broadcasted_iota(jnp.int32, (labels, rows), 1) == place_ref[...][:, 0:1]).astype(F32).astype(BF),
        mid_ref[...],
    ).astype(BF)
    gq_ref[...] = adapter_scale * mm_tn(own_mid, dq)[:rank, :]
    gv_ref[...] = adapter_scale * mm_tn(mid_ref[...], dkv_ref[:, hidden:])[rank : 2 * rank, :]
    dmid_own = mm_nt(dq, adapt_ref[:, :hidden]).astype(BF)
    own = done + mm(dq, w_ref[:hidden, :]) + mm_nt(dmid_own, down_ref[...])
    spread = choose_t.astype(F32).astype(BF)
    own_high = own.astype(BF)
    own_rest = (own - own_high.astype(F32)).astype(BF)
    dmid = mm_nt(dkv_ref[:, hidden:], adapt_ref[:, 2 * hidden :]).astype(BF)
    step = split_of(hidden, 256, 128)
    for start in range(0, hidden, step):
        part = slice(start, start + step)
        dx_ref[:, part] = (
            mm(dkv_ref[...], w_ref[hidden:, part])
            + mm_nt(dmid, down_ref[part, :])
            + mm(spread, own_high[:, part])
            + mm(spread, own_rest[:, part])
        )


def last_backward(du, saved, place_col, place_row, seg_wide, down, w, adapt, wo, up, dn, norms, hb, rank):
    kv = saved[0]
    rows = kv.shape[0]
    labels, hidden = du.shape
    whole = pl.BlockSpec(memory_space=pltpu.VMEM)
    anywhere = pl.BlockSpec(memory_space=pl.ANY)
    shape = jax.ShapeDtypeStruct
    return pl.pallas_call(
        functools.partial(last_backward_body, places=(up[1], dn[1]), rank=rank),
        in_specs=[whole] * 18 + [anywhere] * 2 + [whole] * 2,
        out_specs=[whole] * 4,
        out_shape=[
            shape((rows, hidden), F32),
            shape((hidden, hidden), F32),
            shape((rank, hidden), F32),
            shape((rank, hidden), F32),
        ],
        scratch_shapes=[
            slab_scratch(up),
            slab_scratch(dn),
            pltpu.VMEM(kv.shape, BF),
            pltpu.VMEM((labels, hidden), BF),
            pltpu.SemaphoreType.DMA((2,)),
        ],
        compiler_params=params(),
        name="last_backward",
    )(du, *saved, place_col, place_row, seg_wide, down, w, adapt, wo, up[0], dn[0], norms, hb)


def after_back_sum_body(shards, *refs):
    *plain, parts, dctx_ref, sum_ref, got, sends, gets = refs
    step, last = pl.program_id(0), pl.num_programs(0) - 1
    me = number_of(position())

    @pl.when(step == 0)
    def _():
        greet_all(shards)
        got[me] = parts[me]

    @pl.when(step == jnp.minimum(1, last))
    def _():
        await_all(shards)
        spread(lambda peer: parts.at[peer], got, sends, gets, me, shards)

    after_back_body(*plain, dctx_ref)

    @pl.when(step == last)
    def _():
        collect(lambda peer: parts.at[peer], got, sends, gets, me, shards)
        total = got[0].astype(F32)
        for k in range(1, shards):
            total = total + got[k].astype(F32)
        sum_ref[...] = total


def after_back_body(dout_ref, one_ref, two_ref, slope_ref, wo_ref, up_ref, down_ref, norm_ref, dctx_ref):
    dtwo = norm_back(two_ref[...], norm_ref[2:3, :], dout_ref[...])
    low = dtwo.astype(BF)
    dmiddle = dtwo
    units, step = feed_step(up_ref)
    for start in range(0, units, step):
        part = slice(start, start + step)
        dgate = (
            slope_ref[:, part].astype(F32) * mm_nt(low, rows_of(down_ref, start, step))
        ).astype(BF)
        dmiddle = dmiddle + mm(dgate, rows_of(up_ref, start, step))
    done = norm_back(one_ref[...], norm_ref[0:1, :], dmiddle)
    dctx_ref[...] = mm(done.astype(BF), wo_ref[...]).astype(BF)


def after_back_sum(dout, one, two, slope, wo, up, down, norms, parts, shards):
    rows, width = dout.shape
    tile = split_of(rows, 256, 16)
    row = lambda n: pl.BlockSpec((tile, n), lambda i: (i, 0))
    sems = pltpu.SemaphoreType.DMA
    return pl.pallas_call(
        functools.partial(after_back_sum_body, shards),
        grid=(rows // tile,),
        in_specs=[row(width), row(width), row(width), row(slope.shape[1]), full(wo.shape)]
        + [slab_spec(up), slab_spec(down), full(norms.shape), full(parts.shape)],
        out_specs=[row(width), full(parts.shape[1:])],
        out_shape=[
            jax.ShapeDtypeStruct((rows, width), BF),
            jax.ShapeDtypeStruct(parts.shape[1:], F32),
        ],
        scratch_shapes=[pltpu.VMEM(parts.shape, BF), sems((shards,)), sems((shards,))],
        compiler_params=params(collective_id=3, has_side_effects=True),
        name="after_back_sum",
    )(dout, one, two, slope, wo, up[0], down[0], norms, parts)


def after_back(dout, one, two, slope, wo, up, down, norms):
    rows, width = dout.shape
    tile = split_of(rows, 256, 16)
    row = lambda n: pl.BlockSpec((tile, n), lambda i: (i, 0))
    return pl.pallas_call(
        after_back_body,
        grid=(rows // tile,),
        in_specs=[row(width), row(width), row(width), row(slope.shape[1]), full(wo.shape)]
        + [slab_spec(up), slab_spec(down), full(norms.shape)],
        out_specs=row(width),
        out_shape=jax.ShapeDtypeStruct((rows, width), BF),
        compiler_params=params(),
        name="after_back",
    )(dout, one, two, slope, wo, up[0], down[0], norms)


def attend_back_body(
    q_ref, k_ref, v_ref, dctx_ref, log_ref, seg_ref, seg_row_ref, mid_ref, gq_ref, gv_ref, dv_ref
):
    rows = q_ref.shape[0]
    width = q_ref.shape[1] // 2
    scale = width**-0.5
    rank = gq_ref.shape[0]
    dv_ref[...] = jnp.zeros_like(dv_ref)
    gq = jnp.zeros((2 * width, mid_ref.shape[1]), F32)
    for start in range(0, rows, REACH):
        own = slice(start, start + REACH)
        near = slice(max(0, start - REACH), min(rows, start + 2 * REACH))
        queries = pair_rows(q_ref[own, :].astype(F32) * scale, width)
        outs = pair_rows(dctx_ref[own, :].astype(F32), width)
        same = seg_ref[near, :] == seg_row_ref[:, own]
        keys = k_ref[near, :]
        logs = log_ref[0, :, 2 * start : 2 * start + 2 * REACH]
        weights = jnp.exp(masked(mm_nt(keys, queries), same) - logs)
        dweights = mm_nt(v_ref[near, :], outs)
        inner = jnp.sum(dweights * weights, 0, keepdims=True)
        dscores = (weights * (dweights - inner)).astype(BF)
        dv_ref[near, :] += mm(weights.astype(BF), outs)
        dq = (pair_join(mm_tn(keys, dscores), width) * scale).astype(BF)
        gq = gq + mm(dq, mid_ref[own, :])
    gq_ref[...] = adapter_scale * gq.T[:rank, :]
    gv_ref[...] = adapter_scale * mm_tn(mid_ref[...], dv_ref[...].astype(BF))[rank : 2 * rank, :]


def attend_back(qkv, dctx, logs, seg_wide, seg_row, mid, rank):
    rows, total = qkv.shape
    hidden = total // 3
    lanes = 2 * (hidden // HEADS)
    pairs = hidden // lanes
    column = lambda kind: pl.BlockSpec((rows, lanes), lambda p: (0, kind * pairs + p))
    return pl.pallas_call(
        attend_back_body,
        grid=(pairs,),
        in_specs=[
            column(0),
            column(1),
            column(2),
            column(0),
            pl.BlockSpec((1, 1, 2 * rows), lambda p: (p, 0, 0)),
            full(seg_wide.shape),
            full(seg_row.shape),
            full(mid.shape),
        ],
        out_specs=[pl.BlockSpec((rank, lanes), lambda p: (0, p))] * 2,
        out_shape=[jax.ShapeDtypeStruct((rank, hidden), F32)] * 2,
        scratch_shapes=[pltpu.VMEM((rows, lanes), F32)],
        compiler_params=params(),
        name="attend_back",
    )(qkv, qkv, qkv, dctx, logs, seg_wide, seg_row, mid)


MESH = pl.DeviceIdType.MESH
LINES = {"x": 2, "z": 4, "y": 2}


def position():
    dp, fsdp = lax.axis_index("dp"), lax.axis_index("fsdp")
    return {"x": dp, "z": fsdp // 4, "y": (fsdp // 2) % 2, "c": fsdp % 2}


def device_of(place):
    return (place["x"], (place["z"] * 2 + place["y"]) * 2 + place["c"])


def number_of(place):
    return place["x"] * 16 + (place["z"] * 2 + place["y"]) * 2 + place["c"]


def rank_device(number):
    return (number // 16, number % 16)


def greet_all(shards):
    barrier = pltpu.get_barrier_semaphore()
    me = lax.axis_index("dp") * 16 + lax.axis_index("fsdp")

    @pl.loop(1, shards)
    def _(k):
        pl.semaphore_signal(
            barrier, inc=1, device_id=rank_device((me + k) % shards), device_id_type=MESH
        )


def await_all(shards):
    pl.semaphore_wait(pltpu.get_barrier_semaphore(), shards - 1)


def direct_copy(source, target, sends, receives, me, k, shards):
    return pltpu.make_async_remote_copy(
        src_ref=source,
        dst_ref=target,
        send_sem=sends.at[k],
        recv_sem=receives.at[me],
        device_id=rank_device((me + k) % shards),
        device_id_type=MESH,
    )


def spread(piece_of, buffer, sends, receives, me, shards):
    @pl.loop(1, shards)
    def _(k):
        direct_copy(piece_of((me + k) % shards), buffer.at[me], sends, receives, me, k, shards).start()


def collect(piece_of, buffer, sends, receives, me, shards):
    @pl.loop(1, shards)
    def _(k):
        source = (me + shards - k) % shards
        direct_copy(buffer.at[source], buffer.at[source], sends, receives, source, k, shards).wait_recv()

    @pl.loop(1, shards)
    def _(k):
        direct_copy(piece_of((me + k) % shards), buffer.at[me], sends, receives, me, k, shards).wait_send()


def relative_places(order):
    places = [
        {"x": dx, "z": dz, "y": dy} for dx in (0, 1) for dz in range(-3, 4) for dy in (0, 1)
    ]
    return sorted(places, key=lambda p: (abs(p["x"]) + abs(p["z"]) + abs(p["y"]), [abs(p[a]) for a in order]))


class Gather:
    def __init__(self, chunk, full_buffer, start, rows, order, sends, receives, hands, hands_got):
        self.chunk, self.full, self.order = chunk, full_buffer, order
        self.part = pl.ds(start, rows)
        self.sends, self.receives, self.hands, self.hands_got = sends, receives, hands, hands_got
        self.here = position()
        self.items = relative_places(order)
        self.pending = []

    def origin(self, item):
        here = self.here
        return {"x": (here["x"] + item["x"]) % 2, "z": here["z"] - item["z"], "y": (here["y"] + item["y"]) % 2, "c": here["c"]}

    def key(self, place):
        return (place["x"] * 4 + place["z"]) * 2 + place["y"]

    def outward(self, item):
        deepest = max([k for k, axis in enumerate(self.order) if item[axis]], default=-1)
        ways = []
        if deepest >= 0 and self.order[deepest] == "z":
            ways.append(("z", 1 if item["z"] > 0 else -1))
        for axis in self.order[deepest + 1 :]:
            ways += [("z", 1), ("z", -1)] if axis == "z" else [(axis, 1)]
        return ways

    def copy(self, index, way, slot, item):
        here = self.here
        place = self.origin(item)
        number, key = number_of(place), self.key(place)
        mine = not any(item.values())
        source = self.chunk.at[self.part, :] if mine else self.full.at[number, self.part, :]
        if way is None:
            target = dict(here, c=1 - here["c"])
            sends, receives = self.hands.at[index], self.hands_got.at[key]
        else:
            axis, step = way
            target = dict(here)
            target[axis] = here["z"] + step if axis == "z" else 1 - here[axis]
            sends, receives = self.sends.at[index * 4 + slot], self.receives.at[key]
        return pltpu.make_async_remote_copy(
            src_ref=source,
            dst_ref=self.full.at[number, self.part, :],
            send_sem=sends,
            recv_sem=receives,
            device_id=device_of(target),
            device_id_type=MESH,
        )

    def valid(self, item):
        z = self.here["z"] - item["z"]
        return (z >= 0) & (z <= 3)

    def step(self, index):
        item = self.items[index]

        @pl.when(self.valid(item))
        def _():
            if any(item.values()):
                self.arrived(index, item)
            for slot, way in enumerate(self.outward(item)):
                self.when_way(way, lambda way=way, slot=slot: self.copy(index, way, slot, item).start())
            self.copy(index, None, 0, item).start()

    def when_way(self, way, act):
        axis, step = way
        if axis == "z":
            z = self.here["z"] + step
            pl.when((z >= 0) & (z <= 3))(act)
        else:
            act()

    def arrived(self, index, item):
        place = self.origin(item)
        spot = self.full.at[number_of(place), self.part, :]
        pltpu.make_async_remote_copy(
            src_ref=spot,
            dst_ref=spot,
            send_sem=self.sends.at[index * 4],
            recv_sem=self.receives.at[self.key(place)],
            device_id=device_of(dict(self.here, c=1 - self.here["c"])),
            device_id_type=MESH,
        ).wait_recv()

    def finish(self):
        for index, item in enumerate(self.items):

            @pl.when(self.valid(item))
            def _(index=index, item=item):
                for slot, way in enumerate(self.outward(item)):
                    self.when_way(way, lambda way=way, slot=slot: self.copy(index, way, slot, item).wait_send())
                self.copy(index, None, 0, item).wait_send()
                place = dict(self.origin(item), c=1 - self.here["c"])
                spot = self.full.at[number_of(place), self.part, :]
                pltpu.make_async_remote_copy(
                    src_ref=spot,
                    dst_ref=spot,
                    send_sem=self.hands.at[index],
                    recv_sem=self.hands_got.at[self.key(place)],
                    device_id=device_of(dict(self.here, c=1 - self.here["c"])),
                    device_id_type=MESH,
                ).wait_recv()


ITEMS = 28


def start_body(
    streams, shards, chunk, rows, note, bias, full_chunk, got, notes, biases,
    sends, receives, hands, hands_got, row_sems, note_sends, note_gets, bias_sends, bias_gets, own_sems,
):
    here = position()
    me = number_of(here)
    greet_all(shards)
    own = pltpu.make_async_copy(chunk, full_chunk.at[me], own_sems.at[0])
    own.start()
    own_note = pltpu.make_async_copy(note, notes.at[me], own_sems.at[1])
    own_note.start()
    own_bias = pltpu.make_async_copy(bias, biases.at[me], own_sems.at[2])
    own_bias.start()
    await_all(shards)
    gathers = [
        Gather(
            chunk, full_chunk, start, size, order, sends.at[k], receives.at[k], hands.at[k], hands_got.at[k]
        )
        for k, (start, size, order) in enumerate(streams)
    ]
    across = pltpu.make_async_remote_copy(
        src_ref=rows,
        dst_ref=got,
        send_sem=row_sems.at[0],
        recv_sem=row_sems.at[1],
        device_id=device_of(dict(here, x=1 - here["x"])),
        device_id_type=MESH,
    )
    for gather in gathers:
        gather.step(0)
    spread(lambda peer: note, notes, note_sends, note_gets, me, shards)
    spread(lambda peer: bias, biases, bias_sends, bias_gets, me, shards)
    across.start()
    for index in range(1, ITEMS):
        for gather in gathers:
            gather.step(index)
    for gather in gathers:
        gather.finish()
    collect(lambda peer: note, notes, note_sends, note_gets, me, shards)
    collect(lambda peer: bias, biases, bias_sends, bias_gets, me, shards)
    across.wait()
    own.wait()
    own_note.wait()
    own_bias.wait()


def start_exchange(chunk, rows, note, bias, shards):
    anywhere = pl.BlockSpec(memory_space=pl.ANY)
    cut = (chunk.shape[0] * 5 // 6 + 15) // 16 * 16
    streams = ((0, cut, "xzy"), (cut, chunk.shape[0] - cut, "xyz"))
    shape = jax.ShapeDtypeStruct
    sems = pltpu.SemaphoreType.DMA
    return pl.pallas_call(
        functools.partial(start_body, streams, shards),
        in_specs=[anywhere] * 4,
        out_specs=[anywhere] * 4,
        out_shape=[
            shape((shards, *chunk.shape), chunk.dtype),
            shape(rows.shape, rows.dtype),
            shape((shards, *note.shape), note.dtype),
            shape((shards, *bias.shape), bias.dtype),
        ],
        scratch_shapes=[
            sems((2, 4 * ITEMS)),
            sems((2, 16)),
            sems((2, ITEMS)),
            sems((2, 16)),
            sems((2,)),
            sems((shards,)),
            sems((shards,)),
            sems((shards,)),
            sems((shards,)),
            sems((3,)),
        ],
        compiler_params=params(collective_id=1, has_side_effects=True),
        name="start_exchange",
    )(chunk, rows, note, bias)


def tail_body(shards, parts, dense, loss, total_ref, sums_ref, got, note, notes, send_a, get_a, send_b, get_b):
    me = number_of(position())
    greet_all(shards)
    got[me] = parts[me]
    await_all(shards)
    spread(lambda peer: parts.at[peer], got, send_a, get_a, me, shards)
    dense_square = jnp.sum(dense[...] * dense[...], keepdims=True)
    collect(lambda peer: parts.at[peer], got, send_a, get_a, me, shards)
    total = got[0]
    for k in range(1, shards):
        total = total + got[k]
    total_ref[...] = total
    square = dense_square + jnp.sum(total * total, keepdims=True)
    row = lax.broadcasted_iota(jnp.int32, note.shape, 0)
    note[...] = jnp.where(row == 0, loss[...], jnp.where(row == 1, square, 0.0))
    notes[me] = note[...]
    spread(lambda peer: note, notes, send_b, get_b, me, shards)
    collect(lambda peer: note, notes, send_b, get_b, me, shards)
    total = notes[0]
    for k in range(1, shards):
        total = total + notes[k]
    sums_ref[...] = total


def tail(parts, dense, loss, shards):
    whole = pl.BlockSpec(memory_space=pltpu.VMEM)
    block = parts.shape[1:]
    shape = jax.ShapeDtypeStruct
    sems = pltpu.SemaphoreType.DMA
    return pl.pallas_call(
        functools.partial(tail_body, shards),
        in_specs=[whole] * 3,
        out_specs=[whole] * 2,
        out_shape=[shape(block, F32), shape((8, 128), F32)],
        scratch_shapes=[
            pltpu.VMEM(parts.shape, F32),
            pltpu.VMEM((8, 128), F32),
            pltpu.VMEM((shards, 8, 128), F32),
        ]
        + [sems((shards,))] * 4,
        compiler_params=params(collective_id=2, has_side_effects=True),
        name="tail",
    )(parts, dense, loss)


def seg_positions(segments):
    index = jnp.arange(segments.shape[-1], dtype=jnp.int32)
    fresh = jnp.concatenate([jnp.ones((1,), dtype=bool), segments[1:] != segments[:-1]], -1)
    starts = lax.cummax(jnp.where(fresh, index, jnp.zeros_like(index)), axis=0)
    return index - starts


def optimizer_update(weight, gradient, moment_one, moment_two, step_as_real):
    moment_one = beta_first * moment_one + (1.0 - beta_first) * gradient
    moment_two = beta_second * moment_two + (1.0 - beta_second) * gradient * gradient
    one_hat = moment_one / (1.0 - beta_first**step_as_real)
    two_hat = moment_two / (1.0 - beta_second**step_as_real)
    weight = weight - learn_rate * (one_hat / (jnp.sqrt(two_hat) + adam_eps) + decay_rate * weight)
    return (weight, moment_one, moment_two)


def pad_rows(matrix, multiple):
    return jnp.pad(matrix, ((0, -matrix.shape[0] % multiple), (0, 0)))


def slab_of(gathered, start, rows):
    if rows % 16 == 0 and start % rows == 0:
        return (gathered, start // rows, rows)
    part = gathered[:, start : start + rows].reshape(1, -1, gathered.shape[2])
    return (part, 0, part.shape[1])


def per_device(
    input_token_index,
    sentence_numbers,
    label_positions,
    label_target_token,
    sequence_task_index,
    task_loss_weight,
    optimizer_step_count,
    embed,
    position_embedding,
    norm_gain_vector,
    norm_bias_vector,
    attention_in_weight,
    attention_out_weight,
    feedforward_up,
    feedforward_down,
    layer_bias_vector,
    head_dense_bias,
    vocabulary_bias,
    adapter_down_matrix,
    adapter_up_matrix,
    adapter_moment_first,
    adapter_moment_second,
    head_projection,
    head_moment_first,
    head_moment_second,
):
    shards = lax.axis_size("dp") * lax.axis_size("fsdp")
    dp_index = lax.axis_index("dp")
    fsdp_index = lax.axis_index("fsdp")
    layers, unused, rank, up_part = adapter_up_matrix.shape
    hidden = embed.shape[1]
    tokens = input_token_index.shape[1]
    labels = label_positions.shape[1]
    qkv_rows = attention_in_weight.shape[2]
    out_rows = attention_out_weight.shape[2]
    ff_rows = feedforward_up.shape[2]
    head_rows = head_projection.shape[0]

    grouped = (lax.axis_size("dp"), lax.axis_size("fsdp")) == (2, 16)
    chunks = [
        [
            feedforward_up[layer].T,
            feedforward_down[layer],
            attention_in_weight[layer].T,
            attention_out_weight[layer].T,
        ]
        for layer in range(layers)
    ]
    ups = adapter_up_matrix.astype(BF).reshape(-1)
    up_rows = -(-ups.size // hidden)
    chunks[0] += [
        head_projection.astype(BF),
        jnp.pad(ups, (0, up_rows * hidden - ups.size)).reshape(up_rows, hidden),
    ]
    chunks = [pad_rows(jnp.concatenate(pieces, 0), 32) for pieces in chunks]

    table_rows = embed.shape[0]
    wanted = jnp.concatenate([input_token_index[0], label_target_token[0]])
    dp_count = lax.axis_size("dp")
    group_ids = lax.all_gather(wanted, "dp", axis=0, tiled=False) - dp_index * table_rows
    later_full = [lax.all_gather(chunk, BOTH, axis=0, tiled=False) for chunk in chunks[1:]]

    def look(ids):
        inside = (ids >= 0) & (ids < table_rows)
        found = embed[jnp.clip(ids, 0, table_rows - 1)]
        return jnp.where(inside[:, None], found, jnp.zeros((), BF)), inside

    task_range = jnp.arange(TASKS, dtype=jnp.int32)
    slice_rows = vocabulary_bias.shape[0]
    if grouped:
        pair_ids = jnp.concatenate(
            [
                lax.dynamic_index_in_dim(group_ids, 1 - dp_index, 0, keepdims=False),
                lax.dynamic_index_in_dim(group_ids, dp_index, 0, keepdims=False),
            ]
        )
        looked, inside = look(pair_ids)
        note = jnp.broadcast_to(sequence_task_index.astype(F32)[:, None], (8, 128))
        bias_rows = -(-slice_rows // 1024) * 8
        bias_block = jnp.pad(vocabulary_bias, (0, bias_rows * 128 - slice_rows)).reshape(bias_rows, 128)
        first_full, got, notes, biases = start_exchange(
            chunks[0], looked[: wanted.size], note, bias_block, shards
        )
        rows = jnp.where(inside[wanted.size :, None], looked[wanted.size :], got)
        every_task = notes[:, 0, 0].astype(jnp.int32)
        all_bias = biases.reshape(shards, -1)[:, :slice_rows].reshape(-1)
    else:
        looked, inside = look(group_ids.reshape(-1))
        first_full = lax.all_gather(chunks[0], BOTH, axis=0, tiled=False)
        rows = lax.psum_scatter(looked, "dp", scatter_dimension=0, tiled=True)
        every_task = lax.all_gather(sequence_task_index, BOTH, axis=0, tiled=True)
        all_bias = lax.all_gather(vocabulary_bias, BOTH, axis=0, tiled=True)
    counts = labels * jnp.sum((every_task[:, None] == task_range[None, :]).astype(F32), 0)
    task_hot = (sequence_task_index[:, None] == task_range[None, :]).astype(F32)
    row_weight = jnp.sum(task_hot[0] * (task_loss_weight / jnp.maximum(counts, 1.0)))

    gathered = [first_full, *later_full]
    slabs = [
        (slab_of(gathered[layer], 0, ff_rows), slab_of(gathered[layer], ff_rows, ff_rows))
        for layer in range(layers)
    ]
    in_weights, out_weights = [], []
    for layer in range(layers):
        at = 2 * ff_rows
        in_weights.append(gathered[layer][:, at : at + qkv_rows].reshape(-1, hidden))
        at += qkv_rows
        out_weights.append(gathered[layer][:, at : at + out_rows].reshape(-1, hidden))
    at = 2 * ff_rows + qkv_rows + out_rows
    head_full = first_full[:, at : at + head_rows].reshape(-1, hidden)
    at += head_rows
    ups_full = (
        first_full[:, at : at + up_rows]
        .reshape(shards, -1)[:, : ups.size]
        .reshape(shards, layers, 2, rank, up_part)
        .transpose(1, 2, 3, 0, 4)
        .reshape(layers, 2, rank, hidden)
    )
    adapters = [
        jnp.zeros((128, 3 * hidden), BF)
        .at[:rank, :hidden]
        .set(2 * ups_full[layer, 0])
        .at[rank : 2 * rank, 2 * hidden :]
        .set(2 * ups_full[layer, 1])
        for layer in range(layers)
    ]
    downs = [
        jnp.zeros((hidden, 128), BF)
        .at[:, :rank]
        .set(adapter_down_matrix[layer, 0])
        .at[:, rank : 2 * rank]
        .set(adapter_down_matrix[layer, 1])
        for layer in range(layers)
    ]
    bias_of = []
    for layer in range(layers):
        b = layer_bias_vector[layer][None, :]
        ff = b.shape[1] - 4 * hidden
        bias_of.append(
            (
                jnp.concatenate(
                    [b[:, :hidden], jnp.zeros((1, hidden), F32), b[:, hidden : 2 * hidden]], 1
                ),
                b[:, 2 * hidden : 3 * hidden],
                b[:, 3 * hidden : 3 * hidden + ff],
                b[:, 3 * hidden + ff :],
            )
        )
    norms_of = [
        jnp.concatenate(
            [
                norm_gain_vector[1 + 2 * layer][None],
                norm_bias_vector[1 + 2 * layer][None],
                norm_gain_vector[2 + 2 * layer][None],
                norm_bias_vector[2 + 2 * layer][None],
                norm_gain_vector[-1][None],
                norm_bias_vector[-1][None],
            ],
            0,
        )
        for layer in range(layers)
    ]

    target_rows = rows[tokens:].astype(F32)
    segments = sentence_numbers[0]
    place_hot = (
        seg_positions(segments)[:, None]
        == jnp.arange(position_embedding.shape[0], dtype=jnp.int32)[None, :]
    ).astype(BF)
    hidden_rows = layer_norm(
        rows[:tokens].astype(F32)
        + jnp.dot(place_hot, position_embedding, preferred_element_type=F32),
        norm_gain_vector[0],
        norm_bias_vector[0],
    )
    seg_real = segments.astype(F32)
    seg_wide = jnp.broadcast_to(seg_real[:, None], (tokens, 128))
    seg_row = seg_real[None, :]
    place_row = label_positions
    place_col = jnp.broadcast_to(label_positions.reshape(labels, 1), (labels, 128))

    own_slice = lax.dynamic_slice_in_dim(embed, fsdp_index * slice_rows, slice_rows, 0)
    own_vocab = lax.all_gather(own_slice, "dp", axis=0, tiled=True)
    own_bias = jnp.concatenate(
        [
            lax.dynamic_slice_in_dim(
                all_bias, part * table_rows + fsdp_index * slice_rows, slice_rows, 0
            )
            for part in range(dp_count)
        ]
    )
    bias_wide = jnp.broadcast_to(own_bias[:, None], (own_bias.shape[0], 128))
    target_bias = all_bias[label_target_token[0]]

    qkv, mid = project(hidden_rows, downs[0], in_weights[0], adapters[0], bias_of[0][0])
    context, logs = attend(qkv, seg_wide, seg_row)
    x_last, one, two, slope = after(
        context, hidden_rows, out_weights[0], *slabs[0], *bias_of[0][1:], norms_of[0]
    )
    *saved, features = last_forward(
        x_last, place_col, place_row, seg_wide, downs[1], in_weights[1], adapters[1], bias_of[1][0],
        out_weights[1], *slabs[1], *bias_of[1][1:], norms_of[1], head_full, head_dense_bias[None, :],
    )
    every = lax.all_gather(features, "fsdp", axis=0, tiled=True)
    means, local_logs = vocab(every, own_vocab, own_vocab.T, bias_wide, labels)
    local_logs = local_logs.reshape(-1, labels)
    all_logs = lax.all_gather(local_logs, "fsdp", axis=0, tiled=False)
    whole_logs = jax.nn.logsumexp(all_logs, axis=0)
    scaled = (means * jnp.exp(local_logs - whole_logs)[:, None, :]).astype(BF)
    mean_rows = lax.psum_scatter(scaled, "fsdp", scatter_dimension=0, tiled=True)[0]
    own_logs = lax.dynamic_index_in_dim(whole_logs, fsdp_index, 0, keepdims=False)
    targets = jnp.sum(features.astype(F32) * target_rows, 1) + target_bias
    own_loss = row_weight * jnp.sum(own_logs - targets)
    feat_grad = row_weight * (mean_rows.astype(F32).T - target_rows)

    hidden_grad, dense_gradient, gq_last, gv_last = last_backward(
        feat_grad, saved, place_col, place_row, seg_wide, downs[1], in_weights[1], adapters[1],
        out_weights[1], *slabs[1], norms_of[1], head_full, rank,
    )
    back = (hidden_grad, one, two, slope, out_weights[0], *slabs[0], norms_of[0])
    if grouped:
        block = -(-head_rows * hidden // 2048) * 2048
        dense_parts = jnp.pad(
            dense_gradient.reshape(shards, -1).astype(BF), ((0, 0), (0, block - head_rows * hidden))
        ).reshape(shards, 16, block // 16)
        dctx, dense_sum = after_back_sum(*back, dense_parts, shards)
        dense_portion = dense_sum.reshape(-1)[: head_rows * hidden].reshape(head_rows, hidden)
    else:
        dctx = after_back(*back)
        dense_portion = lax.psum_scatter(dense_gradient, BOTH, scatter_dimension=0, tiled=True)
    gq_first, gv_first = attend_back(qkv, dctx, logs, seg_wide, seg_row, mid, rank)
    adapter_gradient = jnp.stack([gq_first, gv_first, gq_last, gv_last]).reshape(layers, 2, rank, hidden)
    if grouped:
        parts = adapter_gradient.reshape(-1, shards, up_part).transpose(1, 0, 2).reshape(shards, -1)
        block = -(-ups.size // 1024) * 1024
        parts = jnp.pad(parts, ((0, 0), (0, block - ups.size))).reshape(shards, block // 128, 128)
        own_parts, sums = tail(parts, dense_portion, jnp.broadcast_to(own_loss, (8, 128)), shards)
        adapter_portion = own_parts.reshape(-1)[: ups.size].reshape(adapter_up_matrix.shape)
        masked_task_loss, norm_square = sums[0, 0], sums[1, 0]
    else:
        adapter_portion = lax.psum_scatter(adapter_gradient, BOTH, scatter_dimension=3, tiled=True)
        squared_entries = jnp.sum(adapter_portion * adapter_portion) + jnp.sum(
            dense_portion * dense_portion
        )
        masked_task_loss, norm_square = lax.psum((own_loss, squared_entries), BOTH)
    gradient_norm = jnp.sqrt(norm_square)
    scale_factor = jnp.minimum(1.0, clip_limit / (gradient_norm + 1e-06))
    step_as_real = optimizer_step_count[0].astype(F32)
    adapter_new = optimizer_update(
        adapter_up_matrix,
        adapter_portion * scale_factor,
        adapter_moment_first,
        adapter_moment_second,
        step_as_real,
    )
    dense_new = optimizer_update(
        head_projection,
        dense_portion * scale_factor,
        head_moment_first,
        head_moment_second,
        step_as_real,
    )
    return (masked_task_loss, gradient_norm, *adapter_new, *dense_new)


def solution(mesh):
    rows = P(BOTH, None)
    in_specs = (
        rows,
        rows,
        rows,
        rows,
        P(BOTH),
        P(),
        P(),
        P("dp", None),
        P(),
        P(),
        P(),
        P(None, None, BOTH),
        P(None, None, BOTH),
        P(None, None, BOTH),
        P(None, BOTH, None),
        P(),
        P(),
        P(BOTH),
        P(),
        P(None, None, None, BOTH),
        P(None, None, None, BOTH),
        P(None, None, None, BOTH),
        rows,
        rows,
        rows,
    )
    adapter = P(None, None, None, BOTH)
    out_specs = (P(), P(), adapter, adapter, adapter, rows, rows, rows)
    return jax.shard_map(
        per_device, mesh=mesh, in_specs=in_specs, out_specs=out_specs, check_vma=False
    )
```

```python
import functools

import jax
import jax.numpy as jnp
from jax import lax
from jax.experimental import pallas as pl
from jax.experimental.pallas import tpu as pltpu
from jax.sharding import PartitionSpec as P

HEADS = 12
TASKS = 4
REACH = 128

norm_eps = 1e-05
adapter_scale = 2.0
clip_limit = 0.01
learn_rate = 0.05
beta_first = 0.9
beta_second = 0.999
adam_eps = 1e-08
decay_rate = 0.01
masked_score = -1e30

BF = jnp.bfloat16
F32 = jnp.float32
BOTH = ("dp", "fsdp")
VMEM_BYTES = 60 * 1024 * 1024


def mm(a, b):
    return lax.dot_general(a, b, (((1,), (0,)), ((), ())), preferred_element_type=F32)


def mm_nt(a, b):
    return lax.dot_general(a, b, (((1,), (1,)), ((), ())), preferred_element_type=F32)


def mm_tn(a, b):
    return lax.dot_general(a, b, (((0,), (0,)), ((), ())), preferred_element_type=F32)


def layer_norm(rows_in, gain, shift):
    center = rows_in - jnp.mean(rows_in, -1, keepdims=True)
    spread = jnp.mean(center * center, -1, keepdims=True)
    return center * lax.rsqrt(spread + norm_eps) * gain + shift


def norm_back(rows_in, gain, gradient):
    center = rows_in - jnp.mean(rows_in, -1, keepdims=True)
    inverse = lax.rsqrt(jnp.mean(center * center, -1, keepdims=True) + norm_eps)
    unit = center * inverse
    scaled = gradient * gain
    return inverse * (
        scaled
        - jnp.mean(scaled, -1, keepdims=True)
        - unit * jnp.mean(scaled * unit, -1, keepdims=True)
    )


def gelu_pair(v):
    size = jnp.abs(v) * 0.7071067811865476
    base = 1.0 + 0.3275911 * size
    t = pl.reciprocal(base, approx=True)
    t = t * (2.0 - base * t)
    bell = jnp.exp(-0.5 * v * v)
    poly = t * (
        0.127414796 + t * (-0.142248368 + t * (0.7107068705 + t * (-0.7265760135 + t * 0.5307027145)))
    )
    tail = poly * bell
    phi = jnp.where(v >= 0.0, 1.0 - tail, tail)
    return v * phi, phi + v * (bell * 0.3989422804014327)


def params(**more):
    return pltpu.CompilerParams(vmem_limit_bytes=VMEM_BYTES, **more)


def full(shape):
    return pl.BlockSpec(shape, lambda *_: (0,) * len(shape))


def split_of(total, most, step):
    size = (min(most, total) // step) * step
    while size > step and total % size:
        size -= step
    return size if size and total % size == 0 else total


def pair_rows(block, width):
    first = lax.broadcasted_iota(jnp.int32, block.shape, 1) < width
    return jnp.concatenate([jnp.where(first, block, 0.0), jnp.where(first, 0.0, block)], 0).astype(BF)


def pair_join(wide, width):
    rows = wide.shape[1] // 2
    return jnp.concatenate([wide[:width, :rows], wide[width:, rows:]], 0)


def masked(scores, same):
    rows = scores.shape[1] // 2
    return jnp.concatenate(
        [
            jnp.where(same, scores[:, :rows], masked_score),
            jnp.where(same, scores[:, rows:], masked_score),
        ],
        1,
    )


def project_body(x_ref, down_ref, w_ref, up_ref, bias_ref, out_ref, mid_ref):
    low = x_ref[...].astype(BF)
    mid = mm(low, down_ref[...]).astype(BF)
    mid_ref[...] = mid
    total = w_ref.shape[0]
    step = split_of(total, 768, 128)
    for start in range(0, total, step):
        part = slice(start, start + step)
        out_ref[:, part] = (
            mm_nt(low, w_ref[part, :]) + mm(mid, up_ref[:, part]) + bias_ref[:, part]
        ).astype(BF)


def project(x, down, w, up, bias):
    rows, width = x.shape
    tile = split_of(rows, 256, 16)
    total = w.shape[0]
    return pl.pallas_call(
        project_body,
        grid=(rows // tile,),
        in_specs=[
            pl.BlockSpec((tile, width), lambda i: (i, 0)),
            full(down.shape),
            full(w.shape),
            full(up.shape),
            full(bias.shape),
        ],
        out_specs=[
            pl.BlockSpec((tile, total), lambda i: (i, 0)),
            pl.BlockSpec((tile, down.shape[1]), lambda i: (i, 0)),
        ],
        out_shape=[
            jax.ShapeDtypeStruct((rows, total), BF),
            jax.ShapeDtypeStruct((rows, down.shape[1]), BF),
        ],
        compiler_params=params(),
        name="project",
    )(x, down, w, up, bias)


def attend_body(q_ref, k_ref, v_ref, seg_ref, seg_row_ref, ctx_ref, log_ref):
    rows = q_ref.shape[0]
    width = q_ref.shape[1] // 2
    scale = width**-0.5
    for start in range(0, rows, REACH):
        own = slice(start, start + REACH)
        near = slice(max(0, start - REACH), min(rows, start + 2 * REACH))
        queries = pair_rows(q_ref[own, :].astype(F32) * scale, width)
        same = seg_ref[near, :] == seg_row_ref[:, own]
        scores = masked(mm_nt(k_ref[near, :], queries), same)
        top = jnp.max(scores, 0, keepdims=True)
        weights = jnp.exp(scores - top)
        total = jnp.sum(weights, 0, keepdims=True)
        context = mm_tn(v_ref[near, :], weights.astype(BF)) * (1.0 / total)
        ctx_ref[own, :] = pair_join(context, width).T.astype(BF)
        log_ref[0, :, 2 * start : 2 * start + 2 * REACH] = top + jnp.log(total)


def attend(qkv, seg_wide, seg_row):
    rows, total = qkv.shape
    hidden = total // 3
    lanes = 2 * (hidden // HEADS)
    pairs = hidden // lanes
    column = lambda kind: pl.BlockSpec((rows, lanes), lambda p: (0, kind * pairs + p))
    return pl.pallas_call(
        attend_body,
        grid=(pairs,),
        in_specs=[column(0), column(1), column(2), full(seg_wide.shape), full(seg_row.shape)],
        out_specs=[
            pl.BlockSpec((rows, lanes), lambda p: (0, p)),
            pl.BlockSpec((1, 1, 2 * rows), lambda p: (p, 0, 0)),
        ],
        out_shape=[
            jax.ShapeDtypeStruct((rows, hidden), BF),
            jax.ShapeDtypeStruct((pairs, 1, 2 * rows), F32),
        ],
        compiler_params=params(),
        name="attend",
    )(qkv, qkv, qkv, seg_wide, seg_row)


def flat(ref):
    whole = ref[...]
    return whole.reshape(-1, whole.shape[-1])


def rows_of(ref, start, size):
    each = ref.shape[1]
    if size % each == 0 and start % each == 0 and each % 16 == 0:
        part = ref[start // each : (start + size) // each, :, :]
        return part.reshape(size, part.shape[-1])
    return flat(ref)[start : start + size, :]


def feed_step(ref):
    units = ref.shape[0] * ref.shape[1]
    step = ref.shape[1]
    while units % (2 * step) == 0 and 2 * step <= 768 and ref.shape[0] > 1:
        step *= 2
    return units, (step if ref.shape[0] > 1 else split_of(units, 768, 128))


def after_body(
    ctx_ref, x_ref, wo_ref, up_ref, down_ref, bo_ref, b1_ref, b2_ref, norm_ref,
    out_ref, one_ref, two_ref, slope_ref,
):
    one = x_ref[...] + (mm_nt(ctx_ref[...], wo_ref[...]) + bo_ref[...])
    one_ref[...] = one
    middle = layer_norm(one, norm_ref[0:1, :], norm_ref[1:2, :])
    low = middle.astype(BF)
    total = middle + b2_ref[...]
    units, step = feed_step(up_ref)
    for start in range(0, units, step):
        part = slice(start, start + step)
        act, slope = gelu_pair(mm_nt(low, rows_of(up_ref, start, step)) + b1_ref[:, part])
        slope_ref[:, part] = slope.astype(BF)
        total = total + mm(act.astype(BF), rows_of(down_ref, start, step))
    two_ref[...] = total
    out_ref[...] = layer_norm(total, norm_ref[2:3, :], norm_ref[3:4, :])


def slab_spec(slab):
    array, place, rows = slab
    return pl.BlockSpec((array.shape[0], rows, array.shape[2]), lambda *_: (0, place, 0))


def after(ctx, x, wo, up, down, bo, b1, b2, norms):
    rows, width = x.shape
    tile = split_of(rows, 256, 16)
    units = b1.shape[1]
    row = lambda n: pl.BlockSpec((tile, n), lambda i: (i, 0))
    return pl.pallas_call(
        after_body,
        grid=(rows // tile,),
        in_specs=[row(width), row(width), full(wo.shape), slab_spec(up), slab_spec(down)]
        + [full(a.shape) for a in (bo, b1, b2, norms)],
        out_specs=[row(width), row(width), row(width), row(units)],
        out_shape=[jax.ShapeDtypeStruct((rows, width), F32)] * 3
        + [jax.ShapeDtypeStruct((rows, units), BF)],
        compiler_params=params(),
        name="after",
    )(ctx, x, wo, up[0], down[0], bo, b1, b2, norms)


def exact_rows(choose, matrix):
    high = matrix.astype(BF)
    rest = matrix - high.astype(F32)
    middle = rest.astype(BF)
    low = (rest - middle.astype(F32)).astype(BF)
    return mm(choose, high) + mm(choose, middle) + mm(choose, low)


def last_forward_body(
    x_ref, place_ref, place_row_ref, seg_ref, down_ref, w_ref, adapt_ref, bias_ref, wo_ref, up_any, dn_any,
    bo_ref, b1_ref, b2_ref, norm_ref, hb_ref, hbias_ref,
    kv_ref, q_ref, mid_ref, log_ref, one_ref, slope_ref, two_ref, low_ref, act_ref, hslope_ref, feat_ref,
    up_ref, dn_ref, ctx_ref, sems, *, places,
):
    copies = []
    for k, (source, target, place) in enumerate(
        ((up_any, up_ref, places[0]), (dn_any, dn_ref, places[1]))
    ):
        rows = target.shape[1]
        copies.append(
            pltpu.make_async_copy(
                source.at[:, pl.ds(place * rows, rows), :], target, sems.at[k]
            )
        )
        copies[-1].start()
    rows, hidden = x_ref.shape
    labels = place_ref.shape[0]
    lanes = 2 * (hidden // HEADS)
    width = lanes // 2
    low = x_ref[...].astype(BF)
    mid = mm(low, down_ref[...]).astype(BF)
    mid_ref[...] = mid
    step = split_of(2 * hidden, 512, 128)
    for start in range(hidden, 3 * hidden, step):
        part = slice(start, start + step)
        kv_ref[:, start - hidden : start - hidden + step] = (
            mm_nt(low, w_ref[part, :]) + mm(mid, adapt_ref[:, part]) + bias_ref[:, part]
        ).astype(BF)
    choose = (
        lax.broadcasted_iota(jnp.int32, (labels, rows), 1) == place_ref[...][:, 0:1]
    ).astype(F32).astype(BF)
    own = exact_rows(choose, x_ref[...])
    own_low = own.astype(BF)
    own_mid = mm(choose, mid).astype(BF)
    q_ref[...] = (
        mm_nt(own_low, w_ref[:hidden, :]) + mm(own_mid, adapt_ref[:, :hidden]) + bias_ref[:, :hidden]
    ).astype(BF)
    seg = seg_ref[...]
    seg_own = jnp.sum(
        jnp.where(
            lax.broadcasted_iota(jnp.int32, (rows, labels), 0) == place_row_ref[...], seg, 0.0
        ),
        0,
        keepdims=True,
    )
    same = seg == seg_own
    for p in range(hidden // lanes):
        part = slice(p * lanes, (p + 1) * lanes)
        queries = pair_rows(q_ref[:, part].astype(F32) * width**-0.5, width)
        scores = masked(mm_nt(kv_ref[:, part], queries), same)
        top = jnp.max(scores, 0, keepdims=True)
        weights = jnp.exp(scores - top)
        total = jnp.sum(weights, 0, keepdims=True)
        context = mm_tn(
            kv_ref[:, hidden + p * lanes : hidden + (p + 1) * lanes], weights.astype(BF)
        ) * (1.0 / total)
        ctx_ref[:, part] = pair_join(context, width).T.astype(BF)
        log_ref[p : p + 1, :] = top + jnp.log(total)
    one = own + (mm_nt(ctx_ref[...], wo_ref[...]) + bo_ref[...])
    one_ref[...] = one
    middle = layer_norm(one, norm_ref[0:1, :], norm_ref[1:2, :])
    middle_low = middle.astype(BF)
    sum_two = middle + b2_ref[...]
    units, step = feed_step(up_ref)
    for copy in copies:
        copy.wait()
    for start in range(0, units, step):
        part = slice(start, start + step)
        act, slope = gelu_pair(mm_nt(middle_low, rows_of(up_ref, start, step)) + b1_ref[:, part])
        slope_ref[:, part] = slope.astype(BF)
        sum_two = sum_two + mm(act.astype(BF), rows_of(dn_ref, start, step))
    two_ref[...] = sum_two
    out_low = layer_norm(sum_two, norm_ref[2:3, :], norm_ref[3:4, :]).astype(BF)
    low_ref[...] = out_low
    act, slope = gelu_pair(mm(out_low, hb_ref[...]) + hbias_ref[...])
    act_ref[...] = act
    hslope_ref[...] = slope
    feat_ref[...] = layer_norm(act, norm_ref[4:5, :], norm_ref[5:6, :]).astype(BF)


def slab_scratch(slab):
    array, place, rows = slab
    return pltpu.VMEM((array.shape[0], rows, array.shape[2]), BF)


def last_forward(x, place_col, place_row, seg_wide, down, w, adapt, bias, wo, up, dn, bo, b1, b2, norms, hb, hbias):
    rows, hidden = x.shape
    labels = place_col.shape[0]
    units = b1.shape[1]
    whole = pl.BlockSpec(memory_space=pltpu.VMEM)
    anywhere = pl.BlockSpec(memory_space=pl.ANY)
    shape = jax.ShapeDtypeStruct
    pairs = HEADS // 2
    return pl.pallas_call(
        functools.partial(last_forward_body, places=(up[1], dn[1])),
        in_specs=[whole] * 9 + [anywhere] * 2 + [whole] * 6,
        out_specs=[whole] * 11,
        out_shape=[
            shape((rows, 2 * hidden), BF),
            shape((labels, hidden), BF),
            shape((rows, down.shape[1]), BF),
            shape((pairs, 2 * labels), F32),
            shape((labels, hidden), F32),
            shape((labels, units), BF),
            shape((labels, hidden), F32),
            shape((labels, hidden), BF),
            shape((labels, hidden), F32),
            shape((labels, hidden), F32),
            shape((labels, hidden), BF),
        ],
        scratch_shapes=[
            slab_scratch(up),
            slab_scratch(dn),
            pltpu.VMEM((labels, hidden), BF),
            pltpu.SemaphoreType.DMA((2,)),
        ],
        compiler_params=params(),
        name="last_forward",
    )(x, place_col, place_row, seg_wide, down, w, adapt, bias, wo, up[0], dn[0], bo, b1, b2, norms, hb, hbias)


def vocab_body(u_ref, e_ref, et_ref, bias_ref, num_ref, log_ref, scores, weights):
    count = e_ref.shape[0]
    step = split_of(count, 640, 16)
    u = u_ref[...]
    rows = u.shape[0]
    labels = num_ref.shape[2]
    top = jnp.full((1, rows), -jnp.inf, F32)
    for start in range(0, count, step):
        part = slice(start, start + step)
        bias = bias_ref[part, :]
        logits = mm_nt(e_ref[part, :], u) + jnp.concatenate([bias] * (rows // bias.shape[1]), 1)
        scores[part, :] = logits
        top = jnp.maximum(top, jnp.max(logits, 0, keepdims=True))
    total = jnp.zeros((1, rows), F32)
    for start in range(0, count, step):
        part = slice(start, start + step)
        grown = jnp.exp(scores[part, :] - top)
        total = total + jnp.sum(grown, 0, keepdims=True)
        weights[part, :] = grown.astype(BF)
    mean = mm(et_ref[...], weights[...]) * (1.0 / total)
    logs = top + jnp.log(total)
    for k in range(rows // labels):
        num_ref[k, :, :] = mean[:, k * labels : (k + 1) * labels]
        log_ref[k, :, :] = logs[:, k * labels : (k + 1) * labels]


def vocab(u, e, et, bias_wide, labels):
    rows, hidden = u.shape
    count = e.shape[0]
    tile = 2 * labels
    return pl.pallas_call(
        vocab_body,
        grid=(rows // tile,),
        in_specs=[
            pl.BlockSpec((tile, hidden), lambda i: (i, 0)),
            full(e.shape),
            full(et.shape),
            full(bias_wide.shape),
        ],
        out_specs=[
            pl.BlockSpec((2, hidden, labels), lambda i: (i, 0, 0)),
            pl.BlockSpec((2, 1, labels), lambda i: (i, 0, 0)),
        ],
        out_shape=[
            jax.ShapeDtypeStruct((rows // labels, hidden, labels), F32),
            jax.ShapeDtypeStruct((rows // labels, 1, labels), F32),
        ],
        scratch_shapes=[pltpu.VMEM((count, tile), F32), pltpu.VMEM((count, tile), BF)],
        compiler_params=params(),
        name="vocab",
    )(u, e, et, bias_wide)


def last_backward_body(
    du_ref, kv_ref, q_ref, mid_ref, log_ref, one_ref, slope_ref, two_ref, low_ref, act_ref, hslope_ref,
    place_ref, place_row_ref, seg_ref, down_ref, w_ref, adapt_ref, wo_ref, up_any, dn_any, norm_ref, hb_ref,
    dx_ref, gh_ref, gq_ref, gv_ref,
    up_ref, dn_ref, dkv_ref, dq_ref, sems, *, places, rank,
):
    copies = []
    for k, (source, target, place) in enumerate(
        ((up_any, up_ref, places[0]), (dn_any, dn_ref, places[1]))
    ):
        rows = target.shape[1]
        copies.append(
            pltpu.make_async_copy(
                source.at[:, pl.ds(place * rows, rows), :], target, sems.at[k]
            )
        )
        copies[-1].start()
    rows = kv_ref.shape[0]
    labels, hidden = du_ref.shape
    lanes = 2 * (hidden // HEADS)
    width = lanes // 2
    scale = width**-0.5
    dact = norm_back(act_ref[...], norm_ref[4:5, :], du_ref[...])
    dz = (hslope_ref[...] * dact).astype(BF)
    gh_ref[...] = mm_tn(low_ref[...], dz)
    dtwo = norm_back(two_ref[...], norm_ref[2:3, :], mm_nt(dz, hb_ref[...]))
    dtwo_low = dtwo.astype(BF)
    dmiddle = dtwo
    units, step = feed_step(up_ref)
    for copy in copies:
        copy.wait()
    for start in range(0, units, step):
        part = slice(start, start + step)
        dgate = (
            slope_ref[:, part].astype(F32) * mm_nt(dtwo_low, rows_of(dn_ref, start, step))
        ).astype(BF)
        dmiddle = dmiddle + mm(dgate, rows_of(up_ref, start, step))
    done = norm_back(one_ref[...], norm_ref[0:1, :], dmiddle)
    dctx = mm(done.astype(BF), wo_ref[...]).astype(BF)
    seg = seg_ref[...]
    choose_t = lax.broadcasted_iota(jnp.int32, (rows, labels), 0) == place_row_ref[...]
    same = seg == jnp.sum(jnp.where(choose_t, seg, 0.0), 0, keepdims=True)
    for p in range(hidden // lanes):
        part = slice(p * lanes, (p + 1) * lanes)
        later = slice(hidden + p * lanes, hidden + (p + 1) * lanes)
        queries = pair_rows(q_ref[:, part].astype(F32) * scale, width)
        outs = pair_rows(dctx[:, part].astype(F32), width)
        keys = kv_ref[:, part]
        weights = jnp.exp(masked(mm_nt(keys, queries), same) - log_ref[p : p + 1, :])
        dweights = mm_nt(kv_ref[:, later], outs)
        inner = jnp.sum(dweights * weights, 0, keepdims=True)
        dscores = (weights * (dweights - inner)).astype(BF)
        dkv_ref[:, part] = mm(dscores, queries).astype(BF)
        dkv_ref[:, later] = mm(weights.astype(BF), outs).astype(BF)
        dq_ref[:, part] = (pair_join(mm_tn(keys, dscores), width) * scale).T.astype(BF)
    dq = dq_ref[...]
    own_mid = mm(
        (lax.broadcasted_iota(jnp.int32, (labels, rows), 1) == place_ref[...][:, 0:1]).astype(F32).astype(BF),
        mid_ref[...],
    ).astype(BF)
    gq_ref[...] = adapter_scale * mm_tn(own_mid, dq)[:rank, :]
    gv_ref[...] = adapter_scale * mm_tn(mid_ref[...], dkv_ref[:, hidden:])[rank : 2 * rank, :]
    dmid_own = mm_nt(dq, adapt_ref[:, :hidden]).astype(BF)
    own = done + mm(dq, w_ref[:hidden, :]) + mm_nt(dmid_own, down_ref[...])
    spread = choose_t.astype(F32).astype(BF)
    own_high = own.astype(BF)
    own_rest = (own - own_high.astype(F32)).astype(BF)
    dmid = mm_nt(dkv_ref[:, hidden:], adapt_ref[:, 2 * hidden :]).astype(BF)
    step = split_of(hidden, 256, 128)
    for start in range(0, hidden, step):
        part = slice(start, start + step)
        dx_ref[:, part] = (
            mm(dkv_ref[...], w_ref[hidden:, part])
            + mm_nt(dmid, down_ref[part, :])
            + mm(spread, own_high[:, part])
            + mm(spread, own_rest[:, part])
        )


def last_backward(du, saved, place_col, place_row, seg_wide, down, w, adapt, wo, up, dn, norms, hb, rank):
    kv = saved[0]
    rows = kv.shape[0]
    labels, hidden = du.shape
    whole = pl.BlockSpec(memory_space=pltpu.VMEM)
    anywhere = pl.BlockSpec(memory_space=pl.ANY)
    shape = jax.ShapeDtypeStruct
    return pl.pallas_call(
        functools.partial(last_backward_body, places=(up[1], dn[1]), rank=rank),
        in_specs=[whole] * 18 + [anywhere] * 2 + [whole] * 2,
        out_specs=[whole] * 4,
        out_shape=[
            shape((rows, hidden), F32),
            shape((hidden, hidden), F32),
            shape((rank, hidden), F32),
            shape((rank, hidden), F32),
        ],
        scratch_shapes=[
            slab_scratch(up),
            slab_scratch(dn),
            pltpu.VMEM(kv.shape, BF),
            pltpu.VMEM((labels, hidden), BF),
            pltpu.SemaphoreType.DMA((2,)),
        ],
        compiler_params=params(),
        name="last_backward",
    )(du, *saved, place_col, place_row, seg_wide, down, w, adapt, wo, up[0], dn[0], norms, hb)


def after_back_sum_body(shards, *refs):
    *plain, parts, dctx_ref, sum_ref, got, sends, gets = refs
    step, last = pl.program_id(0), pl.num_programs(0) - 1
    me = number_of(position())

    @pl.when(step == 0)
    def _():
        greet_all(shards)
        got[me] = parts[me]

    @pl.when(step == jnp.minimum(1, last))
    def _():
        await_all(shards)
        spread(lambda peer: parts.at[peer], got, sends, gets, me, shards)

    after_back_body(*plain, dctx_ref)

    @pl.when(step == last)
    def _():
        collect(lambda peer: parts.at[peer], got, sends, gets, me, shards)
        total = got[0].astype(F32)
        for k in range(1, shards):
            total = total + got[k].astype(F32)
        sum_ref[...] = total


def after_back_body(dout_ref, one_ref, two_ref, slope_ref, wo_ref, up_ref, down_ref, norm_ref, dctx_ref):
    dtwo = norm_back(two_ref[...], norm_ref[2:3, :], dout_ref[...])
    low = dtwo.astype(BF)
    dmiddle = dtwo
    units, step = feed_step(up_ref)
    for start in range(0, units, step):
        part = slice(start, start + step)
        dgate = (
            slope_ref[:, part].astype(F32) * mm_nt(low, rows_of(down_ref, start, step))
        ).astype(BF)
        dmiddle = dmiddle + mm(dgate, rows_of(up_ref, start, step))
    done = norm_back(one_ref[...], norm_ref[0:1, :], dmiddle)
    dctx_ref[...] = mm(done.astype(BF), wo_ref[...]).astype(BF)


def after_back_sum(dout, one, two, slope, wo, up, down, norms, parts, shards):
    rows, width = dout.shape
    tile = split_of(rows, 256, 16)
    row = lambda n: pl.BlockSpec((tile, n), lambda i: (i, 0))
    sems = pltpu.SemaphoreType.DMA
    return pl.pallas_call(
        functools.partial(after_back_sum_body, shards),
        grid=(rows // tile,),
        in_specs=[row(width), row(width), row(width), row(slope.shape[1]), full(wo.shape)]
        + [slab_spec(up), slab_spec(down), full(norms.shape), full(parts.shape)],
        out_specs=[row(width), full(parts.shape[1:])],
        out_shape=[
            jax.ShapeDtypeStruct((rows, width), BF),
            jax.ShapeDtypeStruct(parts.shape[1:], F32),
        ],
        scratch_shapes=[pltpu.VMEM(parts.shape, BF), sems((shards,)), sems((shards,))],
        compiler_params=params(collective_id=3, has_side_effects=True),
        name="after_back_sum",
    )(dout, one, two, slope, wo, up[0], down[0], norms, parts)


def after_back(dout, one, two, slope, wo, up, down, norms):
    rows, width = dout.shape
    tile = split_of(rows, 256, 16)
    row = lambda n: pl.BlockSpec((tile, n), lambda i: (i, 0))
    return pl.pallas_call(
        after_back_body,
        grid=(rows // tile,),
        in_specs=[row(width), row(width), row(width), row(slope.shape[1]), full(wo.shape)]
        + [slab_spec(up), slab_spec(down), full(norms.shape)],
        out_specs=row(width),
        out_shape=jax.ShapeDtypeStruct((rows, width), BF),
        compiler_params=params(),
        name="after_back",
    )(dout, one, two, slope, wo, up[0], down[0], norms)


def attend_back_body(
    q_ref, k_ref, v_ref, dctx_ref, log_ref, seg_ref, seg_row_ref, mid_ref, gq_ref, gv_ref, dv_ref
):
    rows = q_ref.shape[0]
    width = q_ref.shape[1] // 2
    scale = width**-0.5
    rank = gq_ref.shape[0]
    dv_ref[...] = jnp.zeros_like(dv_ref)
    gq = jnp.zeros((2 * width, mid_ref.shape[1]), F32)
    for start in range(0, rows, REACH):
        own = slice(start, start + REACH)
        near = slice(max(0, start - REACH), min(rows, start + 2 * REACH))
        queries = pair_rows(q_ref[own, :].astype(F32) * scale, width)
        outs = pair_rows(dctx_ref[own, :].astype(F32), width)
        same = seg_ref[near, :] == seg_row_ref[:, own]
        keys = k_ref[near, :]
        logs = log_ref[0, :, 2 * start : 2 * start + 2 * REACH]
        weights = jnp.exp(masked(mm_nt(keys, queries), same) - logs)
        dweights = mm_nt(v_ref[near, :], outs)
        inner = jnp.sum(dweights * weights, 0, keepdims=True)
        dscores = (weights * (dweights - inner)).astype(BF)
        dv_ref[near, :] += mm(weights.astype(BF), outs)
        dq = (pair_join(mm_tn(keys, dscores), width) * scale).astype(BF)
        gq = gq + mm(dq, mid_ref[own, :])
    gq_ref[...] = adapter_scale * gq.T[:rank, :]
    gv_ref[...] = adapter_scale * mm_tn(mid_ref[...], dv_ref[...].astype(BF))[rank : 2 * rank, :]


def attend_back(qkv, dctx, logs, seg_wide, seg_row, mid, rank):
    rows, total = qkv.shape
    hidden = total // 3
    lanes = 2 * (hidden // HEADS)
    pairs = hidden // lanes
    column = lambda kind: pl.BlockSpec((rows, lanes), lambda p: (0, kind * pairs + p))
    return pl.pallas_call(
        attend_back_body,
        grid=(pairs,),
        in_specs=[
            column(0),
            column(1),
            column(2),
            column(0),
            pl.BlockSpec((1, 1, 2 * rows), lambda p: (p, 0, 0)),
            full(seg_wide.shape),
            full(seg_row.shape),
            full(mid.shape),
        ],
        out_specs=[pl.BlockSpec((rank, lanes), lambda p: (0, p))] * 2,
        out_shape=[jax.ShapeDtypeStruct((rank, hidden), F32)] * 2,
        scratch_shapes=[pltpu.VMEM((rows, lanes), F32)],
        compiler_params=params(),
        name="attend_back",
    )(qkv, qkv, qkv, dctx, logs, seg_wide, seg_row, mid)


MESH = pl.DeviceIdType.MESH


def position():
    dp, fsdp = lax.axis_index("dp"), lax.axis_index("fsdp")
    return {"x": dp, "z": fsdp // 4, "y": (fsdp // 2) % 2, "c": fsdp % 2}


def device_of(place):
    return (place["x"], (place["z"] * 2 + place["y"]) * 2 + place["c"])


def number_of(place):
    return place["x"] * 16 + (place["z"] * 2 + place["y"]) * 2 + place["c"]


def rank_device(number):
    return (number // 16, number % 16)


def greet_all(shards):
    barrier = pltpu.get_barrier_semaphore()
    me = lax.axis_index("dp") * 16 + lax.axis_index("fsdp")

    @pl.loop(1, shards)
    def _(k):
        pl.semaphore_signal(
            barrier, inc=1, device_id=rank_device((me + k) % shards), device_id_type=MESH
        )


def await_all(shards):
    pl.semaphore_wait(pltpu.get_barrier_semaphore(), shards - 1)


def direct_copy(source, target, sends, receives, me, k, shards):
    return pltpu.make_async_remote_copy(
        src_ref=source,
        dst_ref=target,
        send_sem=sends.at[k],
        recv_sem=receives.at[me],
        device_id=rank_device((me + k) % shards),
        device_id_type=MESH,
    )


def spread(piece_of, buffer, sends, receives, me, shards):
    @pl.loop(1, shards)
    def _(k):
        direct_copy(piece_of((me + k) % shards), buffer.at[me], sends, receives, me, k, shards).start()


def collect(piece_of, buffer, sends, receives, me, shards):
    @pl.loop(1, shards)
    def _(k):
        source = (me + shards - k) % shards
        direct_copy(buffer.at[source], buffer.at[source], sends, receives, source, k, shards).wait_recv()

    @pl.loop(1, shards)
    def _(k):
        direct_copy(piece_of((me + k) % shards), buffer.at[me], sends, receives, me, k, shards).wait_send()


def start_body(
    shards, rows, note, bias, got, notes, biases,
    row_sems, note_sends, note_gets, bias_sends, bias_gets, own_sems,
):
    here = position()
    me = number_of(here)
    greet_all(shards)
    own_note = pltpu.make_async_copy(note, notes.at[me], own_sems.at[0])
    own_note.start()
    own_bias = pltpu.make_async_copy(bias, biases.at[me], own_sems.at[1])
    own_bias.start()
    await_all(shards)
    across = pltpu.make_async_remote_copy(
        src_ref=rows,
        dst_ref=got,
        send_sem=row_sems.at[0],
        recv_sem=row_sems.at[1],
        device_id=device_of(dict(here, x=1 - here["x"])),
        device_id_type=MESH,
    )
    across.start()
    spread(lambda peer: note, notes, note_sends, note_gets, me, shards)
    spread(lambda peer: bias, biases, bias_sends, bias_gets, me, shards)
    collect(lambda peer: note, notes, note_sends, note_gets, me, shards)
    collect(lambda peer: bias, biases, bias_sends, bias_gets, me, shards)
    across.wait()
    own_note.wait()
    own_bias.wait()


def start_exchange(rows, note, bias, shards):
    anywhere = pl.BlockSpec(memory_space=pl.ANY)
    shape = jax.ShapeDtypeStruct
    sems = pltpu.SemaphoreType.DMA
    return pl.pallas_call(
        functools.partial(start_body, shards),
        in_specs=[anywhere] * 3,
        out_specs=[anywhere] * 3,
        out_shape=[
            shape(rows.shape, rows.dtype),
            shape((shards, *note.shape), note.dtype),
            shape((shards, *bias.shape), bias.dtype),
        ],
        scratch_shapes=[sems((2,))] + [sems((shards,))] * 4 + [sems((2,))],
        compiler_params=params(collective_id=1, has_side_effects=True),
        name="start_exchange",
    )(rows, note, bias)


def tail_body(shards, parts, dense, loss, total_ref, sums_ref, got, note, notes, send_a, get_a, send_b, get_b):
    me = number_of(position())
    greet_all(shards)
    got[me] = parts[me]
    await_all(shards)
    spread(lambda peer: parts.at[peer], got, send_a, get_a, me, shards)
    dense_square = jnp.sum(dense[...] * dense[...], keepdims=True)
    collect(lambda peer: parts.at[peer], got, send_a, get_a, me, shards)
    total = got[0]
    for k in range(1, shards):
        total = total + got[k]
    total_ref[...] = total
    square = dense_square + jnp.sum(total * total, keepdims=True)
    row = lax.broadcasted_iota(jnp.int32, note.shape, 0)
    note[...] = jnp.where(row == 0, loss[...], jnp.where(row == 1, square, 0.0))
    notes[me] = note[...]
    spread(lambda peer: note, notes, send_b, get_b, me, shards)
    collect(lambda peer: note, notes, send_b, get_b, me, shards)
    total = notes[0]
    for k in range(1, shards):
        total = total + notes[k]
    sums_ref[...] = total


def tail(parts, dense, loss, shards):
    whole = pl.BlockSpec(memory_space=pltpu.VMEM)
    block = parts.shape[1:]
    shape = jax.ShapeDtypeStruct
    sems = pltpu.SemaphoreType.DMA
    return pl.pallas_call(
        functools.partial(tail_body, shards),
        in_specs=[whole] * 3,
        out_specs=[whole] * 2,
        out_shape=[shape(block, F32), shape((8, 128), F32)],
        scratch_shapes=[
            pltpu.VMEM(parts.shape, F32),
            pltpu.VMEM((8, 128), F32),
            pltpu.VMEM((shards, 8, 128), F32),
        ]
        + [sems((shards,))] * 4,
        compiler_params=params(collective_id=2, has_side_effects=True),
        name="tail",
    )(parts, dense, loss)


HOPS = 3
LOG_ROWS = 16


def flip(z, k):
    return (z % 2 + k % 2) % 2 + 2 * ((z // 2 + k // 2) % 2)


def pack_log(log_row, rows):
    high = log_row.astype(BF).astype(F32)
    middle = (log_row - high).astype(BF).astype(F32)
    low = log_row - high - middle
    row = lax.broadcasted_iota(jnp.int32, (rows, log_row.shape[1]), 0)
    return jnp.where(
        row == 0, high, jnp.where(row == 1, middle, jnp.where(row == 2, low, 0.0))
    ).astype(BF)


def unpack(block, hidden):
    logs = block[hidden : hidden + LOG_ROWS, :].astype(F32)
    return block[:hidden, :].astype(F32), jnp.sum(logs, 0, keepdims=True)


def merged(one, two):
    top = jnp.maximum(one[1], two[1])
    first, second = jnp.exp(one[1] - top), jnp.exp(two[1] - top)
    total = first + second
    inverse = 1.0 / total
    return one[0] * (first * inverse) + two[0] * (second * inverse), top + jnp.log(total)


def store_packed(ref, pair, hidden):
    ref[:hidden, :] = pair[0].astype(BF)
    ref[hidden : hidden + LOG_ROWS, :] = pack_log(pair[1], LOG_ROWS)


def head_body(
    u_ref, e_any, et_any, bias_any, mean_ref, log_ref,
    e_ref, et_ref, bias_ref, feats, packs, handed, crossed, kept, lined, zouts,
    loads, z_send, z_get, y_send, y_get, c_send, c_get, h_send, h_get, p_send, p_get, l_send, l_get,
):
    here = position()
    z, y, c = here["z"], here["y"], here["c"]
    labels, hidden = u_ref.shape
    slot_of = lambda zz, yy, cc: (zz * 2 + yy) * 2 + cc
    me = slot_of(z, y, c)
    sibling = device_of(dict(here, c=1 - c))
    beside = device_of(dict(here, y=1 - y))
    at_z = lambda zz: device_of(dict(here, z=zz))
    inside = lambda zz: (zz >= 0) & (zz <= HOPS)

    fills = [
        pltpu.make_async_copy(source, target, loads.at[k])
        for k, (source, target) in enumerate(((e_any, e_ref), (bias_any, bias_ref), (et_any, et_ref)))
    ]
    for fill in fills:
        fill.start()
    barrier = pltpu.get_barrier_semaphore()
    for target in (sibling, beside):
        pl.semaphore_signal(barrier, inc=1, device_id=target, device_id_type=MESH)
    for k in range(1, 4):
        pl.semaphore_signal(barrier, inc=1, device_id=at_z(flip(z, k)), device_id_type=MESH)
    feats[me] = u_ref[...]
    pl.semaphore_wait(barrier, 5)

    def move(slot, device, send, get):
        return pltpu.make_async_remote_copy(
            src_ref=feats.at[slot],
            dst_ref=feats.at[slot],
            send_sem=send,
            recv_sem=get,
            device_id=device,
            device_id_type=MESH,
        )

    def hand(zz, other):
        slot = slot_of(zz, (y + other) % 2, c)
        return move(slot, sibling, c_send.at[other * 4 + zz], c_get.at[other * 4 + zz])

    def handed_here(zz, other):
        slot = slot_of(zz, (y + other) % 2, 1 - c)
        return move(slot, sibling, c_send.at[other * 4 + zz], c_get.at[other * 4 + zz])

    def cross(zz):
        return move(slot_of(zz, y, c), beside, y_send.at[zz], y_get.at[zz])

    def crossed_here(zz):
        return move(slot_of(zz, 1 - y, c), beside, y_send.at[zz], y_get.at[zz])

    def along(zz, to, way):
        return move(slot_of(zz, y, c), at_z(to), z_send.at[way * 4 + zz], z_get.at[zz])

    def own_round():
        for way, to in ((0, z + 1), (1, z - 1)):

            @pl.when(inside(to))
            def _(way=way, to=to):
                along(z, to, way).start()

        cross(z).start()
        hand(z, 0).start()

    def later_round(r):
        if r <= HOPS:
            for way, origin, to in ((0, z - r, z + 1), (1, z + r, z - 1)):

                @pl.when(inside(origin))
                def _(way=way, origin=origin, to=to):
                    along(origin, to, way).wait_recv()

                    @pl.when(inside(to))
                    def _():
                        along(origin, to, way).start()

                    cross(origin).start()
                    hand(origin, 0).start()

        for origin in (z - (r - 1), z + (r - 1))[: 1 if r == 1 else 2]:

            @pl.when(inside(origin))
            def _(origin=origin):
                crossed_here(origin).wait_recv()
                hand(origin, 1).start()

    own_round()
    fills[0].wait()
    fills[1].wait()
    fills[2].wait()
    count = e_ref.shape[0]
    step = split_of(count, 640, 128)

    def hand_part(s):
        return pltpu.make_async_remote_copy(
            src_ref=packs.at[s, 1 - c],
            dst_ref=handed.at[s],
            send_sem=h_send.at[s],
            recv_sem=h_get.at[s],
            device_id=sibling,
            device_id_type=MESH,
        )

    def cross_part(k):
        return pltpu.make_async_remote_copy(
            src_ref=packs.at[2 * k + 1, c],
            dst_ref=crossed.at[k],
            send_sem=p_send.at[k],
            recv_sem=p_get.at[k],
            device_id=beside,
            device_id_type=MESH,
        )

    def line_part(k):
        return pltpu.make_async_remote_copy(
            src_ref=zouts.at[k],
            dst_ref=lined.at[k],
            send_sem=l_send.at[k],
            recv_sem=l_get.at[k],
            device_id=at_z(flip(z, k)),
            device_id_type=MESH,
        )

    def compute(s):
        zt, yt = flip(z, s // 2), (y + s % 2) % 2

        handed_here(zt, s % 2).wait_recv()
        first = slot_of(zt, yt, 0)
        u = feats[pl.ds(first, 2)].reshape(2 * labels, hidden)
        top = total = mean = None
        for start in range(0, count, step):
            part = slice(start, start + step)
            bias = bias_ref[part, :]
            logits = mm_nt(e_ref[part, :], u) + jnp.concatenate([bias, bias], 1)
            high = jnp.max(logits, 0, keepdims=True)
            new = high if top is None else jnp.maximum(top, high)
            grown = jnp.exp(logits - new)
            sums = jnp.sum(grown, 0, keepdims=True)
            product = mm(et_ref[:, part], grown.astype(BF))
            if top is None:
                total, mean = sums, product
            else:
                shrink = jnp.exp(top - new)
                total, mean = total * shrink + sums, mean * shrink + product
            top = new
        mean = mean * (1.0 / total)
        logs = top + jnp.log(total)
        for k in range(2):
            half = slice(k * labels, (k + 1) * labels)
            packs[s, k, :hidden, :] = mean[:, half].astype(BF)
            packs[s, k, hidden : hidden + LOG_ROWS, :] = pack_log(logs[:, half], LOG_ROWS)
        hand_part(s).start()

    def settle(s):
        hand_part(s).wait_recv()
        pair = merged(unpack(packs[s, c], hidden), unpack(handed[s], hidden))

        @pl.when(s % 2 == 1)
        def _():
            store_packed(packs.at[s, c], pair, hidden)
            cross_part(s // 2).start()

        @pl.when(s % 2 == 0)
        def _():
            store_packed(kept.at[s // 2], pair, hidden)

    def finish(k):
        cross_part(k).wait_recv()
        pair = merged(unpack(kept[k], hidden), unpack(crossed[k], hidden))

        @pl.when(k > 0)
        def _():
            store_packed(zouts.at[k], pair, hidden)
            line_part(k).start()

        @pl.when(k == 0)
        def _():
            store_packed(zouts.at[k], pair, hidden)

    steps = 8

    @pl.loop(0, steps)
    def _(s):
        for r in range(1, HOPS + 2):
            pl.when(s == r)(functools.partial(later_round, r))
        compute(s)

        @pl.when(s > 0)
        def _():
            settle(s - 1)

        @pl.when((s >= 3) & (s % 2 == 1))
        def _():
            finish((s - 3) // 2)

    settle(steps - 1)
    finish(steps // 2 - 1)
    total = unpack(zouts[0], hidden)
    for k in range(1, 4):
        line_part(k).wait_recv()
        total = merged(total, unpack(lined[k], hidden))
    mean_ref[...] = total[0]
    log_ref[...] = total[1]

    for way, to in ((0, z + 1), (1, z - 1)):

        @pl.when(inside(to))
        def _(way=way, to=to):
            along(z, to, way).wait_send()

    cross(z).wait_send()
    hand(z, 0).wait_send()
    for r in range(1, HOPS + 1):
        for way, origin, to in ((0, z - r, z + 1), (1, z + r, z - 1)):

            @pl.when(inside(origin))
            def _(way=way, origin=origin, to=to):
                @pl.when(inside(to))
                def _():
                    along(origin, to, way).wait_send()

                cross(origin).wait_send()
                hand(origin, 0).wait_send()

    for origin in range(4):
        hand(origin, 1).wait_send()
    for s in range(steps):
        hand_part(s).wait_send()
    for k in range(4):
        cross_part(k).wait_send()
    for k in range(1, 4):
        line_part(k).wait_send()


def head(u, e, et, bias_wide):
    labels, hidden = u.shape
    whole = pl.BlockSpec(memory_space=pltpu.VMEM)
    anywhere = pl.BlockSpec(memory_space=pl.ANY)
    shape = jax.ShapeDtypeStruct
    sems = pltpu.SemaphoreType.DMA
    block = (hidden + LOG_ROWS, labels)
    return pl.pallas_call(
        head_body,
        in_specs=[whole] + [anywhere] * 3,
        out_specs=[whole] * 2,
        out_shape=[shape((hidden, labels), F32), shape((1, labels), F32)],
        scratch_shapes=[
            pltpu.VMEM(e.shape, BF),
            pltpu.VMEM(et.shape, BF),
            pltpu.VMEM(bias_wide.shape, F32),
            pltpu.VMEM((16, labels, hidden), BF),
            pltpu.VMEM((8, 2, *block), BF),
            pltpu.VMEM((8, *block), BF),
            pltpu.VMEM((4, *block), BF),
            pltpu.VMEM((4, *block), BF),
            pltpu.VMEM((4, *block), BF),
            pltpu.VMEM((4, *block), BF),
            sems((3,)),
            sems((8,)),
            sems((4,)),
            sems((4,)),
            sems((4,)),
            sems((8,)),
            sems((8,)),
            sems((8,)),
            sems((8,)),
            sems((4,)),
            sems((4,)),
            sems((4,)),
            sems((4,)),
        ],
        compiler_params=params(collective_id=4, has_side_effects=True),
        name="head",
    )(u, e, et, bias_wide)


def seg_positions(segments):
    index = jnp.arange(segments.shape[-1], dtype=jnp.int32)
    fresh = jnp.concatenate([jnp.ones((1,), dtype=bool), segments[1:] != segments[:-1]], -1)
    starts = lax.cummax(jnp.where(fresh, index, jnp.zeros_like(index)), axis=0)
    return index - starts


def optimizer_update(weight, gradient, moment_one, moment_two, step_as_real):
    moment_one = beta_first * moment_one + (1.0 - beta_first) * gradient
    moment_two = beta_second * moment_two + (1.0 - beta_second) * gradient * gradient
    one_hat = moment_one / (1.0 - beta_first**step_as_real)
    two_hat = moment_two / (1.0 - beta_second**step_as_real)
    weight = weight - learn_rate * (one_hat / (jnp.sqrt(two_hat) + adam_eps) + decay_rate * weight)
    return (weight, moment_one, moment_two)


def pad_rows(matrix, multiple):
    return jnp.pad(matrix, ((0, -matrix.shape[0] % multiple), (0, 0)))


def slab_of(gathered, start, rows):
    if rows % 16 == 0 and start % rows == 0:
        return (gathered, start // rows, rows)
    part = gathered[:, start : start + rows].reshape(1, -1, gathered.shape[2])
    return (part, 0, part.shape[1])


def per_device(
    input_token_index,
    sentence_numbers,
    label_positions,
    label_target_token,
    sequence_task_index,
    task_loss_weight,
    optimizer_step_count,
    embed,
    position_embedding,
    norm_gain_vector,
    norm_bias_vector,
    attention_in_weight,
    attention_out_weight,
    feedforward_up,
    feedforward_down,
    layer_bias_vector,
    head_dense_bias,
    vocabulary_bias,
    adapter_down_matrix,
    adapter_up_matrix,
    adapter_moment_first,
    adapter_moment_second,
    head_projection,
    head_moment_first,
    head_moment_second,
):
    shards = lax.axis_size("dp") * lax.axis_size("fsdp")
    dp_index = lax.axis_index("dp")
    fsdp_index = lax.axis_index("fsdp")
    layers, unused, rank, up_part = adapter_up_matrix.shape
    hidden = embed.shape[1]
    tokens = input_token_index.shape[1]
    labels = label_positions.shape[1]
    qkv_rows = attention_in_weight.shape[2]
    out_rows = attention_out_weight.shape[2]
    ff_rows = feedforward_up.shape[2]
    head_rows = head_projection.shape[0]

    grouped = (lax.axis_size("dp"), lax.axis_size("fsdp")) == (2, 16)
    chunks = [
        [
            feedforward_up[layer].T,
            feedforward_down[layer],
            attention_in_weight[layer].T,
            attention_out_weight[layer].T,
        ]
        for layer in range(layers)
    ]
    ups = adapter_up_matrix.astype(BF).reshape(-1)
    up_rows = -(-ups.size // hidden)
    chunks[0] += [
        head_projection.astype(BF),
        jnp.pad(ups, (0, up_rows * hidden - ups.size)).reshape(up_rows, hidden),
    ]
    chunks = [pad_rows(jnp.concatenate(pieces, 0), 32) for pieces in chunks]

    table_rows = embed.shape[0]
    wanted = jnp.concatenate([input_token_index[0], label_target_token[0]])
    dp_count = lax.axis_size("dp")
    group_ids = lax.all_gather(wanted, "dp", axis=0, tiled=False) - dp_index * table_rows
    gathered = []
    for chunk in chunks:
        if gathered:
            chunk, gathered[-1] = lax.optimization_barrier((chunk, gathered[-1]))
        gathered.append(lax.all_gather(chunk, BOTH, axis=0, tiled=False))
    first_full = gathered[0]

    def look(ids):
        inside = (ids >= 0) & (ids < table_rows)
        found = embed[jnp.clip(ids, 0, table_rows - 1)]
        return jnp.where(inside[:, None], found, jnp.zeros((), BF)), inside

    task_range = jnp.arange(TASKS, dtype=jnp.int32)
    slice_rows = vocabulary_bias.shape[0]
    if grouped:
        pair_ids = jnp.concatenate(
            [
                lax.dynamic_index_in_dim(group_ids, 1 - dp_index, 0, keepdims=False),
                lax.dynamic_index_in_dim(group_ids, dp_index, 0, keepdims=False),
            ]
        )
        looked, inside = look(pair_ids)
        note = jnp.broadcast_to(sequence_task_index.astype(F32)[:, None], (8, 128))
        bias_rows = -(-slice_rows // 1024) * 8
        bias_block = jnp.pad(vocabulary_bias, (0, bias_rows * 128 - slice_rows)).reshape(bias_rows, 128)
        got, notes, biases = start_exchange(looked[: wanted.size], note, bias_block, shards)
        rows = jnp.where(inside[wanted.size :, None], looked[wanted.size :], got)
        every_task = notes[:, 0, 0].astype(jnp.int32)
        all_bias = biases.reshape(shards, -1)[:, :slice_rows].reshape(-1)
    else:
        looked, inside = look(group_ids.reshape(-1))
        rows = lax.psum_scatter(looked, "dp", scatter_dimension=0, tiled=True)
        every_task = lax.all_gather(sequence_task_index, BOTH, axis=0, tiled=True)
        all_bias = lax.all_gather(vocabulary_bias, BOTH, axis=0, tiled=True)
    counts = labels * jnp.sum((every_task[:, None] == task_range[None, :]).astype(F32), 0)
    task_hot = (sequence_task_index[:, None] == task_range[None, :]).astype(F32)
    row_weight = jnp.sum(task_hot[0] * (task_loss_weight / jnp.maximum(counts, 1.0)))

    slabs = [
        (slab_of(gathered[layer], 0, ff_rows), slab_of(gathered[layer], ff_rows, ff_rows))
        for layer in range(layers)
    ]
    in_weights, out_weights = [], []
    for layer in range(layers):
        at = 2 * ff_rows
        in_weights.append(gathered[layer][:, at : at + qkv_rows].reshape(-1, hidden))
        at += qkv_rows
        out_weights.append(gathered[layer][:, at : at + out_rows].reshape(-1, hidden))
    at = 2 * ff_rows + qkv_rows + out_rows
    head_full = first_full[:, at : at + head_rows].reshape(-1, hidden)
    at += head_rows
    ups_full = (
        first_full[:, at : at + up_rows]
        .reshape(shards, -1)[:, : ups.size]
        .reshape(shards, layers, 2, rank, up_part)
        .transpose(1, 2, 3, 0, 4)
        .reshape(layers, 2, rank, hidden)
    )
    adapters = [
        jnp.zeros((128, 3 * hidden), BF)
        .at[:rank, :hidden]
        .set(2 * ups_full[layer, 0])
        .at[rank : 2 * rank, 2 * hidden :]
        .set(2 * ups_full[layer, 1])
        for layer in range(layers)
    ]
    downs = [
        jnp.zeros((hidden, 128), BF)
        .at[:, :rank]
        .set(adapter_down_matrix[layer, 0])
        .at[:, rank : 2 * rank]
        .set(adapter_down_matrix[layer, 1])
        for layer in range(layers)
    ]
    bias_of = []
    for layer in range(layers):
        b = layer_bias_vector[layer][None, :]
        ff = b.shape[1] - 4 * hidden
        bias_of.append(
            (
                jnp.concatenate(
                    [b[:, :hidden], jnp.zeros((1, hidden), F32), b[:, hidden : 2 * hidden]], 1
                ),
                b[:, 2 * hidden : 3 * hidden],
                b[:, 3 * hidden : 3 * hidden + ff],
                b[:, 3 * hidden + ff :],
            )
        )
    norms_of = [
        jnp.concatenate(
            [
                norm_gain_vector[1 + 2 * layer][None],
                norm_bias_vector[1 + 2 * layer][None],
                norm_gain_vector[2 + 2 * layer][None],
                norm_bias_vector[2 + 2 * layer][None],
                norm_gain_vector[-1][None],
                norm_bias_vector[-1][None],
            ],
            0,
        )
        for layer in range(layers)
    ]

    target_rows = rows[tokens:].astype(F32)
    segments = sentence_numbers[0]
    place_hot = (
        seg_positions(segments)[:, None]
        == jnp.arange(position_embedding.shape[0], dtype=jnp.int32)[None, :]
    ).astype(BF)
    hidden_rows = layer_norm(
        rows[:tokens].astype(F32)
        + jnp.dot(place_hot, position_embedding, preferred_element_type=F32),
        norm_gain_vector[0],
        norm_bias_vector[0],
    )
    seg_real = segments.astype(F32)
    seg_wide = jnp.broadcast_to(seg_real[:, None], (tokens, 128))
    seg_row = seg_real[None, :]
    place_row = label_positions
    place_col = jnp.broadcast_to(label_positions.reshape(labels, 1), (labels, 128))

    own_slice = lax.dynamic_slice_in_dim(embed, fsdp_index * slice_rows, slice_rows, 0)
    own_vocab = jnp.concatenate(
        [own_slice]
        + [
            lax.ppermute(own_slice, "dp", [(k, (k + shift) % dp_count) for k in range(dp_count)])
            for shift in range(1, dp_count)
        ],
        0,
    )
    own_bias = jnp.concatenate(
        [
            lax.dynamic_slice_in_dim(
                all_bias,
                ((dp_index - shift) % dp_count) * table_rows + fsdp_index * slice_rows,
                slice_rows,
                0,
            )
            for shift in range(dp_count)
        ]
    )
    vocab_block = (
        own_vocab,
        own_vocab.T,
        jnp.broadcast_to(own_bias[:, None], (own_bias.shape[0], 128)),
    )
    target_bias = all_bias[label_target_token[0]]
    hidden_rows, vocab_block = lax.optimization_barrier((hidden_rows, vocab_block))

    qkv, mid = project(hidden_rows, downs[0], in_weights[0], adapters[0], bias_of[0][0])
    context, logs = attend(qkv, seg_wide, seg_row)
    x_last, one, two, slope = after(
        context, hidden_rows, out_weights[0], *slabs[0], *bias_of[0][1:], norms_of[0]
    )
    *saved, features = last_forward(
        x_last, place_col, place_row, seg_wide, downs[1], in_weights[1], adapters[1], bias_of[1][0],
        out_weights[1], *slabs[1], *bias_of[1][1:], norms_of[1], head_full, head_dense_bias[None, :],
    )
    if grouped:
        mean_t, own_logs = head(features, *vocab_block)
    else:
        every = lax.all_gather(features, "fsdp", axis=0, tiled=True)
        means, local_logs = vocab(every, *vocab_block, labels)
        local_logs = local_logs.reshape(-1, labels)
        all_logs = lax.all_gather(local_logs, "fsdp", axis=0, tiled=False)
        whole_logs = jax.nn.logsumexp(all_logs, axis=0)
        scaled = (means * jnp.exp(local_logs - whole_logs)[:, None, :]).astype(BF)
        mean_t = lax.psum_scatter(scaled, "fsdp", scatter_dimension=0, tiled=True)[0].astype(F32)
        own_logs = lax.dynamic_index_in_dim(whole_logs, fsdp_index, 0, keepdims=False)
    targets = jnp.sum(features.astype(F32) * target_rows, 1) + target_bias
    own_loss = row_weight * jnp.sum(own_logs - targets)
    feat_grad = row_weight * (mean_t.T - target_rows)

    hidden_grad, dense_gradient, gq_last, gv_last = last_backward(
        feat_grad, saved, place_col, place_row, seg_wide, downs[1], in_weights[1], adapters[1],
        out_weights[1], *slabs[1], norms_of[1], head_full, rank,
    )
    back = (hidden_grad, one, two, slope, out_weights[0], *slabs[0], norms_of[0])
    if grouped:
        block = -(-head_rows * hidden // 2048) * 2048
        dense_parts = jnp.pad(
            dense_gradient.reshape(shards, -1).astype(BF), ((0, 0), (0, block - head_rows * hidden))
        ).reshape(shards, 16, block // 16)
        dctx, dense_sum = after_back_sum(*back, dense_parts, shards)
        dense_portion = dense_sum.reshape(-1)[: head_rows * hidden].reshape(head_rows, hidden)
    else:
        dctx = after_back(*back)
        dense_portion = lax.psum_scatter(dense_gradient, BOTH, scatter_dimension=0, tiled=True)
    gq_first, gv_first = attend_back(qkv, dctx, logs, seg_wide, seg_row, mid, rank)
    adapter_gradient = jnp.stack([gq_first, gv_first, gq_last, gv_last]).reshape(layers, 2, rank, hidden)
    if grouped:
        parts = adapter_gradient.reshape(-1, shards, up_part).transpose(1, 0, 2).reshape(shards, -1)
        block = -(-ups.size // 1024) * 1024
        parts = jnp.pad(parts, ((0, 0), (0, block - ups.size))).reshape(shards, block // 128, 128)
        own_parts, sums = tail(parts, dense_portion, jnp.broadcast_to(own_loss, (8, 128)), shards)
        adapter_portion = own_parts.reshape(-1)[: ups.size].reshape(adapter_up_matrix.shape)
        masked_task_loss, norm_square = sums[0, 0], sums[1, 0]
    else:
        adapter_portion = lax.psum_scatter(adapter_gradient, BOTH, scatter_dimension=3, tiled=True)
        squared_entries = jnp.sum(adapter_portion * adapter_portion) + jnp.sum(
            dense_portion * dense_portion
        )
        masked_task_loss, norm_square = lax.psum((own_loss, squared_entries), BOTH)
    gradient_norm = jnp.sqrt(norm_square)
    scale_factor = jnp.minimum(1.0, clip_limit / (gradient_norm + 1e-06))
    step_as_real = optimizer_step_count[0].astype(F32)
    adapter_new = optimizer_update(
        adapter_up_matrix,
        adapter_portion * scale_factor,
        adapter_moment_first,
        adapter_moment_second,
        step_as_real,
    )
    dense_new = optimizer_update(
        head_projection,
        dense_portion * scale_factor,
        head_moment_first,
        head_moment_second,
        step_as_real,
    )
    return (masked_task_loss, gradient_norm, *adapter_new, *dense_new)


def solution(mesh):
    rows = P(BOTH, None)
    in_specs = (
        rows,
        rows,
        rows,
        rows,
        P(BOTH),
        P(),
        P(),
        P("dp", None),
        P(),
        P(),
        P(),
        P(None, None, BOTH),
        P(None, None, BOTH),
        P(None, None, BOTH),
        P(None, BOTH, None),
        P(),
        P(),
        P(BOTH),
        P(),
        P(None, None, None, BOTH),
        P(None, None, None, BOTH),
        P(None, None, None, BOTH),
        rows,
        rows,
        rows,
    )
    adapter = P(None, None, None, BOTH)
    out_specs = (P(), P(), adapter, adapter, adapter, rows, rows, rows)
    return jax.shard_map(
        per_device, mesh=mesh, in_specs=in_specs, out_specs=out_specs, check_vma=False
    )
```

```python
import functools

import jax
import jax.numpy as jnp
from jax import lax
from jax.experimental import pallas as pl
from jax.experimental.pallas import tpu as pltpu
from jax.sharding import PartitionSpec as P

HEADS = 12
TASKS = 4
REACH = 128

norm_eps = 1e-05
adapter_scale = 2.0
clip_limit = 0.01
learn_rate = 0.05
beta_first = 0.9
beta_second = 0.999
adam_eps = 1e-08
decay_rate = 0.01
masked_score = -1e30

BF = jnp.bfloat16
F32 = jnp.float32
BOTH = ("dp", "fsdp")
VMEM_BYTES = 60 * 1024 * 1024


def mm(a, b):
    return lax.dot_general(a, b, (((1,), (0,)), ((), ())), preferred_element_type=F32)


def mm_nt(a, b):
    return lax.dot_general(a, b, (((1,), (1,)), ((), ())), preferred_element_type=F32)


def mm_tn(a, b):
    return lax.dot_general(a, b, (((0,), (0,)), ((), ())), preferred_element_type=F32)


def layer_norm(rows_in, gain, shift):
    center = rows_in - jnp.mean(rows_in, -1, keepdims=True)
    spread = jnp.mean(center * center, -1, keepdims=True)
    return center * lax.rsqrt(spread + norm_eps) * gain + shift


def norm_back(rows_in, gain, gradient):
    center = rows_in - jnp.mean(rows_in, -1, keepdims=True)
    inverse = lax.rsqrt(jnp.mean(center * center, -1, keepdims=True) + norm_eps)
    unit = center * inverse
    scaled = gradient * gain
    return inverse * (
        scaled
        - jnp.mean(scaled, -1, keepdims=True)
        - unit * jnp.mean(scaled * unit, -1, keepdims=True)
    )


def gelu_pair(v):
    size = jnp.abs(v) * 0.7071067811865476
    base = 1.0 + 0.3275911 * size
    t = pl.reciprocal(base, approx=True)
    t = t * (2.0 - base * t)
    bell = jnp.exp(-0.5 * v * v)
    poly = t * (
        0.127414796 + t * (-0.142248368 + t * (0.7107068705 + t * (-0.7265760135 + t * 0.5307027145)))
    )
    tail = poly * bell
    phi = jnp.where(v >= 0.0, 1.0 - tail, tail)
    return v * phi, phi + v * (bell * 0.3989422804014327)


def params(**more):
    return pltpu.CompilerParams(vmem_limit_bytes=VMEM_BYTES, **more)


def full(shape):
    return pl.BlockSpec(shape, lambda *_: (0,) * len(shape))


def split_of(total, most, step):
    size = (min(most, total) // step) * step
    while size > step and total % size:
        size -= step
    return size if size and total % size == 0 else total


def pair_rows(block, width):
    first = lax.broadcasted_iota(jnp.int32, block.shape, 1) < width
    return jnp.concatenate([jnp.where(first, block, 0.0), jnp.where(first, 0.0, block)], 0).astype(BF)


def pair_join(wide, width):
    rows = wide.shape[1] // 2
    return jnp.concatenate([wide[:width, :rows], wide[width:, rows:]], 0)


def masked(scores, same):
    rows = scores.shape[1] // 2
    return jnp.concatenate(
        [
            jnp.where(same, scores[:, :rows], masked_score),
            jnp.where(same, scores[:, rows:], masked_score),
        ],
        1,
    )


def project_body(
    own_ref, got_ref, mine_ref, spot_ref, spots_ref, norm_ref, down_ref, w_ref, up_ref, bias_ref,
    out_ref, mid_ref, x_ref,
):
    choose = lax.broadcasted_iota(jnp.int32, (own_ref.shape[0], spots_ref.shape[0]), 1) == spot_ref[...]
    summed = jnp.where(
        mine_ref[...] > 0, own_ref[...].astype(F32), got_ref[...].astype(F32)
    ) + mm(choose.astype(F32).astype(BF), spots_ref[...])
    x = layer_norm(summed, norm_ref[0:1, :], norm_ref[1:2, :])
    x_ref[...] = x
    low = x.astype(BF)
    mid = mm(low, down_ref[...]).astype(BF)
    mid_ref[...] = mid
    total = w_ref.shape[0]
    step = split_of(total, 768, 128)
    for start in range(0, total, step):
        part = slice(start, start + step)
        out_ref[:, part] = (
            mm_nt(low, w_ref[part, :]) + mm(mid, up_ref[:, part]) + bias_ref[:, part]
        ).astype(BF)


def project(own, got, mine, spot, spots, norms, down, w, up, bias):
    rows, width = mine.shape[0], own.shape[1]
    tile = split_of(rows, 256, 16)
    total = w.shape[0]
    row = lambda n: pl.BlockSpec((tile, n), lambda i: (i, 0))
    return pl.pallas_call(
        project_body,
        grid=(rows // tile,),
        in_specs=[row(width), row(width), row(1), row(1)]
        + [full(a.shape) for a in (spots, norms, down, w, up, bias)],
        out_specs=[row(total), row(down.shape[1]), row(width)],
        out_shape=[
            jax.ShapeDtypeStruct((rows, total), BF),
            jax.ShapeDtypeStruct((rows, down.shape[1]), BF),
            jax.ShapeDtypeStruct((rows, width), F32),
        ],
        compiler_params=params(),
        name="project",
    )(own, got, mine, spot, spots, norms, down, w, up, bias)


def attend_body(q_ref, k_ref, v_ref, seg_ref, seg_row_ref, ctx_ref, log_ref):
    rows = q_ref.shape[0]
    width = q_ref.shape[1] // 2
    scale = width**-0.5
    for start in range(0, rows, REACH):
        own = slice(start, start + REACH)
        near = slice(max(0, start - REACH), min(rows, start + 2 * REACH))
        queries = pair_rows(q_ref[own, :].astype(F32) * scale, width)
        same = seg_ref[near, :] == seg_row_ref[:, own]
        scores = masked(mm_nt(k_ref[near, :], queries), same)
        top = jnp.max(scores, 0, keepdims=True)
        weights = jnp.exp(scores - top)
        total = jnp.sum(weights, 0, keepdims=True)
        context = mm_tn(v_ref[near, :], weights.astype(BF)) * (1.0 / total)
        ctx_ref[own, :] = pair_join(context, width).T.astype(BF)
        log_ref[0, :, 2 * start : 2 * start + 2 * REACH] = top + jnp.log(total)


def attend(qkv, seg_wide, seg_row):
    rows, total = qkv.shape
    hidden = total // 3
    lanes = 2 * (hidden // HEADS)
    pairs = hidden // lanes
    column = lambda kind: pl.BlockSpec((rows, lanes), lambda p: (0, kind * pairs + p))
    return pl.pallas_call(
        attend_body,
        grid=(pairs,),
        in_specs=[column(0), column(1), column(2), full(seg_wide.shape), full(seg_row.shape)],
        out_specs=[
            pl.BlockSpec((rows, lanes), lambda p: (0, p)),
            pl.BlockSpec((1, 1, 2 * rows), lambda p: (p, 0, 0)),
        ],
        out_shape=[
            jax.ShapeDtypeStruct((rows, hidden), BF),
            jax.ShapeDtypeStruct((pairs, 1, 2 * rows), F32),
        ],
        compiler_params=params(),
        name="attend",
    )(qkv, qkv, qkv, seg_wide, seg_row)


def flat(ref):
    whole = ref[...]
    return whole.reshape(-1, whole.shape[-1])


def rows_of(ref, start, size):
    each = ref.shape[1]
    if size % each == 0 and start % each == 0 and each % 16 == 0:
        part = ref[start // each : (start + size) // each, :, :]
        return part.reshape(size, part.shape[-1])
    return flat(ref)[start : start + size, :]


def feed_step(ref):
    units = ref.shape[0] * ref.shape[1]
    step = ref.shape[1]
    while units % (2 * step) == 0 and 2 * step <= 768 and ref.shape[0] > 1:
        step *= 2
    return units, (step if ref.shape[0] > 1 else split_of(units, 768, 128))


def after_body(
    ctx_ref, x_ref, wo_ref, up_ref, down_ref, bo_ref, b1_ref, b2_ref, norm_ref,
    out_ref, one_ref, two_ref, slope_ref,
):
    one = x_ref[...] + (mm_nt(ctx_ref[...], wo_ref[...]) + bo_ref[...])
    one_ref[...] = one
    middle = layer_norm(one, norm_ref[0:1, :], norm_ref[1:2, :])
    low = middle.astype(BF)
    total = middle + b2_ref[...]
    units, step = feed_step(up_ref)
    for start in range(0, units, step):
        part = slice(start, start + step)
        act, slope = gelu_pair(mm_nt(low, rows_of(up_ref, start, step)) + b1_ref[:, part])
        slope_ref[:, part] = slope.astype(BF)
        total = total + mm(act.astype(BF), rows_of(down_ref, start, step))
    two_ref[...] = total
    out_ref[...] = layer_norm(total, norm_ref[2:3, :], norm_ref[3:4, :])


def slab_spec(slab):
    array, place, rows = slab
    return pl.BlockSpec((array.shape[0], rows, array.shape[2]), lambda *_: (0, place, 0))


def after(ctx, x, wo, up, down, bo, b1, b2, norms):
    rows, width = x.shape
    tile = split_of(rows, 256, 16)
    units = b1.shape[1]
    row = lambda n: pl.BlockSpec((tile, n), lambda i: (i, 0))
    return pl.pallas_call(
        after_body,
        grid=(rows // tile,),
        in_specs=[row(width), row(width), full(wo.shape), slab_spec(up), slab_spec(down)]
        + [full(a.shape) for a in (bo, b1, b2, norms)],
        out_specs=[row(width), row(width), row(width), row(units)],
        out_shape=[jax.ShapeDtypeStruct((rows, width), F32)] * 3
        + [jax.ShapeDtypeStruct((rows, units), BF)],
        compiler_params=params(),
        name="after",
    )(ctx, x, wo, up[0], down[0], bo, b1, b2, norms)


def exact_rows(choose, matrix):
    high = matrix.astype(BF)
    rest = matrix - high.astype(F32)
    middle = rest.astype(BF)
    low = (rest - middle.astype(F32)).astype(BF)
    return mm(choose, high) + mm(choose, middle) + mm(choose, low)


def last_forward_body(
    x_ref, place_ref, place_row_ref, seg_ref, down_ref, w_ref, adapt_ref, bias_ref, wo_ref, up_any, dn_any,
    bo_ref, b1_ref, b2_ref, norm_ref, hb_ref, hbias_ref,
    kv_ref, q_ref, mid_ref, log_ref, one_ref, slope_ref, two_ref, low_ref, act_ref, hslope_ref, feat_ref,
    up_ref, dn_ref, ctx_ref, sems, *, places,
):
    copies = []
    for k, (source, target, place) in enumerate(
        ((up_any, up_ref, places[0]), (dn_any, dn_ref, places[1]))
    ):
        rows = target.shape[1]
        copies.append(
            pltpu.make_async_copy(
                source.at[:, pl.ds(place * rows, rows), :], target, sems.at[k]
            )
        )
        copies[-1].start()
    rows, hidden = x_ref.shape
    labels = place_ref.shape[0]
    lanes = 2 * (hidden // HEADS)
    width = lanes // 2
    low = x_ref[...].astype(BF)
    mid = mm(low, down_ref[...]).astype(BF)
    mid_ref[...] = mid
    step = split_of(2 * hidden, 512, 128)
    for start in range(hidden, 3 * hidden, step):
        part = slice(start, start + step)
        kv_ref[:, start - hidden : start - hidden + step] = (
            mm_nt(low, w_ref[part, :]) + mm(mid, adapt_ref[:, part]) + bias_ref[:, part]
        ).astype(BF)
    choose = (
        lax.broadcasted_iota(jnp.int32, (labels, rows), 1) == place_ref[...][:, 0:1]
    ).astype(F32).astype(BF)
    own = exact_rows(choose, x_ref[...])
    own_low = own.astype(BF)
    own_mid = mm(choose, mid).astype(BF)
    q_ref[...] = (
        mm_nt(own_low, w_ref[:hidden, :]) + mm(own_mid, adapt_ref[:, :hidden]) + bias_ref[:, :hidden]
    ).astype(BF)
    seg = seg_ref[...]
    seg_own = jnp.sum(
        jnp.where(
            lax.broadcasted_iota(jnp.int32, (rows, labels), 0) == place_row_ref[...], seg, 0.0
        ),
        0,
        keepdims=True,
    )
    same = seg == seg_own
    for p in range(hidden // lanes):
        part = slice(p * lanes, (p + 1) * lanes)
        queries = pair_rows(q_ref[:, part].astype(F32) * width**-0.5, width)
        scores = masked(mm_nt(kv_ref[:, part], queries), same)
        top = jnp.max(scores, 0, keepdims=True)
        weights = jnp.exp(scores - top)
        total = jnp.sum(weights, 0, keepdims=True)
        context = mm_tn(
            kv_ref[:, hidden + p * lanes : hidden + (p + 1) * lanes], weights.astype(BF)
        ) * (1.0 / total)
        ctx_ref[:, part] = pair_join(context, width).T.astype(BF)
        log_ref[p : p + 1, :] = top + jnp.log(total)
    one = own + (mm_nt(ctx_ref[...], wo_ref[...]) + bo_ref[...])
    one_ref[...] = one
    middle = layer_norm(one, norm_ref[0:1, :], norm_ref[1:2, :])
    middle_low = middle.astype(BF)
    sum_two = middle + b2_ref[...]
    units, step = feed_step(up_ref)
    for copy in copies:
        copy.wait()
    for start in range(0, units, step):
        part = slice(start, start + step)
        act, slope = gelu_pair(mm_nt(middle_low, rows_of(up_ref, start, step)) + b1_ref[:, part])
        slope_ref[:, part] = slope.astype(BF)
        sum_two = sum_two + mm(act.astype(BF), rows_of(dn_ref, start, step))
    two_ref[...] = sum_two
    out_low = layer_norm(sum_two, norm_ref[2:3, :], norm_ref[3:4, :]).astype(BF)
    low_ref[...] = out_low
    act, slope = gelu_pair(mm(out_low, hb_ref[...]) + hbias_ref[...])
    act_ref[...] = act
    hslope_ref[...] = slope
    feat_ref[...] = layer_norm(act, norm_ref[4:5, :], norm_ref[5:6, :]).astype(BF)


def slab_scratch(slab):
    array, place, rows = slab
    return pltpu.VMEM((array.shape[0], rows, array.shape[2]), BF)


def last_forward(x, place_col, place_row, seg_wide, down, w, adapt, bias, wo, up, dn, bo, b1, b2, norms, hb, hbias):
    rows, hidden = x.shape
    labels = place_col.shape[0]
    units = b1.shape[1]
    whole = pl.BlockSpec(memory_space=pltpu.VMEM)
    anywhere = pl.BlockSpec(memory_space=pl.ANY)
    shape = jax.ShapeDtypeStruct
    pairs = HEADS // 2
    return pl.pallas_call(
        functools.partial(last_forward_body, places=(up[1], dn[1])),
        in_specs=[whole] * 9 + [anywhere] * 2 + [whole] * 6,
        out_specs=[whole] * 11,
        out_shape=[
            shape((rows, 2 * hidden), BF),
            shape((labels, hidden), BF),
            shape((rows, down.shape[1]), BF),
            shape((pairs, 2 * labels), F32),
            shape((labels, hidden), F32),
            shape((labels, units), BF),
            shape((labels, hidden), F32),
            shape((labels, hidden), BF),
            shape((labels, hidden), F32),
            shape((labels, hidden), F32),
            shape((labels, hidden), BF),
        ],
        scratch_shapes=[
            slab_scratch(up),
            slab_scratch(dn),
            pltpu.VMEM((labels, hidden), BF),
            pltpu.SemaphoreType.DMA((2,)),
        ],
        compiler_params=params(),
        name="last_forward",
    )(x, place_col, place_row, seg_wide, down, w, adapt, bias, wo, up[0], dn[0], bo, b1, b2, norms, hb, hbias)


def vocab_body(u_ref, e_ref, et_ref, bias_ref, num_ref, log_ref, scores, weights):
    count = e_ref.shape[0]
    step = split_of(count, 640, 16)
    u = u_ref[...]
    rows = u.shape[0]
    labels = num_ref.shape[2]
    top = jnp.full((1, rows), -jnp.inf, F32)
    for start in range(0, count, step):
        part = slice(start, start + step)
        bias = bias_ref[part, :]
        logits = mm_nt(e_ref[part, :], u) + jnp.concatenate([bias] * (rows // bias.shape[1]), 1)
        scores[part, :] = logits
        top = jnp.maximum(top, jnp.max(logits, 0, keepdims=True))
    total = jnp.zeros((1, rows), F32)
    for start in range(0, count, step):
        part = slice(start, start + step)
        grown = jnp.exp(scores[part, :] - top)
        total = total + jnp.sum(grown, 0, keepdims=True)
        weights[part, :] = grown.astype(BF)
    mean = mm(et_ref[...], weights[...]) * (1.0 / total)
    logs = top + jnp.log(total)
    for k in range(rows // labels):
        num_ref[k, :, :] = mean[:, k * labels : (k + 1) * labels]
        log_ref[k, :, :] = logs[:, k * labels : (k + 1) * labels]


def vocab(u, e, et, bias_wide, labels):
    rows, hidden = u.shape
    count = e.shape[0]
    tile = 2 * labels
    return pl.pallas_call(
        vocab_body,
        grid=(rows // tile,),
        in_specs=[
            pl.BlockSpec((tile, hidden), lambda i: (i, 0)),
            full(e.shape),
            full(et.shape),
            full(bias_wide.shape),
        ],
        out_specs=[
            pl.BlockSpec((2, hidden, labels), lambda i: (i, 0, 0)),
            pl.BlockSpec((2, 1, labels), lambda i: (i, 0, 0)),
        ],
        out_shape=[
            jax.ShapeDtypeStruct((rows // labels, hidden, labels), F32),
            jax.ShapeDtypeStruct((rows // labels, 1, labels), F32),
        ],
        scratch_shapes=[pltpu.VMEM((count, tile), F32), pltpu.VMEM((count, tile), BF)],
        compiler_params=params(),
        name="vocab",
    )(u, e, et, bias_wide)


def last_backward_body(
    du_ref, kv_ref, q_ref, mid_ref, log_ref, one_ref, slope_ref, two_ref, low_ref, act_ref, hslope_ref,
    place_ref, place_row_ref, seg_ref, down_ref, w_ref, adapt_ref, wo_ref, up_any, dn_any, norm_ref, hb_ref,
    dx_ref, gh_ref, gq_ref, gv_ref,
    up_ref, dn_ref, dkv_ref, dq_ref, sems, *, places, rank,
):
    copies = []
    for k, (source, target, place) in enumerate(
        ((up_any, up_ref, places[0]), (dn_any, dn_ref, places[1]))
    ):
        rows = target.shape[1]
        copies.append(
            pltpu.make_async_copy(
                source.at[:, pl.ds(place * rows, rows), :], target, sems.at[k]
            )
        )
        copies[-1].start()
    rows = kv_ref.shape[0]
    labels, hidden = du_ref.shape
    lanes = 2 * (hidden // HEADS)
    width = lanes // 2
    scale = width**-0.5
    dact = norm_back(act_ref[...], norm_ref[4:5, :], du_ref[...])
    dz = (hslope_ref[...] * dact).astype(BF)
    gh_ref[...] = mm_tn(low_ref[...], dz)
    dtwo = norm_back(two_ref[...], norm_ref[2:3, :], mm_nt(dz, hb_ref[...]))
    dtwo_low = dtwo.astype(BF)
    dmiddle = dtwo
    units, step = feed_step(up_ref)
    for copy in copies:
        copy.wait()
    for start in range(0, units, step):
        part = slice(start, start + step)
        dgate = (
            slope_ref[:, part].astype(F32) * mm_nt(dtwo_low, rows_of(dn_ref, start, step))
        ).astype(BF)
        dmiddle = dmiddle + mm(dgate, rows_of(up_ref, start, step))
    done = norm_back(one_ref[...], norm_ref[0:1, :], dmiddle)
    dctx = mm(done.astype(BF), wo_ref[...]).astype(BF)
    seg = seg_ref[...]
    choose_t = lax.broadcasted_iota(jnp.int32, (rows, labels), 0) == place_row_ref[...]
    same = seg == jnp.sum(jnp.where(choose_t, seg, 0.0), 0, keepdims=True)
    for p in range(hidden // lanes):
        part = slice(p * lanes, (p + 1) * lanes)
        later = slice(hidden + p * lanes, hidden + (p + 1) * lanes)
        queries = pair_rows(q_ref[:, part].astype(F32) * scale, width)
        outs = pair_rows(dctx[:, part].astype(F32), width)
        keys = kv_ref[:, part]
        weights = jnp.exp(masked(mm_nt(keys, queries), same) - log_ref[p : p + 1, :])
        dweights = mm_nt(kv_ref[:, later], outs)
        inner = jnp.sum(dweights * weights, 0, keepdims=True)
        dscores = (weights * (dweights - inner)).astype(BF)
        dkv_ref[:, part] = mm(dscores, queries).astype(BF)
        dkv_ref[:, later] = mm(weights.astype(BF), outs).astype(BF)
        dq_ref[:, part] = (pair_join(mm_tn(keys, dscores), width) * scale).T.astype(BF)
    dq = dq_ref[...]
    own_mid = mm(
        (lax.broadcasted_iota(jnp.int32, (labels, rows), 1) == place_ref[...][:, 0:1]).astype(F32).astype(BF),
        mid_ref[...],
    ).astype(BF)
    gq_ref[...] = adapter_scale * mm_tn(own_mid, dq)[:rank, :]
    gv_ref[...] = adapter_scale * mm_tn(mid_ref[...], dkv_ref[:, hidden:])[rank : 2 * rank, :]
    dmid_own = mm_nt(dq, adapt_ref[:, :hidden]).astype(BF)
    own = done + mm(dq, w_ref[:hidden, :]) + mm_nt(dmid_own, down_ref[...])
    spread = choose_t.astype(F32).astype(BF)
    own_high = own.astype(BF)
    own_rest = (own - own_high.astype(F32)).astype(BF)
    dmid = mm_nt(dkv_ref[:, hidden:], adapt_ref[:, 2 * hidden :]).astype(BF)
    step = split_of(hidden, 256, 128)
    for start in range(0, hidden, step):
        part = slice(start, start + step)
        dx_ref[:, part] = (
            mm(dkv_ref[...], w_ref[hidden:, part])
            + mm_nt(dmid, down_ref[part, :])
            + mm(spread, own_high[:, part])
            + mm(spread, own_rest[:, part])
        )


def last_backward(du, saved, place_col, place_row, seg_wide, down, w, adapt, wo, up, dn, norms, hb, rank):
    kv = saved[0]
    rows = kv.shape[0]
    labels, hidden = du.shape
    whole = pl.BlockSpec(memory_space=pltpu.VMEM)
    anywhere = pl.BlockSpec(memory_space=pl.ANY)
    shape = jax.ShapeDtypeStruct
    return pl.pallas_call(
        functools.partial(last_backward_body, places=(up[1], dn[1]), rank=rank),
        in_specs=[whole] * 18 + [anywhere] * 2 + [whole] * 2,
        out_specs=[whole] * 4,
        out_shape=[
            shape((rows, hidden), F32),
            shape((hidden, hidden), F32),
            shape((rank, hidden), F32),
            shape((rank, hidden), F32),
        ],
        scratch_shapes=[
            slab_scratch(up),
            slab_scratch(dn),
            pltpu.VMEM(kv.shape, BF),
            pltpu.VMEM((labels, hidden), BF),
            pltpu.SemaphoreType.DMA((2,)),
        ],
        compiler_params=params(),
        name="last_backward",
    )(du, *saved, place_col, place_row, seg_wide, down, w, adapt, wo, up[0], dn[0], norms, hb)


def after_back_sum_body(shards, *refs):
    *plain, parts, dctx_ref, sum_ref, got, sends, gets = refs
    step, last = pl.program_id(0), pl.num_programs(0) - 1
    me = number_of(position())

    @pl.when(step == 0)
    def _():
        greet_all(shards)
        got[me] = parts[me]

    @pl.when(step == jnp.minimum(1, last))
    def _():
        await_all(shards)
        spread(lambda peer: parts.at[peer], got, sends, gets, me, shards)

    after_back_body(*plain, dctx_ref)

    @pl.when(step == last)
    def _():
        collect(lambda peer: parts.at[peer], got, sends, gets, me, shards)
        total = got[0].astype(F32)
        for k in range(1, shards):
            total = total + got[k].astype(F32)
        sum_ref[...] = total


def after_back_body(dout_ref, one_ref, two_ref, slope_ref, wo_ref, up_ref, down_ref, norm_ref, dctx_ref):
    dtwo = norm_back(two_ref[...], norm_ref[2:3, :], dout_ref[...])
    low = dtwo.astype(BF)
    dmiddle = dtwo
    units, step = feed_step(up_ref)
    for start in range(0, units, step):
        part = slice(start, start + step)
        dgate = (
            slope_ref[:, part].astype(F32) * mm_nt(low, rows_of(down_ref, start, step))
        ).astype(BF)
        dmiddle = dmiddle + mm(dgate, rows_of(up_ref, start, step))
    done = norm_back(one_ref[...], norm_ref[0:1, :], dmiddle)
    dctx_ref[...] = mm(done.astype(BF), wo_ref[...]).astype(BF)


def after_back_sum(dout, one, two, slope, wo, up, down, norms, parts, shards):
    rows, width = dout.shape
    tile = split_of(rows, 256, 16)
    row = lambda n: pl.BlockSpec((tile, n), lambda i: (i, 0))
    sems = pltpu.SemaphoreType.DMA
    return pl.pallas_call(
        functools.partial(after_back_sum_body, shards),
        grid=(rows // tile,),
        in_specs=[row(width), row(width), row(width), row(slope.shape[1]), full(wo.shape)]
        + [slab_spec(up), slab_spec(down), full(norms.shape), full(parts.shape)],
        out_specs=[row(width), full(parts.shape[1:])],
        out_shape=[
            jax.ShapeDtypeStruct((rows, width), BF),
            jax.ShapeDtypeStruct(parts.shape[1:], F32),
        ],
        scratch_shapes=[pltpu.VMEM(parts.shape, BF), sems((shards,)), sems((shards,))],
        compiler_params=params(collective_id=3, has_side_effects=True),
        name="after_back_sum",
    )(dout, one, two, slope, wo, up[0], down[0], norms, parts)


def after_back(dout, one, two, slope, wo, up, down, norms):
    rows, width = dout.shape
    tile = split_of(rows, 256, 16)
    row = lambda n: pl.BlockSpec((tile, n), lambda i: (i, 0))
    return pl.pallas_call(
        after_back_body,
        grid=(rows // tile,),
        in_specs=[row(width), row(width), row(width), row(slope.shape[1]), full(wo.shape)]
        + [slab_spec(up), slab_spec(down), full(norms.shape)],
        out_specs=row(width),
        out_shape=jax.ShapeDtypeStruct((rows, width), BF),
        compiler_params=params(),
        name="after_back",
    )(dout, one, two, slope, wo, up[0], down[0], norms)


def attend_back_body(
    q_ref, k_ref, v_ref, dctx_ref, log_ref, seg_ref, seg_row_ref, mid_ref, gq_ref, gv_ref, dv_ref
):
    rows = q_ref.shape[0]
    width = q_ref.shape[1] // 2
    scale = width**-0.5
    rank = gq_ref.shape[0]
    dv_ref[...] = jnp.zeros_like(dv_ref)
    gq = jnp.zeros((2 * width, mid_ref.shape[1]), F32)
    for start in range(0, rows, REACH):
        own = slice(start, start + REACH)
        near = slice(max(0, start - REACH), min(rows, start + 2 * REACH))
        queries = pair_rows(q_ref[own, :].astype(F32) * scale, width)
        outs = pair_rows(dctx_ref[own, :].astype(F32), width)
        same = seg_ref[near, :] == seg_row_ref[:, own]
        keys = k_ref[near, :]
        logs = log_ref[0, :, 2 * start : 2 * start + 2 * REACH]
        weights = jnp.exp(masked(mm_nt(keys, queries), same) - logs)
        dweights = mm_nt(v_ref[near, :], outs)
        inner = jnp.sum(dweights * weights, 0, keepdims=True)
        dscores = (weights * (dweights - inner)).astype(BF)
        dv_ref[near, :] += mm(weights.astype(BF), outs)
        dq = (pair_join(mm_tn(keys, dscores), width) * scale).astype(BF)
        gq = gq + mm(dq, mid_ref[own, :])
    gq_ref[...] = adapter_scale * gq.T[:rank, :]
    gv_ref[...] = adapter_scale * mm_tn(mid_ref[...], dv_ref[...].astype(BF))[rank : 2 * rank, :]


def attend_back(qkv, dctx, logs, seg_wide, seg_row, mid, rank):
    rows, total = qkv.shape
    hidden = total // 3
    lanes = 2 * (hidden // HEADS)
    pairs = hidden // lanes
    column = lambda kind: pl.BlockSpec((rows, lanes), lambda p: (0, kind * pairs + p))
    return pl.pallas_call(
        attend_back_body,
        grid=(pairs,),
        in_specs=[
            column(0),
            column(1),
            column(2),
            column(0),
            pl.BlockSpec((1, 1, 2 * rows), lambda p: (p, 0, 0)),
            full(seg_wide.shape),
            full(seg_row.shape),
            full(mid.shape),
        ],
        out_specs=[pl.BlockSpec((rank, lanes), lambda p: (0, p))] * 2,
        out_shape=[jax.ShapeDtypeStruct((rank, hidden), F32)] * 2,
        scratch_shapes=[pltpu.VMEM((rows, lanes), F32)],
        compiler_params=params(),
        name="attend_back",
    )(qkv, qkv, qkv, dctx, logs, seg_wide, seg_row, mid)


MESH = pl.DeviceIdType.MESH


def position():
    dp, fsdp = lax.axis_index("dp"), lax.axis_index("fsdp")
    return {"x": dp, "z": fsdp // 4, "y": (fsdp // 2) % 2, "c": fsdp % 2}


def device_of(place):
    return (place["x"], (place["z"] * 2 + place["y"]) * 2 + place["c"])


def number_of(place):
    return place["x"] * 16 + (place["z"] * 2 + place["y"]) * 2 + place["c"]


def rank_device(number):
    return (number // 16, number % 16)


def greet_all(shards):
    barrier = pltpu.get_barrier_semaphore()
    me = lax.axis_index("dp") * 16 + lax.axis_index("fsdp")

    @pl.loop(1, shards)
    def _(k):
        pl.semaphore_signal(
            barrier, inc=1, device_id=rank_device((me + k) % shards), device_id_type=MESH
        )


def await_all(shards):
    pl.semaphore_wait(pltpu.get_barrier_semaphore(), shards - 1)


def direct_copy(source, target, sends, receives, me, k, shards):
    return pltpu.make_async_remote_copy(
        src_ref=source,
        dst_ref=target,
        send_sem=sends.at[k],
        recv_sem=receives.at[me],
        device_id=rank_device((me + k) % shards),
        device_id_type=MESH,
    )


def spread(piece_of, buffer, sends, receives, me, shards):
    @pl.loop(1, shards)
    def _(k):
        direct_copy(piece_of((me + k) % shards), buffer.at[me], sends, receives, me, k, shards).start()


def collect(piece_of, buffer, sends, receives, me, shards):
    @pl.loop(1, shards)
    def _(k):
        source = (me + shards - k) % shards
        direct_copy(buffer.at[source], buffer.at[source], sends, receives, source, k, shards).wait_recv()

    @pl.loop(1, shards)
    def _(k):
        direct_copy(piece_of((me + k) % shards), buffer.at[me], sends, receives, me, k, shards).wait_send()


def relative_places(order):
    places = [
        {"x": dx, "z": dz, "y": dy} for dx in (0, 1) for dz in range(-3, 4) for dy in (0, 1)
    ]
    return sorted(places, key=lambda p: (abs(p["x"]) + abs(p["z"]) + abs(p["y"]), [abs(p[a]) for a in order]))


class Gather:
    def __init__(self, chunk, full_buffer, start, rows, order, sends, receives, hands, hands_got):
        self.chunk, self.full, self.order = chunk, full_buffer, order
        self.part = pl.ds(start, rows)
        self.sends, self.receives, self.hands, self.hands_got = sends, receives, hands, hands_got
        self.here = position()
        self.items = relative_places(order)
        self.pending = []

    def origin(self, item):
        here = self.here
        return {"x": (here["x"] + item["x"]) % 2, "z": here["z"] - item["z"], "y": (here["y"] + item["y"]) % 2, "c": here["c"]}

    def key(self, place):
        return (place["x"] * 4 + place["z"]) * 2 + place["y"]

    def outward(self, item):
        deepest = max([k for k, axis in enumerate(self.order) if item[axis]], default=-1)
        ways = []
        if deepest >= 0 and self.order[deepest] == "z":
            ways.append(("z", 1 if item["z"] > 0 else -1))
        for axis in self.order[deepest + 1 :]:
            ways += [("z", 1), ("z", -1)] if axis == "z" else [(axis, 1)]
        return ways

    def copy(self, index, way, slot, item):
        here = self.here
        place = self.origin(item)
        number, key = number_of(place), self.key(place)
        mine = not any(item.values())
        source = self.chunk.at[self.part, :] if mine else self.full.at[number, self.part, :]
        if way is None:
            target = dict(here, c=1 - here["c"])
            sends, receives = self.hands.at[index], self.hands_got.at[key]
        else:
            axis, step = way
            target = dict(here)
            target[axis] = here["z"] + step if axis == "z" else 1 - here[axis]
            sends, receives = self.sends.at[index * 4 + slot], self.receives.at[key]
        return pltpu.make_async_remote_copy(
            src_ref=source,
            dst_ref=self.full.at[number, self.part, :],
            send_sem=sends,
            recv_sem=receives,
            device_id=device_of(target),
            device_id_type=MESH,
        )

    def valid(self, item):
        z = self.here["z"] - item["z"]
        return (z >= 0) & (z <= 3)

    def step(self, index):
        item = self.items[index]

        @pl.when(self.valid(item))
        def _():
            if any(item.values()):
                self.arrived(index, item)
            for slot, way in enumerate(self.outward(item)):
                self.when_way(way, lambda way=way, slot=slot: self.copy(index, way, slot, item).start())
            self.copy(index, None, 0, item).start()

    def when_way(self, way, act):
        axis, step = way
        if axis == "z":
            z = self.here["z"] + step
            pl.when((z >= 0) & (z <= 3))(act)
        else:
            act()

    def arrived(self, index, item):
        place = self.origin(item)
        spot = self.full.at[number_of(place), self.part, :]
        pltpu.make_async_remote_copy(
            src_ref=spot,
            dst_ref=spot,
            send_sem=self.sends.at[index * 4],
            recv_sem=self.receives.at[self.key(place)],
            device_id=device_of(dict(self.here, c=1 - self.here["c"])),
            device_id_type=MESH,
        ).wait_recv()

    def finish(self):
        for index, item in enumerate(self.items):

            @pl.when(self.valid(item))
            def _(index=index, item=item):
                for slot, way in enumerate(self.outward(item)):
                    self.when_way(way, lambda way=way, slot=slot: self.copy(index, way, slot, item).wait_send())
                self.copy(index, None, 0, item).wait_send()
                place = dict(self.origin(item), c=1 - self.here["c"])
                spot = self.full.at[number_of(place), self.part, :]
                pltpu.make_async_remote_copy(
                    src_ref=spot,
                    dst_ref=spot,
                    send_sem=self.hands.at[index],
                    recv_sem=self.hands_got.at[self.key(place)],
                    device_id=device_of(dict(self.here, c=1 - self.here["c"])),
                    device_id_type=MESH,
                ).wait_recv()


ITEMS = 28


ITEMS = 28
PICK = 64
GROUP = 16


def start_body(
    streams, shards, ids, low_ref, groups_any, table_any, chunk, note, bias,
    full_chunk, own_rows, got, notes, biases, e_out, et_out,
    table, stage, rows, e_ref, et_ref,
    sends, receives, hands, hands_got, row_sends, row_gets, note_sends, note_gets, bias_sends, bias_gets,
    own_sems, e_sems, out_sems,
):
    here = position()
    me = number_of(here)
    across = device_of(dict(here, x=1 - here["x"]))
    slice_rows = e_ref.shape[0] // 2
    half = own_rows.shape[0]
    batches = half // PICK
    fill = pltpu.make_async_copy(groups_any, table, own_sems.at[3])
    fill.start()
    greet_all(shards)
    plain = [
        pltpu.make_async_copy(source, target, own_sems.at[k])
        for k, (source, target) in enumerate(
            ((chunk, full_chunk.at[me]), (note, notes.at[me]), (bias, biases.at[me]))
        )
    ]
    for copy in plain:
        copy.start()
    own_slice = table_any.at[
        pl.ds(pl.multiple_of((me % 16) * slice_rows, 16), slice_rows), :
    ]
    keep = pltpu.make_async_copy(own_slice, e_ref.at[pl.ds(0, slice_rows), :], own_sems.at[4])
    keep.start()
    swap = pltpu.make_async_remote_copy(
        src_ref=own_slice,
        dst_ref=e_ref.at[pl.ds(slice_rows, slice_rows), :],
        send_sem=e_sems.at[0],
        recv_sem=e_sems.at[1],
        device_id=across,
        device_id_type=MESH,
    )
    await_all(shards)
    gathers = [
        Gather(
            chunk, full_chunk, start, size, order, sends.at[k], receives.at[k], hands.at[k], hands_got.at[k]
        )
        for k, (start, size, order) in enumerate(streams)
    ]
    for gather in gathers:
        gather.step(0)
    spread(lambda peer: note, notes, note_sends, note_gets, me, shards)
    spread(lambda peer: bias, biases, bias_sends, bias_gets, me, shards)
    swap.start()

    def send_rows(b):
        part = pl.ds(b * PICK, PICK)
        return pltpu.make_async_remote_copy(
            src_ref=rows.at[part, :],
            dst_ref=got.at[part, :],
            send_sem=row_sends.at[b],
            recv_sem=row_gets.at[b],
            device_id=across,
            device_id_type=MESH,
        )

    def pick(b):
        def one(t, carry):
            stage[t] = table[ids[b * PICK + t]]
            return carry

        lax.fori_loop(0, PICK, one, 0, unroll=8)
        choose = (
            lax.broadcasted_iota(jnp.int32, (PICK, PICK * GROUP), 1)
            == low_ref[b * PICK : (b + 1) * PICK, :]
        )
        rows[b * PICK : (b + 1) * PICK, :] = mm(choose.astype(F32).astype(BF), flat(stage)).astype(BF)
        if b < batches:
            send_rows(b).start()

    def turn(k):
        part = slice(k * 128, (k + 1) * 128)
        et_ref[:, part] = e_ref[part, :].astype(F32).T.astype(BF)

    def out_copies():
        return (
            pltpu.make_async_copy(e_ref, e_out, out_sems.at[0]),
            pltpu.make_async_copy(et_ref, et_out, out_sems.at[1]),
            pltpu.make_async_copy(rows.at[pl.ds(half, half), :], own_rows, out_sems.at[2]),
        )

    fill.wait()
    done, turned = 0, 0
    own_turns = slice_rows // 128
    for index in range(1, ITEMS):
        while done < 2 * batches and done < index * 3:
            pick(done)
            done += 1
        if done == 2 * batches and turned < own_turns:
            if turned == 0:
                keep.wait()
            turn(turned)
            turned += 1
        for gather in gathers:
            gather.step(index)
    swap.wait_recv()
    for k in range(turned, e_ref.shape[0] // 128):
        turn(k)
    copies = out_copies()
    for copy in copies:
        copy.start()
    for gather in gathers:
        gather.finish()
    collect(lambda peer: note, notes, note_sends, note_gets, me, shards)
    collect(lambda peer: bias, biases, bias_sends, bias_gets, me, shards)
    for b in range(batches):
        send_rows(b).wait()
    swap.wait_send()
    for copy in plain:
        copy.wait()
    for copy in copies:
        copy.wait()


def start_exchange(ids, low, table, chunk, note, bias, shards, slice_rows):
    anywhere = pl.BlockSpec(memory_space=pl.ANY)
    cut = (chunk.shape[0] * 5 // 6 + 15) // 16 * 16
    streams = ((0, cut, "xzy"), (cut, chunk.shape[0] - cut, "xyz"))
    half = ids.shape[0] // 2
    hidden = table.shape[1]
    shape = jax.ShapeDtypeStruct
    sems = pltpu.SemaphoreType.DMA
    return pl.pallas_call(
        functools.partial(start_body, streams, shards),
        in_specs=[
            pl.BlockSpec(memory_space=pltpu.SMEM),
            pl.BlockSpec(memory_space=pltpu.VMEM),
        ]
        + [anywhere] * 5,
        out_specs=[anywhere] * 7,
        out_shape=[
            shape((shards, *chunk.shape), chunk.dtype),
            shape((half, hidden), table.dtype),
            shape((half, hidden), table.dtype),
            shape((shards, *note.shape), note.dtype),
            shape((shards, *bias.shape), bias.dtype),
            shape((2 * slice_rows, hidden), table.dtype),
            shape((hidden, 2 * slice_rows), table.dtype),
        ],
        scratch_shapes=[
            pltpu.VMEM((table.shape[0] // GROUP, GROUP, hidden), BF),
            pltpu.VMEM((PICK, GROUP, hidden), BF),
            pltpu.VMEM((2 * half, hidden), BF),
            pltpu.VMEM((2 * slice_rows, hidden), BF),
            pltpu.VMEM((hidden, 2 * slice_rows), BF),
            sems((2, 4 * ITEMS)),
            sems((2, 16)),
            sems((2, ITEMS)),
            sems((2, 16)),
            sems((half // PICK,)),
            sems((half // PICK,)),
            sems((shards,)),
            sems((shards,)),
            sems((shards,)),
            sems((shards,)),
            sems((5,)),
            sems((2,)),
            sems((3,)),
        ],
        compiler_params=params(collective_id=1, has_side_effects=True),
        name="start_exchange",
    )(ids, low, table.reshape(-1, GROUP, hidden), table, chunk, note, bias)


def tail_body(shards, parts, dense, loss, total_ref, sums_ref, got, note, notes, send_a, get_a, send_b, get_b):
    me = number_of(position())
    greet_all(shards)
    got[me] = parts[me]
    await_all(shards)
    spread(lambda peer: parts.at[peer], got, send_a, get_a, me, shards)
    dense_square = jnp.sum(dense[...] * dense[...], keepdims=True)
    collect(lambda peer: parts.at[peer], got, send_a, get_a, me, shards)
    total = got[0]
    for k in range(1, shards):
        total = total + got[k]
    total_ref[...] = total
    square = dense_square + jnp.sum(total * total, keepdims=True)
    row = lax.broadcasted_iota(jnp.int32, note.shape, 0)
    note[...] = jnp.where(row == 0, loss[...], jnp.where(row == 1, square, 0.0))
    notes[me] = note[...]
    spread(lambda peer: note, notes, send_b, get_b, me, shards)
    collect(lambda peer: note, notes, send_b, get_b, me, shards)
    total = notes[0]
    for k in range(1, shards):
        total = total + notes[k]
    sums_ref[...] = total


def tail(parts, dense, loss, shards):
    whole = pl.BlockSpec(memory_space=pltpu.VMEM)
    block = parts.shape[1:]
    shape = jax.ShapeDtypeStruct
    sems = pltpu.SemaphoreType.DMA
    return pl.pallas_call(
        functools.partial(tail_body, shards),
        in_specs=[whole] * 3,
        out_specs=[whole] * 2,
        out_shape=[shape(block, F32), shape((8, 128), F32)],
        scratch_shapes=[
            pltpu.VMEM(parts.shape, F32),
            pltpu.VMEM((8, 128), F32),
            pltpu.VMEM((shards, 8, 128), F32),
        ]
        + [sems((shards,))] * 4,
        compiler_params=params(collective_id=2, has_side_effects=True),
        name="tail",
    )(parts, dense, loss)


HOPS = 3
LOG_ROWS = 16


def flip(z, k):
    return (z % 2 + k % 2) % 2 + 2 * ((z // 2 + k // 2) % 2)


def pack_log(log_row, rows):
    high = log_row.astype(BF).astype(F32)
    middle = (log_row - high).astype(BF).astype(F32)
    low = log_row - high - middle
    row = lax.broadcasted_iota(jnp.int32, (rows, log_row.shape[1]), 0)
    return jnp.where(
        row == 0, high, jnp.where(row == 1, middle, jnp.where(row == 2, low, 0.0))
    ).astype(BF)


def unpack(block, hidden):
    logs = block[hidden : hidden + LOG_ROWS, :].astype(F32)
    return block[:hidden, :].astype(F32), jnp.sum(logs, 0, keepdims=True)


def merged(one, two):
    top = jnp.maximum(one[1], two[1])
    first, second = jnp.exp(one[1] - top), jnp.exp(two[1] - top)
    total = first + second
    inverse = 1.0 / total
    return one[0] * (first * inverse) + two[0] * (second * inverse), top + jnp.log(total)


def store_packed(ref, pair, hidden):
    ref[:hidden, :] = pair[0].astype(BF)
    ref[hidden : hidden + LOG_ROWS, :] = pack_log(pair[1], LOG_ROWS)


def head_body(
    u_ref, e_any, et_any, bias_any, mean_ref, log_ref,
    e_ref, et_ref, bias_ref, feats, packs, handed, crossed, kept, lined, zouts,
    loads, z_send, z_get, y_send, y_get, c_send, c_get, h_send, h_get, p_send, p_get, l_send, l_get,
):
    here = position()
    z, y, c = here["z"], here["y"], here["c"]
    labels, hidden = u_ref.shape
    slot_of = lambda zz, yy, cc: (zz * 2 + yy) * 2 + cc
    me = slot_of(z, y, c)
    sibling = device_of(dict(here, c=1 - c))
    beside = device_of(dict(here, y=1 - y))
    at_z = lambda zz: device_of(dict(here, z=zz))
    inside = lambda zz: (zz >= 0) & (zz <= HOPS)

    fills = [
        pltpu.make_async_copy(source, target, loads.at[k])
        for k, (source, target) in enumerate(((e_any, e_ref), (bias_any, bias_ref), (et_any, et_ref)))
    ]
    for fill in fills:
        fill.start()
    barrier = pltpu.get_barrier_semaphore()
    for target in (sibling, beside):
        pl.semaphore_signal(barrier, inc=1, device_id=target, device_id_type=MESH)
    for k in range(1, 4):
        pl.semaphore_signal(barrier, inc=1, device_id=at_z(flip(z, k)), device_id_type=MESH)
    feats[me] = u_ref[...]
    pl.semaphore_wait(barrier, 5)

    def move(slot, device, send, get):
        return pltpu.make_async_remote_copy(
            src_ref=feats.at[slot],
            dst_ref=feats.at[slot],
            send_sem=send,
            recv_sem=get,
            device_id=device,
            device_id_type=MESH,
        )

    def hand(zz, other):
        slot = slot_of(zz, (y + other) % 2, c)
        return move(slot, sibling, c_send.at[other * 4 + zz], c_get.at[other * 4 + zz])

    def handed_here(zz, other):
        slot = slot_of(zz, (y + other) % 2, 1 - c)
        return move(slot, sibling, c_send.at[other * 4 + zz], c_get.at[other * 4 + zz])

    def cross(zz):
        return move(slot_of(zz, y, c), beside, y_send.at[zz], y_get.at[zz])

    def crossed_here(zz):
        return move(slot_of(zz, 1 - y, c), beside, y_send.at[zz], y_get.at[zz])

    def along(zz, to, way):
        return move(slot_of(zz, y, c), at_z(to), z_send.at[way * 4 + zz], z_get.at[zz])

    def own_round():
        for way, to in ((0, z + 1), (1, z - 1)):

            @pl.when(inside(to))
            def _(way=way, to=to):
                along(z, to, way).start()

        cross(z).start()
        hand(z, 0).start()

    def later_round(r):
        if r <= HOPS:
            for way, origin, to in ((0, z - r, z + 1), (1, z + r, z - 1)):

                @pl.when(inside(origin))
                def _(way=way, origin=origin, to=to):
                    along(origin, to, way).wait_recv()

                    @pl.when(inside(to))
                    def _():
                        along(origin, to, way).start()

                    cross(origin).start()
                    hand(origin, 0).start()

        for origin in (z - (r - 1), z + (r - 1))[: 1 if r == 1 else 2]:

            @pl.when(inside(origin))
            def _(origin=origin):
                crossed_here(origin).wait_recv()
                hand(origin, 1).start()

    own_round()
    fills[0].wait()
    fills[1].wait()
    fills[2].wait()
    count = e_ref.shape[0]
    step = split_of(count, 640, 128)

    def hand_part(s):
        return pltpu.make_async_remote_copy(
            src_ref=packs.at[s, 1 - c],
            dst_ref=handed.at[s],
            send_sem=h_send.at[s],
            recv_sem=h_get.at[s],
            device_id=sibling,
            device_id_type=MESH,
        )

    def cross_part(k):
        return pltpu.make_async_remote_copy(
            src_ref=packs.at[2 * k + 1, c],
            dst_ref=crossed.at[k],
            send_sem=p_send.at[k],
            recv_sem=p_get.at[k],
            device_id=beside,
            device_id_type=MESH,
        )

    def line_part(k):
        return pltpu.make_async_remote_copy(
            src_ref=zouts.at[k],
            dst_ref=lined.at[k],
            send_sem=l_send.at[k],
            recv_sem=l_get.at[k],
            device_id=at_z(flip(z, k)),
            device_id_type=MESH,
        )

    def compute(s):
        zt, yt = flip(z, s // 2), (y + s % 2) % 2

        handed_here(zt, s % 2).wait_recv()
        first = slot_of(zt, yt, 0)
        u = feats[pl.ds(first, 2)].reshape(2 * labels, hidden)
        top = total = mean = None
        for start in range(0, count, step):
            part = slice(start, start + step)
            bias = bias_ref[part, :]
            logits = mm_nt(e_ref[part, :], u) + jnp.concatenate([bias, bias], 1)
            high = jnp.max(logits, 0, keepdims=True)
            new = high if top is None else jnp.maximum(top, high)
            grown = jnp.exp(logits - new)
            sums = jnp.sum(grown, 0, keepdims=True)
            product = mm(et_ref[:, part], grown.astype(BF))
            if top is None:
                total, mean = sums, product
            else:
                shrink = jnp.exp(top - new)
                total, mean = total * shrink + sums, mean * shrink + product
            top = new
        mean = mean * (1.0 / total)
        logs = top + jnp.log(total)
        for k in range(2):
            half = slice(k * labels, (k + 1) * labels)
            packs[s, k, :hidden, :] = mean[:, half].astype(BF)
            packs[s, k, hidden : hidden + LOG_ROWS, :] = pack_log(logs[:, half], LOG_ROWS)
        hand_part(s).start()

    def settle(s):
        hand_part(s).wait_recv()
        pair = merged(unpack(packs[s, c], hidden), unpack(handed[s], hidden))

        @pl.when(s % 2 == 1)
        def _():
            store_packed(packs.at[s, c], pair, hidden)
            cross_part(s // 2).start()

        @pl.when(s % 2 == 0)
        def _():
            store_packed(kept.at[s // 2], pair, hidden)

    def finish(k):
        cross_part(k).wait_recv()
        pair = merged(unpack(kept[k], hidden), unpack(crossed[k], hidden))

        @pl.when(k > 0)
        def _():
            store_packed(zouts.at[k], pair, hidden)
            line_part(k).start()

        @pl.when(k == 0)
        def _():
            store_packed(zouts.at[k], pair, hidden)

    steps = 8

    @pl.loop(0, steps)
    def _(s):
        for r in range(1, HOPS + 2):
            pl.when(s == r)(functools.partial(later_round, r))
        compute(s)

        @pl.when(s > 0)
        def _():
            settle(s - 1)

        @pl.when((s >= 3) & (s % 2 == 1))
        def _():
            finish((s - 3) // 2)

    settle(steps - 1)
    finish(steps // 2 - 1)
    total = unpack(zouts[0], hidden)
    for k in range(1, 4):
        line_part(k).wait_recv()
        total = merged(total, unpack(lined[k], hidden))
    mean_ref[...] = total[0]
    log_ref[...] = total[1]

    for way, to in ((0, z + 1), (1, z - 1)):

        @pl.when(inside(to))
        def _(way=way, to=to):
            along(z, to, way).wait_send()

    cross(z).wait_send()
    hand(z, 0).wait_send()
    for r in range(1, HOPS + 1):
        for way, origin, to in ((0, z - r, z + 1), (1, z + r, z - 1)):

            @pl.when(inside(origin))
            def _(way=way, origin=origin, to=to):
                @pl.when(inside(to))
                def _():
                    along(origin, to, way).wait_send()

                cross(origin).wait_send()
                hand(origin, 0).wait_send()

    for origin in range(4):
        hand(origin, 1).wait_send()
    for s in range(steps):
        hand_part(s).wait_send()
    for k in range(4):
        cross_part(k).wait_send()
    for k in range(1, 4):
        line_part(k).wait_send()


def head(u, e, et, bias_wide):
    labels, hidden = u.shape
    whole = pl.BlockSpec(memory_space=pltpu.VMEM)
    anywhere = pl.BlockSpec(memory_space=pl.ANY)
    shape = jax.ShapeDtypeStruct
    sems = pltpu.SemaphoreType.DMA
    block = (hidden + LOG_ROWS, labels)
    return pl.pallas_call(
        head_body,
        in_specs=[whole] + [anywhere] * 3,
        out_specs=[whole] * 2,
        out_shape=[shape((hidden, labels), F32), shape((1, labels), F32)],
        scratch_shapes=[
            pltpu.VMEM(e.shape, BF),
            pltpu.VMEM(et.shape, BF),
            pltpu.VMEM(bias_wide.shape, F32),
            pltpu.VMEM((16, labels, hidden), BF),
            pltpu.VMEM((8, 2, *block), BF),
            pltpu.VMEM((8, *block), BF),
            pltpu.VMEM((4, *block), BF),
            pltpu.VMEM((4, *block), BF),
            pltpu.VMEM((4, *block), BF),
            pltpu.VMEM((4, *block), BF),
            sems((3,)),
            sems((8,)),
            sems((4,)),
            sems((4,)),
            sems((4,)),
            sems((8,)),
            sems((8,)),
            sems((8,)),
            sems((8,)),
            sems((4,)),
            sems((4,)),
            sems((4,)),
            sems((4,)),
        ],
        compiler_params=params(collective_id=4, has_side_effects=True),
        name="head",
    )(u, e, et, bias_wide)


def seg_positions(segments):
    index = jnp.arange(segments.shape[-1], dtype=jnp.int32)
    fresh = jnp.concatenate([jnp.ones((1,), dtype=bool), segments[1:] != segments[:-1]], -1)
    starts = lax.cummax(jnp.where(fresh, index, jnp.zeros_like(index)), axis=0)
    return index - starts


def optimizer_update(weight, gradient, moment_one, moment_two, step_as_real):
    moment_one = beta_first * moment_one + (1.0 - beta_first) * gradient
    moment_two = beta_second * moment_two + (1.0 - beta_second) * gradient * gradient
    one_hat = moment_one / (1.0 - beta_first**step_as_real)
    two_hat = moment_two / (1.0 - beta_second**step_as_real)
    weight = weight - learn_rate * (one_hat / (jnp.sqrt(two_hat) + adam_eps) + decay_rate * weight)
    return (weight, moment_one, moment_two)


def pad_rows(matrix, multiple):
    return jnp.pad(matrix, ((0, -matrix.shape[0] % multiple), (0, 0)))


def slab_of(gathered, start, rows):
    if rows % 16 == 0 and start % rows == 0:
        return (gathered, start // rows, rows)
    part = gathered[:, start : start + rows].reshape(1, -1, gathered.shape[2])
    return (part, 0, part.shape[1])


def per_device(
    input_token_index,
    sentence_numbers,
    label_positions,
    label_target_token,
    sequence_task_index,
    task_loss_weight,
    optimizer_step_count,
    embed,
    position_embedding,
    norm_gain_vector,
    norm_bias_vector,
    attention_in_weight,
    attention_out_weight,
    feedforward_up,
    feedforward_down,
    layer_bias_vector,
    head_dense_bias,
    vocabulary_bias,
    adapter_down_matrix,
    adapter_up_matrix,
    adapter_moment_first,
    adapter_moment_second,
    head_projection,
    head_moment_first,
    head_moment_second,
):
    shards = lax.axis_size("dp") * lax.axis_size("fsdp")
    dp_index = lax.axis_index("dp")
    fsdp_index = lax.axis_index("fsdp")
    layers, unused, rank, up_part = adapter_up_matrix.shape
    hidden = embed.shape[1]
    tokens = input_token_index.shape[1]
    labels = label_positions.shape[1]
    qkv_rows = attention_in_weight.shape[2]
    out_rows = attention_out_weight.shape[2]
    ff_rows = feedforward_up.shape[2]
    head_rows = head_projection.shape[0]

    grouped = (lax.axis_size("dp"), lax.axis_size("fsdp")) == (2, 16)
    chunks = [
        [
            feedforward_up[layer].T,
            feedforward_down[layer],
            attention_in_weight[layer].T,
            attention_out_weight[layer].T,
        ]
        for layer in range(layers)
    ]
    ups = adapter_up_matrix.astype(BF).reshape(-1)
    up_rows = -(-ups.size // hidden)
    chunks[0] += [
        head_projection.astype(BF),
        jnp.pad(ups, (0, up_rows * hidden - ups.size)).reshape(up_rows, hidden),
    ]
    chunks = [pad_rows(jnp.concatenate(pieces, 0), 32) for pieces in chunks]

    table_rows = embed.shape[0]
    wanted = jnp.concatenate([input_token_index[0], label_target_token[0]])
    dp_count = lax.axis_size("dp")
    group_ids = lax.all_gather(wanted, "dp", axis=0, tiled=False) - dp_index * table_rows
    later_full = [lax.all_gather(chunk, BOTH, axis=0, tiled=False) for chunk in chunks[1:]]
    inside = (group_ids >= 0) & (group_ids < table_rows)
    group_ids = jnp.clip(group_ids, 0, table_rows - 1)
    mine = lax.dynamic_index_in_dim(inside, dp_index, 0, keepdims=False)
    task_range = jnp.arange(TASKS, dtype=jnp.int32)
    slice_rows = vocabulary_bias.shape[0]
    if grouped:
        pair_ids = jnp.concatenate(
            [
                lax.dynamic_index_in_dim(group_ids, (dp_index + shift) % 2, 0, keepdims=False)
                for shift in (1, 0)
            ]
        )
        low_ids = jnp.arange(pair_ids.size, dtype=jnp.int32) % PICK * GROUP + pair_ids % GROUP
        note = jnp.broadcast_to(sequence_task_index.astype(F32)[:, None], (8, 128))
        bias_rows = -(-slice_rows // 1024) * 8
        bias_block = jnp.pad(vocabulary_bias, (0, bias_rows * 128 - slice_rows)).reshape(bias_rows, 128)
        first_full, own_rows, got, notes, biases, own_vocab, own_turned = start_exchange(
            pair_ids // GROUP, low_ids[:, None], embed, chunks[0], note, bias_block, shards, slice_rows
        )
        every_task = notes[:, 0, 0].astype(jnp.int32)
        all_bias = biases.reshape(shards, -1)[:, :slice_rows].reshape(-1)
    else:
        first_full = lax.all_gather(chunks[0], BOTH, axis=0, tiled=False)
        looked = jnp.where(
            inside.reshape(-1)[:, None], embed[group_ids.reshape(-1)], jnp.zeros((), BF)
        )
        own_rows = got = lax.psum_scatter(looked, "dp", scatter_dimension=0, tiled=True)
        own_slice = lax.dynamic_slice_in_dim(embed, fsdp_index * slice_rows, slice_rows, 0)
        own_vocab = jnp.concatenate(
            [own_slice]
            + [
                lax.ppermute(
                    own_slice, "dp", [(k, (k + shift) % dp_count) for k in range(dp_count)]
                )
                for shift in range(1, dp_count)
            ],
            0,
        )
        own_turned = own_vocab.T
        every_task = lax.all_gather(sequence_task_index, BOTH, axis=0, tiled=True)
        all_bias = lax.all_gather(vocabulary_bias, BOTH, axis=0, tiled=True)
    gathered = [first_full, *later_full]
    counts = labels * jnp.sum((every_task[:, None] == task_range[None, :]).astype(F32), 0)
    task_hot = (sequence_task_index[:, None] == task_range[None, :]).astype(F32)
    row_weight = jnp.sum(task_hot[0] * (task_loss_weight / jnp.maximum(counts, 1.0)))

    slabs = [
        (slab_of(gathered[layer], 0, ff_rows), slab_of(gathered[layer], ff_rows, ff_rows))
        for layer in range(layers)
    ]
    in_weights, out_weights = [], []
    for layer in range(layers):
        at = 2 * ff_rows
        in_weights.append(gathered[layer][:, at : at + qkv_rows].reshape(-1, hidden))
        at += qkv_rows
        out_weights.append(gathered[layer][:, at : at + out_rows].reshape(-1, hidden))
    at = 2 * ff_rows + qkv_rows + out_rows
    head_full = first_full[:, at : at + head_rows].reshape(-1, hidden)
    at += head_rows
    ups_full = (
        first_full[:, at : at + up_rows]
        .reshape(shards, -1)[:, : ups.size]
        .reshape(shards, layers, 2, rank, up_part)
        .transpose(1, 2, 3, 0, 4)
        .reshape(layers, 2, rank, hidden)
    )
    blank = jnp.zeros((rank, hidden), BF)
    adapters = [
        jnp.pad(
            jnp.concatenate(
                [
                    jnp.concatenate([2 * ups_full[layer, 0], blank, blank], 1),
                    jnp.concatenate([blank, blank, 2 * ups_full[layer, 1]], 1),
                ],
                0,
            ),
            ((0, 128 - 2 * rank), (0, 0)),
        )
        for layer in range(layers)
    ]
    downs = [
        jnp.pad(
            jnp.concatenate([adapter_down_matrix[layer, 0], adapter_down_matrix[layer, 1]], 1),
            ((0, 0), (0, 128 - 2 * rank)),
        )
        for layer in range(layers)
    ]
    bias_of = []
    for layer in range(layers):
        b = layer_bias_vector[layer][None, :]
        ff = b.shape[1] - 4 * hidden
        bias_of.append(
            (
                jnp.concatenate(
                    [b[:, :hidden], jnp.zeros((1, hidden), F32), b[:, hidden : 2 * hidden]], 1
                ),
                b[:, 2 * hidden : 3 * hidden],
                b[:, 3 * hidden : 3 * hidden + ff],
                b[:, 3 * hidden + ff :],
            )
        )
    norms_of = [
        jnp.concatenate(
            [
                norm_gain_vector[1 + 2 * layer][None],
                norm_bias_vector[1 + 2 * layer][None],
                norm_gain_vector[2 + 2 * layer][None],
                norm_bias_vector[2 + 2 * layer][None],
                norm_gain_vector[-1][None],
                norm_bias_vector[-1][None],
            ],
            0,
        )
        for layer in range(layers)
    ]

    target_rows = jnp.where(mine[tokens:, None], own_rows[tokens:], got[tokens:]).astype(F32)
    segments = sentence_numbers[0]
    spot = seg_positions(segments)[:, None]
    seg_real = segments.astype(F32)
    seg_wide = jnp.broadcast_to(seg_real[:, None], (tokens, 128))
    seg_row = seg_real[None, :]
    place_row = label_positions
    place_col = jnp.broadcast_to(label_positions.reshape(labels, 1), (labels, 128))

    own_bias = jnp.concatenate(
        [
            lax.dynamic_slice_in_dim(
                all_bias,
                ((dp_index - shift) % dp_count) * table_rows + fsdp_index * slice_rows,
                slice_rows,
                0,
            )
            for shift in range(dp_count)
        ]
    )
    vocab_block = (
        own_vocab,
        own_turned,
        jnp.broadcast_to(own_bias[:, None], (own_bias.shape[0], 128)),
    )
    target_bias = all_bias[label_target_token[0]]

    first_norm = jnp.concatenate([norm_gain_vector[:1], norm_bias_vector[:1]], 0)
    qkv, mid, hidden_rows = project(
        own_rows, got, mine[:tokens, None].astype(jnp.int32), spot, position_embedding, first_norm,
        downs[0], in_weights[0], adapters[0], bias_of[0][0],
    )
    context, logs = attend(qkv, seg_wide, seg_row)
    x_last, one, two, slope = after(
        context, hidden_rows, out_weights[0], *slabs[0], *bias_of[0][1:], norms_of[0]
    )
    *saved, features = last_forward(
        x_last, place_col, place_row, seg_wide, downs[1], in_weights[1], adapters[1], bias_of[1][0],
        out_weights[1], *slabs[1], *bias_of[1][1:], norms_of[1], head_full, head_dense_bias[None, :],
    )
    if grouped:
        mean_t, own_logs = head(features, *vocab_block)
    else:
        every = lax.all_gather(features, "fsdp", axis=0, tiled=True)
        means, local_logs = vocab(every, *vocab_block, labels)
        local_logs = local_logs.reshape(-1, labels)
        all_logs = lax.all_gather(local_logs, "fsdp", axis=0, tiled=False)
        whole_logs = jax.nn.logsumexp(all_logs, axis=0)
        scaled = (means * jnp.exp(local_logs - whole_logs)[:, None, :]).astype(BF)
        mean_t = lax.psum_scatter(scaled, "fsdp", scatter_dimension=0, tiled=True)[0].astype(F32)
        own_logs = lax.dynamic_index_in_dim(whole_logs, fsdp_index, 0, keepdims=False)
    targets = jnp.sum(features.astype(F32) * target_rows, 1) + target_bias
    own_loss = row_weight * jnp.sum(own_logs - targets)
    feat_grad = row_weight * (mean_t.T - target_rows)

    hidden_grad, dense_gradient, gq_last, gv_last = last_backward(
        feat_grad, saved, place_col, place_row, seg_wide, downs[1], in_weights[1], adapters[1],
        out_weights[1], *slabs[1], norms_of[1], head_full, rank,
    )
    back = (hidden_grad, one, two, slope, out_weights[0], *slabs[0], norms_of[0])
    if grouped:
        block = -(-head_rows * hidden // 2048) * 2048
        dense_parts = jnp.pad(
            dense_gradient.reshape(shards, -1).astype(BF), ((0, 0), (0, block - head_rows * hidden))
        ).reshape(shards, 16, block // 16)
        dctx, dense_sum = after_back_sum(*back, dense_parts, shards)
        dense_portion = dense_sum.reshape(-1)[: head_rows * hidden].reshape(head_rows, hidden)
    else:
        dctx = after_back(*back)
        dense_portion = lax.psum_scatter(dense_gradient, BOTH, scatter_dimension=0, tiled=True)
    gq_first, gv_first = attend_back(qkv, dctx, logs, seg_wide, seg_row, mid, rank)
    adapter_gradient = jnp.stack([gq_first, gv_first, gq_last, gv_last]).reshape(layers, 2, rank, hidden)
    if grouped:
        parts = adapter_gradient.reshape(-1, shards, up_part).transpose(1, 0, 2).reshape(shards, -1)
        block = -(-ups.size // 1024) * 1024
        parts = jnp.pad(parts, ((0, 0), (0, block - ups.size))).reshape(shards, block // 128, 128)
        own_parts, sums = tail(parts, dense_portion, jnp.broadcast_to(own_loss, (8, 128)), shards)
        adapter_portion = own_parts.reshape(-1)[: ups.size].reshape(adapter_up_matrix.shape)
        masked_task_loss, norm_square = sums[0, 0], sums[1, 0]
    else:
        adapter_portion = lax.psum_scatter(adapter_gradient, BOTH, scatter_dimension=3, tiled=True)
        squared_entries = jnp.sum(adapter_portion * adapter_portion) + jnp.sum(
            dense_portion * dense_portion
        )
        masked_task_loss, norm_square = lax.psum((own_loss, squared_entries), BOTH)
    gradient_norm = jnp.sqrt(norm_square)
    scale_factor = jnp.minimum(1.0, clip_limit / (gradient_norm + 1e-06))
    step_as_real = optimizer_step_count[0].astype(F32)
    adapter_new = optimizer_update(
        adapter_up_matrix,
        adapter_portion * scale_factor,
        adapter_moment_first,
        adapter_moment_second,
        step_as_real,
    )
    dense_new = optimizer_update(
        head_projection,
        dense_portion * scale_factor,
        head_moment_first,
        head_moment_second,
        step_as_real,
    )
    return (masked_task_loss, gradient_norm, *adapter_new, *dense_new)


def solution(mesh):
    rows = P(BOTH, None)
    in_specs = (
        rows,
        rows,
        rows,
        rows,
        P(BOTH),
        P(),
        P(),
        P("dp", None),
        P(),
        P(),
        P(),
        P(None, None, BOTH),
        P(None, None, BOTH),
        P(None, None, BOTH),
        P(None, BOTH, None),
        P(),
        P(),
        P(BOTH),
        P(),
        P(None, None, None, BOTH),
        P(None, None, None, BOTH),
        P(None, None, None, BOTH),
        rows,
        rows,
        rows,
    )
    adapter = P(None, None, None, BOTH)
    out_specs = (P(), P(), adapter, adapter, adapter, rows, rows, rows)
    return jax.shard_map(
        per_device, mesh=mesh, in_specs=in_specs, out_specs=out_specs, check_vma=False
    )
```

```python
import functools

import jax
import jax.numpy as jnp
from jax import lax
from jax.experimental import pallas as pl
from jax.experimental.pallas import tpu as pltpu
from jax.sharding import PartitionSpec as P

HEADS = 12
TASKS = 4
REACH = 128

norm_eps = 1e-05
adapter_scale = 2.0
clip_limit = 0.01
learn_rate = 0.05
beta_first = 0.9
beta_second = 0.999
adam_eps = 1e-08
decay_rate = 0.01
masked_score = -1e30

BF = jnp.bfloat16
F32 = jnp.float32
BOTH = ("dp", "fsdp")
VMEM_BYTES = 60 * 1024 * 1024


def mm(a, b):
    return lax.dot_general(a, b, (((1,), (0,)), ((), ())), preferred_element_type=F32)


def mm_nt(a, b):
    return lax.dot_general(a, b, (((1,), (1,)), ((), ())), preferred_element_type=F32)


def mm_tn(a, b):
    return lax.dot_general(a, b, (((0,), (0,)), ((), ())), preferred_element_type=F32)


def layer_norm(rows_in, gain, shift):
    center = rows_in - jnp.mean(rows_in, -1, keepdims=True)
    spread = jnp.mean(center * center, -1, keepdims=True)
    return center * lax.rsqrt(spread + norm_eps) * gain + shift


def norm_back(rows_in, gain, gradient):
    center = rows_in - jnp.mean(rows_in, -1, keepdims=True)
    inverse = lax.rsqrt(jnp.mean(center * center, -1, keepdims=True) + norm_eps)
    unit = center * inverse
    scaled = gradient * gain
    return inverse * (
        scaled
        - jnp.mean(scaled, -1, keepdims=True)
        - unit * jnp.mean(scaled * unit, -1, keepdims=True)
    )


def gelu_pair(v):
    size = jnp.abs(v) * 0.7071067811865476
    base = 1.0 + 0.3275911 * size
    t = pl.reciprocal(base, approx=True)
    t = t * (2.0 - base * t)
    bell = jnp.exp(-0.5 * v * v)
    poly = t * (
        0.127414796 + t * (-0.142248368 + t * (0.7107068705 + t * (-0.7265760135 + t * 0.5307027145)))
    )
    tail = poly * bell
    phi = jnp.where(v >= 0.0, 1.0 - tail, tail)
    return v * phi, phi + v * (bell * 0.3989422804014327)


def params(**more):
    return pltpu.CompilerParams(vmem_limit_bytes=VMEM_BYTES, **more)


def full(shape):
    return pl.BlockSpec(shape, lambda *_: (0,) * len(shape))


def split_of(total, most, step):
    size = (min(most, total) // step) * step
    while size > step and total % size:
        size -= step
    return size if size and total % size == 0 else total


def pair_rows(block, width):
    first = lax.broadcasted_iota(jnp.int32, block.shape, 1) < width
    return jnp.concatenate([jnp.where(first, block, 0.0), jnp.where(first, 0.0, block)], 0).astype(BF)


def pair_join(wide, width):
    rows = wide.shape[1] // 2
    return jnp.concatenate([wide[:width, :rows], wide[width:, rows:]], 0)


def masked(scores, same):
    rows = scores.shape[1] // 2
    return jnp.concatenate(
        [
            jnp.where(same, scores[:, :rows], masked_score),
            jnp.where(same, scores[:, rows:], masked_score),
        ],
        1,
    )


def project_body(
    own_ref, got_ref, mine_ref, spot_ref, spots_ref, norm_ref, down_ref, w_ref, up_ref, bias_ref,
    out_ref, mid_ref, x_ref,
):
    choose = lax.broadcasted_iota(jnp.int32, (own_ref.shape[0], spots_ref.shape[0]), 1) == spot_ref[...]
    summed = jnp.where(
        mine_ref[...] > 0, own_ref[...].astype(F32), got_ref[...].astype(F32)
    ) + mm(choose.astype(F32).astype(BF), spots_ref[...])
    x = layer_norm(summed, norm_ref[0:1, :], norm_ref[1:2, :])
    x_ref[...] = x
    low = x.astype(BF)
    mid = mm(low, down_ref[...]).astype(BF)
    mid_ref[...] = mid
    total = w_ref.shape[0]
    step = split_of(total, 768, 128)
    for start in range(0, total, step):
        part = slice(start, start + step)
        out_ref[:, part] = (
            mm_nt(low, w_ref[part, :]) + mm(mid, up_ref[:, part]) + bias_ref[:, part]
        ).astype(BF)


def project(own, got, mine, spot, spots, norms, down, w, up, bias):
    rows, width = mine.shape[0], own.shape[1]
    tile = split_of(rows, 256, 16)
    total = w.shape[0]
    row = lambda n: pl.BlockSpec((tile, n), lambda i: (i, 0))
    return pl.pallas_call(
        project_body,
        grid=(rows // tile,),
        in_specs=[row(width), row(width), row(1), row(1)]
        + [full(a.shape) for a in (spots, norms, down, w, up, bias)],
        out_specs=[row(total), row(down.shape[1]), row(width)],
        out_shape=[
            jax.ShapeDtypeStruct((rows, total), BF),
            jax.ShapeDtypeStruct((rows, down.shape[1]), BF),
            jax.ShapeDtypeStruct((rows, width), F32),
        ],
        compiler_params=params(),
        name="project",
    )(own, got, mine, spot, spots, norms, down, w, up, bias)


def attend_body(q_ref, k_ref, v_ref, seg_ref, seg_row_ref, ctx_ref, log_ref):
    rows = q_ref.shape[0]
    width = q_ref.shape[1] // 2
    scale = width**-0.5
    for start in range(0, rows, REACH):
        own = slice(start, start + REACH)
        near = slice(max(0, start - REACH), min(rows, start + 2 * REACH))
        queries = pair_rows(q_ref[own, :].astype(F32) * scale, width)
        same = seg_ref[near, :] == seg_row_ref[:, own]
        scores = masked(mm_nt(k_ref[near, :], queries), same)
        top = jnp.max(scores, 0, keepdims=True)
        weights = jnp.exp(scores - top)
        total = jnp.sum(weights, 0, keepdims=True)
        context = mm_tn(v_ref[near, :], weights.astype(BF)) * (1.0 / total)
        ctx_ref[own, :] = pair_join(context, width).T.astype(BF)
        log_ref[0, :, 2 * start : 2 * start + 2 * REACH] = top + jnp.log(total)


def attend(qkv, seg_wide, seg_row):
    rows, total = qkv.shape
    hidden = total // 3
    lanes = 2 * (hidden // HEADS)
    pairs = hidden // lanes
    column = lambda kind: pl.BlockSpec((rows, lanes), lambda p: (0, kind * pairs + p))
    return pl.pallas_call(
        attend_body,
        grid=(pairs,),
        in_specs=[column(0), column(1), column(2), full(seg_wide.shape), full(seg_row.shape)],
        out_specs=[
            pl.BlockSpec((rows, lanes), lambda p: (0, p)),
            pl.BlockSpec((1, 1, 2 * rows), lambda p: (p, 0, 0)),
        ],
        out_shape=[
            jax.ShapeDtypeStruct((rows, hidden), BF),
            jax.ShapeDtypeStruct((pairs, 1, 2 * rows), F32),
        ],
        compiler_params=params(),
        name="attend",
    )(qkv, qkv, qkv, seg_wide, seg_row)


def flat(ref):
    whole = ref[...]
    return whole.reshape(-1, whole.shape[-1])


def rows_of(ref, start, size):
    each = ref.shape[1]
    if size % each == 0 and start % each == 0 and each % 16 == 0:
        part = ref[start // each : (start + size) // each, :, :]
        return part.reshape(size, part.shape[-1])
    return flat(ref)[start : start + size, :]


def feed_step(ref):
    units = ref.shape[0] * ref.shape[1]
    step = ref.shape[1]
    while units % (2 * step) == 0 and 2 * step <= 768 and ref.shape[0] > 1:
        step *= 2
    return units, (step if ref.shape[0] > 1 else split_of(units, 768, 128))


def after_body(
    ctx_ref, x_ref, wo_ref, up_ref, down_ref, bo_ref, b1_ref, b2_ref, norm_ref,
    out_ref, one_ref, two_ref, slope_ref,
):
    one = x_ref[...] + (mm_nt(ctx_ref[...], wo_ref[...]) + bo_ref[...])
    one_ref[...] = one
    middle = layer_norm(one, norm_ref[0:1, :], norm_ref[1:2, :])
    low = middle.astype(BF)
    total = middle + b2_ref[...]
    units, step = feed_step(up_ref)
    for start in range(0, units, step):
        part = slice(start, start + step)
        act, slope = gelu_pair(mm_nt(low, rows_of(up_ref, start, step)) + b1_ref[:, part])
        slope_ref[:, part] = slope.astype(BF)
        total = total + mm(act.astype(BF), rows_of(down_ref, start, step))
    two_ref[...] = total
    out_ref[...] = layer_norm(total, norm_ref[2:3, :], norm_ref[3:4, :])


def slab_spec(slab):
    array, place, rows = slab
    return pl.BlockSpec((array.shape[0], rows, array.shape[2]), lambda *_: (0, place, 0))


def after(ctx, x, wo, up, down, bo, b1, b2, norms):
    rows, width = x.shape
    tile = split_of(rows, 256, 16)
    units = b1.shape[1]
    row = lambda n: pl.BlockSpec((tile, n), lambda i: (i, 0))
    return pl.pallas_call(
        after_body,
        grid=(rows // tile,),
        in_specs=[row(width), row(width), full(wo.shape), slab_spec(up), slab_spec(down)]
        + [full(a.shape) for a in (bo, b1, b2, norms)],
        out_specs=[row(width), row(width), row(width), row(units)],
        out_shape=[jax.ShapeDtypeStruct((rows, width), F32)] * 3
        + [jax.ShapeDtypeStruct((rows, units), BF)],
        compiler_params=params(),
        name="after",
    )(ctx, x, wo, up[0], down[0], bo, b1, b2, norms)


def exact_rows(choose, matrix):
    high = matrix.astype(BF)
    rest = matrix - high.astype(F32)
    middle = rest.astype(BF)
    low = (rest - middle.astype(F32)).astype(BF)
    return mm(choose, high) + mm(choose, middle) + mm(choose, low)


def last_forward_body(
    x_ref, place_ref, place_row_ref, seg_ref, down_ref, w_ref, adapt_ref, bias_ref, wo_ref, up_any, dn_any,
    bo_ref, b1_ref, b2_ref, norm_ref, hb_ref, hbias_ref,
    kv_ref, q_ref, mid_ref, log_ref, one_ref, slope_ref, two_ref, low_ref, act_ref, hslope_ref, feat_ref,
    up_ref, dn_ref, ctx_ref, sems, *, places,
):
    copies = []
    for k, (source, target, place) in enumerate(
        ((up_any, up_ref, places[0]), (dn_any, dn_ref, places[1]))
    ):
        rows = target.shape[1]
        copies.append(
            pltpu.make_async_copy(
                source.at[:, pl.ds(place * rows, rows), :], target, sems.at[k]
            )
        )
        copies[-1].start()
    rows, hidden = x_ref.shape
    labels = place_ref.shape[0]
    lanes = 2 * (hidden // HEADS)
    width = lanes // 2
    low = x_ref[...].astype(BF)
    mid = mm(low, down_ref[...]).astype(BF)
    mid_ref[...] = mid
    step = split_of(2 * hidden, 512, 128)
    for start in range(hidden, 3 * hidden, step):
        part = slice(start, start + step)
        kv_ref[:, start - hidden : start - hidden + step] = (
            mm_nt(low, w_ref[part, :]) + mm(mid, adapt_ref[:, part]) + bias_ref[:, part]
        ).astype(BF)
    choose = (
        lax.broadcasted_iota(jnp.int32, (labels, rows), 1) == place_ref[...][:, 0:1]
    ).astype(F32).astype(BF)
    own = exact_rows(choose, x_ref[...])
    own_low = own.astype(BF)
    own_mid = mm(choose, mid).astype(BF)
    q_ref[...] = (
        mm_nt(own_low, w_ref[:hidden, :]) + mm(own_mid, adapt_ref[:, :hidden]) + bias_ref[:, :hidden]
    ).astype(BF)
    seg = seg_ref[...]
    seg_own = jnp.sum(
        jnp.where(
            lax.broadcasted_iota(jnp.int32, (rows, labels), 0) == place_row_ref[...], seg, 0.0
        ),
        0,
        keepdims=True,
    )
    same = seg == seg_own
    for p in range(hidden // lanes):
        part = slice(p * lanes, (p + 1) * lanes)
        queries = pair_rows(q_ref[:, part].astype(F32) * width**-0.5, width)
        scores = masked(mm_nt(kv_ref[:, part], queries), same)
        top = jnp.max(scores, 0, keepdims=True)
        weights = jnp.exp(scores - top)
        total = jnp.sum(weights, 0, keepdims=True)
        context = mm_tn(
            kv_ref[:, hidden + p * lanes : hidden + (p + 1) * lanes], weights.astype(BF)
        ) * (1.0 / total)
        ctx_ref[:, part] = pair_join(context, width).T.astype(BF)
        log_ref[p : p + 1, :] = top + jnp.log(total)
    one = own + (mm_nt(ctx_ref[...], wo_ref[...]) + bo_ref[...])
    one_ref[...] = one
    middle = layer_norm(one, norm_ref[0:1, :], norm_ref[1:2, :])
    middle_low = middle.astype(BF)
    sum_two = middle + b2_ref[...]
    units, step = feed_step(up_ref)
    for copy in copies:
        copy.wait()
    for start in range(0, units, step):
        part = slice(start, start + step)
        act, slope = gelu_pair(mm_nt(middle_low, rows_of(up_ref, start, step)) + b1_ref[:, part])
        slope_ref[:, part] = slope.astype(BF)
        sum_two = sum_two + mm(act.astype(BF), rows_of(dn_ref, start, step))
    two_ref[...] = sum_two
    out_low = layer_norm(sum_two, norm_ref[2:3, :], norm_ref[3:4, :]).astype(BF)
    low_ref[...] = out_low
    act, slope = gelu_pair(mm(out_low, hb_ref[...]) + hbias_ref[...])
    act_ref[...] = act
    hslope_ref[...] = slope
    feat_ref[...] = layer_norm(act, norm_ref[4:5, :], norm_ref[5:6, :]).astype(BF)


def slab_scratch(slab):
    array, place, rows = slab
    return pltpu.VMEM((array.shape[0], rows, array.shape[2]), BF)


def last_forward(x, place_col, place_row, seg_wide, down, w, adapt, bias, wo, up, dn, bo, b1, b2, norms, hb, hbias):
    rows, hidden = x.shape
    labels = place_col.shape[0]
    units = b1.shape[1]
    whole = pl.BlockSpec(memory_space=pltpu.VMEM)
    anywhere = pl.BlockSpec(memory_space=pl.ANY)
    shape = jax.ShapeDtypeStruct
    pairs = HEADS // 2
    return pl.pallas_call(
        functools.partial(last_forward_body, places=(up[1], dn[1])),
        in_specs=[whole] * 9 + [anywhere] * 2 + [whole] * 6,
        out_specs=[whole] * 11,
        out_shape=[
            shape((rows, 2 * hidden), BF),
            shape((labels, hidden), BF),
            shape((rows, down.shape[1]), BF),
            shape((pairs, 2 * labels), F32),
            shape((labels, hidden), F32),
            shape((labels, units), BF),
            shape((labels, hidden), F32),
            shape((labels, hidden), BF),
            shape((labels, hidden), F32),
            shape((labels, hidden), F32),
            shape((labels, hidden), BF),
        ],
        scratch_shapes=[
            slab_scratch(up),
            slab_scratch(dn),
            pltpu.VMEM((labels, hidden), BF),
            pltpu.SemaphoreType.DMA((2,)),
        ],
        compiler_params=params(),
        name="last_forward",
    )(x, place_col, place_row, seg_wide, down, w, adapt, bias, wo, up[0], dn[0], bo, b1, b2, norms, hb, hbias)


def vocab_body(u_ref, e_ref, et_ref, bias_ref, num_ref, log_ref, scores, weights):
    count = e_ref.shape[0]
    step = split_of(count, 640, 16)
    u = u_ref[...]
    rows = u.shape[0]
    labels = num_ref.shape[2]
    top = jnp.full((1, rows), -jnp.inf, F32)
    for start in range(0, count, step):
        part = slice(start, start + step)
        bias = bias_ref[part, :]
        logits = mm_nt(e_ref[part, :], u) + jnp.concatenate([bias] * (rows // bias.shape[1]), 1)
        scores[part, :] = logits
        top = jnp.maximum(top, jnp.max(logits, 0, keepdims=True))
    total = jnp.zeros((1, rows), F32)
    for start in range(0, count, step):
        part = slice(start, start + step)
        grown = jnp.exp(scores[part, :] - top)
        total = total + jnp.sum(grown, 0, keepdims=True)
        weights[part, :] = grown.astype(BF)
    mean = mm(et_ref[...], weights[...]) * (1.0 / total)
    logs = top + jnp.log(total)
    for k in range(rows // labels):
        num_ref[k, :, :] = mean[:, k * labels : (k + 1) * labels]
        log_ref[k, :, :] = logs[:, k * labels : (k + 1) * labels]


def vocab(u, e, et, bias_wide, labels):
    rows, hidden = u.shape
    count = e.shape[0]
    tile = 2 * labels
    return pl.pallas_call(
        vocab_body,
        grid=(rows // tile,),
        in_specs=[
            pl.BlockSpec((tile, hidden), lambda i: (i, 0)),
            full(e.shape),
            full(et.shape),
            full(bias_wide.shape),
        ],
        out_specs=[
            pl.BlockSpec((2, hidden, labels), lambda i: (i, 0, 0)),
            pl.BlockSpec((2, 1, labels), lambda i: (i, 0, 0)),
        ],
        out_shape=[
            jax.ShapeDtypeStruct((rows // labels, hidden, labels), F32),
            jax.ShapeDtypeStruct((rows // labels, 1, labels), F32),
        ],
        scratch_shapes=[pltpu.VMEM((count, tile), F32), pltpu.VMEM((count, tile), BF)],
        compiler_params=params(),
        name="vocab",
    )(u, e, et, bias_wide)


def last_backward_body(
    du_ref, kv_ref, q_ref, mid_ref, log_ref, one_ref, slope_ref, two_ref, low_ref, act_ref, hslope_ref,
    place_ref, place_row_ref, seg_ref, down_ref, w_ref, adapt_ref, wo_ref, up_any, dn_any, norm_ref, hb_ref,
    dx_ref, gh_ref, g_ref,
    up_ref, dn_ref, dkv_ref, dq_ref, sems, *, places, edge,
):
    copies = []
    for k, (source, target, place) in enumerate(
        ((up_any, up_ref, places[0]), (dn_any, dn_ref, places[1]))
    ):
        rows = target.shape[1]
        copies.append(
            pltpu.make_async_copy(
                source.at[:, pl.ds(place * rows, rows), :], target, sems.at[k]
            )
        )
        copies[-1].start()
    rows = kv_ref.shape[0]
    labels, hidden = du_ref.shape
    lanes = 2 * (hidden // HEADS)
    width = lanes // 2
    scale = width**-0.5
    dact = norm_back(act_ref[...], norm_ref[4:5, :], du_ref[...])
    dz = (hslope_ref[...] * dact).astype(BF)
    dense = mm_tn(low_ref[...], dz)
    if len(gh_ref.shape) == 2:
        gh_ref[...] = dense
    else:
        each = hidden // gh_ref.shape[0]
        spare = jnp.zeros((gh_ref.shape[1] - each, hidden), F32)
        for k in range(gh_ref.shape[0]):
            gh_ref[k] = jnp.concatenate([dense[k * each : (k + 1) * each, :], spare], 0).astype(BF)
    dtwo = norm_back(two_ref[...], norm_ref[2:3, :], mm_nt(dz, hb_ref[...]))
    dtwo_low = dtwo.astype(BF)
    dmiddle = dtwo
    units, step = feed_step(up_ref)
    for copy in copies:
        copy.wait()
    for start in range(0, units, step):
        part = slice(start, start + step)
        dgate = (
            slope_ref[:, part].astype(F32) * mm_nt(dtwo_low, rows_of(dn_ref, start, step))
        ).astype(BF)
        dmiddle = dmiddle + mm(dgate, rows_of(up_ref, start, step))
    done = norm_back(one_ref[...], norm_ref[0:1, :], dmiddle)
    dctx = mm(done.astype(BF), wo_ref[...]).astype(BF)
    seg = seg_ref[...]
    choose_t = lax.broadcasted_iota(jnp.int32, (rows, labels), 0) == place_row_ref[...]
    same = seg == jnp.sum(jnp.where(choose_t, seg, 0.0), 0, keepdims=True)
    for p in range(hidden // lanes):
        part = slice(p * lanes, (p + 1) * lanes)
        later = slice(hidden + p * lanes, hidden + (p + 1) * lanes)
        queries = pair_rows(q_ref[:, part].astype(F32) * scale, width)
        outs = pair_rows(dctx[:, part].astype(F32), width)
        keys = kv_ref[:, part]
        weights = jnp.exp(masked(mm_nt(keys, queries), same) - log_ref[p : p + 1, :])
        dweights = mm_nt(kv_ref[:, later], outs)
        inner = jnp.sum(dweights * weights, 0, keepdims=True)
        dscores = (weights * (dweights - inner)).astype(BF)
        dkv_ref[:, part] = mm(dscores, queries).astype(BF)
        dkv_ref[:, later] = mm(weights.astype(BF), outs).astype(BF)
        dq_ref[:, part] = (pair_join(mm_tn(keys, dscores), width) * scale).T.astype(BF)
    dq = dq_ref[...]
    own_mid = mm(
        (lax.broadcasted_iota(jnp.int32, (labels, rows), 1) == place_ref[...][:, 0:1]).astype(F32).astype(BF),
        mid_ref[...],
    ).astype(BF)
    g_ref[...] = adapter_scale * jnp.where(
        lax.broadcasted_iota(jnp.int32, g_ref.shape, 1) < edge,
        mm_tn(dq, own_mid),
        mm_tn(dkv_ref[:, hidden:], mid_ref[...]),
    )
    dmid_own = mm_nt(dq, adapt_ref[:, :hidden]).astype(BF)
    own = done + mm(dq, w_ref[:hidden, :]) + mm_nt(dmid_own, down_ref[...])
    spread = choose_t.astype(F32).astype(BF)
    own_high = own.astype(BF)
    own_rest = (own - own_high.astype(F32)).astype(BF)
    dmid = mm_nt(dkv_ref[:, hidden:], adapt_ref[:, 2 * hidden :]).astype(BF)
    step = split_of(hidden, 256, 128)
    for start in range(0, hidden, step):
        part = slice(start, start + step)
        dx_ref[:, part] = (
            mm(dkv_ref[...], w_ref[hidden:, part])
            + mm_nt(dmid, down_ref[part, :])
            + mm(spread, own_high[:, part])
            + mm(spread, own_rest[:, part])
        )


def last_backward(du, saved, place_col, place_row, seg_wide, down, w, adapt, wo, up, dn, norms, hb, edge, shards):
    kv = saved[0]
    rows = kv.shape[0]
    labels, hidden = du.shape
    whole = pl.BlockSpec(memory_space=pltpu.VMEM)
    anywhere = pl.BlockSpec(memory_space=pl.ANY)
    shape = jax.ShapeDtypeStruct
    return pl.pallas_call(
        functools.partial(last_backward_body, places=(up[1], dn[1]), edge=edge),
        in_specs=[whole] * 18 + [anywhere] * 2 + [whole] * 2,
        out_specs=[whole] * 3,
        out_shape=[
            shape((rows, hidden), F32),
            shape((hidden, hidden), F32)
            if shards is None
            else shape((shards, -(-hidden // shards // 16) * 16, hidden), BF),
            shape((hidden, down.shape[1]), F32),
        ],
        scratch_shapes=[
            slab_scratch(up),
            slab_scratch(dn),
            pltpu.VMEM(kv.shape, BF),
            pltpu.VMEM((labels, hidden), BF),
            pltpu.SemaphoreType.DMA((2,)),
        ],
        compiler_params=params(),
        name="last_backward",
    )(du, *saved, place_col, place_row, seg_wide, down, w, adapt, wo, up[0], dn[0], norms, hb)


def after_back_body(dout_ref, one_ref, two_ref, slope_ref, wo_ref, up_ref, down_ref, norm_ref, dctx_ref):
    dtwo = norm_back(two_ref[...], norm_ref[2:3, :], dout_ref[...])
    low = dtwo.astype(BF)
    dmiddle = dtwo
    units, step = feed_step(up_ref)
    for start in range(0, units, step):
        part = slice(start, start + step)
        dgate = (
            slope_ref[:, part].astype(F32) * mm_nt(low, rows_of(down_ref, start, step))
        ).astype(BF)
        dmiddle = dmiddle + mm(dgate, rows_of(up_ref, start, step))
    done = norm_back(one_ref[...], norm_ref[0:1, :], dmiddle)
    dctx_ref[...] = mm(done.astype(BF), wo_ref[...]).astype(BF)


def after_back(dout, one, two, slope, wo, up, down, norms):
    rows, width = dout.shape
    tile = split_of(rows, 256, 16)
    row = lambda n: pl.BlockSpec((tile, n), lambda i: (i, 0))
    return pl.pallas_call(
        after_back_body,
        grid=(rows // tile,),
        in_specs=[row(width), row(width), row(width), row(slope.shape[1]), full(wo.shape)]
        + [slab_spec(up), slab_spec(down), full(norms.shape)],
        out_specs=row(width),
        out_shape=jax.ShapeDtypeStruct((rows, width), BF),
        compiler_params=params(),
        name="after_back",
    )(dout, one, two, slope, wo, up[0], down[0], norms)


def attend_back_body(
    q_ref, k_ref, v_ref, dctx_ref, log_ref, seg_ref, seg_row_ref, mid_ref, g_ref, dv_ref, *, edge
):
    rows = q_ref.shape[0]
    width = q_ref.shape[1] // 2
    scale = width**-0.5
    dv_ref[...] = jnp.zeros_like(dv_ref)
    gq = jnp.zeros((2 * width, mid_ref.shape[1]), F32)
    for start in range(0, rows, REACH):
        own = slice(start, start + REACH)
        near = slice(max(0, start - REACH), min(rows, start + 2 * REACH))
        queries = pair_rows(q_ref[own, :].astype(F32) * scale, width)
        outs = pair_rows(dctx_ref[own, :].astype(F32), width)
        same = seg_ref[near, :] == seg_row_ref[:, own]
        keys = k_ref[near, :]
        logs = log_ref[0, :, 2 * start : 2 * start + 2 * REACH]
        weights = jnp.exp(masked(mm_nt(keys, queries), same) - logs)
        dweights = mm_nt(v_ref[near, :], outs)
        inner = jnp.sum(dweights * weights, 0, keepdims=True)
        dscores = (weights * (dweights - inner)).astype(BF)
        dv_ref[near, :] += mm(weights.astype(BF), outs)
        dq = (pair_join(mm_tn(keys, dscores), width) * scale).astype(BF)
        gq = gq + mm(dq, mid_ref[own, :])
    gv = mm_tn(dv_ref[...].astype(BF), mid_ref[...])
    g_ref[...] = adapter_scale * jnp.where(
        lax.broadcasted_iota(jnp.int32, gq.shape, 1) < edge, gq, gv
    )


def attend_back(qkv, dctx, logs, seg_wide, seg_row, mid, edge):
    rows, total = qkv.shape
    hidden = total // 3
    lanes = 2 * (hidden // HEADS)
    pairs = hidden // lanes
    column = lambda kind: pl.BlockSpec((rows, lanes), lambda p: (0, kind * pairs + p))
    return pl.pallas_call(
        functools.partial(attend_back_body, edge=edge),
        grid=(pairs,),
        in_specs=[
            column(0),
            column(1),
            column(2),
            column(0),
            pl.BlockSpec((1, 1, 2 * rows), lambda p: (p, 0, 0)),
            full(seg_wide.shape),
            full(seg_row.shape),
            full(mid.shape),
        ],
        out_specs=pl.BlockSpec((lanes, mid.shape[1]), lambda p: (p, 0)),
        out_shape=jax.ShapeDtypeStruct((hidden, mid.shape[1]), F32),
        scratch_shapes=[pltpu.VMEM((rows, lanes), F32)],
        compiler_params=params(),
        name="attend_back",
    )(qkv, qkv, qkv, dctx, logs, seg_wide, seg_row, mid)


MESH = pl.DeviceIdType.MESH


def position():
    dp, fsdp = lax.axis_index("dp"), lax.axis_index("fsdp")
    return {"x": dp, "z": fsdp // 4, "y": (fsdp // 2) % 2, "c": fsdp % 2}


def device_of(place):
    return (place["x"], (place["z"] * 2 + place["y"]) * 2 + place["c"])


def number_of(place):
    return place["x"] * 16 + (place["z"] * 2 + place["y"]) * 2 + place["c"]


def rank_device(number):
    return (number // 16, number % 16)


def greet_all(shards):
    barrier = pltpu.get_barrier_semaphore()
    me = lax.axis_index("dp") * 16 + lax.axis_index("fsdp")

    @pl.loop(1, shards)
    def _(k):
        pl.semaphore_signal(
            barrier, inc=1, device_id=rank_device((me + k) % shards), device_id_type=MESH
        )


def await_all(shards):
    pl.semaphore_wait(pltpu.get_barrier_semaphore(), shards - 1)


def direct_copy(source, target, sends, receives, me, k, shards):
    return pltpu.make_async_remote_copy(
        src_ref=source,
        dst_ref=target,
        send_sem=sends.at[k],
        recv_sem=receives.at[me],
        device_id=rank_device((me + k) % shards),
        device_id_type=MESH,
    )


def spread(piece_of, buffer, sends, receives, me, shards):
    @pl.loop(1, shards)
    def _(k):
        direct_copy(piece_of((me + k) % shards), buffer.at[me], sends, receives, me, k, shards).start()


def collect(piece_of, buffer, sends, receives, me, shards):
    @pl.loop(1, shards)
    def _(k):
        source = (me + shards - k) % shards
        direct_copy(buffer.at[source], buffer.at[source], sends, receives, source, k, shards).wait_recv()

    @pl.loop(1, shards)
    def _(k):
        direct_copy(piece_of((me + k) % shards), buffer.at[me], sends, receives, me, k, shards).wait_send()


def relative_places(order):
    places = [
        {"x": dx, "z": dz, "y": dy} for dx in (0, 1) for dz in range(-3, 4) for dy in (0, 1)
    ]
    return sorted(places, key=lambda p: (abs(p["x"]) + abs(p["z"]) + abs(p["y"]), [abs(p[a]) for a in order]))


class Gather:
    def __init__(self, chunk, full_buffer, start, rows, order, sends, receives, hands, hands_got):
        self.chunk, self.full, self.order = chunk, full_buffer, order
        self.part = pl.ds(start, rows)
        self.sends, self.receives, self.hands, self.hands_got = sends, receives, hands, hands_got
        self.here = position()
        self.items = relative_places(order)
        self.pending = []

    def origin(self, item):
        here = self.here
        return {"x": (here["x"] + item["x"]) % 2, "z": here["z"] - item["z"], "y": (here["y"] + item["y"]) % 2, "c": here["c"]}

    def key(self, place):
        return (place["x"] * 4 + place["z"]) * 2 + place["y"]

    def outward(self, item):
        deepest = max([k for k, axis in enumerate(self.order) if item[axis]], default=-1)
        ways = []
        if deepest >= 0 and self.order[deepest] == "z":
            ways.append(("z", 1 if item["z"] > 0 else -1))
        for axis in self.order[deepest + 1 :]:
            ways += [("z", 1), ("z", -1)] if axis == "z" else [(axis, 1)]
        return ways

    def copy(self, index, way, slot, item):
        here = self.here
        place = self.origin(item)
        number, key = number_of(place), self.key(place)
        mine = not any(item.values())
        source = self.chunk.at[self.part, :] if mine else self.full.at[number, self.part, :]
        if way is None:
            target = dict(here, c=1 - here["c"])
            sends, receives = self.hands.at[index], self.hands_got.at[key]
        else:
            axis, step = way
            target = dict(here)
            target[axis] = here["z"] + step if axis == "z" else 1 - here[axis]
            sends, receives = self.sends.at[index * 4 + slot], self.receives.at[key]
        return pltpu.make_async_remote_copy(
            src_ref=source,
            dst_ref=self.full.at[number, self.part, :],
            send_sem=sends,
            recv_sem=receives,
            device_id=device_of(target),
            device_id_type=MESH,
        )

    def valid(self, item):
        z = self.here["z"] - item["z"]
        return (z >= 0) & (z <= 3)

    def step(self, index):
        item = self.items[index]

        @pl.when(self.valid(item))
        def _():
            if any(item.values()):
                self.arrived(index, item)
            for slot, way in enumerate(self.outward(item)):
                self.when_way(way, lambda way=way, slot=slot: self.copy(index, way, slot, item).start())
            self.copy(index, None, 0, item).start()

    def when_way(self, way, act):
        axis, step = way
        if axis == "z":
            z = self.here["z"] + step
            pl.when((z >= 0) & (z <= 3))(act)
        else:
            act()

    def arrived(self, index, item):
        place = self.origin(item)
        spot = self.full.at[number_of(place), self.part, :]
        pltpu.make_async_remote_copy(
            src_ref=spot,
            dst_ref=spot,
            send_sem=self.sends.at[index * 4],
            recv_sem=self.receives.at[self.key(place)],
            device_id=device_of(dict(self.here, c=1 - self.here["c"])),
            device_id_type=MESH,
        ).wait_recv()

    def finish(self):
        for index, item in enumerate(self.items):

            @pl.when(self.valid(item))
            def _(index=index, item=item):
                for slot, way in enumerate(self.outward(item)):
                    self.when_way(way, lambda way=way, slot=slot: self.copy(index, way, slot, item).wait_send())
                self.copy(index, None, 0, item).wait_send()
                place = dict(self.origin(item), c=1 - self.here["c"])
                spot = self.full.at[number_of(place), self.part, :]
                pltpu.make_async_remote_copy(
                    src_ref=spot,
                    dst_ref=spot,
                    send_sem=self.hands.at[index],
                    recv_sem=self.hands_got.at[self.key(place)],
                    device_id=device_of(dict(self.here, c=1 - self.here["c"])),
                    device_id_type=MESH,
                ).wait_recv()


ITEMS = 28


ITEMS = 28
PICK = 64
GROUP = 16


def start_body(
    streams, shards, rows, table_any, chunk, note, bias,
    full_chunk, got, notes, biases, e_out, et_out,
    e_ref, et_ref,
    sends, receives, hands, hands_got, row_sems, note_sends, note_gets, bias_sends, bias_gets,
    own_sems, e_sems, out_sems,
):
    here = position()
    me = number_of(here)
    across = device_of(dict(here, x=1 - here["x"]))
    slice_rows = e_ref.shape[0] // 2
    greet_all(shards)
    plain = [
        pltpu.make_async_copy(source, target, own_sems.at[k])
        for k, (source, target) in enumerate(
            ((chunk, full_chunk.at[me]), (note, notes.at[me]), (bias, biases.at[me]))
        )
    ]
    for copy in plain:
        copy.start()
    own_slice = table_any.at[
        pl.ds(pl.multiple_of((me % 16) * slice_rows, 16), slice_rows), :
    ]
    keep = pltpu.make_async_copy(own_slice, e_ref.at[pl.ds(0, slice_rows), :], own_sems.at[4])
    keep.start()
    swap = pltpu.make_async_remote_copy(
        src_ref=own_slice,
        dst_ref=e_ref.at[pl.ds(slice_rows, slice_rows), :],
        send_sem=e_sems.at[0],
        recv_sem=e_sems.at[1],
        device_id=across,
        device_id_type=MESH,
    )
    await_all(shards)
    gathers = [
        Gather(
            chunk, full_chunk, start, size, order, sends.at[k], receives.at[k], hands.at[k], hands_got.at[k]
        )
        for k, (start, size, order) in enumerate(streams)
    ]
    for gather in gathers:
        gather.step(0)
    spread(lambda peer: note, notes, note_sends, note_gets, me, shards)
    spread(lambda peer: bias, biases, bias_sends, bias_gets, me, shards)
    swap.start()

    send_rows = pltpu.make_async_remote_copy(
        src_ref=rows,
        dst_ref=got,
        send_sem=row_sems.at[0],
        recv_sem=row_sems.at[1],
        device_id=across,
        device_id_type=MESH,
    )
    send_rows.start()

    def turn(k):
        part = slice(k * 128, (k + 1) * 128)
        et_ref[:, part] = e_ref[part, :].astype(F32).T.astype(BF)

    def out_copies():
        return (
            pltpu.make_async_copy(e_ref, e_out, out_sems.at[0]),
            pltpu.make_async_copy(et_ref, et_out, out_sems.at[1]),
        )

    turned = 0
    own_turns = slice_rows // 128
    for index in range(1, ITEMS):
        if turned < own_turns:
            if turned == 0:
                keep.wait()
            turn(turned)
            turned += 1
        for gather in gathers:
            gather.step(index)
    swap.wait_recv()
    for k in range(turned, e_ref.shape[0] // 128):
        turn(k)
    copies = out_copies()
    for copy in copies:
        copy.start()
    for gather in gathers:
        gather.finish()
    collect(lambda peer: note, notes, note_sends, note_gets, me, shards)
    collect(lambda peer: bias, biases, bias_sends, bias_gets, me, shards)
    send_rows.wait()
    swap.wait_send()
    for copy in plain:
        copy.wait()
    for copy in copies:
        copy.wait()


def start_exchange(rows, table, chunk, note, bias, shards, slice_rows):
    anywhere = pl.BlockSpec(memory_space=pl.ANY)
    cut = (chunk.shape[0] * 5 // 6 + 15) // 16 * 16
    streams = ((0, cut, "xzy"), (cut, chunk.shape[0] - cut, "xyz"))
    hidden = table.shape[1]
    shape = jax.ShapeDtypeStruct
    sems = pltpu.SemaphoreType.DMA
    return pl.pallas_call(
        functools.partial(start_body, streams, shards),
        in_specs=[anywhere] * 5,
        out_specs=[anywhere] * 6,
        out_shape=[
            shape((shards, *chunk.shape), chunk.dtype),
            shape(rows.shape, rows.dtype),
            shape((shards, *note.shape), note.dtype),
            shape((shards, *bias.shape), bias.dtype),
            shape((2 * slice_rows, hidden), table.dtype),
            shape((hidden, 2 * slice_rows), table.dtype),
        ],
        scratch_shapes=[
            pltpu.VMEM((2 * slice_rows, hidden), BF),
            pltpu.VMEM((hidden, 2 * slice_rows), BF),
            sems((2, 4 * ITEMS)),
            sems((2, 16)),
            sems((2, ITEMS)),
            sems((2, 16)),
            sems((2,)),
            sems((shards,)),
            sems((shards,)),
            sems((shards,)),
            sems((shards,)),
            sems((5,)),
            sems((2,)),
            sems((2,)),
        ],
        compiler_params=params(collective_id=1, has_side_effects=True),
        name="start_exchange",
    )(rows, table, chunk, note, bias)


def look_up_body(ids, low_ref, table, first_ref, second_ref, stage):
    batches = first_ref.shape[0] // PICK
    for k, out in enumerate((first_ref, second_ref)):

        @pl.loop(0, batches)
        def _(b, k=k, out=out):
            at = (k * batches + b) * PICK

            def one(t, carry):
                stage[t] = table[ids[at + t]]
                return carry

            lax.fori_loop(0, PICK, one, 0, unroll=8)
            choose = (
                lax.broadcasted_iota(jnp.int32, (PICK, PICK * GROUP), 1)
                == low_ref[pl.ds(pl.multiple_of(at, PICK), PICK), :]
            )
            out[pl.ds(pl.multiple_of(b * PICK, PICK), PICK), :] = mm(
                choose.astype(F32).astype(BF), flat(stage)
            ).astype(BF)


def look_up(ids, table):
    whole = pl.BlockSpec(memory_space=pltpu.VMEM)
    hidden = table.shape[1]
    low = jnp.arange(ids.size, dtype=jnp.int32) % PICK * GROUP + ids % GROUP
    return pl.pallas_call(
        look_up_body,
        in_specs=[pl.BlockSpec(memory_space=pltpu.SMEM), whole, whole],
        out_specs=[whole] * 2,
        out_shape=[jax.ShapeDtypeStruct((ids.size // 2, hidden), table.dtype)] * 2,
        scratch_shapes=[pltpu.VMEM((PICK, GROUP, hidden), table.dtype)],
        compiler_params=params(),
        name="look_up",
    )(ids // GROUP, low[:, None], table.reshape(-1, GROUP, hidden))


def adam(weight, gradient, moment_one, moment_two, fade_one, fade_two):
    moment_one = beta_first * moment_one + (1.0 - beta_first) * gradient
    moment_two = beta_second * moment_two + (1.0 - beta_second) * gradient * gradient
    one_hat = moment_one / fade_one
    two_hat = moment_two / fade_two
    weight = weight - learn_rate * (one_hat / (jnp.sqrt(two_hat) + adam_eps) + decay_rate * weight)
    return (weight, moment_one, moment_two)


def finish_body(
    shards, places, edge,
    dout_any, one_any, two_any, slope_any, wo_any, up_any, dn_any, qkv_any, norm_ref, log_ref, seg_ref,
    seg_row_ref, mid_ref, parts, late_ref, facts, head_w, head_m, head_v, adapt_w, adapt_m, adapt_v,
    sums_ref, head_w_out, head_m_out, head_v_out, adapt_w_out, adapt_m_out, adapt_v_out,
    dout, one, two, slope, wo, up, dn, qkv, dctx, dv, grad, dense_got, grad_got, note, notes,
    tile_sems, load_sems, dense_send, dense_get, grad_send, grad_get, note_send, note_get,
):
    rows, hidden = dout.shape
    tile = split_of(rows, 256, 16)
    tiles = rows // tile
    me = number_of(position())

    def tile_loads(i):
        part = pl.ds(pl.multiple_of(i * tile, tile), tile)
        return [
            pltpu.make_async_copy(source.at[part, :], target.at[part, :], tile_sems.at[k, i])
            for k, (source, target) in enumerate(
                ((two_any, two), (dout_any, dout), (slope_any, slope), (one_any, one))
            )
        ]

    def slab(source, target, place):
        each = target.shape[1]
        return source.at[:, pl.ds(place * each, each), :]

    loads = [
        pltpu.make_async_copy(source, target, load_sems.at[k])
        for k, (source, target) in enumerate(
            (
                (slab(dn_any, dn, places[1]), dn),
                (slab(up_any, up, places[0]), up),
                (wo_any, wo),
                (qkv_any, qkv),
            )
        )
    ]
    for copy in tile_loads(0) + loads[:3]:
        copy.start()
    for i in range(1, tiles):
        for copy in tile_loads(i):
            copy.start()
    loads[3].start()
    greet_all(shards)
    dense_got[me] = parts[me]
    for copy in loads[:3]:
        copy.wait()

    @pl.loop(0, tiles)
    def _(i):
        for copy in tile_loads(i):
            copy.wait()
        part = pl.ds(pl.multiple_of(i * tile, tile), tile)
        after_back_body(
            dout.at[part, :], one.at[part, :], two.at[part, :], slope.at[part, :], wo, up, dn, norm_ref,
            dctx.at[part, :],
        )

        @pl.when(i == 0)
        def _():
            await_all(shards)
            spread(lambda peer: parts.at[peer], dense_got, dense_send, dense_get, me, shards)

    loads[3].wait()
    lanes = 2 * (hidden // HEADS)
    pairs = hidden // lanes

    @pl.loop(0, pairs)
    def _(p):
        column = lambda kind: pl.ds(pl.multiple_of((kind * pairs + p) * lanes, lanes), lanes)
        attend_back_body(
            qkv.at[:, column(0)], qkv.at[:, column(1)], qkv.at[:, column(2)], dctx.at[:, column(0)],
            log_ref.at[pl.ds(p, 1)], seg_ref, seg_row_ref, mid_ref, grad.at[column(0), :], dv, edge=edge,
        )

    grad[...] = grad[...] + late_ref[...]
    each = hidden // shards
    piece = lambda peer: grad.at[pl.ds(pl.multiple_of(peer * each, each), each), :]
    grad_got[me] = piece(me)[...]
    spread(piece, grad_got, grad_send, grad_get, me, shards)
    collect(lambda peer: parts.at[peer], dense_got, dense_send, dense_get, me, shards)
    dense = jnp.zeros((each, hidden), F32)
    for k in range(shards):
        dense = dense + dense_got[k].astype(F32)[:each, :]
    square = jnp.sum(dense * dense, keepdims=True)
    collect(piece, grad_got, grad_send, grad_get, me, shards)
    total = grad_got[0]
    for k in range(1, shards):
        total = total + grad_got[k]
    square = square + jnp.sum(total * total, keepdims=True)
    row = lax.broadcasted_iota(jnp.int32, note.shape, 0)
    note[...] = jnp.where(row == 0, facts[...], jnp.where(row == 1, square, 0.0))
    notes[me] = note[...]
    spread(lambda peer: note, notes, note_send, note_get, me, shards)
    collect(lambda peer: note, notes, note_send, note_get, me, shards)
    sums = notes[0]
    for k in range(1, shards):
        sums = sums + notes[k]
    norm = jnp.sqrt(sums[1:2, :])
    sums_ref[...] = jnp.where(row == 1, norm, sums)
    factor = jnp.minimum(1.0, clip_limit / (norm + 1e-06))[:, 0:1]
    fades = facts[1:2, 0:1], facts[2:3, 0:1]
    new = adam(head_w[...], dense * factor, head_m[...], head_v[...], *fades)
    head_w_out[...], head_m_out[...], head_v_out[...] = new
    new = adam(adapt_w[...], total * factor, adapt_m[...], adapt_v[...], *fades)
    adapt_w_out[...], adapt_m_out[...], adapt_v_out[...] = new


def finish(back, qkv, logs, seg_wide, seg_row, mid, parts, late, facts, heads, adapts, edge, shards):
    dout, one, two, slope, wo, up, dn, norms = back
    rows, hidden = dout.shape
    each = hidden // shards
    whole = pl.BlockSpec(memory_space=pltpu.VMEM)
    anywhere = pl.BlockSpec(memory_space=pl.ANY)
    shape = jax.ShapeDtypeStruct
    sems = pltpu.SemaphoreType.DMA
    tiles = rows // split_of(rows, 256, 16)
    return pl.pallas_call(
        functools.partial(finish_body, shards, (up[1], dn[1]), edge),
        in_specs=[anywhere] * 8 + [whole] * 14,
        out_specs=[whole] * 7,
        out_shape=[shape((8, 128), F32)]
        + [shape(a.shape, F32) for a in heads]
        + [shape(a.shape, F32) for a in adapts],
        scratch_shapes=[
            pltpu.VMEM((rows, hidden), F32),
            pltpu.VMEM((rows, hidden), F32),
            pltpu.VMEM((rows, hidden), F32),
            pltpu.VMEM(slope.shape, BF),
            pltpu.VMEM(wo.shape, BF),
            slab_scratch(up),
            slab_scratch(dn),
            pltpu.VMEM(qkv.shape, BF),
            pltpu.VMEM((rows, hidden), BF),
            pltpu.VMEM((rows, 2 * (hidden // HEADS)), F32),
            pltpu.VMEM(late.shape, F32),
            pltpu.VMEM(parts.shape, BF),
            pltpu.VMEM((shards, each, late.shape[1]), F32),
            pltpu.VMEM((8, 128), F32),
            pltpu.VMEM((shards, 8, 128), F32),
            sems((4, tiles)),
            sems((4,)),
        ]
        + [sems((shards,))] * 6,
        compiler_params=params(collective_id=2, has_side_effects=True),
        name="finish",
    )(dout, one, two, slope, wo, up[0], dn[0], qkv, norms, logs, seg_wide, seg_row, mid, parts, late, facts, *heads, *adapts)


HOPS = 3
LOG_ROWS = 16


def flip(z, k):
    return (z % 2 + k % 2) % 2 + 2 * ((z // 2 + k // 2) % 2)


def pack_log(log_row, rows):
    high = log_row.astype(BF).astype(F32)
    middle = (log_row - high).astype(BF).astype(F32)
    low = log_row - high - middle
    row = lax.broadcasted_iota(jnp.int32, (rows, log_row.shape[1]), 0)
    return jnp.where(
        row == 0, high, jnp.where(row == 1, middle, jnp.where(row == 2, low, 0.0))
    ).astype(BF)


def unpack(block, hidden):
    logs = block[hidden : hidden + LOG_ROWS, :].astype(F32)
    return block[:hidden, :].astype(F32), jnp.sum(logs, 0, keepdims=True)


def merged(one, two):
    top = jnp.maximum(one[1], two[1])
    first, second = jnp.exp(one[1] - top), jnp.exp(two[1] - top)
    total = first + second
    inverse = 1.0 / total
    return one[0] * (first * inverse) + two[0] * (second * inverse), top + jnp.log(total)


def store_packed(ref, pair, hidden):
    ref[:hidden, :] = pair[0].astype(BF)
    ref[hidden : hidden + LOG_ROWS, :] = pack_log(pair[1], LOG_ROWS)


def head_body(
    u_ref, e_any, et_any, bias_any, mean_ref, log_ref,
    e_ref, et_ref, bias_ref, feats, packs, handed, crossed, kept, lined, zouts,
    loads, z_send, z_get, y_send, y_get, c_send, c_get, h_send, h_get, p_send, p_get, l_send, l_get,
):
    here = position()
    z, y, c = here["z"], here["y"], here["c"]
    labels, hidden = u_ref.shape
    slot_of = lambda zz, yy, cc: (zz * 2 + yy) * 2 + cc
    me = slot_of(z, y, c)
    sibling = device_of(dict(here, c=1 - c))
    beside = device_of(dict(here, y=1 - y))
    at_z = lambda zz: device_of(dict(here, z=zz))
    inside = lambda zz: (zz >= 0) & (zz <= HOPS)

    fills = [
        pltpu.make_async_copy(source, target, loads.at[k])
        for k, (source, target) in enumerate(((e_any, e_ref), (bias_any, bias_ref), (et_any, et_ref)))
    ]
    for fill in fills:
        fill.start()
    barrier = pltpu.get_barrier_semaphore()
    for target in (sibling, beside):
        pl.semaphore_signal(barrier, inc=1, device_id=target, device_id_type=MESH)
    for k in range(1, 4):
        pl.semaphore_signal(barrier, inc=1, device_id=at_z(flip(z, k)), device_id_type=MESH)
    feats[me] = u_ref[...]
    pl.semaphore_wait(barrier, 5)

    def move(slot, device, send, get):
        return pltpu.make_async_remote_copy(
            src_ref=feats.at[slot],
            dst_ref=feats.at[slot],
            send_sem=send,
            recv_sem=get,
            device_id=device,
            device_id_type=MESH,
        )

    def hand(zz, other):
        slot = slot_of(zz, (y + other) % 2, c)
        return move(slot, sibling, c_send.at[other * 4 + zz], c_get.at[other * 4 + zz])

    def handed_here(zz, other):
        slot = slot_of(zz, (y + other) % 2, 1 - c)
        return move(slot, sibling, c_send.at[other * 4 + zz], c_get.at[other * 4 + zz])

    def cross(zz):
        return move(slot_of(zz, y, c), beside, y_send.at[zz], y_get.at[zz])

    def crossed_here(zz):
        return move(slot_of(zz, 1 - y, c), beside, y_send.at[zz], y_get.at[zz])

    def along(zz, to, way):
        return move(slot_of(zz, y, c), at_z(to), z_send.at[way * 4 + zz], z_get.at[zz])

    def own_round():
        for way, to in ((0, z + 1), (1, z - 1)):

            @pl.when(inside(to))
            def _(way=way, to=to):
                along(z, to, way).start()

        cross(z).start()
        hand(z, 0).start()

    def later_round(r):
        if r <= HOPS:
            for way, origin, to in ((0, z - r, z + 1), (1, z + r, z - 1)):

                @pl.when(inside(origin))
                def _(way=way, origin=origin, to=to):
                    along(origin, to, way).wait_recv()

                    @pl.when(inside(to))
                    def _():
                        along(origin, to, way).start()

                    cross(origin).start()
                    hand(origin, 0).start()

        for origin in (z - (r - 1), z + (r - 1))[: 1 if r == 1 else 2]:

            @pl.when(inside(origin))
            def _(origin=origin):
                crossed_here(origin).wait_recv()
                hand(origin, 1).start()

    own_round()
    fills[0].wait()
    fills[1].wait()
    fills[2].wait()
    count = e_ref.shape[0]
    step = split_of(count, 640, 128)

    def hand_part(s):
        return pltpu.make_async_remote_copy(
            src_ref=packs.at[s, 1 - c],
            dst_ref=handed.at[s],
            send_sem=h_send.at[s],
            recv_sem=h_get.at[s],
            device_id=sibling,
            device_id_type=MESH,
        )

    def cross_part(k):
        return pltpu.make_async_remote_copy(
            src_ref=packs.at[2 * k + 1, c],
            dst_ref=crossed.at[k],
            send_sem=p_send.at[k],
            recv_sem=p_get.at[k],
            device_id=beside,
            device_id_type=MESH,
        )

    def line_part(k):
        return pltpu.make_async_remote_copy(
            src_ref=zouts.at[k],
            dst_ref=lined.at[k],
            send_sem=l_send.at[k],
            recv_sem=l_get.at[k],
            device_id=at_z(flip(z, k)),
            device_id_type=MESH,
        )

    def compute(s):
        zt, yt = flip(z, s // 2), (y + s % 2) % 2

        handed_here(zt, s % 2).wait_recv()
        first = slot_of(zt, yt, 0)
        u = feats[pl.ds(first, 2)].reshape(2 * labels, hidden)
        top = total = mean = None
        for start in range(0, count, step):
            part = slice(start, start + step)
            bias = bias_ref[part, :]
            logits = mm_nt(e_ref[part, :], u) + jnp.concatenate([bias, bias], 1)
            high = jnp.max(logits, 0, keepdims=True)
            new = high if top is None else jnp.maximum(top, high)
            grown = jnp.exp(logits - new)
            sums = jnp.sum(grown, 0, keepdims=True)
            product = mm(et_ref[:, part], grown.astype(BF))
            if top is None:
                total, mean = sums, product
            else:
                shrink = jnp.exp(top - new)
                total, mean = total * shrink + sums, mean * shrink + product
            top = new
        mean = mean * (1.0 / total)
        logs = top + jnp.log(total)
        for k in range(2):
            half = slice(k * labels, (k + 1) * labels)
            packs[s, k, :hidden, :] = mean[:, half].astype(BF)
            packs[s, k, hidden : hidden + LOG_ROWS, :] = pack_log(logs[:, half], LOG_ROWS)
        hand_part(s).start()

    def settle(s):
        hand_part(s).wait_recv()
        pair = merged(unpack(packs[s, c], hidden), unpack(handed[s], hidden))

        @pl.when(s % 2 == 1)
        def _():
            store_packed(packs.at[s, c], pair, hidden)
            cross_part(s // 2).start()

        @pl.when(s % 2 == 0)
        def _():
            store_packed(kept.at[s // 2], pair, hidden)

    def finish(k):
        cross_part(k).wait_recv()
        pair = merged(unpack(kept[k], hidden), unpack(crossed[k], hidden))

        @pl.when(k > 0)
        def _():
            store_packed(zouts.at[k], pair, hidden)
            line_part(k).start()

        @pl.when(k == 0)
        def _():
            store_packed(zouts.at[k], pair, hidden)

    steps = 8

    @pl.loop(0, steps)
    def _(s):
        for r in range(1, HOPS + 2):
            pl.when(s == r)(functools.partial(later_round, r))
        compute(s)

        @pl.when(s > 0)
        def _():
            settle(s - 1)

        @pl.when((s >= 3) & (s % 2 == 1))
        def _():
            finish((s - 3) // 2)

    settle(steps - 1)
    finish(steps // 2 - 1)
    total = unpack(zouts[0], hidden)
    for k in range(1, 4):
        line_part(k).wait_recv()
        total = merged(total, unpack(lined[k], hidden))
    mean_ref[...] = total[0]
    log_ref[...] = total[1]

    for way, to in ((0, z + 1), (1, z - 1)):

        @pl.when(inside(to))
        def _(way=way, to=to):
            along(z, to, way).wait_send()

    cross(z).wait_send()
    hand(z, 0).wait_send()
    for r in range(1, HOPS + 1):
        for way, origin, to in ((0, z - r, z + 1), (1, z + r, z - 1)):

            @pl.when(inside(origin))
            def _(way=way, origin=origin, to=to):
                @pl.when(inside(to))
                def _():
                    along(origin, to, way).wait_send()

                cross(origin).wait_send()
                hand(origin, 0).wait_send()

    for origin in range(4):
        hand(origin, 1).wait_send()
    for s in range(steps):
        hand_part(s).wait_send()
    for k in range(4):
        cross_part(k).wait_send()
    for k in range(1, 4):
        line_part(k).wait_send()


def head(u, e, et, bias_wide):
    labels, hidden = u.shape
    whole = pl.BlockSpec(memory_space=pltpu.VMEM)
    anywhere = pl.BlockSpec(memory_space=pl.ANY)
    shape = jax.ShapeDtypeStruct
    sems = pltpu.SemaphoreType.DMA
    block = (hidden + LOG_ROWS, labels)
    return pl.pallas_call(
        head_body,
        in_specs=[whole] + [anywhere] * 3,
        out_specs=[whole] * 2,
        out_shape=[shape((hidden, labels), F32), shape((1, labels), F32)],
        scratch_shapes=[
            pltpu.VMEM(e.shape, BF),
            pltpu.VMEM(et.shape, BF),
            pltpu.VMEM(bias_wide.shape, F32),
            pltpu.VMEM((16, labels, hidden), BF),
            pltpu.VMEM((8, 2, *block), BF),
            pltpu.VMEM((8, *block), BF),
            pltpu.VMEM((4, *block), BF),
            pltpu.VMEM((4, *block), BF),
            pltpu.VMEM((4, *block), BF),
            pltpu.VMEM((4, *block), BF),
            sems((3,)),
            sems((8,)),
            sems((4,)),
            sems((4,)),
            sems((4,)),
            sems((8,)),
            sems((8,)),
            sems((8,)),
            sems((8,)),
            sems((4,)),
            sems((4,)),
            sems((4,)),
            sems((4,)),
        ],
        compiler_params=params(collective_id=4, has_side_effects=True),
        name="head",
    )(u, e, et, bias_wide)


def seg_positions(segments):
    index = jnp.arange(segments.shape[-1], dtype=jnp.int32)
    fresh = jnp.concatenate([jnp.ones((1,), dtype=bool), segments[1:] != segments[:-1]], -1)
    starts = lax.cummax(jnp.where(fresh, index, jnp.zeros_like(index)), axis=0)
    return index - starts


def pad_rows(matrix, multiple):
    return jnp.pad(matrix, ((0, -matrix.shape[0] % multiple), (0, 0)))


def slab_of(gathered, start, rows):
    if rows % 16 == 0 and start % rows == 0:
        return (gathered, start // rows, rows)
    part = gathered[:, start : start + rows].reshape(1, -1, gathered.shape[2])
    return (part, 0, part.shape[1])


def per_device(
    input_token_index,
    sentence_numbers,
    label_positions,
    label_target_token,
    sequence_task_index,
    task_loss_weight,
    optimizer_step_count,
    embed,
    position_embedding,
    norm_gain_vector,
    norm_bias_vector,
    attention_in_weight,
    attention_out_weight,
    feedforward_up,
    feedforward_down,
    layer_bias_vector,
    head_dense_bias,
    vocabulary_bias,
    adapter_down_matrix,
    adapter_up_matrix,
    adapter_moment_first,
    adapter_moment_second,
    head_projection,
    head_moment_first,
    head_moment_second,
):
    shards = lax.axis_size("dp") * lax.axis_size("fsdp")
    dp_index = lax.axis_index("dp")
    fsdp_index = lax.axis_index("fsdp")
    layers, unused, rank, up_part = adapter_up_matrix.shape
    hidden = embed.shape[1]
    tokens = input_token_index.shape[1]
    labels = label_positions.shape[1]
    qkv_rows = attention_in_weight.shape[2]
    out_rows = attention_out_weight.shape[2]
    ff_rows = feedforward_up.shape[2]
    head_rows = head_projection.shape[0]

    grouped = (lax.axis_size("dp"), lax.axis_size("fsdp")) == (2, 16)
    chunks = [
        [
            feedforward_up[layer].T,
            feedforward_down[layer],
            attention_in_weight[layer].T,
            attention_out_weight[layer].T,
        ]
        for layer in range(layers)
    ]
    ups = adapter_up_matrix.astype(BF).reshape(-1)
    up_rows = -(-ups.size // hidden)
    chunks[0] += [
        head_projection.astype(BF),
        jnp.pad(ups, (0, up_rows * hidden - ups.size)).reshape(up_rows, hidden),
    ]
    chunks = [pad_rows(jnp.concatenate(pieces, 0), 32) for pieces in chunks]

    table_rows = embed.shape[0]
    wanted = jnp.concatenate([input_token_index[0], label_target_token[0]])
    dp_count = lax.axis_size("dp")
    group_ids = lax.all_gather(wanted, "dp", axis=0, tiled=False) - dp_index * table_rows
    later_full = [lax.all_gather(chunk, BOTH, axis=0, tiled=False) for chunk in chunks[1:]]
    inside = (group_ids >= 0) & (group_ids < table_rows)
    group_ids = jnp.clip(group_ids, 0, table_rows - 1)
    mine = lax.dynamic_index_in_dim(inside, dp_index, 0, keepdims=False)
    task_range = jnp.arange(TASKS, dtype=jnp.int32)
    slice_rows = vocabulary_bias.shape[0]
    if grouped:
        pair_ids = jnp.concatenate(
            [
                lax.dynamic_index_in_dim(group_ids, (dp_index + shift) % 2, 0, keepdims=False)
                for shift in (1, 0)
            ]
        )
        other_rows, own_rows = look_up(pair_ids, embed)
        note = jnp.broadcast_to(sequence_task_index.astype(F32)[:, None], (8, 128))
        bias_rows = -(-slice_rows // 1024) * 8
        bias_block = jnp.pad(vocabulary_bias, (0, bias_rows * 128 - slice_rows)).reshape(bias_rows, 128)
        first_full, got, notes, biases, own_vocab, own_turned = start_exchange(
            other_rows, embed, chunks[0], note, bias_block, shards, slice_rows
        )
        every_task = notes[:, 0, 0].astype(jnp.int32)
        all_bias = biases.reshape(shards, -1)[:, :slice_rows].reshape(-1)
    else:
        first_full = lax.all_gather(chunks[0], BOTH, axis=0, tiled=False)
        looked = jnp.where(
            inside.reshape(-1)[:, None], embed[group_ids.reshape(-1)], jnp.zeros((), BF)
        )
        own_rows = got = lax.psum_scatter(looked, "dp", scatter_dimension=0, tiled=True)
        own_slice = lax.dynamic_slice_in_dim(embed, fsdp_index * slice_rows, slice_rows, 0)
        own_vocab = jnp.concatenate(
            [own_slice]
            + [
                lax.ppermute(
                    own_slice, "dp", [(k, (k + shift) % dp_count) for k in range(dp_count)]
                )
                for shift in range(1, dp_count)
            ],
            0,
        )
        own_turned = own_vocab.T
        every_task = lax.all_gather(sequence_task_index, BOTH, axis=0, tiled=True)
        all_bias = lax.all_gather(vocabulary_bias, BOTH, axis=0, tiled=True)
    gathered = [first_full, *later_full]
    counts = labels * jnp.sum((every_task[:, None] == task_range[None, :]).astype(F32), 0)
    task_hot = (sequence_task_index[:, None] == task_range[None, :]).astype(F32)
    row_weight = jnp.sum(task_hot[0] * (task_loss_weight / jnp.maximum(counts, 1.0)))

    slabs = [
        (slab_of(gathered[layer], 0, ff_rows), slab_of(gathered[layer], ff_rows, ff_rows))
        for layer in range(layers)
    ]
    in_weights, out_weights = [], []
    for layer in range(layers):
        at = 2 * ff_rows
        in_weights.append(gathered[layer][:, at : at + qkv_rows].reshape(-1, hidden))
        at += qkv_rows
        out_weights.append(gathered[layer][:, at : at + out_rows].reshape(-1, hidden))
    at = 2 * ff_rows + qkv_rows + out_rows
    head_full = first_full[:, at : at + head_rows].reshape(-1, hidden)
    at += head_rows
    ups_full = (
        first_full[:, at : at + up_rows]
        .reshape(shards, -1)[:, : ups.size]
        .reshape(shards, layers, 2, rank, up_part)
        .transpose(1, 2, 3, 0, 4)
        .reshape(layers, 2, rank, hidden)
    )
    blank = jnp.zeros((rank, hidden), BF)
    adapters = [
        jnp.pad(
            jnp.concatenate(
                [
                    jnp.concatenate([2 * ups_full[layer, 0], blank, blank], 1),
                    jnp.concatenate([blank, blank, 2 * ups_full[layer, 1]], 1),
                ],
                0,
            ),
            ((2 * rank * layer, 128 - 2 * rank * (layer + 1)), (0, 0)),
        )
        for layer in range(layers)
    ]
    downs = [
        jnp.pad(
            jnp.concatenate([adapter_down_matrix[layer, 0], adapter_down_matrix[layer, 1]], 1),
            ((0, 0), (2 * rank * layer, 128 - 2 * rank * (layer + 1))),
        )
        for layer in range(layers)
    ]
    bias_of = []
    for layer in range(layers):
        b = layer_bias_vector[layer][None, :]
        ff = b.shape[1] - 4 * hidden
        bias_of.append(
            (
                jnp.concatenate(
                    [b[:, :hidden], jnp.zeros((1, hidden), F32), b[:, hidden : 2 * hidden]], 1
                ),
                b[:, 2 * hidden : 3 * hidden],
                b[:, 3 * hidden : 3 * hidden + ff],
                b[:, 3 * hidden + ff :],
            )
        )
    norms_of = [
        jnp.concatenate(
            [
                norm_gain_vector[1 + 2 * layer][None],
                norm_bias_vector[1 + 2 * layer][None],
                norm_gain_vector[2 + 2 * layer][None],
                norm_bias_vector[2 + 2 * layer][None],
                norm_gain_vector[-1][None],
                norm_bias_vector[-1][None],
            ],
            0,
        )
        for layer in range(layers)
    ]

    target_rows = jnp.where(mine[tokens:, None], own_rows[tokens:], got[tokens:]).astype(F32)
    segments = sentence_numbers[0]
    spot = seg_positions(segments)[:, None]
    seg_real = segments.astype(F32)
    seg_wide = jnp.broadcast_to(seg_real[:, None], (tokens, 128))
    seg_row = seg_real[None, :]
    place_row = label_positions
    place_col = jnp.broadcast_to(label_positions.reshape(labels, 1), (labels, 128))

    own_bias = jnp.concatenate(
        [
            lax.dynamic_slice_in_dim(
                all_bias,
                ((dp_index - shift) % dp_count) * table_rows + fsdp_index * slice_rows,
                slice_rows,
                0,
            )
            for shift in range(dp_count)
        ]
    )
    vocab_block = (
        own_vocab,
        own_turned,
        jnp.broadcast_to(own_bias[:, None], (own_bias.shape[0], 128)),
    )
    target_bias = all_bias[label_target_token[0]]

    first_norm = jnp.concatenate([norm_gain_vector[:1], norm_bias_vector[:1]], 0)
    qkv, mid, hidden_rows = project(
        own_rows, got, mine[:tokens, None].astype(jnp.int32), spot, position_embedding, first_norm,
        downs[0], in_weights[0], adapters[0], bias_of[0][0],
    )
    context, logs = attend(qkv, seg_wide, seg_row)
    x_last, one, two, slope = after(
        context, hidden_rows, out_weights[0], *slabs[0], *bias_of[0][1:], norms_of[0]
    )
    *saved, features = last_forward(
        x_last, place_col, place_row, seg_wide, downs[1], in_weights[1], adapters[1], bias_of[1][0],
        out_weights[1], *slabs[1], *bias_of[1][1:], norms_of[1], head_full, head_dense_bias[None, :],
    )
    if grouped:
        mean_t, own_logs = head(features, *vocab_block)
    else:
        every = lax.all_gather(features, "fsdp", axis=0, tiled=True)
        means, local_logs = vocab(every, *vocab_block, labels)
        local_logs = local_logs.reshape(-1, labels)
        all_logs = lax.all_gather(local_logs, "fsdp", axis=0, tiled=False)
        whole_logs = jax.nn.logsumexp(all_logs, axis=0)
        scaled = (means * jnp.exp(local_logs - whole_logs)[:, None, :]).astype(BF)
        mean_t = lax.psum_scatter(scaled, "fsdp", scatter_dimension=0, tiled=True)[0].astype(F32)
        own_logs = lax.dynamic_index_in_dim(whole_logs, fsdp_index, 0, keepdims=False)
    targets = jnp.sum(features.astype(F32) * target_rows, 1) + target_bias
    own_loss = row_weight * jnp.sum(own_logs - targets)
    feat_grad = row_weight * (mean_t.T - target_rows)

    hidden_grad, dense_gradient, late = last_backward(
        feat_grad, saved, place_col, place_row, seg_wide, downs[1], in_weights[1], adapters[1],
        out_weights[1], *slabs[1], norms_of[1], head_full, 3 * rank, shards if grouped else None,
    )
    back = (hidden_grad, one, two, slope, out_weights[0], *slabs[0], norms_of[0])
    step_as_real = optimizer_step_count[0].astype(F32)
    fades = (1.0 - beta_first**step_as_real, 1.0 - beta_second**step_as_real)
    adapts = (adapter_up_matrix, adapter_moment_first, adapter_moment_second)
    heads = (head_projection, head_moment_first, head_moment_second)
    if grouped:
        facts = jnp.concatenate(
            [jnp.broadcast_to(value, (1, 128)) for value in (own_loss, *fades)]
            + [jnp.zeros((5, 128), F32)]
        )
        turned = [
            jnp.pad(a.reshape(-1, up_part).T, ((0, 0), (0, 128 - a.size // up_part))) for a in adapts
        ]
        sums, *new = finish(
            back, qkv, logs, seg_wide, seg_row, mid, dense_gradient, late, facts, heads, turned, rank, shards
        )
        dense_new = new[:3]
        adapter_new = [
            a[:, : ups.size // up_part].T.reshape(adapter_up_matrix.shape) for a in new[3:]
        ]
        masked_task_loss, gradient_norm = sums[0, 0], sums[1, 0]
    else:
        dctx = after_back(*back)
        first = attend_back(qkv, dctx, logs, seg_wide, seg_row, mid, rank)
        adapter_gradient = (first + late)[:, : 2 * rank * layers].T.reshape(layers, 2, rank, hidden)
        dense_portion = lax.psum_scatter(dense_gradient, BOTH, scatter_dimension=0, tiled=True)
        adapter_portion = lax.psum_scatter(adapter_gradient, BOTH, scatter_dimension=3, tiled=True)
        squared_entries = jnp.sum(adapter_portion * adapter_portion) + jnp.sum(
            dense_portion * dense_portion
        )
        masked_task_loss, norm_square = lax.psum((own_loss, squared_entries), BOTH)
        gradient_norm = jnp.sqrt(norm_square)
        factor = jnp.minimum(1.0, clip_limit / (gradient_norm + 1e-06))
        adapter_new = adam(adapts[0], adapter_portion * factor, *adapts[1:], *fades)
        dense_new = adam(heads[0], dense_portion * factor, *heads[1:], *fades)
    return (masked_task_loss, gradient_norm, *adapter_new, *dense_new)


def solution(mesh):
    rows = P(BOTH, None)
    in_specs = (
        rows,
        rows,
        rows,
        rows,
        P(BOTH),
        P(),
        P(),
        P("dp", None),
        P(),
        P(),
        P(),
        P(None, None, BOTH),
        P(None, None, BOTH),
        P(None, None, BOTH),
        P(None, BOTH, None),
        P(),
        P(),
        P(BOTH),
        P(),
        P(None, None, None, BOTH),
        P(None, None, None, BOTH),
        P(None, None, None, BOTH),
        rows,
        rows,
        rows,
    )
    adapter = P(None, None, None, BOTH)
    out_specs = (P(), P(), adapter, adapter, adapter, rows, rows, rows)
    return jax.shard_map(
        per_device, mesh=mesh, in_specs=in_specs, out_specs=out_specs, check_vma=False
    )
```

```python
import functools

import jax
import jax.numpy as jnp
from jax import lax
from jax.experimental import pallas as pl
from jax.experimental.pallas import tpu as pltpu
from jax.sharding import PartitionSpec as P

HEADS = 12
TASKS = 4
REACH = 128

norm_eps = 1e-05
adapter_scale = 2.0
clip_limit = 0.01
learn_rate = 0.05
beta_first = 0.9
beta_second = 0.999
adam_eps = 1e-08
decay_rate = 0.01
masked_score = -1e30

BF = jnp.bfloat16
F32 = jnp.float32
BOTH = ("dp", "fsdp")
VMEM_BYTES = 60 * 1024 * 1024


def mm(a, b):
    return lax.dot_general(a, b, (((1,), (0,)), ((), ())), preferred_element_type=F32)


def mm_nt(a, b):
    return lax.dot_general(a, b, (((1,), (1,)), ((), ())), preferred_element_type=F32)


def mm_tn(a, b):
    return lax.dot_general(a, b, (((0,), (0,)), ((), ())), preferred_element_type=F32)


def layer_norm(rows_in, gain, shift):
    center = rows_in - jnp.mean(rows_in, -1, keepdims=True)
    spread = jnp.mean(center * center, -1, keepdims=True)
    return center * lax.rsqrt(spread + norm_eps) * gain + shift


def norm_back(rows_in, gain, gradient):
    center = rows_in - jnp.mean(rows_in, -1, keepdims=True)
    inverse = lax.rsqrt(jnp.mean(center * center, -1, keepdims=True) + norm_eps)
    unit = center * inverse
    scaled = gradient * gain
    return inverse * (
        scaled
        - jnp.mean(scaled, -1, keepdims=True)
        - unit * jnp.mean(scaled * unit, -1, keepdims=True)
    )


def gelu_pair(v):
    size = jnp.abs(v) * 0.7071067811865476
    base = 1.0 + 0.3275911 * size
    t = pl.reciprocal(base, approx=True)
    t = t * (2.0 - base * t)
    bell = jnp.exp(-0.5 * v * v)
    poly = t * (
        0.127414796 + t * (-0.142248368 + t * (0.7107068705 + t * (-0.7265760135 + t * 0.5307027145)))
    )
    tail = poly * bell
    phi = jnp.where(v >= 0.0, 1.0 - tail, tail)
    return v * phi, phi + v * (bell * 0.3989422804014327)


def params(**more):
    return pltpu.CompilerParams(vmem_limit_bytes=VMEM_BYTES, **more)


def full(shape):
    return pl.BlockSpec(shape, lambda *_: (0,) * len(shape))


def split_of(total, most, step):
    size = (min(most, total) // step) * step
    while size > step and total % size:
        size -= step
    return size if size and total % size == 0 else total


def pair_rows(block, width):
    first = lax.broadcasted_iota(jnp.int32, block.shape, 1) < width
    return jnp.concatenate([jnp.where(first, block, 0.0), jnp.where(first, 0.0, block)], 0).astype(BF)


def pair_join(wide, width):
    rows = wide.shape[1] // 2
    return jnp.concatenate([wide[:width, :rows], wide[width:, rows:]], 0)


def masked(scores, same):
    rows = scores.shape[1] // 2
    return jnp.concatenate(
        [
            jnp.where(same, scores[:, :rows], masked_score),
            jnp.where(same, scores[:, rows:], masked_score),
        ],
        1,
    )


def project_body(
    own_ref, got_ref, mine_ref, spot_ref, spots_ref, norm_ref, down_ref, w_ref, up_ref, bias_ref,
    out_ref, mid_ref, x_ref,
):
    choose = lax.broadcasted_iota(jnp.int32, (own_ref.shape[0], spots_ref.shape[0]), 1) == spot_ref[...]
    summed = jnp.where(
        mine_ref[...] > 0, own_ref[...].astype(F32), got_ref[...].astype(F32)
    ) + mm(choose.astype(F32).astype(BF), spots_ref[...])
    x = layer_norm(summed, norm_ref[0:1, :], norm_ref[1:2, :])
    x_ref[...] = x
    low = x.astype(BF)
    mid = mm(low, down_ref[...]).astype(BF)
    mid_ref[...] = mid
    total = w_ref.shape[0]
    step = split_of(total, 768, 128)
    for start in range(0, total, step):
        part = slice(start, start + step)
        out_ref[:, part] = (
            mm_nt(low, w_ref[part, :]) + mm(mid, up_ref[:, part]) + bias_ref[:, part]
        ).astype(BF)


def project(own, got, mine, spot, spots, norms, down, w, up, bias):
    rows, width = mine.shape[0], own.shape[1]
    tile = split_of(rows, 256, 16)
    total = w.shape[0]
    row = lambda n: pl.BlockSpec((tile, n), lambda i: (i, 0))
    return pl.pallas_call(
        project_body,
        grid=(rows // tile,),
        in_specs=[row(width), row(width), row(1), row(1)]
        + [full(a.shape) for a in (spots, norms, down, w, up, bias)],
        out_specs=[row(total), row(down.shape[1]), row(width)],
        out_shape=[
            jax.ShapeDtypeStruct((rows, total), BF),
            jax.ShapeDtypeStruct((rows, down.shape[1]), BF),
            jax.ShapeDtypeStruct((rows, width), F32),
        ],
        compiler_params=params(),
        name="project",
    )(own, got, mine, spot, spots, norms, down, w, up, bias)


def attend_body(q_ref, k_ref, v_ref, seg_ref, seg_row_ref, ctx_ref, log_ref):
    rows = q_ref.shape[0]
    width = q_ref.shape[1] // 2
    scale = width**-0.5
    for start in range(0, rows, REACH):
        own = slice(start, start + REACH)
        near = slice(max(0, start - REACH), min(rows, start + 2 * REACH))
        queries = pair_rows(q_ref[own, :].astype(F32) * scale, width)
        same = seg_ref[near, :] == seg_row_ref[:, own]
        scores = masked(mm_nt(k_ref[near, :], queries), same)
        top = jnp.max(scores, 0, keepdims=True)
        weights = jnp.exp(scores - top)
        total = jnp.sum(weights, 0, keepdims=True)
        context = mm_tn(v_ref[near, :], weights.astype(BF)) * (1.0 / total)
        ctx_ref[own, :] = pair_join(context, width).T.astype(BF)
        log_ref[0, :, 2 * start : 2 * start + 2 * REACH] = top + jnp.log(total)


def attend(qkv, seg_wide, seg_row):
    rows, total = qkv.shape
    hidden = total // 3
    lanes = 2 * (hidden // HEADS)
    pairs = hidden // lanes
    column = lambda kind: pl.BlockSpec((rows, lanes), lambda p: (0, kind * pairs + p))
    return pl.pallas_call(
        attend_body,
        grid=(pairs,),
        in_specs=[column(0), column(1), column(2), full(seg_wide.shape), full(seg_row.shape)],
        out_specs=[
            pl.BlockSpec((rows, lanes), lambda p: (0, p)),
            pl.BlockSpec((1, 1, 2 * rows), lambda p: (p, 0, 0)),
        ],
        out_shape=[
            jax.ShapeDtypeStruct((rows, hidden), BF),
            jax.ShapeDtypeStruct((pairs, 1, 2 * rows), F32),
        ],
        compiler_params=params(),
        name="attend",
    )(qkv, qkv, qkv, seg_wide, seg_row)


def flat(ref):
    whole = ref[...]
    return whole.reshape(-1, whole.shape[-1])


def rows_of(ref, start, size):
    each = ref.shape[1]
    if size % each == 0 and start % each == 0 and each % 16 == 0:
        part = ref[start // each : (start + size) // each, :, :]
        return part.reshape(size, part.shape[-1])
    return flat(ref)[start : start + size, :]


def feed_step(ref):
    units = ref.shape[0] * ref.shape[1]
    step = ref.shape[1]
    while units % (2 * step) == 0 and 2 * step <= 768 and ref.shape[0] > 1:
        step *= 2
    return units, (step if ref.shape[0] > 1 else split_of(units, 768, 128))


def after_body(
    ctx_ref, x_ref, wo_ref, up_ref, down_ref, bo_ref, b1_ref, b2_ref, norm_ref,
    out_ref, one_ref, two_ref, slope_ref,
):
    one = x_ref[...] + (mm_nt(ctx_ref[...], wo_ref[...]) + bo_ref[...])
    one_ref[...] = one
    middle = layer_norm(one, norm_ref[0:1, :], norm_ref[1:2, :])
    low = middle.astype(BF)
    total = middle + b2_ref[...]
    units, step = feed_step(up_ref)
    for start in range(0, units, step):
        part = slice(start, start + step)
        act, slope = gelu_pair(mm_nt(low, rows_of(up_ref, start, step)) + b1_ref[:, part])
        slope_ref[:, part] = slope.astype(BF)
        total = total + mm(act.astype(BF), rows_of(down_ref, start, step))
    two_ref[...] = total
    out_ref[...] = layer_norm(total, norm_ref[2:3, :], norm_ref[3:4, :])


def slab_spec(slab):
    array, place, rows = slab
    return pl.BlockSpec((array.shape[0], rows, array.shape[2]), lambda *_: (0, place, 0))


def after(ctx, x, wo, up, down, bo, b1, b2, norms):
    rows, width = x.shape
    tile = split_of(rows, 256, 16)
    units = b1.shape[1]
    row = lambda n: pl.BlockSpec((tile, n), lambda i: (i, 0))
    return pl.pallas_call(
        after_body,
        grid=(rows // tile,),
        in_specs=[row(width), row(width), full(wo.shape), slab_spec(up), slab_spec(down)]
        + [full(a.shape) for a in (bo, b1, b2, norms)],
        out_specs=[row(width), row(width), row(width), row(units)],
        out_shape=[jax.ShapeDtypeStruct((rows, width), F32)] * 3
        + [jax.ShapeDtypeStruct((rows, units), BF)],
        compiler_params=params(),
        name="after",
    )(ctx, x, wo, up[0], down[0], bo, b1, b2, norms)


def exact_rows(choose, matrix):
    high = matrix.astype(BF)
    rest = matrix - high.astype(F32)
    middle = rest.astype(BF)
    low = (rest - middle.astype(F32)).astype(BF)
    return mm(choose, high) + mm(choose, middle) + mm(choose, low)


def unpack_rows(slab_ref, targets):
    shards = slab_ref.shape[0]

    @pl.loop(0, shards // 2)
    def _(k):
        first, second = slab_ref[2 * k].astype(F32), slab_ref[2 * k + 1].astype(F32)
        at = 0
        for target in targets:
            each = target.shape[0] // shards
            both = jnp.concatenate([first[at : at + each], second[at : at + each]], 0)
            target[pl.ds(pl.multiple_of(2 * each * k, 2 * each), 2 * each), :] = both.astype(BF)
            at += each


def last_forward_body(
    x_ref, place_ref, place_row_ref, seg_ref, down_ref, adapt_ref, bias_ref, weights_any, up_any, dn_any,
    bo_ref, b1_ref, b2_ref, norm_ref, hbias_ref,
    kv_ref, q_ref, mid_ref, log_ref, one_ref, slope_ref, two_ref, low_ref, act_ref, hslope_ref, feat_ref, *more,
    places, starts,
):
    copies = []
    if starts is None:
        up_ref, dn_ref, ctx_ref, w_ref, wo_ref, hb_ref, sems = more
        sources = zip(weights_any, (w_ref, wo_ref, hb_ref))
    else:
        w_out, wo_out, hb_out, up_ref, dn_ref, ctx_ref, w_ref, wo_ref, hb_ref, in_slab, hb_slab, sems = more
        sources = [
            (weights_any[0].at[:, pl.ds(start, slab.shape[1]), :], slab)
            for start, slab in zip(starts, (in_slab, hb_slab))
        ]
    for source, target in sources:
        copies.append((source, target))
    early = len(copies)
    for source, target, place in ((up_any, up_ref, places[0]), (dn_any, dn_ref, places[1])):
        each = target.shape[1]
        copies.append((source.at[:, pl.ds(place * each, each), :], target))
    copies = [pltpu.make_async_copy(*ends, sems.at[k]) for k, ends in enumerate(copies)]
    for copy in copies:
        copy.start()
    for copy in copies[:early]:
        copy.wait()
    copies = copies[early:]
    if starts is not None:
        unpack_rows(in_slab, (w_ref, wo_ref))
        unpack_rows(hb_slab, (hb_ref,))
        for k, ends in enumerate(((w_ref, w_out), (wo_ref, wo_out), (hb_ref, hb_out))):
            copies.append(pltpu.make_async_copy(*ends, sems.at[4 + k]))
            copies[-1].start()
    rows, hidden = x_ref.shape
    labels = place_ref.shape[0]
    lanes = 2 * (hidden // HEADS)
    width = lanes // 2
    low = x_ref[...].astype(BF)
    mid = mm(low, down_ref[...]).astype(BF)
    mid_ref[...] = mid
    step = split_of(2 * hidden, 512, 128)
    for start in range(hidden, 3 * hidden, step):
        part = slice(start, start + step)
        kv_ref[:, start - hidden : start - hidden + step] = (
            mm_nt(low, w_ref[part, :]) + mm(mid, adapt_ref[:, part]) + bias_ref[:, part]
        ).astype(BF)
    choose = (
        lax.broadcasted_iota(jnp.int32, (labels, rows), 1) == place_ref[...][:, 0:1]
    ).astype(F32).astype(BF)
    own = exact_rows(choose, x_ref[...])
    own_low = own.astype(BF)
    own_mid = mm(choose, mid).astype(BF)
    q_ref[...] = (
        mm_nt(own_low, w_ref[:hidden, :]) + mm(own_mid, adapt_ref[:, :hidden]) + bias_ref[:, :hidden]
    ).astype(BF)
    seg = seg_ref[...]
    seg_own = jnp.sum(
        jnp.where(
            lax.broadcasted_iota(jnp.int32, (rows, labels), 0) == place_row_ref[...], seg, 0.0
        ),
        0,
        keepdims=True,
    )
    same = seg == seg_own
    for p in range(hidden // lanes):
        part = slice(p * lanes, (p + 1) * lanes)
        queries = pair_rows(q_ref[:, part].astype(F32) * width**-0.5, width)
        scores = masked(mm_nt(kv_ref[:, part], queries), same)
        top = jnp.max(scores, 0, keepdims=True)
        weights = jnp.exp(scores - top)
        total = jnp.sum(weights, 0, keepdims=True)
        context = mm_tn(
            kv_ref[:, hidden + p * lanes : hidden + (p + 1) * lanes], weights.astype(BF)
        ) * (1.0 / total)
        ctx_ref[:, part] = pair_join(context, width).T.astype(BF)
        log_ref[p : p + 1, :] = top + jnp.log(total)
    one = own + (mm_nt(ctx_ref[...], wo_ref[...]) + bo_ref[...])
    one_ref[...] = one
    middle = layer_norm(one, norm_ref[0:1, :], norm_ref[1:2, :])
    middle_low = middle.astype(BF)
    sum_two = middle + b2_ref[...]
    units, step = feed_step(up_ref)
    for copy in copies:
        copy.wait()
    for start in range(0, units, step):
        part = slice(start, start + step)
        act, slope = gelu_pair(mm_nt(middle_low, rows_of(up_ref, start, step)) + b1_ref[:, part])
        slope_ref[:, part] = slope.astype(BF)
        sum_two = sum_two + mm(act.astype(BF), rows_of(dn_ref, start, step))
    two_ref[...] = sum_two
    out_low = layer_norm(sum_two, norm_ref[2:3, :], norm_ref[3:4, :]).astype(BF)
    low_ref[...] = out_low
    act, slope = gelu_pair(mm(out_low, hb_ref[...]) + hbias_ref[...])
    act_ref[...] = act
    hslope_ref[...] = slope
    feat_ref[...] = layer_norm(act, norm_ref[4:5, :], norm_ref[5:6, :]).astype(BF)


def slab_scratch(slab):
    array, place, rows = slab
    return pltpu.VMEM((array.shape[0], rows, array.shape[2]), BF)


def last_forward(
    x, place_col, place_row, seg_wide, down, adapt, bias, weights, starts, up, dn, bo, b1, b2, norms, hbias
):
    rows, hidden = x.shape
    labels = place_col.shape[0]
    units = b1.shape[1]
    whole = pl.BlockSpec(memory_space=pltpu.VMEM)
    anywhere = pl.BlockSpec(memory_space=pl.ANY)
    shape = jax.ShapeDtypeStruct
    pairs = HEADS // 2
    matrices = [(3 * hidden, hidden), (hidden, hidden), (hidden, hidden)]
    slabs = []
    if starts is not None:
        shards = weights[0].shape[0]
        slabs = [
            pltpu.VMEM((shards, 4 * hidden // shards, hidden), BF),
            pltpu.VMEM((shards, weights[0].shape[1] - starts[1], hidden), BF),
        ]

    def body(*refs):
        head, rest = refs[:7], refs[7:]
        return last_forward_body(
            *head, rest[: len(weights)], *rest[len(weights) :], places=(up[1], dn[1]), starts=starts
        )

    return pl.pallas_call(
        body,
        in_specs=[whole] * 7 + [anywhere] * (len(weights) + 2) + [whole] * 5,
        out_specs=[whole] * 11 + ([anywhere] * 3 if slabs else []),
        out_shape=[
            shape((rows, 2 * hidden), BF),
            shape((labels, hidden), BF),
            shape((rows, down.shape[1]), BF),
            shape((pairs, 2 * labels), F32),
            shape((labels, hidden), F32),
            shape((labels, units), BF),
            shape((labels, hidden), F32),
            shape((labels, hidden), BF),
            shape((labels, hidden), F32),
            shape((labels, hidden), F32),
            shape((labels, hidden), BF),
        ]
        + ([shape(m, BF) for m in matrices] if slabs else []),
        scratch_shapes=[
            slab_scratch(up),
            slab_scratch(dn),
            pltpu.VMEM((labels, hidden), BF),
            *[pltpu.VMEM(m, BF) for m in matrices],
            *slabs,
            pltpu.SemaphoreType.DMA((7,)),
        ],
        compiler_params=params(),
        name="last_forward",
    )(x, place_col, place_row, seg_wide, down, adapt, bias, *weights, up[0], dn[0], bo, b1, b2, norms, hbias)


def vocab_body(u_ref, e_ref, et_ref, bias_ref, num_ref, log_ref, scores, weights):
    count = e_ref.shape[0]
    step = split_of(count, 640, 16)
    u = u_ref[...]
    rows = u.shape[0]
    labels = num_ref.shape[2]
    top = jnp.full((1, rows), -jnp.inf, F32)
    for start in range(0, count, step):
        part = slice(start, start + step)
        bias = bias_ref[part, :]
        logits = mm_nt(e_ref[part, :], u) + jnp.concatenate([bias] * (rows // bias.shape[1]), 1)
        scores[part, :] = logits
        top = jnp.maximum(top, jnp.max(logits, 0, keepdims=True))
    total = jnp.zeros((1, rows), F32)
    for start in range(0, count, step):
        part = slice(start, start + step)
        grown = jnp.exp(scores[part, :] - top)
        total = total + jnp.sum(grown, 0, keepdims=True)
        weights[part, :] = grown.astype(BF)
    mean = mm(et_ref[...], weights[...]) * (1.0 / total)
    logs = top + jnp.log(total)
    for k in range(rows // labels):
        num_ref[k, :, :] = mean[:, k * labels : (k + 1) * labels]
        log_ref[k, :, :] = logs[:, k * labels : (k + 1) * labels]


def vocab(u, e, et, bias_wide, labels):
    rows, hidden = u.shape
    count = e.shape[0]
    tile = 2 * labels
    return pl.pallas_call(
        vocab_body,
        grid=(rows // tile,),
        in_specs=[
            pl.BlockSpec((tile, hidden), lambda i: (i, 0)),
            full(e.shape),
            full(et.shape),
            full(bias_wide.shape),
        ],
        out_specs=[
            pl.BlockSpec((2, hidden, labels), lambda i: (i, 0, 0)),
            pl.BlockSpec((2, 1, labels), lambda i: (i, 0, 0)),
        ],
        out_shape=[
            jax.ShapeDtypeStruct((rows // labels, hidden, labels), F32),
            jax.ShapeDtypeStruct((rows // labels, 1, labels), F32),
        ],
        scratch_shapes=[pltpu.VMEM((count, tile), F32), pltpu.VMEM((count, tile), BF)],
        compiler_params=params(),
        name="vocab",
    )(u, e, et, bias_wide)


def last_backward_body(
    du_ref, kv_ref, q_ref, mid_ref, log_ref, one_ref, slope_ref, two_ref, low_ref, act_ref, hslope_ref,
    place_ref, place_row_ref, seg_ref, down_ref, w_ref, adapt_ref, wo_ref, up_any, dn_any, norm_ref, hb_ref,
    dx_ref, gh_ref, g_ref,
    up_ref, dn_ref, dkv_ref, dq_ref, sems, *, places, edge,
):
    copies = []
    for k, (source, target, place) in enumerate(
        ((up_any, up_ref, places[0]), (dn_any, dn_ref, places[1]))
    ):
        rows = target.shape[1]
        copies.append(
            pltpu.make_async_copy(
                source.at[:, pl.ds(place * rows, rows), :], target, sems.at[k]
            )
        )
        copies[-1].start()
    rows = kv_ref.shape[0]
    labels, hidden = du_ref.shape
    lanes = 2 * (hidden // HEADS)
    width = lanes // 2
    scale = width**-0.5
    dact = norm_back(act_ref[...], norm_ref[4:5, :], du_ref[...])
    dz = (hslope_ref[...] * dact).astype(BF)
    dense = mm_tn(low_ref[...], dz)
    if len(gh_ref.shape) == 2:
        gh_ref[...] = dense
    else:
        each = hidden // gh_ref.shape[0]
        spare = jnp.zeros((gh_ref.shape[1] - each, hidden), F32)
        for k in range(gh_ref.shape[0]):
            gh_ref[k] = jnp.concatenate([dense[k * each : (k + 1) * each, :], spare], 0).astype(BF)
    dtwo = norm_back(two_ref[...], norm_ref[2:3, :], mm_nt(dz, hb_ref[...]))
    dtwo_low = dtwo.astype(BF)
    dmiddle = dtwo
    units, step = feed_step(up_ref)
    for copy in copies:
        copy.wait()
    for start in range(0, units, step):
        part = slice(start, start + step)
        dgate = (
            slope_ref[:, part].astype(F32) * mm_nt(dtwo_low, rows_of(dn_ref, start, step))
        ).astype(BF)
        dmiddle = dmiddle + mm(dgate, rows_of(up_ref, start, step))
    done = norm_back(one_ref[...], norm_ref[0:1, :], dmiddle)
    dctx = mm(done.astype(BF), wo_ref[...]).astype(BF)
    seg = seg_ref[...]
    choose_t = lax.broadcasted_iota(jnp.int32, (rows, labels), 0) == place_row_ref[...]
    same = seg == jnp.sum(jnp.where(choose_t, seg, 0.0), 0, keepdims=True)
    for p in range(hidden // lanes):
        part = slice(p * lanes, (p + 1) * lanes)
        later = slice(hidden + p * lanes, hidden + (p + 1) * lanes)
        queries = pair_rows(q_ref[:, part].astype(F32) * scale, width)
        outs = pair_rows(dctx[:, part].astype(F32), width)
        keys = kv_ref[:, part]
        weights = jnp.exp(masked(mm_nt(keys, queries), same) - log_ref[p : p + 1, :])
        dweights = mm_nt(kv_ref[:, later], outs)
        inner = jnp.sum(dweights * weights, 0, keepdims=True)
        dscores = (weights * (dweights - inner)).astype(BF)
        dkv_ref[:, part] = mm(dscores, queries).astype(BF)
        dkv_ref[:, later] = mm(weights.astype(BF), outs).astype(BF)
        dq_ref[:, part] = (pair_join(mm_tn(keys, dscores), width) * scale).T.astype(BF)
    dq = dq_ref[...]
    own_mid = mm(
        (lax.broadcasted_iota(jnp.int32, (labels, rows), 1) == place_ref[...][:, 0:1]).astype(F32).astype(BF),
        mid_ref[...],
    ).astype(BF)
    g_ref[...] = adapter_scale * jnp.where(
        lax.broadcasted_iota(jnp.int32, g_ref.shape, 1) < edge,
        mm_tn(dq, own_mid),
        mm_tn(dkv_ref[:, hidden:], mid_ref[...]),
    )
    dmid_own = mm_nt(dq, adapt_ref[:, :hidden]).astype(BF)
    own = done + mm(dq, w_ref[:hidden, :]) + mm_nt(dmid_own, down_ref[...])
    spread = choose_t.astype(F32).astype(BF)
    own_high = own.astype(BF)
    own_rest = (own - own_high.astype(F32)).astype(BF)
    dmid = mm_nt(dkv_ref[:, hidden:], adapt_ref[:, 2 * hidden :]).astype(BF)
    step = split_of(hidden, 256, 128)
    for start in range(0, hidden, step):
        part = slice(start, start + step)
        dx_ref[:, part] = (
            mm(dkv_ref[...], w_ref[hidden:, part])
            + mm_nt(dmid, down_ref[part, :])
            + mm(spread, own_high[:, part])
            + mm(spread, own_rest[:, part])
        )


def last_backward(du, saved, place_col, place_row, seg_wide, down, w, adapt, wo, up, dn, norms, hb, edge, shards):
    kv = saved[0]
    rows = kv.shape[0]
    labels, hidden = du.shape
    whole = pl.BlockSpec(memory_space=pltpu.VMEM)
    anywhere = pl.BlockSpec(memory_space=pl.ANY)
    shape = jax.ShapeDtypeStruct
    return pl.pallas_call(
        functools.partial(last_backward_body, places=(up[1], dn[1]), edge=edge),
        in_specs=[whole] * 18 + [anywhere] * 2 + [whole] * 2,
        out_specs=[whole] * 3,
        out_shape=[
            shape((rows, hidden), F32),
            shape((hidden, hidden), F32)
            if shards is None
            else shape((shards, -(-hidden // shards // 16) * 16, hidden), BF),
            shape((hidden, down.shape[1]), F32),
        ],
        scratch_shapes=[
            slab_scratch(up),
            slab_scratch(dn),
            pltpu.VMEM(kv.shape, BF),
            pltpu.VMEM((labels, hidden), BF),
            pltpu.SemaphoreType.DMA((2,)),
        ],
        compiler_params=params(),
        name="last_backward",
    )(du, *saved, place_col, place_row, seg_wide, down, w, adapt, wo, up[0], dn[0], norms, hb)


def after_back_body(dout_ref, one_ref, two_ref, slope_ref, wo_ref, up_ref, down_ref, norm_ref, dctx_ref):
    dtwo = norm_back(two_ref[...], norm_ref[2:3, :], dout_ref[...])
    low = dtwo.astype(BF)
    dmiddle = dtwo
    units, step = feed_step(up_ref)
    for start in range(0, units, step):
        part = slice(start, start + step)
        dgate = (
            slope_ref[:, part].astype(F32) * mm_nt(low, rows_of(down_ref, start, step))
        ).astype(BF)
        dmiddle = dmiddle + mm(dgate, rows_of(up_ref, start, step))
    done = norm_back(one_ref[...], norm_ref[0:1, :], dmiddle)
    dctx_ref[...] = mm(done.astype(BF), wo_ref[...]).astype(BF)


def after_back(dout, one, two, slope, wo, up, down, norms):
    rows, width = dout.shape
    tile = split_of(rows, 256, 16)
    row = lambda n: pl.BlockSpec((tile, n), lambda i: (i, 0))
    return pl.pallas_call(
        after_back_body,
        grid=(rows // tile,),
        in_specs=[row(width), row(width), row(width), row(slope.shape[1]), full(wo.shape)]
        + [slab_spec(up), slab_spec(down), full(norms.shape)],
        out_specs=row(width),
        out_shape=jax.ShapeDtypeStruct((rows, width), BF),
        compiler_params=params(),
        name="after_back",
    )(dout, one, two, slope, wo, up[0], down[0], norms)


def attend_back_body(
    q_ref, k_ref, v_ref, dctx_ref, log_ref, seg_ref, seg_row_ref, mid_ref, g_ref, dv_ref, *, edge
):
    rows = q_ref.shape[0]
    width = q_ref.shape[1] // 2
    scale = width**-0.5
    dv_ref[...] = jnp.zeros_like(dv_ref)
    gq = jnp.zeros((2 * width, mid_ref.shape[1]), F32)
    for start in range(0, rows, REACH):
        own = slice(start, start + REACH)
        near = slice(max(0, start - REACH), min(rows, start + 2 * REACH))
        queries = pair_rows(q_ref[own, :].astype(F32) * scale, width)
        outs = pair_rows(dctx_ref[own, :].astype(F32), width)
        same = seg_ref[near, :] == seg_row_ref[:, own]
        keys = k_ref[near, :]
        logs = log_ref[0, :, 2 * start : 2 * start + 2 * REACH]
        weights = jnp.exp(masked(mm_nt(keys, queries), same) - logs)
        dweights = mm_nt(v_ref[near, :], outs)
        inner = jnp.sum(dweights * weights, 0, keepdims=True)
        dscores = (weights * (dweights - inner)).astype(BF)
        dv_ref[near, :] += mm(weights.astype(BF), outs)
        dq = (pair_join(mm_tn(keys, dscores), width) * scale).astype(BF)
        gq = gq + mm(dq, mid_ref[own, :])
    gv = mm_tn(dv_ref[...].astype(BF), mid_ref[...])
    g_ref[...] = adapter_scale * jnp.where(
        lax.broadcasted_iota(jnp.int32, gq.shape, 1) < edge, gq, gv
    )


def attend_back(qkv, dctx, logs, seg_wide, seg_row, mid, edge):
    rows, total = qkv.shape
    hidden = total // 3
    lanes = 2 * (hidden // HEADS)
    pairs = hidden // lanes
    column = lambda kind: pl.BlockSpec((rows, lanes), lambda p: (0, kind * pairs + p))
    return pl.pallas_call(
        functools.partial(attend_back_body, edge=edge),
        grid=(pairs,),
        in_specs=[
            column(0),
            column(1),
            column(2),
            column(0),
            pl.BlockSpec((1, 1, 2 * rows), lambda p: (p, 0, 0)),
            full(seg_wide.shape),
            full(seg_row.shape),
            full(mid.shape),
        ],
        out_specs=pl.BlockSpec((lanes, mid.shape[1]), lambda p: (p, 0)),
        out_shape=jax.ShapeDtypeStruct((hidden, mid.shape[1]), F32),
        scratch_shapes=[pltpu.VMEM((rows, lanes), F32)],
        compiler_params=params(),
        name="attend_back",
    )(qkv, qkv, qkv, dctx, logs, seg_wide, seg_row, mid)


MESH = pl.DeviceIdType.MESH


def position():
    dp, fsdp = lax.axis_index("dp"), lax.axis_index("fsdp")
    return {"x": dp, "z": fsdp // 4, "y": (fsdp // 2) % 2, "c": fsdp % 2}


def device_of(place):
    return (place["x"], (place["z"] * 2 + place["y"]) * 2 + place["c"])


def number_of(place):
    return place["x"] * 16 + (place["z"] * 2 + place["y"]) * 2 + place["c"]


def rank_device(number):
    return (number // 16, number % 16)


def greet_all(shards):
    barrier = pltpu.get_barrier_semaphore()
    me = lax.axis_index("dp") * 16 + lax.axis_index("fsdp")

    @pl.loop(1, shards)
    def _(k):
        pl.semaphore_signal(
            barrier, inc=1, device_id=rank_device((me + k) % shards), device_id_type=MESH
        )


def await_all(shards):
    pl.semaphore_wait(pltpu.get_barrier_semaphore(), shards - 1)


def direct_copy(source, target, sends, receives, me, k, shards):
    return pltpu.make_async_remote_copy(
        src_ref=source,
        dst_ref=target,
        send_sem=sends.at[k],
        recv_sem=receives.at[me],
        device_id=rank_device((me + k) % shards),
        device_id_type=MESH,
    )


def spread(piece_of, buffer, sends, receives, me, shards):
    @pl.loop(1, shards)
    def _(k):
        direct_copy(piece_of((me + k) % shards), buffer.at[me], sends, receives, me, k, shards).start()


def collect(piece_of, buffer, sends, receives, me, shards):
    @pl.loop(1, shards)
    def _(k):
        source = (me + shards - k) % shards
        direct_copy(buffer.at[source], buffer.at[source], sends, receives, source, k, shards).wait_recv()

    @pl.loop(1, shards)
    def _(k):
        direct_copy(piece_of((me + k) % shards), buffer.at[me], sends, receives, me, k, shards).wait_send()


def relative_places(order):
    places = [
        {"x": dx, "z": dz, "y": dy} for dx in (0, 1) for dz in range(-3, 4) for dy in (0, 1)
    ]
    return sorted(places, key=lambda p: (abs(p["x"]) + abs(p["z"]) + abs(p["y"]), [abs(p[a]) for a in order]))


class Gather:
    def __init__(self, chunk, full_buffer, start, rows, order, sends, receives, hands, hands_got):
        self.chunk, self.full, self.order = chunk, full_buffer, order
        self.part = pl.ds(start, rows)
        self.sends, self.receives, self.hands, self.hands_got = sends, receives, hands, hands_got
        self.here = position()
        self.items = relative_places(order)
        self.pending = []

    def origin(self, item):
        here = self.here
        return {"x": (here["x"] + item["x"]) % 2, "z": here["z"] - item["z"], "y": (here["y"] + item["y"]) % 2, "c": here["c"]}

    def key(self, place):
        return (place["x"] * 4 + place["z"]) * 2 + place["y"]

    def outward(self, item):
        deepest = max([k for k, axis in enumerate(self.order) if item[axis]], default=-1)
        ways = []
        if deepest >= 0 and self.order[deepest] == "z":
            ways.append(("z", 1 if item["z"] > 0 else -1))
        for axis in self.order[deepest + 1 :]:
            ways += [("z", 1), ("z", -1)] if axis == "z" else [(axis, 1)]
        return ways

    def copy(self, index, way, slot, item):
        here = self.here
        place = self.origin(item)
        number, key = number_of(place), self.key(place)
        mine = not any(item.values())
        source = self.chunk.at[self.part, :] if mine else self.full.at[number, self.part, :]
        if way is None:
            target = dict(here, c=1 - here["c"])
            sends, receives = self.hands.at[index], self.hands_got.at[key]
        else:
            axis, step = way
            target = dict(here)
            target[axis] = here["z"] + step if axis == "z" else 1 - here[axis]
            sends, receives = self.sends.at[index * 4 + slot], self.receives.at[key]
        return pltpu.make_async_remote_copy(
            src_ref=source,
            dst_ref=self.full.at[number, self.part, :],
            send_sem=sends,
            recv_sem=receives,
            device_id=device_of(target),
            device_id_type=MESH,
        )

    def valid(self, item):
        z = self.here["z"] - item["z"]
        return (z >= 0) & (z <= 3)

    def step(self, index):
        item = self.items[index]

        @pl.when(self.valid(item))
        def _():
            if any(item.values()):
                self.arrived(index, item)
            for slot, way in enumerate(self.outward(item)):
                self.when_way(way, lambda way=way, slot=slot: self.copy(index, way, slot, item).start())
            self.copy(index, None, 0, item).start()

    def when_way(self, way, act):
        axis, step = way
        if axis == "z":
            z = self.here["z"] + step
            pl.when((z >= 0) & (z <= 3))(act)
        else:
            act()

    def arrived(self, index, item):
        place = self.origin(item)
        spot = self.full.at[number_of(place), self.part, :]
        pltpu.make_async_remote_copy(
            src_ref=spot,
            dst_ref=spot,
            send_sem=self.sends.at[index * 4],
            recv_sem=self.receives.at[self.key(place)],
            device_id=device_of(dict(self.here, c=1 - self.here["c"])),
            device_id_type=MESH,
        ).wait_recv()

    def finish(self):
        for index, item in enumerate(self.items):

            @pl.when(self.valid(item))
            def _(index=index, item=item):
                for slot, way in enumerate(self.outward(item)):
                    self.when_way(way, lambda way=way, slot=slot: self.copy(index, way, slot, item).wait_send())
                self.copy(index, None, 0, item).wait_send()
                place = dict(self.origin(item), c=1 - self.here["c"])
                spot = self.full.at[number_of(place), self.part, :]
                pltpu.make_async_remote_copy(
                    src_ref=spot,
                    dst_ref=spot,
                    send_sem=self.hands.at[index],
                    recv_sem=self.hands_got.at[self.key(place)],
                    device_id=device_of(dict(self.here, c=1 - self.here["c"])),
                    device_id_type=MESH,
                ).wait_recv()


ITEMS = 28


def start_body(shards, rows, fact, got, facts, row_sems, sends, receives, own_sem):
    here = position()
    me = number_of(here)
    greet_all(shards)
    own = pltpu.make_async_copy(fact, facts.at[me], own_sem.at[0])
    own.start()
    await_all(shards)
    swap = pltpu.make_async_remote_copy(
        src_ref=rows,
        dst_ref=got,
        send_sem=row_sems.at[0],
        recv_sem=row_sems.at[1],
        device_id=device_of(dict(here, x=1 - here["x"])),
        device_id_type=MESH,
    )
    swap.start()
    spread(lambda peer: fact, facts, sends, receives, me, shards)
    collect(lambda peer: fact, facts, sends, receives, me, shards)
    swap.wait()
    own.wait()


def start_exchange(rows, fact, shards):
    anywhere = pl.BlockSpec(memory_space=pl.ANY)
    shape = jax.ShapeDtypeStruct
    sems = pltpu.SemaphoreType.DMA
    return pl.pallas_call(
        functools.partial(start_body, shards),
        in_specs=[anywhere] * 2,
        out_specs=[anywhere] * 2,
        out_shape=[shape(rows.shape, rows.dtype), shape((shards, *fact.shape), fact.dtype)],
        scratch_shapes=[sems((2,)), sems((shards,)), sems((shards,)), sems((1,))],
        compiler_params=params(collective_id=1, has_side_effects=True),
        name="start_exchange",
    )(rows, fact)


def first_layer_body(
    streams, shards, places,
    own_any, got_any, first_any, chunk, table_any, mine_ref, spot_ref, spots_ref, first_norm_ref, down_ref,
    adapt_ref, bias_ref, seg_ref, seg_row_ref, bo_ref, b1_ref, b2_ref, norm_ref,
    qkv_out, x_out, one_out, two_out, slope_out, wo_out, full_chunk, e_out, et_out, mid_ref, log_ref,
    own, got, in_slab, w, wo, up, dn, x, qkv, ctx, two, out, slope, e_ref, et_ref,
    load_sems, tile_sems, out_sems, swap_sems, sends, receives, hands, hands_got,
):
    here = position()
    me = number_of(here)
    across = device_of(dict(here, x=1 - here["x"]))
    rows, hidden = x.shape
    tile = split_of(rows, 256, 16)
    tiles = rows // tile
    lanes = 2 * (hidden // HEADS)
    pairs = hidden // lanes
    slice_rows = e_ref.shape[0] // 2
    own_slice = table_any.at[pl.ds(pl.multiple_of((me % 16) * slice_rows, 16), slice_rows), :]

    def slab(target, place):
        each = target.shape[1]
        return first_any.at[:, pl.ds(place * each, each), :]

    loads = [
        pltpu.make_async_copy(source, target, load_sems.at[k])
        for k, (source, target) in enumerate(
            (
                (own_any.at[pl.ds(0, rows), :], own),
                (got_any.at[pl.ds(0, rows), :], got),
                (first_any.at[:, pl.ds(places[2], in_slab.shape[1]), :], in_slab),
                (slab(up, places[0]), up),
                (slab(dn, places[1]), dn),
                (own_slice, e_ref.at[pl.ds(0, slice_rows), :]),
                (chunk, full_chunk.at[me]),
            )
        )
    ]
    for copy in loads:
        copy.start()
    barrier = pltpu.get_barrier_semaphore()
    peers = [
        dict(here, c=1 - here["c"]),
        dict(here, x=1 - here["x"]),
        dict(here, y=1 - here["y"]),
        *[dict(here, z=flip(here["z"], k)) for k in (1, 2, 3)],
    ]
    for peer in peers:
        pl.semaphore_signal(barrier, inc=1, device_id=device_of(peer), device_id_type=MESH)
    pl.semaphore_wait(barrier, len(peers))
    gathers = [
        Gather(
            chunk, full_chunk, start, size, order, sends.at[k], receives.at[k], hands.at[k], hands_got.at[k]
        )
        for k, (start, size, order) in enumerate(streams)
    ]
    swap = pltpu.make_async_remote_copy(
        src_ref=own_slice,
        dst_ref=e_ref.at[pl.ds(slice_rows, slice_rows), :],
        send_sem=swap_sems.at[0],
        recv_sem=swap_sems.at[1],
        device_id=across,
        device_id_type=MESH,
    )

    def advance(first, last):
        for index in range(first, last + 1):
            for gather in gathers:
                gather.step(index)

    advance(0, 0)
    for copy in loads[:3]:
        copy.wait()
    unpack_rows(in_slab, (w, wo))

    @pl.loop(0, tiles)
    def _(i):
        part = pl.ds(pl.multiple_of(i * tile, tile), tile)
        project_body(
            own.at[part, :], got.at[part, :], mine_ref.at[part, :], spot_ref.at[part, :], spots_ref,
            first_norm_ref, down_ref, w, adapt_ref, bias_ref, qkv.at[part, :], mid_ref.at[part, :],
            x.at[part, :],
        )

        @pl.when(i == tiles - 2)
        def _():
            advance(1, 4)
            swap.start()

    early = [
        pltpu.make_async_copy(qkv, qkv_out, out_sems.at[0]),
        pltpu.make_async_copy(wo, wo_out, out_sems.at[1]),
    ]
    for copy in early:
        copy.start()

    @pl.loop(0, pairs)
    def _(p):
        column = lambda kind: pl.ds(pl.multiple_of((kind * pairs + p) * lanes, lanes), lanes)
        attend_body(
            qkv.at[:, column(0)], qkv.at[:, column(1)], qkv.at[:, column(2)], seg_ref, seg_row_ref,
            ctx.at[:, column(0)], log_ref.at[pl.ds(p, 1)],
        )

        @pl.when(p == pairs // 2 - 1)
        def _():
            advance(5, 11)

        @pl.when(p == pairs - 1)
        def _():
            advance(12, 15)

    for copy in loads[3:5]:
        copy.wait()

    def tile_copies(i):
        part = pl.ds(pl.multiple_of(i * tile, tile), tile)
        turn = i % 2
        return [
            pltpu.make_async_copy(source, target.at[part, :], tile_sems.at[k, i])
            for k, (source, target) in enumerate(
                (
                    (out.at[turn], x_out),
                    (two.at[turn], two_out),
                    (slope.at[turn], slope_out),
                    (x.at[part, :], one_out),
                )
            )
        ]

    plan = {tiles - 4: (16, 19), tiles - 3: (20, 22), tiles - 2: (23, 25), tiles - 1: (26, 27)}

    @pl.loop(0, tiles)
    def _(i):
        part = pl.ds(pl.multiple_of(i * tile, tile), tile)
        turn = i % 2

        @pl.when(i >= 2)
        def _():
            for copy in tile_copies(i - 2):
                copy.wait()

        after_body(
            ctx.at[part, :], x.at[part, :], wo, up, dn, bo_ref, b1_ref, b2_ref, norm_ref, out.at[turn],
            x.at[part, :], two.at[turn], slope.at[turn],
        )
        for copy in tile_copies(i):
            copy.start()
        for k, (first, last) in plan.items():
            pl.when(i == k)(functools.partial(advance, first, last))

    loads[5].wait()
    swap.wait_recv()

    @pl.loop(0, e_ref.shape[0] // 128)
    def _(k):
        part = pl.ds(pl.multiple_of(k * 128, 128), 128)
        et_ref[:, part] = e_ref[part, :].astype(F32).T.astype(BF)

    late = [
        pltpu.make_async_copy(e_ref, e_out, out_sems.at[2]),
        pltpu.make_async_copy(et_ref, et_out, out_sems.at[3]),
    ]
    for copy in late:
        copy.start()
    for gather in gathers:
        gather.finish()
    for i in (tiles - 2, tiles - 1):
        for copy in tile_copies(i):
            copy.wait()
    swap.wait_send()
    for copy in early + late + loads[6:]:
        copy.wait()


def first_layer(own, got, first, chunk, table, more, places, units, slice_rows, shards):
    whole = pl.BlockSpec(memory_space=pltpu.VMEM)
    anywhere = pl.BlockSpec(memory_space=pl.ANY)
    mine, down = more[0], more[4]
    rows, hidden = mine.shape[0], table.shape[1]
    tile = split_of(rows, 256, 16)
    pairs = HEADS // 2
    cut = (chunk.shape[0] * 5 // 6 + 15) // 16 * 16
    streams = ((0, cut, "xzy"), (cut, chunk.shape[0] - cut, "xyz"))
    each = units // shards
    shape = jax.ShapeDtypeStruct
    sems = pltpu.SemaphoreType.DMA
    return pl.pallas_call(
        functools.partial(first_layer_body, streams, shards, places),
        in_specs=[anywhere] * 5 + [whole] * len(more),
        out_specs=[anywhere] * 9 + [whole] * 2,
        out_shape=[
            shape((rows, 3 * hidden), BF),
            shape((rows, hidden), F32),
            shape((rows, hidden), F32),
            shape((rows, hidden), F32),
            shape((rows, units), BF),
            shape((hidden, hidden), BF),
            shape((shards, *chunk.shape), BF),
            shape((2 * slice_rows, hidden), BF),
            shape((hidden, 2 * slice_rows), BF),
            shape((rows, down.shape[1]), BF),
            shape((pairs, 1, 2 * rows), F32),
        ],
        scratch_shapes=[
            pltpu.VMEM((rows, hidden), BF),
            pltpu.VMEM((rows, hidden), BF),
            pltpu.VMEM((shards, 4 * hidden // shards, hidden), BF),
            pltpu.VMEM((3 * hidden, hidden), BF),
            pltpu.VMEM((hidden, hidden), BF),
            pltpu.VMEM((shards, each, hidden), BF),
            pltpu.VMEM((shards, each, hidden), BF),
            pltpu.VMEM((rows, hidden), F32),
            pltpu.VMEM((rows, 3 * hidden), BF),
            pltpu.VMEM((rows, hidden), BF),
            pltpu.VMEM((2, tile, hidden), F32),
            pltpu.VMEM((2, tile, hidden), F32),
            pltpu.VMEM((2, tile, units), BF),
            pltpu.VMEM((2 * slice_rows, hidden), BF),
            pltpu.VMEM((hidden, 2 * slice_rows), BF),
            sems((7,)),
            sems((4, rows // tile)),
            sems((4,)),
            sems((2,)),
            sems((2, 4 * ITEMS)),
            sems((2, 16)),
            sems((2, ITEMS)),
            sems((2, 16)),
        ],
        compiler_params=params(collective_id=3, has_side_effects=True),
        name="first_layer",
    )(own, got, first, chunk, table, *more)


PICK = 64
GROUP = 16


def look_up_body(ids, low_ref, table, first_ref, second_ref, stage):
    batches = first_ref.shape[0] // PICK
    for k, out in enumerate((first_ref, second_ref)):

        @pl.loop(0, batches)
        def _(b, k=k, out=out):
            at = (k * batches + b) * PICK

            def one(t, carry):
                stage[t] = table[ids[at + t]]
                return carry

            lax.fori_loop(0, PICK, one, 0, unroll=8)
            choose = (
                lax.broadcasted_iota(jnp.int32, (PICK, PICK * GROUP), 1)
                == low_ref[pl.ds(pl.multiple_of(at, PICK), PICK), :]
            )
            out[pl.ds(pl.multiple_of(b * PICK, PICK), PICK), :] = mm(
                choose.astype(F32).astype(BF), flat(stage)
            ).astype(BF)


def look_up(ids, table):
    whole = pl.BlockSpec(memory_space=pltpu.VMEM)
    hidden = table.shape[1]
    low = jnp.arange(ids.size, dtype=jnp.int32) % PICK * GROUP + ids % GROUP
    return pl.pallas_call(
        look_up_body,
        in_specs=[pl.BlockSpec(memory_space=pltpu.SMEM), whole, whole],
        out_specs=[whole] * 2,
        out_shape=[jax.ShapeDtypeStruct((ids.size // 2, hidden), table.dtype)] * 2,
        scratch_shapes=[pltpu.VMEM((PICK, GROUP, hidden), table.dtype)],
        compiler_params=params(),
        name="look_up",
    )(ids // GROUP, low[:, None], table.reshape(-1, GROUP, hidden))


def adam(weight, gradient, moment_one, moment_two, fade_one, fade_two):
    moment_one = beta_first * moment_one + (1.0 - beta_first) * gradient
    moment_two = beta_second * moment_two + (1.0 - beta_second) * gradient * gradient
    one_hat = moment_one / fade_one
    two_hat = moment_two / fade_two
    weight = weight - learn_rate * (one_hat / (jnp.sqrt(two_hat) + adam_eps) + decay_rate * weight)
    return (weight, moment_one, moment_two)


def finish_body(
    shards, places, edge,
    dout_any, one_any, two_any, slope_any, wo_any, up_any, dn_any, qkv_any, norm_ref, log_ref, seg_ref,
    seg_row_ref, mid_ref, parts, late_ref, facts, head_w, head_m, head_v, adapt_w, adapt_m, adapt_v,
    sums_ref, head_w_out, head_m_out, head_v_out, adapt_w_out, adapt_m_out, adapt_v_out,
    dout, one, two, slope, wo, up, dn, qkv, dctx, dv, grad, dense_got, grad_got, note, notes,
    tile_sems, load_sems, dense_send, dense_get, grad_send, grad_get, note_send, note_get,
):
    rows, hidden = dout.shape
    tile = split_of(rows, 256, 16)
    tiles = rows // tile
    me = number_of(position())

    def tile_loads(i):
        part = pl.ds(pl.multiple_of(i * tile, tile), tile)
        return [
            pltpu.make_async_copy(source.at[part, :], target.at[part, :], tile_sems.at[k, i])
            for k, (source, target) in enumerate(
                ((two_any, two), (dout_any, dout), (slope_any, slope), (one_any, one))
            )
        ]

    def slab(source, target, place):
        each = target.shape[1]
        return source.at[:, pl.ds(place * each, each), :]

    loads = [
        pltpu.make_async_copy(source, target, load_sems.at[k])
        for k, (source, target) in enumerate(
            (
                (slab(dn_any, dn, places[1]), dn),
                (slab(up_any, up, places[0]), up),
                (wo_any, wo),
                (qkv_any, qkv),
            )
        )
    ]
    for copy in tile_loads(0) + loads[:3]:
        copy.start()
    for i in range(1, tiles):
        for copy in tile_loads(i):
            copy.start()
    loads[3].start()
    greet_all(shards)
    dense_got[me] = parts[me]
    for copy in loads[:3]:
        copy.wait()

    @pl.loop(0, tiles)
    def _(i):
        for copy in tile_loads(i):
            copy.wait()
        part = pl.ds(pl.multiple_of(i * tile, tile), tile)
        after_back_body(
            dout.at[part, :], one.at[part, :], two.at[part, :], slope.at[part, :], wo, up, dn, norm_ref,
            dctx.at[part, :],
        )

        @pl.when(i == 0)
        def _():
            await_all(shards)
            spread(lambda peer: parts.at[peer], dense_got, dense_send, dense_get, me, shards)

    loads[3].wait()
    lanes = 2 * (hidden // HEADS)
    pairs = hidden // lanes

    @pl.loop(0, pairs)
    def _(p):
        column = lambda kind: pl.ds(pl.multiple_of((kind * pairs + p) * lanes, lanes), lanes)
        attend_back_body(
            qkv.at[:, column(0)], qkv.at[:, column(1)], qkv.at[:, column(2)], dctx.at[:, column(0)],
            log_ref.at[pl.ds(p, 1)], seg_ref, seg_row_ref, mid_ref, grad.at[column(0), :], dv, edge=edge,
        )

    grad[...] = grad[...] + late_ref[...]
    each = hidden // shards
    piece = lambda peer: grad.at[pl.ds(pl.multiple_of(peer * each, each), each), :]
    grad_got[me] = piece(me)[...]
    spread(piece, grad_got, grad_send, grad_get, me, shards)
    collect(lambda peer: parts.at[peer], dense_got, dense_send, dense_get, me, shards)
    dense = jnp.zeros((each, hidden), F32)
    for k in range(shards):
        dense = dense + dense_got[k].astype(F32)[:each, :]
    square = jnp.sum(dense * dense, keepdims=True)
    collect(piece, grad_got, grad_send, grad_get, me, shards)
    total = grad_got[0]
    for k in range(1, shards):
        total = total + grad_got[k]
    square = square + jnp.sum(total * total, keepdims=True)
    row = lax.broadcasted_iota(jnp.int32, note.shape, 0)
    note[...] = jnp.where(row == 0, facts[...], jnp.where(row == 1, square, 0.0))
    notes[me] = note[...]
    spread(lambda peer: note, notes, note_send, note_get, me, shards)
    collect(lambda peer: note, notes, note_send, note_get, me, shards)
    sums = notes[0]
    for k in range(1, shards):
        sums = sums + notes[k]
    norm = jnp.sqrt(sums[1:2, :])
    sums_ref[...] = jnp.where(row == 1, norm, sums)
    factor = jnp.minimum(1.0, clip_limit / (norm + 1e-06))[:, 0:1]
    fades = facts[1:2, 0:1], facts[2:3, 0:1]
    new = adam(head_w[...], dense * factor, head_m[...], head_v[...], *fades)
    head_w_out[...], head_m_out[...], head_v_out[...] = new
    new = adam(adapt_w[...], total * factor, adapt_m[...], adapt_v[...], *fades)
    adapt_w_out[...], adapt_m_out[...], adapt_v_out[...] = new


def finish(back, qkv, logs, seg_wide, seg_row, mid, parts, late, facts, heads, adapts, edge, shards):
    dout, one, two, slope, wo, up, dn, norms = back
    rows, hidden = dout.shape
    each = hidden // shards
    whole = pl.BlockSpec(memory_space=pltpu.VMEM)
    anywhere = pl.BlockSpec(memory_space=pl.ANY)
    shape = jax.ShapeDtypeStruct
    sems = pltpu.SemaphoreType.DMA
    tiles = rows // split_of(rows, 256, 16)
    return pl.pallas_call(
        functools.partial(finish_body, shards, (up[1], dn[1]), edge),
        in_specs=[anywhere] * 8 + [whole] * 14,
        out_specs=[whole] * 7,
        out_shape=[shape((8, 128), F32)]
        + [shape(a.shape, F32) for a in heads]
        + [shape(a.shape, F32) for a in adapts],
        scratch_shapes=[
            pltpu.VMEM((rows, hidden), F32),
            pltpu.VMEM((rows, hidden), F32),
            pltpu.VMEM((rows, hidden), F32),
            pltpu.VMEM(slope.shape, BF),
            pltpu.VMEM(wo.shape, BF),
            slab_scratch(up),
            slab_scratch(dn),
            pltpu.VMEM(qkv.shape, BF),
            pltpu.VMEM((rows, hidden), BF),
            pltpu.VMEM((rows, 2 * (hidden // HEADS)), F32),
            pltpu.VMEM(late.shape, F32),
            pltpu.VMEM(parts.shape, BF),
            pltpu.VMEM((shards, each, late.shape[1]), F32),
            pltpu.VMEM((8, 128), F32),
            pltpu.VMEM((shards, 8, 128), F32),
            sems((4, tiles)),
            sems((4,)),
        ]
        + [sems((shards,))] * 6,
        compiler_params=params(collective_id=2, has_side_effects=True),
        name="finish",
    )(dout, one, two, slope, wo, up[0], dn[0], qkv, norms, logs, seg_wide, seg_row, mid, parts, late, facts, *heads, *adapts)


HOPS = 3
LOG_ROWS = 16


def flip(z, k):
    return (z % 2 + k % 2) % 2 + 2 * ((z // 2 + k // 2) % 2)


def pack_log(log_row, rows):
    high = log_row.astype(BF).astype(F32)
    middle = (log_row - high).astype(BF).astype(F32)
    low = log_row - high - middle
    row = lax.broadcasted_iota(jnp.int32, (rows, log_row.shape[1]), 0)
    return jnp.where(
        row == 0, high, jnp.where(row == 1, middle, jnp.where(row == 2, low, 0.0))
    ).astype(BF)


def unpack(block, hidden):
    logs = block[hidden : hidden + LOG_ROWS, :].astype(F32)
    return block[:hidden, :].astype(F32), jnp.sum(logs, 0, keepdims=True)


def merged(one, two):
    top = jnp.maximum(one[1], two[1])
    first, second = jnp.exp(one[1] - top), jnp.exp(two[1] - top)
    total = first + second
    inverse = 1.0 / total
    return one[0] * (first * inverse) + two[0] * (second * inverse), top + jnp.log(total)


def store_packed(ref, pair, hidden):
    ref[:hidden, :] = pair[0].astype(BF)
    ref[hidden : hidden + LOG_ROWS, :] = pack_log(pair[1], LOG_ROWS)


def head_body(
    u_ref, e_any, et_any, bias_any, mean_ref, log_ref,
    e_ref, et_ref, bias_ref, feats, packs, handed, crossed, kept, lined, zouts,
    loads, z_send, z_get, y_send, y_get, c_send, c_get, h_send, h_get, p_send, p_get, l_send, l_get,
):
    here = position()
    z, y, c = here["z"], here["y"], here["c"]
    labels, hidden = u_ref.shape
    slot_of = lambda zz, yy, cc: (zz * 2 + yy) * 2 + cc
    me = slot_of(z, y, c)
    sibling = device_of(dict(here, c=1 - c))
    beside = device_of(dict(here, y=1 - y))
    at_z = lambda zz: device_of(dict(here, z=zz))
    inside = lambda zz: (zz >= 0) & (zz <= HOPS)

    fills = [
        pltpu.make_async_copy(source, target, loads.at[k])
        for k, (source, target) in enumerate(((e_any, e_ref), (bias_any, bias_ref), (et_any, et_ref)))
    ]
    for fill in fills:
        fill.start()
    barrier = pltpu.get_barrier_semaphore()
    for target in (sibling, beside):
        pl.semaphore_signal(barrier, inc=1, device_id=target, device_id_type=MESH)
    for k in range(1, 4):
        pl.semaphore_signal(barrier, inc=1, device_id=at_z(flip(z, k)), device_id_type=MESH)
    feats[me] = u_ref[...]
    pl.semaphore_wait(barrier, 5)

    def move(slot, device, send, get):
        return pltpu.make_async_remote_copy(
            src_ref=feats.at[slot],
            dst_ref=feats.at[slot],
            send_sem=send,
            recv_sem=get,
            device_id=device,
            device_id_type=MESH,
        )

    def hand(zz, other):
        slot = slot_of(zz, (y + other) % 2, c)
        return move(slot, sibling, c_send.at[other * 4 + zz], c_get.at[other * 4 + zz])

    def handed_here(zz, other):
        slot = slot_of(zz, (y + other) % 2, 1 - c)
        return move(slot, sibling, c_send.at[other * 4 + zz], c_get.at[other * 4 + zz])

    def cross(zz):
        return move(slot_of(zz, y, c), beside, y_send.at[zz], y_get.at[zz])

    def crossed_here(zz):
        return move(slot_of(zz, 1 - y, c), beside, y_send.at[zz], y_get.at[zz])

    def along(zz, to, way):
        return move(slot_of(zz, y, c), at_z(to), z_send.at[way * 4 + zz], z_get.at[zz])

    def own_round():
        for way, to in ((0, z + 1), (1, z - 1)):

            @pl.when(inside(to))
            def _(way=way, to=to):
                along(z, to, way).start()

        cross(z).start()
        hand(z, 0).start()

    def later_round(r):
        if r <= HOPS:
            for way, origin, to in ((0, z - r, z + 1), (1, z + r, z - 1)):

                @pl.when(inside(origin))
                def _(way=way, origin=origin, to=to):
                    along(origin, to, way).wait_recv()

                    @pl.when(inside(to))
                    def _():
                        along(origin, to, way).start()

                    cross(origin).start()
                    hand(origin, 0).start()

        for origin in (z - (r - 1), z + (r - 1))[: 1 if r == 1 else 2]:

            @pl.when(inside(origin))
            def _(origin=origin):
                crossed_here(origin).wait_recv()
                hand(origin, 1).start()

    own_round()
    fills[0].wait()
    fills[1].wait()
    fills[2].wait()
    count = e_ref.shape[0]
    step = split_of(count, 640, 128)

    def hand_part(s):
        return pltpu.make_async_remote_copy(
            src_ref=packs.at[s, 1 - c],
            dst_ref=handed.at[s],
            send_sem=h_send.at[s],
            recv_sem=h_get.at[s],
            device_id=sibling,
            device_id_type=MESH,
        )

    def cross_part(k):
        return pltpu.make_async_remote_copy(
            src_ref=packs.at[2 * k + 1, c],
            dst_ref=crossed.at[k],
            send_sem=p_send.at[k],
            recv_sem=p_get.at[k],
            device_id=beside,
            device_id_type=MESH,
        )

    def line_part(k):
        return pltpu.make_async_remote_copy(
            src_ref=zouts.at[k],
            dst_ref=lined.at[k],
            send_sem=l_send.at[k],
            recv_sem=l_get.at[k],
            device_id=at_z(flip(z, k)),
            device_id_type=MESH,
        )

    def compute(s):
        zt, yt = flip(z, s // 2), (y + s % 2) % 2

        handed_here(zt, s % 2).wait_recv()
        first = slot_of(zt, yt, 0)
        u = feats[pl.ds(first, 2)].reshape(2 * labels, hidden)
        top = total = mean = None
        for start in range(0, count, step):
            part = slice(start, start + step)
            bias = bias_ref[part, :]
            logits = mm_nt(e_ref[part, :], u) + jnp.concatenate([bias, bias], 1)
            high = jnp.max(logits, 0, keepdims=True)
            new = high if top is None else jnp.maximum(top, high)
            grown = jnp.exp(logits - new)
            sums = jnp.sum(grown, 0, keepdims=True)
            product = mm(et_ref[:, part], grown.astype(BF))
            if top is None:
                total, mean = sums, product
            else:
                shrink = jnp.exp(top - new)
                total, mean = total * shrink + sums, mean * shrink + product
            top = new
        mean = mean * (1.0 / total)
        logs = top + jnp.log(total)
        for k in range(2):
            half = slice(k * labels, (k + 1) * labels)
            packs[s, k, :hidden, :] = mean[:, half].astype(BF)
            packs[s, k, hidden : hidden + LOG_ROWS, :] = pack_log(logs[:, half], LOG_ROWS)
        hand_part(s).start()

    def settle(s):
        hand_part(s).wait_recv()
        pair = merged(unpack(packs[s, c], hidden), unpack(handed[s], hidden))

        @pl.when(s % 2 == 1)
        def _():
            store_packed(packs.at[s, c], pair, hidden)
            cross_part(s // 2).start()

        @pl.when(s % 2 == 0)
        def _():
            store_packed(kept.at[s // 2], pair, hidden)

    def finish(k):
        cross_part(k).wait_recv()
        pair = merged(unpack(kept[k], hidden), unpack(crossed[k], hidden))

        @pl.when(k > 0)
        def _():
            store_packed(zouts.at[k], pair, hidden)
            line_part(k).start()

        @pl.when(k == 0)
        def _():
            store_packed(zouts.at[k], pair, hidden)

    steps = 8

    @pl.loop(0, steps)
    def _(s):
        for r in range(1, HOPS + 2):
            pl.when(s == r)(functools.partial(later_round, r))
        compute(s)

        @pl.when(s > 0)
        def _():
            settle(s - 1)

        @pl.when((s >= 3) & (s % 2 == 1))
        def _():
            finish((s - 3) // 2)

    settle(steps - 1)
    finish(steps // 2 - 1)
    total = unpack(zouts[0], hidden)
    for k in range(1, 4):
        line_part(k).wait_recv()
        total = merged(total, unpack(lined[k], hidden))
    mean_ref[...] = total[0]
    log_ref[...] = total[1]

    for way, to in ((0, z + 1), (1, z - 1)):

        @pl.when(inside(to))
        def _(way=way, to=to):
            along(z, to, way).wait_send()

    cross(z).wait_send()
    hand(z, 0).wait_send()
    for r in range(1, HOPS + 1):
        for way, origin, to in ((0, z - r, z + 1), (1, z + r, z - 1)):

            @pl.when(inside(origin))
            def _(way=way, origin=origin, to=to):
                @pl.when(inside(to))
                def _():
                    along(origin, to, way).wait_send()

                cross(origin).wait_send()
                hand(origin, 0).wait_send()

    for origin in range(4):
        hand(origin, 1).wait_send()
    for s in range(steps):
        hand_part(s).wait_send()
    for k in range(4):
        cross_part(k).wait_send()
    for k in range(1, 4):
        line_part(k).wait_send()


def head(u, e, et, bias_wide):
    labels, hidden = u.shape
    whole = pl.BlockSpec(memory_space=pltpu.VMEM)
    anywhere = pl.BlockSpec(memory_space=pl.ANY)
    shape = jax.ShapeDtypeStruct
    sems = pltpu.SemaphoreType.DMA
    block = (hidden + LOG_ROWS, labels)
    return pl.pallas_call(
        head_body,
        in_specs=[whole] + [anywhere] * 3,
        out_specs=[whole] * 2,
        out_shape=[shape((hidden, labels), F32), shape((1, labels), F32)],
        scratch_shapes=[
            pltpu.VMEM(e.shape, BF),
            pltpu.VMEM(et.shape, BF),
            pltpu.VMEM(bias_wide.shape, F32),
            pltpu.VMEM((16, labels, hidden), BF),
            pltpu.VMEM((8, 2, *block), BF),
            pltpu.VMEM((8, *block), BF),
            pltpu.VMEM((4, *block), BF),
            pltpu.VMEM((4, *block), BF),
            pltpu.VMEM((4, *block), BF),
            pltpu.VMEM((4, *block), BF),
            sems((3,)),
            sems((8,)),
            sems((4,)),
            sems((4,)),
            sems((4,)),
            sems((8,)),
            sems((8,)),
            sems((8,)),
            sems((8,)),
            sems((4,)),
            sems((4,)),
            sems((4,)),
            sems((4,)),
        ],
        compiler_params=params(collective_id=4, has_side_effects=True),
        name="head",
    )(u, e, et, bias_wide)


def seg_positions(segments):
    index = jnp.arange(segments.shape[-1], dtype=jnp.int32)
    fresh = jnp.concatenate([jnp.ones((1,), dtype=bool), segments[1:] != segments[:-1]], -1)
    starts = lax.cummax(jnp.where(fresh, index, jnp.zeros_like(index)), axis=0)
    return index - starts


def pad_rows(matrix, multiple):
    return jnp.pad(matrix, ((0, -matrix.shape[0] % multiple), (0, 0)))


def slab_of(gathered, start, rows):
    if rows % 16 == 0 and start % rows == 0:
        return (gathered, start // rows, rows)
    part = gathered[:, start : start + rows].reshape(1, -1, gathered.shape[2])
    return (part, 0, part.shape[1])


def per_device(
    input_token_index,
    sentence_numbers,
    label_positions,
    label_target_token,
    sequence_task_index,
    task_loss_weight,
    optimizer_step_count,
    embed,
    position_embedding,
    norm_gain_vector,
    norm_bias_vector,
    attention_in_weight,
    attention_out_weight,
    feedforward_up,
    feedforward_down,
    layer_bias_vector,
    head_dense_bias,
    vocabulary_bias,
    adapter_down_matrix,
    adapter_up_matrix,
    adapter_moment_first,
    adapter_moment_second,
    head_projection,
    head_moment_first,
    head_moment_second,
):
    shards = lax.axis_size("dp") * lax.axis_size("fsdp")
    dp_index = lax.axis_index("dp")
    fsdp_index = lax.axis_index("fsdp")
    layers, unused, rank, up_part = adapter_up_matrix.shape
    hidden = embed.shape[1]
    tokens = input_token_index.shape[1]
    labels = label_positions.shape[1]
    qkv_rows = attention_in_weight.shape[2]
    out_rows = attention_out_weight.shape[2]
    ff_rows = feedforward_up.shape[2]
    head_rows = head_projection.shape[0]

    grouped = (lax.axis_size("dp"), lax.axis_size("fsdp")) == (2, 16)
    chunks = [
        [
            feedforward_up[layer].T,
            feedforward_down[layer],
            attention_in_weight[layer].T,
            attention_out_weight[layer].T,
        ]
        for layer in range(layers)
    ]
    chunks[-1].append(head_projection.astype(BF))
    chunks = [pad_rows(jnp.concatenate(pieces, 0), 32) for pieces in chunks]
    first_full = lax.all_gather(chunks[0], BOTH, axis=0, tiled=False)

    table_rows = embed.shape[0]
    wanted = jnp.concatenate([input_token_index[0], label_target_token[0]])
    dp_count = lax.axis_size("dp")
    group_ids = lax.all_gather(wanted, "dp", axis=0, tiled=False) - dp_index * table_rows
    inside = (group_ids >= 0) & (group_ids < table_rows)
    group_ids = jnp.clip(group_ids, 0, table_rows - 1)
    mine = lax.dynamic_index_in_dim(inside, dp_index, 0, keepdims=False)

    task_range = jnp.arange(TASKS, dtype=jnp.int32)
    slice_rows = vocabulary_bias.shape[0]
    ups = adapter_up_matrix.reshape(-1)
    if grouped:
        pair_ids = jnp.concatenate(
            [
                lax.dynamic_index_in_dim(group_ids, (dp_index + shift) % 2, 0, keepdims=False)
                for shift in (1, 0)
            ]
        )
        other_rows, own_rows = look_up(pair_ids, embed)
        fact = jnp.concatenate([vocabulary_bias, ups, sequence_task_index.astype(F32)])
        fact_rows = -(-fact.size // 1024) * 8
        got, facts = start_exchange(
            other_rows, jnp.pad(fact, (0, fact_rows * 128 - fact.size)).reshape(fact_rows, 128), shards
        )
        facts = facts.reshape(shards, -1)
        all_bias = facts[:, :slice_rows].reshape(-1)
        every_up = facts[:, slice_rows : slice_rows + ups.size]
        every_task = facts[:, slice_rows + ups.size].astype(jnp.int32)
    else:
        looked = jnp.where(
            inside.reshape(-1)[:, None], embed[group_ids.reshape(-1)], jnp.zeros((), BF)
        )
        own_rows = got = lax.psum_scatter(looked, "dp", scatter_dimension=0, tiled=True)
        all_bias = lax.all_gather(vocabulary_bias, BOTH, axis=0, tiled=True)
        every_up = lax.all_gather(ups, BOTH, axis=0, tiled=False)
        every_task = lax.all_gather(sequence_task_index, BOTH, axis=0, tiled=True)
    counts = labels * jnp.sum((every_task[:, None] == task_range[None, :]).astype(F32), 0)
    task_hot = (sequence_task_index[:, None] == task_range[None, :]).astype(F32)
    row_weight = jnp.sum(task_hot[0] * (task_loss_weight / jnp.maximum(counts, 1.0)))
    ups_full = (
        every_up.astype(BF)
        .reshape(shards, layers, 2, rank, up_part)
        .transpose(1, 2, 3, 0, 4)
        .reshape(layers, 2, rank, hidden)
    )
    blank = jnp.zeros((rank, hidden), BF)
    adapters = [
        jnp.pad(
            jnp.concatenate(
                [
                    jnp.concatenate([2 * ups_full[layer, 0], blank, blank], 1),
                    jnp.concatenate([blank, blank, 2 * ups_full[layer, 1]], 1),
                ],
                0,
            ),
            ((2 * rank * layer, 128 - 2 * rank * (layer + 1)), (0, 0)),
        )
        for layer in range(layers)
    ]
    downs = [
        jnp.pad(
            jnp.concatenate([adapter_down_matrix[layer, 0], adapter_down_matrix[layer, 1]], 1),
            ((0, 0), (2 * rank * layer, 128 - 2 * rank * (layer + 1))),
        )
        for layer in range(layers)
    ]
    bias_of = []
    for layer in range(layers):
        b = layer_bias_vector[layer][None, :]
        ff = b.shape[1] - 4 * hidden
        bias_of.append(
            (
                jnp.concatenate(
                    [b[:, :hidden], jnp.zeros((1, hidden), F32), b[:, hidden : 2 * hidden]], 1
                ),
                b[:, 2 * hidden : 3 * hidden],
                b[:, 3 * hidden : 3 * hidden + ff],
                b[:, 3 * hidden + ff :],
            )
        )
    norms_of = [
        jnp.concatenate(
            [
                norm_gain_vector[1 + 2 * layer][None],
                norm_bias_vector[1 + 2 * layer][None],
                norm_gain_vector[2 + 2 * layer][None],
                norm_bias_vector[2 + 2 * layer][None],
                norm_gain_vector[-1][None],
                norm_bias_vector[-1][None],
            ],
            0,
        )
        for layer in range(layers)
    ]

    target_rows = jnp.where(mine[tokens:, None], own_rows[tokens:], got[tokens:]).astype(F32)
    segments = sentence_numbers[0]
    spot = seg_positions(segments)[:, None]
    seg_real = segments.astype(F32)
    seg_wide = jnp.broadcast_to(seg_real[:, None], (tokens, 128))
    seg_row = seg_real[None, :]
    place_row = label_positions
    place_col = jnp.broadcast_to(label_positions.reshape(labels, 1), (labels, 128))

    own_bias = jnp.concatenate(
        [
            lax.dynamic_slice_in_dim(
                all_bias,
                ((dp_index - shift) % dp_count) * table_rows + fsdp_index * slice_rows,
                slice_rows,
                0,
            )
            for shift in range(dp_count)
        ]
    )
    bias_wide = jnp.broadcast_to(own_bias[:, None], (own_bias.shape[0], 128))
    target_bias = all_bias[label_target_token[0]]

    first_norm = jnp.concatenate([norm_gain_vector[:1], norm_bias_vector[:1]], 0)
    mine_col = mine[:tokens, None].astype(jnp.int32)
    in_start = 2 * ff_rows
    slabs_of = lambda full_chunk: (slab_of(full_chunk, 0, ff_rows), slab_of(full_chunk, ff_rows, ff_rows))
    slabs = [slabs_of(first_full)]
    last_inputs = (place_col, place_row, seg_wide, downs[1], adapters[1], bias_of[1][0])
    if grouped:
        more = (
            mine_col, spot, position_embedding, first_norm, downs[0], adapters[0], bias_of[0][0],
            seg_wide, seg_row, *bias_of[0][1:], norms_of[0],
        )
        qkv, x_last, one, two, slope, out_first, last_full, own_vocab, own_turned, mid, logs = first_layer(
            own_rows, got, first_full, chunks[1], embed, more, (0, 1, in_start), shards * ff_rows, slice_rows,
            shards,
        )
        slabs.append(slabs_of(last_full))
        *saved, features, in_last, out_last, head_full = last_forward(
            x_last, *last_inputs, (last_full,), (in_start, in_start + qkv_rows + out_rows),
            *slabs[1], *bias_of[1][1:], norms_of[1], head_dense_bias[None, :],
        )
        mean_t, own_logs = head(features, own_vocab, own_turned, bias_wide)
    else:
        last_full = lax.all_gather(chunks[1], BOTH, axis=0, tiled=False)
        slabs.append(slabs_of(last_full))
        taken = lambda full_chunk, start, size: full_chunk[:, start : start + size].reshape(-1, hidden)
        in_first, in_last = [taken(f, in_start, qkv_rows) for f in (first_full, last_full)]
        out_first, out_last = [taken(f, in_start + qkv_rows, out_rows) for f in (first_full, last_full)]
        head_full = taken(last_full, in_start + qkv_rows + out_rows, head_rows)
        qkv, mid, hidden_rows = project(
            own_rows, got, mine_col, spot, position_embedding, first_norm, downs[0], in_first, adapters[0],
            bias_of[0][0],
        )
        context, logs = attend(qkv, seg_wide, seg_row)
        x_last, one, two, slope = after(
            context, hidden_rows, out_first, *slabs[0], *bias_of[0][1:], norms_of[0]
        )
        *saved, features = last_forward(
            x_last, *last_inputs, (in_last, out_last, head_full), None, *slabs[1], *bias_of[1][1:],
            norms_of[1], head_dense_bias[None, :],
        )
        own_slice = lax.dynamic_slice_in_dim(embed, fsdp_index * slice_rows, slice_rows, 0)
        own_vocab = jnp.concatenate(
            [own_slice]
            + [
                lax.ppermute(
                    own_slice, "dp", [(k, (k + shift) % dp_count) for k in range(dp_count)]
                )
                for shift in range(1, dp_count)
            ],
            0,
        )
        every = lax.all_gather(features, "fsdp", axis=0, tiled=True)
        means, local_logs = vocab(every, own_vocab, own_vocab.T, bias_wide, labels)
        local_logs = local_logs.reshape(-1, labels)
        all_logs = lax.all_gather(local_logs, "fsdp", axis=0, tiled=False)
        whole_logs = jax.nn.logsumexp(all_logs, axis=0)
        scaled = (means * jnp.exp(local_logs - whole_logs)[:, None, :]).astype(BF)
        mean_t = lax.psum_scatter(scaled, "fsdp", scatter_dimension=0, tiled=True)[0].astype(F32)
        own_logs = lax.dynamic_index_in_dim(whole_logs, fsdp_index, 0, keepdims=False)
    targets = jnp.sum(features.astype(F32) * target_rows, 1) + target_bias
    own_loss = row_weight * jnp.sum(own_logs - targets)
    feat_grad = row_weight * (mean_t.T - target_rows)

    hidden_grad, dense_gradient, late = last_backward(
        feat_grad, saved, place_col, place_row, seg_wide, downs[1], in_last, adapters[1],
        out_last, *slabs[1], norms_of[1], head_full, 3 * rank, shards if grouped else None,
    )
    back = (hidden_grad, one, two, slope, out_first, *slabs[0], norms_of[0])
    step_as_real = optimizer_step_count[0].astype(F32)
    fades = (1.0 - beta_first**step_as_real, 1.0 - beta_second**step_as_real)
    adapts = (adapter_up_matrix, adapter_moment_first, adapter_moment_second)
    heads = (head_projection, head_moment_first, head_moment_second)
    if grouped:
        facts = jnp.concatenate(
            [jnp.broadcast_to(value, (1, 128)) for value in (own_loss, *fades)]
            + [jnp.zeros((5, 128), F32)]
        )
        turned = [
            jnp.pad(a.reshape(-1, up_part).T, ((0, 0), (0, 128 - a.size // up_part))) for a in adapts
        ]
        sums, *new = finish(
            back, qkv, logs, seg_wide, seg_row, mid, dense_gradient, late, facts, heads, turned, rank, shards
        )
        dense_new = new[:3]
        adapter_new = [
            a[:, : ups.size // up_part].T.reshape(adapter_up_matrix.shape) for a in new[3:]
        ]
        masked_task_loss, gradient_norm = sums[0, 0], sums[1, 0]
    else:
        dctx = after_back(*back)
        first = attend_back(qkv, dctx, logs, seg_wide, seg_row, mid, rank)
        adapter_gradient = (first + late)[:, : 2 * rank * layers].T.reshape(layers, 2, rank, hidden)
        dense_portion = lax.psum_scatter(dense_gradient, BOTH, scatter_dimension=0, tiled=True)
        adapter_portion = lax.psum_scatter(adapter_gradient, BOTH, scatter_dimension=3, tiled=True)
        squared_entries = jnp.sum(adapter_portion * adapter_portion) + jnp.sum(
            dense_portion * dense_portion
        )
        masked_task_loss, norm_square = lax.psum((own_loss, squared_entries), BOTH)
        gradient_norm = jnp.sqrt(norm_square)
        factor = jnp.minimum(1.0, clip_limit / (gradient_norm + 1e-06))
        adapter_new = adam(adapts[0], adapter_portion * factor, *adapts[1:], *fades)
        dense_new = adam(heads[0], dense_portion * factor, *heads[1:], *fades)
    return (masked_task_loss, gradient_norm, *adapter_new, *dense_new)


def solution(mesh):
    rows = P(BOTH, None)
    in_specs = (
        rows,
        rows,
        rows,
        rows,
        P(BOTH),
        P(),
        P(),
        P("dp", None),
        P(),
        P(),
        P(),
        P(None, None, BOTH),
        P(None, None, BOTH),
        P(None, None, BOTH),
        P(None, BOTH, None),
        P(),
        P(),
        P(BOTH),
        P(),
        P(None, None, None, BOTH),
        P(None, None, None, BOTH),
        P(None, None, None, BOTH),
        rows,
        rows,
        rows,
    )
    adapter = P(None, None, None, BOTH)
    out_specs = (P(), P(), adapter, adapter, adapter, rows, rows, rows)
    return jax.shard_map(
        per_device, mesh=mesh, in_specs=in_specs, out_specs=out_specs, check_vma=False
    )
```

```python
import functools

import jax
import jax.numpy as jnp
from jax import lax
from jax.experimental import pallas as pl
from jax.experimental.pallas import tpu as pltpu
from jax.sharding import PartitionSpec as P

HEADS = 12
TASKS = 4
REACH = 128

norm_eps = 1e-05
adapter_scale = 2.0
clip_limit = 0.01
learn_rate = 0.05
beta_first = 0.9
beta_second = 0.999
adam_eps = 1e-08
decay_rate = 0.01
masked_score = -1e30

BF = jnp.bfloat16
F32 = jnp.float32
BOTH = ("dp", "fsdp")
VMEM_BYTES = 60 * 1024 * 1024


def mm(a, b):
    return lax.dot_general(a, b, (((1,), (0,)), ((), ())), preferred_element_type=F32)


def mm_nt(a, b):
    return lax.dot_general(a, b, (((1,), (1,)), ((), ())), preferred_element_type=F32)


def mm_tn(a, b):
    return lax.dot_general(a, b, (((0,), (0,)), ((), ())), preferred_element_type=F32)


def layer_norm(rows_in, gain, shift):
    center = rows_in - jnp.mean(rows_in, -1, keepdims=True)
    spread = jnp.mean(center * center, -1, keepdims=True)
    return center * lax.rsqrt(spread + norm_eps) * gain + shift


def norm_back(rows_in, gain, gradient):
    center = rows_in - jnp.mean(rows_in, -1, keepdims=True)
    inverse = lax.rsqrt(jnp.mean(center * center, -1, keepdims=True) + norm_eps)
    unit = center * inverse
    scaled = gradient * gain
    return inverse * (
        scaled
        - jnp.mean(scaled, -1, keepdims=True)
        - unit * jnp.mean(scaled * unit, -1, keepdims=True)
    )


def gelu_pair(v):
    size = jnp.abs(v) * 0.7071067811865476
    base = 1.0 + 0.3275911 * size
    t = pl.reciprocal(base, approx=True)
    t = t * (2.0 - base * t)
    bell = jnp.exp(-0.5 * v * v)
    poly = t * (
        0.127414796 + t * (-0.142248368 + t * (0.7107068705 + t * (-0.7265760135 + t * 0.5307027145)))
    )
    tail = poly * bell
    phi = jnp.where(v >= 0.0, 1.0 - tail, tail)
    return v * phi, phi + v * (bell * 0.3989422804014327)


def params(**more):
    return pltpu.CompilerParams(vmem_limit_bytes=VMEM_BYTES, **more)


def full(shape):
    return pl.BlockSpec(shape, lambda *_: (0,) * len(shape))


def split_of(total, most, step):
    size = (min(most, total) // step) * step
    while size > step and total % size:
        size -= step
    return size if size and total % size == 0 else total


def pair_rows(block, width):
    first = lax.broadcasted_iota(jnp.int32, block.shape, 1) < width
    return jnp.concatenate([jnp.where(first, block, 0.0), jnp.where(first, 0.0, block)], 0).astype(BF)


def pair_join(wide, width):
    rows = wide.shape[1] // 2
    return jnp.concatenate([wide[:width, :rows], wide[width:, rows:]], 0)


def masked(scores, same):
    rows = scores.shape[1] // 2
    return jnp.concatenate(
        [
            jnp.where(same, scores[:, :rows], masked_score),
            jnp.where(same, scores[:, rows:], masked_score),
        ],
        1,
    )


def qkv_bias(bias_ref, layer, start, size):
    hidden = bias_ref.shape[1] // 8
    if start >= 2 * hidden:
        return bias_ref[layer : layer + 1, start - hidden : start - hidden + size]
    return bias_ref[layer : layer + 1, start : start + size] if start < hidden else 0.0


def norm_of(norm_refs, k):
    return norm_refs[0][k : k + 1, :], norm_refs[1][k : k + 1, :]


def project_body(
    own_ref, got_ref, code_ref, spots_ref, gain_ref, shift_ref, down_ref, w_ref, up_ref, bias_ref,
    out_ref, mid_ref, x_ref,
):
    mine = code_ref[...] % 2
    choose = (
        lax.broadcasted_iota(jnp.int32, (own_ref.shape[0], spots_ref.shape[0]), 1) == code_ref[...] // 2
    )
    summed = jnp.where(
        mine > 0, own_ref[...].astype(F32), got_ref[...].astype(F32)
    ) + mm(choose.astype(F32).astype(BF), spots_ref[...])
    x = layer_norm(summed, *norm_of((gain_ref, shift_ref), 0))
    x_ref[...] = x
    low = x.astype(BF)
    mid = mm(low, down_ref[0]).astype(BF)
    mid_ref[...] = mid
    total = w_ref.shape[0]
    step = total // 3
    for start in range(0, total, step):
        part = slice(start, start + step)
        out_ref[:, part] = (
            mm_nt(low, w_ref[part, :]) + mm(mid, up_ref[0, :, part]) + qkv_bias(bias_ref, 0, start, step)
        ).astype(BF)


def project(own, got, code, spots, gains, shifts, down, w, up, bias):
    rows, width = code.shape[0], own.shape[1]
    tile = split_of(rows, 256, 16)
    total = w.shape[0]
    row = lambda n: pl.BlockSpec((tile, n), lambda i: (i, 0))
    return pl.pallas_call(
        project_body,
        grid=(rows // tile,),
        in_specs=[row(width), row(width), row(1)]
        + [full(a.shape) for a in (spots, gains, shifts, down, w, up, bias)],
        out_specs=[row(total), row(down.shape[2]), row(width)],
        out_shape=[
            jax.ShapeDtypeStruct((rows, total), BF),
            jax.ShapeDtypeStruct((rows, down.shape[2]), BF),
            jax.ShapeDtypeStruct((rows, width), F32),
        ],
        compiler_params=params(),
        name="project",
    )(own, got, code, spots, gains, shifts, down, w, up, bias)


def attend_body(q_ref, k_ref, v_ref, seg_ref, seg_row_ref, ctx_ref, log_ref):
    rows = q_ref.shape[0]
    width = q_ref.shape[1] // 2
    scale = width**-0.5
    for start in range(0, rows, REACH):
        own = slice(start, start + REACH)
        near = slice(max(0, start - REACH), min(rows, start + 2 * REACH))
        queries = pair_rows(q_ref[own, :].astype(F32) * scale, width)
        same = seg_ref[near, :] == seg_row_ref[:, own]
        scores = masked(mm_nt(k_ref[near, :], queries), same)
        top = jnp.max(scores, 0, keepdims=True)
        weights = jnp.exp(scores - top)
        total = jnp.sum(weights, 0, keepdims=True)
        context = mm_tn(v_ref[near, :], weights.astype(BF)) * (1.0 / total)
        ctx_ref[own, :] = pair_join(context, width).T.astype(BF)
        log_ref[0, :, 2 * start : 2 * start + 2 * REACH] = top + jnp.log(total)


def attend(qkv, seg_wide, seg_row):
    rows, total = qkv.shape
    hidden = total // 3
    lanes = 2 * (hidden // HEADS)
    pairs = hidden // lanes
    column = lambda kind: pl.BlockSpec((rows, lanes), lambda p: (0, kind * pairs + p))
    return pl.pallas_call(
        attend_body,
        grid=(pairs,),
        in_specs=[column(0), column(1), column(2), full(seg_wide.shape), full(seg_row.shape)],
        out_specs=[
            pl.BlockSpec((rows, lanes), lambda p: (0, p)),
            pl.BlockSpec((1, 1, 2 * rows), lambda p: (p, 0, 0)),
        ],
        out_shape=[
            jax.ShapeDtypeStruct((rows, hidden), BF),
            jax.ShapeDtypeStruct((pairs, 1, 2 * rows), F32),
        ],
        compiler_params=params(),
        name="attend",
    )(qkv, qkv, qkv, seg_wide, seg_row)


def flat(ref):
    whole = ref[...]
    return whole.reshape(-1, whole.shape[-1])


def rows_of(ref, start, size):
    each = ref.shape[1]
    if size % each == 0 and start % each == 0 and each % 16 == 0:
        part = ref[start // each : (start + size) // each, :, :]
        return part.reshape(size, part.shape[-1])
    return flat(ref)[start : start + size, :]


def feed_step(ref):
    units = ref.shape[0] * ref.shape[1]
    step = ref.shape[1]
    while units % (2 * step) == 0 and 2 * step <= 768 and ref.shape[0] > 1:
        step *= 2
    return units, (step if ref.shape[0] > 1 else split_of(units, 768, 128))


def later_biases(bias_ref, layer):
    hidden = bias_ref.shape[1] // 8
    row = bias_ref[layer : layer + 1, :]
    return row[:, 2 * hidden : 3 * hidden], row[:, 3 * hidden : 7 * hidden], row[:, 7 * hidden :]


def after_body(
    ctx_ref, x_ref, wo_ref, up_ref, down_ref, bias_ref, gain_ref, shift_ref,
    out_ref, one_ref, two_ref, slope_ref,
):
    bo, b1, b2 = later_biases(bias_ref, 0)
    one = x_ref[...] + (mm_nt(ctx_ref[...], wo_ref[...]) + bo)
    one_ref[...] = one
    middle = layer_norm(one, *norm_of((gain_ref, shift_ref), 1))
    low = middle.astype(BF)
    total = middle + b2
    units, step = feed_step(up_ref)
    for start in range(0, units, step):
        part = slice(start, start + step)
        act, slope = gelu_pair(mm_nt(low, rows_of(up_ref, start, step)) + b1[:, part])
        slope_ref[:, part] = slope.astype(BF)
        total = total + mm(act.astype(BF), rows_of(down_ref, start, step))
    two_ref[...] = total
    out_ref[...] = layer_norm(total, *norm_of((gain_ref, shift_ref), 2))


def slab_spec(slab):
    array, place, rows = slab
    return pl.BlockSpec((array.shape[0], rows, array.shape[2]), lambda *_: (0, place, 0))


def after(ctx, x, wo, up, down, bias, gains, shifts):
    rows, width = x.shape
    tile = split_of(rows, 256, 16)
    units = 4 * width
    row = lambda n: pl.BlockSpec((tile, n), lambda i: (i, 0))
    return pl.pallas_call(
        after_body,
        grid=(rows // tile,),
        in_specs=[row(width), row(width), full(wo.shape), slab_spec(up), slab_spec(down)]
        + [full(a.shape) for a in (bias, gains, shifts)],
        out_specs=[row(width), row(width), row(width), row(units)],
        out_shape=[jax.ShapeDtypeStruct((rows, width), F32)] * 3
        + [jax.ShapeDtypeStruct((rows, units), BF)],
        compiler_params=params(),
        name="after",
    )(ctx, x, wo, up[0], down[0], bias, gains, shifts)


def exact_rows(choose, matrix):
    high = matrix.astype(BF)
    rest = matrix - high.astype(F32)
    middle = rest.astype(BF)
    low = (rest - middle.astype(F32)).astype(BF)
    return mm(choose, high) + mm(choose, middle) + mm(choose, low)


def unpack_rows(slab_ref, targets):
    shards = slab_ref.shape[0]

    @pl.loop(0, shards // 2)
    def _(k):
        first, second = slab_ref[2 * k].astype(F32), slab_ref[2 * k + 1].astype(F32)
        at = 0
        for target in targets:
            each = target.shape[0] // shards
            both = jnp.concatenate([first[at : at + each], second[at : at + each]], 0)
            target[pl.ds(pl.multiple_of(2 * each * k, 2 * each), 2 * each), :] = both.astype(BF)
            at += each


def last_forward_body(
    x_ref, place_ref, place_row_ref, seg_ref, down_ref, adapt_ref, bias_ref, weights_any, up_any, dn_any,
    gain_ref, shift_ref, hbias_ref,
    kv_ref, q_ref, mid_ref, log_ref, one_ref, slope_ref, two_ref, low_ref, act_ref, hslope_ref, feat_ref, *more,
    places, starts,
):
    copies = []
    if starts is None:
        up_ref, dn_ref, ctx_ref, w_ref, wo_ref, hb_ref, sems = more
        sources = zip(weights_any, (w_ref, wo_ref, hb_ref))
    else:
        w_out, wo_out, hb_out, up_ref, dn_ref, ctx_ref, w_ref, wo_ref, hb_ref, in_slab, hb_slab, sems = more
        sources = [
            (weights_any[0].at[:, pl.ds(start, slab.shape[1]), :], slab)
            for start, slab in zip(starts, (in_slab, hb_slab))
        ]
    for source, target in sources:
        copies.append((source, target))
    early = len(copies)
    for source, target, place in ((up_any, up_ref, places[0]), (dn_any, dn_ref, places[1])):
        each = target.shape[1]
        copies.append((source.at[:, pl.ds(place * each, each), :], target))
    copies = [pltpu.make_async_copy(*ends, sems.at[k]) for k, ends in enumerate(copies)]
    for copy in copies:
        copy.start()
    for copy in copies[:early]:
        copy.wait()
    copies = copies[early:]
    if starts is not None:
        unpack_rows(in_slab, (w_ref, wo_ref))
        unpack_rows(hb_slab, (hb_ref,))
        for k, ends in enumerate(((w_ref, w_out), (wo_ref, wo_out), (hb_ref, hb_out))):
            copies.append(pltpu.make_async_copy(*ends, sems.at[4 + k]))
            copies[-1].start()
    rows, hidden = x_ref.shape
    labels = place_ref.shape[0]
    lanes = 2 * (hidden // HEADS)
    width = lanes // 2
    low = x_ref[...].astype(BF)
    mid = mm(low, down_ref[1]).astype(BF)
    mid_ref[...] = mid
    step = split_of(hidden, 768, 128)
    for start in range(hidden, 3 * hidden, step):
        part = slice(start, start + step)
        kv_ref[:, start - hidden : start - hidden + step] = (
            mm_nt(low, w_ref[part, :]) + mm(mid, adapt_ref[1, :, part]) + qkv_bias(bias_ref, 1, start, step)
        ).astype(BF)
    choose = (
        lax.broadcasted_iota(jnp.int32, (labels, rows), 1) == place_ref[...][:, 0:1]
    ).astype(F32).astype(BF)
    own = exact_rows(choose, x_ref[...])
    own_low = own.astype(BF)
    own_mid = mm(choose, mid).astype(BF)
    q_ref[...] = (
        mm_nt(own_low, w_ref[:hidden, :])
        + mm(own_mid, adapt_ref[1, :, :hidden])
        + qkv_bias(bias_ref, 1, 0, hidden)
    ).astype(BF)
    seg = seg_ref[...]
    seg_own = jnp.sum(
        jnp.where(
            lax.broadcasted_iota(jnp.int32, (rows, labels), 0) == place_row_ref[...], seg, 0.0
        ),
        0,
        keepdims=True,
    )
    same = seg == seg_own
    for p in range(hidden // lanes):
        part = slice(p * lanes, (p + 1) * lanes)
        queries = pair_rows(q_ref[:, part].astype(F32) * width**-0.5, width)
        scores = masked(mm_nt(kv_ref[:, part], queries), same)
        top = jnp.max(scores, 0, keepdims=True)
        weights = jnp.exp(scores - top)
        total = jnp.sum(weights, 0, keepdims=True)
        context = mm_tn(
            kv_ref[:, hidden + p * lanes : hidden + (p + 1) * lanes], weights.astype(BF)
        ) * (1.0 / total)
        ctx_ref[:, part] = pair_join(context, width).T.astype(BF)
        log_ref[p : p + 1, :] = top + jnp.log(total)
    bo, b1, b2 = later_biases(bias_ref, 1)
    norms = (gain_ref, shift_ref)
    one = own + (mm_nt(ctx_ref[...], wo_ref[...]) + bo)
    one_ref[...] = one
    middle = layer_norm(one, *norm_of(norms, 3))
    middle_low = middle.astype(BF)
    sum_two = middle + b2
    units, step = feed_step(up_ref)
    for copy in copies:
        copy.wait()
    for start in range(0, units, step):
        part = slice(start, start + step)
        act, slope = gelu_pair(mm_nt(middle_low, rows_of(up_ref, start, step)) + b1[:, part])
        slope_ref[:, part] = slope.astype(BF)
        sum_two = sum_two + mm(act.astype(BF), rows_of(dn_ref, start, step))
    two_ref[...] = sum_two
    out_low = layer_norm(sum_two, *norm_of(norms, 4)).astype(BF)
    low_ref[...] = out_low
    act, slope = gelu_pair(mm(out_low, hb_ref[...]) + hbias_ref[...])
    act_ref[...] = act
    hslope_ref[...] = slope
    feat_ref[...] = layer_norm(act, *norm_of(norms, 5)).astype(BF)


def slab_scratch(slab):
    array, place, rows = slab
    return pltpu.VMEM((array.shape[0], rows, array.shape[2]), BF)


def last_forward(
    x, place_col, place_row, seg_wide, down, adapt, bias, weights, starts, up, dn, gains, shifts, hbias
):
    rows, hidden = x.shape
    labels = place_col.shape[0]
    units = 4 * hidden
    whole = pl.BlockSpec(memory_space=pltpu.VMEM)
    anywhere = pl.BlockSpec(memory_space=pl.ANY)
    shape = jax.ShapeDtypeStruct
    pairs = HEADS // 2
    matrices = [(3 * hidden, hidden), (hidden, hidden), (hidden, hidden)]
    slabs = []
    if starts is not None:
        shards = weights[0].shape[0]
        slabs = [
            pltpu.VMEM((shards, 4 * hidden // shards, hidden), BF),
            pltpu.VMEM((shards, weights[0].shape[1] - starts[1], hidden), BF),
        ]

    def body(*refs):
        head, rest = refs[:7], refs[7:]
        return last_forward_body(
            *head, rest[: len(weights)], *rest[len(weights) :], places=(up[1], dn[1]), starts=starts
        )

    return pl.pallas_call(
        body,
        in_specs=[whole] * 7 + [anywhere] * (len(weights) + 2) + [whole] * 3,
        out_specs=[whole] * 11 + ([anywhere] * 3 if slabs else []),
        out_shape=[
            shape((rows, 2 * hidden), BF),
            shape((labels, hidden), BF),
            shape((rows, down.shape[2]), BF),
            shape((pairs, 2 * labels), F32),
            shape((labels, hidden), F32),
            shape((labels, units), BF),
            shape((labels, hidden), F32),
            shape((labels, hidden), BF),
            shape((labels, hidden), F32),
            shape((labels, hidden), F32),
            shape((labels, hidden), BF),
        ]
        + ([shape(m, BF) for m in matrices] if slabs else []),
        scratch_shapes=[
            slab_scratch(up),
            slab_scratch(dn),
            pltpu.VMEM((labels, hidden), BF),
            *[pltpu.VMEM(m, BF) for m in matrices],
            *slabs,
            pltpu.SemaphoreType.DMA((7,)),
        ],
        compiler_params=params(),
        name="last_forward",
    )(x, place_col, place_row, seg_wide, down, adapt, bias, *weights, up[0], dn[0], gains, shifts, hbias)


def vocab_body(u_ref, e_ref, et_ref, bias_ref, num_ref, log_ref, scores, weights):
    count = e_ref.shape[0]
    step = split_of(count, 640, 16)
    u = u_ref[...]
    rows = u.shape[0]
    labels = num_ref.shape[2]
    top = jnp.full((1, rows), -jnp.inf, F32)
    for start in range(0, count, step):
        part = slice(start, start + step)
        bias = bias_ref[part, :]
        logits = mm_nt(e_ref[part, :], u) + jnp.concatenate([bias] * (rows // bias.shape[1]), 1)
        scores[part, :] = logits
        top = jnp.maximum(top, jnp.max(logits, 0, keepdims=True))
    total = jnp.zeros((1, rows), F32)
    for start in range(0, count, step):
        part = slice(start, start + step)
        grown = jnp.exp(scores[part, :] - top)
        total = total + jnp.sum(grown, 0, keepdims=True)
        weights[part, :] = grown.astype(BF)
    mean = mm(et_ref[...], weights[...]) * (1.0 / total)
    logs = top + jnp.log(total)
    for k in range(rows // labels):
        num_ref[k, :, :] = mean[:, k * labels : (k + 1) * labels]
        log_ref[k, :, :] = logs[:, k * labels : (k + 1) * labels]


def vocab(u, e, et, bias_wide, labels):
    rows, hidden = u.shape
    count = e.shape[0]
    tile = 2 * labels
    return pl.pallas_call(
        vocab_body,
        grid=(rows // tile,),
        in_specs=[
            pl.BlockSpec((tile, hidden), lambda i: (i, 0)),
            full(e.shape),
            full(et.shape),
            full(bias_wide.shape),
        ],
        out_specs=[
            pl.BlockSpec((2, hidden, labels), lambda i: (i, 0, 0)),
            pl.BlockSpec((2, 1, labels), lambda i: (i, 0, 0)),
        ],
        out_shape=[
            jax.ShapeDtypeStruct((rows // labels, hidden, labels), F32),
            jax.ShapeDtypeStruct((rows // labels, 1, labels), F32),
        ],
        scratch_shapes=[pltpu.VMEM((count, tile), F32), pltpu.VMEM((count, tile), BF)],
        compiler_params=params(),
        name="vocab",
    )(u, e, et, bias_wide)


def last_backward_body(
    mean_ref, all_log_ref, target_ref, fact_ref, kv_ref, q_ref, mid_ref, log_ref, one_ref, slope_ref, two_ref,
    low_ref, act_ref, hslope_ref, feat_ref, place_ref, place_row_ref, seg_ref, down_ref, w_ref, adapt_ref, wo_ref,
    up_any, dn_any, gain_ref, hb_ref,
    dx_ref, gh_ref, g_ref, out_fact_ref,
    up_ref, dn_ref, dkv_ref, dq_ref, sems, *, places, edge,
):
    copies = []
    for k, (source, target, place) in enumerate(
        ((up_any, up_ref, places[0]), (dn_any, dn_ref, places[1]))
    ):
        rows = target.shape[1]
        copies.append(
            pltpu.make_async_copy(
                source.at[:, pl.ds(place * rows, rows), :], target, sems.at[k]
            )
        )
        copies[-1].start()
    rows = kv_ref.shape[0]
    labels, hidden = feat_ref.shape
    lanes = 2 * (hidden // HEADS)
    width = lanes // 2
    scale = width**-0.5
    targets = target_ref[...].astype(F32)
    weight = fact_ref[0:1, 0:1]
    chosen = jnp.sum(feat_ref[...].astype(F32) * targets, keepdims=True)
    loss = weight * (jnp.sum(all_log_ref[...] - fact_ref[3:4, :labels], keepdims=True) - chosen)
    out_fact_ref[...] = jnp.where(
        lax.broadcasted_iota(jnp.int32, fact_ref.shape, 0) == 0, loss, fact_ref[...]
    )
    du = weight * (mean_ref[...].T - targets)
    dact = norm_back(act_ref[...], gain_ref[5:6, :], du)
    dz = (hslope_ref[...] * dact).astype(BF)
    dense = mm_tn(low_ref[...], dz)
    if len(gh_ref.shape) == 2:
        gh_ref[...] = dense
    else:
        each = hidden // gh_ref.shape[0]
        spare = jnp.zeros((gh_ref.shape[1] - each, hidden), F32)
        for k in range(gh_ref.shape[0]):
            gh_ref[k] = jnp.concatenate([dense[k * each : (k + 1) * each, :], spare], 0).astype(BF)
    dtwo = norm_back(two_ref[...], gain_ref[4:5, :], mm_nt(dz, hb_ref[...]))
    dtwo_low = dtwo.astype(BF)
    dmiddle = dtwo
    units, step = feed_step(up_ref)
    for copy in copies:
        copy.wait()
    for start in range(0, units, step):
        part = slice(start, start + step)
        dgate = (
            slope_ref[:, part].astype(F32) * mm_nt(dtwo_low, rows_of(dn_ref, start, step))
        ).astype(BF)
        dmiddle = dmiddle + mm(dgate, rows_of(up_ref, start, step))
    done = norm_back(one_ref[...], gain_ref[3:4, :], dmiddle)
    dctx = mm(done.astype(BF), wo_ref[...]).astype(BF)
    seg = seg_ref[...]
    choose_t = lax.broadcasted_iota(jnp.int32, (rows, labels), 0) == place_row_ref[...]
    same = seg == jnp.sum(jnp.where(choose_t, seg, 0.0), 0, keepdims=True)
    for p in range(hidden // lanes):
        part = slice(p * lanes, (p + 1) * lanes)
        later = slice(hidden + p * lanes, hidden + (p + 1) * lanes)
        queries = pair_rows(q_ref[:, part].astype(F32) * scale, width)
        outs = pair_rows(dctx[:, part].astype(F32), width)
        keys = kv_ref[:, part]
        weights = jnp.exp(masked(mm_nt(keys, queries), same) - log_ref[p : p + 1, :])
        dweights = mm_nt(kv_ref[:, later], outs)
        inner = jnp.sum(dweights * weights, 0, keepdims=True)
        dscores = (weights * (dweights - inner)).astype(BF)
        dkv_ref[:, part] = mm(dscores, queries).astype(BF)
        dkv_ref[:, later] = mm(weights.astype(BF), outs).astype(BF)
        dq_ref[:, part] = (pair_join(mm_tn(keys, dscores), width) * scale).T.astype(BF)
    dq = dq_ref[...]
    own_mid = mm(
        (lax.broadcasted_iota(jnp.int32, (labels, rows), 1) == place_ref[...][:, 0:1]).astype(F32).astype(BF),
        mid_ref[...],
    ).astype(BF)
    g_ref[...] = adapter_scale * jnp.where(
        lax.broadcasted_iota(jnp.int32, g_ref.shape, 1) < edge,
        mm_tn(dq, own_mid),
        mm_tn(dkv_ref[:, hidden:], mid_ref[...]),
    )
    dmid_own = mm_nt(dq, adapt_ref[1, :, :hidden]).astype(BF)
    own = done + mm(dq, w_ref[:hidden, :]) + mm_nt(dmid_own, down_ref[1])
    spread = choose_t.astype(F32).astype(BF)
    own_high = own.astype(BF)
    own_rest = (own - own_high.astype(F32)).astype(BF)
    dmid = mm_nt(dkv_ref[:, hidden:], adapt_ref[1, :, 2 * hidden :]).astype(BF)
    step = split_of(hidden, 256, 128)
    for start in range(0, hidden, step):
        part = slice(start, start + step)
        dx_ref[:, part] = (
            mm(dkv_ref[...], w_ref[hidden:, part])
            + mm_nt(dmid, down_ref[1, part, :])
            + mm(spread, own_high[:, part])
            + mm(spread, own_rest[:, part])
        )


def last_backward(
    mean, logs, targets, facts, saved, place_col, place_row, seg_wide, down, w, adapt, wo, up, dn, gains, hb, edge, shards
):
    kv = saved[0]
    rows = kv.shape[0]
    labels, hidden = targets.shape
    whole = pl.BlockSpec(memory_space=pltpu.VMEM)
    anywhere = pl.BlockSpec(memory_space=pl.ANY)
    shape = jax.ShapeDtypeStruct
    return pl.pallas_call(
        functools.partial(last_backward_body, places=(up[1], dn[1]), edge=edge),
        in_specs=[whole] * 22 + [anywhere] * 2 + [whole] * 2,
        out_specs=[whole] * 4,
        out_shape=[
            shape((rows, hidden), F32),
            shape((hidden, hidden), F32)
            if shards is None
            else shape((shards, -(-hidden // shards // 16) * 16, hidden), BF),
            shape((hidden, down.shape[2]), F32),
            shape(facts.shape, F32),
        ],
        scratch_shapes=[
            slab_scratch(up),
            slab_scratch(dn),
            pltpu.VMEM(kv.shape, BF),
            pltpu.VMEM((labels, hidden), BF),
            pltpu.SemaphoreType.DMA((2,)),
        ],
        compiler_params=params(),
        name="last_backward",
    )(mean, logs, targets, facts, *saved, place_col, place_row, seg_wide, down, w, adapt, wo, up[0], dn[0], gains, hb)


def after_back_body(dout_ref, one_ref, two_ref, slope_ref, wo_ref, up_ref, down_ref, gain_ref, dctx_ref):
    dtwo = norm_back(two_ref[...], gain_ref[2:3, :], dout_ref[...])
    low = dtwo.astype(BF)
    dmiddle = dtwo
    units, step = feed_step(up_ref)
    for start in range(0, units, step):
        part = slice(start, start + step)
        dgate = (
            slope_ref[:, part].astype(F32) * mm_nt(low, rows_of(down_ref, start, step))
        ).astype(BF)
        dmiddle = dmiddle + mm(dgate, rows_of(up_ref, start, step))
    done = norm_back(one_ref[...], gain_ref[1:2, :], dmiddle)
    dctx_ref[...] = mm(done.astype(BF), wo_ref[...]).astype(BF)


def after_back(dout, one, two, slope, wo, up, down, norms):
    rows, width = dout.shape
    tile = split_of(rows, 256, 16)
    row = lambda n: pl.BlockSpec((tile, n), lambda i: (i, 0))
    return pl.pallas_call(
        after_back_body,
        grid=(rows // tile,),
        in_specs=[row(width), row(width), row(width), row(slope.shape[1]), full(wo.shape)]
        + [slab_spec(up), slab_spec(down), full(norms.shape)],
        out_specs=row(width),
        out_shape=jax.ShapeDtypeStruct((rows, width), BF),
        compiler_params=params(),
        name="after_back",
    )(dout, one, two, slope, wo, up[0], down[0], norms)


def attend_back_body(
    q_ref, k_ref, v_ref, dctx_ref, log_ref, seg_ref, seg_row_ref, mid_ref, g_ref, dv_ref, *, edge
):
    rows = q_ref.shape[0]
    width = q_ref.shape[1] // 2
    scale = width**-0.5
    dv_ref[...] = jnp.zeros_like(dv_ref)
    gq = jnp.zeros((2 * width, mid_ref.shape[1]), F32)
    for start in range(0, rows, REACH):
        own = slice(start, start + REACH)
        near = slice(max(0, start - REACH), min(rows, start + 2 * REACH))
        queries = pair_rows(q_ref[own, :].astype(F32) * scale, width)
        outs = pair_rows(dctx_ref[own, :].astype(F32), width)
        same = seg_ref[near, :] == seg_row_ref[:, own]
        keys = k_ref[near, :]
        logs = log_ref[0, :, 2 * start : 2 * start + 2 * REACH]
        weights = jnp.exp(masked(mm_nt(keys, queries), same) - logs)
        dweights = mm_nt(v_ref[near, :], outs)
        inner = jnp.sum(dweights * weights, 0, keepdims=True)
        dscores = (weights * (dweights - inner)).astype(BF)
        dv_ref[near, :] += mm(weights.astype(BF), outs)
        dq = (pair_join(mm_tn(keys, dscores), width) * scale).astype(BF)
        gq = gq + mm(dq, mid_ref[own, :])
    gv = mm_tn(dv_ref[...].astype(BF), mid_ref[...])
    g_ref[...] = adapter_scale * jnp.where(
        lax.broadcasted_iota(jnp.int32, gq.shape, 1) < edge, gq, gv
    )


def attend_back(qkv, dctx, logs, seg_wide, seg_row, mid, edge):
    rows, total = qkv.shape
    hidden = total // 3
    lanes = 2 * (hidden // HEADS)
    pairs = hidden // lanes
    column = lambda kind: pl.BlockSpec((rows, lanes), lambda p: (0, kind * pairs + p))
    return pl.pallas_call(
        functools.partial(attend_back_body, edge=edge),
        grid=(pairs,),
        in_specs=[
            column(0),
            column(1),
            column(2),
            column(0),
            pl.BlockSpec((1, 1, 2 * rows), lambda p: (p, 0, 0)),
            full(seg_wide.shape),
            full(seg_row.shape),
            full(mid.shape),
        ],
        out_specs=pl.BlockSpec((lanes, mid.shape[1]), lambda p: (p, 0)),
        out_shape=jax.ShapeDtypeStruct((hidden, mid.shape[1]), F32),
        scratch_shapes=[pltpu.VMEM((rows, lanes), F32)],
        compiler_params=params(),
        name="attend_back",
    )(qkv, qkv, qkv, dctx, logs, seg_wide, seg_row, mid)


MESH = pl.DeviceIdType.MESH


def position():
    dp, fsdp = lax.axis_index("dp"), lax.axis_index("fsdp")
    return {"x": dp, "z": fsdp // 4, "y": (fsdp // 2) % 2, "c": fsdp % 2}


def device_of(place):
    return (place["x"], (place["z"] * 2 + place["y"]) * 2 + place["c"])


def number_of(place):
    return place["x"] * 16 + (place["z"] * 2 + place["y"]) * 2 + place["c"]


def rank_device(number):
    return (number // 16, number % 16)


def greet_all(shards):
    barrier = pltpu.get_barrier_semaphore()
    me = lax.axis_index("dp") * 16 + lax.axis_index("fsdp")

    @pl.loop(1, shards)
    def _(k):
        pl.semaphore_signal(
            barrier, inc=1, device_id=rank_device((me + k) % shards), device_id_type=MESH
        )


def await_all(shards):
    pl.semaphore_wait(pltpu.get_barrier_semaphore(), shards - 1)


def direct_copy(source, target, sems, me, k, shards):
    return pltpu.make_async_remote_copy(
        src_ref=source,
        dst_ref=target,
        send_sem=sems.at[0],
        recv_sem=sems.at[1],
        device_id=rank_device((me + k) % shards),
        device_id_type=MESH,
    )


def spread(piece_of, buffer, sems, me, shards):
    @pl.loop(1, shards)
    def _(k):
        direct_copy(piece_of((me + k) % shards), buffer.at[me], sems, me, k, shards).start()


def collect(buffer, sems, me, shards):
    whole = buffer.at[pl.ds(0, shards - 1)]
    copy = direct_copy(whole, whole, sems, me, 1, shards)
    copy.wait_recv()
    copy.wait_send()


def relative_places(order):
    places = [
        {"x": dx, "z": dz, "y": dy} for dx in (0, 1) for dz in range(-3, 4) for dy in (0, 1)
    ]
    return sorted(places, key=lambda p: (abs(p["x"]) + abs(p["z"]) + abs(p["y"]), [abs(p[a]) for a in order]))


class Gather:
    def __init__(self, chunk, full_buffer, start, rows, order, sends, receives, hands, hands_got):
        self.chunk, self.full, self.order = chunk, full_buffer, order
        self.part = pl.ds(start, rows)
        self.sends, self.receives, self.hands, self.hands_got = sends, receives, hands, hands_got
        self.here = position()
        self.items = relative_places(order)
        self.pending = []

    def origin(self, item):
        here = self.here
        return {"x": (here["x"] + item["x"]) % 2, "z": here["z"] - item["z"], "y": (here["y"] + item["y"]) % 2, "c": here["c"]}

    def key(self, place):
        return (place["x"] * 4 + place["z"]) * 2 + place["y"]

    def outward(self, item):
        deepest = max([k for k, axis in enumerate(self.order) if item[axis]], default=-1)
        ways = []
        if deepest >= 0 and self.order[deepest] == "z":
            ways.append(("z", 1 if item["z"] > 0 else -1))
        for axis in self.order[deepest + 1 :]:
            ways += [("z", 1), ("z", -1)] if axis == "z" else [(axis, 1)]
        return ways

    def copy(self, index, way, slot, item):
        here = self.here
        place = self.origin(item)
        number, key = number_of(place), self.key(place)
        mine = not any(item.values())
        source = self.chunk.at[self.part, :] if mine else self.full.at[number, self.part, :]
        if way is None:
            target = dict(here, c=1 - here["c"])
            sends, receives = self.hands.at[index], self.hands_got.at[key]
        else:
            axis, step = way
            target = dict(here)
            target[axis] = here["z"] + step if axis == "z" else 1 - here[axis]
            sends, receives = self.sends.at[index * 4 + slot], self.receives.at[key]
        return pltpu.make_async_remote_copy(
            src_ref=source,
            dst_ref=self.full.at[number, self.part, :],
            send_sem=sends,
            recv_sem=receives,
            device_id=device_of(target),
            device_id_type=MESH,
        )

    def valid(self, item):
        z = self.here["z"] - item["z"]
        return (z >= 0) & (z <= 3)

    def step(self, index):
        item = self.items[index]

        @pl.when(self.valid(item))
        def _():
            if any(item.values()):
                self.arrived(index, item)
            for slot, way in enumerate(self.outward(item)):
                self.when_way(way, lambda way=way, slot=slot: self.copy(index, way, slot, item).start())
            self.copy(index, None, 0, item).start()

    def when_way(self, way, act):
        axis, step = way
        if axis == "z":
            z = self.here["z"] + step
            pl.when((z >= 0) & (z <= 3))(act)
        else:
            act()

    def arrived(self, index, item):
        place = self.origin(item)
        spot = self.full.at[number_of(place), self.part, :]
        pltpu.make_async_remote_copy(
            src_ref=spot,
            dst_ref=spot,
            send_sem=self.sends.at[index * 4],
            recv_sem=self.receives.at[self.key(place)],
            device_id=device_of(dict(self.here, c=1 - self.here["c"])),
            device_id_type=MESH,
        ).wait_recv()

    def finish(self):
        for index, item in enumerate(self.items):

            @pl.when(self.valid(item))
            def _(index=index, item=item):
                for slot, way in enumerate(self.outward(item)):
                    self.when_way(way, lambda way=way, slot=slot: self.copy(index, way, slot, item).wait_send())
                self.copy(index, None, 0, item).wait_send()
                place = dict(self.origin(item), c=1 - self.here["c"])
                spot = self.full.at[number_of(place), self.part, :]
                pltpu.make_async_remote_copy(
                    src_ref=spot,
                    dst_ref=spot,
                    send_sem=self.hands.at[index],
                    recv_sem=self.hands_got.at[self.key(place)],
                    device_id=device_of(dict(self.here, c=1 - self.here["c"])),
                    device_id_type=MESH,
                ).wait_recv()


ITEMS = 28


def start_body(
    streams, shards, rows, fact, chunk, got, facts, full_chunk,
    row_sems, fact_sems, own_sems, sends, receives, hands, hands_got,
):
    here = position()
    me = number_of(here)
    greet_all(shards)
    own = [
        pltpu.make_async_copy(source, target, own_sems.at[k])
        for k, (source, target) in enumerate(((fact, facts.at[me]), (chunk, full_chunk.at[me])))
    ]
    for copy in own:
        copy.start()
    await_all(shards)
    gathers = [
        Gather(
            chunk, full_chunk, start, size, order, sends.at[k], receives.at[k], hands.at[k], hands_got.at[k]
        )
        for k, (start, size, order) in enumerate(streams)
    ]
    swap = pltpu.make_async_remote_copy(
        src_ref=rows,
        dst_ref=got,
        send_sem=row_sems.at[0],
        recv_sem=row_sems.at[1],
        device_id=device_of(dict(here, x=1 - here["x"])),
        device_id_type=MESH,
    )
    for gather in gathers:
        gather.step(0)
    swap.start()
    spread(lambda peer: fact, facts, fact_sems, me, shards)
    for index in range(1, ITEMS):
        for gather in gathers:
            gather.step(index)
    for gather in gathers:
        gather.finish()
    collect(facts, fact_sems, me, shards)
    swap.wait()
    for copy in own:
        copy.wait()


def gather_sems():
    sems = pltpu.SemaphoreType.DMA
    return [sems((2, 4 * ITEMS)), sems((2, 16)), sems((2, ITEMS)), sems((2, 16))]


def streams_of(rows):
    cut = (rows * 5 // 6 + 15) // 16 * 16
    return ((0, cut, "xzy"), (cut, rows - cut, "xyz"))


def start_exchange(rows, fact, chunk, shards):
    anywhere = pl.BlockSpec(memory_space=pl.ANY)
    shape = jax.ShapeDtypeStruct
    sems = pltpu.SemaphoreType.DMA
    return pl.pallas_call(
        functools.partial(start_body, streams_of(chunk.shape[0]), shards),
        in_specs=[anywhere] * 3,
        out_specs=[anywhere] * 3,
        out_shape=[
            shape(rows.shape, rows.dtype),
            shape((shards, *fact.shape), fact.dtype),
            shape((shards, *chunk.shape), chunk.dtype),
        ],
        scratch_shapes=[sems((2,)), sems((2,)), sems((2,)), *gather_sems()],
        compiler_params=params(collective_id=1, has_side_effects=True),
        name="start_exchange",
    )(rows, fact, chunk)


def first_layer_body(
    streams, shards, places,
    own_any, got_any, in_any, feed_any, chunk, table_any, code_ref, spots_ref, gain_ref, shift_ref, down_ref,
    adapt_ref, bias_ref, seg_ref, seg_row_ref,
    qkv_out, x_out, one_out, two_out, slope_out, wo_out, full_chunk, e_out, et_out, mid_ref, log_ref,
    own, got, in_slab, w, wo, up, dn, x, qkv, ctx, two, out, slope, e_ref, et_ref,
    load_sems, tile_sems, out_sems, swap_sems, sends, receives, hands, hands_got,
):
    here = position()
    me = number_of(here)
    across = device_of(dict(here, x=1 - here["x"]))
    rows, hidden = x.shape
    tile = split_of(rows, 256, 16)
    tiles = rows // tile
    lanes = 2 * (hidden // HEADS)
    pairs = hidden // lanes
    slice_rows = e_ref.shape[0] // 2
    own_slice = table_any.at[pl.ds(pl.multiple_of((me % 16) * slice_rows, 16), slice_rows), :]

    def slab(target, place):
        each = target.shape[1]
        return feed_any.at[:, pl.ds(place * each, each), :]

    loads = [
        pltpu.make_async_copy(source, target, load_sems.at[k])
        for k, (source, target) in enumerate(
            (
                (own_any.at[pl.ds(0, rows), :], own),
                (got_any.at[pl.ds(0, rows), :], got),
                (in_any, in_slab),
                (slab(up, places[0]), up),
                (slab(dn, places[1]), dn),
                (own_slice, e_ref.at[pl.ds(0, slice_rows), :]),
                (chunk, full_chunk.at[me]),
            )
        )
    ]
    for copy in loads:
        copy.start()
    barrier = pltpu.get_barrier_semaphore()
    peers = [
        dict(here, c=1 - here["c"]),
        dict(here, x=1 - here["x"]),
        dict(here, y=1 - here["y"]),
        *[dict(here, z=flip(here["z"], k)) for k in (1, 2, 3)],
    ]
    for peer in peers:
        pl.semaphore_signal(barrier, inc=1, device_id=device_of(peer), device_id_type=MESH)
    pl.semaphore_wait(barrier, len(peers))
    gathers = [
        Gather(
            chunk, full_chunk, start, size, order, sends.at[k], receives.at[k], hands.at[k], hands_got.at[k]
        )
        for k, (start, size, order) in enumerate(streams)
    ]
    swap = pltpu.make_async_remote_copy(
        src_ref=own_slice,
        dst_ref=e_ref.at[pl.ds(slice_rows, slice_rows), :],
        send_sem=swap_sems.at[0],
        recv_sem=swap_sems.at[1],
        device_id=across,
        device_id_type=MESH,
    )

    def advance(first, last):
        for index in range(first, last + 1):
            for gather in gathers:
                gather.step(index)

    advance(0, 0)
    for copy in loads[:3]:
        copy.wait()
    unpack_rows(in_slab, (w, wo))

    @pl.loop(0, tiles)
    def _(i):
        part = pl.ds(pl.multiple_of(i * tile, tile), tile)
        project_body(
            own.at[part, :], got.at[part, :], code_ref.at[part, :], spots_ref, gain_ref, shift_ref, down_ref, w,
            adapt_ref, bias_ref, qkv.at[part, :], mid_ref.at[part, :], x.at[part, :],
        )

        @pl.when(i == tiles - 2)
        def _():
            advance(1, 4)
            swap.start()

    early = [
        pltpu.make_async_copy(qkv, qkv_out, out_sems.at[0]),
        pltpu.make_async_copy(wo, wo_out, out_sems.at[1]),
    ]
    for copy in early:
        copy.start()

    @pl.loop(0, pairs)
    def _(p):
        column = lambda kind: pl.ds(pl.multiple_of((kind * pairs + p) * lanes, lanes), lanes)
        attend_body(
            qkv.at[:, column(0)], qkv.at[:, column(1)], qkv.at[:, column(2)], seg_ref, seg_row_ref,
            ctx.at[:, column(0)], log_ref.at[pl.ds(p, 1)],
        )

        @pl.when(p == pairs // 2 - 1)
        def _():
            advance(5, 11)

        @pl.when(p == pairs - 1)
        def _():
            advance(12, 15)

    for copy in loads[3:5]:
        copy.wait()

    def tile_copies(i):
        part = pl.ds(pl.multiple_of(i * tile, tile), tile)
        turn = i % 2
        return [
            pltpu.make_async_copy(source, target.at[part, :], tile_sems.at[k, i])
            for k, (source, target) in enumerate(
                (
                    (out.at[turn], x_out),
                    (two.at[turn], two_out),
                    (slope.at[turn], slope_out),
                    (x.at[part, :], one_out),
                )
            )
        ]

    plan = {tiles - 4: (16, 19), tiles - 3: (20, 22), tiles - 2: (23, 25), tiles - 1: (26, 27)}

    @pl.loop(0, tiles)
    def _(i):
        part = pl.ds(pl.multiple_of(i * tile, tile), tile)
        turn = i % 2

        @pl.when(i >= 2)
        def _():
            for copy in tile_copies(i - 2):
                copy.wait()

        after_body(
            ctx.at[part, :], x.at[part, :], wo, up, dn, bias_ref, gain_ref, shift_ref, out.at[turn],
            x.at[part, :], two.at[turn], slope.at[turn],
        )
        for copy in tile_copies(i):
            copy.start()
        for k, (first, last) in plan.items():
            pl.when(i == k)(functools.partial(advance, first, last))

    loads[5].wait()
    swap.wait_recv()

    @pl.loop(0, e_ref.shape[0] // 128)
    def _(k):
        part = pl.ds(pl.multiple_of(k * 128, 128), 128)
        et_ref[:, part] = e_ref[part, :].astype(F32).T.astype(BF)

    late = [
        pltpu.make_async_copy(e_ref, e_out, out_sems.at[2]),
        pltpu.make_async_copy(et_ref, et_out, out_sems.at[3]),
    ]
    for copy in late:
        copy.start()
    for gather in gathers:
        gather.finish()
    for i in (tiles - 2, tiles - 1):
        for copy in tile_copies(i):
            copy.wait()
    swap.wait_send()
    for copy in early + late + loads[6:]:
        copy.wait()


def first_layer(own, got, first_in, feed, chunk, table, more, places, slice_rows, shards):
    whole = pl.BlockSpec(memory_space=pltpu.VMEM)
    anywhere = pl.BlockSpec(memory_space=pl.ANY)
    code, down = more[0], more[4]
    rows, hidden = code.shape[0], table.shape[1]
    tile = split_of(rows, 256, 16)
    pairs = HEADS // 2
    units = 4 * hidden
    each = units // shards
    shape = jax.ShapeDtypeStruct
    sems = pltpu.SemaphoreType.DMA
    return pl.pallas_call(
        functools.partial(first_layer_body, streams_of(chunk.shape[0]), shards, places),
        in_specs=[anywhere] * 6 + [whole] * len(more),
        out_specs=[anywhere] * 9 + [whole] * 2,
        out_shape=[
            shape((rows, 3 * hidden), BF),
            shape((rows, hidden), F32),
            shape((rows, hidden), F32),
            shape((rows, hidden), F32),
            shape((rows, units), BF),
            shape((hidden, hidden), BF),
            shape((shards, *chunk.shape), BF),
            shape((2 * slice_rows, hidden), BF),
            shape((hidden, 2 * slice_rows), BF),
            shape((rows, down.shape[2]), BF),
            shape((pairs, 1, 2 * rows), F32),
        ],
        scratch_shapes=[
            pltpu.VMEM((rows, hidden), BF),
            pltpu.VMEM((rows, hidden), BF),
            pltpu.VMEM((shards, 4 * hidden // shards, hidden), BF),
            pltpu.VMEM((3 * hidden, hidden), BF),
            pltpu.VMEM((hidden, hidden), BF),
            pltpu.VMEM((shards, each, hidden), BF),
            pltpu.VMEM((shards, each, hidden), BF),
            pltpu.VMEM((rows, hidden), F32),
            pltpu.VMEM((rows, 3 * hidden), BF),
            pltpu.VMEM((rows, hidden), BF),
            pltpu.VMEM((2, tile, hidden), F32),
            pltpu.VMEM((2, tile, hidden), F32),
            pltpu.VMEM((2, tile, units), BF),
            pltpu.VMEM((2 * slice_rows, hidden), BF),
            pltpu.VMEM((hidden, 2 * slice_rows), BF),
            sems((7,)),
            sems((4, rows // tile)),
            sems((4,)),
            sems((2,)),
            *gather_sems(),
        ],
        compiler_params=params(collective_id=3, has_side_effects=True),
        name="first_layer",
    )(own, got, first_in, feed, chunk, table, *more)


PICK = 64
GROUP = 16


def look_up_body(ids, low_ref, table, first_ref, second_ref, stage):
    batches = first_ref.shape[0] // PICK
    for k, out in enumerate((first_ref, second_ref)):

        @pl.loop(0, batches)
        def _(b, k=k, out=out):
            at = (k * batches + b) * PICK

            def one(t, carry):
                stage[t] = table[ids[at + t]]
                return carry

            lax.fori_loop(0, PICK, one, 0, unroll=8)
            choose = (
                lax.broadcasted_iota(jnp.int32, (PICK, PICK * GROUP), 1)
                == low_ref[pl.ds(pl.multiple_of(at, PICK), PICK), :]
            )
            out[pl.ds(pl.multiple_of(b * PICK, PICK), PICK), :] = mm(
                choose.astype(F32).astype(BF), flat(stage)
            ).astype(BF)


def look_up(ids, table):
    whole = pl.BlockSpec(memory_space=pltpu.VMEM)
    hidden = table.shape[1]
    low = jnp.arange(ids.size, dtype=jnp.int32) % PICK * GROUP + ids % GROUP
    return pl.pallas_call(
        look_up_body,
        in_specs=[pl.BlockSpec(memory_space=pltpu.SMEM), whole, whole],
        out_specs=[whole] * 2,
        out_shape=[jax.ShapeDtypeStruct((ids.size // 2, hidden), table.dtype)] * 2,
        scratch_shapes=[pltpu.VMEM((PICK, GROUP, hidden), table.dtype)],
        compiler_params=params(),
        name="look_up",
    )(ids // GROUP, low[:, None], table.reshape(-1, GROUP, hidden))


def adam(weight, gradient, moment_one, moment_two, fade_one, fade_two):
    moment_one = beta_first * moment_one + (1.0 - beta_first) * gradient
    moment_two = beta_second * moment_two + (1.0 - beta_second) * gradient * gradient
    one_hat = moment_one / fade_one
    two_hat = moment_two / fade_two
    weight = weight - learn_rate * (one_hat / (jnp.sqrt(two_hat) + adam_eps) + decay_rate * weight)
    return (weight, moment_one, moment_two)


BACK_TILE = 512


def finish_body(
    shards, places, edge,
    dout_any, one_any, two_any, slope_any, wo_any, up_any, dn_any, qkv_any, gain_ref, log_ref, seg_ref,
    seg_row_ref, mid_ref, parts, late_ref, facts,
    sums_ref, dense_ref, total_ref,
    dout, one, two, slope, wo, up, dn, qkv, dctx, dv, grad, dense_got, grad_got, note, notes,
    tile_sems, load_sems, dense_sems, grad_sems, note_sems,
):
    rows, hidden = dout.shape
    tile = split_of(rows, BACK_TILE, 16)
    tiles = rows // tile
    me = number_of(position())

    def tile_loads(i):
        part = pl.ds(pl.multiple_of(i * tile, tile), tile)
        return [
            pltpu.make_async_copy(source.at[part, :], target.at[part, :], tile_sems.at[k, i])
            for k, (source, target) in enumerate(
                ((two_any, two), (dout_any, dout), (slope_any, slope), (one_any, one))
            )
        ]

    def slab(source, target, place):
        each = target.shape[1]
        return source.at[:, pl.ds(place * each, each), :]

    loads = [
        pltpu.make_async_copy(source, target, load_sems.at[k])
        for k, (source, target) in enumerate(
            (
                (slab(dn_any, dn, places[1]), dn),
                (slab(up_any, up, places[0]), up),
                (wo_any, wo),
                (qkv_any, qkv),
            )
        )
    ]
    for copy in tile_loads(0) + loads[:3]:
        copy.start()
    for i in range(1, tiles):
        for copy in tile_loads(i):
            copy.start()
    loads[3].start()
    greet_all(shards)
    dense_got[me] = parts[me]
    for copy in loads[:3]:
        copy.wait()

    @pl.loop(0, tiles)
    def _(i):
        for copy in tile_loads(i):
            copy.wait()
        part = pl.ds(pl.multiple_of(i * tile, tile), tile)
        after_back_body(
            dout.at[part, :], one.at[part, :], two.at[part, :], slope.at[part, :], wo, up, dn, gain_ref,
            dctx.at[part, :],
        )

        @pl.when(i == 0)
        def _():
            await_all(shards)
            spread(lambda peer: parts.at[peer], dense_got, dense_sems, me, shards)

    loads[3].wait()
    lanes = 2 * (hidden // HEADS)
    pairs = hidden // lanes

    @pl.loop(0, pairs)
    def _(p):
        column = lambda kind: pl.ds(pl.multiple_of((kind * pairs + p) * lanes, lanes), lanes)
        attend_back_body(
            qkv.at[:, column(0)], qkv.at[:, column(1)], qkv.at[:, column(2)], dctx.at[:, column(0)],
            log_ref.at[pl.ds(p, 1)], seg_ref, seg_row_ref, mid_ref, grad.at[column(0), :], dv, edge=edge,
        )

    grad[...] = grad[...] + late_ref[...]
    each = hidden // shards
    piece = lambda peer: grad.at[pl.ds(pl.multiple_of(peer * each, each), each), :]
    grad_got[me] = piece(me)[...]
    spread(piece, grad_got, grad_sems, me, shards)
    collect(dense_got, dense_sems, me, shards)
    dense = jnp.zeros((each, hidden), F32)
    for k in range(shards):
        dense = dense + dense_got[k].astype(F32)[:each, :]
    dense_ref[...] = dense
    square = jnp.sum(dense * dense, keepdims=True)
    collect(grad_got, grad_sems, me, shards)
    total = grad_got[0]
    for k in range(1, shards):
        total = total + grad_got[k]
    total_ref[...] = total
    square = square + jnp.sum(total * total, keepdims=True)
    row = lax.broadcasted_iota(jnp.int32, note.shape, 0)
    note[...] = jnp.where(row == 0, facts[...], jnp.where(row == 1, square, 0.0))
    notes[me] = note[...]
    spread(lambda peer: note, notes, note_sems, me, shards)
    collect(notes, note_sems, me, shards)
    sums = notes[0]
    for k in range(1, shards):
        sums = sums + notes[k]
    sums_ref[...] = sums


def update_body(
    sums_ref, dense_ref, total_ref, facts, head_w, head_m, head_v, adapt_w, adapt_m, adapt_v,
    loss_out, norm_out, head_w_out, head_m_out, head_v_out, adapt_w_out, adapt_m_out, adapt_v_out,
):
    norm = jnp.sqrt(sums_ref[1:2, 0:1])
    loss_out[...] = sums_ref[0:1, 0:1]
    norm_out[...] = norm
    factor = jnp.minimum(1.0, clip_limit / (norm + 1e-06))
    fades = facts[1:2, 0:1], facts[2:3, 0:1]
    new = adam(head_w[...], dense_ref[...] * factor, head_m[...], head_v[...], *fades)
    head_w_out[...], head_m_out[...], head_v_out[...] = new
    grad = (total_ref[...] * factor).T
    layers, kinds, rank, unused = adapt_w.shape
    for layer in range(layers):
        for kind in range(kinds):
            at = (layer * kinds + kind) * rank
            new = adam(
                adapt_w[layer, kind], grad[at : at + rank], adapt_m[layer, kind], adapt_v[layer, kind], *fades
            )
            adapt_w_out[layer, kind], adapt_m_out[layer, kind], adapt_v_out[layer, kind] = new


def update(sums, dense, total, facts, heads, adapts):
    whole = pl.BlockSpec(memory_space=pltpu.VMEM)
    shape = jax.ShapeDtypeStruct
    return pl.pallas_call(
        update_body,
        in_specs=[whole] * 10,
        out_specs=[whole] * 8,
        out_shape=[shape((1, 1), F32)] * 2 + [shape(a.shape, F32) for a in (*heads, *adapts)],
        compiler_params=params(),
        name="update",
    )(sums, dense, total, facts, *heads, *adapts)


def finish(back, qkv, logs, seg_wide, seg_row, mid, parts, late, facts, edge, shards):
    dout, one, two, slope, wo, up, dn, gains = back
    rows, hidden = dout.shape
    each = hidden // shards
    whole = pl.BlockSpec(memory_space=pltpu.VMEM)
    anywhere = pl.BlockSpec(memory_space=pl.ANY)
    shape = jax.ShapeDtypeStruct
    sems = pltpu.SemaphoreType.DMA
    tiles = rows // split_of(rows, BACK_TILE, 16)
    return pl.pallas_call(
        functools.partial(finish_body, shards, (up[1], dn[1]), edge),
        in_specs=[anywhere] * 8 + [whole] * 8,
        out_specs=[whole] * 3,
        out_shape=[
            shape((8, 128), F32),
            shape((each, hidden), F32),
            shape((each, late.shape[1]), F32),
        ],
        scratch_shapes=[
            pltpu.VMEM((rows, hidden), F32),
            pltpu.VMEM((rows, hidden), F32),
            pltpu.VMEM((rows, hidden), F32),
            pltpu.VMEM(slope.shape, BF),
            pltpu.VMEM(wo.shape, BF),
            slab_scratch(up),
            slab_scratch(dn),
            pltpu.VMEM(qkv.shape, BF),
            pltpu.VMEM((rows, hidden), BF),
            pltpu.VMEM((rows, 2 * (hidden // HEADS)), F32),
            pltpu.VMEM(late.shape, F32),
            pltpu.VMEM(parts.shape, BF),
            pltpu.VMEM((shards, each, late.shape[1]), F32),
            pltpu.VMEM((8, 128), F32),
            pltpu.VMEM((shards, 8, 128), F32),
            sems((4, tiles)),
            sems((4,)),
            sems((2,)),
            sems((2,)),
            sems((2,)),
        ],
        compiler_params=params(collective_id=2, has_side_effects=True),
        name="finish",
    )(dout, one, two, slope, wo, up[0], dn[0], qkv, gains, logs, seg_wide, seg_row, mid, parts, late, facts)


HOPS = 3
LOG_ROWS = 16


def flip(z, k):
    return (z % 2 + k % 2) % 2 + 2 * ((z // 2 + k // 2) % 2)


def pack_log(log_row, rows):
    high = log_row.astype(BF).astype(F32)
    middle = (log_row - high).astype(BF).astype(F32)
    low = log_row - high - middle
    row = lax.broadcasted_iota(jnp.int32, (rows, log_row.shape[1]), 0)
    return jnp.where(
        row == 0, high, jnp.where(row == 1, middle, jnp.where(row == 2, low, 0.0))
    ).astype(BF)


def unpack(block, hidden):
    logs = block[hidden : hidden + LOG_ROWS, :].astype(F32)
    return block[:hidden, :].astype(F32), jnp.sum(logs, 0, keepdims=True)


def merged(one, two):
    top = jnp.maximum(one[1], two[1])
    first, second = jnp.exp(one[1] - top), jnp.exp(two[1] - top)
    total = first + second
    inverse = 1.0 / total
    return one[0] * (first * inverse) + two[0] * (second * inverse), top + jnp.log(total)


def store_packed(ref, pair, hidden):
    ref[:hidden, :] = pair[0].astype(BF)
    ref[hidden : hidden + LOG_ROWS, :] = pack_log(pair[1], LOG_ROWS)


def head_body(
    u_ref, e_any, et_any, bias_any, mean_ref, log_ref,
    e_ref, et_ref, bias_ref, feats, packs, handed, crossed, kept, lined, zouts,
    loads, z_send, z_get, y_send, y_get, c_send, c_get, h_send, h_get, p_send, p_get, l_send, l_get,
):
    here = position()
    z, y, c = here["z"], here["y"], here["c"]
    labels, hidden = u_ref.shape
    slot_of = lambda zz, yy, cc: (zz * 2 + yy) * 2 + cc
    me = slot_of(z, y, c)
    sibling = device_of(dict(here, c=1 - c))
    beside = device_of(dict(here, y=1 - y))
    at_z = lambda zz: device_of(dict(here, z=zz))
    inside = lambda zz: (zz >= 0) & (zz <= HOPS)

    fills = [
        pltpu.make_async_copy(source, target, loads.at[k])
        for k, (source, target) in enumerate(((e_any, e_ref), (bias_any, bias_ref), (et_any, et_ref)))
    ]
    for fill in fills:
        fill.start()
    barrier = pltpu.get_barrier_semaphore()
    for target in (sibling, beside):
        pl.semaphore_signal(barrier, inc=1, device_id=target, device_id_type=MESH)
    for k in range(1, 4):
        pl.semaphore_signal(barrier, inc=1, device_id=at_z(flip(z, k)), device_id_type=MESH)
    feats[me] = u_ref[...]
    pl.semaphore_wait(barrier, 5)

    def move(slot, device, send, get):
        return pltpu.make_async_remote_copy(
            src_ref=feats.at[slot],
            dst_ref=feats.at[slot],
            send_sem=send,
            recv_sem=get,
            device_id=device,
            device_id_type=MESH,
        )

    def hand(zz, other):
        slot = slot_of(zz, (y + other) % 2, c)
        return move(slot, sibling, c_send.at[other * 4 + zz], c_get.at[other * 4 + zz])

    def handed_here(zz, other):
        slot = slot_of(zz, (y + other) % 2, 1 - c)
        return move(slot, sibling, c_send.at[other * 4 + zz], c_get.at[other * 4 + zz])

    def cross(zz):
        return move(slot_of(zz, y, c), beside, y_send.at[zz], y_get.at[zz])

    def crossed_here(zz):
        return move(slot_of(zz, 1 - y, c), beside, y_send.at[zz], y_get.at[zz])

    def along(zz, to, way):
        return move(slot_of(zz, y, c), at_z(to), z_send.at[way * 4 + zz], z_get.at[zz])

    def own_round():
        for way, to in ((0, z + 1), (1, z - 1)):

            @pl.when(inside(to))
            def _(way=way, to=to):
                along(z, to, way).start()

        cross(z).start()
        hand(z, 0).start()

    def later_round(r):
        if r <= HOPS:
            for way, origin, to in ((0, z - r, z + 1), (1, z + r, z - 1)):

                @pl.when(inside(origin))
                def _(way=way, origin=origin, to=to):
                    along(origin, to, way).wait_recv()

                    @pl.when(inside(to))
                    def _():
                        along(origin, to, way).start()

                    cross(origin).start()
                    hand(origin, 0).start()

        for origin in (z - (r - 1), z + (r - 1))[: 1 if r == 1 else 2]:

            @pl.when(inside(origin))
            def _(origin=origin):
                crossed_here(origin).wait_recv()
                hand(origin, 1).start()

    own_round()
    fills[0].wait()
    fills[1].wait()
    fills[2].wait()
    count = e_ref.shape[0]

    def hand_part(s):
        return pltpu.make_async_remote_copy(
            src_ref=packs.at[s, 1 - c],
            dst_ref=handed.at[s],
            send_sem=h_send.at[s],
            recv_sem=h_get.at[s],
            device_id=sibling,
            device_id_type=MESH,
        )

    def cross_part(k):
        return pltpu.make_async_remote_copy(
            src_ref=packs.at[cross_step(k), c],
            dst_ref=crossed.at[k],
            send_sem=p_send.at[k],
            recv_sem=p_get.at[k],
            device_id=beside,
            device_id_type=MESH,
        )

    def line_part(k):
        return pltpu.make_async_remote_copy(
            src_ref=zouts.at[k],
            dst_ref=lined.at[k],
            send_sem=l_send.at[k],
            recv_sem=l_get.at[k],
            device_id=at_z(flip(z, k)),
            device_id_type=MESH,
        )

    def row_of(s):
        return (s + 1) // 2 % 4

    def other_of(s):
        return (s % 2 + (7 - s) // 7 + s // 7) % 2

    def cross_step(k):
        return 2 * k - 1 + (3 - k) // 3

    def compute(s):
        zt, yt = flip(z, row_of(s)), (y + other_of(s)) % 2
        handed_here(zt, other_of(s)).wait_recv()
        first = slot_of(zt, yt, 0)
        u = feats[pl.ds(first, 2)].reshape(2 * labels, hidden)
        top = total = mean = None
        for start in range(0, count, 1280):
            if start == 1280:
                between(s)
            part = slice(start, min(start + 1280, count))
            bias = bias_ref[part, :]
            logits = mm_nt(e_ref[part, :], u) + jnp.concatenate([bias, bias], 1)
            high = jnp.max(logits, 0, keepdims=True)
            new = high if top is None else jnp.maximum(top, high)
            grown = jnp.exp(logits - new)
            sums = jnp.sum(grown, 0, keepdims=True)
            product = mm(et_ref[:, part], grown.astype(BF))
            if top is None:
                total, mean = sums, product
            else:
                shrink = jnp.exp(top - new)
                total, mean = total * shrink + sums, mean * shrink + product
            top = new
        mean = mean * (1.0 / total)
        logs = top + jnp.log(total)
        for k in range(2):
            half = slice(k * labels, (k + 1) * labels)
            packs[s, k, :hidden, :] = mean[:, half].astype(BF)
            packs[s, k, hidden : hidden + LOG_ROWS, :] = pack_log(logs[:, half], LOG_ROWS)
        hand_part(s).start()

    def settle(s):
        hand_part(s).wait_recv()
        pair = merged(unpack(packs[s, c], hidden), unpack(handed[s], hidden))

        @pl.when(other_of(s) == 1)
        def _():
            store_packed(packs.at[s, c], pair, hidden)
            cross_part(row_of(s)).start()

        @pl.when(other_of(s) == 0)
        def _():
            store_packed(kept.at[row_of(s)], pair, hidden)

    def finish(k):
        cross_part(k).wait_recv()
        pair = merged(unpack(kept[k], hidden), unpack(crossed[k], hidden))

        @pl.when(k > 0)
        def _():
            store_packed(zouts.at[k], pair, hidden)
            line_part(k).start()

        @pl.when(k == 0)
        def _():
            store_packed(zouts.at[k], pair, hidden)

    steps = 8

    def between(s):
        @pl.when(s > 0)
        def _():
            settle(s - 1)

        @pl.when((s >= 3) & (s % 2 == 1))
        def _():
            finish((s - 1) // 2)

    @pl.loop(0, steps)
    def _(s):
        for r in range(1, HOPS + 2):
            pl.when(s == r - 1)(functools.partial(later_round, r))
        compute(s)

    settle(steps - 1)
    finish(0)
    total = unpack(zouts[0], hidden)
    for k in range(1, 4):
        line_part(k).wait_recv()
        total = merged(total, unpack(lined[k], hidden))
    mean_ref[...] = total[0]
    log_ref[...] = total[1]

    for way, to in ((0, z + 1), (1, z - 1)):

        @pl.when(inside(to))
        def _(way=way, to=to):
            along(z, to, way).wait_send()

    cross(z).wait_send()
    hand(z, 0).wait_send()
    for r in range(1, HOPS + 1):
        for way, origin, to in ((0, z - r, z + 1), (1, z + r, z - 1)):

            @pl.when(inside(origin))
            def _(way=way, origin=origin, to=to):
                @pl.when(inside(to))
                def _():
                    along(origin, to, way).wait_send()

                cross(origin).wait_send()
                hand(origin, 0).wait_send()

    for origin in range(4):
        hand(origin, 1).wait_send()
    for s in range(steps):
        hand_part(s).wait_send()
    for k in range(4):
        cross_part(k).wait_send()
    for k in range(1, 4):
        line_part(k).wait_send()


def head(u, e, et, bias_wide):
    labels, hidden = u.shape
    whole = pl.BlockSpec(memory_space=pltpu.VMEM)
    anywhere = pl.BlockSpec(memory_space=pl.ANY)
    shape = jax.ShapeDtypeStruct
    sems = pltpu.SemaphoreType.DMA
    block = (hidden + LOG_ROWS, labels)
    return pl.pallas_call(
        head_body,
        in_specs=[whole] + [anywhere] * 3,
        out_specs=[whole] * 2,
        out_shape=[shape((hidden, labels), F32), shape((1, labels), F32)],
        scratch_shapes=[
            pltpu.VMEM(e.shape, BF),
            pltpu.VMEM(et.shape, BF),
            pltpu.VMEM(bias_wide.shape, F32),
            pltpu.VMEM((16, labels, hidden), BF),
            pltpu.VMEM((8, 2, *block), BF),
            pltpu.VMEM((8, *block), BF),
            pltpu.VMEM((4, *block), BF),
            pltpu.VMEM((4, *block), BF),
            pltpu.VMEM((4, *block), BF),
            pltpu.VMEM((4, *block), BF),
            sems((3,)),
            sems((8,)),
            sems((4,)),
            sems((4,)),
            sems((4,)),
            sems((8,)),
            sems((8,)),
            sems((8,)),
            sems((8,)),
            sems((4,)),
            sems((4,)),
            sems((4,)),
            sems((4,)),
        ],
        compiler_params=params(collective_id=4, has_side_effects=True),
        name="head",
    )(u, e, et, bias_wide)


def seg_positions(segments):
    index = jnp.arange(segments.shape[-1], dtype=jnp.int32)
    fresh = jnp.concatenate([jnp.ones((1,), dtype=bool), segments[1:] != segments[:-1]], -1)
    starts = lax.cummax(jnp.where(fresh, index, jnp.zeros_like(index)), axis=0)
    return index - starts


def pad_rows(matrix, multiple):
    return jnp.pad(matrix, ((0, -matrix.shape[0] % multiple), (0, 0)))


def slab_of(gathered, start, rows):
    if rows % 16 == 0 and start % rows == 0:
        return (gathered, start // rows, rows)
    part = gathered[:, start : start + rows].reshape(1, -1, gathered.shape[2])
    return (part, 0, part.shape[1])


def per_device(
    input_token_index,
    sentence_numbers,
    label_positions,
    label_target_token,
    sequence_task_index,
    task_loss_weight,
    optimizer_step_count,
    embed,
    position_embedding,
    norm_gain_vector,
    norm_bias_vector,
    attention_in_weight,
    attention_out_weight,
    feedforward_up,
    feedforward_down,
    layer_bias_vector,
    head_dense_bias,
    vocabulary_bias,
    adapter_down_matrix,
    adapter_up_matrix,
    adapter_moment_first,
    adapter_moment_second,
    head_projection,
    head_moment_first,
    head_moment_second,
):
    shards = lax.axis_size("dp") * lax.axis_size("fsdp")
    dp_index = lax.axis_index("dp")
    fsdp_index = lax.axis_index("fsdp")
    layers, unused, rank, up_part = adapter_up_matrix.shape
    hidden = embed.shape[1]
    tokens = input_token_index.shape[1]
    labels = label_positions.shape[1]
    qkv_rows = attention_in_weight.shape[2]
    out_rows = attention_out_weight.shape[2]
    ff_rows = feedforward_up.shape[2]
    head_rows = head_projection.shape[0]

    grouped = (lax.axis_size("dp"), lax.axis_size("fsdp")) == (2, 16)
    feeds = [[feedforward_up[layer].T, feedforward_down[layer]] for layer in range(layers)]
    attends = [[attention_in_weight[layer].T, attention_out_weight[layer].T] for layer in range(layers)]
    first_in = lax.all_gather(jnp.concatenate(attends[0], 0), BOTH, axis=0, tiled=False)
    feed_chunk = jnp.concatenate(feeds[0], 0)
    last_chunk = pad_rows(
        jnp.concatenate(feeds[1] + attends[1] + [head_projection.astype(BF)], 0), 32
    )

    table_rows = embed.shape[0]
    wanted = jnp.concatenate([input_token_index[0], label_target_token[0]])
    dp_count = lax.axis_size("dp")
    group_ids = lax.all_gather(wanted, "dp", axis=0, tiled=False) - dp_index * table_rows
    inside = (group_ids >= 0) & (group_ids < table_rows)
    group_ids = jnp.clip(group_ids, 0, table_rows - 1)
    mine = lax.dynamic_index_in_dim(inside, dp_index, 0, keepdims=False)

    task_range = jnp.arange(TASKS, dtype=jnp.int32)
    slice_rows = vocabulary_bias.shape[0]
    ups = adapter_up_matrix.reshape(-1)
    if grouped:
        pair_ids = jnp.concatenate(
            [
                lax.dynamic_index_in_dim(group_ids, (dp_index + shift) % 2, 0, keepdims=False)
                for shift in (1, 0)
            ]
        )
        other_rows, own_rows = look_up(pair_ids, embed)
        fact = jnp.concatenate([vocabulary_bias, ups, sequence_task_index.astype(F32)])
        fact_rows = -(-fact.size // 1024) * 8
        got, facts, feed_full = start_exchange(
            other_rows,
            jnp.pad(fact, (0, fact_rows * 128 - fact.size)).reshape(fact_rows, 128),
            feed_chunk,
            shards,
        )
        facts = facts.reshape(shards, -1)
        all_bias = facts[:, :slice_rows].reshape(-1)
        every_up = facts[:, slice_rows : slice_rows + ups.size]
        every_task = facts[:, slice_rows + ups.size].astype(jnp.int32)
    else:
        looked = jnp.where(
            inside.reshape(-1)[:, None], embed[group_ids.reshape(-1)], jnp.zeros((), BF)
        )
        own_rows = got = lax.psum_scatter(looked, "dp", scatter_dimension=0, tiled=True)
        all_bias = lax.all_gather(vocabulary_bias, BOTH, axis=0, tiled=True)
        every_up = lax.all_gather(ups, BOTH, axis=0, tiled=False)
        every_task = lax.all_gather(sequence_task_index, BOTH, axis=0, tiled=True)
    counts = labels * jnp.sum((every_task[:, None] == task_range[None, :]).astype(F32), 0)
    task_hot = (sequence_task_index[:, None] == task_range[None, :]).astype(F32)
    row_weight = jnp.sum(task_hot[0] * (task_loss_weight / jnp.maximum(counts, 1.0)))
    ups_full = (
        every_up.astype(BF)
        .reshape(shards, layers, 2, rank, up_part)
        .transpose(1, 2, 3, 0, 4)
        .reshape(layers, 2, rank, hidden)
    )
    blank = jnp.zeros((rank, hidden), BF)
    spare = lambda rows: jnp.zeros((rows, 3 * hidden), BF)
    adapters = jnp.stack(
        [
            jnp.concatenate(
                [
                    spare(2 * rank * layer),
                    jnp.concatenate([2 * ups_full[layer, 0], blank, blank], 1),
                    jnp.concatenate([blank, blank, 2 * ups_full[layer, 1]], 1),
                    spare(128 - 2 * rank * (layer + 1)),
                ],
                0,
            )
            for layer in range(layers)
        ]
    )
    downs = jnp.stack(
        [
            jnp.pad(
                jnp.concatenate([adapter_down_matrix[layer, 0], adapter_down_matrix[layer, 1]], 1),
                ((0, 0), (2 * rank * layer, 128 - 2 * rank * (layer + 1))),
            )
            for layer in range(layers)
        ]
    )
    target_rows = jnp.where(mine[tokens:, None], own_rows[tokens:], got[tokens:])
    segments = sentence_numbers[0]
    code = (2 * seg_positions(segments) + mine[:tokens].astype(jnp.int32))[:, None]
    seg_real = segments.astype(F32)
    seg_wide = jnp.broadcast_to(seg_real[:, None], (tokens, 128))
    seg_row = seg_real[None, :]
    place_row = label_positions
    place_col = jnp.broadcast_to(label_positions.reshape(labels, 1), (labels, 128))

    own_bias = jnp.concatenate(
        [
            lax.dynamic_slice_in_dim(
                all_bias,
                ((dp_index - shift) % dp_count) * table_rows + fsdp_index * slice_rows,
                slice_rows,
                0,
            )
            for shift in range(dp_count)
        ]
    )
    bias_wide = jnp.broadcast_to(own_bias[:, None], (own_bias.shape[0], 128))
    target_bias = all_bias[label_target_token[0]]

    gains, shifts = norm_gain_vector, norm_bias_vector
    last_inputs = (place_col, place_row, seg_wide, downs, adapters, layer_bias_vector)
    in_start = 2 * ff_rows
    slabs_of = lambda full_chunk: (slab_of(full_chunk, 0, ff_rows), slab_of(full_chunk, ff_rows, ff_rows))
    if grouped:
        more = (
            code, position_embedding, gains, shifts, downs, adapters, layer_bias_vector, seg_wide, seg_row,
        )
        qkv, x_last, one, two, slope, out_first, last_full, own_vocab, own_turned, mid, logs = first_layer(
            own_rows, got, first_in, feed_full, last_chunk, embed, more, (0, 1), slice_rows, shards
        )
        slabs = [slabs_of(feed_full), slabs_of(last_full)]
        *saved, in_last, out_last, head_full = last_forward(
            x_last, *last_inputs, (last_full,), (in_start, in_start + qkv_rows + out_rows), *slabs[1], gains,
            shifts, head_dense_bias[None, :],
        )
        mean_t, own_logs = head(saved[-1], own_vocab, own_turned, bias_wide)
    else:
        feed_full = lax.all_gather(feed_chunk, BOTH, axis=0, tiled=False)
        last_full = lax.all_gather(last_chunk, BOTH, axis=0, tiled=False)
        slabs = [slabs_of(feed_full), slabs_of(last_full)]
        taken = lambda full_chunk, start, size: full_chunk[:, start : start + size].reshape(-1, hidden)
        in_first, out_first = taken(first_in, 0, qkv_rows), taken(first_in, qkv_rows, out_rows)
        in_last = taken(last_full, in_start, qkv_rows)
        out_last = taken(last_full, in_start + qkv_rows, out_rows)
        head_full = taken(last_full, in_start + qkv_rows + out_rows, head_rows)
        qkv, mid, hidden_rows = project(
            own_rows, got, code, position_embedding, gains, shifts, downs, in_first, adapters, layer_bias_vector
        )
        context, logs = attend(qkv, seg_wide, seg_row)
        x_last, one, two, slope = after(
            context, hidden_rows, out_first, *slabs[0], layer_bias_vector, gains, shifts
        )
        saved = last_forward(
            x_last, *last_inputs, (in_last, out_last, head_full), None, *slabs[1], gains, shifts,
            head_dense_bias[None, :],
        )
        features = saved[-1]
        own_slice = lax.dynamic_slice_in_dim(embed, fsdp_index * slice_rows, slice_rows, 0)
        own_vocab = jnp.concatenate(
            [own_slice]
            + [
                lax.ppermute(
                    own_slice, "dp", [(k, (k + shift) % dp_count) for k in range(dp_count)]
                )
                for shift in range(1, dp_count)
            ],
            0,
        )
        every = lax.all_gather(features, "fsdp", axis=0, tiled=True)
        means, local_logs = vocab(every, own_vocab, own_vocab.T, bias_wide, labels)
        local_logs = local_logs.reshape(-1, labels)
        all_logs = lax.all_gather(local_logs, "fsdp", axis=0, tiled=False)
        whole_logs = jax.nn.logsumexp(all_logs, axis=0)
        scaled = (means * jnp.exp(local_logs - whole_logs)[:, None, :]).astype(BF)
        mean_t = lax.psum_scatter(scaled, "fsdp", scatter_dimension=0, tiled=True)[0].astype(F32)
        own_logs = lax.dynamic_index_in_dim(whole_logs, fsdp_index, 0, keepdims=False)
        own_logs = own_logs[None, :]

    step_as_real = optimizer_step_count[0].astype(F32)
    fades = (1.0 - beta_first**step_as_real, 1.0 - beta_second**step_as_real)
    lanes = lambda value: jnp.pad(
        jnp.broadcast_to(value, (1, value.size if value.ndim else 128)), ((0, 0), (0, 128))
    )[:, :128]
    facts = jnp.concatenate(
        [lanes(value) for value in (row_weight, *fades, target_bias)] + [jnp.zeros((4, 128), F32)]
    )
    hidden_grad, dense_gradient, late, facts = last_backward(
        mean_t, own_logs, target_rows, facts, saved, place_col, place_row, seg_wide, downs, in_last, adapters,
        out_last, *slabs[1], gains, head_full, 3 * rank, shards if grouped else None,
    )
    back = (hidden_grad, one, two, slope, out_first, *slabs[0], gains)
    adapts = (adapter_up_matrix, adapter_moment_first, adapter_moment_second)
    heads = (head_projection, head_moment_first, head_moment_second)
    if grouped:
        sums, dense_portion, adapter_portion = finish(
            back, qkv, logs, seg_wide, seg_row, mid, dense_gradient, late, facts, rank, shards
        )
        loss, norm, *new = update(sums, dense_portion, adapter_portion, facts, heads, adapts)
        return (loss[0, 0], norm[0, 0], *new[3:], *new[:3])
    dctx = after_back(*back)
    first = attend_back(qkv, dctx, logs, seg_wide, seg_row, mid, rank)
    adapter_gradient = (first + late)[:, : 2 * rank * layers].T.reshape(layers, 2, rank, hidden)
    dense_portion = lax.psum_scatter(dense_gradient, BOTH, scatter_dimension=0, tiled=True)
    adapter_portion = lax.psum_scatter(adapter_gradient, BOTH, scatter_dimension=3, tiled=True)
    squared_entries = jnp.sum(adapter_portion * adapter_portion) + jnp.sum(dense_portion * dense_portion)
    masked_task_loss, norm_square = lax.psum((facts[0, 0], squared_entries), BOTH)
    gradient_norm = jnp.sqrt(norm_square)
    factor = jnp.minimum(1.0, clip_limit / (gradient_norm + 1e-06))
    adapter_new = adam(adapts[0], adapter_portion * factor, *adapts[1:], *fades)
    dense_new = adam(heads[0], dense_portion * factor, *heads[1:], *fades)
    return (masked_task_loss, gradient_norm, *adapter_new, *dense_new)


def solution(mesh):
    rows = P(BOTH, None)
    in_specs = (
        rows,
        rows,
        rows,
        rows,
        P(BOTH),
        P(),
        P(),
        P("dp", None),
        P(),
        P(),
        P(),
        P(None, None, BOTH),
        P(None, None, BOTH),
        P(None, None, BOTH),
        P(None, BOTH, None),
        P(),
        P(),
        P(BOTH),
        P(),
        P(None, None, None, BOTH),
        P(None, None, None, BOTH),
        P(None, None, None, BOTH),
        rows,
        rows,
        rows,
    )
    adapter = P(None, None, None, BOTH)
    out_specs = (P(), P(), adapter, adapter, adapter, rows, rows, rows)
    return jax.shard_map(
        per_device, mesh=mesh, in_specs=in_specs, out_specs=out_specs, check_vma=False
    )
```

```python
import functools

import jax
import jax.numpy as jnp
from jax import lax
from jax.experimental import pallas as pl
from jax.experimental.pallas import tpu as pltpu
from jax.sharding import PartitionSpec as P

HEADS = 12
TASKS = 4
REACH = 128

norm_eps = 1e-05
adapter_scale = 2.0
clip_limit = 0.01
learn_rate = 0.05
beta_first = 0.9
beta_second = 0.999
adam_eps = 1e-08
decay_rate = 0.01
masked_score = -1e30

BF = jnp.bfloat16
F32 = jnp.float32
BOTH = ("dp", "fsdp")
VMEM_BYTES = 60 * 1024 * 1024


def mm(a, b):
    return lax.dot_general(a, b, (((1,), (0,)), ((), ())), preferred_element_type=F32)


def mm_nt(a, b):
    return lax.dot_general(a, b, (((1,), (1,)), ((), ())), preferred_element_type=F32)


def mm_tn(a, b):
    return lax.dot_general(a, b, (((0,), (0,)), ((), ())), preferred_element_type=F32)


def layer_norm(rows_in, gain, shift):
    center = rows_in - jnp.mean(rows_in, -1, keepdims=True)
    spread = jnp.mean(center * center, -1, keepdims=True)
    return center * lax.rsqrt(spread + norm_eps) * gain + shift


def norm_back(rows_in, gain, gradient):
    center = rows_in - jnp.mean(rows_in, -1, keepdims=True)
    inverse = lax.rsqrt(jnp.mean(center * center, -1, keepdims=True) + norm_eps)
    unit = center * inverse
    scaled = gradient * gain
    return inverse * (
        scaled
        - jnp.mean(scaled, -1, keepdims=True)
        - unit * jnp.mean(scaled * unit, -1, keepdims=True)
    )


def gelu_pair(v):
    size = jnp.abs(v) * 0.7071067811865476
    base = 1.0 + 0.3275911 * size
    t = pl.reciprocal(base, approx=True)
    t = t * (2.0 - base * t)
    bell = jnp.exp(-0.5 * v * v)
    poly = t * (
        0.127414796 + t * (-0.142248368 + t * (0.7107068705 + t * (-0.7265760135 + t * 0.5307027145)))
    )
    tail = poly * bell
    phi = jnp.where(v >= 0.0, 1.0 - tail, tail)
    return v * phi, phi + v * (bell * 0.3989422804014327)


def params(**more):
    return pltpu.CompilerParams(vmem_limit_bytes=VMEM_BYTES, **more)


def full(shape):
    return pl.BlockSpec(shape, lambda *_: (0,) * len(shape))


def split_of(total, most, step):
    size = (min(most, total) // step) * step
    while size > step and total % size:
        size -= step
    return size if size and total % size == 0 else total


def pair_rows(block, width):
    first = lax.broadcasted_iota(jnp.int32, block.shape, 1) < width
    return jnp.concatenate([jnp.where(first, block, 0.0), jnp.where(first, 0.0, block)], 0).astype(BF)


def pair_join(wide, width):
    rows = wide.shape[1] // 2
    return jnp.concatenate([wide[:width, :rows], wide[width:, rows:]], 0)


def masked(scores, same):
    rows = scores.shape[1] // 2
    return jnp.concatenate(
        [
            jnp.where(same, scores[:, :rows], masked_score),
            jnp.where(same, scores[:, rows:], masked_score),
        ],
        1,
    )


def qkv_bias(bias_ref, layer, start, size):
    hidden = bias_ref.shape[1] // 8
    if start >= 2 * hidden:
        return bias_ref[layer : layer + 1, start - hidden : start - hidden + size]
    return bias_ref[layer : layer + 1, start : start + size] if start < hidden else 0.0


def norm_of(norm_refs, k):
    return norm_refs[0][k : k + 1, :], norm_refs[1][k : k + 1, :]


def project_body(
    own_ref, got_ref, code_ref, spots_ref, gain_ref, shift_ref, down_ref, w_ref, up_ref, bias_ref,
    out_ref, mid_ref, x_ref,
):
    mine = code_ref[...] % 2
    choose = (
        lax.broadcasted_iota(jnp.int32, (own_ref.shape[0], spots_ref.shape[0]), 1) == code_ref[...] // 2
    )
    summed = jnp.where(
        mine > 0, own_ref[...].astype(F32), got_ref[...].astype(F32)
    ) + mm(choose.astype(F32).astype(BF), spots_ref[...])
    x = layer_norm(summed, *norm_of((gain_ref, shift_ref), 0))
    x_ref[...] = x
    low = x.astype(BF)
    mid = mm(low, down_ref[0]).astype(BF)
    mid_ref[...] = mid
    total = w_ref.shape[0]
    step = total // 3
    for start in range(0, total, step):
        part = slice(start, start + step)
        out_ref[:, part] = (
            mm_nt(low, w_ref[part, :]) + mm(mid, up_ref[0, :, part]) + qkv_bias(bias_ref, 0, start, step)
        ).astype(BF)


def project(own, got, code, spots, gains, shifts, down, w, up, bias):
    rows, width = code.shape[0], own.shape[1]
    tile = split_of(rows, 256, 16)
    total = w.shape[0]
    row = lambda n: pl.BlockSpec((tile, n), lambda i: (i, 0))
    return pl.pallas_call(
        project_body,
        grid=(rows // tile,),
        in_specs=[row(width), row(width), row(1)]
        + [full(a.shape) for a in (spots, gains, shifts, down, w, up, bias)],
        out_specs=[row(total), row(down.shape[2]), row(width)],
        out_shape=[
            jax.ShapeDtypeStruct((rows, total), BF),
            jax.ShapeDtypeStruct((rows, down.shape[2]), BF),
            jax.ShapeDtypeStruct((rows, width), F32),
        ],
        compiler_params=params(),
        name="project",
    )(own, got, code, spots, gains, shifts, down, w, up, bias)


def attend_body(q_ref, k_ref, v_ref, seg_ref, seg_row_ref, ctx_ref, log_ref):
    rows = q_ref.shape[0]
    width = q_ref.shape[1] // 2
    scale = width**-0.5
    for start in range(0, rows, REACH):
        own = slice(start, start + REACH)
        near = slice(max(0, start - REACH), min(rows, start + 2 * REACH))
        queries = pair_rows(q_ref[own, :].astype(F32) * scale, width)
        same = seg_ref[near, :] == seg_row_ref[:, own]
        scores = masked(mm_nt(k_ref[near, :], queries), same)
        top = jnp.max(scores, 0, keepdims=True)
        weights = jnp.exp(scores - top)
        total = jnp.sum(weights, 0, keepdims=True)
        context = mm_tn(v_ref[near, :], weights.astype(BF)) * (1.0 / total)
        ctx_ref[own, :] = pair_join(context, width).T.astype(BF)
        log_ref[0, :, 2 * start : 2 * start + 2 * REACH] = top + jnp.log(total)


def attend(qkv, seg_wide, seg_row):
    rows, total = qkv.shape
    hidden = total // 3
    lanes = 2 * (hidden // HEADS)
    pairs = hidden // lanes
    column = lambda kind: pl.BlockSpec((rows, lanes), lambda p: (0, kind * pairs + p))
    return pl.pallas_call(
        attend_body,
        grid=(pairs,),
        in_specs=[column(0), column(1), column(2), full(seg_wide.shape), full(seg_row.shape)],
        out_specs=[
            pl.BlockSpec((rows, lanes), lambda p: (0, p)),
            pl.BlockSpec((1, 1, 2 * rows), lambda p: (p, 0, 0)),
        ],
        out_shape=[
            jax.ShapeDtypeStruct((rows, hidden), BF),
            jax.ShapeDtypeStruct((pairs, 1, 2 * rows), F32),
        ],
        compiler_params=params(),
        name="attend",
    )(qkv, qkv, qkv, seg_wide, seg_row)


def flat(ref):
    whole = ref[...]
    return whole.reshape(-1, whole.shape[-1])


def rows_of(ref, start, size):
    each = ref.shape[1]
    if size % each == 0 and start % each == 0 and each % 16 == 0:
        part = ref[start // each : (start + size) // each, :, :]
        return part.reshape(size, part.shape[-1])
    return flat(ref)[start : start + size, :]


def feed_step(ref):
    units = ref.shape[0] * ref.shape[1]
    step = ref.shape[1]
    while units % (2 * step) == 0 and 2 * step <= 768 and ref.shape[0] > 1:
        step *= 2
    return units, (step if ref.shape[0] > 1 else split_of(units, 768, 128))


def later_biases(bias_ref, layer):
    hidden = bias_ref.shape[1] // 8
    row = bias_ref[layer : layer + 1, :]
    return row[:, 2 * hidden : 3 * hidden], row[:, 3 * hidden : 7 * hidden], row[:, 7 * hidden :]


def after_body(
    ctx_ref, x_ref, wo_ref, up_ref, down_ref, bias_ref, gain_ref, shift_ref,
    out_ref, one_ref, two_ref, slope_ref,
):
    bo, b1, b2 = later_biases(bias_ref, 0)
    one = x_ref[...] + (mm_nt(ctx_ref[...], wo_ref[...]) + bo)
    one_ref[...] = one
    middle = layer_norm(one, *norm_of((gain_ref, shift_ref), 1))
    low = middle.astype(BF)
    total = middle + b2
    units, step = feed_step(up_ref)
    for start in range(0, units, step):
        part = slice(start, start + step)
        act, slope = gelu_pair(mm_nt(low, rows_of(up_ref, start, step)) + b1[:, part])
        slope_ref[:, part] = slope.astype(BF)
        total = total + mm(act.astype(BF), rows_of(down_ref, start, step))
    two_ref[...] = total
    out_ref[...] = layer_norm(total, *norm_of((gain_ref, shift_ref), 2))


def slab_spec(slab):
    array, place, rows = slab
    return pl.BlockSpec((array.shape[0], rows, array.shape[2]), lambda *_: (0, place, 0))


def after(ctx, x, wo, up, down, bias, gains, shifts):
    rows, width = x.shape
    tile = split_of(rows, 256, 16)
    units = 4 * width
    row = lambda n: pl.BlockSpec((tile, n), lambda i: (i, 0))
    return pl.pallas_call(
        after_body,
        grid=(rows // tile,),
        in_specs=[row(width), row(width), full(wo.shape), slab_spec(up), slab_spec(down)]
        + [full(a.shape) for a in (bias, gains, shifts)],
        out_specs=[row(width), row(width), row(width), row(units)],
        out_shape=[jax.ShapeDtypeStruct((rows, width), F32)] * 3
        + [jax.ShapeDtypeStruct((rows, units), BF)],
        compiler_params=params(),
        name="after",
    )(ctx, x, wo, up[0], down[0], bias, gains, shifts)


def exact_rows(choose, matrix):
    high = matrix.astype(BF)
    rest = matrix - high.astype(F32)
    middle = rest.astype(BF)
    low = (rest - middle.astype(F32)).astype(BF)
    return mm(choose, high) + mm(choose, middle) + mm(choose, low)


def unpack_rows(slab_ref, targets):
    shards = slab_ref.shape[0]

    @pl.loop(0, shards // 2)
    def _(k):
        first, second = slab_ref[2 * k].astype(F32), slab_ref[2 * k + 1].astype(F32)
        at = 0
        for target in targets:
            each = target.shape[0] // shards
            both = jnp.concatenate([first[at : at + each], second[at : at + each]], 0)
            target[pl.ds(pl.multiple_of(2 * each * k, 2 * each), 2 * each), :] = both.astype(BF)
            at += each


def last_forward_body(
    x_ref, place_ref, place_row_ref, seg_ref, down_ref, adapt_ref, bias_ref, weights_any, up_any, dn_any,
    gain_ref, shift_ref, hbias_ref,
    kv_ref, q_ref, mid_ref, log_ref, one_ref, slope_ref, two_ref, low_ref, act_ref, hslope_ref, feat_ref, *more,
    places, starts,
):
    copies = []
    if starts is None:
        up_ref, dn_ref, ctx_ref, w_ref, wo_ref, hb_ref, sems = more
        sources = zip(weights_any, (w_ref, wo_ref, hb_ref))
    else:
        w_out, wo_out, hb_out, up_ref, dn_ref, ctx_ref, w_ref, wo_ref, hb_ref, in_slab, hb_slab, sems = more
        sources = [
            (weights_any[0].at[:, pl.ds(start, slab.shape[1]), :], slab)
            for start, slab in zip(starts, (in_slab, hb_slab))
        ]
    for source, target in sources:
        copies.append((source, target))
    early = len(copies)
    for source, target, place in ((up_any, up_ref, places[0]), (dn_any, dn_ref, places[1])):
        each = target.shape[1]
        copies.append((source.at[:, pl.ds(place * each, each), :], target))
    copies = [pltpu.make_async_copy(*ends, sems.at[k]) for k, ends in enumerate(copies)]
    for copy in copies:
        copy.start()
    for copy in copies[:early]:
        copy.wait()
    copies = copies[early:]
    if starts is not None:
        unpack_rows(in_slab, (w_ref, wo_ref))
        unpack_rows(hb_slab, (hb_ref,))
        for k, ends in enumerate(((w_ref, w_out), (wo_ref, wo_out), (hb_ref, hb_out))):
            copies.append(pltpu.make_async_copy(*ends, sems.at[4 + k]))
            copies[-1].start()
    rows, hidden = x_ref.shape
    labels = place_ref.shape[0]
    lanes = 2 * (hidden // HEADS)
    width = lanes // 2
    low = x_ref[...].astype(BF)
    mid = mm(low, down_ref[1]).astype(BF)
    mid_ref[...] = mid
    step = split_of(hidden, 768, 128)
    for start in range(hidden, 3 * hidden, step):
        part = slice(start, start + step)
        kv_ref[:, start - hidden : start - hidden + step] = (
            mm_nt(low, w_ref[part, :]) + mm(mid, adapt_ref[1, :, part]) + qkv_bias(bias_ref, 1, start, step)
        ).astype(BF)
    choose = (
        lax.broadcasted_iota(jnp.int32, (labels, rows), 1) == place_ref[...][:, 0:1]
    ).astype(F32).astype(BF)
    own = exact_rows(choose, x_ref[...])
    own_low = own.astype(BF)
    own_mid = mm(choose, mid).astype(BF)
    q_ref[...] = (
        mm_nt(own_low, w_ref[:hidden, :])
        + mm(own_mid, adapt_ref[1, :, :hidden])
        + qkv_bias(bias_ref, 1, 0, hidden)
    ).astype(BF)
    seg = seg_ref[...]
    seg_own = jnp.sum(
        jnp.where(
            lax.broadcasted_iota(jnp.int32, (rows, labels), 0) == place_row_ref[...], seg, 0.0
        ),
        0,
        keepdims=True,
    )
    same = seg == seg_own
    for p in range(hidden // lanes):
        part = slice(p * lanes, (p + 1) * lanes)
        queries = pair_rows(q_ref[:, part].astype(F32) * width**-0.5, width)
        scores = masked(mm_nt(kv_ref[:, part], queries), same)
        top = jnp.max(scores, 0, keepdims=True)
        weights = jnp.exp(scores - top)
        total = jnp.sum(weights, 0, keepdims=True)
        context = mm_tn(
            kv_ref[:, hidden + p * lanes : hidden + (p + 1) * lanes], weights.astype(BF)
        ) * (1.0 / total)
        ctx_ref[:, part] = pair_join(context, width).T.astype(BF)
        log_ref[p : p + 1, :] = top + jnp.log(total)
    bo, b1, b2 = later_biases(bias_ref, 1)
    norms = (gain_ref, shift_ref)
    one = own + (mm_nt(ctx_ref[...], wo_ref[...]) + bo)
    one_ref[...] = one
    middle = layer_norm(one, *norm_of(norms, 3))
    middle_low = middle.astype(BF)
    sum_two = middle + b2
    units, step = feed_step(up_ref)
    for copy in copies:
        copy.wait()
    for start in range(0, units, step):
        part = slice(start, start + step)
        act, slope = gelu_pair(mm_nt(middle_low, rows_of(up_ref, start, step)) + b1[:, part])
        slope_ref[:, part] = slope.astype(BF)
        sum_two = sum_two + mm(act.astype(BF), rows_of(dn_ref, start, step))
    two_ref[...] = sum_two
    out_low = layer_norm(sum_two, *norm_of(norms, 4)).astype(BF)
    low_ref[...] = out_low
    act, slope = gelu_pair(mm(out_low, hb_ref[...]) + hbias_ref[...])
    act_ref[...] = act
    hslope_ref[...] = slope
    feat_ref[...] = layer_norm(act, *norm_of(norms, 5)).astype(BF)


def slab_scratch(slab):
    array, place, rows = slab
    return pltpu.VMEM((array.shape[0], rows, array.shape[2]), BF)


def last_forward(
    x, place_col, place_row, seg_wide, down, adapt, bias, weights, starts, up, dn, gains, shifts, hbias
):
    rows, hidden = x.shape
    labels = place_col.shape[0]
    units = 4 * hidden
    whole = pl.BlockSpec(memory_space=pltpu.VMEM)
    anywhere = pl.BlockSpec(memory_space=pl.ANY)
    shape = jax.ShapeDtypeStruct
    pairs = HEADS // 2
    matrices = [(3 * hidden, hidden), (hidden, hidden), (hidden, hidden)]
    slabs = []
    if starts is not None:
        shards = weights[0].shape[0]
        slabs = [
            pltpu.VMEM((shards, 4 * hidden // shards, hidden), BF),
            pltpu.VMEM((shards, weights[0].shape[1] - starts[1], hidden), BF),
        ]

    def body(*refs):
        head, rest = refs[:7], refs[7:]
        return last_forward_body(
            *head, rest[: len(weights)], *rest[len(weights) :], places=(up[1], dn[1]), starts=starts
        )

    return pl.pallas_call(
        body,
        in_specs=[whole] * 7 + [anywhere] * (len(weights) + 2) + [whole] * 3,
        out_specs=[whole] * 11 + ([anywhere] * 3 if slabs else []),
        out_shape=[
            shape((rows, 2 * hidden), BF),
            shape((labels, hidden), BF),
            shape((rows, down.shape[2]), BF),
            shape((pairs, 2 * labels), F32),
            shape((labels, hidden), F32),
            shape((labels, units), BF),
            shape((labels, hidden), F32),
            shape((labels, hidden), BF),
            shape((labels, hidden), F32),
            shape((labels, hidden), F32),
            shape((labels, hidden), BF),
        ]
        + ([shape(m, BF) for m in matrices] if slabs else []),
        scratch_shapes=[
            slab_scratch(up),
            slab_scratch(dn),
            pltpu.VMEM((labels, hidden), BF),
            *[pltpu.VMEM(m, BF) for m in matrices],
            *slabs,
            pltpu.SemaphoreType.DMA((7,)),
        ],
        compiler_params=params(),
        name="last_forward",
    )(x, place_col, place_row, seg_wide, down, adapt, bias, *weights, up[0], dn[0], gains, shifts, hbias)


def vocab_body(u_ref, e_ref, et_ref, bias_ref, num_ref, log_ref, scores, weights):
    count = e_ref.shape[0]
    step = split_of(count, 640, 16)
    u = u_ref[...]
    rows = u.shape[0]
    labels = num_ref.shape[2]
    top = jnp.full((1, rows), -jnp.inf, F32)
    for start in range(0, count, step):
        part = slice(start, start + step)
        bias = bias_ref[part, :]
        logits = mm_nt(e_ref[part, :], u) + jnp.concatenate([bias] * (rows // bias.shape[1]), 1)
        scores[part, :] = logits
        top = jnp.maximum(top, jnp.max(logits, 0, keepdims=True))
    total = jnp.zeros((1, rows), F32)
    for start in range(0, count, step):
        part = slice(start, start + step)
        grown = jnp.exp(scores[part, :] - top)
        total = total + jnp.sum(grown, 0, keepdims=True)
        weights[part, :] = grown.astype(BF)
    mean = mm(et_ref[...], weights[...]) * (1.0 / total)
    logs = top + jnp.log(total)
    for k in range(rows // labels):
        num_ref[k, :, :] = mean[:, k * labels : (k + 1) * labels]
        log_ref[k, :, :] = logs[:, k * labels : (k + 1) * labels]


def vocab(u, e, et, bias_wide, labels):
    rows, hidden = u.shape
    count = e.shape[0]
    tile = 2 * labels
    return pl.pallas_call(
        vocab_body,
        grid=(rows // tile,),
        in_specs=[
            pl.BlockSpec((tile, hidden), lambda i: (i, 0)),
            full(e.shape),
            full(et.shape),
            full(bias_wide.shape),
        ],
        out_specs=[
            pl.BlockSpec((2, hidden, labels), lambda i: (i, 0, 0)),
            pl.BlockSpec((2, 1, labels), lambda i: (i, 0, 0)),
        ],
        out_shape=[
            jax.ShapeDtypeStruct((rows // labels, hidden, labels), F32),
            jax.ShapeDtypeStruct((rows // labels, 1, labels), F32),
        ],
        scratch_shapes=[pltpu.VMEM((count, tile), F32), pltpu.VMEM((count, tile), BF)],
        compiler_params=params(),
        name="vocab",
    )(u, e, et, bias_wide)


def last_backward_body(
    mean_ref, all_log_ref, target_ref, fact_ref, kv_ref, q_ref, mid_ref, log_ref, one_ref, slope_ref, two_ref,
    low_ref, act_ref, hslope_ref, feat_ref, place_ref, place_row_ref, seg_ref, down_ref, w_ref, adapt_ref, wo_ref,
    up_any, dn_any, gain_ref, hb_ref,
    dx_ref, gh_ref, g_ref, out_fact_ref,
    up_ref, dn_ref, dkv_ref, dq_ref, sems, *, places, edge,
):
    copies = []
    for k, (source, target, place) in enumerate(
        ((up_any, up_ref, places[0]), (dn_any, dn_ref, places[1]))
    ):
        rows = target.shape[1]
        copies.append(
            pltpu.make_async_copy(
                source.at[:, pl.ds(place * rows, rows), :], target, sems.at[k]
            )
        )
        copies[-1].start()
    rows = kv_ref.shape[0]
    labels, hidden = feat_ref.shape
    lanes = 2 * (hidden // HEADS)
    width = lanes // 2
    scale = width**-0.5
    targets = target_ref[...].astype(F32)
    weight = fact_ref[0:1, 0:1]
    chosen = jnp.sum(feat_ref[...].astype(F32) * targets, keepdims=True)
    loss = weight * (jnp.sum(all_log_ref[...] - fact_ref[3:4, :labels], keepdims=True) - chosen)
    out_fact_ref[...] = jnp.where(
        lax.broadcasted_iota(jnp.int32, fact_ref.shape, 0) == 0, loss, fact_ref[...]
    )
    du = weight * (mean_ref[...].T - targets)
    dact = norm_back(act_ref[...], gain_ref[5:6, :], du)
    dz = (hslope_ref[...] * dact).astype(BF)
    dense = mm_tn(low_ref[...], dz)
    if len(gh_ref.shape) == 2:
        gh_ref[...] = dense
    else:
        each = hidden // gh_ref.shape[0]
        spare = jnp.zeros((gh_ref.shape[1] - each, hidden), F32)
        for k in range(gh_ref.shape[0]):
            gh_ref[k] = jnp.concatenate([dense[k * each : (k + 1) * each, :], spare], 0).astype(BF)
    dtwo = norm_back(two_ref[...], gain_ref[4:5, :], mm_nt(dz, hb_ref[...]))
    dtwo_low = dtwo.astype(BF)
    dmiddle = dtwo
    units, step = feed_step(up_ref)
    for copy in copies:
        copy.wait()
    for start in range(0, units, step):
        part = slice(start, start + step)
        dgate = (
            slope_ref[:, part].astype(F32) * mm_nt(dtwo_low, rows_of(dn_ref, start, step))
        ).astype(BF)
        dmiddle = dmiddle + mm(dgate, rows_of(up_ref, start, step))
    done = norm_back(one_ref[...], gain_ref[3:4, :], dmiddle)
    dctx = mm(done.astype(BF), wo_ref[...]).astype(BF)
    seg = seg_ref[...]
    choose_t = lax.broadcasted_iota(jnp.int32, (rows, labels), 0) == place_row_ref[...]
    same = seg == jnp.sum(jnp.where(choose_t, seg, 0.0), 0, keepdims=True)
    for p in range(hidden // lanes):
        part = slice(p * lanes, (p + 1) * lanes)
        later = slice(hidden + p * lanes, hidden + (p + 1) * lanes)
        queries = pair_rows(q_ref[:, part].astype(F32) * scale, width)
        outs = pair_rows(dctx[:, part].astype(F32), width)
        keys = kv_ref[:, part]
        weights = jnp.exp(masked(mm_nt(keys, queries), same) - log_ref[p : p + 1, :])
        dweights = mm_nt(kv_ref[:, later], outs)
        inner = jnp.sum(dweights * weights, 0, keepdims=True)
        dscores = (weights * (dweights - inner)).astype(BF)
        dkv_ref[:, part] = mm(dscores, queries).astype(BF)
        dkv_ref[:, later] = mm(weights.astype(BF), outs).astype(BF)
        dq_ref[:, part] = (pair_join(mm_tn(keys, dscores), width) * scale).T.astype(BF)
    dq = dq_ref[...]
    own_mid = mm(
        (lax.broadcasted_iota(jnp.int32, (labels, rows), 1) == place_ref[...][:, 0:1]).astype(F32).astype(BF),
        mid_ref[...],
    ).astype(BF)
    g_ref[...] = adapter_scale * jnp.where(
        lax.broadcasted_iota(jnp.int32, g_ref.shape, 1) < edge,
        mm_tn(dq, own_mid),
        mm_tn(dkv_ref[:, hidden:], mid_ref[...]),
    )
    dmid_own = mm_nt(dq, adapt_ref[1, :, :hidden]).astype(BF)
    own = done + mm(dq, w_ref[:hidden, :]) + mm_nt(dmid_own, down_ref[1])
    spread = choose_t.astype(F32).astype(BF)
    own_high = own.astype(BF)
    own_rest = (own - own_high.astype(F32)).astype(BF)
    dmid = mm_nt(dkv_ref[:, hidden:], adapt_ref[1, :, 2 * hidden :]).astype(BF)
    step = split_of(hidden, 256, 128)
    for start in range(0, hidden, step):
        part = slice(start, start + step)
        dx_ref[:, part] = (
            mm(dkv_ref[...], w_ref[hidden:, part])
            + mm_nt(dmid, down_ref[1, part, :])
            + mm(spread, own_high[:, part])
            + mm(spread, own_rest[:, part])
        )


def last_backward(
    mean, logs, targets, facts, saved, place_col, place_row, seg_wide, down, w, adapt, wo, up, dn, gains, hb, edge, shards
):
    kv = saved[0]
    rows = kv.shape[0]
    labels, hidden = targets.shape
    whole = pl.BlockSpec(memory_space=pltpu.VMEM)
    anywhere = pl.BlockSpec(memory_space=pl.ANY)
    shape = jax.ShapeDtypeStruct
    return pl.pallas_call(
        functools.partial(last_backward_body, places=(up[1], dn[1]), edge=edge),
        in_specs=[whole] * 22 + [anywhere] * 2 + [whole] * 2,
        out_specs=[whole] * 4,
        out_shape=[
            shape((rows, hidden), F32),
            shape((hidden, hidden), F32)
            if shards is None
            else shape((shards, -(-hidden // shards // 16) * 16, hidden), BF),
            shape((hidden, down.shape[2]), F32),
            shape(facts.shape, F32),
        ],
        scratch_shapes=[
            slab_scratch(up),
            slab_scratch(dn),
            pltpu.VMEM(kv.shape, BF),
            pltpu.VMEM((labels, hidden), BF),
            pltpu.SemaphoreType.DMA((2,)),
        ],
        compiler_params=params(),
        name="last_backward",
    )(mean, logs, targets, facts, *saved, place_col, place_row, seg_wide, down, w, adapt, wo, up[0], dn[0], gains, hb)


def after_back_body(dout_ref, one_ref, two_ref, slope_ref, wo_ref, up_ref, down_ref, gain_ref, dctx_ref):
    dtwo = norm_back(two_ref[...], gain_ref[2:3, :], dout_ref[...])
    low = dtwo.astype(BF)
    dmiddle = dtwo
    units, step = feed_step(up_ref)
    for start in range(0, units, step):
        part = slice(start, start + step)
        dgate = (
            slope_ref[:, part].astype(F32) * mm_nt(low, rows_of(down_ref, start, step))
        ).astype(BF)
        dmiddle = dmiddle + mm(dgate, rows_of(up_ref, start, step))
    done = norm_back(one_ref[...], gain_ref[1:2, :], dmiddle)
    dctx_ref[...] = mm(done.astype(BF), wo_ref[...]).astype(BF)


def after_back(dout, one, two, slope, wo, up, down, norms):
    rows, width = dout.shape
    tile = split_of(rows, 256, 16)
    row = lambda n: pl.BlockSpec((tile, n), lambda i: (i, 0))
    return pl.pallas_call(
        after_back_body,
        grid=(rows // tile,),
        in_specs=[row(width), row(width), row(width), row(slope.shape[1]), full(wo.shape)]
        + [slab_spec(up), slab_spec(down), full(norms.shape)],
        out_specs=row(width),
        out_shape=jax.ShapeDtypeStruct((rows, width), BF),
        compiler_params=params(),
        name="after_back",
    )(dout, one, two, slope, wo, up[0], down[0], norms)


def attend_back_body(
    q_ref, k_ref, v_ref, dctx_ref, log_ref, seg_ref, seg_row_ref, mid_ref, g_ref, dv_ref, *, edge
):
    rows = q_ref.shape[0]
    width = q_ref.shape[1] // 2
    scale = width**-0.5
    dv_ref[...] = jnp.zeros_like(dv_ref)
    gq = jnp.zeros((2 * width, mid_ref.shape[1]), F32)
    for start in range(0, rows, REACH):
        own = slice(start, start + REACH)
        near = slice(max(0, start - REACH), min(rows, start + 2 * REACH))
        queries = pair_rows(q_ref[own, :].astype(F32) * scale, width)
        outs = pair_rows(dctx_ref[own, :].astype(F32), width)
        same = seg_ref[near, :] == seg_row_ref[:, own]
        keys = k_ref[near, :]
        logs = log_ref[0, :, 2 * start : 2 * start + 2 * REACH]
        weights = jnp.exp(masked(mm_nt(keys, queries), same) - logs)
        dweights = mm_nt(v_ref[near, :], outs)
        inner = jnp.sum(dweights * weights, 0, keepdims=True)
        dscores = (weights * (dweights - inner)).astype(BF)
        dv_ref[near, :] += mm(weights.astype(BF), outs)
        dq = (pair_join(mm_tn(keys, dscores), width) * scale).astype(BF)
        gq = gq + mm(dq, mid_ref[own, :])
    gv = mm_tn(dv_ref[...].astype(BF), mid_ref[...])
    g_ref[...] = adapter_scale * jnp.where(
        lax.broadcasted_iota(jnp.int32, gq.shape, 1) < edge, gq, gv
    )


def attend_back(qkv, dctx, logs, seg_wide, seg_row, mid, edge):
    rows, total = qkv.shape
    hidden = total // 3
    lanes = 2 * (hidden // HEADS)
    pairs = hidden // lanes
    column = lambda kind: pl.BlockSpec((rows, lanes), lambda p: (0, kind * pairs + p))
    return pl.pallas_call(
        functools.partial(attend_back_body, edge=edge),
        grid=(pairs,),
        in_specs=[
            column(0),
            column(1),
            column(2),
            column(0),
            pl.BlockSpec((1, 1, 2 * rows), lambda p: (p, 0, 0)),
            full(seg_wide.shape),
            full(seg_row.shape),
            full(mid.shape),
        ],
        out_specs=pl.BlockSpec((lanes, mid.shape[1]), lambda p: (p, 0)),
        out_shape=jax.ShapeDtypeStruct((hidden, mid.shape[1]), F32),
        scratch_shapes=[pltpu.VMEM((rows, lanes), F32)],
        compiler_params=params(),
        name="attend_back",
    )(qkv, qkv, qkv, dctx, logs, seg_wide, seg_row, mid)


MESH = pl.DeviceIdType.MESH


def position():
    dp, fsdp = lax.axis_index("dp"), lax.axis_index("fsdp")
    return {"x": dp, "z": fsdp // 4, "y": (fsdp // 2) % 2, "c": fsdp % 2}


def device_of(place):
    return (place["x"], (place["z"] * 2 + place["y"]) * 2 + place["c"])


def number_of(place):
    return place["x"] * 16 + (place["z"] * 2 + place["y"]) * 2 + place["c"]


def rank_device(number):
    return (number // 16, number % 16)


def greet_all(shards):
    barrier = pltpu.get_barrier_semaphore()
    me = lax.axis_index("dp") * 16 + lax.axis_index("fsdp")

    @pl.loop(1, shards)
    def _(k):
        pl.semaphore_signal(
            barrier, inc=1, device_id=rank_device((me + k) % shards), device_id_type=MESH
        )


def await_all(shards):
    pl.semaphore_wait(pltpu.get_barrier_semaphore(), shards - 1)


def direct_copy(source, target, sems, me, k, shards):
    return pltpu.make_async_remote_copy(
        src_ref=source,
        dst_ref=target,
        send_sem=sems.at[0],
        recv_sem=sems.at[1],
        device_id=rank_device((me + k) % shards),
        device_id_type=MESH,
    )


def spread(piece_of, buffer, sems, me, shards):
    @pl.loop(1, shards)
    def _(k):
        direct_copy(piece_of((me + k) % shards), buffer.at[me], sems, me, k, shards).start()


def collect(buffer, sems, me, shards):
    whole = buffer.at[pl.ds(0, shards - 1)]
    copy = direct_copy(whole, whole, sems, me, 1, shards)
    copy.wait_recv()
    copy.wait_send()


def relative_places(order):
    places = [
        {"x": dx, "z": dz, "y": dy} for dx in (0, 1) for dz in range(-3, 4) for dy in (0, 1)
    ]
    size = lambda p: abs(p["x"]) + abs(p["z"]) + abs(p["y"])
    return sorted(places, key=lambda p: (abs(p[order[-1]]), size(p), [abs(p[a]) for a in order]))


class Gather:
    def __init__(self, chunk, full_buffer, start, rows, order, sends, receives, hands, hands_got):
        self.chunk, self.full, self.order = chunk, full_buffer, order
        self.part = pl.ds(start, rows)
        self.sends, self.receives, self.hands, self.hands_got = sends, receives, hands, hands_got
        self.here = position()
        self.items = relative_places(order)
        self.pending = []

    def origin(self, item):
        here = self.here
        return {"x": (here["x"] + item["x"]) % 2, "z": here["z"] - item["z"], "y": (here["y"] + item["y"]) % 2, "c": here["c"]}

    def key(self, place):
        return (place["x"] * 4 + place["z"]) * 2 + place["y"]

    def outward(self, item):
        deepest = max([k for k, axis in enumerate(self.order) if item[axis]], default=-1)
        ways = []
        if deepest >= 0 and self.order[deepest] == "z":
            ways.append(("z", 1 if item["z"] > 0 else -1))
        for axis in self.order[deepest + 1 :]:
            ways += [("z", 1), ("z", -1)] if axis == "z" else [(axis, 1)]
        return ways

    def copy(self, index, way, slot, item):
        here = self.here
        place = self.origin(item)
        number, key = number_of(place), self.key(place)
        mine = not any(item.values())
        source = self.chunk.at[self.part, :] if mine else self.full.at[number, self.part, :]
        if way is None:
            target = dict(here, c=1 - here["c"])
            sends, receives = self.hands.at[index], self.hands_got.at[key]
        else:
            axis, step = way
            target = dict(here)
            target[axis] = here["z"] + step if axis == "z" else 1 - here[axis]
            sends, receives = self.sends.at[index * 4 + slot], self.receives.at[key]
        return pltpu.make_async_remote_copy(
            src_ref=source,
            dst_ref=self.full.at[number, self.part, :],
            send_sem=sends,
            recv_sem=receives,
            device_id=device_of(target),
            device_id_type=MESH,
        )

    def valid(self, item):
        z = self.here["z"] - item["z"]
        return (z >= 0) & (z <= 3)

    def step(self, index):
        item = self.items[index]

        @pl.when(self.valid(item))
        def _():
            if any(item.values()):
                self.arrived(index, item)
            for slot, way in enumerate(self.outward(item)):
                self.when_way(way, lambda way=way, slot=slot: self.copy(index, way, slot, item).start())
            self.copy(index, None, 0, item).start()

    def when_way(self, way, act):
        axis, step = way
        if axis == "z":
            z = self.here["z"] + step
            pl.when((z >= 0) & (z <= 3))(act)
        else:
            act()

    def arrived(self, index, item):
        place = self.origin(item)
        spot = self.full.at[number_of(place), self.part, :]
        pltpu.make_async_remote_copy(
            src_ref=spot,
            dst_ref=spot,
            send_sem=self.sends.at[index * 4],
            recv_sem=self.receives.at[self.key(place)],
            device_id=device_of(dict(self.here, c=1 - self.here["c"])),
            device_id_type=MESH,
        ).wait_recv()

    def finish(self):
        for index, item in enumerate(self.items):

            @pl.when(self.valid(item))
            def _(index=index, item=item):
                for slot, way in enumerate(self.outward(item)):
                    self.when_way(way, lambda way=way, slot=slot: self.copy(index, way, slot, item).wait_send())
                self.copy(index, None, 0, item).wait_send()
                place = dict(self.origin(item), c=1 - self.here["c"])
                spot = self.full.at[number_of(place), self.part, :]
                pltpu.make_async_remote_copy(
                    src_ref=spot,
                    dst_ref=spot,
                    send_sem=self.hands.at[index],
                    recv_sem=self.hands_got.at[self.key(place)],
                    device_id=device_of(dict(self.here, c=1 - self.here["c"])),
                    device_id_type=MESH,
                ).wait_recv()


ITEMS = 28


def start_body(
    streams, shards, rows, fact, chunk, table_any, got, facts, full_chunk, et_out, e_ref, et_ref,
    row_sems, fact_sems, own_sems, sends, receives, hands, hands_got,
):
    here = position()
    me = number_of(here)
    own = [
        pltpu.make_async_copy(source, target, own_sems.at[k])
        for k, (source, target) in enumerate(
            ((vocab_rows(table_any, e_ref), e_ref), (fact, facts.at[me]), (chunk, full_chunk.at[me]))
        )
    ]
    for copy in own:
        copy.start()
    greet_all(shards)
    await_all(shards)
    gathers = [
        Gather(
            chunk, full_chunk, start, size, order, sends.at[k], receives.at[k], hands.at[k], hands_got.at[k]
        )
        for k, (start, size, order) in enumerate(streams)
    ]
    swap = pltpu.make_async_remote_copy(
        src_ref=rows,
        dst_ref=got,
        send_sem=row_sems.at[0],
        recv_sem=row_sems.at[1],
        device_id=device_of(dict(here, x=1 - here["x"])),
        device_id_type=MESH,
    )
    for gather in gathers:
        gather.step(0)
    swap.start()
    spread(lambda peer: fact, facts, fact_sems, me, shards)
    own[0].wait()
    blocks = e_ref.shape[0] // 128
    each = -(-blocks // (ITEMS - 1))
    for index in range(1, ITEMS):
        for k in range((index - 1) * each, min(index * each, blocks)):
            part = slice(k * 128, (k + 1) * 128)
            et_ref[:, part] = e_ref[part, :].astype(F32).T.astype(BF)
        for gather in gathers:
            gather.step(index)
    turned = pltpu.make_async_copy(et_ref, et_out, own_sems.at[3])
    turned.start()
    for gather in gathers:
        gather.finish()
    collect(facts, fact_sems, me, shards)
    swap.wait()
    for copy in own[1:] + [turned]:
        copy.wait()


def vocab_rows(table, like):
    here = position()
    count = like.shape[0]
    return table.at[pl.ds(pl.multiple_of((here["y"] * 2 + here["c"]) * count, 16), count), :]


def gather_sems(streams):
    sems = pltpu.SemaphoreType.DMA
    count = len(streams)
    return [sems((count, 4 * ITEMS)), sems((count, 16)), sems((count, ITEMS)), sems((count, 16))]


def streams_of(rows, parts):
    streams, start = [], 0
    for k, (order, share) in enumerate(parts):
        size = rows - start if k == len(parts) - 1 else round(rows * share / 16) * 16
        streams.append((start, size, order))
        start += size
    return streams


def start_exchange(rows, fact, chunk, table, shards):
    anywhere = pl.BlockSpec(memory_space=pl.ANY)
    shape = jax.ShapeDtypeStruct
    sems = pltpu.SemaphoreType.DMA
    streams = streams_of(chunk.shape[0], (("xzy", 5 / 6), ("xyz", 1 / 6)))
    count, hidden = table.shape[0] // 4, table.shape[1]
    return pl.pallas_call(
        functools.partial(start_body, streams, shards),
        in_specs=[anywhere] * 4,
        out_specs=[anywhere] * 4,
        out_shape=[
            shape(rows.shape, rows.dtype),
            shape((shards, *fact.shape), fact.dtype),
            shape((shards, *chunk.shape), chunk.dtype),
            shape((hidden, count), BF),
        ],
        scratch_shapes=[
            pltpu.VMEM((count, hidden), BF),
            pltpu.VMEM((hidden, count), BF),
            sems((2,)),
            sems((2,)),
            sems((4,)),
            *gather_sems(streams),
        ],
        compiler_params=params(collective_id=1, has_side_effects=True),
        name="start_exchange",
    )(rows, fact, chunk, table)


def first_layer_body(
    streams, shards,
    own_any, got_any, in_any, feed_any, chunk, code_ref, spots_ref, gain_ref, shift_ref, down_ref,
    adapt_ref, bias_ref, seg_ref, seg_row_ref,
    qkv_out, x_out, one_out, two_out, slope_out, wo_out, full_chunk, mid_ref, log_ref,
    own, got, in_slab, w, wo, up, dn, x, qkv, ctx, two, out, slope,
    load_sems, tile_sems, out_sems, sends, receives, hands, hands_got,
):
    here = position()
    me = number_of(here)
    rows, hidden = x.shape
    tile = split_of(rows, 256, 16)
    tiles = rows // tile
    lanes = 2 * (hidden // HEADS)
    pairs = hidden // lanes

    def slab(source, target, start):
        return source.at[:, pl.ds(start, target.shape[1]), :]

    loads = [
        pltpu.make_async_copy(source, target, load_sems.at[k])
        for k, (source, target) in enumerate(
            (
                (own_any.at[pl.ds(0, rows), :], own),
                (got_any.at[pl.ds(0, rows), :], got),
                (slab(in_any, in_slab, up.shape[1]), in_slab),
                (slab(in_any, up, 0), up),
                (slab(feed_any, dn, 0), dn),
                (chunk, full_chunk.at[me]),
            )
        )
    ]
    for copy in loads:
        copy.start()
    barrier = pltpu.get_barrier_semaphore()
    peers = [
        dict(here, c=1 - here["c"]),
        dict(here, x=1 - here["x"]),
        dict(here, y=1 - here["y"]),
        *[dict(here, z=flip(here["z"], k)) for k in (1, 2, 3)],
    ]
    for peer in peers:
        pl.semaphore_signal(barrier, inc=1, device_id=device_of(peer), device_id_type=MESH)
    pl.semaphore_wait(barrier, len(peers))
    gathers = [
        Gather(
            chunk, full_chunk, start, size, order, sends.at[k], receives.at[k], hands.at[k], hands_got.at[k]
        )
        for k, (start, size, order) in enumerate(streams)
    ]
    def advance(first, last):
        for index in range(first, last + 1):
            for gather in gathers:
                gather.step(index)

    advance(0, 0)
    for copy in loads[:3]:
        copy.wait()
    unpack_rows(in_slab, (w, wo))

    @pl.loop(0, tiles)
    def _(i):
        part = pl.ds(pl.multiple_of(i * tile, tile), tile)
        project_body(
            own.at[part, :], got.at[part, :], code_ref.at[part, :], spots_ref, gain_ref, shift_ref, down_ref, w,
            adapt_ref, bias_ref, qkv.at[part, :], mid_ref.at[part, :], x.at[part, :],
        )

        @pl.when(i == tiles - 3)
        def _():
            advance(1, 3)

        @pl.when(i == tiles - 1)
        def _():
            advance(4, 5)

    early = [
        pltpu.make_async_copy(qkv, qkv_out, out_sems.at[0]),
        pltpu.make_async_copy(wo, wo_out, out_sems.at[1]),
    ]
    for copy in early:
        copy.start()

    @pl.loop(0, pairs)
    def _(p):
        column = lambda kind: pl.ds(pl.multiple_of((kind * pairs + p) * lanes, lanes), lanes)
        attend_body(
            qkv.at[:, column(0)], qkv.at[:, column(1)], qkv.at[:, column(2)], seg_ref, seg_row_ref,
            ctx.at[:, column(0)], log_ref.at[pl.ds(p, 1)],
        )

        for k, (first, last) in {1: (6, 7), 3: (8, 9), 5: (10, 13)}.items():
            pl.when(p == pairs - 6 + k)(functools.partial(advance, first, last))

    for copy in loads[3:5]:
        copy.wait()

    def tile_copies(i):
        part = pl.ds(pl.multiple_of(i * tile, tile), tile)
        turn = i % 2
        return [
            pltpu.make_async_copy(source, target.at[part, :], tile_sems.at[k, i])
            for k, (source, target) in enumerate(
                (
                    (out.at[turn], x_out),
                    (two.at[turn], two_out),
                    (slope.at[turn], slope_out),
                    (x.at[part, :], one_out),
                )
            )
        ]

    plan = {tiles - 4: (14, 16), tiles - 3: (17, 19), tiles - 2: (20, 23), tiles - 1: (24, 27)}

    @pl.loop(0, tiles)
    def _(i):
        part = pl.ds(pl.multiple_of(i * tile, tile), tile)
        turn = i % 2

        @pl.when(i >= 2)
        def _():
            for copy in tile_copies(i - 2):
                copy.wait()

        after_body(
            ctx.at[part, :], x.at[part, :], wo, up, dn, bias_ref, gain_ref, shift_ref, out.at[turn],
            x.at[part, :], two.at[turn], slope.at[turn],
        )
        for copy in tile_copies(i):
            copy.start()
        for k, (first, last) in plan.items():
            pl.when(i == k)(functools.partial(advance, first, last))

    for gather in gathers:
        gather.finish()
    for i in (tiles - 2, tiles - 1):
        for copy in tile_copies(i):
            copy.wait()
    for copy in early + loads[5:]:
        copy.wait()


def first_layer(own, got, first_in, feed, chunk, more, shards):
    whole = pl.BlockSpec(memory_space=pltpu.VMEM)
    anywhere = pl.BlockSpec(memory_space=pl.ANY)
    code, down = more[0], more[4]
    rows, hidden = code.shape[0], own.shape[1]
    tile = split_of(rows, 256, 16)
    pairs = HEADS // 2
    units = 4 * hidden
    each = units // shards
    shape = jax.ShapeDtypeStruct
    sems = pltpu.SemaphoreType.DMA
    streams = streams_of(chunk.shape[0], (("zxy", 0.4), ("zyx", 0.4), ("xyz", 0.2)))
    return pl.pallas_call(
        functools.partial(first_layer_body, streams, shards),
        in_specs=[anywhere] * 5 + [whole] * len(more),
        out_specs=[anywhere] * 7 + [whole] * 2,
        out_shape=[
            shape((rows, 3 * hidden), BF),
            shape((rows, hidden), F32),
            shape((rows, hidden), F32),
            shape((rows, hidden), F32),
            shape((rows, units), BF),
            shape((hidden, hidden), BF),
            shape((shards, *chunk.shape), BF),
            shape((rows, down.shape[2]), BF),
            shape((pairs, 1, 2 * rows), F32),
        ],
        scratch_shapes=[
            pltpu.VMEM((rows, hidden), BF),
            pltpu.VMEM((rows, hidden), BF),
            pltpu.VMEM((shards, 4 * hidden // shards, hidden), BF),
            pltpu.VMEM((3 * hidden, hidden), BF),
            pltpu.VMEM((hidden, hidden), BF),
            pltpu.VMEM((shards, each, hidden), BF),
            pltpu.VMEM((shards, each, hidden), BF),
            pltpu.VMEM((rows, hidden), F32),
            pltpu.VMEM((rows, 3 * hidden), BF),
            pltpu.VMEM((rows, hidden), BF),
            pltpu.VMEM((2, tile, hidden), F32),
            pltpu.VMEM((2, tile, hidden), F32),
            pltpu.VMEM((2, tile, units), BF),
            sems((6,)),
            sems((4, rows // tile)),
            sems((2,)),
            *gather_sems(streams),
        ],
        compiler_params=params(collective_id=3, has_side_effects=True),
        name="first_layer",
    )(own, got, first_in, feed, chunk, *more)


PICK = 64
GROUP = 16


def look_up_body(ids, low_ref, table, first_ref, second_ref, stage):
    batches = first_ref.shape[0] // PICK
    for k, out in enumerate((first_ref, second_ref)):

        @pl.loop(0, batches)
        def _(b, k=k, out=out):
            at = (k * batches + b) * PICK

            def one(t, carry):
                stage[t] = table[ids[at + t]]
                return carry

            lax.fori_loop(0, PICK, one, 0, unroll=8)
            choose = (
                lax.broadcasted_iota(jnp.int32, (PICK, PICK * GROUP), 1)
                == low_ref[pl.ds(pl.multiple_of(at, PICK), PICK), :]
            )
            out[pl.ds(pl.multiple_of(b * PICK, PICK), PICK), :] = mm(
                choose.astype(F32).astype(BF), flat(stage)
            ).astype(BF)


def look_up(ids, table):
    whole = pl.BlockSpec(memory_space=pltpu.VMEM)
    hidden = table.shape[1]
    low = jnp.arange(ids.size, dtype=jnp.int32) % PICK * GROUP + ids % GROUP
    return pl.pallas_call(
        look_up_body,
        in_specs=[pl.BlockSpec(memory_space=pltpu.SMEM), whole, whole],
        out_specs=[whole] * 2,
        out_shape=[jax.ShapeDtypeStruct((ids.size // 2, hidden), table.dtype)] * 2,
        scratch_shapes=[pltpu.VMEM((PICK, GROUP, hidden), table.dtype)],
        compiler_params=params(),
        name="look_up",
    )(ids // GROUP, low[:, None], table.reshape(-1, GROUP, hidden))


def adam(weight, gradient, moment_one, moment_two, fade_one, fade_two):
    moment_one = beta_first * moment_one + (1.0 - beta_first) * gradient
    moment_two = beta_second * moment_two + (1.0 - beta_second) * gradient * gradient
    one_hat = moment_one / fade_one
    two_hat = moment_two / fade_two
    weight = weight - learn_rate * (one_hat / (jnp.sqrt(two_hat) + adam_eps) + decay_rate * weight)
    return (weight, moment_one, moment_two)


BACK_TILE = 256


def finish_body(
    shards, edge,
    dout_any, one_any, two_any, slope_any, wo_any, up_any, dn_any, qkv_any, gain_ref, log_ref, seg_ref,
    seg_row_ref, mid_ref, parts, late_ref, facts,
    sums_ref, dense_ref, total_ref,
    dout, one, two, slope, wo, up, dn, qkv, dctx, dv, grad, core_got, chip_sum, dense_got, grad_got, note, notes,
    tile_sems, load_sems, core_sems, dense_sems, grad_sems, note_sems,
):
    rows, hidden = dout.shape
    tile = split_of(rows, BACK_TILE, 16)
    tiles = rows // tile
    me = number_of(position())

    def tile_loads(i):
        part = pl.ds(pl.multiple_of(i * tile, tile), tile)
        return [
            pltpu.make_async_copy(source.at[part, :], target.at[part, :], tile_sems.at[k, i])
            for k, (source, target) in enumerate(
                ((two_any, two), (dout_any, dout), (slope_any, slope), (one_any, one))
            )
        ]

    here = position()
    chips = shards // 2
    chip, core = me // 2, here["c"]
    to_core = pltpu.make_async_remote_copy(
        src_ref=parts.at[:, 1 - core],
        dst_ref=core_got,
        send_sem=core_sems.at[0],
        recv_sem=core_sems.at[1],
        device_id=device_of(dict(here, c=1 - core)),
        device_id_type=MESH,
    )

    def to_chip(k):
        peer = (chip + k) % chips
        return pltpu.make_async_remote_copy(
            src_ref=chip_sum.at[peer],
            dst_ref=dense_got.at[chip],
            send_sem=dense_sems.at[0],
            recv_sem=dense_sems.at[1],
            device_id=rank_device(2 * peer + core),
            device_id_type=MESH,
        )

    loads = [
        pltpu.make_async_copy(source, target, load_sems.at[k])
        for k, (source, target) in enumerate(
            (
                (dn_any.at[:, pl.ds(0, dn.shape[1]), :], dn),
                (up_any.at[:, pl.ds(0, up.shape[1]), :], up),
                (wo_any, wo),
                (qkv_any, qkv),
            )
        )
    ]
    for copy in tile_loads(0) + loads[:3]:
        copy.start()
    for i in range(1, tiles):
        for copy in tile_loads(i):
            copy.start()
    loads[3].start()
    greet_all(shards)
    for copy in loads[:3]:
        copy.wait()

    @pl.loop(0, tiles)
    def _(i):
        for copy in tile_loads(i):
            copy.wait()
        part = pl.ds(pl.multiple_of(i * tile, tile), tile)
        after_back_body(
            dout.at[part, :], one.at[part, :], two.at[part, :], slope.at[part, :], wo, up, dn, gain_ref,
            dctx.at[part, :],
        )

        @pl.when(i == 0)
        def _():
            await_all(shards)
            to_core.start()

        @pl.when(i == 1)
        def _():
            to_core.wait_recv()

            @pl.loop(0, chips)
            def _(k):
                chip_sum[k] = (parts[k, core].astype(F32) + core_got[k].astype(F32)).astype(BF)

            dense_got[chip] = chip_sum[chip]

            @pl.loop(1, chips)
            def _(k):
                to_chip(k).start()

    loads[3].wait()
    lanes = 2 * (hidden // HEADS)
    pairs = hidden // lanes

    @pl.loop(0, pairs)
    def _(p):
        column = lambda kind: pl.ds(pl.multiple_of((kind * pairs + p) * lanes, lanes), lanes)
        attend_back_body(
            qkv.at[:, column(0)], qkv.at[:, column(1)], qkv.at[:, column(2)], dctx.at[:, column(0)],
            log_ref.at[pl.ds(p, 1)], seg_ref, seg_row_ref, mid_ref, grad.at[column(0), :], dv, edge=edge,
        )

    grad[...] = grad[...] + late_ref[...]
    each = hidden // shards
    piece = lambda peer: grad.at[pl.ds(pl.multiple_of(peer * each, each), each), :]
    grad_got[me] = piece(me)[...]
    spread(piece, grad_got, grad_sems, me, shards)
    others = chip_sum.at[pl.ds(0, chips - 1)]
    every = pltpu.make_async_remote_copy(
        src_ref=others,
        dst_ref=dense_got.at[pl.ds(0, chips - 1)],
        send_sem=dense_sems.at[0],
        recv_sem=dense_sems.at[1],
        device_id=device_of(dict(here, c=1 - core)),
        device_id_type=MESH,
    )
    every.wait_recv()
    every.wait_send()
    to_core.wait_send()
    dense = jnp.zeros((each, hidden), F32)
    for k in range(chips):
        dense = dense + dense_got[k].astype(F32)[:each, :]
    dense_ref[...] = dense
    square = jnp.sum(dense * dense, keepdims=True)
    collect(grad_got, grad_sems, me, shards)
    total = grad_got[0]
    for k in range(1, shards):
        total = total + grad_got[k]
    total_ref[...] = total
    square = square + jnp.sum(total * total, keepdims=True)
    row = lax.broadcasted_iota(jnp.int32, note.shape, 0)
    note[...] = jnp.where(row == 0, facts[...], jnp.where(row == 1, square, 0.0))
    notes[me] = note[...]
    spread(lambda peer: note, notes, note_sems, me, shards)
    collect(notes, note_sems, me, shards)
    sums = notes[0]
    for k in range(1, shards):
        sums = sums + notes[k]
    sums_ref[...] = sums


def update_body(
    sums_ref, dense_ref, total_ref, facts, head_w, head_m, head_v, adapt_w, adapt_m, adapt_v,
    loss_out, norm_out, head_w_out, head_m_out, head_v_out, adapt_w_out, adapt_m_out, adapt_v_out,
):
    norm = jnp.sqrt(sums_ref[1:2, 0:1])
    loss_out[...] = sums_ref[0:1, 0:1]
    norm_out[...] = norm
    factor = jnp.minimum(1.0, clip_limit / (norm + 1e-06))
    fades = facts[1:2, 0:1], facts[2:3, 0:1]
    new = adam(head_w[...], dense_ref[...] * factor, head_m[...], head_v[...], *fades)
    head_w_out[...], head_m_out[...], head_v_out[...] = new
    grad = (total_ref[...] * factor).T
    layers, kinds, rank, unused = adapt_w.shape
    for layer in range(layers):
        for kind in range(kinds):
            at = (layer * kinds + kind) * rank
            new = adam(
                adapt_w[layer, kind], grad[at : at + rank], adapt_m[layer, kind], adapt_v[layer, kind], *fades
            )
            adapt_w_out[layer, kind], adapt_m_out[layer, kind], adapt_v_out[layer, kind] = new


def update(sums, dense, total, facts, heads, adapts):
    whole = pl.BlockSpec(memory_space=pltpu.VMEM)
    shape = jax.ShapeDtypeStruct
    return pl.pallas_call(
        update_body,
        in_specs=[whole] * 10,
        out_specs=[whole] * 8,
        out_shape=[shape((1, 1), F32)] * 2 + [shape(a.shape, F32) for a in (*heads, *adapts)],
        compiler_params=params(),
        name="update",
    )(sums, dense, total, facts, *heads, *adapts)


def finish(back, qkv, logs, seg_wide, seg_row, mid, parts, late, facts, edge, shards):
    dout, one, two, slope, wo, up, dn, gains = back
    parts = parts.reshape(-1, 2, *parts.shape[1:])
    rows, hidden = dout.shape
    each = hidden // shards
    whole = pl.BlockSpec(memory_space=pltpu.VMEM)
    anywhere = pl.BlockSpec(memory_space=pl.ANY)
    shape = jax.ShapeDtypeStruct
    sems = pltpu.SemaphoreType.DMA
    tiles = rows // split_of(rows, BACK_TILE, 16)
    return pl.pallas_call(
        functools.partial(finish_body, shards, edge),
        in_specs=[anywhere] * 8 + [whole] * 8,
        out_specs=[whole] * 3,
        out_shape=[
            shape((8, 128), F32),
            shape((each, hidden), F32),
            shape((each, late.shape[1]), F32),
        ],
        scratch_shapes=[
            pltpu.VMEM((rows, hidden), F32),
            pltpu.VMEM((rows, hidden), F32),
            pltpu.VMEM((rows, hidden), F32),
            pltpu.VMEM(slope.shape, BF),
            pltpu.VMEM(wo.shape, BF),
            slab_scratch(up),
            slab_scratch(dn),
            pltpu.VMEM(qkv.shape, BF),
            pltpu.VMEM((rows, hidden), BF),
            pltpu.VMEM((rows, 2 * (hidden // HEADS)), F32),
            pltpu.VMEM(late.shape, F32),
            pltpu.VMEM((shards // 2, *parts.shape[2:]), BF),
            pltpu.VMEM((shards // 2, *parts.shape[2:]), BF),
            pltpu.VMEM((shards // 2, *parts.shape[2:]), BF),
            pltpu.VMEM((shards, each, late.shape[1]), F32),
            pltpu.VMEM((8, 128), F32),
            pltpu.VMEM((shards, 8, 128), F32),
            sems((4, tiles)),
            sems((4,)),
            sems((2,)),
            sems((2,)),
            sems((2,)),
            sems((2,)),
        ],
        compiler_params=params(collective_id=2, has_side_effects=True),
        name="finish",
    )(dout, one, two, slope, wo, up[0], dn[0], qkv, gains, logs, seg_wide, seg_row, mid, parts, late, facts)


LOG_ROWS = 16


def flip(z, k):
    return (z % 2 + k % 2) % 2 + 2 * ((z // 2 + k // 2) % 2)


def pack_log(log_row, rows):
    high = log_row.astype(BF).astype(F32)
    middle = (log_row - high).astype(BF).astype(F32)
    low = log_row - high - middle
    row = lax.broadcasted_iota(jnp.int32, (rows, log_row.shape[1]), 0)
    return jnp.where(
        row == 0, high, jnp.where(row == 1, middle, jnp.where(row == 2, low, 0.0))
    ).astype(BF)


def unpack(block, hidden):
    logs = block[hidden : hidden + LOG_ROWS, :].astype(F32)
    return block[:hidden, :].astype(F32), jnp.sum(logs, 0, keepdims=True)


def merged(one, two):
    top = jnp.maximum(one[1], two[1])
    first, second = jnp.exp(one[1] - top), jnp.exp(two[1] - top)
    total = first + second
    inverse = 1.0 / total
    return one[0] * (first * inverse) + two[0] * (second * inverse), top + jnp.log(total)


def store_packed(ref, pair, hidden):
    ref[:hidden, :] = pair[0].astype(BF)
    ref[hidden : hidden + LOG_ROWS, :] = pack_log(pair[1], LOG_ROWS)


def head_body(
    u_ref, bias_ref, table_any, et_any, mean_ref, log_ref,
    e_ref, et_ref, bias_wide, feats, packs, handed, sums,
    loads, far_send, far_get, hand_send, hand_get, part_send, part_get, sum_send, sum_get,
):
    here = position()
    x, y, c = here["x"], here["y"], here["c"]
    labels, hidden = u_ref.shape
    sibling = device_of(dict(here, c=1 - c))

    def chip_at(k):
        return (x + k % 2) % 2, (y + k // 2) % 2

    def device_at(k):
        there = chip_at(k)
        return device_of(dict(here, x=there[0], y=there[1]))

    def slot(k, core):
        there = chip_at(k)
        return (there[0] * 2 + there[1]) * 2 + core

    fills = [
        pltpu.make_async_copy(source, target, loads.at[k])
        for k, (source, target) in enumerate(
            ((vocab_rows(table_any, e_ref), e_ref), (et_any, et_ref))
        )
    ]
    for fill in fills:
        fill.start()
    barrier = pltpu.get_barrier_semaphore()
    for target in (sibling, *[device_at(k) for k in (1, 2, 3)]):
        pl.semaphore_signal(barrier, inc=1, device_id=target, device_id_type=MESH)
    feats[slot(0, c)] = u_ref[...]
    pl.semaphore_wait(barrier, 4)

    def move(place, device, send, get):
        return pltpu.make_async_remote_copy(
            src_ref=feats.at[place],
            dst_ref=feats.at[place],
            send_sem=send,
            recv_sem=get,
            device_id=device,
            device_id_type=MESH,
        )

    def far(k):
        return move(slot(0, c), device_at(k), far_send.at[k], far_get.at[k])

    def far_here(k):
        return move(slot(k, c), device_at(k), far_send.at[k], far_get.at[k])

    def hand(k, core):
        return move(slot(k, core), sibling, hand_send.at[k], hand_get.at[k])

    for k in (1, 2, 3):
        far(k).start()
    hand(0, c).start()

    @pl.loop(0, bias_ref.shape[0])
    def _(b):
        row = jnp.broadcast_to(bias_ref[pl.ds(b, 1), :], (128, 128))
        bias_wide[pl.ds(pl.multiple_of(b * 128, 128), 128), :] = row.T

    for k in (1, 2, 3):
        far_here(k).wait_recv()
        hand(k, c).start()
    for fill in fills:
        fill.wait()
    count = e_ref.shape[0]
    steps = 4

    def target_of(s):
        return (s + 1) % steps

    def hand_part(s):
        return pltpu.make_async_remote_copy(
            src_ref=packs.at[s, 1 - c],
            dst_ref=handed.at[s],
            send_sem=part_send.at[s],
            recv_sem=part_get.at[s],
            device_id=sibling,
            device_id_type=MESH,
        )

    def sum_part(s):
        return pltpu.make_async_remote_copy(
            src_ref=packs.at[s, c],
            dst_ref=sums.at[s],
            send_sem=sum_send.at[s],
            recv_sem=sum_get.at[s],
            device_id=device_at(target_of(s)),
            device_id_type=MESH,
        )

    def together(s):
        hand_part(s).wait_recv()
        return merged(unpack(packs[s, c], hidden), unpack(handed[s], hidden))

    def settle(s):
        store_packed(packs.at[s, c], together(s), hidden)
        sum_part(s).start()

    @pl.loop(0, steps)
    def _(s):
        k = target_of(s)
        hand(k, 1 - c).wait_recv()
        u = feats[pl.ds(slot(k, 0), 2)].reshape(2 * labels, hidden)
        top = total = mean = None
        for start in range(0, count, 1280):
            if start == 1280:

                @pl.when(s > 0)
                def _():
                    settle(s - 1)

            part = slice(start, min(start + 1280, count))
            bias = bias_wide[part, :]
            logits = mm_nt(e_ref[part, :], u) + jnp.concatenate([bias, bias], 1)
            high = jnp.max(logits, 0, keepdims=True)
            new = high if top is None else jnp.maximum(top, high)
            grown = jnp.exp(logits - new)
            part_sums = jnp.sum(grown, 0, keepdims=True)
            product = mm(et_ref[:, part], grown.astype(BF))
            if top is None:
                total, mean = part_sums, product
            else:
                shrink = jnp.exp(top - new)
                total, mean = total * shrink + part_sums, mean * shrink + product
            top = new
        mean = mean * (1.0 / total)
        logs = top + jnp.log(total)
        for core in range(2):
            half = slice(core * labels, (core + 1) * labels)
            packs[s, core, :hidden, :] = mean[:, half].astype(BF)
            packs[s, core, hidden : hidden + LOG_ROWS, :] = pack_log(logs[:, half], LOG_ROWS)
        hand_part(s).start()

    total = together(steps - 1)
    for s in range(steps - 1):
        sum_part(s).wait_recv()
        total = merged(total, unpack(sums[s], hidden))
    mean_ref[...] = total[0]
    log_ref[...] = total[1]
    for k in (1, 2, 3):
        far(k).wait_send()
    for k in range(4):
        hand(k, c).wait_send()
    for s in range(steps):
        hand_part(s).wait_send()
    for s in range(steps - 1):
        sum_part(s).wait_send()


def head(u, bias, table, et):
    labels, hidden = u.shape
    whole = pl.BlockSpec(memory_space=pltpu.VMEM)
    anywhere = pl.BlockSpec(memory_space=pl.ANY)
    shape = jax.ShapeDtypeStruct
    sems = pltpu.SemaphoreType.DMA
    block = (hidden + LOG_ROWS, labels)
    count = et.shape[1]
    return pl.pallas_call(
        head_body,
        in_specs=[whole] * 2 + [anywhere] * 2,
        out_specs=[whole] * 2,
        out_shape=[shape((hidden, labels), F32), shape((1, labels), F32)],
        scratch_shapes=[
            pltpu.VMEM((count, hidden), BF),
            pltpu.VMEM((hidden, count), BF),
            pltpu.VMEM((count, 128), F32),
            pltpu.VMEM((8, labels, hidden), BF),
            pltpu.VMEM((4, 2, *block), BF),
            pltpu.VMEM((4, *block), BF),
            pltpu.VMEM((4, *block), BF),
            sems((2,)),
        ]
        + [sems((4,))] * 8,
        compiler_params=params(collective_id=4, has_side_effects=True),
        name="head",
    )(u, bias, table, et)


def seg_positions(segments):
    index = jnp.arange(segments.shape[-1], dtype=jnp.int32)
    fresh = jnp.concatenate([jnp.ones((1,), dtype=bool), segments[1:] != segments[:-1]], -1)
    starts = lax.cummax(jnp.where(fresh, index, jnp.zeros_like(index)), axis=0)
    return index - starts


def pad_rows(matrix, multiple):
    return jnp.pad(matrix, ((0, -matrix.shape[0] % multiple), (0, 0)))


def slab_of(gathered, start, rows):
    if rows % 16 == 0 and start % rows == 0:
        return (gathered, start // rows, rows)
    part = gathered[:, start : start + rows].reshape(1, -1, gathered.shape[2])
    return (part, 0, part.shape[1])


def per_device(
    input_token_index,
    sentence_numbers,
    label_positions,
    label_target_token,
    sequence_task_index,
    task_loss_weight,
    optimizer_step_count,
    embed,
    position_embedding,
    norm_gain_vector,
    norm_bias_vector,
    attention_in_weight,
    attention_out_weight,
    feedforward_up,
    feedforward_down,
    layer_bias_vector,
    head_dense_bias,
    vocabulary_bias,
    adapter_down_matrix,
    adapter_up_matrix,
    adapter_moment_first,
    adapter_moment_second,
    head_projection,
    head_moment_first,
    head_moment_second,
):
    shards = lax.axis_size("dp") * lax.axis_size("fsdp")
    dp_index = lax.axis_index("dp")
    fsdp_index = lax.axis_index("fsdp")
    layers, unused, rank, up_part = adapter_up_matrix.shape
    hidden = embed.shape[1]
    tokens = input_token_index.shape[1]
    labels = label_positions.shape[1]
    qkv_rows = attention_in_weight.shape[2]
    out_rows = attention_out_weight.shape[2]
    ff_rows = feedforward_up.shape[2]
    head_rows = head_projection.shape[0]

    grouped = (lax.axis_size("dp"), lax.axis_size("fsdp")) == (2, 16)
    feeds = [[feedforward_up[layer].T, feedforward_down[layer]] for layer in range(layers)]
    attends = [[attention_in_weight[layer].T, attention_out_weight[layer].T] for layer in range(layers)]
    first_in = lax.all_gather(
        jnp.concatenate([feeds[0][0], *attends[0]], 0), BOTH, axis=0, tiled=False
    )
    feed_chunk = feeds[0][1]
    last_chunk = pad_rows(
        jnp.concatenate(feeds[1] + attends[1] + [head_projection.astype(BF)], 0), 32
    )

    table_rows = embed.shape[0]
    wanted = jnp.concatenate([input_token_index[0], label_target_token[0]])
    dp_count = lax.axis_size("dp")
    group_ids = lax.all_gather(wanted, "dp", axis=0, tiled=False) - dp_index * table_rows
    inside = (group_ids >= 0) & (group_ids < table_rows)
    group_ids = jnp.clip(group_ids, 0, table_rows - 1)
    mine = lax.dynamic_index_in_dim(inside, dp_index, 0, keepdims=False)

    task_range = jnp.arange(TASKS, dtype=jnp.int32)
    slice_rows = vocabulary_bias.shape[0]
    ups = adapter_up_matrix.reshape(-1)
    if grouped:
        pair_ids = jnp.concatenate(
            [
                lax.dynamic_index_in_dim(group_ids, (dp_index + shift) % 2, 0, keepdims=False)
                for shift in (1, 0)
            ]
        )
        other_rows, own_rows = look_up(pair_ids, embed)
        fact = jnp.concatenate([vocabulary_bias, ups, sequence_task_index.astype(F32)])
        fact_rows = -(-fact.size // 1024) * 8
        got, facts, feed_full, own_turned = start_exchange(
            other_rows,
            jnp.pad(fact, (0, fact_rows * 128 - fact.size)).reshape(fact_rows, 128),
            feed_chunk,
            embed,
            shards,
        )
        facts = facts.reshape(shards, -1)
        all_bias = facts[:, :slice_rows].reshape(-1)
        every_up = facts[:, slice_rows : slice_rows + ups.size]
        every_task = facts[:, slice_rows + ups.size].astype(jnp.int32)
    else:
        looked = jnp.where(
            inside.reshape(-1)[:, None], embed[group_ids.reshape(-1)], jnp.zeros((), BF)
        )
        own_rows = got = lax.psum_scatter(looked, "dp", scatter_dimension=0, tiled=True)
        all_bias = lax.all_gather(vocabulary_bias, BOTH, axis=0, tiled=True)
        every_up = lax.all_gather(ups, BOTH, axis=0, tiled=False)
        every_task = lax.all_gather(sequence_task_index, BOTH, axis=0, tiled=True)
    counts = labels * jnp.sum((every_task[:, None] == task_range[None, :]).astype(F32), 0)
    task_hot = (sequence_task_index[:, None] == task_range[None, :]).astype(F32)
    row_weight = jnp.sum(task_hot[0] * (task_loss_weight / jnp.maximum(counts, 1.0)))
    ups_full = (
        every_up.astype(BF)
        .reshape(shards, layers, 2, rank, up_part)
        .transpose(1, 2, 3, 0, 4)
        .reshape(layers, 2, rank, hidden)
    )
    blank = jnp.zeros((rank, hidden), BF)
    spare = lambda rows: jnp.zeros((rows, 3 * hidden), BF)
    adapters = jnp.stack(
        [
            jnp.concatenate(
                [
                    spare(2 * rank * layer),
                    jnp.concatenate([2 * ups_full[layer, 0], blank, blank], 1),
                    jnp.concatenate([blank, blank, 2 * ups_full[layer, 1]], 1),
                    spare(128 - 2 * rank * (layer + 1)),
                ],
                0,
            )
            for layer in range(layers)
        ]
    )
    downs = jnp.stack(
        [
            jnp.pad(
                jnp.concatenate([adapter_down_matrix[layer, 0], adapter_down_matrix[layer, 1]], 1),
                ((0, 0), (2 * rank * layer, 128 - 2 * rank * (layer + 1))),
            )
            for layer in range(layers)
        ]
    )
    target_rows = jnp.where(mine[tokens:, None], own_rows[tokens:], got[tokens:])
    segments = sentence_numbers[0]
    code = (2 * seg_positions(segments) + mine[:tokens].astype(jnp.int32))[:, None]
    seg_real = segments.astype(F32)
    seg_wide = jnp.broadcast_to(seg_real[:, None], (tokens, 128))
    seg_row = seg_real[None, :]
    place_row = label_positions
    place_col = jnp.broadcast_to(label_positions.reshape(labels, 1), (labels, 128))

    target_bias = all_bias[label_target_token[0]]

    gains, shifts = norm_gain_vector, norm_bias_vector
    last_inputs = (place_col, place_row, seg_wide, downs, adapters, layer_bias_vector)
    in_start = 2 * ff_rows
    slabs_of = lambda full_chunk: (slab_of(full_chunk, 0, ff_rows), slab_of(full_chunk, ff_rows, ff_rows))
    if grouped:
        more = (
            code, position_embedding, gains, shifts, downs, adapters, layer_bias_vector, seg_wide, seg_row,
        )
        qkv, x_last, one, two, slope, out_first, last_full, mid, logs = first_layer(
            own_rows, got, first_in, feed_full, last_chunk, more, shards
        )
        slabs = [(slab_of(first_in, 0, ff_rows), slab_of(feed_full, 0, ff_rows)), slabs_of(last_full)]
        *saved, in_last, out_last, head_full = last_forward(
            x_last, *last_inputs, (last_full,), (in_start, in_start + qkv_rows + out_rows), *slabs[1], gains,
            shifts, head_dense_bias[None, :],
        )
        count = own_turned.shape[1]
        own_bias = lax.dynamic_slice_in_dim(
            all_bias, dp_index * table_rows + fsdp_index % 4 * count, count, 0
        ).reshape(-1, 128)
        mean_t, own_logs = head(saved[-1], own_bias, embed, own_turned)
    else:
        feed_full = lax.all_gather(feed_chunk, BOTH, axis=0, tiled=False)
        last_full = lax.all_gather(last_chunk, BOTH, axis=0, tiled=False)
        slabs = [(slab_of(first_in, 0, ff_rows), slab_of(feed_full, 0, ff_rows)), slabs_of(last_full)]
        taken = lambda full_chunk, start, size: full_chunk[:, start : start + size].reshape(-1, hidden)
        in_first = taken(first_in, ff_rows, qkv_rows)
        out_first = taken(first_in, ff_rows + qkv_rows, out_rows)
        in_last = taken(last_full, in_start, qkv_rows)
        out_last = taken(last_full, in_start + qkv_rows, out_rows)
        head_full = taken(last_full, in_start + qkv_rows + out_rows, head_rows)
        qkv, mid, hidden_rows = project(
            own_rows, got, code, position_embedding, gains, shifts, downs, in_first, adapters, layer_bias_vector
        )
        context, logs = attend(qkv, seg_wide, seg_row)
        x_last, one, two, slope = after(
            context, hidden_rows, out_first, *slabs[0], layer_bias_vector, gains, shifts
        )
        saved = last_forward(
            x_last, *last_inputs, (in_last, out_last, head_full), None, *slabs[1], gains, shifts,
            head_dense_bias[None, :],
        )
        features = saved[-1]
        own_slice = lax.dynamic_slice_in_dim(embed, fsdp_index * slice_rows, slice_rows, 0)
        own_vocab = jnp.concatenate(
            [own_slice]
            + [
                lax.ppermute(
                    own_slice, "dp", [(k, (k + shift) % dp_count) for k in range(dp_count)]
                )
                for shift in range(1, dp_count)
            ],
            0,
        )
        own_bias = jnp.concatenate(
            [
                lax.dynamic_slice_in_dim(
                    all_bias,
                    ((dp_index - shift) % dp_count) * table_rows + fsdp_index * slice_rows,
                    slice_rows,
                    0,
                )
                for shift in range(dp_count)
            ]
        )
        bias_wide = jnp.broadcast_to(own_bias[:, None], (own_bias.shape[0], 128))
        every = lax.all_gather(features, "fsdp", axis=0, tiled=True)
        means, local_logs = vocab(every, own_vocab, own_vocab.T, bias_wide, labels)
        local_logs = local_logs.reshape(-1, labels)
        all_logs = lax.all_gather(local_logs, "fsdp", axis=0, tiled=False)
        whole_logs = jax.nn.logsumexp(all_logs, axis=0)
        scaled = (means * jnp.exp(local_logs - whole_logs)[:, None, :]).astype(BF)
        mean_t = lax.psum_scatter(scaled, "fsdp", scatter_dimension=0, tiled=True)[0].astype(F32)
        own_logs = lax.dynamic_index_in_dim(whole_logs, fsdp_index, 0, keepdims=False)
        own_logs = own_logs[None, :]

    step_as_real = optimizer_step_count[0].astype(F32)
    fades = (1.0 - beta_first**step_as_real, 1.0 - beta_second**step_as_real)
    lanes = lambda value: jnp.pad(
        jnp.broadcast_to(value, (1, value.size if value.ndim else 128)), ((0, 0), (0, 128))
    )[:, :128]
    facts = jnp.concatenate(
        [lanes(value) for value in (row_weight, *fades, target_bias)] + [jnp.zeros((4, 128), F32)]
    )
    hidden_grad, dense_gradient, late, facts = last_backward(
        mean_t, own_logs, target_rows, facts, saved, place_col, place_row, seg_wide, downs, in_last, adapters,
        out_last, *slabs[1], gains, head_full, 3 * rank, shards if grouped else None,
    )
    back = (hidden_grad, one, two, slope, out_first, *slabs[0], gains)
    adapts = (adapter_up_matrix, adapter_moment_first, adapter_moment_second)
    heads = (head_projection, head_moment_first, head_moment_second)
    if grouped:
        sums, dense_portion, adapter_portion = finish(
            back, qkv, logs, seg_wide, seg_row, mid, dense_gradient, late, facts, rank, shards
        )
        loss, norm, *new = update(sums, dense_portion, adapter_portion, facts, heads, adapts)
        return (loss[0, 0], norm[0, 0], *new[3:], *new[:3])
    dctx = after_back(*back)
    first = attend_back(qkv, dctx, logs, seg_wide, seg_row, mid, rank)
    adapter_gradient = (first + late)[:, : 2 * rank * layers].T.reshape(layers, 2, rank, hidden)
    dense_portion = lax.psum_scatter(dense_gradient, BOTH, scatter_dimension=0, tiled=True)
    adapter_portion = lax.psum_scatter(adapter_gradient, BOTH, scatter_dimension=3, tiled=True)
    squared_entries = jnp.sum(adapter_portion * adapter_portion) + jnp.sum(dense_portion * dense_portion)
    masked_task_loss, norm_square = lax.psum((facts[0, 0], squared_entries), BOTH)
    gradient_norm = jnp.sqrt(norm_square)
    factor = jnp.minimum(1.0, clip_limit / (gradient_norm + 1e-06))
    adapter_new = adam(adapts[0], adapter_portion * factor, *adapts[1:], *fades)
    dense_new = adam(heads[0], dense_portion * factor, *heads[1:], *fades)
    return (masked_task_loss, gradient_norm, *adapter_new, *dense_new)


def solution(mesh):
    rows = P(BOTH, None)
    in_specs = (
        rows,
        rows,
        rows,
        rows,
        P(BOTH),
        P(),
        P(),
        P("dp", None),
        P(),
        P(),
        P(),
        P(None, None, BOTH),
        P(None, None, BOTH),
        P(None, None, BOTH),
        P(None, BOTH, None),
        P(),
        P(),
        P(BOTH),
        P(),
        P(None, None, None, BOTH),
        P(None, None, None, BOTH),
        P(None, None, None, BOTH),
        rows,
        rows,
        rows,
    )
    adapter = P(None, None, None, BOTH)
    out_specs = (P(), P(), adapter, adapter, adapter, rows, rows, rows)
    return jax.shard_map(
        per_device, mesh=mesh, in_specs=in_specs, out_specs=out_specs, check_vma=False
    )
```

```python
import functools

import jax
import jax.numpy as jnp
from jax import lax
from jax.experimental import pallas as pl
from jax.experimental.pallas import tpu as pltpu
from jax.sharding import PartitionSpec as P

HEADS = 12
TASKS = 4
REACH = 128

norm_eps = 1e-05
adapter_scale = 2.0
clip_limit = 0.01
learn_rate = 0.05
beta_first = 0.9
beta_second = 0.999
adam_eps = 1e-08
decay_rate = 0.01
masked_score = -1e30

BF = jnp.bfloat16
F32 = jnp.float32
BOTH = ("dp", "fsdp")
VMEM_BYTES = 60 * 1024 * 1024


def mm(a, b):
    return lax.dot_general(a, b, (((1,), (0,)), ((), ())), preferred_element_type=F32)


def mm_nt(a, b):
    return lax.dot_general(a, b, (((1,), (1,)), ((), ())), preferred_element_type=F32)


def mm_tn(a, b):
    return lax.dot_general(a, b, (((0,), (0,)), ((), ())), preferred_element_type=F32)


def layer_norm(rows_in, gain, shift):
    center = rows_in - jnp.mean(rows_in, -1, keepdims=True)
    spread = jnp.mean(center * center, -1, keepdims=True)
    return center * lax.rsqrt(spread + norm_eps) * gain + shift


def norm_back(rows_in, gain, gradient):
    center = rows_in - jnp.mean(rows_in, -1, keepdims=True)
    inverse = lax.rsqrt(jnp.mean(center * center, -1, keepdims=True) + norm_eps)
    unit = center * inverse
    scaled = gradient * gain
    return inverse * (
        scaled
        - jnp.mean(scaled, -1, keepdims=True)
        - unit * jnp.mean(scaled * unit, -1, keepdims=True)
    )


def gelu_pair(v):
    size = jnp.abs(v) * 0.7071067811865476
    base = 1.0 + 0.3275911 * size
    t = pl.reciprocal(base, approx=True)
    t = t * (2.0 - base * t)
    bell = jnp.exp(-0.5 * v * v)
    poly = t * (
        0.127414796 + t * (-0.142248368 + t * (0.7107068705 + t * (-0.7265760135 + t * 0.5307027145)))
    )
    tail = poly * bell
    phi = jnp.where(v >= 0.0, 1.0 - tail, tail)
    return v * phi, phi + v * (bell * 0.3989422804014327)


def params(**more):
    return pltpu.CompilerParams(vmem_limit_bytes=VMEM_BYTES, **more)


def full(shape):
    return pl.BlockSpec(shape, lambda *_: (0,) * len(shape))


def split_of(total, most, step):
    size = (min(most, total) // step) * step
    while size > step and total % size:
        size -= step
    return size if size and total % size == 0 else total


def pair_rows(block, width):
    first = lax.broadcasted_iota(jnp.int32, block.shape, 1) < width
    return jnp.concatenate([jnp.where(first, block, 0.0), jnp.where(first, 0.0, block)], 0).astype(BF)


def pair_join(wide, width):
    rows = wide.shape[1] // 2
    return jnp.concatenate([wide[:width, :rows], wide[width:, rows:]], 0)


def masked(scores, same):
    rows = scores.shape[1] // 2
    return jnp.concatenate(
        [
            jnp.where(same, scores[:, :rows], masked_score),
            jnp.where(same, scores[:, rows:], masked_score),
        ],
        1,
    )


def qkv_bias(bias_ref, layer, start, size):
    hidden = bias_ref.shape[1] // 8
    if start >= 2 * hidden:
        return bias_ref[layer : layer + 1, start - hidden : start - hidden + size]
    return bias_ref[layer : layer + 1, start : start + size] if start < hidden else 0.0


def norm_of(norm_refs, k):
    return norm_refs[0][k : k + 1, :], norm_refs[1][k : k + 1, :]


def project_body(
    own_ref, got_ref, code_ref, spots_ref, gain_ref, shift_ref, down_ref, w_ref, up_ref, bias_ref,
    out_ref, mid_ref, x_ref,
):
    mine = code_ref[...] % 2
    choose = (
        lax.broadcasted_iota(jnp.int32, (own_ref.shape[0], spots_ref.shape[0]), 1) == code_ref[...] // 2
    )
    summed = jnp.where(
        mine > 0, own_ref[...].astype(F32), got_ref[...].astype(F32)
    ) + mm(choose.astype(F32).astype(BF), spots_ref[...])
    x = layer_norm(summed, *norm_of((gain_ref, shift_ref), 0))
    x_ref[...] = x
    low = x.astype(BF)
    mid = mm(low, down_ref[0]).astype(BF)
    mid_ref[...] = mid
    total = w_ref.shape[0]
    step = total // 3
    for start in range(0, total, step):
        part = slice(start, start + step)
        out_ref[:, part] = (
            mm_nt(low, w_ref[part, :]) + mm(mid, up_ref[0, :, part]) + qkv_bias(bias_ref, 0, start, step)
        ).astype(BF)


def project(own, got, code, spots, gains, shifts, down, w, up, bias):
    rows, width = code.shape[0], own.shape[1]
    tile = split_of(rows, 256, 16)
    total = w.shape[0]
    row = lambda n: pl.BlockSpec((tile, n), lambda i: (i, 0))
    return pl.pallas_call(
        project_body,
        grid=(rows // tile,),
        in_specs=[row(width), row(width), row(1)]
        + [full(a.shape) for a in (spots, gains, shifts, down, w, up, bias)],
        out_specs=[row(total), row(down.shape[2]), row(width)],
        out_shape=[
            jax.ShapeDtypeStruct((rows, total), BF),
            jax.ShapeDtypeStruct((rows, down.shape[2]), BF),
            jax.ShapeDtypeStruct((rows, width), F32),
        ],
        compiler_params=params(),
        name="project",
    )(own, got, code, spots, gains, shifts, down, w, up, bias)


def attend_body(q_ref, k_ref, v_ref, seg_ref, seg_row_ref, ctx_ref, log_ref):
    rows = q_ref.shape[0]
    width = q_ref.shape[1] // 2
    scale = width**-0.5
    turned = turn_blocks(v_ref)

    def scored(start):
        own, near = reach_of(start, rows)
        return mm_nt(k_ref[near, :], pair_rows(q_ref[own, :].astype(F32) * scale, width))

    scores = scored(0)
    for start in range(0, rows, REACH):
        own, near = reach_of(start, rows)
        later = scored(start + REACH) if start + REACH < rows else None
        same = seg_ref[near, :] == seg_row_ref[:, own]
        scores = masked(scores, same)
        top = jnp.max(scores, 0, keepdims=True)
        weights = jnp.exp(scores - top)
        total = jnp.sum(weights, 0, keepdims=True)
        context = mm(turned[:, near], weights.astype(BF)) * (1.0 / total)
        ctx_ref[own, :] = pair_join(context, width).T.astype(BF)
        log_ref[0, :, 2 * start : 2 * start + 2 * REACH] = top + jnp.log(total)
        scores = later


def reach_of(start, rows):
    return slice(start, start + REACH), slice(max(0, start - REACH), min(rows, start + 2 * REACH))


def turn_blocks(ref):
    blocks = [ref[k : k + 128, :].astype(F32).T.astype(BF) for k in range(0, ref.shape[0], 128)]
    return jnp.concatenate(blocks, 1)


def attend(qkv, seg_wide, seg_row):
    rows, total = qkv.shape
    hidden = total // 3
    lanes = 2 * (hidden // HEADS)
    pairs = hidden // lanes
    column = lambda kind: pl.BlockSpec((rows, lanes), lambda p: (0, kind * pairs + p))
    return pl.pallas_call(
        attend_body,
        grid=(pairs,),
        in_specs=[column(0), column(1), column(2), full(seg_wide.shape), full(seg_row.shape)],
        out_specs=[
            pl.BlockSpec((rows, lanes), lambda p: (0, p)),
            pl.BlockSpec((1, 1, 2 * rows), lambda p: (p, 0, 0)),
        ],
        out_shape=[
            jax.ShapeDtypeStruct((rows, hidden), BF),
            jax.ShapeDtypeStruct((pairs, 1, 2 * rows), F32),
        ],
        compiler_params=params(),
        name="attend",
    )(qkv, qkv, qkv, seg_wide, seg_row)


def flat(ref):
    whole = ref[...]
    return whole.reshape(-1, whole.shape[-1])


def rows_of(ref, start, size):
    each = ref.shape[1]
    if size % each == 0 and start % each == 0 and each % 16 == 0:
        part = ref[start // each : (start + size) // each, :, :]
        return part.reshape(size, part.shape[-1])
    return flat(ref)[start : start + size, :]


def feed_step(ref):
    units = ref.shape[0] * ref.shape[1]
    step = ref.shape[1]
    while units % (2 * step) == 0 and 2 * step <= 768 and ref.shape[0] > 1:
        step *= 2
    return units, (step if ref.shape[0] > 1 else split_of(units, 768, 128))


def later_biases(bias_ref, layer):
    hidden = bias_ref.shape[1] // 8
    row = bias_ref[layer : layer + 1, :]
    return row[:, 2 * hidden : 3 * hidden], row[:, 3 * hidden : 7 * hidden], row[:, 7 * hidden :]


def after_body(
    ctx_ref, x_ref, wo_ref, up_ref, down_ref, bias_ref, gain_ref, shift_ref,
    out_ref, one_ref, two_ref, slope_ref,
):
    bo, b1, b2 = later_biases(bias_ref, 0)
    one = x_ref[...] + (mm_nt(ctx_ref[...], wo_ref[...]) + bo)
    one_ref[...] = one
    middle = layer_norm(one, *norm_of((gain_ref, shift_ref), 1))
    low = middle.astype(BF)
    total = middle + b2
    units, step = feed_step(up_ref)
    gate = mm_nt(low, rows_of(up_ref, 0, step))
    for start in range(0, units, step):
        part = slice(start, start + step)
        later = mm_nt(low, rows_of(up_ref, start + step, step)) if start + step < units else None
        act, slope = gelu_pair(gate + b1[:, part])
        slope_ref[:, part] = slope.astype(BF)
        total = total + mm(act.astype(BF), rows_of(down_ref, start, step))
        gate = later
    two_ref[...] = total
    out_ref[...] = layer_norm(total, *norm_of((gain_ref, shift_ref), 2))


def slab_spec(slab):
    array, place, rows = slab
    return pl.BlockSpec((array.shape[0], rows, array.shape[2]), lambda *_: (0, place, 0))


def after(ctx, x, wo, up, down, bias, gains, shifts):
    rows, width = x.shape
    tile = split_of(rows, 256, 16)
    units = 4 * width
    row = lambda n: pl.BlockSpec((tile, n), lambda i: (i, 0))
    return pl.pallas_call(
        after_body,
        grid=(rows // tile,),
        in_specs=[row(width), row(width), full(wo.shape), slab_spec(up), slab_spec(down)]
        + [full(a.shape) for a in (bias, gains, shifts)],
        out_specs=[row(width), row(width), row(width), row(units)],
        out_shape=[jax.ShapeDtypeStruct((rows, width), F32)] * 3
        + [jax.ShapeDtypeStruct((rows, units), BF)],
        compiler_params=params(),
        name="after",
    )(ctx, x, wo, up[0], down[0], bias, gains, shifts)


def exact_rows(choose, matrix):
    high = matrix.astype(BF)
    rest = matrix - high.astype(F32)
    middle = rest.astype(BF)
    low = (rest - middle.astype(F32)).astype(BF)
    return mm(choose, high) + mm(choose, middle) + mm(choose, low)


def unpack_rows(slab_ref, targets):
    shards = slab_ref.shape[0]

    @pl.loop(0, shards // 2)
    def _(k):
        first, second = slab_ref[2 * k].astype(F32), slab_ref[2 * k + 1].astype(F32)
        at = 0
        for target in targets:
            each = target.shape[0] // shards
            both = jnp.concatenate([first[at : at + each], second[at : at + each]], 0)
            target[pl.ds(pl.multiple_of(2 * each * k, 2 * each), 2 * each), :] = both.astype(BF)
            at += each


def last_forward_body(
    x_ref, place_ref, place_row_ref, seg_ref, down_ref, adapt_ref, bias_ref, weights_any, up_any, dn_any,
    gain_ref, shift_ref, hbias_ref,
    kv_ref, q_ref, mid_ref, log_ref, one_ref, slope_ref, two_ref, low_ref, act_ref, hslope_ref, feat_ref, *more,
    places, starts,
):
    copies = []
    if starts is None:
        up_ref, dn_ref, ctx_ref, w_ref, wo_ref, hb_ref, sems = more
        sources = zip(weights_any, (w_ref, wo_ref, hb_ref))
    else:
        w_out, wo_out, hb_out, up_ref, dn_ref, ctx_ref, w_ref, wo_ref, hb_ref, in_slab, hb_slab, sems = more
        sources = [
            (weights_any[0].at[:, pl.ds(start, slab.shape[1]), :], slab)
            for start, slab in zip(starts, (in_slab, hb_slab))
        ]
    for source, target in sources:
        copies.append((source, target))
    early = len(copies)
    for source, target, place in ((up_any, up_ref, places[0]), (dn_any, dn_ref, places[1])):
        each = target.shape[1]
        copies.append((source.at[:, pl.ds(place * each, each), :], target))
    copies = [pltpu.make_async_copy(*ends, sems.at[k]) for k, ends in enumerate(copies)]
    for copy in copies:
        copy.start()
    for copy in copies[:early]:
        copy.wait()
    copies = copies[early:]
    if starts is not None:
        unpack_rows(in_slab, (w_ref, wo_ref))
        unpack_rows(hb_slab, (hb_ref,))
        for k, ends in enumerate(((w_ref, w_out), (wo_ref, wo_out), (hb_ref, hb_out))):
            copies.append(pltpu.make_async_copy(*ends, sems.at[4 + k]))
            copies[-1].start()
    rows, hidden = x_ref.shape
    labels = place_ref.shape[0]
    lanes = 2 * (hidden // HEADS)
    width = lanes // 2
    low = x_ref[...].astype(BF)
    mid = mm(low, down_ref[1]).astype(BF)
    mid_ref[...] = mid
    step = split_of(hidden, 768, 128)
    for start in range(hidden, 3 * hidden, step):
        part = slice(start, start + step)
        kv_ref[:, start - hidden : start - hidden + step] = (
            mm_nt(low, w_ref[part, :]) + mm(mid, adapt_ref[1, :, part]) + qkv_bias(bias_ref, 1, start, step)
        ).astype(BF)
    choose = (
        lax.broadcasted_iota(jnp.int32, (labels, rows), 1) == place_ref[...][:, 0:1]
    ).astype(F32).astype(BF)
    own = exact_rows(choose, x_ref[...])
    own_low = own.astype(BF)
    own_mid = mm(choose, mid).astype(BF)
    q_ref[...] = (
        mm_nt(own_low, w_ref[:hidden, :])
        + mm(own_mid, adapt_ref[1, :, :hidden])
        + qkv_bias(bias_ref, 1, 0, hidden)
    ).astype(BF)
    seg = seg_ref[...]
    seg_own = jnp.sum(
        jnp.where(
            lax.broadcasted_iota(jnp.int32, (rows, labels), 0) == place_row_ref[...], seg, 0.0
        ),
        0,
        keepdims=True,
    )
    same = seg == seg_own
    for p in range(hidden // lanes):
        part = slice(p * lanes, (p + 1) * lanes)
        queries = pair_rows(q_ref[:, part].astype(F32) * width**-0.5, width)
        scores = masked(mm_nt(kv_ref[:, part], queries), same)
        top = jnp.max(scores, 0, keepdims=True)
        weights = jnp.exp(scores - top)
        total = jnp.sum(weights, 0, keepdims=True)
        context = mm_tn(
            kv_ref[:, hidden + p * lanes : hidden + (p + 1) * lanes], weights.astype(BF)
        ) * (1.0 / total)
        ctx_ref[:, part] = pair_join(context, width).T.astype(BF)
        log_ref[p : p + 1, :] = top + jnp.log(total)
    bo, b1, b2 = later_biases(bias_ref, 1)
    norms = (gain_ref, shift_ref)
    one = own + (mm_nt(ctx_ref[...], wo_ref[...]) + bo)
    one_ref[...] = one
    middle = layer_norm(one, *norm_of(norms, 3))
    middle_low = middle.astype(BF)
    sum_two = middle + b2
    units, step = feed_step(up_ref)
    for copy in copies:
        copy.wait()
    for start in range(0, units, step):
        part = slice(start, start + step)
        act, slope = gelu_pair(mm_nt(middle_low, rows_of(up_ref, start, step)) + b1[:, part])
        slope_ref[:, part] = slope.astype(BF)
        sum_two = sum_two + mm(act.astype(BF), rows_of(dn_ref, start, step))
    two_ref[...] = sum_two
    out_low = layer_norm(sum_two, *norm_of(norms, 4)).astype(BF)
    low_ref[...] = out_low
    act, slope = gelu_pair(mm(out_low, hb_ref[...]) + hbias_ref[...])
    act_ref[...] = act
    hslope_ref[...] = slope
    feat_ref[...] = layer_norm(act, *norm_of(norms, 5)).astype(BF)


def slab_scratch(slab):
    array, place, rows = slab
    return pltpu.VMEM((array.shape[0], rows, array.shape[2]), BF)


def last_forward(
    x, place_col, place_row, seg_wide, down, adapt, bias, weights, starts, up, dn, gains, shifts, hbias
):
    rows, hidden = x.shape
    labels = place_col.shape[0]
    units = 4 * hidden
    whole = pl.BlockSpec(memory_space=pltpu.VMEM)
    anywhere = pl.BlockSpec(memory_space=pl.ANY)
    shape = jax.ShapeDtypeStruct
    pairs = HEADS // 2
    matrices = [(3 * hidden, hidden), (hidden, hidden), (hidden, hidden)]
    slabs = []
    if starts is not None:
        shards = weights[0].shape[0]
        slabs = [
            pltpu.VMEM((shards, 4 * hidden // shards, hidden), BF),
            pltpu.VMEM((shards, weights[0].shape[1] - starts[1], hidden), BF),
        ]

    def body(*refs):
        head, rest = refs[:7], refs[7:]
        return last_forward_body(
            *head, rest[: len(weights)], *rest[len(weights) :], places=(up[1], dn[1]), starts=starts
        )

    return pl.pallas_call(
        body,
        in_specs=[whole] * 7 + [anywhere] * (len(weights) + 2) + [whole] * 3,
        out_specs=[whole] * 11 + ([anywhere] * 3 if slabs else []),
        out_shape=[
            shape((rows, 2 * hidden), BF),
            shape((labels, hidden), BF),
            shape((rows, down.shape[2]), BF),
            shape((pairs, 2 * labels), F32),
            shape((labels, hidden), F32),
            shape((labels, units), BF),
            shape((labels, hidden), F32),
            shape((labels, hidden), BF),
            shape((labels, hidden), F32),
            shape((labels, hidden), F32),
            shape((labels, hidden), BF),
        ]
        + ([shape(m, BF) for m in matrices] if slabs else []),
        scratch_shapes=[
            slab_scratch(up),
            slab_scratch(dn),
            pltpu.VMEM((labels, hidden), BF),
            *[pltpu.VMEM(m, BF) for m in matrices],
            *slabs,
            pltpu.SemaphoreType.DMA((7,)),
        ],
        compiler_params=params(),
        name="last_forward",
    )(x, place_col, place_row, seg_wide, down, adapt, bias, *weights, up[0], dn[0], gains, shifts, hbias)


def vocab_body(u_ref, e_ref, et_ref, bias_ref, num_ref, log_ref, scores, weights):
    count = e_ref.shape[0]
    step = split_of(count, 640, 16)
    u = u_ref[...]
    rows = u.shape[0]
    labels = num_ref.shape[2]
    top = jnp.full((1, rows), -jnp.inf, F32)
    for start in range(0, count, step):
        part = slice(start, start + step)
        bias = bias_ref[part, :]
        logits = mm_nt(e_ref[part, :], u) + jnp.concatenate([bias] * (rows // bias.shape[1]), 1)
        scores[part, :] = logits
        top = jnp.maximum(top, jnp.max(logits, 0, keepdims=True))
    total = jnp.zeros((1, rows), F32)
    for start in range(0, count, step):
        part = slice(start, start + step)
        grown = jnp.exp(scores[part, :] - top)
        total = total + jnp.sum(grown, 0, keepdims=True)
        weights[part, :] = grown.astype(BF)
    mean = mm(et_ref[...], weights[...]) * (1.0 / total)
    logs = top + jnp.log(total)
    for k in range(rows // labels):
        num_ref[k, :, :] = mean[:, k * labels : (k + 1) * labels]
        log_ref[k, :, :] = logs[:, k * labels : (k + 1) * labels]


def vocab(u, e, et, bias_wide, labels):
    rows, hidden = u.shape
    count = e.shape[0]
    tile = 2 * labels
    return pl.pallas_call(
        vocab_body,
        grid=(rows // tile,),
        in_specs=[
            pl.BlockSpec((tile, hidden), lambda i: (i, 0)),
            full(e.shape),
            full(et.shape),
            full(bias_wide.shape),
        ],
        out_specs=[
            pl.BlockSpec((2, hidden, labels), lambda i: (i, 0, 0)),
            pl.BlockSpec((2, 1, labels), lambda i: (i, 0, 0)),
        ],
        out_shape=[
            jax.ShapeDtypeStruct((rows // labels, hidden, labels), F32),
            jax.ShapeDtypeStruct((rows // labels, 1, labels), F32),
        ],
        scratch_shapes=[pltpu.VMEM((count, tile), F32), pltpu.VMEM((count, tile), BF)],
        compiler_params=params(),
        name="vocab",
    )(u, e, et, bias_wide)


def last_backward_body(
    mean_ref, all_log_ref, target_ref, fact_ref, kv_ref, q_ref, mid_ref, log_ref, one_ref, slope_ref, two_ref,
    low_ref, act_ref, hslope_ref, feat_ref, place_ref, place_row_ref, seg_ref, down_ref, w_ref, adapt_ref, wo_ref,
    up_any, dn_any, gain_ref, hb_ref,
    dx_ref, gh_ref, g_ref, out_fact_ref,
    up_ref, dn_ref, dkv_ref, dq_ref, sems, *, places, edge,
):
    copies = []
    for k, (source, target, place) in enumerate(
        ((up_any, up_ref, places[0]), (dn_any, dn_ref, places[1]))
    ):
        rows = target.shape[1]
        copies.append(
            pltpu.make_async_copy(
                source.at[:, pl.ds(place * rows, rows), :], target, sems.at[k]
            )
        )
        copies[-1].start()
    rows = kv_ref.shape[0]
    labels, hidden = feat_ref.shape
    lanes = 2 * (hidden // HEADS)
    width = lanes // 2
    scale = width**-0.5
    targets = target_ref[...].astype(F32)
    weight = fact_ref[0:1, 0:1]
    chosen = jnp.sum(feat_ref[...].astype(F32) * targets, keepdims=True)
    loss = weight * (jnp.sum(all_log_ref[...] - fact_ref[3:4, :labels], keepdims=True) - chosen)
    out_fact_ref[...] = jnp.where(
        lax.broadcasted_iota(jnp.int32, fact_ref.shape, 0) == 0, loss, fact_ref[...]
    )
    du = weight * (mean_ref[...].T - targets)
    dact = norm_back(act_ref[...], gain_ref[5:6, :], du)
    dz = (hslope_ref[...] * dact).astype(BF)
    dense = mm_tn(low_ref[...], dz)
    if len(gh_ref.shape) == 2:
        gh_ref[...] = dense
    else:
        each = hidden // gh_ref.shape[0]
        spare = jnp.zeros((gh_ref.shape[1] - each, hidden), F32)
        for k in range(gh_ref.shape[0]):
            gh_ref[k] = jnp.concatenate([dense[k * each : (k + 1) * each, :], spare], 0).astype(BF)
    dtwo = norm_back(two_ref[...], gain_ref[4:5, :], mm_nt(dz, hb_ref[...]))
    dtwo_low = dtwo.astype(BF)
    dmiddle = dtwo
    units, step = feed_step(up_ref)
    for copy in copies:
        copy.wait()
    for start in range(0, units, step):
        part = slice(start, start + step)
        dgate = (
            slope_ref[:, part].astype(F32) * mm_nt(dtwo_low, rows_of(dn_ref, start, step))
        ).astype(BF)
        dmiddle = dmiddle + mm(dgate, rows_of(up_ref, start, step))
    done = norm_back(one_ref[...], gain_ref[3:4, :], dmiddle)
    dctx = mm(done.astype(BF), wo_ref[...]).astype(BF)
    seg = seg_ref[...]
    choose_t = lax.broadcasted_iota(jnp.int32, (rows, labels), 0) == place_row_ref[...]
    same = seg == jnp.sum(jnp.where(choose_t, seg, 0.0), 0, keepdims=True)
    for p in range(hidden // lanes):
        part = slice(p * lanes, (p + 1) * lanes)
        later = slice(hidden + p * lanes, hidden + (p + 1) * lanes)
        queries = pair_rows(q_ref[:, part].astype(F32) * scale, width)
        outs = pair_rows(dctx[:, part].astype(F32), width)
        keys = kv_ref[:, part]
        weights = jnp.exp(masked(mm_nt(keys, queries), same) - log_ref[p : p + 1, :])
        dweights = mm_nt(kv_ref[:, later], outs)
        inner = jnp.sum(dweights * weights, 0, keepdims=True)
        dscores = (weights * (dweights - inner)).astype(BF)
        dkv_ref[:, part] = mm(dscores, queries).astype(BF)
        dkv_ref[:, later] = mm(weights.astype(BF), outs).astype(BF)
        dq_ref[:, part] = (pair_join(mm_tn(keys, dscores), width) * scale).T.astype(BF)
    dq = dq_ref[...]
    own_mid = mm(
        (lax.broadcasted_iota(jnp.int32, (labels, rows), 1) == place_ref[...][:, 0:1]).astype(F32).astype(BF),
        mid_ref[...],
    ).astype(BF)
    g_ref[...] = adapter_scale * jnp.where(
        lax.broadcasted_iota(jnp.int32, g_ref.shape, 1) < edge,
        mm_tn(dq, own_mid),
        mm_tn(dkv_ref[:, hidden:], mid_ref[...]),
    )
    dmid_own = mm_nt(dq, adapt_ref[1, :, :hidden]).astype(BF)
    own = done + mm(dq, w_ref[:hidden, :]) + mm_nt(dmid_own, down_ref[1])
    spread = choose_t.astype(F32).astype(BF)
    own_high = own.astype(BF)
    own_rest = (own - own_high.astype(F32)).astype(BF)
    dmid = mm_nt(dkv_ref[:, hidden:], adapt_ref[1, :, 2 * hidden :]).astype(BF)
    step = split_of(hidden, 256, 128)
    for start in range(0, hidden, step):
        part = slice(start, start + step)
        dx_ref[:, part] = (
            mm(dkv_ref[...], w_ref[hidden:, part])
            + mm_nt(dmid, down_ref[1, part, :])
            + mm(spread, own_high[:, part])
            + mm(spread, own_rest[:, part])
        )


def last_backward(
    mean, logs, targets, facts, saved, place_col, place_row, seg_wide, down, w, adapt, wo, up, dn, gains, hb, edge, shards
):
    kv = saved[0]
    rows = kv.shape[0]
    labels, hidden = targets.shape
    whole = pl.BlockSpec(memory_space=pltpu.VMEM)
    anywhere = pl.BlockSpec(memory_space=pl.ANY)
    shape = jax.ShapeDtypeStruct
    return pl.pallas_call(
        functools.partial(last_backward_body, places=(up[1], dn[1]), edge=edge),
        in_specs=[whole] * 22 + [anywhere] * 2 + [whole] * 2,
        out_specs=[whole] * 4,
        out_shape=[
            shape((rows, hidden), F32),
            shape((hidden, hidden), F32)
            if shards is None
            else shape((shards, -(-hidden // shards // 16) * 16, hidden), BF),
            shape((hidden, down.shape[2]), F32),
            shape(facts.shape, F32),
        ],
        scratch_shapes=[
            slab_scratch(up),
            slab_scratch(dn),
            pltpu.VMEM(kv.shape, BF),
            pltpu.VMEM((labels, hidden), BF),
            pltpu.SemaphoreType.DMA((2,)),
        ],
        compiler_params=params(),
        name="last_backward",
    )(mean, logs, targets, facts, *saved, place_col, place_row, seg_wide, down, w, adapt, wo, up[0], dn[0], gains, hb)


def after_back_body(dout_ref, one_ref, two_ref, slope_ref, wo_ref, up_ref, down_ref, gain_ref, dctx_ref):
    dtwo = norm_back(two_ref[...], gain_ref[2:3, :], dout_ref[...])
    low = dtwo.astype(BF)
    dmiddle = dtwo
    units, step = feed_step(up_ref)
    dact = mm_nt(low, rows_of(down_ref, 0, step))
    for start in range(0, units, step):
        part = slice(start, start + step)
        later = mm_nt(low, rows_of(down_ref, start + step, step)) if start + step < units else None
        dgate = (slope_ref[:, part].astype(F32) * dact).astype(BF)
        dmiddle = dmiddle + mm(dgate, rows_of(up_ref, start, step))
        dact = later
    done = norm_back(one_ref[...], gain_ref[1:2, :], dmiddle)
    dctx_ref[...] = mm(done.astype(BF), wo_ref[...]).astype(BF)


def after_back(dout, one, two, slope, wo, up, down, norms):
    rows, width = dout.shape
    tile = split_of(rows, 256, 16)
    row = lambda n: pl.BlockSpec((tile, n), lambda i: (i, 0))
    return pl.pallas_call(
        after_back_body,
        grid=(rows // tile,),
        in_specs=[row(width), row(width), row(width), row(slope.shape[1]), full(wo.shape)]
        + [slab_spec(up), slab_spec(down), full(norms.shape)],
        out_specs=row(width),
        out_shape=jax.ShapeDtypeStruct((rows, width), BF),
        compiler_params=params(),
        name="after_back",
    )(dout, one, two, slope, wo, up[0], down[0], norms)


def attend_back_body(
    q_ref, k_ref, v_ref, dctx_ref, log_ref, seg_ref, seg_row_ref, mid_ref, g_ref, dv_ref, *, edge
):
    rows = q_ref.shape[0]
    width = q_ref.shape[1] // 2
    scale = width**-0.5
    dv_ref[...] = jnp.zeros_like(dv_ref)
    gq = jnp.zeros((2 * width, mid_ref.shape[1]), F32)
    turned = turn_blocks(k_ref)

    def products(start):
        own, near = reach_of(start, rows)
        queries = pair_rows(q_ref[own, :].astype(F32) * scale, width)
        outs = pair_rows(dctx_ref[own, :].astype(F32), width)
        return outs, mm_nt(k_ref[near, :], queries), mm_nt(v_ref[near, :], outs)

    now = products(0)
    for start in range(0, rows, REACH):
        own, near = reach_of(start, rows)
        later = products(start + REACH) if start + REACH < rows else None
        outs, scores, dweights = now
        same = seg_ref[near, :] == seg_row_ref[:, own]
        logs = log_ref[0, :, 2 * start : 2 * start + 2 * REACH]
        weights = jnp.exp(masked(scores, same) - logs)
        inner = jnp.sum(dweights * weights, 0, keepdims=True)
        dscores = (weights * (dweights - inner)).astype(BF)
        dv_ref[near, :] += mm(weights.astype(BF), outs)
        dq = (pair_join(mm(turned[:, near], dscores), width) * scale).astype(BF)
        gq = gq + mm(dq, mid_ref[own, :])
        now = later
    gv = mm_tn(dv_ref[...].astype(BF), mid_ref[...])
    g_ref[...] = adapter_scale * jnp.where(
        lax.broadcasted_iota(jnp.int32, gq.shape, 1) < edge, gq, gv
    )


def attend_back(qkv, dctx, logs, seg_wide, seg_row, mid, edge):
    rows, total = qkv.shape
    hidden = total // 3
    lanes = 2 * (hidden // HEADS)
    pairs = hidden // lanes
    column = lambda kind: pl.BlockSpec((rows, lanes), lambda p: (0, kind * pairs + p))
    return pl.pallas_call(
        functools.partial(attend_back_body, edge=edge),
        grid=(pairs,),
        in_specs=[
            column(0),
            column(1),
            column(2),
            column(0),
            pl.BlockSpec((1, 1, 2 * rows), lambda p: (p, 0, 0)),
            full(seg_wide.shape),
            full(seg_row.shape),
            full(mid.shape),
        ],
        out_specs=pl.BlockSpec((lanes, mid.shape[1]), lambda p: (p, 0)),
        out_shape=jax.ShapeDtypeStruct((hidden, mid.shape[1]), F32),
        scratch_shapes=[pltpu.VMEM((rows, lanes), F32)],
        compiler_params=params(),
        name="attend_back",
    )(qkv, qkv, qkv, dctx, logs, seg_wide, seg_row, mid)


MESH = pl.DeviceIdType.MESH


def position():
    dp, fsdp = lax.axis_index("dp"), lax.axis_index("fsdp")
    return {"x": dp, "z": fsdp // 4, "y": (fsdp // 2) % 2, "c": fsdp % 2}


def device_of(place):
    return (place["x"], (place["z"] * 2 + place["y"]) * 2 + place["c"])


def number_of(place):
    return place["x"] * 16 + (place["z"] * 2 + place["y"]) * 2 + place["c"]


def rank_device(number):
    return (number // 16, number % 16)


def greet_all(shards):
    barrier = pltpu.get_barrier_semaphore()
    me = lax.axis_index("dp") * 16 + lax.axis_index("fsdp")

    @pl.loop(1, shards)
    def _(k):
        pl.semaphore_signal(
            barrier, inc=1, device_id=rank_device((me + k) % shards), device_id_type=MESH
        )


def await_all(shards):
    pl.semaphore_wait(pltpu.get_barrier_semaphore(), shards - 1)


def direct_copy(source, target, sems, me, k, shards):
    return pltpu.make_async_remote_copy(
        src_ref=source,
        dst_ref=target,
        send_sem=sems.at[0],
        recv_sem=sems.at[1],
        device_id=rank_device((me + k) % shards),
        device_id_type=MESH,
    )


def spread(piece_of, buffer, sems, me, shards):
    @pl.loop(1, shards)
    def _(k):
        direct_copy(piece_of((me + k) % shards), buffer.at[me], sems, me, k, shards).start()


def collect(buffer, sems, me, shards):
    whole = buffer.at[pl.ds(0, shards - 1)]
    copy = direct_copy(whole, whole, sems, me, 1, shards)
    copy.wait_recv()
    copy.wait_send()


def relative_places(order):
    places = [
        {"x": dx, "z": dz, "y": dy} for dx in (0, 1) for dz in range(-3, 4) for dy in (0, 1)
    ]
    size = lambda p: abs(p["x"]) + abs(p["z"]) + abs(p["y"])
    return sorted(places, key=lambda p: (abs(p[order[-1]]), size(p), [abs(p[a]) for a in order]))


class Gather:
    def __init__(self, chunk, full_buffer, start, rows, order, sends, receives, hands, hands_got):
        self.chunk, self.full, self.order = chunk, full_buffer, order
        self.part = pl.ds(start, rows)
        self.sends, self.receives, self.hands, self.hands_got = sends, receives, hands, hands_got
        self.here = position()
        self.items = relative_places(order)
        self.pending = []

    def origin(self, item):
        here = self.here
        return {"x": (here["x"] + item["x"]) % 2, "z": here["z"] - item["z"], "y": (here["y"] + item["y"]) % 2, "c": here["c"]}

    def key(self, place):
        return (place["x"] * 4 + place["z"]) * 2 + place["y"]

    def outward(self, item):
        deepest = max([k for k, axis in enumerate(self.order) if item[axis]], default=-1)
        ways = []
        if deepest >= 0 and self.order[deepest] == "z":
            ways.append(("z", 1 if item["z"] > 0 else -1))
        for axis in self.order[deepest + 1 :]:
            ways += [("z", 1), ("z", -1)] if axis == "z" else [(axis, 1)]
        return ways

    def copy(self, index, way, slot, item):
        here = self.here
        place = self.origin(item)
        number, key = number_of(place), self.key(place)
        mine = not any(item.values())
        source = self.chunk.at[self.part, :] if mine else self.full.at[number, self.part, :]
        if way is None:
            target = dict(here, c=1 - here["c"])
            sends, receives = self.hands.at[index], self.hands_got.at[key]
        else:
            axis, step = way
            target = dict(here)
            target[axis] = here["z"] + step if axis == "z" else 1 - here[axis]
            sends, receives = self.sends.at[index * 4 + slot], self.receives.at[key]
        return pltpu.make_async_remote_copy(
            src_ref=source,
            dst_ref=self.full.at[number, self.part, :],
            send_sem=sends,
            recv_sem=receives,
            device_id=device_of(target),
            device_id_type=MESH,
        )

    def valid(self, item):
        z = self.here["z"] - item["z"]
        return (z >= 0) & (z <= 3)

    def step(self, index):
        item = self.items[index]

        @pl.when(self.valid(item))
        def _():
            if any(item.values()):
                self.arrived(index, item)
            for slot, way in enumerate(self.outward(item)):
                self.when_way(way, lambda way=way, slot=slot: self.copy(index, way, slot, item).start())
            self.copy(index, None, 0, item).start()

    def when_way(self, way, act):
        axis, step = way
        if axis == "z":
            z = self.here["z"] + step
            pl.when((z >= 0) & (z <= 3))(act)
        else:
            act()

    def arrived(self, index, item):
        place = self.origin(item)
        spot = self.full.at[number_of(place), self.part, :]
        pltpu.make_async_remote_copy(
            src_ref=spot,
            dst_ref=spot,
            send_sem=self.sends.at[index * 4],
            recv_sem=self.receives.at[self.key(place)],
            device_id=device_of(dict(self.here, c=1 - self.here["c"])),
            device_id_type=MESH,
        ).wait_recv()

    def finish(self):
        for index, item in enumerate(self.items):

            @pl.when(self.valid(item))
            def _(index=index, item=item):
                for slot, way in enumerate(self.outward(item)):
                    self.when_way(way, lambda way=way, slot=slot: self.copy(index, way, slot, item).wait_send())
                self.copy(index, None, 0, item).wait_send()
                place = dict(self.origin(item), c=1 - self.here["c"])
                spot = self.full.at[number_of(place), self.part, :]
                pltpu.make_async_remote_copy(
                    src_ref=spot,
                    dst_ref=spot,
                    send_sem=self.hands.at[index],
                    recv_sem=self.hands_got.at[self.key(place)],
                    device_id=device_of(dict(self.here, c=1 - self.here["c"])),
                    device_id_type=MESH,
                ).wait_recv()


ITEMS = 28


def start_body(
    streams, shards, fact, chunk, table_any, facts, full_chunk, et_out, e_ref, et_ref,
    fact_sems, own_sems, sends, receives, hands, hands_got,
):
    here = position()
    me = number_of(here)
    own = [
        pltpu.make_async_copy(source, target, own_sems.at[k])
        for k, (source, target) in enumerate(
            ((vocab_rows(table_any, e_ref), e_ref), (fact, facts.at[me]), (chunk, full_chunk.at[me]))
        )
    ]
    for copy in own:
        copy.start()
    greet_all(shards)
    await_all(shards)
    gathers = [
        Gather(
            chunk, full_chunk, start, size, order, sends.at[k], receives.at[k], hands.at[k], hands_got.at[k]
        )
        for k, (start, size, order) in enumerate(streams)
    ]
    for gather in gathers:
        gather.step(0)
    spread(lambda peer: fact, facts, fact_sems, me, shards)
    own[0].wait()
    blocks = e_ref.shape[0] // 128
    each = -(-blocks // (ITEMS - 1))
    for index in range(1, ITEMS):
        for k in range((index - 1) * each, min(index * each, blocks)):
            part = slice(k * 128, (k + 1) * 128)
            et_ref[:, part] = e_ref[part, :].astype(F32).T.astype(BF)
        for gather in gathers:
            gather.step(index)
    turned = pltpu.make_async_copy(et_ref, et_out, own_sems.at[3])
    turned.start()
    for gather in gathers:
        gather.finish()
    collect(facts, fact_sems, me, shards)
    for copy in own[1:] + [turned]:
        copy.wait()


def vocab_rows(table, like):
    here = position()
    count = like.shape[0]
    return table.at[pl.ds(pl.multiple_of((here["y"] * 2 + here["c"]) * count, 16), count), :]


def gather_sems(streams):
    sems = pltpu.SemaphoreType.DMA
    count = len(streams)
    return [sems((count, 4 * ITEMS)), sems((count, 16)), sems((count, ITEMS)), sems((count, 16))]


def streams_of(rows, parts):
    streams, start = [], 0
    for k, (order, share) in enumerate(parts):
        size = rows - start if k == len(parts) - 1 else round(rows * share / 16) * 16
        streams.append((start, size, order))
        start += size
    return streams


def start_exchange(fact, chunk, table, shards):
    anywhere = pl.BlockSpec(memory_space=pl.ANY)
    shape = jax.ShapeDtypeStruct
    sems = pltpu.SemaphoreType.DMA
    streams = streams_of(chunk.shape[0], (("zxy", 0.34), ("zyx", 0.34), ("xzy", 0.32)))
    count, hidden = table.shape[0] // 4, table.shape[1]
    return pl.pallas_call(
        functools.partial(start_body, streams, shards),
        in_specs=[anywhere] * 3,
        out_specs=[anywhere] * 3,
        out_shape=[
            shape((shards, *fact.shape), fact.dtype),
            shape((shards, *chunk.shape), chunk.dtype),
            shape((hidden, count), BF),
        ],
        scratch_shapes=[
            pltpu.VMEM((count, hidden), BF),
            pltpu.VMEM((hidden, count), BF),
            sems((2,)),
            sems((4,)),
            *gather_sems(streams),
        ],
        compiler_params=params(collective_id=1, has_side_effects=True),
        name="start_exchange",
    )(fact, chunk, table)


def first_layer_body(
    streams, shards,
    own_any, got_any, in_any, feed_any, chunk, code_ref, spots_ref, gain_ref, shift_ref, down_ref,
    adapt_ref, bias_ref, seg_ref, seg_row_ref,
    qkv_out, x_out, one_out, two_out, slope_out, wo_out, full_chunk, mid_ref, log_ref,
    own, got, in_slab, w, wo, up, dn, x, qkv, ctx, two, out, slope,
    load_sems, tile_sems, out_sems, sends, receives, hands, hands_got,
):
    here = position()
    me = number_of(here)
    rows, hidden = x.shape
    tile = split_of(rows, 256, 16)
    tiles = rows // tile
    lanes = 2 * (hidden // HEADS)
    pairs = hidden // lanes

    def slab(source, target, start):
        return source.at[:, pl.ds(start, target.shape[1]), :]

    loads = [
        pltpu.make_async_copy(source, target, load_sems.at[k])
        for k, (source, target) in enumerate(
            (
                (own_any.at[pl.ds(0, rows), :], own),
                (got_any.at[pl.ds(0, rows), :], got),
                (slab(in_any, in_slab, up.shape[1]), in_slab),
                (slab(in_any, up, 0), up),
                (slab(feed_any, dn, 0), dn),
                (chunk, full_chunk.at[me]),
            )
        )
    ]
    for copy in loads:
        copy.start()
    barrier = pltpu.get_barrier_semaphore()
    peers = [
        dict(here, c=1 - here["c"]),
        dict(here, x=1 - here["x"]),
        dict(here, y=1 - here["y"]),
        *[dict(here, z=flip(here["z"], k)) for k in (1, 2, 3)],
    ]
    for peer in peers:
        pl.semaphore_signal(barrier, inc=1, device_id=device_of(peer), device_id_type=MESH)
    pl.semaphore_wait(barrier, len(peers))
    gathers = [
        Gather(
            chunk, full_chunk, start, size, order, sends.at[k], receives.at[k], hands.at[k], hands_got.at[k]
        )
        for k, (start, size, order) in enumerate(streams)
    ]
    def advance(first, last):
        for index in range(first, last + 1):
            for gather in gathers:
                gather.step(index)

    advance(0, 0)
    for copy in loads[:3]:
        copy.wait()
    unpack_rows(in_slab, (w, wo))

    @pl.loop(0, tiles)
    def _(i):
        part = pl.ds(pl.multiple_of(i * tile, tile), tile)
        project_body(
            own.at[part, :], got.at[part, :], code_ref.at[part, :], spots_ref, gain_ref, shift_ref, down_ref, w,
            adapt_ref, bias_ref, qkv.at[part, :], mid_ref.at[part, :], x.at[part, :],
        )

        @pl.when(i == tiles - 3)
        def _():
            advance(1, 3)

        @pl.when(i == tiles - 1)
        def _():
            advance(4, 5)

    early = [
        pltpu.make_async_copy(qkv, qkv_out, out_sems.at[0]),
        pltpu.make_async_copy(wo, wo_out, out_sems.at[1]),
    ]
    for copy in early:
        copy.start()

    @pl.loop(0, pairs)
    def _(p):
        column = lambda kind: pl.ds(pl.multiple_of((kind * pairs + p) * lanes, lanes), lanes)
        attend_body(
            qkv.at[:, column(0)], qkv.at[:, column(1)], qkv.at[:, column(2)], seg_ref, seg_row_ref,
            ctx.at[:, column(0)], log_ref.at[pl.ds(p, 1)],
        )

        for k, (first, last) in {1: (6, 7), 3: (8, 9), 5: (10, 13)}.items():
            pl.when(p == pairs - 6 + k)(functools.partial(advance, first, last))

    for copy in loads[3:5]:
        copy.wait()

    def tile_copies(i):
        part = pl.ds(pl.multiple_of(i * tile, tile), tile)
        turn = i % 2
        return [
            pltpu.make_async_copy(source, target.at[part, :], tile_sems.at[k, i])
            for k, (source, target) in enumerate(
                (
                    (out.at[turn], x_out),
                    (two.at[turn], two_out),
                    (slope.at[turn], slope_out),
                    (x.at[part, :], one_out),
                )
            )
        ]

    plan = {tiles - 4: (14, 16), tiles - 3: (17, 19), tiles - 2: (20, 23), tiles - 1: (24, 27)}

    @pl.loop(0, tiles)
    def _(i):
        part = pl.ds(pl.multiple_of(i * tile, tile), tile)
        turn = i % 2

        @pl.when(i >= 2)
        def _():
            for copy in tile_copies(i - 2):
                copy.wait()

        after_body(
            ctx.at[part, :], x.at[part, :], wo, up, dn, bias_ref, gain_ref, shift_ref, out.at[turn],
            x.at[part, :], two.at[turn], slope.at[turn],
        )
        for copy in tile_copies(i):
            copy.start()
        for k, (first, last) in plan.items():
            pl.when(i == k)(functools.partial(advance, first, last))

    for gather in gathers:
        gather.finish()
    for i in (tiles - 2, tiles - 1):
        for copy in tile_copies(i):
            copy.wait()
    for copy in early + loads[5:]:
        copy.wait()


def first_layer(own, got, first_in, feed, chunk, more, shards):
    whole = pl.BlockSpec(memory_space=pltpu.VMEM)
    anywhere = pl.BlockSpec(memory_space=pl.ANY)
    code, down = more[0], more[4]
    rows, hidden = code.shape[0], own.shape[1]
    tile = split_of(rows, 256, 16)
    pairs = HEADS // 2
    units = 4 * hidden
    each = units // shards
    shape = jax.ShapeDtypeStruct
    sems = pltpu.SemaphoreType.DMA
    streams = streams_of(chunk.shape[0], (("zxy", 0.4), ("zyx", 0.4), ("xyz", 0.2)))
    return pl.pallas_call(
        functools.partial(first_layer_body, streams, shards),
        in_specs=[anywhere] * 5 + [whole] * len(more),
        out_specs=[anywhere] * 7 + [whole] * 2,
        out_shape=[
            shape((rows, 3 * hidden), BF),
            shape((rows, hidden), F32),
            shape((rows, hidden), F32),
            shape((rows, hidden), F32),
            shape((rows, units), BF),
            shape((hidden, hidden), BF),
            shape((shards, *chunk.shape), BF),
            shape((rows, down.shape[2]), BF),
            shape((pairs, 1, 2 * rows), F32),
        ],
        scratch_shapes=[
            pltpu.VMEM((rows, hidden), BF),
            pltpu.VMEM((rows, hidden), BF),
            pltpu.VMEM((shards, 4 * hidden // shards, hidden), BF),
            pltpu.VMEM((3 * hidden, hidden), BF),
            pltpu.VMEM((hidden, hidden), BF),
            pltpu.VMEM((shards, each, hidden), BF),
            pltpu.VMEM((shards, each, hidden), BF),
            pltpu.VMEM((rows, hidden), F32),
            pltpu.VMEM((rows, 3 * hidden), BF),
            pltpu.VMEM((rows, hidden), BF),
            pltpu.VMEM((2, tile, hidden), F32),
            pltpu.VMEM((2, tile, hidden), F32),
            pltpu.VMEM((2, tile, units), BF),
            sems((6,)),
            sems((4, rows // tile)),
            sems((2,)),
            *gather_sems(streams),
        ],
        compiler_params=params(collective_id=3, has_side_effects=True),
        name="first_layer",
    )(own, got, first_in, feed, chunk, *more)


PICK = 64
GROUP = 16


def look_up_body(ids, low_ref, table, out_ref, stage):
    @pl.loop(0, out_ref.shape[0] // PICK)
    def _(b):
        part = pl.ds(pl.multiple_of(b * PICK, PICK), PICK)

        def one(t, carry):
            stage[t] = table[ids[b * PICK + t]]
            return carry

        lax.fori_loop(0, PICK, one, 0, unroll=8)
        choose = lax.broadcasted_iota(jnp.int32, (PICK, PICK * GROUP), 1) == low_ref[part, :]
        out_ref[part, :] = mm(choose.astype(F32).astype(BF), flat(stage)).astype(BF)


def look_up(ids, table):
    whole = pl.BlockSpec(memory_space=pltpu.VMEM)
    hidden = table.shape[1]
    low = jnp.arange(ids.size, dtype=jnp.int32) % PICK * GROUP + ids % GROUP
    return pl.pallas_call(
        look_up_body,
        in_specs=[pl.BlockSpec(memory_space=pltpu.SMEM), whole, whole],
        out_specs=whole,
        out_shape=jax.ShapeDtypeStruct((ids.size, hidden), table.dtype),
        scratch_shapes=[pltpu.VMEM((PICK, GROUP, hidden), table.dtype)],
        compiler_params=params(),
        name="look_up",
    )(ids // GROUP, low[:, None], table.reshape(-1, GROUP, hidden))


def adam(weight, gradient, moment_one, moment_two, fade_one, fade_two):
    moment_one = beta_first * moment_one + (1.0 - beta_first) * gradient
    moment_two = beta_second * moment_two + (1.0 - beta_second) * gradient * gradient
    one_hat = moment_one / fade_one
    two_hat = moment_two / fade_two
    weight = weight - learn_rate * (one_hat / (jnp.sqrt(two_hat) + adam_eps) + decay_rate * weight)
    return (weight, moment_one, moment_two)


BACK_TILE = 256


def finish_body(
    shards, edge,
    dout_any, one_any, two_any, slope_any, wo_any, up_any, dn_any, qkv_any, gain_ref, log_ref, seg_ref,
    seg_row_ref, mid_ref, parts, late_ref, facts,
    sums_ref, dense_ref, total_ref,
    dout, one, two, slope, wo, up, dn, qkv, dctx, dv, grad, core_got, chip_sum, dense_got, grad_got, note, notes,
    tile_sems, load_sems, core_sems, dense_sems, grad_sems, note_sems,
):
    rows, hidden = dout.shape
    tile = split_of(rows, BACK_TILE, 16)
    tiles = rows // tile
    me = number_of(position())

    def tile_loads(i):
        part = pl.ds(pl.multiple_of(i * tile, tile), tile)
        return [
            pltpu.make_async_copy(source.at[part, :], target.at[part, :], tile_sems.at[k, i])
            for k, (source, target) in enumerate(
                ((two_any, two), (dout_any, dout), (slope_any, slope), (one_any, one))
            )
        ]

    here = position()
    chips = shards // 2
    chip, core = me // 2, here["c"]
    to_core = pltpu.make_async_remote_copy(
        src_ref=parts.at[:, 1 - core],
        dst_ref=core_got,
        send_sem=core_sems.at[0],
        recv_sem=core_sems.at[1],
        device_id=device_of(dict(here, c=1 - core)),
        device_id_type=MESH,
    )

    def to_chip(k):
        peer = (chip + k) % chips
        return pltpu.make_async_remote_copy(
            src_ref=chip_sum.at[peer],
            dst_ref=dense_got.at[chip],
            send_sem=dense_sems.at[0],
            recv_sem=dense_sems.at[1],
            device_id=rank_device(2 * peer + core),
            device_id_type=MESH,
        )

    loads = [
        pltpu.make_async_copy(source, target, load_sems.at[k])
        for k, (source, target) in enumerate(
            (
                (dn_any.at[:, pl.ds(0, dn.shape[1]), :], dn),
                (up_any.at[:, pl.ds(0, up.shape[1]), :], up),
                (wo_any, wo),
                (qkv_any, qkv),
            )
        )
    ]
    for copy in tile_loads(0) + loads[:3]:
        copy.start()
    for i in range(1, tiles):
        for copy in tile_loads(i):
            copy.start()
    loads[3].start()
    greet_all(shards)
    for copy in loads[:3]:
        copy.wait()

    @pl.loop(0, tiles)
    def _(i):
        for copy in tile_loads(i):
            copy.wait()
        part = pl.ds(pl.multiple_of(i * tile, tile), tile)
        after_back_body(
            dout.at[part, :], one.at[part, :], two.at[part, :], slope.at[part, :], wo, up, dn, gain_ref,
            dctx.at[part, :],
        )

        @pl.when(i == 0)
        def _():
            await_all(shards)
            to_core.start()

        @pl.when(i == 1)
        def _():
            to_core.wait_recv()

            @pl.loop(0, chips)
            def _(k):
                chip_sum[k] = (parts[k, core].astype(F32) + core_got[k].astype(F32)).astype(BF)

            dense_got[chip] = chip_sum[chip]

            @pl.loop(1, chips)
            def _(k):
                to_chip(k).start()

    loads[3].wait()
    lanes = 2 * (hidden // HEADS)
    pairs = hidden // lanes

    @pl.loop(0, pairs)
    def _(p):
        column = lambda kind: pl.ds(pl.multiple_of((kind * pairs + p) * lanes, lanes), lanes)
        attend_back_body(
            qkv.at[:, column(0)], qkv.at[:, column(1)], qkv.at[:, column(2)], dctx.at[:, column(0)],
            log_ref.at[pl.ds(p, 1)], seg_ref, seg_row_ref, mid_ref, grad.at[column(0), :], dv, edge=edge,
        )

    grad[...] = grad[...] + late_ref[...]
    each = hidden // shards
    piece = lambda peer: grad.at[pl.ds(pl.multiple_of(peer * each, each), each), :]
    grad_got[me] = piece(me)[...]
    spread(piece, grad_got, grad_sems, me, shards)
    others = chip_sum.at[pl.ds(0, chips - 1)]
    every = pltpu.make_async_remote_copy(
        src_ref=others,
        dst_ref=dense_got.at[pl.ds(0, chips - 1)],
        send_sem=dense_sems.at[0],
        recv_sem=dense_sems.at[1],
        device_id=device_of(dict(here, c=1 - core)),
        device_id_type=MESH,
    )
    every.wait_recv()
    every.wait_send()
    to_core.wait_send()
    dense = jnp.zeros((each, hidden), F32)
    for k in range(chips):
        dense = dense + dense_got[k].astype(F32)[:each, :]
    dense_ref[...] = dense
    square = jnp.sum(dense * dense, keepdims=True)
    collect(grad_got, grad_sems, me, shards)
    total = grad_got[0]
    for k in range(1, shards):
        total = total + grad_got[k]
    total_ref[...] = total
    square = square + jnp.sum(total * total, keepdims=True)
    row = lax.broadcasted_iota(jnp.int32, note.shape, 0)
    note[...] = jnp.where(row == 0, facts[...], jnp.where(row == 1, square, 0.0))
    notes[me] = note[...]
    spread(lambda peer: note, notes, note_sems, me, shards)
    collect(notes, note_sems, me, shards)
    sums = notes[0]
    for k in range(1, shards):
        sums = sums + notes[k]
    sums_ref[...] = sums


def update_body(
    sums_ref, dense_ref, total_ref, facts, head_w, head_m, head_v, adapt_w, adapt_m, adapt_v,
    loss_out, norm_out, head_w_out, head_m_out, head_v_out, adapt_w_out, adapt_m_out, adapt_v_out,
):
    norm = jnp.sqrt(sums_ref[1:2, 0:1])
    loss_out[...] = sums_ref[0:1, 0:1]
    norm_out[...] = norm
    factor = jnp.minimum(1.0, clip_limit / (norm + 1e-06))
    fades = facts[1:2, 0:1], facts[2:3, 0:1]
    new = adam(head_w[...], dense_ref[...] * factor, head_m[...], head_v[...], *fades)
    head_w_out[...], head_m_out[...], head_v_out[...] = new
    grad = (total_ref[...] * factor).T
    layers, kinds, rank, unused = adapt_w.shape
    for layer in range(layers):
        for kind in range(kinds):
            at = (layer * kinds + kind) * rank
            new = adam(
                adapt_w[layer, kind], grad[at : at + rank], adapt_m[layer, kind], adapt_v[layer, kind], *fades
            )
            adapt_w_out[layer, kind], adapt_m_out[layer, kind], adapt_v_out[layer, kind] = new


def update(sums, dense, total, facts, heads, adapts):
    whole = pl.BlockSpec(memory_space=pltpu.VMEM)
    shape = jax.ShapeDtypeStruct
    return pl.pallas_call(
        update_body,
        in_specs=[whole] * 10,
        out_specs=[whole] * 8,
        out_shape=[shape((1, 1), F32)] * 2 + [shape(a.shape, F32) for a in (*heads, *adapts)],
        compiler_params=params(),
        name="update",
    )(sums, dense, total, facts, *heads, *adapts)


def finish(back, qkv, logs, seg_wide, seg_row, mid, parts, late, facts, edge, shards):
    dout, one, two, slope, wo, up, dn, gains = back
    parts = parts.reshape(-1, 2, *parts.shape[1:])
    rows, hidden = dout.shape
    each = hidden // shards
    whole = pl.BlockSpec(memory_space=pltpu.VMEM)
    anywhere = pl.BlockSpec(memory_space=pl.ANY)
    shape = jax.ShapeDtypeStruct
    sems = pltpu.SemaphoreType.DMA
    tiles = rows // split_of(rows, BACK_TILE, 16)
    return pl.pallas_call(
        functools.partial(finish_body, shards, edge),
        in_specs=[anywhere] * 8 + [whole] * 8,
        out_specs=[whole] * 3,
        out_shape=[
            shape((8, 128), F32),
            shape((each, hidden), F32),
            shape((each, late.shape[1]), F32),
        ],
        scratch_shapes=[
            pltpu.VMEM((rows, hidden), F32),
            pltpu.VMEM((rows, hidden), F32),
            pltpu.VMEM((rows, hidden), F32),
            pltpu.VMEM(slope.shape, BF),
            pltpu.VMEM(wo.shape, BF),
            slab_scratch(up),
            slab_scratch(dn),
            pltpu.VMEM(qkv.shape, BF),
            pltpu.VMEM((rows, hidden), BF),
            pltpu.VMEM((rows, 2 * (hidden // HEADS)), F32),
            pltpu.VMEM(late.shape, F32),
            pltpu.VMEM((shards // 2, *parts.shape[2:]), BF),
            pltpu.VMEM((shards // 2, *parts.shape[2:]), BF),
            pltpu.VMEM((shards // 2, *parts.shape[2:]), BF),
            pltpu.VMEM((shards, each, late.shape[1]), F32),
            pltpu.VMEM((8, 128), F32),
            pltpu.VMEM((shards, 8, 128), F32),
            sems((4, tiles)),
            sems((4,)),
            sems((2,)),
            sems((2,)),
            sems((2,)),
            sems((2,)),
        ],
        compiler_params=params(collective_id=2, has_side_effects=True),
        name="finish",
    )(dout, one, two, slope, wo, up[0], dn[0], qkv, gains, logs, seg_wide, seg_row, mid, parts, late, facts)


LOG_ROWS = 16


def flip(z, k):
    return (z % 2 + k % 2) % 2 + 2 * ((z // 2 + k // 2) % 2)


def pack_log(log_row, rows):
    high = log_row.astype(BF).astype(F32)
    middle = (log_row - high).astype(BF).astype(F32)
    low = log_row - high - middle
    row = lax.broadcasted_iota(jnp.int32, (rows, log_row.shape[1]), 0)
    return jnp.where(
        row == 0, high, jnp.where(row == 1, middle, jnp.where(row == 2, low, 0.0))
    ).astype(BF)


def unpack(block, hidden):
    logs = block[hidden : hidden + LOG_ROWS, :].astype(F32)
    return block[:hidden, :].astype(F32), jnp.sum(logs, 0, keepdims=True)


def merged(one, two):
    top = jnp.maximum(one[1], two[1])
    first, second = jnp.exp(one[1] - top), jnp.exp(two[1] - top)
    total = first + second
    inverse = 1.0 / total
    return one[0] * (first * inverse) + two[0] * (second * inverse), top + jnp.log(total)


def store_packed(ref, pair, hidden):
    ref[:hidden, :] = pair[0].astype(BF)
    ref[hidden : hidden + LOG_ROWS, :] = pack_log(pair[1], LOG_ROWS)


def head_body(
    u_ref, bias_ref, table_any, et_any, mean_ref, log_ref,
    e_ref, et_ref, bias_wide, feats, packs, handed, sums,
    loads, far_send, far_get, hand_send, hand_get, part_send, part_get, sum_send, sum_get,
):
    here = position()
    x, y, c = here["x"], here["y"], here["c"]
    labels, hidden = u_ref.shape
    sibling = device_of(dict(here, c=1 - c))

    def chip_at(k):
        return (x + k % 2) % 2, (y + k // 2) % 2

    def device_at(k):
        there = chip_at(k)
        return device_of(dict(here, x=there[0], y=there[1]))

    def slot(k, core):
        there = chip_at(k)
        return (there[0] * 2 + there[1]) * 2 + core

    fills = [
        pltpu.make_async_copy(source, target, loads.at[k])
        for k, (source, target) in enumerate(
            ((vocab_rows(table_any, e_ref), e_ref), (et_any, et_ref))
        )
    ]
    for fill in fills:
        fill.start()
    barrier = pltpu.get_barrier_semaphore()
    for target in (sibling, *[device_at(k) for k in (1, 2, 3)]):
        pl.semaphore_signal(barrier, inc=1, device_id=target, device_id_type=MESH)
    feats[slot(0, c)] = u_ref[...]
    pl.semaphore_wait(barrier, 4)

    def move(place, device, send, get):
        return pltpu.make_async_remote_copy(
            src_ref=feats.at[place],
            dst_ref=feats.at[place],
            send_sem=send,
            recv_sem=get,
            device_id=device,
            device_id_type=MESH,
        )

    def far(k):
        return move(slot(0, c), device_at(k), far_send.at[k], far_get.at[k])

    def far_here(k):
        return move(slot(k, c), device_at(k), far_send.at[k], far_get.at[k])

    def hand(k, core):
        return move(slot(k, core), sibling, hand_send.at[k], hand_get.at[k])

    for k in (1, 2, 3):
        far(k).start()
    hand(0, c).start()

    @pl.loop(0, bias_ref.shape[0])
    def _(b):
        row = jnp.broadcast_to(bias_ref[pl.ds(b, 1), :], (128, 128))
        bias_wide[pl.ds(pl.multiple_of(b * 128, 128), 128), :] = row.T

    for k in (1, 2, 3):
        far_here(k).wait_recv()
        hand(k, c).start()
    for fill in fills:
        fill.wait()
    count = e_ref.shape[0]
    steps = 4

    def target_of(s):
        return (s + 1) % steps

    def hand_part(s):
        return pltpu.make_async_remote_copy(
            src_ref=packs.at[s, 1 - c],
            dst_ref=handed.at[s],
            send_sem=part_send.at[s],
            recv_sem=part_get.at[s],
            device_id=sibling,
            device_id_type=MESH,
        )

    def sum_part(s):
        return pltpu.make_async_remote_copy(
            src_ref=packs.at[s, c],
            dst_ref=sums.at[s],
            send_sem=sum_send.at[s],
            recv_sem=sum_get.at[s],
            device_id=device_at(target_of(s)),
            device_id_type=MESH,
        )

    def together(s):
        hand_part(s).wait_recv()
        return merged(unpack(packs[s, c], hidden), unpack(handed[s], hidden))

    def settle(s):
        store_packed(packs.at[s, c], together(s), hidden)
        sum_part(s).start()

    @pl.loop(0, steps)
    def _(s):
        k = target_of(s)
        hand(k, 1 - c).wait_recv()
        u = feats[pl.ds(slot(k, 0), 2)].reshape(2 * labels, hidden)
        top = total = mean = None

        def scored(start):
            part = slice(start, min(start + 1280, count))
            bias = bias_wide[part, :]
            return mm_nt(e_ref[part, :], u) + jnp.concatenate([bias, bias], 1)

        @pl.when(s > 0)
        def _():
            settle(s - 1)

        logits = scored(0)
        for start in range(0, count, 1280):
            part = slice(start, min(start + 1280, count))
            later = scored(start + 1280) if start + 1280 < count else None
            high = jnp.max(logits, 0, keepdims=True)
            new = high if top is None else jnp.maximum(top, high)
            grown = jnp.exp(logits - new)
            part_sums = jnp.sum(grown, 0, keepdims=True)
            product = mm(et_ref[:, part], grown.astype(BF))
            if top is None:
                total, mean = part_sums, product
            else:
                shrink = jnp.exp(top - new)
                total, mean = total * shrink + part_sums, mean * shrink + product
            top = new
            logits = later
        mean = mean * (1.0 / total)
        logs = top + jnp.log(total)
        for core in range(2):
            half = slice(core * labels, (core + 1) * labels)
            packs[s, core, :hidden, :] = mean[:, half].astype(BF)
            packs[s, core, hidden : hidden + LOG_ROWS, :] = pack_log(logs[:, half], LOG_ROWS)
        hand_part(s).start()

    total = together(steps - 1)
    for s in range(steps - 1):
        sum_part(s).wait_recv()
        total = merged(total, unpack(sums[s], hidden))
    mean_ref[...] = total[0]
    log_ref[...] = total[1]
    for k in (1, 2, 3):
        far(k).wait_send()
    for k in range(4):
        hand(k, c).wait_send()
    for s in range(steps):
        hand_part(s).wait_send()
    for s in range(steps - 1):
        sum_part(s).wait_send()


def head(u, bias, table, et):
    labels, hidden = u.shape
    whole = pl.BlockSpec(memory_space=pltpu.VMEM)
    anywhere = pl.BlockSpec(memory_space=pl.ANY)
    shape = jax.ShapeDtypeStruct
    sems = pltpu.SemaphoreType.DMA
    block = (hidden + LOG_ROWS, labels)
    count = et.shape[1]
    return pl.pallas_call(
        head_body,
        in_specs=[whole] * 2 + [anywhere] * 2,
        out_specs=[whole] * 2,
        out_shape=[shape((hidden, labels), F32), shape((1, labels), F32)],
        scratch_shapes=[
            pltpu.VMEM((count, hidden), BF),
            pltpu.VMEM((hidden, count), BF),
            pltpu.VMEM((count, 128), F32),
            pltpu.VMEM((8, labels, hidden), BF),
            pltpu.VMEM((4, 2, *block), BF),
            pltpu.VMEM((4, *block), BF),
            pltpu.VMEM((4, *block), BF),
            sems((2,)),
        ]
        + [sems((4,))] * 8,
        compiler_params=params(collective_id=4, has_side_effects=True),
        name="head",
    )(u, bias, table, et)


def seg_positions(segments):
    index = jnp.arange(segments.shape[-1], dtype=jnp.int32)
    fresh = jnp.concatenate([jnp.ones((1,), dtype=bool), segments[1:] != segments[:-1]], -1)
    starts = lax.cummax(jnp.where(fresh, index, jnp.zeros_like(index)), axis=0)
    return index - starts


def pad_rows(matrix, multiple):
    return jnp.pad(matrix, ((0, -matrix.shape[0] % multiple), (0, 0)))


def slab_of(gathered, start, rows):
    if rows % 16 == 0 and start % rows == 0:
        return (gathered, start // rows, rows)
    part = gathered[:, start : start + rows].reshape(1, -1, gathered.shape[2])
    return (part, 0, part.shape[1])


def per_device(
    input_token_index,
    sentence_numbers,
    label_positions,
    label_target_token,
    sequence_task_index,
    task_loss_weight,
    optimizer_step_count,
    embed,
    position_embedding,
    norm_gain_vector,
    norm_bias_vector,
    attention_in_weight,
    attention_out_weight,
    feedforward_up,
    feedforward_down,
    layer_bias_vector,
    head_dense_bias,
    vocabulary_bias,
    adapter_down_matrix,
    adapter_up_matrix,
    adapter_moment_first,
    adapter_moment_second,
    head_projection,
    head_moment_first,
    head_moment_second,
):
    shards = lax.axis_size("dp") * lax.axis_size("fsdp")
    dp_index = lax.axis_index("dp")
    fsdp_index = lax.axis_index("fsdp")
    layers, unused, rank, up_part = adapter_up_matrix.shape
    hidden = embed.shape[1]
    tokens = input_token_index.shape[1]
    labels = label_positions.shape[1]
    qkv_rows = attention_in_weight.shape[2]
    out_rows = attention_out_weight.shape[2]
    ff_rows = feedforward_up.shape[2]
    head_rows = head_projection.shape[0]

    grouped = (lax.axis_size("dp"), lax.axis_size("fsdp")) == (2, 16)
    feeds = [[feedforward_up[layer].T, feedforward_down[layer]] for layer in range(layers)]
    attends = [[attention_in_weight[layer].T, attention_out_weight[layer].T] for layer in range(layers)]
    first_in = lax.all_gather(
        jnp.concatenate([feeds[0][0], *attends[0]], 0), BOTH, axis=0, tiled=False
    )
    feed_chunk = feeds[0][1]
    last_chunk = pad_rows(
        jnp.concatenate([feeds[1][0], *attends[1], head_projection.astype(BF)], 0), 32
    )
    last_feed = feeds[1][1]

    table_rows = embed.shape[0]
    wanted = jnp.concatenate([input_token_index[0], label_target_token[0]])
    dp_count = lax.axis_size("dp")
    group_ids = lax.all_gather(wanted, "dp", axis=0, tiled=False) - dp_index * table_rows
    inside = (group_ids >= 0) & (group_ids < table_rows)
    group_ids = jnp.clip(group_ids, 0, table_rows - 1)
    mine = lax.dynamic_index_in_dim(inside, dp_index, 0, keepdims=False)

    task_range = jnp.arange(TASKS, dtype=jnp.int32)
    slice_rows = vocabulary_bias.shape[0]
    ups = adapter_up_matrix.reshape(-1)
    if grouped:
        ids_of = lambda part: lax.dynamic_index_in_dim(group_ids, part, 0, keepdims=False)
        other_rows = look_up(ids_of(1 - dp_index), embed)
        got = lax.ppermute(other_rows, "dp", [(0, 1), (1, 0)])
        own_ids, other_rows = lax.optimization_barrier((ids_of(dp_index), other_rows))
        own_rows = look_up(own_ids, embed)
        fact = jnp.concatenate([vocabulary_bias, ups, sequence_task_index.astype(F32)])
        fact_rows = -(-fact.size // 1024) * 8
        facts, feed_full, own_turned = start_exchange(
            jnp.pad(fact, (0, fact_rows * 128 - fact.size)).reshape(fact_rows, 128),
            feed_chunk,
            embed,
            shards,
        )
        last_feed, facts = lax.optimization_barrier((last_feed, facts))
        facts = facts.reshape(shards, -1)
        all_bias = facts[:, :slice_rows].reshape(-1)
        every_up = facts[:, slice_rows : slice_rows + ups.size]
        every_task = facts[:, slice_rows + ups.size].astype(jnp.int32)
    else:
        looked = jnp.where(
            inside.reshape(-1)[:, None], embed[group_ids.reshape(-1)], jnp.zeros((), BF)
        )
        own_rows = got = lax.psum_scatter(looked, "dp", scatter_dimension=0, tiled=True)
        all_bias = lax.all_gather(vocabulary_bias, BOTH, axis=0, tiled=True)
        every_up = lax.all_gather(ups, BOTH, axis=0, tiled=False)
        every_task = lax.all_gather(sequence_task_index, BOTH, axis=0, tiled=True)
    counts = labels * jnp.sum((every_task[:, None] == task_range[None, :]).astype(F32), 0)
    task_hot = (sequence_task_index[:, None] == task_range[None, :]).astype(F32)
    row_weight = jnp.sum(task_hot[0] * (task_loss_weight / jnp.maximum(counts, 1.0)))
    ups_full = (
        every_up.astype(BF)
        .reshape(shards, layers, 2, rank, up_part)
        .transpose(1, 2, 3, 0, 4)
        .reshape(layers, 2, rank, hidden)
    )
    blank = jnp.zeros((rank, hidden), BF)
    spare = lambda rows: jnp.zeros((rows, 3 * hidden), BF)
    adapters = jnp.stack(
        [
            jnp.concatenate(
                [
                    spare(2 * rank * layer),
                    jnp.concatenate([2 * ups_full[layer, 0], blank, blank], 1),
                    jnp.concatenate([blank, blank, 2 * ups_full[layer, 1]], 1),
                    spare(128 - 2 * rank * (layer + 1)),
                ],
                0,
            )
            for layer in range(layers)
        ]
    )
    downs = jnp.stack(
        [
            jnp.pad(
                jnp.concatenate([adapter_down_matrix[layer, 0], adapter_down_matrix[layer, 1]], 1),
                ((0, 0), (2 * rank * layer, 128 - 2 * rank * (layer + 1))),
            )
            for layer in range(layers)
        ]
    )
    target_rows = jnp.where(mine[tokens:, None], own_rows[tokens:], got[tokens:])
    segments = sentence_numbers[0]
    code = (2 * seg_positions(segments) + mine[:tokens].astype(jnp.int32))[:, None]
    seg_real = segments.astype(F32)
    seg_wide = jnp.broadcast_to(seg_real[:, None], (tokens, 128))
    seg_row = seg_real[None, :]
    place_row = label_positions
    place_col = jnp.broadcast_to(label_positions.reshape(labels, 1), (labels, 128))

    target_bias = all_bias[label_target_token[0]]

    gains, shifts = norm_gain_vector, norm_bias_vector
    last_inputs = (place_col, place_row, seg_wide, downs, adapters, layer_bias_vector)
    in_start = ff_rows
    last_dn = lax.all_gather(last_feed, BOTH, axis=0, tiled=False)
    slabs_of = lambda up_full, dn_full: (slab_of(up_full, 0, ff_rows), slab_of(dn_full, 0, ff_rows))
    if grouped:
        more = (
            code, position_embedding, gains, shifts, downs, adapters, layer_bias_vector, seg_wide, seg_row,
        )
        qkv, x_last, one, two, slope, out_first, last_full, mid, logs = first_layer(
            own_rows, got, first_in, feed_full, last_chunk, more, shards
        )
        slabs = [slabs_of(first_in, feed_full), slabs_of(last_full, last_dn)]
        *saved, in_last, out_last, head_full = last_forward(
            x_last, *last_inputs, (last_full,), (in_start, in_start + qkv_rows + out_rows), *slabs[1], gains,
            shifts, head_dense_bias[None, :],
        )
        count = own_turned.shape[1]
        own_bias = lax.dynamic_slice_in_dim(
            all_bias, dp_index * table_rows + fsdp_index % 4 * count, count, 0
        ).reshape(-1, 128)
        mean_t, own_logs = head(saved[-1], own_bias, embed, own_turned)
    else:
        feed_full = lax.all_gather(feed_chunk, BOTH, axis=0, tiled=False)
        last_full = lax.all_gather(last_chunk, BOTH, axis=0, tiled=False)
        slabs = [slabs_of(first_in, feed_full), slabs_of(last_full, last_dn)]
        taken = lambda full_chunk, start, size: full_chunk[:, start : start + size].reshape(-1, hidden)
        in_first = taken(first_in, ff_rows, qkv_rows)
        out_first = taken(first_in, ff_rows + qkv_rows, out_rows)
        in_last = taken(last_full, in_start, qkv_rows)
        out_last = taken(last_full, in_start + qkv_rows, out_rows)
        head_full = taken(last_full, in_start + qkv_rows + out_rows, head_rows)
        qkv, mid, hidden_rows = project(
            own_rows, got, code, position_embedding, gains, shifts, downs, in_first, adapters, layer_bias_vector
        )
        context, logs = attend(qkv, seg_wide, seg_row)
        x_last, one, two, slope = after(
            context, hidden_rows, out_first, *slabs[0], layer_bias_vector, gains, shifts
        )
        saved = last_forward(
            x_last, *last_inputs, (in_last, out_last, head_full), None, *slabs[1], gains, shifts,
            head_dense_bias[None, :],
        )
        features = saved[-1]
        own_slice = lax.dynamic_slice_in_dim(embed, fsdp_index * slice_rows, slice_rows, 0)
        own_vocab = jnp.concatenate(
            [own_slice]
            + [
                lax.ppermute(
                    own_slice, "dp", [(k, (k + shift) % dp_count) for k in range(dp_count)]
                )
                for shift in range(1, dp_count)
            ],
            0,
        )
        own_bias = jnp.concatenate(
            [
                lax.dynamic_slice_in_dim(
                    all_bias,
                    ((dp_index - shift) % dp_count) * table_rows + fsdp_index * slice_rows,
                    slice_rows,
                    0,
                )
                for shift in range(dp_count)
            ]
        )
        bias_wide = jnp.broadcast_to(own_bias[:, None], (own_bias.shape[0], 128))
        every = lax.all_gather(features, "fsdp", axis=0, tiled=True)
        means, local_logs = vocab(every, own_vocab, own_vocab.T, bias_wide, labels)
        local_logs = local_logs.reshape(-1, labels)
        all_logs = lax.all_gather(local_logs, "fsdp", axis=0, tiled=False)
        whole_logs = jax.nn.logsumexp(all_logs, axis=0)
        scaled = (means * jnp.exp(local_logs - whole_logs)[:, None, :]).astype(BF)
        mean_t = lax.psum_scatter(scaled, "fsdp", scatter_dimension=0, tiled=True)[0].astype(F32)
        own_logs = lax.dynamic_index_in_dim(whole_logs, fsdp_index, 0, keepdims=False)
        own_logs = own_logs[None, :]

    step_as_real = optimizer_step_count[0].astype(F32)
    fades = (1.0 - beta_first**step_as_real, 1.0 - beta_second**step_as_real)
    lanes = lambda value: jnp.pad(
        jnp.broadcast_to(value, (1, value.size if value.ndim else 128)), ((0, 0), (0, 128))
    )[:, :128]
    facts = jnp.concatenate(
        [lanes(value) for value in (row_weight, *fades, target_bias)] + [jnp.zeros((4, 128), F32)]
    )
    hidden_grad, dense_gradient, late, facts = last_backward(
        mean_t, own_logs, target_rows, facts, saved, place_col, place_row, seg_wide, downs, in_last, adapters,
        out_last, *slabs[1], gains, head_full, 3 * rank, shards if grouped else None,
    )
    back = (hidden_grad, one, two, slope, out_first, *slabs[0], gains)
    adapts = (adapter_up_matrix, adapter_moment_first, adapter_moment_second)
    heads = (head_projection, head_moment_first, head_moment_second)
    if grouped:
        sums, dense_portion, adapter_portion = finish(
            back, qkv, logs, seg_wide, seg_row, mid, dense_gradient, late, facts, rank, shards
        )
        loss, norm, *new = update(sums, dense_portion, adapter_portion, facts, heads, adapts)
        return (loss[0, 0], norm[0, 0], *new[3:], *new[:3])
    dctx = after_back(*back)
    first = attend_back(qkv, dctx, logs, seg_wide, seg_row, mid, rank)
    adapter_gradient = (first + late)[:, : 2 * rank * layers].T.reshape(layers, 2, rank, hidden)
    dense_portion = lax.psum_scatter(dense_gradient, BOTH, scatter_dimension=0, tiled=True)
    adapter_portion = lax.psum_scatter(adapter_gradient, BOTH, scatter_dimension=3, tiled=True)
    squared_entries = jnp.sum(adapter_portion * adapter_portion) + jnp.sum(dense_portion * dense_portion)
    masked_task_loss, norm_square = lax.psum((facts[0, 0], squared_entries), BOTH)
    gradient_norm = jnp.sqrt(norm_square)
    factor = jnp.minimum(1.0, clip_limit / (gradient_norm + 1e-06))
    adapter_new = adam(adapts[0], adapter_portion * factor, *adapts[1:], *fades)
    dense_new = adam(heads[0], dense_portion * factor, *heads[1:], *fades)
    return (masked_task_loss, gradient_norm, *adapter_new, *dense_new)


def solution(mesh):
    rows = P(BOTH, None)
    in_specs = (
        rows,
        rows,
        rows,
        rows,
        P(BOTH),
        P(),
        P(),
        P("dp", None),
        P(),
        P(),
        P(),
        P(None, None, BOTH),
        P(None, None, BOTH),
        P(None, None, BOTH),
        P(None, BOTH, None),
        P(),
        P(),
        P(BOTH),
        P(),
        P(None, None, None, BOTH),
        P(None, None, None, BOTH),
        P(None, None, None, BOTH),
        rows,
        rows,
        rows,
    )
    adapter = P(None, None, None, BOTH)
    out_specs = (P(), P(), adapter, adapter, adapter, rows, rows, rows)
    return jax.shard_map(
        per_device, mesh=mesh, in_specs=in_specs, out_specs=out_specs, check_vma=False
    )
```

```python
import functools

import jax
import jax.numpy as jnp
from jax import lax
from jax.experimental import pallas as pl
from jax.experimental.pallas import tpu as pltpu
from jax.sharding import PartitionSpec as P

HEADS = 12
TASKS = 4
REACH = 128

norm_eps = 1e-05
adapter_scale = 2.0
clip_limit = 0.01
learn_rate = 0.05
beta_first = 0.9
beta_second = 0.999
adam_eps = 1e-08
decay_rate = 0.01
masked_score = -1e30

BF = jnp.bfloat16
F32 = jnp.float32
BOTH = ("dp", "fsdp")
VMEM_BYTES = 60 * 1024 * 1024


def mm(a, b):
    return lax.dot_general(a, b, (((1,), (0,)), ((), ())), preferred_element_type=F32)


def mm_nt(a, b):
    return lax.dot_general(a, b, (((1,), (1,)), ((), ())), preferred_element_type=F32)


def mm_tn(a, b):
    return lax.dot_general(a, b, (((0,), (0,)), ((), ())), preferred_element_type=F32)


def layer_norm(rows_in, gain, shift):
    center = rows_in - jnp.mean(rows_in, -1, keepdims=True)
    spread = jnp.mean(center * center, -1, keepdims=True)
    return center * lax.rsqrt(spread + norm_eps) * gain + shift


def norm_back(rows_in, gain, gradient):
    center = rows_in - jnp.mean(rows_in, -1, keepdims=True)
    inverse = lax.rsqrt(jnp.mean(center * center, -1, keepdims=True) + norm_eps)
    unit = center * inverse
    scaled = gradient * gain
    return inverse * (
        scaled
        - jnp.mean(scaled, -1, keepdims=True)
        - unit * jnp.mean(scaled * unit, -1, keepdims=True)
    )


def gelu_pair(v):
    size = jnp.abs(v) * 0.7071067811865476
    base = 1.0 + 0.3275911 * size
    t = pl.reciprocal(base, approx=True)
    t = t * (2.0 - base * t)
    bell = jnp.exp(-0.5 * v * v)
    poly = t * (
        0.127414796 + t * (-0.142248368 + t * (0.7107068705 + t * (-0.7265760135 + t * 0.5307027145)))
    )
    tail = poly * bell
    phi = jnp.where(v >= 0.0, 1.0 - tail, tail)
    return v * phi, phi + v * (bell * 0.3989422804014327)


def params(**more):
    return pltpu.CompilerParams(vmem_limit_bytes=VMEM_BYTES, **more)


def full(shape):
    return pl.BlockSpec(shape, lambda *_: (0,) * len(shape))


def split_of(total, most, step):
    size = (min(most, total) // step) * step
    while size > step and total % size:
        size -= step
    return size if size and total % size == 0 else total


def pair_rows(block, width):
    first = lax.broadcasted_iota(jnp.int32, block.shape, 1) < width
    return jnp.concatenate([jnp.where(first, block, 0.0), jnp.where(first, 0.0, block)], 0).astype(BF)


def pair_join(wide, width):
    rows = wide.shape[1] // 2
    return jnp.concatenate([wide[:width, :rows], wide[width:, rows:]], 0)


def masked(scores, same):
    rows = scores.shape[1] // 2
    return jnp.concatenate(
        [
            jnp.where(same, scores[:, :rows], masked_score),
            jnp.where(same, scores[:, rows:], masked_score),
        ],
        1,
    )


def qkv_bias(bias_ref, layer, start, size):
    hidden = bias_ref.shape[1] // 8
    if start >= 2 * hidden:
        return bias_ref[layer : layer + 1, start - hidden : start - hidden + size]
    return bias_ref[layer : layer + 1, start : start + size] if start < hidden else 0.0


def norm_of(norm_refs, k):
    return norm_refs[0][k : k + 1, :], norm_refs[1][k : k + 1, :]


def project_body(
    own_ref, got_ref, code_ref, spots_ref, gain_ref, shift_ref, down_ref, w_ref, up_ref, bias_ref,
    out_ref, mid_ref, x_ref,
):
    mine = code_ref[...] % 2
    choose = (
        lax.broadcasted_iota(jnp.int32, (own_ref.shape[0], spots_ref.shape[0]), 1) == code_ref[...] // 2
    )
    summed = jnp.where(
        mine > 0, own_ref[...].astype(F32), got_ref[...].astype(F32)
    ) + mm(choose.astype(F32).astype(BF), spots_ref[...])
    x = layer_norm(summed, *norm_of((gain_ref, shift_ref), 0))
    x_ref[...] = x
    low = x.astype(BF)
    mid = mm(low, down_ref[0]).astype(BF)
    mid_ref[...] = mid
    total = w_ref.shape[0]
    step = total // 3
    for start in range(0, total, step):
        part = slice(start, start + step)
        out_ref[:, part] = (
            mm_nt(low, w_ref[part, :]) + mm(mid, up_ref[0, :, part]) + qkv_bias(bias_ref, 0, start, step)
        ).astype(BF)


def project(own, got, code, spots, gains, shifts, down, w, up, bias, rows):
    width = own.shape[1]
    tile = split_of(rows, 256, 16)
    total = w.shape[0]
    row = lambda n: pl.BlockSpec((tile, n), lambda i: (i, 0))
    return pl.pallas_call(
        project_body,
        grid=(rows // tile,),
        in_specs=[row(width), row(width), row(1)]
        + [full(a.shape) for a in (spots, gains, shifts, down, w, up, bias)],
        out_specs=[row(total), row(down.shape[2]), row(width)],
        out_shape=[
            jax.ShapeDtypeStruct((rows, total), BF),
            jax.ShapeDtypeStruct((rows, down.shape[2]), BF),
            jax.ShapeDtypeStruct((rows, width), F32),
        ],
        compiler_params=params(),
        name="project",
    )(own, got, code, spots, gains, shifts, down, w, up, bias)


def attend_body(q_ref, k_ref, v_ref, seg_ref, seg_row_ref, ctx_ref, log_ref):
    rows = q_ref.shape[0]
    width = q_ref.shape[1] // 2
    scale = width**-0.5
    turned = turn_blocks(v_ref)

    def scored(start):
        own, near = reach_of(start, rows)
        return mm_nt(k_ref[near, :], pair_rows(q_ref[own, :].astype(F32) * scale, width))

    scores = scored(0)
    for start in range(0, rows, REACH):
        own, near = reach_of(start, rows)
        later = scored(start + REACH) if start + REACH < rows else None
        same = seg_ref[near, :] == seg_row_ref[:, own]
        scores = masked(scores, same)
        top = jnp.max(scores, 0, keepdims=True)
        weights = jnp.exp(scores - top)
        total = jnp.sum(weights, 0, keepdims=True)
        context = mm(turned[:, near], weights.astype(BF)) * (1.0 / total)
        ctx_ref[own, :] = pair_join(context, width).T.astype(BF)
        log_ref[0, :, 2 * start : 2 * start + 2 * REACH] = top + jnp.log(total)
        scores = later


def reach_of(start, rows):
    return slice(start, start + REACH), slice(max(0, start - REACH), min(rows, start + 2 * REACH))


def turn_blocks(ref):
    blocks = [ref[k : k + 128, :].astype(F32).T.astype(BF) for k in range(0, ref.shape[0], 128)]
    return jnp.concatenate(blocks, 1)


def attend(qkv, seg_wide, seg_row):
    rows, total = qkv.shape
    hidden = total // 3
    lanes = 2 * (hidden // HEADS)
    pairs = hidden // lanes
    column = lambda kind: pl.BlockSpec((rows, lanes), lambda p: (0, kind * pairs + p))
    return pl.pallas_call(
        attend_body,
        grid=(pairs,),
        in_specs=[column(0), column(1), column(2), full(seg_wide.shape), full(seg_row.shape)],
        out_specs=[
            pl.BlockSpec((rows, lanes), lambda p: (0, p)),
            pl.BlockSpec((1, 1, 2 * rows), lambda p: (p, 0, 0)),
        ],
        out_shape=[
            jax.ShapeDtypeStruct((rows, hidden), BF),
            jax.ShapeDtypeStruct((pairs, 1, 2 * rows), F32),
        ],
        compiler_params=params(),
        name="attend",
    )(qkv, qkv, qkv, seg_wide, seg_row)


def flat(ref):
    whole = ref[...]
    return whole.reshape(-1, whole.shape[-1])


def rows_of(ref, start, size):
    each = ref.shape[1]
    if size % each == 0 and start % each == 0 and each % 16 == 0:
        part = ref[start // each : (start + size) // each, :, :]
        return part.reshape(size, part.shape[-1])
    return flat(ref)[start : start + size, :]


def feed_step(ref):
    units = ref.shape[0] * ref.shape[1]
    step = ref.shape[1]
    while units % (2 * step) == 0 and 2 * step <= 768 and ref.shape[0] > 1:
        step *= 2
    return units, (step if ref.shape[0] > 1 else split_of(units, 768, 128))


def later_biases(bias_ref, layer):
    hidden = bias_ref.shape[1] // 8
    row = bias_ref[layer : layer + 1, :]
    return row[:, 2 * hidden : 3 * hidden], row[:, 3 * hidden : 7 * hidden], row[:, 7 * hidden :]


def after_body(
    ctx_ref, x_ref, wo_ref, up_ref, down_ref, bias_ref, gain_ref, shift_ref,
    out_ref, one_ref, two_ref, slope_ref,
):
    bo, b1, b2 = later_biases(bias_ref, 0)
    one = x_ref[...] + (mm_nt(ctx_ref[...], wo_ref[...]) + bo)
    one_ref[...] = one
    middle = layer_norm(one, *norm_of((gain_ref, shift_ref), 1))
    low = middle.astype(BF)
    total = middle + b2
    units, step = feed_step(up_ref)
    gate = mm_nt(low, rows_of(up_ref, 0, step))
    for start in range(0, units, step):
        part = slice(start, start + step)
        later = mm_nt(low, rows_of(up_ref, start + step, step)) if start + step < units else None
        act, slope = gelu_pair(gate + b1[:, part])
        slope_ref[:, part] = slope.astype(BF)
        total = total + mm(act.astype(BF), rows_of(down_ref, start, step))
        gate = later
    two_ref[...] = total
    out_ref[...] = layer_norm(total, *norm_of((gain_ref, shift_ref), 2))


def slab_spec(slab):
    array, place, rows = slab
    return pl.BlockSpec((array.shape[0], rows, array.shape[2]), lambda *_: (0, place, 0))


def after(ctx, x, wo, up, down, bias, gains, shifts):
    rows, width = x.shape
    tile = split_of(rows, 256, 16)
    units = 4 * width
    row = lambda n: pl.BlockSpec((tile, n), lambda i: (i, 0))
    return pl.pallas_call(
        after_body,
        grid=(rows // tile,),
        in_specs=[row(width), row(width), full(wo.shape), slab_spec(up), slab_spec(down)]
        + [full(a.shape) for a in (bias, gains, shifts)],
        out_specs=[row(width), row(width), row(width), row(units)],
        out_shape=[jax.ShapeDtypeStruct((rows, width), F32)] * 3
        + [jax.ShapeDtypeStruct((rows, units), BF)],
        compiler_params=params(),
        name="after",
    )(ctx, x, wo, up[0], down[0], bias, gains, shifts)


def exact_rows(choose, matrix):
    high = matrix.astype(BF)
    rest = matrix - high.astype(F32)
    middle = rest.astype(BF)
    low = (rest - middle.astype(F32)).astype(BF)
    return mm(choose, high) + mm(choose, middle) + mm(choose, low)


def unpack_rows(slab_ref, targets):
    shards = slab_ref.shape[0]

    @pl.loop(0, shards // 2)
    def _(k):
        first, second = slab_ref[2 * k].astype(F32), slab_ref[2 * k + 1].astype(F32)
        at = 0
        for target in targets:
            each = target.shape[0] // shards
            both = jnp.concatenate([first[at : at + each], second[at : at + each]], 0)
            target[pl.ds(pl.multiple_of(2 * each * k, 2 * each), 2 * each), :] = both.astype(BF)
            at += each


def last_forward_body(
    x_ref, place_ref, place_row_ref, seg_ref, down_ref, adapt_ref, bias_ref, weights_any, up_any, dn_any,
    gain_ref, shift_ref, hbias_ref,
    kv_ref, q_ref, mid_ref, log_ref, one_ref, slope_ref, two_ref, low_ref, act_ref, hslope_ref, feat_ref, *more,
    places, starts,
):
    copies = []
    if starts is None:
        up_ref, dn_ref, ctx_ref, w_ref, wo_ref, hb_ref, sems = more
        sources = zip(weights_any, (w_ref, wo_ref, hb_ref))
    else:
        w_out, wo_out, hb_out, up_ref, dn_ref, ctx_ref, w_ref, wo_ref, hb_ref, in_slab, hb_slab, sems = more
        sources = [
            (weights_any[0].at[:, pl.ds(start, slab.shape[1]), :], slab)
            for start, slab in zip(starts, (in_slab, hb_slab))
        ]
    for source, target in sources:
        copies.append((source, target))
    early = len(copies)
    for source, target, place in ((up_any, up_ref, places[0]), (dn_any, dn_ref, places[1])):
        each = target.shape[1]
        copies.append((source.at[:, pl.ds(place * each, each), :], target))
    copies = [pltpu.make_async_copy(*ends, sems.at[k]) for k, ends in enumerate(copies)]
    for copy in copies:
        copy.start()
    for copy in copies[:early]:
        copy.wait()
    copies = copies[early:]
    if starts is not None:
        unpack_rows(in_slab, (w_ref, wo_ref))
        unpack_rows(hb_slab, (hb_ref,))
        for k, ends in enumerate(((w_ref, w_out), (wo_ref, wo_out), (hb_ref, hb_out))):
            copies.append(pltpu.make_async_copy(*ends, sems.at[4 + k]))
            copies[-1].start()
    rows, hidden = x_ref.shape
    labels = place_ref.shape[0]
    lanes = 2 * (hidden // HEADS)
    width = lanes // 2
    low = x_ref[...].astype(BF)
    mid = mm(low, down_ref[1]).astype(BF)
    mid_ref[...] = mid
    step = split_of(hidden, 768, 128)
    for start in range(hidden, 3 * hidden, step):
        part = slice(start, start + step)
        kv_ref[:, start - hidden : start - hidden + step] = (
            mm_nt(low, w_ref[part, :]) + mm(mid, adapt_ref[1, :, part]) + qkv_bias(bias_ref, 1, start, step)
        ).astype(BF)
    choose = (
        lax.broadcasted_iota(jnp.int32, (labels, rows), 1) == place_ref[...][:, 0:1]
    ).astype(F32).astype(BF)
    own = exact_rows(choose, x_ref[...])
    own_low = own.astype(BF)
    own_mid = mm(choose, mid).astype(BF)
    q_ref[...] = (
        mm_nt(own_low, w_ref[:hidden, :])
        + mm(own_mid, adapt_ref[1, :, :hidden])
        + qkv_bias(bias_ref, 1, 0, hidden)
    ).astype(BF)
    seg = seg_ref[...]
    seg_own = jnp.sum(
        jnp.where(
            lax.broadcasted_iota(jnp.int32, (rows, labels), 0) == place_row_ref[...], seg, 0.0
        ),
        0,
        keepdims=True,
    )
    same = seg == seg_own

    def scored(p):
        part = slice(p * lanes, (p + 1) * lanes)
        return mm_nt(kv_ref[:, part], pair_rows(q_ref[:, part].astype(F32) * width**-0.5, width))

    later = scored(0)
    for p in range(hidden // lanes):
        part = slice(p * lanes, (p + 1) * lanes)
        scores = masked(later, same)
        later = scored(p + 1) if (p + 1) * lanes < hidden else None
        top = jnp.max(scores, 0, keepdims=True)
        weights = jnp.exp(scores - top)
        total = jnp.sum(weights, 0, keepdims=True)
        context = mm_tn(
            kv_ref[:, hidden + p * lanes : hidden + (p + 1) * lanes], weights.astype(BF)
        ) * (1.0 / total)
        ctx_ref[:, part] = pair_join(context, width).T.astype(BF)
        log_ref[p : p + 1, :] = top + jnp.log(total)
    bo, b1, b2 = later_biases(bias_ref, 1)
    norms = (gain_ref, shift_ref)
    one = own + (mm_nt(ctx_ref[...], wo_ref[...]) + bo)
    one_ref[...] = one
    middle = layer_norm(one, *norm_of(norms, 3))
    middle_low = middle.astype(BF)
    sum_two = middle + b2
    units, step = feed_step(up_ref)
    for copy in copies:
        copy.wait()
    gate = mm_nt(middle_low, rows_of(up_ref, 0, step))
    for start in range(0, units, step):
        part = slice(start, start + step)
        later = mm_nt(middle_low, rows_of(up_ref, start + step, step)) if start + step < units else None
        act, slope = gelu_pair(gate + b1[:, part])
        gate = later
        slope_ref[:, part] = slope.astype(BF)
        sum_two = sum_two + mm(act.astype(BF), rows_of(dn_ref, start, step))
    two_ref[...] = sum_two
    out_low = layer_norm(sum_two, *norm_of(norms, 4)).astype(BF)
    low_ref[...] = out_low
    act, slope = gelu_pair(mm(out_low, hb_ref[...]) + hbias_ref[...])
    act_ref[...] = act
    hslope_ref[...] = slope
    feat_ref[...] = layer_norm(act, *norm_of(norms, 5)).astype(BF)


def slab_scratch(slab):
    array, place, rows = slab
    return pltpu.VMEM((array.shape[0], rows, array.shape[2]), BF)


def last_forward(
    x, place_col, place_row, seg_wide, down, adapt, bias, weights, starts, up, dn, gains, shifts, hbias
):
    rows, hidden = x.shape
    labels = place_col.shape[0]
    units = 4 * hidden
    whole = pl.BlockSpec(memory_space=pltpu.VMEM)
    anywhere = pl.BlockSpec(memory_space=pl.ANY)
    shape = jax.ShapeDtypeStruct
    pairs = HEADS // 2
    matrices = [(3 * hidden, hidden), (hidden, hidden), (hidden, hidden)]
    slabs = []
    if starts is not None:
        shards = weights[0].shape[0]
        slabs = [
            pltpu.VMEM((shards, 4 * hidden // shards, hidden), BF),
            pltpu.VMEM((shards, weights[0].shape[1] - starts[1], hidden), BF),
        ]

    def body(*refs):
        head, rest = refs[:7], refs[7:]
        return last_forward_body(
            *head, rest[: len(weights)], *rest[len(weights) :], places=(up[1], dn[1]), starts=starts
        )

    return pl.pallas_call(
        body,
        in_specs=[whole] * 7 + [anywhere] * (len(weights) + 2) + [whole] * 3,
        out_specs=[whole] * 11 + ([anywhere] * 3 if slabs else []),
        out_shape=[
            shape((rows, 2 * hidden), BF),
            shape((labels, hidden), BF),
            shape((rows, down.shape[2]), BF),
            shape((pairs, 2 * labels), F32),
            shape((labels, hidden), F32),
            shape((labels, units), BF),
            shape((labels, hidden), F32),
            shape((labels, hidden), BF),
            shape((labels, hidden), F32),
            shape((labels, hidden), F32),
            shape((labels, hidden), BF),
        ]
        + ([shape(m, BF) for m in matrices] if slabs else []),
        scratch_shapes=[
            slab_scratch(up),
            slab_scratch(dn),
            pltpu.VMEM((labels, hidden), BF),
            *[pltpu.VMEM(m, BF) for m in matrices],
            *slabs,
            pltpu.SemaphoreType.DMA((7,)),
        ],
        compiler_params=params(),
        name="last_forward",
    )(x, place_col, place_row, seg_wide, down, adapt, bias, *weights, up[0], dn[0], gains, shifts, hbias)


def vocab_body(u_ref, e_ref, et_ref, bias_ref, num_ref, log_ref, scores, weights):
    count = e_ref.shape[0]
    step = split_of(count, 640, 16)
    u = u_ref[...]
    rows = u.shape[0]
    labels = num_ref.shape[2]
    top = jnp.full((1, rows), -jnp.inf, F32)
    for start in range(0, count, step):
        part = slice(start, start + step)
        bias = bias_ref[part, :]
        logits = mm_nt(e_ref[part, :], u) + jnp.concatenate([bias] * (rows // bias.shape[1]), 1)
        scores[part, :] = logits
        top = jnp.maximum(top, jnp.max(logits, 0, keepdims=True))
    total = jnp.zeros((1, rows), F32)
    for start in range(0, count, step):
        part = slice(start, start + step)
        grown = jnp.exp(scores[part, :] - top)
        total = total + jnp.sum(grown, 0, keepdims=True)
        weights[part, :] = grown.astype(BF)
    mean = mm(et_ref[...], weights[...]) * (1.0 / total)
    logs = top + jnp.log(total)
    for k in range(rows // labels):
        num_ref[k, :, :] = mean[:, k * labels : (k + 1) * labels]
        log_ref[k, :, :] = logs[:, k * labels : (k + 1) * labels]


def vocab(u, e, et, bias_wide, labels):
    rows, hidden = u.shape
    count = e.shape[0]
    tile = 2 * labels
    return pl.pallas_call(
        vocab_body,
        grid=(rows // tile,),
        in_specs=[
            pl.BlockSpec((tile, hidden), lambda i: (i, 0)),
            full(e.shape),
            full(et.shape),
            full(bias_wide.shape),
        ],
        out_specs=[
            pl.BlockSpec((2, hidden, labels), lambda i: (i, 0, 0)),
            pl.BlockSpec((2, 1, labels), lambda i: (i, 0, 0)),
        ],
        out_shape=[
            jax.ShapeDtypeStruct((rows // labels, hidden, labels), F32),
            jax.ShapeDtypeStruct((rows // labels, 1, labels), F32),
        ],
        scratch_shapes=[pltpu.VMEM((count, tile), F32), pltpu.VMEM((count, tile), BF)],
        compiler_params=params(),
        name="vocab",
    )(u, e, et, bias_wide)


def last_backward_body(
    own_any, got_any, mean_ref, all_log_ref, code_ref, fact_ref, kv_ref, q_ref, mid_ref, log_ref, one_ref, slope_ref, two_ref,
    low_ref, act_ref, hslope_ref, feat_ref, place_ref, place_row_ref, seg_ref, down_ref, w_ref, adapt_ref, wo_ref,
    up_any, dn_any, gain_ref, hb_ref,
    dx_ref, gh_ref, g_ref, out_fact_ref,
    up_ref, dn_ref, dkv_ref, dq_ref, aims, sems, *, places, edge,
):
    labels = place_ref.shape[0]
    tail = pl.ds(kv_ref.shape[0], labels)
    aimed = [
        pltpu.make_async_copy(source.at[tail, :], aims.at[k], sems.at[2 + k])
        for k, source in enumerate((own_any, got_any))
    ]
    for copy in aimed:
        copy.start()
    copies = []
    for k, (source, target, place) in enumerate(
        ((up_any, up_ref, places[0]), (dn_any, dn_ref, places[1]))
    ):
        rows = target.shape[1]
        copies.append(
            pltpu.make_async_copy(
                source.at[:, pl.ds(place * rows, rows), :], target, sems.at[k]
            )
        )
        copies[-1].start()
    rows = kv_ref.shape[0]
    labels, hidden = feat_ref.shape
    lanes = 2 * (hidden // HEADS)
    width = lanes // 2
    scale = width**-0.5
    for copy in aimed:
        copy.wait()
    mine = code_ref[kv_ref.shape[0] :, :] % 2
    targets = jnp.where(mine > 0, aims[0].astype(F32), aims[1].astype(F32))
    weight = fact_ref[0:1, 0:1]
    chosen = jnp.sum(feat_ref[...].astype(F32) * targets, keepdims=True)
    loss = weight * (jnp.sum(all_log_ref[...] - fact_ref[3:4, :labels], keepdims=True) - chosen)
    out_fact_ref[...] = jnp.where(
        lax.broadcasted_iota(jnp.int32, fact_ref.shape, 0) == 0, loss, fact_ref[...]
    )
    du = weight * (mean_ref[...].T - targets)
    dact = norm_back(act_ref[...], gain_ref[5:6, :], du)
    dz = (hslope_ref[...] * dact).astype(BF)
    dense = mm_tn(low_ref[...], dz)
    if len(gh_ref.shape) == 2:
        gh_ref[...] = dense
    else:
        each = hidden // gh_ref.shape[0]
        spare = jnp.zeros((gh_ref.shape[1] - each, hidden), F32)
        for k in range(gh_ref.shape[0]):
            gh_ref[k] = jnp.concatenate([dense[k * each : (k + 1) * each, :], spare], 0).astype(BF)
    dtwo = norm_back(two_ref[...], gain_ref[4:5, :], mm_nt(dz, hb_ref[...]))
    dtwo_low = dtwo.astype(BF)
    dmiddle = dtwo
    units, step = feed_step(up_ref)
    for copy in copies:
        copy.wait()
    dact = mm_nt(dtwo_low, rows_of(dn_ref, 0, step))
    for start in range(0, units, step):
        part = slice(start, start + step)
        later = mm_nt(dtwo_low, rows_of(dn_ref, start + step, step)) if start + step < units else None
        dgate = (slope_ref[:, part].astype(F32) * dact).astype(BF)
        dmiddle = dmiddle + mm(dgate, rows_of(up_ref, start, step))
        dact = later
    done = norm_back(one_ref[...], gain_ref[3:4, :], dmiddle)
    dctx = mm(done.astype(BF), wo_ref[...]).astype(BF)
    seg = seg_ref[...]
    choose_t = lax.broadcasted_iota(jnp.int32, (rows, labels), 0) == place_row_ref[...]
    same = seg == jnp.sum(jnp.where(choose_t, seg, 0.0), 0, keepdims=True)

    def products(p):
        part = slice(p * lanes, (p + 1) * lanes)
        later = slice(hidden + p * lanes, hidden + (p + 1) * lanes)
        queries = pair_rows(q_ref[:, part].astype(F32) * scale, width)
        outs = pair_rows(dctx[:, part].astype(F32), width)
        return queries, outs, mm_nt(kv_ref[:, part], queries), mm_nt(kv_ref[:, later], outs)

    ahead = products(0)
    for p in range(hidden // lanes):
        part = slice(p * lanes, (p + 1) * lanes)
        later = slice(hidden + p * lanes, hidden + (p + 1) * lanes)
        queries, outs, scores, dweights = ahead
        ahead = products(p + 1) if (p + 1) * lanes < hidden else None
        keys = kv_ref[:, part]
        weights = jnp.exp(masked(scores, same) - log_ref[p : p + 1, :])
        inner = jnp.sum(dweights * weights, 0, keepdims=True)
        dscores = (weights * (dweights - inner)).astype(BF)
        dkv_ref[:, part] = mm(dscores, queries).astype(BF)
        dkv_ref[:, later] = mm(weights.astype(BF), outs).astype(BF)
        dq_ref[:, part] = (pair_join(mm_tn(keys, dscores), width) * scale).T.astype(BF)
    dq = dq_ref[...]
    own_mid = mm(
        (lax.broadcasted_iota(jnp.int32, (labels, rows), 1) == place_ref[...][:, 0:1]).astype(F32).astype(BF),
        mid_ref[...],
    ).astype(BF)
    g_ref[...] = adapter_scale * jnp.where(
        lax.broadcasted_iota(jnp.int32, g_ref.shape, 1) < edge,
        mm_tn(dq, own_mid),
        mm_tn(dkv_ref[:, hidden:], mid_ref[...]),
    )
    dmid_own = mm_nt(dq, adapt_ref[1, :, :hidden]).astype(BF)
    own = done + mm(dq, w_ref[:hidden, :]) + mm_nt(dmid_own, down_ref[1])
    spread = choose_t.astype(F32).astype(BF)
    own_high = own.astype(BF)
    own_rest = (own - own_high.astype(F32)).astype(BF)
    dmid = mm_nt(dkv_ref[:, hidden:], adapt_ref[1, :, 2 * hidden :]).astype(BF)
    step = split_of(hidden, 256, 128)
    for start in range(0, hidden, step):
        part = slice(start, start + step)
        dx_ref[:, part] = (
            mm(dkv_ref[...], w_ref[hidden:, part])
            + mm_nt(dmid, down_ref[1, part, :])
            + mm(spread, own_high[:, part])
            + mm(spread, own_rest[:, part])
        )


def last_backward(
    mean, logs, own, got, code, facts, saved, place_col, place_row, seg_wide, down, w, adapt, wo, up, dn, gains, hb, edge, shards
):
    kv = saved[0]
    rows = kv.shape[0]
    labels, hidden = saved[-1].shape
    whole = pl.BlockSpec(memory_space=pltpu.VMEM)
    anywhere = pl.BlockSpec(memory_space=pl.ANY)
    shape = jax.ShapeDtypeStruct
    return pl.pallas_call(
        functools.partial(last_backward_body, places=(up[1], dn[1]), edge=edge),
        in_specs=[anywhere] * 2 + [whole] * 22 + [anywhere] * 2 + [whole] * 2,
        out_specs=[whole] * 4,
        out_shape=[
            shape((rows, hidden), F32),
            shape((hidden, hidden), F32)
            if shards is None
            else shape((shards, -(-hidden // shards // 16) * 16, hidden), BF),
            shape((hidden, down.shape[2]), F32),
            shape(facts.shape, F32),
        ],
        scratch_shapes=[
            slab_scratch(up),
            slab_scratch(dn),
            pltpu.VMEM(kv.shape, BF),
            pltpu.VMEM((labels, hidden), BF),
            pltpu.VMEM((2, labels, hidden), BF),
            pltpu.SemaphoreType.DMA((4,)),
        ],
        compiler_params=params(),
        name="last_backward",
    )(own, got, mean, logs, code, facts, *saved, place_col, place_row, seg_wide, down, w, adapt, wo, up[0], dn[0], gains, hb)


def after_back_body(dout_ref, one_ref, two_ref, slope_ref, wo_ref, up_ref, down_ref, gain_ref, dctx_ref):
    dtwo = norm_back(two_ref[...], gain_ref[2:3, :], dout_ref[...])
    low = dtwo.astype(BF)
    dmiddle = dtwo
    units, step = feed_step(up_ref)
    dact = mm_nt(low, rows_of(down_ref, 0, step))
    for start in range(0, units, step):
        part = slice(start, start + step)
        later = mm_nt(low, rows_of(down_ref, start + step, step)) if start + step < units else None
        dgate = (slope_ref[:, part].astype(F32) * dact).astype(BF)
        dmiddle = dmiddle + mm(dgate, rows_of(up_ref, start, step))
        dact = later
    done = norm_back(one_ref[...], gain_ref[1:2, :], dmiddle)
    dctx_ref[...] = mm(done.astype(BF), wo_ref[...]).astype(BF)


def after_back(dout, one, two, slope, wo, up, down, norms):
    rows, width = dout.shape
    tile = split_of(rows, 256, 16)
    row = lambda n: pl.BlockSpec((tile, n), lambda i: (i, 0))
    return pl.pallas_call(
        after_back_body,
        grid=(rows // tile,),
        in_specs=[row(width), row(width), row(width), row(slope.shape[1]), full(wo.shape)]
        + [slab_spec(up), slab_spec(down), full(norms.shape)],
        out_specs=row(width),
        out_shape=jax.ShapeDtypeStruct((rows, width), BF),
        compiler_params=params(),
        name="after_back",
    )(dout, one, two, slope, wo, up[0], down[0], norms)


def attend_back_body(
    q_ref, k_ref, v_ref, dctx_ref, log_ref, seg_ref, seg_row_ref, mid_ref, g_ref, dv_ref, *, edge
):
    rows = q_ref.shape[0]
    width = q_ref.shape[1] // 2
    scale = width**-0.5
    dv_ref[...] = jnp.zeros_like(dv_ref)
    gq = jnp.zeros((2 * width, mid_ref.shape[1]), F32)
    turned = turn_blocks(k_ref)

    def products(start):
        own, near = reach_of(start, rows)
        queries = pair_rows(q_ref[own, :].astype(F32) * scale, width)
        outs = pair_rows(dctx_ref[own, :].astype(F32), width)
        return outs, mm_nt(k_ref[near, :], queries), mm_nt(v_ref[near, :], outs)

    now = products(0)
    for start in range(0, rows, REACH):
        own, near = reach_of(start, rows)
        later = products(start + REACH) if start + REACH < rows else None
        outs, scores, dweights = now
        same = seg_ref[near, :] == seg_row_ref[:, own]
        logs = log_ref[0, :, 2 * start : 2 * start + 2 * REACH]
        weights = jnp.exp(masked(scores, same) - logs)
        inner = jnp.sum(dweights * weights, 0, keepdims=True)
        dscores = (weights * (dweights - inner)).astype(BF)
        dv_ref[near, :] += mm(weights.astype(BF), outs)
        dq = (pair_join(mm(turned[:, near], dscores), width) * scale).astype(BF)
        gq = gq + mm(dq, mid_ref[own, :])
        now = later
    gv = mm_tn(dv_ref[...].astype(BF), mid_ref[...])
    g_ref[...] = adapter_scale * jnp.where(
        lax.broadcasted_iota(jnp.int32, gq.shape, 1) < edge, gq, gv
    )


def attend_back(qkv, dctx, logs, seg_wide, seg_row, mid, edge):
    rows, total = qkv.shape
    hidden = total // 3
    lanes = 2 * (hidden // HEADS)
    pairs = hidden // lanes
    column = lambda kind: pl.BlockSpec((rows, lanes), lambda p: (0, kind * pairs + p))
    return pl.pallas_call(
        functools.partial(attend_back_body, edge=edge),
        grid=(pairs,),
        in_specs=[
            column(0),
            column(1),
            column(2),
            column(0),
            pl.BlockSpec((1, 1, 2 * rows), lambda p: (p, 0, 0)),
            full(seg_wide.shape),
            full(seg_row.shape),
            full(mid.shape),
        ],
        out_specs=pl.BlockSpec((lanes, mid.shape[1]), lambda p: (p, 0)),
        out_shape=jax.ShapeDtypeStruct((hidden, mid.shape[1]), F32),
        scratch_shapes=[pltpu.VMEM((rows, lanes), F32)],
        compiler_params=params(),
        name="attend_back",
    )(qkv, qkv, qkv, dctx, logs, seg_wide, seg_row, mid)


MESH = pl.DeviceIdType.MESH


def position():
    dp, fsdp = lax.axis_index("dp"), lax.axis_index("fsdp")
    return {"x": dp, "z": fsdp // 4, "y": (fsdp // 2) % 2, "c": fsdp % 2}


def device_of(place):
    return (place["x"], (place["z"] * 2 + place["y"]) * 2 + place["c"])


def number_of(place):
    return place["x"] * 16 + (place["z"] * 2 + place["y"]) * 2 + place["c"]


def rank_device(number):
    return (number // 16, number % 16)


def greet_all(shards):
    barrier = pltpu.get_barrier_semaphore()
    me = lax.axis_index("dp") * 16 + lax.axis_index("fsdp")

    @pl.loop(1, shards)
    def _(k):
        pl.semaphore_signal(
            barrier, inc=1, device_id=rank_device((me + k) % shards), device_id_type=MESH
        )


def await_all(shards):
    pl.semaphore_wait(pltpu.get_barrier_semaphore(), shards - 1)


def direct_copy(source, target, sems, me, k, shards):
    return pltpu.make_async_remote_copy(
        src_ref=source,
        dst_ref=target,
        send_sem=sems.at[0],
        recv_sem=sems.at[1],
        device_id=rank_device((me + k) % shards),
        device_id_type=MESH,
    )


def spread(piece_of, buffer, sems, me, shards):
    @pl.loop(1, shards)
    def _(k):
        direct_copy(piece_of((me + k) % shards), buffer.at[me], sems, me, k, shards).start()


def collect(buffer, sems, me, shards):
    whole = buffer.at[pl.ds(0, shards - 1)]
    copy = direct_copy(whole, whole, sems, me, 1, shards)
    copy.wait_recv()
    copy.wait_send()


def relative_places(order):
    places = [
        {"x": dx, "z": dz, "y": dy} for dx in (0, 1) for dz in range(-3, 4) for dy in (0, 1)
    ]
    size = lambda p: abs(p["x"]) + abs(p["z"]) + abs(p["y"])
    return sorted(places, key=lambda p: (abs(p[order[-1]]), size(p), [abs(p[a]) for a in order]))


class Gather:
    def __init__(self, chunk, full_buffer, start, rows, order, sends, receives, hands, hands_got):
        self.chunk, self.full, self.order = chunk, full_buffer, order
        self.part = pl.ds(start, rows)
        self.sends, self.receives, self.hands, self.hands_got = sends, receives, hands, hands_got
        self.here = position()
        self.items = relative_places(order)
        self.pending = []

    def origin(self, item):
        here = self.here
        return {"x": (here["x"] + item["x"]) % 2, "z": here["z"] - item["z"], "y": (here["y"] + item["y"]) % 2, "c": here["c"]}

    def key(self, place):
        return (place["x"] * 4 + place["z"]) * 2 + place["y"]

    def outward(self, item):
        deepest = max([k for k, axis in enumerate(self.order) if item[axis]], default=-1)
        ways = []
        if deepest >= 0 and self.order[deepest] == "z":
            ways.append(("z", 1 if item["z"] > 0 else -1))
        for axis in self.order[deepest + 1 :]:
            ways += [("z", 1), ("z", -1)] if axis == "z" else [(axis, 1)]
        return ways

    def copy(self, index, way, slot, item):
        here = self.here
        place = self.origin(item)
        number, key = number_of(place), self.key(place)
        mine = not any(item.values())
        source = self.chunk.at[self.part, :] if mine else self.full.at[number, self.part, :]
        if way is None:
            target = dict(here, c=1 - here["c"])
            sends, receives = self.hands.at[index], self.hands_got.at[key]
        else:
            axis, step = way
            target = dict(here)
            target[axis] = here["z"] + step if axis == "z" else 1 - here[axis]
            sends, receives = self.sends.at[index * 4 + slot], self.receives.at[key]
        return pltpu.make_async_remote_copy(
            src_ref=source,
            dst_ref=self.full.at[number, self.part, :],
            send_sem=sends,
            recv_sem=receives,
            device_id=device_of(target),
            device_id_type=MESH,
        )

    def valid(self, item):
        z = self.here["z"] - item["z"]
        return (z >= 0) & (z <= 3)

    def step(self, index):
        item = self.items[index]

        @pl.when(self.valid(item))
        def _():
            if any(item.values()):
                self.arrived(index, item)
            for slot, way in enumerate(self.outward(item)):
                self.when_way(way, lambda way=way, slot=slot: self.copy(index, way, slot, item).start())
            self.copy(index, None, 0, item).start()

    def when_way(self, way, act):
        axis, step = way
        if axis == "z":
            z = self.here["z"] + step
            pl.when((z >= 0) & (z <= 3))(act)
        else:
            act()

    def arrived(self, index, item):
        place = self.origin(item)
        spot = self.full.at[number_of(place), self.part, :]
        pltpu.make_async_remote_copy(
            src_ref=spot,
            dst_ref=spot,
            send_sem=self.sends.at[index * 4],
            recv_sem=self.receives.at[self.key(place)],
            device_id=device_of(dict(self.here, c=1 - self.here["c"])),
            device_id_type=MESH,
        ).wait_recv()

    def finish(self):
        for index, item in enumerate(self.items):

            @pl.when(self.valid(item))
            def _(index=index, item=item):
                for slot, way in enumerate(self.outward(item)):
                    self.when_way(way, lambda way=way, slot=slot: self.copy(index, way, slot, item).wait_send())
                self.copy(index, None, 0, item).wait_send()
                place = dict(self.origin(item), c=1 - self.here["c"])
                spot = self.full.at[number_of(place), self.part, :]
                pltpu.make_async_remote_copy(
                    src_ref=spot,
                    dst_ref=spot,
                    send_sem=self.hands.at[index],
                    recv_sem=self.hands_got.at[self.key(place)],
                    device_id=device_of(dict(self.here, c=1 - self.here["c"])),
                    device_id_type=MESH,
                ).wait_recv()


ITEMS = 28


def start_body(
    streams, shards, fact, chunk, table_any, facts, full_chunk, et_out, e_ref, et_ref,
    fact_sems, own_sems, sends, receives, hands, hands_got,
):
    here = position()
    me = number_of(here)
    own = [
        pltpu.make_async_copy(source, target, own_sems.at[k])
        for k, (source, target) in enumerate(
            ((vocab_rows(table_any, e_ref), e_ref), (fact, facts.at[me]), (chunk, full_chunk.at[me]))
        )
    ]
    for copy in own:
        copy.start()
    greet_all(shards)
    await_all(shards)
    gathers = [
        Gather(
            chunk, full_chunk, start, size, order, sends.at[k], receives.at[k], hands.at[k], hands_got.at[k]
        )
        for k, (start, size, order) in enumerate(streams)
    ]
    for gather in gathers:
        gather.step(0)
    spread(lambda peer: fact, facts, fact_sems, me, shards)
    own[0].wait()
    blocks = e_ref.shape[0] // 128
    each = -(-blocks // (ITEMS - 1))
    for index in range(1, ITEMS):
        for k in range((index - 1) * each, min(index * each, blocks)):
            part = slice(k * 128, (k + 1) * 128)
            et_ref[:, part] = e_ref[part, :].astype(F32).T.astype(BF)
        for gather in gathers:
            gather.step(index)
    turned = pltpu.make_async_copy(et_ref, et_out, own_sems.at[3])
    turned.start()
    for gather in gathers:
        gather.finish()
    collect(facts, fact_sems, me, shards)
    for copy in own[1:] + [turned]:
        copy.wait()


def vocab_rows(table, like):
    here = position()
    count = like.shape[0]
    return table.at[pl.ds(pl.multiple_of((here["y"] * 2 + here["c"]) * count, 16), count), :]


def gather_sems(streams):
    sems = pltpu.SemaphoreType.DMA
    count = len(streams)
    return [sems((count, 4 * ITEMS)), sems((count, 16)), sems((count, ITEMS)), sems((count, 16))]


def streams_of(rows, parts):
    streams, start = [], 0
    for k, (order, share) in enumerate(parts):
        size = rows - start if k == len(parts) - 1 else round(rows * share / 16) * 16
        streams.append((start, size, order))
        start += size
    return streams


def start_exchange(fact, chunk, table, shards):
    anywhere = pl.BlockSpec(memory_space=pl.ANY)
    shape = jax.ShapeDtypeStruct
    sems = pltpu.SemaphoreType.DMA
    streams = streams_of(chunk.shape[0], (("zxy", 0.34), ("zyx", 0.34), ("xzy", 0.32)))
    count, hidden = table.shape[0] // 4, table.shape[1]
    return pl.pallas_call(
        functools.partial(start_body, streams, shards),
        in_specs=[anywhere] * 3,
        out_specs=[anywhere] * 3,
        out_shape=[
            shape((shards, *fact.shape), fact.dtype),
            shape((shards, *chunk.shape), chunk.dtype),
            shape((hidden, count), BF),
        ],
        scratch_shapes=[
            pltpu.VMEM((count, hidden), BF),
            pltpu.VMEM((hidden, count), BF),
            sems((2,)),
            sems((4,)),
            *gather_sems(streams),
        ],
        compiler_params=params(collective_id=1, has_side_effects=True),
        cost_estimate=pl.CostEstimate(flops=0, bytes_accessed=200_000_000, transcendentals=0),
        name="start_exchange",
    )(fact, chunk, table)


def first_layer_body(
    streams, shards,
    own_any, got_any, in_any, feed_any, chunk, code_ref, spots_ref, gain_ref, shift_ref, down_ref,
    adapt_ref, bias_ref, seg_ref, seg_row_ref,
    qkv_out, x_out, one_out, two_out, slope_out, wo_out, full_chunk, mid_ref, log_ref,
    own, got, in_slab, w, wo, up, dn, x, qkv, ctx, two, out, slope,
    load_sems, tile_sems, out_sems, sends, receives, hands, hands_got,
):
    here = position()
    me = number_of(here)
    rows, hidden = x.shape
    tile = split_of(rows, 256, 16)
    tiles = rows // tile
    lanes = 2 * (hidden // HEADS)
    pairs = hidden // lanes

    cut = dn.shape[1] - feed_any.shape[1]

    def slab(source, target, start):
        return source.at[:, pl.ds(start, target.shape[1]), :]

    loads = [
        pltpu.make_async_copy(source, target, load_sems.at[k])
        for k, (source, target) in enumerate(
            (
                (own_any.at[pl.ds(0, rows), :], own),
                (got_any.at[pl.ds(0, rows), :], got),
                (slab(in_any, in_slab, in_any.shape[1] - in_slab.shape[1]), in_slab),
                (slab(in_any, up, 0), up),
                (in_any.at[:, pl.ds(up.shape[1], cut), :], dn.at[:, pl.ds(0, cut), :]),
                (feed_any, dn.at[:, pl.ds(cut, dn.shape[1] - cut), :]),
                (chunk, full_chunk.at[me]),
            )
        )
    ]
    for copy in loads:
        copy.start()
    barrier = pltpu.get_barrier_semaphore()
    peers = [
        dict(here, c=1 - here["c"]),
        dict(here, x=1 - here["x"]),
        dict(here, y=1 - here["y"]),
        *[dict(here, z=flip(here["z"], k)) for k in (1, 2, 3)],
    ]
    for peer in peers:
        pl.semaphore_signal(barrier, inc=1, device_id=device_of(peer), device_id_type=MESH)
    pl.semaphore_wait(barrier, len(peers))
    gathers = [
        Gather(
            chunk, full_chunk, start, size, order, sends.at[k], receives.at[k], hands.at[k], hands_got.at[k]
        )
        for k, (start, size, order) in enumerate(streams)
    ]
    def advance(*ranges):
        pairs_of = [(0, ranges[0]), (1, ranges[0])] + [(2, r) for r in ranges[1:]]
        for k, (first, last) in pairs_of:
            for index in range(first, last + 1):
                gathers[k].step(index)

    def at(i, plan):
        for k, ranges in plan.items():
            pl.when(i == k)(functools.partial(advance, *ranges))

    advance((0, 0), (0, 0))
    for copy in loads[:3]:
        copy.wait()
    unpack_rows(in_slab, (w, wo))

    @pl.loop(0, tiles)
    def _(i):
        part = pl.ds(pl.multiple_of(i * tile, tile), tile)
        project_body(
            own.at[part, :], got.at[part, :], code_ref.at[part, :], spots_ref, gain_ref, shift_ref, down_ref, w,
            adapt_ref, bias_ref, qkv.at[part, :], mid_ref.at[part, :], x.at[part, :],
        )

        at(i, {tiles - 3: ((1, 3), (1, 3)), tiles - 1: ((4, 5),)})

    early = [
        pltpu.make_async_copy(qkv, qkv_out, out_sems.at[0]),
        pltpu.make_async_copy(wo, wo_out, out_sems.at[1]),
    ]
    for copy in early:
        copy.start()

    @pl.loop(0, pairs)
    def _(p):
        column = lambda kind: pl.ds(pl.multiple_of((kind * pairs + p) * lanes, lanes), lanes)
        attend_body(
            qkv.at[:, column(0)], qkv.at[:, column(1)], qkv.at[:, column(2)], seg_ref, seg_row_ref,
            ctx.at[:, column(0)], log_ref.at[pl.ds(p, 1)],
        )

        at(
            p - (pairs - 6),
            {0: ((1, 0), (4, 11)), 1: ((6, 7),), 3: ((8, 9), (12, 19)), 4: ((10, 11),)},
        )

    for copy in loads[3:6]:
        copy.wait()

    def tile_copies(i):
        part = pl.ds(pl.multiple_of(i * tile, tile), tile)
        turn = i % 2
        return [
            pltpu.make_async_copy(source, target.at[part, :], tile_sems.at[k, i])
            for k, (source, target) in enumerate(
                (
                    (out.at[turn], x_out),
                    (two.at[turn], two_out),
                    (slope.at[turn], slope_out),
                    (x.at[part, :], one_out),
                )
            )
        ]

    plan = {0: ((12, 13), (20, 27)), 1: ((14, 17),), 2: ((18, 21),), 3: ((22, 27),)}

    @pl.loop(0, tiles)
    def _(i):
        part = pl.ds(pl.multiple_of(i * tile, tile), tile)
        turn = i % 2

        @pl.when(i >= 2)
        def _():
            for copy in tile_copies(i - 2):
                copy.wait()

        after_body(
            ctx.at[part, :], x.at[part, :], wo, up, dn, bias_ref, gain_ref, shift_ref, out.at[turn],
            x.at[part, :], two.at[turn], slope.at[turn],
        )
        for copy in tile_copies(i):
            copy.start()
        at(i - (tiles - 4), plan)

    for gather in gathers:
        gather.finish()
    for i in (tiles - 2, tiles - 1):
        for copy in tile_copies(i):
            copy.wait()
    for copy in early + loads[6:]:
        copy.wait()


def first_layer(own, got, first_in, feed, chunk, more, shards):
    whole = pl.BlockSpec(memory_space=pltpu.VMEM)
    anywhere = pl.BlockSpec(memory_space=pl.ANY)
    down, seg_row = more[4], more[-1]
    rows, hidden = seg_row.shape[1], own.shape[1]
    tile = split_of(rows, 256, 16)
    pairs = HEADS // 2
    units = 4 * hidden
    each = units // shards
    shape = jax.ShapeDtypeStruct
    sems = pltpu.SemaphoreType.DMA
    streams = streams_of(chunk.shape[0], (("zxy", 0.4), ("zyx", 0.4), ("xyz", 0.2)))
    return pl.pallas_call(
        functools.partial(first_layer_body, streams, shards),
        in_specs=[anywhere] * 5 + [whole] * len(more),
        out_specs=[anywhere] * 7 + [whole] * 2,
        out_shape=[
            shape((rows, 3 * hidden), BF),
            shape((rows, hidden), F32),
            shape((rows, hidden), F32),
            shape((rows, hidden), F32),
            shape((rows, units), BF),
            shape((hidden, hidden), BF),
            shape((shards, *chunk.shape), BF),
            shape((rows, down.shape[2]), BF),
            shape((pairs, 1, 2 * rows), F32),
        ],
        scratch_shapes=[
            pltpu.VMEM((rows, hidden), BF),
            pltpu.VMEM((rows, hidden), BF),
            pltpu.VMEM((shards, 4 * hidden // shards, hidden), BF),
            pltpu.VMEM((3 * hidden, hidden), BF),
            pltpu.VMEM((hidden, hidden), BF),
            pltpu.VMEM((shards, each, hidden), BF),
            pltpu.VMEM((shards, each, hidden), BF),
            pltpu.VMEM((rows, hidden), F32),
            pltpu.VMEM((rows, 3 * hidden), BF),
            pltpu.VMEM((rows, hidden), BF),
            pltpu.VMEM((2, tile, hidden), F32),
            pltpu.VMEM((2, tile, hidden), F32),
            pltpu.VMEM((2, tile, units), BF),
            sems((7,)),
            sems((4, rows // tile)),
            sems((2,)),
            *gather_sems(streams),
        ],
        compiler_params=params(collective_id=3, has_side_effects=True),
        name="first_layer",
    )(own, got, first_in, feed, chunk, *more)


PICK = 64
GROUP = 16


def look_up_body(ids, low_ref, table, first_ref, second_ref, stage):
    half = first_ref.shape[0]
    for k, out_ref in enumerate((first_ref, second_ref)):

        @pl.loop(0, half // PICK)
        def _(b, k=k, out_ref=out_ref):
            at = k * half + b * PICK

            def one(t, carry):
                stage[t] = table[ids[at + t]]
                return carry

            lax.fori_loop(0, PICK, one, 0, unroll=16)
            choose = (
                lax.broadcasted_iota(jnp.int32, (PICK, PICK * GROUP), 1)
                == low_ref[pl.ds(pl.multiple_of(at, PICK), PICK), :]
            )
            out_ref[pl.ds(pl.multiple_of(b * PICK, PICK), PICK), :] = mm(
                choose.astype(F32).astype(BF), flat(stage)
            ).astype(BF)


def look_up(ids, table):
    whole = pl.BlockSpec(memory_space=pltpu.VMEM)
    hidden = table.shape[1]
    low = jnp.arange(ids.size, dtype=jnp.int32) % PICK * GROUP + ids % GROUP
    return pl.pallas_call(
        look_up_body,
        in_specs=[pl.BlockSpec(memory_space=pltpu.SMEM), whole, whole],
        out_specs=[whole] * 2,
        out_shape=[jax.ShapeDtypeStruct((ids.size // 2, hidden), table.dtype)] * 2,
        scratch_shapes=[pltpu.VMEM((PICK, GROUP, hidden), table.dtype)],
        compiler_params=params(),
        name="look_up",
    )(ids // GROUP, low[:, None], table.reshape(-1, GROUP, hidden))


def adam(weight, gradient, moment_one, moment_two, fade_one, fade_two):
    moment_one = beta_first * moment_one + (1.0 - beta_first) * gradient
    moment_two = beta_second * moment_two + (1.0 - beta_second) * gradient * gradient
    one_hat = moment_one / fade_one
    two_hat = moment_two / fade_two
    weight = weight - learn_rate * (one_hat / (jnp.sqrt(two_hat) + adam_eps) + decay_rate * weight)
    return (weight, moment_one, moment_two)


BACK_TILE = 256


def finish_body(
    shards, edge,
    dout_any, one_any, two_any, slope_any, wo_any, in_any, feed_any, qkv_any, gain_ref, log_ref, seg_ref,
    seg_row_ref, mid_ref, parts, late_ref, facts,
    sums_ref, dense_ref, total_ref,
    dout, one, two, slope, wo, up, dn, qkv, dctx, dv, grad, core_got, chip_sum, dense_got, grad_got, note, notes,
    tile_sems, load_sems, core_sems, dense_sems, grad_sems, note_sems,
):
    rows, hidden = dout.shape
    tile = split_of(rows, BACK_TILE, 16)
    tiles = rows // tile
    me = number_of(position())

    def tile_loads(i):
        part = pl.ds(pl.multiple_of(i * tile, tile), tile)
        return [
            pltpu.make_async_copy(source.at[part, :], target.at[part, :], tile_sems.at[k, i])
            for k, (source, target) in enumerate(
                ((two_any, two), (dout_any, dout), (slope_any, slope), (one_any, one))
            )
        ]

    here = position()
    cut = dn.shape[1] - feed_any.shape[1]
    chips = shards // 2
    chip, core = me // 2, here["c"]
    to_core = pltpu.make_async_remote_copy(
        src_ref=parts.at[:, 1 - core],
        dst_ref=core_got,
        send_sem=core_sems.at[0],
        recv_sem=core_sems.at[1],
        device_id=device_of(dict(here, c=1 - core)),
        device_id_type=MESH,
    )

    def to_chip(k):
        peer = (chip + k) % chips
        return pltpu.make_async_remote_copy(
            src_ref=chip_sum.at[peer],
            dst_ref=dense_got.at[chip],
            send_sem=dense_sems.at[0],
            recv_sem=dense_sems.at[1],
            device_id=rank_device(2 * peer + core),
            device_id_type=MESH,
        )

    loads = [
        pltpu.make_async_copy(source, target, load_sems.at[k])
        for k, (source, target) in enumerate(
            (
                (in_any.at[:, pl.ds(up.shape[1], cut), :], dn.at[:, pl.ds(0, cut), :]),
                (feed_any, dn.at[:, pl.ds(cut, dn.shape[1] - cut), :]),
                (in_any.at[:, pl.ds(0, up.shape[1]), :], up),
                (wo_any, wo),
                (qkv_any, qkv),
            )
        )
    ]
    for copy in tile_loads(0) + loads[:4]:
        copy.start()
    for i in range(1, tiles):
        for copy in tile_loads(i):
            copy.start()
    loads[4].start()
    greet_all(shards)
    for copy in loads[:4]:
        copy.wait()

    @pl.loop(0, tiles)
    def _(i):
        for copy in tile_loads(i):
            copy.wait()
        part = pl.ds(pl.multiple_of(i * tile, tile), tile)
        after_back_body(
            dout.at[part, :], one.at[part, :], two.at[part, :], slope.at[part, :], wo, up, dn, gain_ref,
            dctx.at[part, :],
        )

        @pl.when(i == 0)
        def _():
            await_all(shards)
            to_core.start()

        @pl.when(i == 1)
        def _():
            to_core.wait_recv()

            @pl.loop(0, chips)
            def _(k):
                chip_sum[k] = (parts[k, core].astype(F32) + core_got[k].astype(F32)).astype(BF)

            dense_got[chip] = chip_sum[chip]

            @pl.loop(1, chips)
            def _(k):
                to_chip(k).start()

    loads[4].wait()
    lanes = 2 * (hidden // HEADS)
    pairs = hidden // lanes

    @pl.loop(0, pairs)
    def _(p):
        column = lambda kind: pl.ds(pl.multiple_of((kind * pairs + p) * lanes, lanes), lanes)
        attend_back_body(
            qkv.at[:, column(0)], qkv.at[:, column(1)], qkv.at[:, column(2)], dctx.at[:, column(0)],
            log_ref.at[pl.ds(p, 1)], seg_ref, seg_row_ref, mid_ref, grad.at[column(0), :], dv, edge=edge,
        )

    grad[...] = grad[...] + late_ref[...]
    each = hidden // shards
    piece = lambda peer: grad.at[pl.ds(pl.multiple_of(peer * each, each), each), :]
    grad_got[me] = piece(me)[...]
    spread(piece, grad_got, grad_sems, me, shards)
    others = chip_sum.at[pl.ds(0, chips - 1)]
    every = pltpu.make_async_remote_copy(
        src_ref=others,
        dst_ref=dense_got.at[pl.ds(0, chips - 1)],
        send_sem=dense_sems.at[0],
        recv_sem=dense_sems.at[1],
        device_id=device_of(dict(here, c=1 - core)),
        device_id_type=MESH,
    )
    every.wait_recv()
    every.wait_send()
    to_core.wait_send()
    dense = jnp.zeros((each, hidden), F32)
    for k in range(chips):
        dense = dense + dense_got[k].astype(F32)[:each, :]
    dense_ref[...] = dense
    square = jnp.sum(dense * dense, keepdims=True)
    collect(grad_got, grad_sems, me, shards)
    total = grad_got[0]
    for k in range(1, shards):
        total = total + grad_got[k]
    total_ref[...] = total
    square = square + jnp.sum(total * total, keepdims=True)
    row = lax.broadcasted_iota(jnp.int32, note.shape, 0)
    note[...] = jnp.where(row == 0, facts[...], jnp.where(row == 1, square, 0.0))
    notes[me] = note[...]
    spread(lambda peer: note, notes, note_sems, me, shards)
    collect(notes, note_sems, me, shards)
    sums = notes[0]
    for k in range(1, shards):
        sums = sums + notes[k]
    sums_ref[...] = sums


def update_body(
    sums_ref, dense_ref, total_ref, facts, head_w, head_m, head_v, adapt_w, adapt_m, adapt_v,
    loss_out, norm_out, head_w_out, head_m_out, head_v_out, adapt_w_out, adapt_m_out, adapt_v_out,
):
    norm = jnp.sqrt(sums_ref[1:2, 0:1])
    loss_out[...] = sums_ref[0:1, 0:1]
    norm_out[...] = norm
    factor = jnp.minimum(1.0, clip_limit / (norm + 1e-06))
    fades = facts[1:2, 0:1], facts[2:3, 0:1]
    new = adam(head_w[...], dense_ref[...] * factor, head_m[...], head_v[...], *fades)
    head_w_out[...], head_m_out[...], head_v_out[...] = new
    grad = (total_ref[...] * factor).T
    layers, kinds, rank, unused = adapt_w.shape
    for layer in range(layers):
        for kind in range(kinds):
            at = (layer * kinds + kind) * rank
            new = adam(
                adapt_w[layer, kind], grad[at : at + rank], adapt_m[layer, kind], adapt_v[layer, kind], *fades
            )
            adapt_w_out[layer, kind], adapt_m_out[layer, kind], adapt_v_out[layer, kind] = new


def update(sums, dense, total, facts, heads, adapts):
    whole = pl.BlockSpec(memory_space=pltpu.VMEM)
    shape = jax.ShapeDtypeStruct
    return pl.pallas_call(
        update_body,
        in_specs=[whole] * 10,
        out_specs=[whole] * 8,
        out_shape=[shape((1, 1), F32)] * 2 + [shape(a.shape, F32) for a in (*heads, *adapts)],
        compiler_params=params(),
        name="update",
    )(sums, dense, total, facts, *heads, *adapts)


def finish(back, qkv, logs, seg_wide, seg_row, mid, parts, late, facts, edge, shards):
    dout, one, two, slope, wo, first_in, feed, gains = back
    slab = pltpu.VMEM((shards, slope.shape[1] // shards, dout.shape[1]), BF)
    parts = parts.reshape(-1, 2, *parts.shape[1:])
    rows, hidden = dout.shape
    each = hidden // shards
    whole = pl.BlockSpec(memory_space=pltpu.VMEM)
    anywhere = pl.BlockSpec(memory_space=pl.ANY)
    shape = jax.ShapeDtypeStruct
    sems = pltpu.SemaphoreType.DMA
    tiles = rows // split_of(rows, BACK_TILE, 16)
    return pl.pallas_call(
        functools.partial(finish_body, shards, edge),
        in_specs=[anywhere] * 8 + [whole] * 8,
        out_specs=[whole] * 3,
        out_shape=[
            shape((8, 128), F32),
            shape((each, hidden), F32),
            shape((each, late.shape[1]), F32),
        ],
        scratch_shapes=[
            pltpu.VMEM((rows, hidden), F32),
            pltpu.VMEM((rows, hidden), F32),
            pltpu.VMEM((rows, hidden), F32),
            pltpu.VMEM(slope.shape, BF),
            pltpu.VMEM(wo.shape, BF),
            slab,
            slab,
            pltpu.VMEM(qkv.shape, BF),
            pltpu.VMEM((rows, hidden), BF),
            pltpu.VMEM((rows, 2 * (hidden // HEADS)), F32),
            pltpu.VMEM(late.shape, F32),
            pltpu.VMEM((shards // 2, *parts.shape[2:]), BF),
            pltpu.VMEM((shards // 2, *parts.shape[2:]), BF),
            pltpu.VMEM((shards // 2, *parts.shape[2:]), BF),
            pltpu.VMEM((shards, each, late.shape[1]), F32),
            pltpu.VMEM((8, 128), F32),
            pltpu.VMEM((shards, 8, 128), F32),
            sems((4, tiles)),
            sems((5,)),
            sems((2,)),
            sems((2,)),
            sems((2,)),
            sems((2,)),
        ],
        compiler_params=params(collective_id=2, has_side_effects=True),
        name="finish",
    )(dout, one, two, slope, wo, first_in, feed, qkv, gains, logs, seg_wide, seg_row, mid, parts, late, facts)


LOG_ROWS = 16


def flip(z, k):
    return (z % 2 + k % 2) % 2 + 2 * ((z // 2 + k // 2) % 2)


def pack_log(log_row, rows):
    high = log_row.astype(BF).astype(F32)
    middle = (log_row - high).astype(BF).astype(F32)
    low = log_row - high - middle
    row = lax.broadcasted_iota(jnp.int32, (rows, log_row.shape[1]), 0)
    return jnp.where(
        row == 0, high, jnp.where(row == 1, middle, jnp.where(row == 2, low, 0.0))
    ).astype(BF)


def unpack(block, hidden):
    logs = block[hidden : hidden + LOG_ROWS, :].astype(F32)
    return block[:hidden, :].astype(F32), jnp.sum(logs, 0, keepdims=True)


def merged(one, two):
    top = jnp.maximum(one[1], two[1])
    first, second = jnp.exp(one[1] - top), jnp.exp(two[1] - top)
    total = first + second
    inverse = 1.0 / total
    return one[0] * (first * inverse) + two[0] * (second * inverse), top + jnp.log(total)


def store_packed(ref, pair, hidden):
    ref[:hidden, :] = pair[0].astype(BF)
    ref[hidden : hidden + LOG_ROWS, :] = pack_log(pair[1], LOG_ROWS)


def head_body(
    u_ref, bias_ref, table_any, et_any, mean_ref, log_ref,
    e_ref, et_ref, bias_wide, feats, packs, handed, sums,
    loads, far_send, far_get, hand_send, hand_get, part_send, part_get, sum_send, sum_get,
):
    here = position()
    x, y, c = here["x"], here["y"], here["c"]
    labels, hidden = u_ref.shape
    sibling = device_of(dict(here, c=1 - c))

    def chip_at(k):
        return (x + k % 2) % 2, (y + k // 2) % 2

    def device_at(k):
        there = chip_at(k)
        return device_of(dict(here, x=there[0], y=there[1]))

    def slot(k, core):
        there = chip_at(k)
        return (there[0] * 2 + there[1]) * 2 + core

    fills = [
        pltpu.make_async_copy(source, target, loads.at[k])
        for k, (source, target) in enumerate(
            ((vocab_rows(table_any, e_ref), e_ref), (et_any, et_ref))
        )
    ]
    for fill in fills:
        fill.start()
    barrier = pltpu.get_barrier_semaphore()
    for target in (sibling, *[device_at(k) for k in (1, 2, 3)]):
        pl.semaphore_signal(barrier, inc=1, device_id=target, device_id_type=MESH)
    feats[slot(0, c)] = u_ref[...]
    pl.semaphore_wait(barrier, 4)

    def move(place, device, send, get):
        return pltpu.make_async_remote_copy(
            src_ref=feats.at[place],
            dst_ref=feats.at[place],
            send_sem=send,
            recv_sem=get,
            device_id=device,
            device_id_type=MESH,
        )

    def far(k):
        return move(slot(0, c), device_at(k), far_send.at[k], far_get.at[k])

    def far_here(k):
        return move(slot(k, c), device_at(k), far_send.at[k], far_get.at[k])

    def hand(k, core):
        return move(slot(k, core), sibling, hand_send.at[k], hand_get.at[k])

    for k in (1, 2, 3):
        far(k).start()
    hand(0, c).start()

    @pl.loop(0, bias_ref.shape[0])
    def _(b):
        row = jnp.broadcast_to(bias_ref[pl.ds(b, 1), :], (128, 128))
        bias_wide[pl.ds(pl.multiple_of(b * 128, 128), 128), :] = row.T

    for k in (1, 2, 3):
        far_here(k).wait_recv()
        hand(k, c).start()
    for fill in fills:
        fill.wait()
    count = e_ref.shape[0]
    steps = 4

    def target_of(s):
        return (s + 1) % steps

    def hand_part(s):
        return pltpu.make_async_remote_copy(
            src_ref=packs.at[s, 1 - c],
            dst_ref=handed.at[s],
            send_sem=part_send.at[s],
            recv_sem=part_get.at[s],
            device_id=sibling,
            device_id_type=MESH,
        )

    def sum_part(s):
        return pltpu.make_async_remote_copy(
            src_ref=packs.at[s, c],
            dst_ref=sums.at[s],
            send_sem=sum_send.at[s],
            recv_sem=sum_get.at[s],
            device_id=device_at(target_of(s)),
            device_id_type=MESH,
        )

    def together(s):
        hand_part(s).wait_recv()
        return merged(unpack(packs[s, c], hidden), unpack(handed[s], hidden))

    def settle(s):
        store_packed(packs.at[s, c], together(s), hidden)
        sum_part(s).start()

    @pl.loop(0, steps)
    def _(s):
        k = target_of(s)
        hand(k, 1 - c).wait_recv()
        u = feats[pl.ds(slot(k, 0), 2)].reshape(2 * labels, hidden)
        top = total = mean = None

        def scored(start):
            part = slice(start, min(start + 1280, count))
            bias = bias_wide[part, :]
            return mm_nt(e_ref[part, :], u) + jnp.concatenate([bias, bias], 1)

        @pl.when(s > 0)
        def _():
            settle(s - 1)

        logits = scored(0)
        for start in range(0, count, 1280):
            part = slice(start, min(start + 1280, count))
            later = scored(start + 1280) if start + 1280 < count else None
            high = jnp.max(logits, 0, keepdims=True)
            new = high if top is None else jnp.maximum(top, high)
            grown = jnp.exp(logits - new)
            part_sums = jnp.sum(grown, 0, keepdims=True)
            product = mm(et_ref[:, part], grown.astype(BF))
            if top is None:
                total, mean = part_sums, product
            else:
                shrink = jnp.exp(top - new)
                total, mean = total * shrink + part_sums, mean * shrink + product
            top = new
            logits = later
        mean = mean * (1.0 / total)
        logs = top + jnp.log(total)
        for core in range(2):
            half = slice(core * labels, (core + 1) * labels)
            packs[s, core, :hidden, :] = mean[:, half].astype(BF)
            packs[s, core, hidden : hidden + LOG_ROWS, :] = pack_log(logs[:, half], LOG_ROWS)
        hand_part(s).start()

    total = together(steps - 1)
    for s in range(steps - 1):
        sum_part(s).wait_recv()
        total = merged(total, unpack(sums[s], hidden))
    mean_ref[...] = total[0]
    log_ref[...] = total[1]
    for k in (1, 2, 3):
        far(k).wait_send()
    for k in range(4):
        hand(k, c).wait_send()
    for s in range(steps):
        hand_part(s).wait_send()
    for s in range(steps - 1):
        sum_part(s).wait_send()


def head(u, bias, table, et):
    labels, hidden = u.shape
    whole = pl.BlockSpec(memory_space=pltpu.VMEM)
    anywhere = pl.BlockSpec(memory_space=pl.ANY)
    shape = jax.ShapeDtypeStruct
    sems = pltpu.SemaphoreType.DMA
    block = (hidden + LOG_ROWS, labels)
    count = et.shape[1]
    return pl.pallas_call(
        head_body,
        in_specs=[whole] * 2 + [anywhere] * 2,
        out_specs=[whole] * 2,
        out_shape=[shape((hidden, labels), F32), shape((1, labels), F32)],
        scratch_shapes=[
            pltpu.VMEM((count, hidden), BF),
            pltpu.VMEM((hidden, count), BF),
            pltpu.VMEM((count, 128), F32),
            pltpu.VMEM((8, labels, hidden), BF),
            pltpu.VMEM((4, 2, *block), BF),
            pltpu.VMEM((4, *block), BF),
            pltpu.VMEM((4, *block), BF),
            sems((2,)),
        ]
        + [sems((4,))] * 8,
        compiler_params=params(collective_id=4, has_side_effects=True),
        name="head",
    )(u, bias, table, et)


def seg_positions(segments):
    index = jnp.arange(segments.shape[-1], dtype=jnp.int32)
    fresh = jnp.concatenate([jnp.ones((1,), dtype=bool), segments[1:] != segments[:-1]], -1)
    starts = lax.cummax(jnp.where(fresh, index, jnp.zeros_like(index)), axis=0)
    return index - starts


def pad_rows(matrix, multiple):
    return jnp.pad(matrix, ((0, -matrix.shape[0] % multiple), (0, 0)))


def slab_of(gathered, start, rows):
    if rows % 16 == 0 and start % rows == 0:
        return (gathered, start // rows, rows)
    part = gathered[:, start : start + rows].reshape(1, -1, gathered.shape[2])
    return (part, 0, part.shape[1])


def per_device(
    input_token_index,
    sentence_numbers,
    label_positions,
    label_target_token,
    sequence_task_index,
    task_loss_weight,
    optimizer_step_count,
    embed,
    position_embedding,
    norm_gain_vector,
    norm_bias_vector,
    attention_in_weight,
    attention_out_weight,
    feedforward_up,
    feedforward_down,
    layer_bias_vector,
    head_dense_bias,
    vocabulary_bias,
    adapter_down_matrix,
    adapter_up_matrix,
    adapter_moment_first,
    adapter_moment_second,
    head_projection,
    head_moment_first,
    head_moment_second,
):
    shards = lax.axis_size("dp") * lax.axis_size("fsdp")
    dp_index = lax.axis_index("dp")
    fsdp_index = lax.axis_index("fsdp")
    layers, unused, rank, up_part = adapter_up_matrix.shape
    hidden = embed.shape[1]
    tokens = input_token_index.shape[1]
    labels = label_positions.shape[1]
    qkv_rows = attention_in_weight.shape[2]
    out_rows = attention_out_weight.shape[2]
    ff_rows = feedforward_up.shape[2]
    head_rows = head_projection.shape[0]

    grouped = (lax.axis_size("dp"), lax.axis_size("fsdp")) == (2, 16)
    feeds = [[feedforward_up[layer].T, feedforward_down[layer]] for layer in range(layers)]
    attends = [[attention_in_weight[layer].T, attention_out_weight[layer].T] for layer in range(layers)]
    cut = ff_rows // 32 * 16
    first_in = lax.all_gather(
        jnp.concatenate([feeds[0][0], feeds[0][1][:cut], *attends[0]], 0), BOTH, axis=0, tiled=False
    )
    feed_chunk = feeds[0][1][cut:]
    last_chunk = pad_rows(
        jnp.concatenate([feeds[1][0], *attends[1], head_projection.astype(BF)], 0), 32
    )
    last_feed = feeds[1][1]

    table_rows = embed.shape[0]
    wanted = jnp.concatenate([input_token_index[0], label_target_token[0]])
    dp_count = lax.axis_size("dp")
    group_ids = lax.all_gather(wanted, "dp", axis=0, tiled=False) - dp_index * table_rows
    inside = (group_ids >= 0) & (group_ids < table_rows)
    group_ids = jnp.clip(group_ids, 0, table_rows - 1)
    mine = lax.dynamic_index_in_dim(inside, dp_index, 0, keepdims=False)

    task_range = jnp.arange(TASKS, dtype=jnp.int32)
    slice_rows = vocabulary_bias.shape[0]
    ups = adapter_up_matrix.reshape(-1)
    if grouped:
        pair_ids = jnp.concatenate(
            [
                lax.dynamic_index_in_dim(group_ids, (dp_index + shift) % 2, 0, keepdims=False)
                for shift in (1, 0)
            ]
        )
        other_rows, own_rows = look_up(pair_ids, embed)
        got = lax.ppermute(other_rows, "dp", [(0, 1), (1, 0)])
        feed_chunk, own_rows = lax.optimization_barrier((feed_chunk, own_rows))
        fact = jnp.concatenate([vocabulary_bias, ups, sequence_task_index.astype(F32)])
        fact_rows = -(-fact.size // 1024) * 8
        facts, feed_full, own_turned = start_exchange(
            jnp.pad(fact, (0, fact_rows * 128 - fact.size)).reshape(fact_rows, 128),
            feed_chunk,
            embed,
            shards,
        )
        facts, got, last_feed = lax.optimization_barrier((facts, got, last_feed))
        facts = facts.reshape(shards, -1)
        all_bias = facts[:, :slice_rows].reshape(-1)
        every_up = facts[:, slice_rows : slice_rows + ups.size]
        every_task = facts[:, slice_rows + ups.size].astype(jnp.int32)
    else:
        looked = jnp.where(
            inside.reshape(-1)[:, None], embed[group_ids.reshape(-1)], jnp.zeros((), BF)
        )
        own_rows = got = lax.psum_scatter(looked, "dp", scatter_dimension=0, tiled=True)
        all_bias = lax.all_gather(vocabulary_bias, BOTH, axis=0, tiled=True)
        every_up = lax.all_gather(ups, BOTH, axis=0, tiled=False)
        every_task = lax.all_gather(sequence_task_index, BOTH, axis=0, tiled=True)
    counts = labels * jnp.sum((every_task[:, None] == task_range[None, :]).astype(F32), 0)
    task_hot = (sequence_task_index[:, None] == task_range[None, :]).astype(F32)
    row_weight = jnp.sum(task_hot[0] * (task_loss_weight / jnp.maximum(counts, 1.0)))
    ups_full = (
        every_up.astype(BF)
        .reshape(shards, layers, 2, rank, up_part)
        .transpose(1, 2, 3, 0, 4)
        .reshape(layers, 2, rank, hidden)
    )
    blank = jnp.zeros((rank, hidden), BF)
    spare = lambda rows: jnp.zeros((rows, 3 * hidden), BF)
    adapters = jnp.stack(
        [
            jnp.concatenate(
                [
                    spare(2 * rank * layer),
                    jnp.concatenate([2 * ups_full[layer, 0], blank, blank], 1),
                    jnp.concatenate([blank, blank, 2 * ups_full[layer, 1]], 1),
                    spare(128 - 2 * rank * (layer + 1)),
                ],
                0,
            )
            for layer in range(layers)
        ]
    )
    downs = jnp.stack(
        [
            jnp.pad(
                jnp.concatenate([adapter_down_matrix[layer, 0], adapter_down_matrix[layer, 1]], 1),
                ((0, 0), (2 * rank * layer, 128 - 2 * rank * (layer + 1))),
            )
            for layer in range(layers)
        ]
    )
    segments = sentence_numbers[0]
    code = (jnp.pad(2 * seg_positions(segments), (0, labels)) + mine.astype(jnp.int32))[:, None]
    seg_real = segments.astype(F32)
    seg_wide = jnp.broadcast_to(seg_real[:, None], (tokens, 128))
    seg_row = seg_real[None, :]
    place_row = label_positions
    place_col = jnp.broadcast_to(label_positions.reshape(labels, 1), (labels, 128))

    target_bias = all_bias[label_target_token[0]]

    gains, shifts = norm_gain_vector, norm_bias_vector
    last_inputs = (place_col, place_row, seg_wide, downs, adapters, layer_bias_vector)
    in_start = ff_rows
    last_dn = lax.all_gather(last_feed, BOTH, axis=0, tiled=False)
    slabs_of = lambda up_full, dn_full: (slab_of(up_full, 0, ff_rows), slab_of(dn_full, 0, ff_rows))
    if grouped:
        more = (
            code, position_embedding, gains, shifts, downs, adapters, layer_bias_vector, seg_wide, seg_row,
        )
        qkv, x_last, one, two, slope, out_first, last_full, mid, logs = first_layer(
            own_rows, got, first_in, feed_full, last_chunk, more, shards
        )
        slabs = [None, slabs_of(last_full, last_dn)]
        *saved, in_last, out_last, head_full = last_forward(
            x_last, *last_inputs, (last_full,), (in_start, in_start + qkv_rows + out_rows), *slabs[1], gains,
            shifts, head_dense_bias[None, :],
        )
        count = own_turned.shape[1]
        own_bias = lax.dynamic_slice_in_dim(
            all_bias, dp_index * table_rows + fsdp_index % 4 * count, count, 0
        ).reshape(-1, 128)
        mean_t, own_logs = head(saved[-1], own_bias, embed, own_turned)
    else:
        feed_full = lax.all_gather(feed_chunk, BOTH, axis=0, tiled=False)
        last_full = lax.all_gather(last_chunk, BOTH, axis=0, tiled=False)
        dn_full = jnp.concatenate([first_in[:, ff_rows : ff_rows + cut], feed_full], 1)
        slabs = [slabs_of(first_in, dn_full), slabs_of(last_full, last_dn)]
        taken = lambda full_chunk, start, size: full_chunk[:, start : start + size].reshape(-1, hidden)
        in_first = taken(first_in, ff_rows + cut, qkv_rows)
        out_first = taken(first_in, ff_rows + cut + qkv_rows, out_rows)
        in_last = taken(last_full, in_start, qkv_rows)
        out_last = taken(last_full, in_start + qkv_rows, out_rows)
        head_full = taken(last_full, in_start + qkv_rows + out_rows, head_rows)
        qkv, mid, hidden_rows = project(
            own_rows, got, code, position_embedding, gains, shifts, downs, in_first, adapters, layer_bias_vector, tokens
        )
        context, logs = attend(qkv, seg_wide, seg_row)
        x_last, one, two, slope = after(
            context, hidden_rows, out_first, *slabs[0], layer_bias_vector, gains, shifts
        )
        saved = last_forward(
            x_last, *last_inputs, (in_last, out_last, head_full), None, *slabs[1], gains, shifts,
            head_dense_bias[None, :],
        )
        features = saved[-1]
        own_slice = lax.dynamic_slice_in_dim(embed, fsdp_index * slice_rows, slice_rows, 0)
        own_vocab = jnp.concatenate(
            [own_slice]
            + [
                lax.ppermute(
                    own_slice, "dp", [(k, (k + shift) % dp_count) for k in range(dp_count)]
                )
                for shift in range(1, dp_count)
            ],
            0,
        )
        own_bias = jnp.concatenate(
            [
                lax.dynamic_slice_in_dim(
                    all_bias,
                    ((dp_index - shift) % dp_count) * table_rows + fsdp_index * slice_rows,
                    slice_rows,
                    0,
                )
                for shift in range(dp_count)
            ]
        )
        bias_wide = jnp.broadcast_to(own_bias[:, None], (own_bias.shape[0], 128))
        every = lax.all_gather(features, "fsdp", axis=0, tiled=True)
        means, local_logs = vocab(every, own_vocab, own_vocab.T, bias_wide, labels)
        local_logs = local_logs.reshape(-1, labels)
        all_logs = lax.all_gather(local_logs, "fsdp", axis=0, tiled=False)
        whole_logs = jax.nn.logsumexp(all_logs, axis=0)
        scaled = (means * jnp.exp(local_logs - whole_logs)[:, None, :]).astype(BF)
        mean_t = lax.psum_scatter(scaled, "fsdp", scatter_dimension=0, tiled=True)[0].astype(F32)
        own_logs = lax.dynamic_index_in_dim(whole_logs, fsdp_index, 0, keepdims=False)
        own_logs = own_logs[None, :]

    step_as_real = optimizer_step_count[0].astype(F32)
    fades = (1.0 - beta_first**step_as_real, 1.0 - beta_second**step_as_real)
    lanes = lambda value: jnp.pad(
        jnp.broadcast_to(value, (1, value.size if value.ndim else 128)), ((0, 0), (0, 128))
    )[:, :128]
    facts = jnp.concatenate(
        [lanes(value) for value in (row_weight, *fades, target_bias)] + [jnp.zeros((4, 128), F32)]
    )
    hidden_grad, dense_gradient, late, facts = last_backward(
        mean_t, own_logs, own_rows, got, code, facts, saved, place_col, place_row, seg_wide, downs, in_last, adapters,
        out_last, *slabs[1], gains, head_full, 3 * rank, shards if grouped else None,
    )
    back = (hidden_grad, one, two, slope, out_first)
    adapts = (adapter_up_matrix, adapter_moment_first, adapter_moment_second)
    heads = (head_projection, head_moment_first, head_moment_second)
    if grouped:
        sums, dense_portion, adapter_portion = finish(
            (*back, first_in, feed_full, gains), qkv, logs, seg_wide, seg_row, mid, dense_gradient, late, facts, rank, shards
        )
        loss, norm, *new = update(sums, dense_portion, adapter_portion, facts, heads, adapts)
        return (loss[0, 0], norm[0, 0], *new[3:], *new[:3])
    dctx = after_back(*back, *slabs[0], gains)
    first = attend_back(qkv, dctx, logs, seg_wide, seg_row, mid, rank)
    adapter_gradient = (first + late)[:, : 2 * rank * layers].T.reshape(layers, 2, rank, hidden)
    dense_portion = lax.psum_scatter(dense_gradient, BOTH, scatter_dimension=0, tiled=True)
    adapter_portion = lax.psum_scatter(adapter_gradient, BOTH, scatter_dimension=3, tiled=True)
    squared_entries = jnp.sum(adapter_portion * adapter_portion) + jnp.sum(dense_portion * dense_portion)
    masked_task_loss, norm_square = lax.psum((facts[0, 0], squared_entries), BOTH)
    gradient_norm = jnp.sqrt(norm_square)
    factor = jnp.minimum(1.0, clip_limit / (gradient_norm + 1e-06))
    adapter_new = adam(adapts[0], adapter_portion * factor, *adapts[1:], *fades)
    dense_new = adam(heads[0], dense_portion * factor, *heads[1:], *fades)
    return (masked_task_loss, gradient_norm, *adapter_new, *dense_new)


def solution(mesh):
    rows = P(BOTH, None)
    in_specs = (
        rows,
        rows,
        rows,
        rows,
        P(BOTH),
        P(),
        P(),
        P("dp", None),
        P(),
        P(),
        P(),
        P(None, None, BOTH),
        P(None, None, BOTH),
        P(None, None, BOTH),
        P(None, BOTH, None),
        P(),
        P(),
        P(BOTH),
        P(),
        P(None, None, None, BOTH),
        P(None, None, None, BOTH),
        P(None, None, None, BOTH),
        rows,
        rows,
        rows,
    )
    adapter = P(None, None, None, BOTH)
    out_specs = (P(), P(), adapter, adapter, adapter, rows, rows, rows)
    return jax.shard_map(
        per_device, mesh=mesh, in_specs=in_specs, out_specs=out_specs, check_vma=False
    )
```

```python
import functools

import jax
import jax.numpy as jnp
from jax import lax
from jax.experimental import pallas as pl
from jax.experimental.pallas import tpu as pltpu
from jax.sharding import PartitionSpec as P

HEADS = 12
TASKS = 4
REACH = 128

norm_eps = 1e-05
adapter_scale = 2.0
clip_limit = 0.01
learn_rate = 0.05
beta_first = 0.9
beta_second = 0.999
adam_eps = 1e-08
decay_rate = 0.01
masked_score = -1e30

BF = jnp.bfloat16
F32 = jnp.float32
BOTH = ("dp", "fsdp")
VMEM_BYTES = 60 * 1024 * 1024


def mm(a, b):
    return lax.dot_general(a, b, (((1,), (0,)), ((), ())), preferred_element_type=F32)


def mm_nt(a, b):
    return lax.dot_general(a, b, (((1,), (1,)), ((), ())), preferred_element_type=F32)


def mm_tn(a, b):
    return lax.dot_general(a, b, (((0,), (0,)), ((), ())), preferred_element_type=F32)


def layer_norm(rows_in, gain, shift):
    center = rows_in - jnp.mean(rows_in, -1, keepdims=True)
    spread = jnp.mean(center * center, -1, keepdims=True)
    return center * lax.rsqrt(spread + norm_eps) * gain + shift


def norm_back(rows_in, gain, gradient):
    center = rows_in - jnp.mean(rows_in, -1, keepdims=True)
    inverse = lax.rsqrt(jnp.mean(center * center, -1, keepdims=True) + norm_eps)
    unit = center * inverse
    scaled = gradient * gain
    return inverse * (
        scaled
        - jnp.mean(scaled, -1, keepdims=True)
        - unit * jnp.mean(scaled * unit, -1, keepdims=True)
    )


def gelu_pair(v):
    size = jnp.abs(v) * 0.7071067811865476
    base = 1.0 + 0.3275911 * size
    t = pl.reciprocal(base, approx=True)
    t = t * (2.0 - base * t)
    bell = jnp.exp(-0.5 * v * v)
    poly = t * (
        0.127414796 + t * (-0.142248368 + t * (0.7107068705 + t * (-0.7265760135 + t * 0.5307027145)))
    )
    tail = poly * bell
    phi = jnp.where(v >= 0.0, 1.0 - tail, tail)
    return v * phi, phi + v * (bell * 0.3989422804014327)


def params(**more):
    return pltpu.CompilerParams(vmem_limit_bytes=VMEM_BYTES, **more)


def full(shape):
    return pl.BlockSpec(shape, lambda *_: (0,) * len(shape))


def split_of(total, most, step):
    size = (min(most, total) // step) * step
    while size > step and total % size:
        size -= step
    return size if size and total % size == 0 else total


def pair_rows(block, width):
    first = lax.broadcasted_iota(jnp.int32, block.shape, 1) < width
    return jnp.concatenate([jnp.where(first, block, 0.0), jnp.where(first, 0.0, block)], 0).astype(BF)


def pair_join(wide, width):
    rows = wide.shape[1] // 2
    return jnp.concatenate([wide[:width, :rows], wide[width:, rows:]], 0)


def masked(scores, same):
    rows = scores.shape[1] // 2
    return jnp.concatenate(
        [
            jnp.where(same, scores[:, :rows], masked_score),
            jnp.where(same, scores[:, rows:], masked_score),
        ],
        1,
    )


def qkv_bias(bias_ref, layer, start, size):
    hidden = bias_ref.shape[1] // 8
    if start >= 2 * hidden:
        return bias_ref[layer : layer + 1, start - hidden : start - hidden + size]
    return bias_ref[layer : layer + 1, start : start + size] if start < hidden else 0.0


def norm_of(norm_refs, k):
    return norm_refs[0][k : k + 1, :], norm_refs[1][k : k + 1, :]


def project_body(
    own_ref, got_ref, code_ref, spots_ref, gain_ref, shift_ref, down_ref, w_ref, up_ref, bias_ref,
    out_ref, mid_ref, x_ref,
):
    mine = code_ref[...] % 2
    choose = (
        lax.broadcasted_iota(jnp.int32, (own_ref.shape[0], spots_ref.shape[0]), 1) == code_ref[...] // 2
    )
    summed = jnp.where(
        mine > 0, own_ref[...].astype(F32), got_ref[...].astype(F32)
    ) + mm(choose.astype(F32).astype(BF), spots_ref[...])
    x = layer_norm(summed, *norm_of((gain_ref, shift_ref), 0))
    x_ref[...] = x
    low = x.astype(BF)
    mid = mm(low, down_ref[0]).astype(BF)
    mid_ref[...] = mid
    total = w_ref.shape[0]
    step = total // 3
    for start in range(0, total, step):
        part = slice(start, start + step)
        out_ref[:, part] = (
            mm_nt(low, w_ref[part, :]) + mm(mid, up_ref[0, :, part]) + qkv_bias(bias_ref, 0, start, step)
        ).astype(BF)


def project(own, got, code, spots, gains, shifts, down, w, up, bias, rows):
    width = own.shape[1]
    tile = split_of(rows, 256, 16)
    total = w.shape[0]
    row = lambda n: pl.BlockSpec((tile, n), lambda i: (i, 0))
    return pl.pallas_call(
        project_body,
        grid=(rows // tile,),
        in_specs=[row(width), row(width), row(1)]
        + [full(a.shape) for a in (spots, gains, shifts, down, w, up, bias)],
        out_specs=[row(total), row(down.shape[2]), row(width)],
        out_shape=[
            jax.ShapeDtypeStruct((rows, total), BF),
            jax.ShapeDtypeStruct((rows, down.shape[2]), BF),
            jax.ShapeDtypeStruct((rows, width), F32),
        ],
        compiler_params=params(),
        name="project",
    )(own, got, code, spots, gains, shifts, down, w, up, bias)


def attend_body(q_ref, k_ref, v_ref, seg_ref, seg_row_ref, ctx_ref, log_ref):
    rows = q_ref.shape[0]
    width = q_ref.shape[1] // 2
    scale = width**-0.5
    turned = turn_blocks(v_ref)

    def scored(start):
        own, near = reach_of(start, rows)
        return mm_nt(k_ref[near, :], pair_rows(q_ref[own, :].astype(F32) * scale, width))

    scores = scored(0)
    for start in range(0, rows, REACH):
        own, near = reach_of(start, rows)
        later = scored(start + REACH) if start + REACH < rows else None
        same = seg_ref[near, :] == seg_row_ref[:, own]
        scores = masked(scores, same)
        top = jnp.max(scores, 0, keepdims=True)
        weights = jnp.exp(scores - top)
        total = jnp.sum(weights, 0, keepdims=True)
        context = mm(turned[:, near], weights.astype(BF)) * (1.0 / total)
        ctx_ref[own, :] = pair_join(context, width).T.astype(BF)
        log_ref[0, :, 2 * start : 2 * start + 2 * REACH] = top + jnp.log(total)
        scores = later


def reach_of(start, rows):
    return slice(start, start + REACH), slice(max(0, start - REACH), min(rows, start + 2 * REACH))


def turn_blocks(ref):
    blocks = [ref[k : k + 128, :].astype(F32).T.astype(BF) for k in range(0, ref.shape[0], 128)]
    return jnp.concatenate(blocks, 1)


def attend(qkv, seg_wide, seg_row):
    rows, total = qkv.shape
    hidden = total // 3
    lanes = 2 * (hidden // HEADS)
    pairs = hidden // lanes
    column = lambda kind: pl.BlockSpec((rows, lanes), lambda p: (0, kind * pairs + p))
    return pl.pallas_call(
        attend_body,
        grid=(pairs,),
        in_specs=[column(0), column(1), column(2), full(seg_wide.shape), full(seg_row.shape)],
        out_specs=[
            pl.BlockSpec((rows, lanes), lambda p: (0, p)),
            pl.BlockSpec((1, 1, 2 * rows), lambda p: (p, 0, 0)),
        ],
        out_shape=[
            jax.ShapeDtypeStruct((rows, hidden), BF),
            jax.ShapeDtypeStruct((pairs, 1, 2 * rows), F32),
        ],
        compiler_params=params(),
        name="attend",
    )(qkv, qkv, qkv, seg_wide, seg_row)


def flat(ref):
    whole = ref[...]
    return whole.reshape(-1, whole.shape[-1])


def rows_of(ref, start, size):
    each = ref.shape[1]
    if size % each == 0 and start % each == 0 and each % 16 == 0:
        part = ref[start // each : (start + size) // each, :, :]
        return part.reshape(size, part.shape[-1])
    return flat(ref)[start : start + size, :]


def feed_step(ref):
    units = ref.shape[0] * ref.shape[1]
    step = ref.shape[1]
    while units % (2 * step) == 0 and 2 * step <= 768 and ref.shape[0] > 1:
        step *= 2
    return units, (step if ref.shape[0] > 1 else split_of(units, 768, 128))


def later_biases(bias_ref, layer):
    hidden = bias_ref.shape[1] // 8
    row = bias_ref[layer : layer + 1, :]
    return row[:, 2 * hidden : 3 * hidden], row[:, 3 * hidden : 7 * hidden], row[:, 7 * hidden :]


def after_body(
    ctx_ref, x_ref, wo_ref, up_ref, down_ref, bias_ref, gain_ref, shift_ref,
    out_ref, one_ref, two_ref, slope_ref,
):
    bo, b1, b2 = later_biases(bias_ref, 0)
    one = x_ref[...] + (mm_nt(ctx_ref[...], wo_ref[...]) + bo)
    one_ref[...] = one
    middle = layer_norm(one, *norm_of((gain_ref, shift_ref), 1))
    low = middle.astype(BF)
    total = middle + b2
    units, step = feed_step(up_ref)
    gate = mm_nt(low, rows_of(up_ref, 0, step))
    for start in range(0, units, step):
        part = slice(start, start + step)
        later = mm_nt(low, rows_of(up_ref, start + step, step)) if start + step < units else None
        act, slope = gelu_pair(gate + b1[:, part])
        slope_ref[:, part] = slope.astype(BF)
        total = total + mm(act.astype(BF), rows_of(down_ref, start, step))
        gate = later
    two_ref[...] = total
    out_ref[...] = layer_norm(total, *norm_of((gain_ref, shift_ref), 2))


def slab_spec(slab):
    array, place, rows = slab
    return pl.BlockSpec((array.shape[0], rows, array.shape[2]), lambda *_: (0, place, 0))


def after(ctx, x, wo, up, down, bias, gains, shifts):
    rows, width = x.shape
    tile = split_of(rows, 256, 16)
    units = 4 * width
    row = lambda n: pl.BlockSpec((tile, n), lambda i: (i, 0))
    return pl.pallas_call(
        after_body,
        grid=(rows // tile,),
        in_specs=[row(width), row(width), full(wo.shape), slab_spec(up), slab_spec(down)]
        + [full(a.shape) for a in (bias, gains, shifts)],
        out_specs=[row(width), row(width), row(width), row(units)],
        out_shape=[jax.ShapeDtypeStruct((rows, width), F32)] * 3
        + [jax.ShapeDtypeStruct((rows, units), BF)],
        compiler_params=params(),
        name="after",
    )(ctx, x, wo, up[0], down[0], bias, gains, shifts)


def exact_rows(choose, matrix):
    high = matrix.astype(BF)
    rest = matrix - high.astype(F32)
    middle = rest.astype(BF)
    low = (rest - middle.astype(F32)).astype(BF)
    return mm(choose, high) + mm(choose, middle) + mm(choose, low)


def unpack_rows(slab_ref, targets):
    shards = slab_ref.shape[0]

    @pl.loop(0, shards // 2)
    def _(k):
        first, second = slab_ref[2 * k].astype(F32), slab_ref[2 * k + 1].astype(F32)
        at = 0
        for target in targets:
            each = target.shape[0] // shards
            both = jnp.concatenate([first[at : at + each], second[at : at + each]], 0)
            target[pl.ds(pl.multiple_of(2 * each * k, 2 * each), 2 * each), :] = both.astype(BF)
            at += each


def last_forward_body(
    x_ref, place_ref, place_row_ref, seg_ref, down_ref, adapt_ref, bias_ref, weights_any, up_any, dn_any,
    gain_ref, shift_ref, hbias_ref,
    kv_ref, q_ref, mid_ref, log_ref, one_ref, slope_ref, two_ref, low_ref, act_ref, hslope_ref, feat_ref, *more,
    places, starts,
):
    copies = []
    if starts is None:
        up_ref, dn_ref, ctx_ref, w_ref, wo_ref, hb_ref, sems = more
        sources = zip(weights_any, (w_ref, wo_ref, hb_ref))
    else:
        w_out, wo_out, hb_out, up_ref, dn_ref, ctx_ref, w_ref, wo_ref, hb_ref, in_slab, hb_slab, sems = more
        sources = [
            (weights_any[0].at[:, pl.ds(start, slab.shape[1]), :], slab)
            for start, slab in zip(starts, (in_slab, hb_slab))
        ]
    for source, target in sources:
        copies.append((source, target))
    early = len(copies)
    for source, target, place in ((up_any, up_ref, places[0]), (dn_any, dn_ref, places[1])):
        each = target.shape[1]
        copies.append((source.at[:, pl.ds(place * each, each), :], target))
    copies = [pltpu.make_async_copy(*ends, sems.at[k]) for k, ends in enumerate(copies)]
    for copy in copies:
        copy.start()
    for copy in copies[:early]:
        copy.wait()
    copies = copies[early:]
    if starts is not None:
        unpack_rows(in_slab, (w_ref, wo_ref))
        unpack_rows(hb_slab, (hb_ref,))
        for k, ends in enumerate(((w_ref, w_out), (wo_ref, wo_out), (hb_ref, hb_out))):
            copies.append(pltpu.make_async_copy(*ends, sems.at[4 + k]))
            copies[-1].start()
    rows, hidden = x_ref.shape
    labels = place_ref.shape[0]
    lanes = 2 * (hidden // HEADS)
    width = lanes // 2
    low = x_ref[...].astype(BF)
    mid = mm(low, down_ref[1]).astype(BF)
    mid_ref[...] = mid
    step = split_of(hidden, 768, 128)
    for start in range(hidden, 3 * hidden, step):
        part = slice(start, start + step)
        kv_ref[:, start - hidden : start - hidden + step] = (
            mm_nt(low, w_ref[part, :]) + mm(mid, adapt_ref[1, :, part]) + qkv_bias(bias_ref, 1, start, step)
        ).astype(BF)
    choose = (
        lax.broadcasted_iota(jnp.int32, (labels, rows), 1) == place_ref[...][:, 0:1]
    ).astype(F32).astype(BF)
    own = exact_rows(choose, x_ref[...])
    own_low = own.astype(BF)
    own_mid = mm(choose, mid).astype(BF)
    q_ref[...] = (
        mm_nt(own_low, w_ref[:hidden, :])
        + mm(own_mid, adapt_ref[1, :, :hidden])
        + qkv_bias(bias_ref, 1, 0, hidden)
    ).astype(BF)
    seg = seg_ref[...]
    seg_own = jnp.sum(
        jnp.where(
            lax.broadcasted_iota(jnp.int32, (rows, labels), 0) == place_row_ref[...], seg, 0.0
        ),
        0,
        keepdims=True,
    )
    same = seg == seg_own

    def scored(p):
        part = slice(p * lanes, (p + 1) * lanes)
        return mm_nt(kv_ref[:, part], pair_rows(q_ref[:, part].astype(F32) * width**-0.5, width))

    later = scored(0)
    for p in range(hidden // lanes):
        part = slice(p * lanes, (p + 1) * lanes)
        scores = masked(later, same)
        later = scored(p + 1) if (p + 1) * lanes < hidden else None
        top = jnp.max(scores, 0, keepdims=True)
        weights = jnp.exp(scores - top)
        total = jnp.sum(weights, 0, keepdims=True)
        context = mm_tn(
            kv_ref[:, hidden + p * lanes : hidden + (p + 1) * lanes], weights.astype(BF)
        ) * (1.0 / total)
        ctx_ref[:, part] = pair_join(context, width).T.astype(BF)
        log_ref[p : p + 1, :] = top + jnp.log(total)
    bo, b1, b2 = later_biases(bias_ref, 1)
    norms = (gain_ref, shift_ref)
    one = own + (mm_nt(ctx_ref[...], wo_ref[...]) + bo)
    one_ref[...] = one
    middle = layer_norm(one, *norm_of(norms, 3))
    middle_low = middle.astype(BF)
    sum_two = middle + b2
    units, step = feed_step(up_ref)
    for copy in copies:
        copy.wait()
    gate = mm_nt(middle_low, rows_of(up_ref, 0, step))
    for start in range(0, units, step):
        part = slice(start, start + step)
        later = mm_nt(middle_low, rows_of(up_ref, start + step, step)) if start + step < units else None
        act, slope = gelu_pair(gate + b1[:, part])
        gate = later
        slope_ref[:, part] = slope.astype(BF)
        sum_two = sum_two + mm(act.astype(BF), rows_of(dn_ref, start, step))
    two_ref[...] = sum_two
    out_low = layer_norm(sum_two, *norm_of(norms, 4)).astype(BF)
    low_ref[...] = out_low
    act, slope = gelu_pair(mm(out_low, hb_ref[...]) + hbias_ref[...])
    act_ref[...] = act
    hslope_ref[...] = slope
    feat_ref[...] = layer_norm(act, *norm_of(norms, 5)).astype(BF)


def slab_scratch(slab):
    array, place, rows = slab
    return pltpu.VMEM((array.shape[0], rows, array.shape[2]), BF)


def last_forward(
    x, place_col, place_row, seg_wide, down, adapt, bias, weights, starts, up, dn, gains, shifts, hbias
):
    rows, hidden = x.shape
    labels = place_col.shape[0]
    units = 4 * hidden
    whole = pl.BlockSpec(memory_space=pltpu.VMEM)
    anywhere = pl.BlockSpec(memory_space=pl.ANY)
    shape = jax.ShapeDtypeStruct
    pairs = HEADS // 2
    matrices = [(3 * hidden, hidden), (hidden, hidden), (hidden, hidden)]
    slabs = []
    if starts is not None:
        shards = weights[0].shape[0]
        slabs = [
            pltpu.VMEM((shards, 4 * hidden // shards, hidden), BF),
            pltpu.VMEM((shards, weights[0].shape[1] - starts[1], hidden), BF),
        ]

    def body(*refs):
        head, rest = refs[:7], refs[7:]
        return last_forward_body(
            *head, rest[: len(weights)], *rest[len(weights) :], places=(up[1], dn[1]), starts=starts
        )

    return pl.pallas_call(
        body,
        in_specs=[whole] * 7 + [anywhere] * (len(weights) + 2) + [whole] * 3,
        out_specs=[whole] * 11 + ([anywhere] * 3 if slabs else []),
        out_shape=[
            shape((rows, 2 * hidden), BF),
            shape((labels, hidden), BF),
            shape((rows, down.shape[2]), BF),
            shape((pairs, 2 * labels), F32),
            shape((labels, hidden), F32),
            shape((labels, units), BF),
            shape((labels, hidden), F32),
            shape((labels, hidden), BF),
            shape((labels, hidden), F32),
            shape((labels, hidden), F32),
            shape((labels, hidden), BF),
        ]
        + ([shape(m, BF) for m in matrices] if slabs else []),
        scratch_shapes=[
            slab_scratch(up),
            slab_scratch(dn),
            pltpu.VMEM((labels, hidden), BF),
            *[pltpu.VMEM(m, BF) for m in matrices],
            *slabs,
            pltpu.SemaphoreType.DMA((7,)),
        ],
        compiler_params=params(),
        name="last_forward",
    )(x, place_col, place_row, seg_wide, down, adapt, bias, *weights, up[0], dn[0], gains, shifts, hbias)


def vocab_body(u_ref, e_ref, et_ref, bias_ref, num_ref, log_ref, scores, weights):
    count = e_ref.shape[0]
    step = split_of(count, 640, 16)
    u = u_ref[...]
    rows = u.shape[0]
    labels = num_ref.shape[2]
    top = jnp.full((1, rows), -jnp.inf, F32)
    for start in range(0, count, step):
        part = slice(start, start + step)
        bias = bias_ref[part, :]
        logits = mm_nt(e_ref[part, :], u) + jnp.concatenate([bias] * (rows // bias.shape[1]), 1)
        scores[part, :] = logits
        top = jnp.maximum(top, jnp.max(logits, 0, keepdims=True))
    total = jnp.zeros((1, rows), F32)
    for start in range(0, count, step):
        part = slice(start, start + step)
        grown = jnp.exp(scores[part, :] - top)
        total = total + jnp.sum(grown, 0, keepdims=True)
        weights[part, :] = grown.astype(BF)
    mean = mm(et_ref[...], weights[...]) * (1.0 / total)
    logs = top + jnp.log(total)
    for k in range(rows // labels):
        num_ref[k, :, :] = mean[:, k * labels : (k + 1) * labels]
        log_ref[k, :, :] = logs[:, k * labels : (k + 1) * labels]


def vocab(u, e, et, bias_wide, labels):
    rows, hidden = u.shape
    count = e.shape[0]
    tile = 2 * labels
    return pl.pallas_call(
        vocab_body,
        grid=(rows // tile,),
        in_specs=[
            pl.BlockSpec((tile, hidden), lambda i: (i, 0)),
            full(e.shape),
            full(et.shape),
            full(bias_wide.shape),
        ],
        out_specs=[
            pl.BlockSpec((2, hidden, labels), lambda i: (i, 0, 0)),
            pl.BlockSpec((2, 1, labels), lambda i: (i, 0, 0)),
        ],
        out_shape=[
            jax.ShapeDtypeStruct((rows // labels, hidden, labels), F32),
            jax.ShapeDtypeStruct((rows // labels, 1, labels), F32),
        ],
        scratch_shapes=[pltpu.VMEM((count, tile), F32), pltpu.VMEM((count, tile), BF)],
        compiler_params=params(),
        name="vocab",
    )(u, e, et, bias_wide)


def last_backward_body(
    own_any, got_any, mean_ref, all_log_ref, code_ref, fact_ref, kv_ref, q_ref, mid_ref, log_ref, one_ref, slope_ref, two_ref,
    low_ref, act_ref, hslope_ref, feat_ref, place_ref, place_row_ref, seg_ref, down_ref, w_ref, adapt_ref, wo_ref,
    up_any, dn_any, gain_ref, hb_ref,
    dx_ref, gh_ref, g_ref, out_fact_ref,
    up_ref, dn_ref, dkv_ref, dq_ref, aims, sems, *, places, edge,
):
    labels = place_ref.shape[0]
    tail = pl.ds(kv_ref.shape[0], labels)
    aimed = [
        pltpu.make_async_copy(source.at[tail, :], aims.at[k], sems.at[2 + k])
        for k, source in enumerate((own_any, got_any))
    ]
    for copy in aimed:
        copy.start()
    copies = []
    for k, (source, target, place) in enumerate(
        ((up_any, up_ref, places[0]), (dn_any, dn_ref, places[1]))
    ):
        rows = target.shape[1]
        copies.append(
            pltpu.make_async_copy(
                source.at[:, pl.ds(place * rows, rows), :], target, sems.at[k]
            )
        )
        copies[-1].start()
    rows = kv_ref.shape[0]
    labels, hidden = feat_ref.shape
    lanes = 2 * (hidden // HEADS)
    width = lanes // 2
    scale = width**-0.5
    for copy in aimed:
        copy.wait()
    mine = code_ref[kv_ref.shape[0] :, :] % 2
    targets = jnp.where(mine > 0, aims[0].astype(F32), aims[1].astype(F32))
    weight = fact_ref[0:1, 0:1]
    chosen = jnp.sum(feat_ref[...].astype(F32) * targets, keepdims=True)
    loss = weight * (jnp.sum(all_log_ref[...] - fact_ref[3:4, :labels], keepdims=True) - chosen)
    out_fact_ref[...] = jnp.where(
        lax.broadcasted_iota(jnp.int32, fact_ref.shape, 0) == 0, loss, fact_ref[...]
    )
    du = weight * (mean_ref[...].T - targets)
    dact = norm_back(act_ref[...], gain_ref[5:6, :], du)
    dz = (hslope_ref[...] * dact).astype(BF)
    dense = mm_tn(low_ref[...], dz)
    if len(gh_ref.shape) == 2:
        gh_ref[...] = dense
    else:
        each = hidden // gh_ref.shape[0]
        spare = jnp.zeros((gh_ref.shape[1] - each, hidden), F32)
        for k in range(gh_ref.shape[0]):
            gh_ref[k] = jnp.concatenate([dense[k * each : (k + 1) * each, :], spare], 0).astype(BF)
    dtwo = norm_back(two_ref[...], gain_ref[4:5, :], mm_nt(dz, hb_ref[...]))
    dtwo_low = dtwo.astype(BF)
    dmiddle = dtwo
    units, step = feed_step(up_ref)
    for copy in copies:
        copy.wait()
    dact = mm_nt(dtwo_low, rows_of(dn_ref, 0, step))
    for start in range(0, units, step):
        part = slice(start, start + step)
        later = mm_nt(dtwo_low, rows_of(dn_ref, start + step, step)) if start + step < units else None
        dgate = (slope_ref[:, part].astype(F32) * dact).astype(BF)
        dmiddle = dmiddle + mm(dgate, rows_of(up_ref, start, step))
        dact = later
    done = norm_back(one_ref[...], gain_ref[3:4, :], dmiddle)
    dctx = mm(done.astype(BF), wo_ref[...]).astype(BF)
    seg = seg_ref[...]
    choose_t = lax.broadcasted_iota(jnp.int32, (rows, labels), 0) == place_row_ref[...]
    same = seg == jnp.sum(jnp.where(choose_t, seg, 0.0), 0, keepdims=True)

    def products(p):
        part = slice(p * lanes, (p + 1) * lanes)
        later = slice(hidden + p * lanes, hidden + (p + 1) * lanes)
        queries = pair_rows(q_ref[:, part].astype(F32) * scale, width)
        outs = pair_rows(dctx[:, part].astype(F32), width)
        return queries, outs, mm_nt(kv_ref[:, part], queries), mm_nt(kv_ref[:, later], outs)

    ahead = products(0)
    for p in range(hidden // lanes):
        part = slice(p * lanes, (p + 1) * lanes)
        later = slice(hidden + p * lanes, hidden + (p + 1) * lanes)
        queries, outs, scores, dweights = ahead
        ahead = products(p + 1) if (p + 1) * lanes < hidden else None
        keys = kv_ref[:, part]
        weights = jnp.exp(masked(scores, same) - log_ref[p : p + 1, :])
        inner = jnp.sum(dweights * weights, 0, keepdims=True)
        dscores = (weights * (dweights - inner)).astype(BF)
        dkv_ref[:, part] = mm(dscores, queries).astype(BF)
        dkv_ref[:, later] = mm(weights.astype(BF), outs).astype(BF)
        dq_ref[:, part] = (pair_join(mm_tn(keys, dscores), width) * scale).T.astype(BF)
    dq = dq_ref[...]
    own_mid = mm(
        (lax.broadcasted_iota(jnp.int32, (labels, rows), 1) == place_ref[...][:, 0:1]).astype(F32).astype(BF),
        mid_ref[...],
    ).astype(BF)
    g_ref[...] = adapter_scale * jnp.where(
        lax.broadcasted_iota(jnp.int32, g_ref.shape, 1) < edge,
        mm_tn(dq, own_mid),
        mm_tn(dkv_ref[:, hidden:], mid_ref[...]),
    )
    dmid_own = mm_nt(dq, adapt_ref[1, :, :hidden]).astype(BF)
    own = done + mm(dq, w_ref[:hidden, :]) + mm_nt(dmid_own, down_ref[1])
    spread = choose_t.astype(F32).astype(BF)
    own_high = own.astype(BF)
    own_rest = (own - own_high.astype(F32)).astype(BF)
    dmid = mm_nt(dkv_ref[:, hidden:], adapt_ref[1, :, 2 * hidden :]).astype(BF)
    step = split_of(hidden, 256, 128)
    for start in range(0, hidden, step):
        part = slice(start, start + step)
        dx_ref[:, part] = (
            mm(dkv_ref[...], w_ref[hidden:, part])
            + mm_nt(dmid, down_ref[1, part, :])
            + mm(spread, own_high[:, part])
            + mm(spread, own_rest[:, part])
        )


def last_backward(
    mean, logs, own, got, code, facts, saved, place_col, place_row, seg_wide, down, w, adapt, wo, up, dn, gains, hb, edge, shards
):
    kv = saved[0]
    rows = kv.shape[0]
    labels, hidden = saved[-1].shape
    whole = pl.BlockSpec(memory_space=pltpu.VMEM)
    anywhere = pl.BlockSpec(memory_space=pl.ANY)
    shape = jax.ShapeDtypeStruct
    return pl.pallas_call(
        functools.partial(last_backward_body, places=(up[1], dn[1]), edge=edge),
        in_specs=[anywhere] * 2 + [whole] * 22 + [anywhere] * 2 + [whole] * 2,
        out_specs=[whole] * 4,
        out_shape=[
            shape((rows, hidden), F32),
            shape((hidden, hidden), F32)
            if shards is None
            else shape((shards, -(-hidden // shards // 16) * 16, hidden), BF),
            shape((hidden, down.shape[2]), F32),
            shape(facts.shape, F32),
        ],
        scratch_shapes=[
            slab_scratch(up),
            slab_scratch(dn),
            pltpu.VMEM(kv.shape, BF),
            pltpu.VMEM((labels, hidden), BF),
            pltpu.VMEM((2, labels, hidden), BF),
            pltpu.SemaphoreType.DMA((4,)),
        ],
        compiler_params=params(),
        name="last_backward",
    )(own, got, mean, logs, code, facts, *saved, place_col, place_row, seg_wide, down, w, adapt, wo, up[0], dn[0], gains, hb)


def after_back_body(dout_ref, one_ref, two_ref, slope_ref, wo_ref, up_ref, down_ref, gain_ref, dctx_ref):
    dtwo = norm_back(two_ref[...], gain_ref[2:3, :], dout_ref[...])
    low = dtwo.astype(BF)
    dmiddle = dtwo
    units, step = feed_step(up_ref)
    dact = mm_nt(low, rows_of(down_ref, 0, step))
    for start in range(0, units, step):
        part = slice(start, start + step)
        later = mm_nt(low, rows_of(down_ref, start + step, step)) if start + step < units else None
        dgate = (slope_ref[:, part].astype(F32) * dact).astype(BF)
        dmiddle = dmiddle + mm(dgate, rows_of(up_ref, start, step))
        dact = later
    done = norm_back(one_ref[...], gain_ref[1:2, :], dmiddle)
    dctx_ref[...] = mm(done.astype(BF), wo_ref[...]).astype(BF)


def after_back(dout, one, two, slope, wo, up, down, norms):
    rows, width = dout.shape
    tile = split_of(rows, 256, 16)
    row = lambda n: pl.BlockSpec((tile, n), lambda i: (i, 0))
    return pl.pallas_call(
        after_back_body,
        grid=(rows // tile,),
        in_specs=[row(width), row(width), row(width), row(slope.shape[1]), full(wo.shape)]
        + [slab_spec(up), slab_spec(down), full(norms.shape)],
        out_specs=row(width),
        out_shape=jax.ShapeDtypeStruct((rows, width), BF),
        compiler_params=params(),
        name="after_back",
    )(dout, one, two, slope, wo, up[0], down[0], norms)


def attend_back_body(
    q_ref, k_ref, v_ref, dctx_ref, log_ref, seg_ref, seg_row_ref, mid_ref, g_ref, dv_ref, *, edge
):
    rows = q_ref.shape[0]
    width = q_ref.shape[1] // 2
    scale = width**-0.5
    dv_ref[...] = jnp.zeros_like(dv_ref)
    gq = jnp.zeros((2 * width, mid_ref.shape[1]), F32)
    turned = turn_blocks(k_ref)

    def products(start):
        own, near = reach_of(start, rows)
        queries = pair_rows(q_ref[own, :].astype(F32) * scale, width)
        outs = pair_rows(dctx_ref[own, :].astype(F32), width)
        return outs, mm_nt(k_ref[near, :], queries), mm_nt(v_ref[near, :], outs)

    now = products(0)
    for start in range(0, rows, REACH):
        own, near = reach_of(start, rows)
        later = products(start + REACH) if start + REACH < rows else None
        outs, scores, dweights = now
        same = seg_ref[near, :] == seg_row_ref[:, own]
        logs = log_ref[0, :, 2 * start : 2 * start + 2 * REACH]
        weights = jnp.exp(masked(scores, same) - logs)
        inner = jnp.sum(dweights * weights, 0, keepdims=True)
        dscores = (weights * (dweights - inner)).astype(BF)
        dv_ref[near, :] += mm(weights.astype(BF), outs)
        dq = (pair_join(mm(turned[:, near], dscores), width) * scale).astype(BF)
        gq = gq + mm(dq, mid_ref[own, :])
        now = later
    gv = mm_tn(dv_ref[...].astype(BF), mid_ref[...])
    g_ref[...] = adapter_scale * jnp.where(
        lax.broadcasted_iota(jnp.int32, gq.shape, 1) < edge, gq, gv
    )


def attend_back(qkv, dctx, logs, seg_wide, seg_row, mid, edge):
    rows, total = qkv.shape
    hidden = total // 3
    lanes = 2 * (hidden // HEADS)
    pairs = hidden // lanes
    column = lambda kind: pl.BlockSpec((rows, lanes), lambda p: (0, kind * pairs + p))
    return pl.pallas_call(
        functools.partial(attend_back_body, edge=edge),
        grid=(pairs,),
        in_specs=[
            column(0),
            column(1),
            column(2),
            column(0),
            pl.BlockSpec((1, 1, 2 * rows), lambda p: (p, 0, 0)),
            full(seg_wide.shape),
            full(seg_row.shape),
            full(mid.shape),
        ],
        out_specs=pl.BlockSpec((lanes, mid.shape[1]), lambda p: (p, 0)),
        out_shape=jax.ShapeDtypeStruct((hidden, mid.shape[1]), F32),
        scratch_shapes=[pltpu.VMEM((rows, lanes), F32)],
        compiler_params=params(),
        name="attend_back",
    )(qkv, qkv, qkv, dctx, logs, seg_wide, seg_row, mid)


MESH = pl.DeviceIdType.MESH


def position():
    dp, fsdp = lax.axis_index("dp"), lax.axis_index("fsdp")
    return {"x": dp, "z": fsdp // 4, "y": (fsdp // 2) % 2, "c": fsdp % 2}


def device_of(place):
    return (place["x"], (place["z"] * 2 + place["y"]) * 2 + place["c"])


def number_of(place):
    return place["x"] * 16 + (place["z"] * 2 + place["y"]) * 2 + place["c"]


def rank_device(number):
    return (number // 16, number % 16)


def greet_all(shards):
    barrier = pltpu.get_barrier_semaphore()
    me = lax.axis_index("dp") * 16 + lax.axis_index("fsdp")

    @pl.loop(1, shards)
    def _(k):
        pl.semaphore_signal(
            barrier, inc=1, device_id=rank_device((me + k) % shards), device_id_type=MESH
        )


def await_all(shards):
    pl.semaphore_wait(pltpu.get_barrier_semaphore(), shards - 1)


def direct_copy(source, target, sems, me, k, shards):
    return pltpu.make_async_remote_copy(
        src_ref=source,
        dst_ref=target,
        send_sem=sems.at[0],
        recv_sem=sems.at[1],
        device_id=rank_device((me + k) % shards),
        device_id_type=MESH,
    )


def spread(piece_of, buffer, sems, me, shards):
    @pl.loop(1, shards)
    def _(k):
        direct_copy(piece_of((me + k) % shards), buffer.at[me], sems, me, k, shards).start()


def collect(buffer, sems, me, shards):
    whole = buffer.at[pl.ds(0, shards - 1)]
    copy = direct_copy(whole, whole, sems, me, 1, shards)
    copy.wait_recv()
    copy.wait_send()


def relative_places(order):
    places = [
        {"x": dx, "z": dz, "y": dy} for dx in (0, 1) for dz in range(-3, 4) for dy in (0, 1)
    ]
    size = lambda p: abs(p["x"]) + abs(p["z"]) + abs(p["y"])
    return sorted(places, key=lambda p: (abs(p[order[-1]]), size(p), [abs(p[a]) for a in order]))


class Gather:
    def __init__(self, chunk, full_buffer, start, rows, order, sends, receives, hands, hands_got):
        self.chunk, self.full, self.order = chunk, full_buffer, order
        self.part = pl.ds(start, rows)
        self.sends, self.receives, self.hands, self.hands_got = sends, receives, hands, hands_got
        self.here = position()
        self.items = relative_places(order)
        self.pending = []

    def origin(self, item):
        here = self.here
        return {"x": (here["x"] + item["x"]) % 2, "z": here["z"] - item["z"], "y": (here["y"] + item["y"]) % 2, "c": here["c"]}

    def key(self, place):
        return (place["x"] * 4 + place["z"]) * 2 + place["y"]

    def outward(self, item):
        deepest = max([k for k, axis in enumerate(self.order) if item[axis]], default=-1)
        ways = []
        if deepest >= 0 and self.order[deepest] == "z":
            ways.append(("z", 1 if item["z"] > 0 else -1))
        for axis in self.order[deepest + 1 :]:
            ways += [("z", 1), ("z", -1)] if axis == "z" else [(axis, 1)]
        return ways

    def copy(self, index, way, slot, item):
        here = self.here
        place = self.origin(item)
        number, key = number_of(place), self.key(place)
        mine = not any(item.values())
        source = self.chunk.at[self.part, :] if mine else self.full.at[number, self.part, :]
        if way is None:
            target = dict(here, c=1 - here["c"])
            sends, receives = self.hands.at[index], self.hands_got.at[key]
        else:
            axis, step = way
            target = dict(here)
            target[axis] = here["z"] + step if axis == "z" else 1 - here[axis]
            sends, receives = self.sends.at[index * 4 + slot], self.receives.at[key]
        return pltpu.make_async_remote_copy(
            src_ref=source,
            dst_ref=self.full.at[number, self.part, :],
            send_sem=sends,
            recv_sem=receives,
            device_id=device_of(target),
            device_id_type=MESH,
        )

    def valid(self, item):
        z = self.here["z"] - item["z"]
        return (z >= 0) & (z <= 3)

    def step(self, index):
        item = self.items[index]

        @pl.when(self.valid(item))
        def _():
            if any(item.values()):
                self.arrived(index, item)
            for slot, way in enumerate(self.outward(item)):
                self.when_way(way, lambda way=way, slot=slot: self.copy(index, way, slot, item).start())
            self.copy(index, None, 0, item).start()

    def when_way(self, way, act):
        axis, step = way
        if axis == "z":
            z = self.here["z"] + step
            pl.when((z >= 0) & (z <= 3))(act)
        else:
            act()

    def arrived(self, index, item):
        place = self.origin(item)
        spot = self.full.at[number_of(place), self.part, :]
        pltpu.make_async_remote_copy(
            src_ref=spot,
            dst_ref=spot,
            send_sem=self.sends.at[index * 4],
            recv_sem=self.receives.at[self.key(place)],
            device_id=device_of(dict(self.here, c=1 - self.here["c"])),
            device_id_type=MESH,
        ).wait_recv()

    def finish(self):
        for index, item in enumerate(self.items):

            @pl.when(self.valid(item))
            def _(index=index, item=item):
                for slot, way in enumerate(self.outward(item)):
                    self.when_way(way, lambda way=way, slot=slot: self.copy(index, way, slot, item).wait_send())
                self.copy(index, None, 0, item).wait_send()
                place = dict(self.origin(item), c=1 - self.here["c"])
                spot = self.full.at[number_of(place), self.part, :]
                pltpu.make_async_remote_copy(
                    src_ref=spot,
                    dst_ref=spot,
                    send_sem=self.hands.at[index],
                    recv_sem=self.hands_got.at[self.key(place)],
                    device_id=device_of(dict(self.here, c=1 - self.here["c"])),
                    device_id_type=MESH,
                ).wait_recv()


ITEMS = 28


PICK = 64
GROUP = 16


def start_body(
    streams, shards, ids, low_ref, groups_any, fact, chunk, got, own_rows, facts, full_chunk, et_out,
    table, stage, rows, et_ref,
    row_sends, row_gets, fact_sems, own_sems, sends, receives, hands, hands_got,
):
    here = position()
    me = number_of(here)
    across = device_of(dict(here, x=1 - here["x"]))
    half, hidden = own_rows.shape
    batches = half // PICK
    fill = pltpu.make_async_copy(groups_any, table, own_sems.at[0])
    fill.start()
    greet_all(shards)
    own = [
        pltpu.make_async_copy(source, target, own_sems.at[1 + k])
        for k, (source, target) in enumerate(((fact, facts.at[me]), (chunk, full_chunk.at[me])))
    ]
    for copy in own:
        copy.start()
    await_all(shards)
    gathers = [
        Gather(
            chunk, full_chunk, start, size, order, sends.at[k], receives.at[k], hands.at[k], hands_got.at[k]
        )
        for k, (start, size, order) in enumerate(streams)
    ]
    for gather in gathers:
        gather.step(0)
    spread(lambda peer: fact, facts, fact_sems, me, shards)

    def send_rows(b):
        part = pl.ds(b * PICK, PICK)
        return pltpu.make_async_remote_copy(
            src_ref=rows.at[part, :],
            dst_ref=got.at[part, :],
            send_sem=row_sends.at[b],
            recv_sem=row_gets.at[b],
            device_id=across,
            device_id_type=MESH,
        )

    def pick(b):
        @pl.loop(0, PICK // 8)
        def _(t):
            found = [table[ids[b * PICK + t * 8 + k]] for k in range(8)]
            stage[pl.ds(pl.multiple_of(t * 8, 8), 8)] = jnp.stack(found)

        choose = (
            lax.broadcasted_iota(jnp.int32, (PICK, PICK * GROUP), 1)
            == low_ref[b * PICK : (b + 1) * PICK, :]
        )
        rows[b * PICK : (b + 1) * PICK, :] = mm(choose.astype(F32).astype(BF), flat(stage)).astype(BF)
        if b < batches:
            send_rows(b).start()

    count = et_ref.shape[1]
    first_group = (here["y"] * 2 + here["c"]) * (count // GROUP)

    def turn(k):
        block = table[pl.ds(first_group + k * (128 // GROUP), 128 // GROUP)].reshape(128, hidden)
        et_ref[:, k * 128 : (k + 1) * 128] = block.astype(F32).T.astype(BF)

    fill.wait()
    picked, turned, blocks = 0, 0, count // 128
    for index in range(1, ITEMS):
        while picked < min(2 * batches, 6 + 4 * index):
            pick(picked)
            picked += 1
        if picked == 2 * batches:
            for k in range(turned, min(turned + 3, blocks)):
                turn(k)
            turned = min(turned + 3, blocks)
        for gather in gathers:
            gather.step(index)
    for k in range(turned, blocks):
        turn(k)
    outs = [
        pltpu.make_async_copy(et_ref, et_out, own_sems.at[3]),
        pltpu.make_async_copy(rows.at[pl.ds(half, half), :], own_rows, own_sems.at[4]),
    ]
    for copy in outs:
        copy.start()
    for gather in gathers:
        gather.finish()
    collect(facts, fact_sems, me, shards)
    for b in range(batches):
        send_rows(b).wait()
    for copy in own + outs:
        copy.wait()


def vocab_rows(table, like):
    here = position()
    count = like.shape[0]
    return table.at[pl.ds(pl.multiple_of((here["y"] * 2 + here["c"]) * count, 16), count), :]


def gather_sems(streams):
    sems = pltpu.SemaphoreType.DMA
    count = len(streams)
    return [sems((count, 4 * ITEMS)), sems((count, 16)), sems((count, ITEMS)), sems((count, 16))]


def streams_of(rows, parts):
    streams, start = [], 0
    for k, (order, share) in enumerate(parts):
        size = rows - start if k == len(parts) - 1 else round(rows * share / 16) * 16
        streams.append((start, size, order))
        start += size
    return streams


def start_exchange(ids, table, fact, chunk, shards):
    anywhere = pl.BlockSpec(memory_space=pl.ANY)
    shape = jax.ShapeDtypeStruct
    sems = pltpu.SemaphoreType.DMA
    streams = streams_of(chunk.shape[0], (("xzy", 0.5), ("zxy", 0.28), ("xyz", 0.22)))
    half, hidden = ids.shape[0] // 2, table.shape[1]
    count = table.shape[0] // 4
    low = jnp.arange(ids.size, dtype=jnp.int32) % PICK * GROUP + ids % GROUP
    return pl.pallas_call(
        functools.partial(start_body, streams, shards),
        in_specs=[
            pl.BlockSpec(memory_space=pltpu.SMEM),
            pl.BlockSpec(memory_space=pltpu.VMEM),
        ]
        + [anywhere] * 3,
        out_specs=[anywhere] * 5,
        out_shape=[
            shape((half, hidden), table.dtype),
            shape((half, hidden), table.dtype),
            shape((shards, *fact.shape), fact.dtype),
            shape((shards, *chunk.shape), chunk.dtype),
            shape((hidden, count), BF),
        ],
        scratch_shapes=[
            pltpu.VMEM((table.shape[0] // GROUP, GROUP, hidden), BF),
            pltpu.VMEM((PICK, GROUP, hidden), BF),
            pltpu.VMEM((2 * half, hidden), BF),
            pltpu.VMEM((hidden, count), BF),
            sems((half // PICK,)),
            sems((half // PICK,)),
            sems((2,)),
            sems((5,)),
            *gather_sems(streams),
        ],
        compiler_params=params(collective_id=1, has_side_effects=True),
        name="start_exchange",
    )(ids // GROUP, low[:, None], table.reshape(-1, GROUP, hidden), fact, chunk)


def first_layer_body(
    streams, shards,
    own_any, got_any, first_any, chunk, code_ref, spots_ref, gain_ref, shift_ref, down_ref,
    adapt_ref, bias_ref, seg_ref, seg_row_ref,
    qkv_out, x_out, one_out, two_out, slope_out, wo_out, full_chunk, mid_ref, log_ref,
    own, got, in_slab, w, wo, up, dn, x, qkv, ctx, two, out, slope,
    load_sems, tile_sems, out_sems, sends, receives, hands, hands_got,
):
    here = position()
    me = number_of(here)
    rows, hidden = x.shape
    tile = split_of(rows, 256, 16)
    tiles = rows // tile
    lanes = 2 * (hidden // HEADS)
    pairs = hidden // lanes

    def slab(source, target, start):
        return source.at[:, pl.ds(start, target.shape[1]), :]

    loads = [
        pltpu.make_async_copy(source, target, load_sems.at[k])
        for k, (source, target) in enumerate(
            (
                (own_any.at[pl.ds(0, rows), :], own),
                (got_any.at[pl.ds(0, rows), :], got),
                (slab(first_any, in_slab, 2 * up.shape[1]), in_slab),
                (slab(first_any, up, 0), up),
                (slab(first_any, dn, up.shape[1]), dn),
                (chunk, full_chunk.at[me]),
            )
        )
    ]
    for copy in loads:
        copy.start()
    barrier = pltpu.get_barrier_semaphore()
    peers = [
        dict(here, c=1 - here["c"]),
        dict(here, x=1 - here["x"]),
        dict(here, y=1 - here["y"]),
        *[dict(here, z=flip(here["z"], k)) for k in (1, 2, 3)],
    ]
    for peer in peers:
        pl.semaphore_signal(barrier, inc=1, device_id=device_of(peer), device_id_type=MESH)
    pl.semaphore_wait(barrier, len(peers))
    gathers = [
        Gather(
            chunk, full_chunk, start, size, order, sends.at[k], receives.at[k], hands.at[k], hands_got.at[k]
        )
        for k, (start, size, order) in enumerate(streams)
    ]
    def advance(*ranges):
        pairs_of = [(0, ranges[0]), (1, ranges[0])] + [(2, r) for r in ranges[1:]]
        for k, (first, last) in pairs_of:
            for index in range(first, last + 1):
                gathers[k].step(index)

    def at(i, plan):
        for k, ranges in plan.items():
            pl.when(i == k)(functools.partial(advance, *ranges))

    advance((0, 0), (0, 0))
    for copy in loads[:3]:
        copy.wait()
    unpack_rows(in_slab, (w, wo))

    @pl.loop(0, tiles)
    def _(i):
        part = pl.ds(pl.multiple_of(i * tile, tile), tile)
        project_body(
            own.at[part, :], got.at[part, :], code_ref.at[part, :], spots_ref, gain_ref, shift_ref, down_ref, w,
            adapt_ref, bias_ref, qkv.at[part, :], mid_ref.at[part, :], x.at[part, :],
        )

        at(i, {tiles - 3: ((1, 3), (1, 3)), tiles - 1: ((4, 5),)})

    early = [
        pltpu.make_async_copy(qkv, qkv_out, out_sems.at[0]),
        pltpu.make_async_copy(wo, wo_out, out_sems.at[1]),
    ]
    for copy in early:
        copy.start()

    @pl.loop(0, pairs)
    def _(p):
        column = lambda kind: pl.ds(pl.multiple_of((kind * pairs + p) * lanes, lanes), lanes)
        attend_body(
            qkv.at[:, column(0)], qkv.at[:, column(1)], qkv.at[:, column(2)], seg_ref, seg_row_ref,
            ctx.at[:, column(0)], log_ref.at[pl.ds(p, 1)],
        )

        at(
            p - (pairs - 6),
            {0: ((1, 0), (4, 11)), 1: ((6, 7),), 3: ((8, 9), (12, 19)), 4: ((10, 11),)},
        )

    for copy in loads[3:5]:
        copy.wait()

    def tile_copies(i):
        part = pl.ds(pl.multiple_of(i * tile, tile), tile)
        turn = i % 2
        return [
            pltpu.make_async_copy(source, target.at[part, :], tile_sems.at[k, i])
            for k, (source, target) in enumerate(
                (
                    (out.at[turn], x_out),
                    (two.at[turn], two_out),
                    (slope.at[turn], slope_out),
                    (x.at[part, :], one_out),
                )
            )
        ]

    plan = {0: ((12, 13), (20, 27)), 1: ((14, 17),), 2: ((18, 21),), 3: ((22, 27),)}

    @pl.loop(0, tiles)
    def _(i):
        part = pl.ds(pl.multiple_of(i * tile, tile), tile)
        turn = i % 2

        @pl.when(i >= 2)
        def _():
            for copy in tile_copies(i - 2):
                copy.wait()

        after_body(
            ctx.at[part, :], x.at[part, :], wo, up, dn, bias_ref, gain_ref, shift_ref, out.at[turn],
            x.at[part, :], two.at[turn], slope.at[turn],
        )
        for copy in tile_copies(i):
            copy.start()
        at(i - (tiles - 4), plan)

    for gather in gathers:
        gather.finish()
    for i in (tiles - 2, tiles - 1):
        for copy in tile_copies(i):
            copy.wait()
    for copy in early + loads[5:]:
        copy.wait()


def first_layer(own, got, first, chunk, more, shards):
    whole = pl.BlockSpec(memory_space=pltpu.VMEM)
    anywhere = pl.BlockSpec(memory_space=pl.ANY)
    down, seg_row = more[4], more[-1]
    rows, hidden = seg_row.shape[1], own.shape[1]
    tile = split_of(rows, 256, 16)
    pairs = HEADS // 2
    units = 4 * hidden
    each = units // shards
    shape = jax.ShapeDtypeStruct
    sems = pltpu.SemaphoreType.DMA
    streams = streams_of(chunk.shape[0], (("zxy", 0.4), ("zyx", 0.4), ("xyz", 0.2)))
    return pl.pallas_call(
        functools.partial(first_layer_body, streams, shards),
        in_specs=[anywhere] * 4 + [whole] * len(more),
        out_specs=[anywhere] * 7 + [whole] * 2,
        out_shape=[
            shape((rows, 3 * hidden), BF),
            shape((rows, hidden), F32),
            shape((rows, hidden), F32),
            shape((rows, hidden), F32),
            shape((rows, units), BF),
            shape((hidden, hidden), BF),
            shape((shards, *chunk.shape), BF),
            shape((rows, down.shape[2]), BF),
            shape((pairs, 1, 2 * rows), F32),
        ],
        scratch_shapes=[
            pltpu.VMEM((rows, hidden), BF),
            pltpu.VMEM((rows, hidden), BF),
            pltpu.VMEM((shards, 4 * hidden // shards, hidden), BF),
            pltpu.VMEM((3 * hidden, hidden), BF),
            pltpu.VMEM((hidden, hidden), BF),
            pltpu.VMEM((shards, each, hidden), BF),
            pltpu.VMEM((shards, each, hidden), BF),
            pltpu.VMEM((rows, hidden), F32),
            pltpu.VMEM((rows, 3 * hidden), BF),
            pltpu.VMEM((rows, hidden), BF),
            pltpu.VMEM((2, tile, hidden), F32),
            pltpu.VMEM((2, tile, hidden), F32),
            pltpu.VMEM((2, tile, units), BF),
            sems((6,)),
            sems((4, rows // tile)),
            sems((2,)),
            *gather_sems(streams),
        ],
        compiler_params=params(collective_id=3, has_side_effects=True),
        name="first_layer",
    )(own, got, first, chunk, *more)


def adam(weight, gradient, moment_one, moment_two, fade_one, fade_two):
    moment_one = beta_first * moment_one + (1.0 - beta_first) * gradient
    moment_two = beta_second * moment_two + (1.0 - beta_second) * gradient * gradient
    one_hat = moment_one / fade_one
    two_hat = moment_two / fade_two
    weight = weight - learn_rate * (one_hat / (jnp.sqrt(two_hat) + adam_eps) + decay_rate * weight)
    return (weight, moment_one, moment_two)


BACK_TILE = 256


def finish_body(
    shards, edge,
    dout_any, one_any, two_any, slope_any, wo_any, first_any, qkv_any, gain_ref, log_ref, seg_ref,
    seg_row_ref, mid_ref, parts, late_ref, facts,
    sums_ref, dense_ref, total_ref,
    dout, one, two, slope, wo, up, dn, qkv, dctx, dv, grad, core_got, chip_sum, dense_got, grad_got, note, notes,
    tile_sems, load_sems, core_sems, dense_sems, grad_sems, note_sems,
):
    rows, hidden = dout.shape
    tile = split_of(rows, BACK_TILE, 16)
    tiles = rows // tile
    me = number_of(position())

    def tile_loads(i):
        part = pl.ds(pl.multiple_of(i * tile, tile), tile)
        return [
            pltpu.make_async_copy(source.at[part, :], target.at[part, :], tile_sems.at[k, i])
            for k, (source, target) in enumerate(
                ((two_any, two), (dout_any, dout), (slope_any, slope), (one_any, one))
            )
        ]

    here = position()
    chips = shards // 2
    chip, core = me // 2, here["c"]
    to_core = pltpu.make_async_remote_copy(
        src_ref=parts.at[:, 1 - core],
        dst_ref=core_got,
        send_sem=core_sems.at[0],
        recv_sem=core_sems.at[1],
        device_id=device_of(dict(here, c=1 - core)),
        device_id_type=MESH,
    )

    def to_chip(k):
        peer = (chip + k) % chips
        return pltpu.make_async_remote_copy(
            src_ref=chip_sum.at[peer],
            dst_ref=dense_got.at[chip],
            send_sem=dense_sems.at[0],
            recv_sem=dense_sems.at[1],
            device_id=rank_device(2 * peer + core),
            device_id_type=MESH,
        )

    loads = [
        pltpu.make_async_copy(source, target, load_sems.at[k])
        for k, (source, target) in enumerate(
            (
                (first_any.at[:, pl.ds(up.shape[1], dn.shape[1]), :], dn),
                (first_any.at[:, pl.ds(0, up.shape[1]), :], up),
                (wo_any, wo),
                (qkv_any, qkv),
            )
        )
    ]
    for copy in tile_loads(0) + loads[:3]:
        copy.start()
    for i in range(1, tiles):
        for copy in tile_loads(i):
            copy.start()
    loads[3].start()
    greet_all(shards)
    for copy in loads[:3]:
        copy.wait()

    @pl.loop(0, tiles)
    def _(i):
        for copy in tile_loads(i):
            copy.wait()
        part = pl.ds(pl.multiple_of(i * tile, tile), tile)
        after_back_body(
            dout.at[part, :], one.at[part, :], two.at[part, :], slope.at[part, :], wo, up, dn, gain_ref,
            dctx.at[part, :],
        )

        @pl.when(i == 0)
        def _():
            await_all(shards)
            to_core.start()

        @pl.when(i == 1)
        def _():
            to_core.wait_recv()

            @pl.loop(0, chips)
            def _(k):
                chip_sum[k] = (parts[k, core].astype(F32) + core_got[k].astype(F32)).astype(BF)

            dense_got[chip] = chip_sum[chip]

            @pl.loop(1, chips)
            def _(k):
                to_chip(k).start()

    loads[3].wait()
    lanes = 2 * (hidden // HEADS)
    pairs = hidden // lanes

    @pl.loop(0, pairs)
    def _(p):
        column = lambda kind: pl.ds(pl.multiple_of((kind * pairs + p) * lanes, lanes), lanes)
        attend_back_body(
            qkv.at[:, column(0)], qkv.at[:, column(1)], qkv.at[:, column(2)], dctx.at[:, column(0)],
            log_ref.at[pl.ds(p, 1)], seg_ref, seg_row_ref, mid_ref, grad.at[column(0), :], dv, edge=edge,
        )

    grad[...] = grad[...] + late_ref[...]
    each = hidden // shards
    piece = lambda peer: grad.at[pl.ds(pl.multiple_of(peer * each, each), each), :]
    grad_got[me] = piece(me)[...]
    spread(piece, grad_got, grad_sems, me, shards)
    others = chip_sum.at[pl.ds(0, chips - 1)]
    every = pltpu.make_async_remote_copy(
        src_ref=others,
        dst_ref=dense_got.at[pl.ds(0, chips - 1)],
        send_sem=dense_sems.at[0],
        recv_sem=dense_sems.at[1],
        device_id=device_of(dict(here, c=1 - core)),
        device_id_type=MESH,
    )
    every.wait_recv()
    every.wait_send()
    to_core.wait_send()
    dense = jnp.zeros((each, hidden), F32)
    for k in range(chips):
        dense = dense + dense_got[k].astype(F32)[:each, :]
    dense_ref[...] = dense
    square = jnp.sum(dense * dense, keepdims=True)
    collect(grad_got, grad_sems, me, shards)
    total = grad_got[0]
    for k in range(1, shards):
        total = total + grad_got[k]
    total_ref[...] = total
    square = square + jnp.sum(total * total, keepdims=True)
    row = lax.broadcasted_iota(jnp.int32, note.shape, 0)
    note[...] = jnp.where(row == 0, facts[...], jnp.where(row == 1, square, 0.0))
    notes[me] = note[...]
    spread(lambda peer: note, notes, note_sems, me, shards)
    collect(notes, note_sems, me, shards)
    sums = notes[0]
    for k in range(1, shards):
        sums = sums + notes[k]
    sums_ref[...] = sums


def update_body(
    sums_ref, dense_ref, total_ref, facts, head_w, head_m, head_v, adapt_w, adapt_m, adapt_v,
    loss_out, norm_out, head_w_out, head_m_out, head_v_out, adapt_w_out, adapt_m_out, adapt_v_out,
):
    norm = jnp.sqrt(sums_ref[1:2, 0:1])
    loss_out[...] = sums_ref[0:1, 0:1]
    norm_out[...] = norm
    factor = jnp.minimum(1.0, clip_limit / (norm + 1e-06))
    fades = facts[1:2, 0:1], facts[2:3, 0:1]
    new = adam(head_w[...], dense_ref[...] * factor, head_m[...], head_v[...], *fades)
    head_w_out[...], head_m_out[...], head_v_out[...] = new
    grad = (total_ref[...] * factor).T
    layers, kinds, rank, unused = adapt_w.shape
    for layer in range(layers):
        for kind in range(kinds):
            at = (layer * kinds + kind) * rank
            new = adam(
                adapt_w[layer, kind], grad[at : at + rank], adapt_m[layer, kind], adapt_v[layer, kind], *fades
            )
            adapt_w_out[layer, kind], adapt_m_out[layer, kind], adapt_v_out[layer, kind] = new


def update(sums, dense, total, facts, heads, adapts):
    whole = pl.BlockSpec(memory_space=pltpu.VMEM)
    shape = jax.ShapeDtypeStruct
    return pl.pallas_call(
        update_body,
        in_specs=[whole] * 10,
        out_specs=[whole] * 8,
        out_shape=[shape((1, 1), F32)] * 2 + [shape(a.shape, F32) for a in (*heads, *adapts)],
        compiler_params=params(),
        name="update",
    )(sums, dense, total, facts, *heads, *adapts)


def finish(back, qkv, logs, seg_wide, seg_row, mid, parts, late, facts, edge, shards):
    dout, one, two, slope, wo, first, gains = back
    slab = pltpu.VMEM((shards, slope.shape[1] // shards, dout.shape[1]), BF)
    parts = parts.reshape(-1, 2, *parts.shape[1:])
    rows, hidden = dout.shape
    each = hidden // shards
    whole = pl.BlockSpec(memory_space=pltpu.VMEM)
    anywhere = pl.BlockSpec(memory_space=pl.ANY)
    shape = jax.ShapeDtypeStruct
    sems = pltpu.SemaphoreType.DMA
    tiles = rows // split_of(rows, BACK_TILE, 16)
    return pl.pallas_call(
        functools.partial(finish_body, shards, edge),
        in_specs=[anywhere] * 7 + [whole] * 8,
        out_specs=[whole] * 3,
        out_shape=[
            shape((8, 128), F32),
            shape((each, hidden), F32),
            shape((each, late.shape[1]), F32),
        ],
        scratch_shapes=[
            pltpu.VMEM((rows, hidden), F32),
            pltpu.VMEM((rows, hidden), F32),
            pltpu.VMEM((rows, hidden), F32),
            pltpu.VMEM(slope.shape, BF),
            pltpu.VMEM(wo.shape, BF),
            slab,
            slab,
            pltpu.VMEM(qkv.shape, BF),
            pltpu.VMEM((rows, hidden), BF),
            pltpu.VMEM((rows, 2 * (hidden // HEADS)), F32),
            pltpu.VMEM(late.shape, F32),
            pltpu.VMEM((shards // 2, *parts.shape[2:]), BF),
            pltpu.VMEM((shards // 2, *parts.shape[2:]), BF),
            pltpu.VMEM((shards // 2, *parts.shape[2:]), BF),
            pltpu.VMEM((shards, each, late.shape[1]), F32),
            pltpu.VMEM((8, 128), F32),
            pltpu.VMEM((shards, 8, 128), F32),
            sems((4, tiles)),
            sems((4,)),
            sems((2,)),
            sems((2,)),
            sems((2,)),
            sems((2,)),
        ],
        compiler_params=params(collective_id=2, has_side_effects=True),
        name="finish",
    )(dout, one, two, slope, wo, first, qkv, gains, logs, seg_wide, seg_row, mid, parts, late, facts)


LOG_ROWS = 16


def flip(z, k):
    return (z % 2 + k % 2) % 2 + 2 * ((z // 2 + k // 2) % 2)


def pack_log(log_row, rows):
    high = log_row.astype(BF).astype(F32)
    middle = (log_row - high).astype(BF).astype(F32)
    low = log_row - high - middle
    row = lax.broadcasted_iota(jnp.int32, (rows, log_row.shape[1]), 0)
    return jnp.where(
        row == 0, high, jnp.where(row == 1, middle, jnp.where(row == 2, low, 0.0))
    ).astype(BF)


def unpack(block, hidden):
    logs = block[hidden : hidden + LOG_ROWS, :].astype(F32)
    return block[:hidden, :].astype(F32), jnp.sum(logs, 0, keepdims=True)


def merged(one, two):
    top = jnp.maximum(one[1], two[1])
    first, second = jnp.exp(one[1] - top), jnp.exp(two[1] - top)
    total = first + second
    inverse = 1.0 / total
    return one[0] * (first * inverse) + two[0] * (second * inverse), top + jnp.log(total)


def store_packed(ref, pair, hidden):
    ref[:hidden, :] = pair[0].astype(BF)
    ref[hidden : hidden + LOG_ROWS, :] = pack_log(pair[1], LOG_ROWS)


def head_body(
    u_ref, bias_ref, table_any, et_any, mean_ref, log_ref,
    e_ref, et_ref, bias_wide, feats, packs, handed, sums,
    loads, far_send, far_get, hand_send, hand_get, part_send, part_get, sum_send, sum_get,
):
    here = position()
    x, y, c = here["x"], here["y"], here["c"]
    labels, hidden = u_ref.shape
    sibling = device_of(dict(here, c=1 - c))

    def chip_at(k):
        return (x + k % 2) % 2, (y + k // 2) % 2

    def device_at(k):
        there = chip_at(k)
        return device_of(dict(here, x=there[0], y=there[1]))

    def slot(k, core):
        there = chip_at(k)
        return (there[0] * 2 + there[1]) * 2 + core

    fills = [
        pltpu.make_async_copy(source, target, loads.at[k])
        for k, (source, target) in enumerate(
            ((vocab_rows(table_any, e_ref), e_ref), (et_any, et_ref))
        )
    ]
    for fill in fills:
        fill.start()
    barrier = pltpu.get_barrier_semaphore()
    for target in (sibling, *[device_at(k) for k in (1, 2, 3)]):
        pl.semaphore_signal(barrier, inc=1, device_id=target, device_id_type=MESH)
    feats[slot(0, c)] = u_ref[...]
    pl.semaphore_wait(barrier, 4)

    def move(place, device, send, get):
        return pltpu.make_async_remote_copy(
            src_ref=feats.at[place],
            dst_ref=feats.at[place],
            send_sem=send,
            recv_sem=get,
            device_id=device,
            device_id_type=MESH,
        )

    def far(k):
        return move(slot(0, c), device_at(k), far_send.at[k], far_get.at[k])

    def far_here(k):
        return move(slot(k, c), device_at(k), far_send.at[k], far_get.at[k])

    def hand(k, core):
        return move(slot(k, core), sibling, hand_send.at[k], hand_get.at[k])

    for k in (1, 2, 3):
        far(k).start()
    hand(0, c).start()

    @pl.loop(0, bias_ref.shape[0])
    def _(b):
        row = jnp.broadcast_to(bias_ref[pl.ds(b, 1), :], (128, 128))
        bias_wide[pl.ds(pl.multiple_of(b * 128, 128), 128), :] = row.T

    for k in (1, 2, 3):
        far_here(k).wait_recv()
        hand(k, c).start()
    for fill in fills:
        fill.wait()
    count = e_ref.shape[0]
    steps = 4

    def target_of(s):
        return (s + 1) % steps

    def hand_part(s):
        return pltpu.make_async_remote_copy(
            src_ref=packs.at[s, 1 - c],
            dst_ref=handed.at[s],
            send_sem=part_send.at[s],
            recv_sem=part_get.at[s],
            device_id=sibling,
            device_id_type=MESH,
        )

    def sum_part(s):
        return pltpu.make_async_remote_copy(
            src_ref=packs.at[s, c],
            dst_ref=sums.at[s],
            send_sem=sum_send.at[s],
            recv_sem=sum_get.at[s],
            device_id=device_at(target_of(s)),
            device_id_type=MESH,
        )

    def together(s):
        hand_part(s).wait_recv()
        return merged(unpack(packs[s, c], hidden), unpack(handed[s], hidden))

    def settle(s):
        store_packed(packs.at[s, c], together(s), hidden)
        sum_part(s).start()

    @pl.loop(0, steps)
    def _(s):
        k = target_of(s)
        hand(k, 1 - c).wait_recv()
        u = feats[pl.ds(slot(k, 0), 2)].reshape(2 * labels, hidden)
        top = total = mean = None

        def scored(start):
            part = slice(start, min(start + 1280, count))
            bias = bias_wide[part, :]
            return mm_nt(e_ref[part, :], u) + jnp.concatenate([bias, bias], 1)

        @pl.when(s > 0)
        def _():
            settle(s - 1)

        logits = scored(0)
        for start in range(0, count, 1280):
            part = slice(start, min(start + 1280, count))
            later = scored(start + 1280) if start + 1280 < count else None
            high = jnp.max(logits, 0, keepdims=True)
            new = high if top is None else jnp.maximum(top, high)
            grown = jnp.exp(logits - new)
            part_sums = jnp.sum(grown, 0, keepdims=True)
            product = mm(et_ref[:, part], grown.astype(BF))
            if top is None:
                total, mean = part_sums, product
            else:
                shrink = jnp.exp(top - new)
                total, mean = total * shrink + part_sums, mean * shrink + product
            top = new
            logits = later
        mean = mean * (1.0 / total)
        logs = top + jnp.log(total)
        for core in range(2):
            half = slice(core * labels, (core + 1) * labels)
            packs[s, core, :hidden, :] = mean[:, half].astype(BF)
            packs[s, core, hidden : hidden + LOG_ROWS, :] = pack_log(logs[:, half], LOG_ROWS)
        hand_part(s).start()

    total = together(steps - 1)
    for s in range(steps - 1):
        sum_part(s).wait_recv()
        total = merged(total, unpack(sums[s], hidden))
    mean_ref[...] = total[0]
    log_ref[...] = total[1]
    for k in (1, 2, 3):
        far(k).wait_send()
    for k in range(4):
        hand(k, c).wait_send()
    for s in range(steps):
        hand_part(s).wait_send()
    for s in range(steps - 1):
        sum_part(s).wait_send()


def head(u, bias, table, et):
    labels, hidden = u.shape
    whole = pl.BlockSpec(memory_space=pltpu.VMEM)
    anywhere = pl.BlockSpec(memory_space=pl.ANY)
    shape = jax.ShapeDtypeStruct
    sems = pltpu.SemaphoreType.DMA
    block = (hidden + LOG_ROWS, labels)
    count = et.shape[1]
    return pl.pallas_call(
        head_body,
        in_specs=[whole] * 2 + [anywhere] * 2,
        out_specs=[whole] * 2,
        out_shape=[shape((hidden, labels), F32), shape((1, labels), F32)],
        scratch_shapes=[
            pltpu.VMEM((count, hidden), BF),
            pltpu.VMEM((hidden, count), BF),
            pltpu.VMEM((count, 128), F32),
            pltpu.VMEM((8, labels, hidden), BF),
            pltpu.VMEM((4, 2, *block), BF),
            pltpu.VMEM((4, *block), BF),
            pltpu.VMEM((4, *block), BF),
            sems((2,)),
        ]
        + [sems((4,))] * 8,
        compiler_params=params(collective_id=4, has_side_effects=True),
        name="head",
    )(u, bias, table, et)


def seg_positions(segments):
    index = jnp.arange(segments.shape[-1], dtype=jnp.int32)
    fresh = jnp.concatenate([jnp.ones((1,), dtype=bool), segments[1:] != segments[:-1]], -1)
    starts = lax.cummax(jnp.where(fresh, index, jnp.zeros_like(index)), axis=0)
    return index - starts


def pad_rows(matrix, multiple):
    return jnp.pad(matrix, ((0, -matrix.shape[0] % multiple), (0, 0)))


def slab_of(gathered, start, rows):
    if rows % 16 == 0 and start % rows == 0:
        return (gathered, start // rows, rows)
    part = gathered[:, start : start + rows].reshape(1, -1, gathered.shape[2])
    return (part, 0, part.shape[1])


def per_device(
    input_token_index,
    sentence_numbers,
    label_positions,
    label_target_token,
    sequence_task_index,
    task_loss_weight,
    optimizer_step_count,
    embed,
    position_embedding,
    norm_gain_vector,
    norm_bias_vector,
    attention_in_weight,
    attention_out_weight,
    feedforward_up,
    feedforward_down,
    layer_bias_vector,
    head_dense_bias,
    vocabulary_bias,
    adapter_down_matrix,
    adapter_up_matrix,
    adapter_moment_first,
    adapter_moment_second,
    head_projection,
    head_moment_first,
    head_moment_second,
):
    shards = lax.axis_size("dp") * lax.axis_size("fsdp")
    dp_index = lax.axis_index("dp")
    fsdp_index = lax.axis_index("fsdp")
    layers, unused, rank, up_part = adapter_up_matrix.shape
    hidden = embed.shape[1]
    tokens = input_token_index.shape[1]
    labels = label_positions.shape[1]
    qkv_rows = attention_in_weight.shape[2]
    out_rows = attention_out_weight.shape[2]
    ff_rows = feedforward_up.shape[2]
    head_rows = head_projection.shape[0]

    grouped = (lax.axis_size("dp"), lax.axis_size("fsdp")) == (2, 16)
    feeds = [[feedforward_up[layer].T, feedforward_down[layer]] for layer in range(layers)]
    attends = [[attention_in_weight[layer].T, attention_out_weight[layer].T] for layer in range(layers)]
    first_chunk = jnp.concatenate(feeds[0] + attends[0], 0)
    last_chunk = pad_rows(
        jnp.concatenate([feeds[1][0], *attends[1], head_projection.astype(BF)], 0), 32
    )
    last_feed = feeds[1][1]

    table_rows = embed.shape[0]
    wanted = jnp.concatenate([input_token_index[0], label_target_token[0]])
    dp_count = lax.axis_size("dp")
    group_ids = lax.all_gather(wanted, "dp", axis=0, tiled=False) - dp_index * table_rows
    inside = (group_ids >= 0) & (group_ids < table_rows)
    group_ids = jnp.clip(group_ids, 0, table_rows - 1)
    mine = lax.dynamic_index_in_dim(inside, dp_index, 0, keepdims=False)

    task_range = jnp.arange(TASKS, dtype=jnp.int32)
    slice_rows = vocabulary_bias.shape[0]
    ups = adapter_up_matrix.reshape(-1)
    if grouped:
        pair_ids = jnp.concatenate(
            [
                lax.dynamic_index_in_dim(group_ids, (dp_index + shift) % 2, 0, keepdims=False)
                for shift in (1, 0)
            ]
        )
        fact = jnp.concatenate([vocabulary_bias, ups, sequence_task_index.astype(F32)])
        fact_rows = -(-fact.size // 1024) * 8
        got, own_rows, facts, first_full, own_turned = start_exchange(
            pair_ids,
            embed,
            jnp.pad(fact, (0, fact_rows * 128 - fact.size)).reshape(fact_rows, 128),
            first_chunk,
            shards,
        )
        facts, last_feed = lax.optimization_barrier((facts, last_feed))
        facts = facts.reshape(shards, -1)
        all_bias = facts[:, :slice_rows].reshape(-1)
        every_up = facts[:, slice_rows : slice_rows + ups.size]
        every_task = facts[:, slice_rows + ups.size].astype(jnp.int32)
    else:
        looked = jnp.where(
            inside.reshape(-1)[:, None], embed[group_ids.reshape(-1)], jnp.zeros((), BF)
        )
        own_rows = got = lax.psum_scatter(looked, "dp", scatter_dimension=0, tiled=True)
        all_bias = lax.all_gather(vocabulary_bias, BOTH, axis=0, tiled=True)
        every_up = lax.all_gather(ups, BOTH, axis=0, tiled=False)
        every_task = lax.all_gather(sequence_task_index, BOTH, axis=0, tiled=True)
    counts = labels * jnp.sum((every_task[:, None] == task_range[None, :]).astype(F32), 0)
    task_hot = (sequence_task_index[:, None] == task_range[None, :]).astype(F32)
    row_weight = jnp.sum(task_hot[0] * (task_loss_weight / jnp.maximum(counts, 1.0)))
    ups_full = (
        every_up.astype(BF)
        .reshape(shards, layers, 2, rank, up_part)
        .transpose(1, 2, 3, 0, 4)
        .reshape(layers, 2, rank, hidden)
    )
    blank = jnp.zeros((rank, hidden), BF)
    spare = lambda rows: jnp.zeros((rows, 3 * hidden), BF)
    adapters = jnp.stack(
        [
            jnp.concatenate(
                [
                    spare(2 * rank * layer),
                    jnp.concatenate([2 * ups_full[layer, 0], blank, blank], 1),
                    jnp.concatenate([blank, blank, 2 * ups_full[layer, 1]], 1),
                    spare(128 - 2 * rank * (layer + 1)),
                ],
                0,
            )
            for layer in range(layers)
        ]
    )
    downs = jnp.stack(
        [
            jnp.pad(
                jnp.concatenate([adapter_down_matrix[layer, 0], adapter_down_matrix[layer, 1]], 1),
                ((0, 0), (2 * rank * layer, 128 - 2 * rank * (layer + 1))),
            )
            for layer in range(layers)
        ]
    )
    segments = sentence_numbers[0]
    code = (jnp.pad(2 * seg_positions(segments), (0, labels)) + mine.astype(jnp.int32))[:, None]
    seg_real = segments.astype(F32)
    seg_wide = jnp.broadcast_to(seg_real[:, None], (tokens, 128))
    seg_row = seg_real[None, :]
    place_row = label_positions
    place_col = jnp.broadcast_to(label_positions.reshape(labels, 1), (labels, 128))

    target_bias = all_bias[label_target_token[0]]

    gains, shifts = norm_gain_vector, norm_bias_vector
    last_inputs = (place_col, place_row, seg_wide, downs, adapters, layer_bias_vector)
    in_start = ff_rows
    last_dn = lax.all_gather(last_feed, BOTH, axis=0, tiled=False)
    slabs_of = lambda up_full, dn_full: (slab_of(up_full, 0, ff_rows), slab_of(dn_full, 0, ff_rows))
    if grouped:
        more = (
            code, position_embedding, gains, shifts, downs, adapters, layer_bias_vector, seg_wide, seg_row,
        )
        qkv, x_last, one, two, slope, out_first, last_full, mid, logs = first_layer(
            own_rows, got, first_full, last_chunk, more, shards
        )
        slabs = [None, slabs_of(last_full, last_dn)]
        *saved, in_last, out_last, head_full = last_forward(
            x_last, *last_inputs, (last_full,), (in_start, in_start + qkv_rows + out_rows), *slabs[1], gains,
            shifts, head_dense_bias[None, :],
        )
        count = own_turned.shape[1]
        own_bias = lax.dynamic_slice_in_dim(
            all_bias, dp_index * table_rows + fsdp_index % 4 * count, count, 0
        ).reshape(-1, 128)
        mean_t, own_logs = head(saved[-1], own_bias, embed, own_turned)
    else:
        first_full = lax.all_gather(first_chunk, BOTH, axis=0, tiled=False)
        last_full = lax.all_gather(last_chunk, BOTH, axis=0, tiled=False)
        slabs = [
            (slab_of(first_full, 0, ff_rows), slab_of(first_full, ff_rows, ff_rows)),
            slabs_of(last_full, last_dn),
        ]
        taken = lambda full_chunk, start, size: full_chunk[:, start : start + size].reshape(-1, hidden)
        in_first = taken(first_full, 2 * ff_rows, qkv_rows)
        out_first = taken(first_full, 2 * ff_rows + qkv_rows, out_rows)
        in_last = taken(last_full, in_start, qkv_rows)
        out_last = taken(last_full, in_start + qkv_rows, out_rows)
        head_full = taken(last_full, in_start + qkv_rows + out_rows, head_rows)
        qkv, mid, hidden_rows = project(
            own_rows, got, code, position_embedding, gains, shifts, downs, in_first, adapters, layer_bias_vector, tokens
        )
        context, logs = attend(qkv, seg_wide, seg_row)
        x_last, one, two, slope = after(
            context, hidden_rows, out_first, *slabs[0], layer_bias_vector, gains, shifts
        )
        saved = last_forward(
            x_last, *last_inputs, (in_last, out_last, head_full), None, *slabs[1], gains, shifts,
            head_dense_bias[None, :],
        )
        features = saved[-1]
        own_slice = lax.dynamic_slice_in_dim(embed, fsdp_index * slice_rows, slice_rows, 0)
        own_vocab = jnp.concatenate(
            [own_slice]
            + [
                lax.ppermute(
                    own_slice, "dp", [(k, (k + shift) % dp_count) for k in range(dp_count)]
                )
                for shift in range(1, dp_count)
            ],
            0,
        )
        own_bias = jnp.concatenate(
            [
                lax.dynamic_slice_in_dim(
                    all_bias,
                    ((dp_index - shift) % dp_count) * table_rows + fsdp_index * slice_rows,
                    slice_rows,
                    0,
                )
                for shift in range(dp_count)
            ]
        )
        bias_wide = jnp.broadcast_to(own_bias[:, None], (own_bias.shape[0], 128))
        every = lax.all_gather(features, "fsdp", axis=0, tiled=True)
        means, local_logs = vocab(every, own_vocab, own_vocab.T, bias_wide, labels)
        local_logs = local_logs.reshape(-1, labels)
        all_logs = lax.all_gather(local_logs, "fsdp", axis=0, tiled=False)
        whole_logs = jax.nn.logsumexp(all_logs, axis=0)
        scaled = (means * jnp.exp(local_logs - whole_logs)[:, None, :]).astype(BF)
        mean_t = lax.psum_scatter(scaled, "fsdp", scatter_dimension=0, tiled=True)[0].astype(F32)
        own_logs = lax.dynamic_index_in_dim(whole_logs, fsdp_index, 0, keepdims=False)
        own_logs = own_logs[None, :]

    step_as_real = optimizer_step_count[0].astype(F32)
    fades = (1.0 - beta_first**step_as_real, 1.0 - beta_second**step_as_real)
    lanes = lambda value: jnp.pad(
        jnp.broadcast_to(value, (1, value.size if value.ndim else 128)), ((0, 0), (0, 128))
    )[:, :128]
    facts = jnp.concatenate(
        [lanes(value) for value in (row_weight, *fades, target_bias)] + [jnp.zeros((4, 128), F32)]
    )
    hidden_grad, dense_gradient, late, facts = last_backward(
        mean_t, own_logs, own_rows, got, code, facts, saved, place_col, place_row, seg_wide, downs, in_last, adapters,
        out_last, *slabs[1], gains, head_full, 3 * rank, shards if grouped else None,
    )
    back = (hidden_grad, one, two, slope, out_first)
    adapts = (adapter_up_matrix, adapter_moment_first, adapter_moment_second)
    heads = (head_projection, head_moment_first, head_moment_second)
    if grouped:
        sums, dense_portion, adapter_portion = finish(
            (*back, first_full, gains), qkv, logs, seg_wide, seg_row, mid, dense_gradient, late, facts, rank, shards
        )
        loss, norm, *new = update(sums, dense_portion, adapter_portion, facts, heads, adapts)
        return (loss[0, 0], norm[0, 0], *new[3:], *new[:3])
    dctx = after_back(*back, *slabs[0], gains)
    first = attend_back(qkv, dctx, logs, seg_wide, seg_row, mid, rank)
    adapter_gradient = (first + late)[:, : 2 * rank * layers].T.reshape(layers, 2, rank, hidden)
    dense_portion = lax.psum_scatter(dense_gradient, BOTH, scatter_dimension=0, tiled=True)
    adapter_portion = lax.psum_scatter(adapter_gradient, BOTH, scatter_dimension=3, tiled=True)
    squared_entries = jnp.sum(adapter_portion * adapter_portion) + jnp.sum(dense_portion * dense_portion)
    masked_task_loss, norm_square = lax.psum((facts[0, 0], squared_entries), BOTH)
    gradient_norm = jnp.sqrt(norm_square)
    factor = jnp.minimum(1.0, clip_limit / (gradient_norm + 1e-06))
    adapter_new = adam(adapts[0], adapter_portion * factor, *adapts[1:], *fades)
    dense_new = adam(heads[0], dense_portion * factor, *heads[1:], *fades)
    return (masked_task_loss, gradient_norm, *adapter_new, *dense_new)


def solution(mesh):
    rows = P(BOTH, None)
    in_specs = (
        rows,
        rows,
        rows,
        rows,
        P(BOTH),
        P(),
        P(),
        P("dp", None),
        P(),
        P(),
        P(),
        P(None, None, BOTH),
        P(None, None, BOTH),
        P(None, None, BOTH),
        P(None, BOTH, None),
        P(),
        P(),
        P(BOTH),
        P(),
        P(None, None, None, BOTH),
        P(None, None, None, BOTH),
        P(None, None, None, BOTH),
        rows,
        rows,
        rows,
    )
    adapter = P(None, None, None, BOTH)
    out_specs = (P(), P(), adapter, adapter, adapter, rows, rows, rows)
    return jax.shard_map(
        per_device, mesh=mesh, in_specs=in_specs, out_specs=out_specs, check_vma=False
    )
```

```python
import functools

import jax
import jax.numpy as jnp
from jax import lax
from jax.experimental import pallas as pl
from jax.experimental.pallas import tpu as pltpu
from jax.sharding import PartitionSpec as P

HEADS = 12
TASKS = 4
REACH = 128

norm_eps = 1e-05
adapter_scale = 2.0
clip_limit = 0.01
learn_rate = 0.05
beta_first = 0.9
beta_second = 0.999
adam_eps = 1e-08
decay_rate = 0.01
masked_score = -1e30

BF = jnp.bfloat16
F32 = jnp.float32
BOTH = ("dp", "fsdp")
VMEM_BYTES = 60 * 1024 * 1024


def mm(a, b):
    return lax.dot_general(a, b, (((1,), (0,)), ((), ())), preferred_element_type=F32)


def mm_nt(a, b):
    return lax.dot_general(a, b, (((1,), (1,)), ((), ())), preferred_element_type=F32)


def mm_tn(a, b):
    return lax.dot_general(a, b, (((0,), (0,)), ((), ())), preferred_element_type=F32)


def layer_norm(rows_in, gain, shift):
    center = rows_in - jnp.mean(rows_in, -1, keepdims=True)
    spread = jnp.mean(center * center, -1, keepdims=True)
    return center * lax.rsqrt(spread + norm_eps) * gain + shift


def norm_back(rows_in, gain, gradient):
    center = rows_in - jnp.mean(rows_in, -1, keepdims=True)
    inverse = lax.rsqrt(jnp.mean(center * center, -1, keepdims=True) + norm_eps)
    unit = center * inverse
    scaled = gradient * gain
    return inverse * (
        scaled
        - jnp.mean(scaled, -1, keepdims=True)
        - unit * jnp.mean(scaled * unit, -1, keepdims=True)
    )


def gelu_pair(v):
    size = jnp.abs(v) * 0.7071067811865476
    base = 1.0 + 0.3275911 * size
    t = pl.reciprocal(base, approx=True)
    t = t * (2.0 - base * t)
    bell = jnp.exp(-0.5 * v * v)
    poly = t * (
        0.127414796 + t * (-0.142248368 + t * (0.7107068705 + t * (-0.7265760135 + t * 0.5307027145)))
    )
    tail = poly * bell
    phi = jnp.where(v >= 0.0, 1.0 - tail, tail)
    return v * phi, phi + v * (bell * 0.3989422804014327)


def params(**more):
    return pltpu.CompilerParams(vmem_limit_bytes=VMEM_BYTES, **more)


def full(shape):
    return pl.BlockSpec(shape, lambda *_: (0,) * len(shape))


def split_of(total, most, step):
    size = (min(most, total) // step) * step
    while size > step and total % size:
        size -= step
    return size if size and total % size == 0 else total


def pair_rows(block, width):
    first = lax.broadcasted_iota(jnp.int32, block.shape, 1) < width
    return jnp.concatenate([jnp.where(first, block, 0.0), jnp.where(first, 0.0, block)], 0).astype(BF)


def pair_join(wide, width):
    rows = wide.shape[1] // 2
    return jnp.concatenate([wide[:width, :rows], wide[width:, rows:]], 0)


def masked(scores, same):
    rows = scores.shape[1] // 2
    return jnp.concatenate(
        [
            jnp.where(same, scores[:, :rows], masked_score),
            jnp.where(same, scores[:, rows:], masked_score),
        ],
        1,
    )


def qkv_bias(bias_ref, layer, start, size):
    hidden = bias_ref.shape[1] // 8
    if start >= 2 * hidden:
        return bias_ref[layer : layer + 1, start - hidden : start - hidden + size]
    return bias_ref[layer : layer + 1, start : start + size] if start < hidden else 0.0


def norm_of(norm_refs, k):
    return norm_refs[0][k : k + 1, :], norm_refs[1][k : k + 1, :]


def project_body(
    own_ref, got_ref, code_ref, spots_ref, gain_ref, shift_ref, down_ref, w_ref, up_ref, bias_ref,
    out_ref, mid_ref, x_ref,
):
    mine = code_ref[...] % 2
    choose = (
        lax.broadcasted_iota(jnp.int32, (own_ref.shape[0], spots_ref.shape[0]), 1) == code_ref[...] // 2
    )
    summed = jnp.where(
        mine > 0, own_ref[...].astype(F32), got_ref[...].astype(F32)
    ) + mm(choose.astype(F32).astype(BF), spots_ref[...])
    x = layer_norm(summed, *norm_of((gain_ref, shift_ref), 0))
    x_ref[...] = x
    low = x.astype(BF)
    mid = mm(low, down_ref[0]).astype(BF)
    mid_ref[...] = mid
    total = w_ref.shape[0]
    step = total // 3
    for start in range(0, total, step):
        part = slice(start, start + step)
        out_ref[:, part] = (
            mm_nt(low, w_ref[part, :]) + mm(mid, up_ref[0, :, part]) + qkv_bias(bias_ref, 0, start, step)
        ).astype(BF)


def project(own, got, code, spots, gains, shifts, down, w, up, bias, rows):
    width = own.shape[1]
    tile = split_of(rows, 256, 16)
    total = w.shape[0]
    row = lambda n: pl.BlockSpec((tile, n), lambda i: (i, 0))
    return pl.pallas_call(
        project_body,
        grid=(rows // tile,),
        in_specs=[row(width), row(width), row(1)]
        + [full(a.shape) for a in (spots, gains, shifts, down, w, up, bias)],
        out_specs=[row(total), row(down.shape[2]), row(width)],
        out_shape=[
            jax.ShapeDtypeStruct((rows, total), BF),
            jax.ShapeDtypeStruct((rows, down.shape[2]), BF),
            jax.ShapeDtypeStruct((rows, width), F32),
        ],
        compiler_params=params(),
        name="project",
    )(own, got, code, spots, gains, shifts, down, w, up, bias)


def attend_body(q_ref, k_ref, v_ref, seg_ref, seg_row_ref, ctx_ref, log_ref):
    rows = q_ref.shape[0]
    width = q_ref.shape[1] // 2
    scale = width**-0.5
    turned = turn_blocks(v_ref)

    def scored(start):
        own, near = reach_of(start, rows)
        return mm_nt(k_ref[near, :], pair_rows(q_ref[own, :].astype(F32) * scale, width))

    scores = scored(0)
    for start in range(0, rows, REACH):
        own, near = reach_of(start, rows)
        later = scored(start + REACH) if start + REACH < rows else None
        same = seg_ref[near, :] == seg_row_ref[:, own]
        scores = masked(scores, same)
        top = jnp.max(scores, 0, keepdims=True)
        weights = jnp.exp(scores - top)
        total = jnp.sum(weights, 0, keepdims=True)
        context = mm(turned[:, near], weights.astype(BF)) * (1.0 / total)
        ctx_ref[own, :] = pair_join(context, width).T.astype(BF)
        log_ref[0, :, 2 * start : 2 * start + 2 * REACH] = top + jnp.log(total)
        scores = later


def reach_of(start, rows):
    return slice(start, start + REACH), slice(max(0, start - REACH), min(rows, start + 2 * REACH))


def turn_blocks(ref):
    blocks = [ref[k : k + 128, :].astype(F32).T.astype(BF) for k in range(0, ref.shape[0], 128)]
    return jnp.concatenate(blocks, 1)


def attend(qkv, seg_wide, seg_row):
    rows, total = qkv.shape
    hidden = total // 3
    lanes = 2 * (hidden // HEADS)
    pairs = hidden // lanes
    column = lambda kind: pl.BlockSpec((rows, lanes), lambda p: (0, kind * pairs + p))
    return pl.pallas_call(
        attend_body,
        grid=(pairs,),
        in_specs=[column(0), column(1), column(2), full(seg_wide.shape), full(seg_row.shape)],
        out_specs=[
            pl.BlockSpec((rows, lanes), lambda p: (0, p)),
            pl.BlockSpec((1, 1, 2 * rows), lambda p: (p, 0, 0)),
        ],
        out_shape=[
            jax.ShapeDtypeStruct((rows, hidden), BF),
            jax.ShapeDtypeStruct((pairs, 1, 2 * rows), F32),
        ],
        compiler_params=params(),
        name="attend",
    )(qkv, qkv, qkv, seg_wide, seg_row)


def flat(ref):
    whole = ref[...]
    return whole.reshape(-1, whole.shape[-1])


def rows_of(ref, start, size):
    each = ref.shape[1]
    if size % each == 0 and start % each == 0 and each % 16 == 0:
        part = ref[start // each : (start + size) // each, :, :]
        return part.reshape(size, part.shape[-1])
    return flat(ref)[start : start + size, :]


def feed_step(ref):
    units = ref.shape[0] * ref.shape[1]
    step = ref.shape[1]
    while units % (2 * step) == 0 and 2 * step <= 768 and ref.shape[0] > 1:
        step *= 2
    return units, (step if ref.shape[0] > 1 else split_of(units, 768, 128))


def later_biases(bias_ref, layer):
    hidden = bias_ref.shape[1] // 8
    row = bias_ref[layer : layer + 1, :]
    return row[:, 2 * hidden : 3 * hidden], row[:, 3 * hidden : 7 * hidden], row[:, 7 * hidden :]


def after_body(
    ctx_ref, x_ref, wo_ref, up_ref, down_ref, bias_ref, gain_ref, shift_ref,
    out_ref, one_ref, two_ref, slope_ref,
):
    bo, b1, b2 = later_biases(bias_ref, 0)
    one = x_ref[...] + (mm_nt(ctx_ref[...], wo_ref[...]) + bo)
    one_ref[...] = one
    middle = layer_norm(one, *norm_of((gain_ref, shift_ref), 1))
    low = middle.astype(BF)
    total = middle + b2
    units, step = feed_step(up_ref)
    gate = mm_nt(low, rows_of(up_ref, 0, step))
    for start in range(0, units, step):
        part = slice(start, start + step)
        later = mm_nt(low, rows_of(up_ref, start + step, step)) if start + step < units else None
        act, slope = gelu_pair(gate + b1[:, part])
        slope_ref[:, part] = slope.astype(BF)
        total = total + mm(act.astype(BF), rows_of(down_ref, start, step))
        gate = later
    two_ref[...] = total
    out_ref[...] = layer_norm(total, *norm_of((gain_ref, shift_ref), 2))


def slab_spec(slab):
    array, place, rows = slab
    return pl.BlockSpec((array.shape[0], rows, array.shape[2]), lambda *_: (0, place, 0))


def after(ctx, x, wo, up, down, bias, gains, shifts):
    rows, width = x.shape
    tile = split_of(rows, 256, 16)
    units = 4 * width
    row = lambda n: pl.BlockSpec((tile, n), lambda i: (i, 0))
    return pl.pallas_call(
        after_body,
        grid=(rows // tile,),
        in_specs=[row(width), row(width), full(wo.shape), slab_spec(up), slab_spec(down)]
        + [full(a.shape) for a in (bias, gains, shifts)],
        out_specs=[row(width), row(width), row(width), row(units)],
        out_shape=[jax.ShapeDtypeStruct((rows, width), F32)] * 3
        + [jax.ShapeDtypeStruct((rows, units), BF)],
        compiler_params=params(),
        name="after",
    )(ctx, x, wo, up[0], down[0], bias, gains, shifts)


def exact_rows(choose, matrix):
    high = matrix.astype(BF)
    rest = matrix - high.astype(F32)
    middle = rest.astype(BF)
    low = (rest - middle.astype(F32)).astype(BF)
    return mm(choose, high) + mm(choose, middle) + mm(choose, low)


def unpack_rows(slab_ref, targets):
    shards = slab_ref.shape[0]

    @pl.loop(0, shards // 2)
    def _(k):
        first, second = slab_ref[2 * k].astype(F32), slab_ref[2 * k + 1].astype(F32)
        at = 0
        for target in targets:
            each = target.shape[0] // shards
            both = jnp.concatenate([first[at : at + each], second[at : at + each]], 0)
            target[pl.ds(pl.multiple_of(2 * each * k, 2 * each), 2 * each), :] = both.astype(BF)
            at += each


def last_forward_body(
    x_ref, place_ref, place_row_ref, seg_ref, down_ref, adapt_ref, bias_ref, weights_any, up_any, dn_any,
    gain_ref, shift_ref, hbias_ref,
    kv_ref, q_ref, mid_ref, log_ref, one_ref, slope_ref, two_ref, low_ref, act_ref, hslope_ref, feat_ref, *more,
    places, starts,
):
    copies = []
    if starts is None:
        up_ref, dn_ref, ctx_ref, w_ref, wo_ref, hb_ref, sems = more
        sources = zip(weights_any, (w_ref, wo_ref, hb_ref))
    else:
        w_out, wo_out, hb_out, up_ref, dn_ref, ctx_ref, w_ref, wo_ref, hb_ref, in_slab, hb_slab, sems = more
        sources = [
            (weights_any[0].at[:, pl.ds(start, slab.shape[1]), :], slab)
            for start, slab in zip(starts, (in_slab, hb_slab))
        ]
    for source, target in sources:
        copies.append((source, target))
    early = len(copies)
    for source, target, place in ((up_any, up_ref, places[0]), (dn_any, dn_ref, places[1])):
        each = target.shape[1]
        copies.append((source.at[:, pl.ds(place * each, each), :], target))
    copies = [pltpu.make_async_copy(*ends, sems.at[k]) for k, ends in enumerate(copies)]
    for copy in copies:
        copy.start()
    for copy in copies[:early]:
        copy.wait()
    copies = copies[early:]
    if starts is not None:
        unpack_rows(in_slab, (w_ref, wo_ref))
        unpack_rows(hb_slab, (hb_ref,))
        for k, ends in enumerate(((w_ref, w_out), (wo_ref, wo_out), (hb_ref, hb_out))):
            copies.append(pltpu.make_async_copy(*ends, sems.at[4 + k]))
            copies[-1].start()
    rows, hidden = x_ref.shape
    labels = place_ref.shape[0]
    lanes = 2 * (hidden // HEADS)
    width = lanes // 2
    low = x_ref[...].astype(BF)
    mid = mm(low, down_ref[1]).astype(BF)
    mid_ref[...] = mid
    step = split_of(hidden, 768, 128)
    for start in range(hidden, 3 * hidden, step):
        part = slice(start, start + step)
        kv_ref[:, start - hidden : start - hidden + step] = (
            mm_nt(low, w_ref[part, :]) + mm(mid, adapt_ref[1, :, part]) + qkv_bias(bias_ref, 1, start, step)
        ).astype(BF)
    choose = (
        lax.broadcasted_iota(jnp.int32, (labels, rows), 1) == place_ref[...][:, 0:1]
    ).astype(F32).astype(BF)
    own = exact_rows(choose, x_ref[...])
    own_low = own.astype(BF)
    own_mid = mm(choose, mid).astype(BF)
    q_ref[...] = (
        mm_nt(own_low, w_ref[:hidden, :])
        + mm(own_mid, adapt_ref[1, :, :hidden])
        + qkv_bias(bias_ref, 1, 0, hidden)
    ).astype(BF)
    seg = seg_ref[...]
    seg_own = jnp.sum(
        jnp.where(
            lax.broadcasted_iota(jnp.int32, (rows, labels), 0) == place_row_ref[...], seg, 0.0
        ),
        0,
        keepdims=True,
    )
    same = seg == seg_own

    def scored(p):
        part = slice(p * lanes, (p + 1) * lanes)
        return mm_nt(kv_ref[:, part], pair_rows(q_ref[:, part].astype(F32) * width**-0.5, width))

    later = scored(0)
    for p in range(hidden // lanes):
        part = slice(p * lanes, (p + 1) * lanes)
        scores = masked(later, same)
        later = scored(p + 1) if (p + 1) * lanes < hidden else None
        top = jnp.max(scores, 0, keepdims=True)
        weights = jnp.exp(scores - top)
        total = jnp.sum(weights, 0, keepdims=True)
        context = mm_tn(
            kv_ref[:, hidden + p * lanes : hidden + (p + 1) * lanes], weights.astype(BF)
        ) * (1.0 / total)
        ctx_ref[:, part] = pair_join(context, width).T.astype(BF)
        log_ref[p : p + 1, :] = top + jnp.log(total)
    bo, b1, b2 = later_biases(bias_ref, 1)
    norms = (gain_ref, shift_ref)
    one = own + (mm_nt(ctx_ref[...], wo_ref[...]) + bo)
    one_ref[...] = one
    middle = layer_norm(one, *norm_of(norms, 3))
    middle_low = middle.astype(BF)
    sum_two = middle + b2
    units, step = feed_step(up_ref)
    for copy in copies:
        copy.wait()
    gate = mm_nt(middle_low, rows_of(up_ref, 0, step))
    for start in range(0, units, step):
        part = slice(start, start + step)
        later = mm_nt(middle_low, rows_of(up_ref, start + step, step)) if start + step < units else None
        act, slope = gelu_pair(gate + b1[:, part])
        gate = later
        slope_ref[:, part] = slope.astype(BF)
        sum_two = sum_two + mm(act.astype(BF), rows_of(dn_ref, start, step))
    two_ref[...] = sum_two
    out_low = layer_norm(sum_two, *norm_of(norms, 4)).astype(BF)
    low_ref[...] = out_low
    act, slope = gelu_pair(mm(out_low, hb_ref[...]) + hbias_ref[...])
    act_ref[...] = act
    hslope_ref[...] = slope
    feat_ref[...] = layer_norm(act, *norm_of(norms, 5)).astype(BF)


def slab_scratch(slab):
    array, place, rows = slab
    return pltpu.VMEM((array.shape[0], rows, array.shape[2]), BF)


def last_forward(
    x, place_col, place_row, seg_wide, down, adapt, bias, weights, starts, up, dn, gains, shifts, hbias
):
    rows, hidden = x.shape
    labels = place_col.shape[0]
    units = 4 * hidden
    whole = pl.BlockSpec(memory_space=pltpu.VMEM)
    anywhere = pl.BlockSpec(memory_space=pl.ANY)
    shape = jax.ShapeDtypeStruct
    pairs = HEADS // 2
    matrices = [(3 * hidden, hidden), (hidden, hidden), (hidden, hidden)]
    slabs = []
    if starts is not None:
        shards = weights[0].shape[0]
        slabs = [
            pltpu.VMEM((shards, 4 * hidden // shards, hidden), BF),
            pltpu.VMEM((shards, weights[0].shape[1] - starts[1], hidden), BF),
        ]

    def body(*refs):
        head, rest = refs[:7], refs[7:]
        return last_forward_body(
            *head, rest[: len(weights)], *rest[len(weights) :], places=(up[1], dn[1]), starts=starts
        )

    return pl.pallas_call(
        body,
        in_specs=[whole] * 7 + [anywhere] * (len(weights) + 2) + [whole] * 3,
        out_specs=[whole] * 11 + ([anywhere] * 3 if slabs else []),
        out_shape=[
            shape((rows, 2 * hidden), BF),
            shape((labels, hidden), BF),
            shape((rows, down.shape[2]), BF),
            shape((pairs, 2 * labels), F32),
            shape((labels, hidden), F32),
            shape((labels, units), BF),
            shape((labels, hidden), F32),
            shape((labels, hidden), BF),
            shape((labels, hidden), F32),
            shape((labels, hidden), F32),
            shape((labels, hidden), BF),
        ]
        + ([shape(m, BF) for m in matrices] if slabs else []),
        scratch_shapes=[
            slab_scratch(up),
            slab_scratch(dn),
            pltpu.VMEM((labels, hidden), BF),
            *[pltpu.VMEM(m, BF) for m in matrices],
            *slabs,
            pltpu.SemaphoreType.DMA((7,)),
        ],
        compiler_params=params(),
        name="last_forward",
    )(x, place_col, place_row, seg_wide, down, adapt, bias, *weights, up[0], dn[0], gains, shifts, hbias)


def vocab_body(u_ref, e_ref, et_ref, bias_ref, num_ref, log_ref, scores, weights):
    count = e_ref.shape[0]
    step = split_of(count, 640, 16)
    u = u_ref[...]
    rows = u.shape[0]
    labels = num_ref.shape[2]
    top = jnp.full((1, rows), -jnp.inf, F32)
    for start in range(0, count, step):
        part = slice(start, start + step)
        bias = bias_ref[part, :]
        logits = mm_nt(e_ref[part, :], u) + jnp.concatenate([bias] * (rows // bias.shape[1]), 1)
        scores[part, :] = logits
        top = jnp.maximum(top, jnp.max(logits, 0, keepdims=True))
    total = jnp.zeros((1, rows), F32)
    for start in range(0, count, step):
        part = slice(start, start + step)
        grown = jnp.exp(scores[part, :] - top)
        total = total + jnp.sum(grown, 0, keepdims=True)
        weights[part, :] = grown.astype(BF)
    mean = mm(et_ref[...], weights[...]) * (1.0 / total)
    logs = top + jnp.log(total)
    for k in range(rows // labels):
        num_ref[k, :, :] = mean[:, k * labels : (k + 1) * labels]
        log_ref[k, :, :] = logs[:, k * labels : (k + 1) * labels]


def vocab(u, e, et, bias_wide, labels):
    rows, hidden = u.shape
    count = e.shape[0]
    tile = 2 * labels
    return pl.pallas_call(
        vocab_body,
        grid=(rows // tile,),
        in_specs=[
            pl.BlockSpec((tile, hidden), lambda i: (i, 0)),
            full(e.shape),
            full(et.shape),
            full(bias_wide.shape),
        ],
        out_specs=[
            pl.BlockSpec((2, hidden, labels), lambda i: (i, 0, 0)),
            pl.BlockSpec((2, 1, labels), lambda i: (i, 0, 0)),
        ],
        out_shape=[
            jax.ShapeDtypeStruct((rows // labels, hidden, labels), F32),
            jax.ShapeDtypeStruct((rows // labels, 1, labels), F32),
        ],
        scratch_shapes=[pltpu.VMEM((count, tile), F32), pltpu.VMEM((count, tile), BF)],
        compiler_params=params(),
        name="vocab",
    )(u, e, et, bias_wide)


def last_backward_body(
    own_any, got_any, mean_ref, all_log_ref, code_ref, fact_ref, kv_ref, q_ref, mid_ref, log_ref, one_ref, slope_ref, two_ref,
    low_ref, act_ref, hslope_ref, feat_ref, place_ref, place_row_ref, seg_ref, down_ref, w_ref, adapt_ref, wo_ref,
    up_any, dn_any, gain_ref, hb_ref,
    dx_ref, gh_ref, g_ref, out_fact_ref,
    up_ref, dn_ref, dkv_ref, dq_ref, aims, sems, *, places, edge,
):
    labels = place_ref.shape[0]
    tail = pl.ds(kv_ref.shape[0], labels)
    aimed = [
        pltpu.make_async_copy(source.at[tail, :], aims.at[k], sems.at[2 + k])
        for k, source in enumerate((own_any, got_any))
    ]
    for copy in aimed:
        copy.start()
    copies = []
    for k, (source, target, place) in enumerate(
        ((up_any, up_ref, places[0]), (dn_any, dn_ref, places[1]))
    ):
        rows = target.shape[1]
        copies.append(
            pltpu.make_async_copy(
                source.at[:, pl.ds(place * rows, rows), :], target, sems.at[k]
            )
        )
        copies[-1].start()
    rows = kv_ref.shape[0]
    labels, hidden = feat_ref.shape
    lanes = 2 * (hidden // HEADS)
    width = lanes // 2
    scale = width**-0.5
    for copy in aimed:
        copy.wait()
    mine = code_ref[kv_ref.shape[0] :, :] % 2
    targets = jnp.where(mine > 0, aims[0].astype(F32), aims[1].astype(F32))
    weight = fact_ref[0:1, 0:1]
    chosen = jnp.sum(feat_ref[...].astype(F32) * targets, keepdims=True)
    loss = weight * (jnp.sum(all_log_ref[...] - fact_ref[3:4, :labels], keepdims=True) - chosen)
    out_fact_ref[...] = jnp.where(
        lax.broadcasted_iota(jnp.int32, fact_ref.shape, 0) == 0, loss, fact_ref[...]
    )
    du = weight * (mean_ref[...].T - targets)
    dact = norm_back(act_ref[...], gain_ref[5:6, :], du)
    dz = (hslope_ref[...] * dact).astype(BF)
    dense = mm_tn(low_ref[...], dz)
    if len(gh_ref.shape) == 2:
        gh_ref[...] = dense
    else:
        each = hidden // gh_ref.shape[0]
        spare = jnp.zeros((gh_ref.shape[1] - each, hidden), F32)
        for k in range(gh_ref.shape[0]):
            gh_ref[k] = jnp.concatenate([dense[k * each : (k + 1) * each, :], spare], 0).astype(BF)
    dtwo = norm_back(two_ref[...], gain_ref[4:5, :], mm_nt(dz, hb_ref[...]))
    dtwo_low = dtwo.astype(BF)
    dmiddle = dtwo
    units, step = feed_step(up_ref)
    for copy in copies:
        copy.wait()
    dact = mm_nt(dtwo_low, rows_of(dn_ref, 0, step))
    for start in range(0, units, step):
        part = slice(start, start + step)
        later = mm_nt(dtwo_low, rows_of(dn_ref, start + step, step)) if start + step < units else None
        dgate = (slope_ref[:, part].astype(F32) * dact).astype(BF)
        dmiddle = dmiddle + mm(dgate, rows_of(up_ref, start, step))
        dact = later
    done = norm_back(one_ref[...], gain_ref[3:4, :], dmiddle)
    dctx = mm(done.astype(BF), wo_ref[...]).astype(BF)
    seg = seg_ref[...]
    choose_t = lax.broadcasted_iota(jnp.int32, (rows, labels), 0) == place_row_ref[...]
    same = seg == jnp.sum(jnp.where(choose_t, seg, 0.0), 0, keepdims=True)

    def products(p):
        part = slice(p * lanes, (p + 1) * lanes)
        later = slice(hidden + p * lanes, hidden + (p + 1) * lanes)
        queries = pair_rows(q_ref[:, part].astype(F32) * scale, width)
        outs = pair_rows(dctx[:, part].astype(F32), width)
        return queries, outs, mm_nt(kv_ref[:, part], queries), mm_nt(kv_ref[:, later], outs)

    ahead = products(0)
    for p in range(hidden // lanes):
        part = slice(p * lanes, (p + 1) * lanes)
        later = slice(hidden + p * lanes, hidden + (p + 1) * lanes)
        queries, outs, scores, dweights = ahead
        ahead = products(p + 1) if (p + 1) * lanes < hidden else None
        keys = kv_ref[:, part]
        weights = jnp.exp(masked(scores, same) - log_ref[p : p + 1, :])
        inner = jnp.sum(dweights * weights, 0, keepdims=True)
        dscores = (weights * (dweights - inner)).astype(BF)
        dkv_ref[:, part] = mm(dscores, queries).astype(BF)
        dkv_ref[:, later] = mm(weights.astype(BF), outs).astype(BF)
        dq_ref[:, part] = (pair_join(mm_tn(keys, dscores), width) * scale).T.astype(BF)
    dq = dq_ref[...]
    own_mid = mm(
        (lax.broadcasted_iota(jnp.int32, (labels, rows), 1) == place_ref[...][:, 0:1]).astype(F32).astype(BF),
        mid_ref[...],
    ).astype(BF)
    g_ref[...] = adapter_scale * jnp.where(
        lax.broadcasted_iota(jnp.int32, g_ref.shape, 1) < edge,
        mm_tn(dq, own_mid),
        mm_tn(dkv_ref[:, hidden:], mid_ref[...]),
    )
    dmid_own = mm_nt(dq, adapt_ref[1, :, :hidden]).astype(BF)
    own = done + mm(dq, w_ref[:hidden, :]) + mm_nt(dmid_own, down_ref[1])
    spread = choose_t.astype(F32).astype(BF)
    own_high = own.astype(BF)
    own_rest = (own - own_high.astype(F32)).astype(BF)
    dmid = mm_nt(dkv_ref[:, hidden:], adapt_ref[1, :, 2 * hidden :]).astype(BF)
    step = split_of(hidden, 256, 128)
    for start in range(0, hidden, step):
        part = slice(start, start + step)
        dx_ref[:, part] = (
            mm(dkv_ref[...], w_ref[hidden:, part])
            + mm_nt(dmid, down_ref[1, part, :])
            + mm(spread, own_high[:, part])
            + mm(spread, own_rest[:, part])
        )


def last_backward(
    mean, logs, own, got, code, facts, saved, place_col, place_row, seg_wide, down, w, adapt, wo, up, dn, gains, hb, edge, shards
):
    kv = saved[0]
    rows = kv.shape[0]
    labels, hidden = saved[-1].shape
    whole = pl.BlockSpec(memory_space=pltpu.VMEM)
    anywhere = pl.BlockSpec(memory_space=pl.ANY)
    shape = jax.ShapeDtypeStruct
    return pl.pallas_call(
        functools.partial(last_backward_body, places=(up[1], dn[1]), edge=edge),
        in_specs=[anywhere] * 2 + [whole] * 22 + [anywhere] * 2 + [whole] * 2,
        out_specs=[whole] * 4,
        out_shape=[
            shape((rows, hidden), F32),
            shape((hidden, hidden), F32)
            if shards is None
            else shape((shards, -(-hidden // shards // 16) * 16, hidden), BF),
            shape((hidden, down.shape[2]), F32),
            shape(facts.shape, F32),
        ],
        scratch_shapes=[
            slab_scratch(up),
            slab_scratch(dn),
            pltpu.VMEM(kv.shape, BF),
            pltpu.VMEM((labels, hidden), BF),
            pltpu.VMEM((2, labels, hidden), BF),
            pltpu.SemaphoreType.DMA((4,)),
        ],
        compiler_params=params(),
        name="last_backward",
    )(own, got, mean, logs, code, facts, *saved, place_col, place_row, seg_wide, down, w, adapt, wo, up[0], dn[0], gains, hb)


def after_back_body(dout_ref, one_ref, two_ref, slope_ref, wo_ref, up_ref, down_ref, gain_ref, dctx_ref):
    dtwo = norm_back(two_ref[...], gain_ref[2:3, :], dout_ref[...])
    low = dtwo.astype(BF)
    dmiddle = dtwo
    units, step = feed_step(up_ref)
    dact = mm_nt(low, rows_of(down_ref, 0, step))
    for start in range(0, units, step):
        part = slice(start, start + step)
        later = mm_nt(low, rows_of(down_ref, start + step, step)) if start + step < units else None
        dgate = (slope_ref[:, part].astype(F32) * dact).astype(BF)
        dmiddle = dmiddle + mm(dgate, rows_of(up_ref, start, step))
        dact = later
    done = norm_back(one_ref[...], gain_ref[1:2, :], dmiddle)
    dctx_ref[...] = mm(done.astype(BF), wo_ref[...]).astype(BF)


def after_back(dout, one, two, slope, wo, up, down, norms):
    rows, width = dout.shape
    tile = split_of(rows, 256, 16)
    row = lambda n: pl.BlockSpec((tile, n), lambda i: (i, 0))
    return pl.pallas_call(
        after_back_body,
        grid=(rows // tile,),
        in_specs=[row(width), row(width), row(width), row(slope.shape[1]), full(wo.shape)]
        + [slab_spec(up), slab_spec(down), full(norms.shape)],
        out_specs=row(width),
        out_shape=jax.ShapeDtypeStruct((rows, width), BF),
        compiler_params=params(),
        name="after_back",
    )(dout, one, two, slope, wo, up[0], down[0], norms)


def attend_back_body(
    q_ref, k_ref, v_ref, dctx_ref, log_ref, seg_ref, seg_row_ref, mid_ref, g_ref, dv_ref, *, edge
):
    rows = q_ref.shape[0]
    width = q_ref.shape[1] // 2
    scale = width**-0.5
    dv_ref[...] = jnp.zeros_like(dv_ref)
    gq = jnp.zeros((2 * width, mid_ref.shape[1]), F32)
    turned = turn_blocks(k_ref)

    def products(start):
        own, near = reach_of(start, rows)
        queries = pair_rows(q_ref[own, :].astype(F32) * scale, width)
        outs = pair_rows(dctx_ref[own, :].astype(F32), width)
        return outs, mm_nt(k_ref[near, :], queries), mm_nt(v_ref[near, :], outs)

    now = products(0)
    for start in range(0, rows, REACH):
        own, near = reach_of(start, rows)
        later = products(start + REACH) if start + REACH < rows else None
        outs, scores, dweights = now
        same = seg_ref[near, :] == seg_row_ref[:, own]
        logs = log_ref[0, :, 2 * start : 2 * start + 2 * REACH]
        weights = jnp.exp(masked(scores, same) - logs)
        inner = jnp.sum(dweights * weights, 0, keepdims=True)
        dscores = (weights * (dweights - inner)).astype(BF)
        dv_ref[near, :] += mm(weights.astype(BF), outs)
        dq = (pair_join(mm(turned[:, near], dscores), width) * scale).astype(BF)
        gq = gq + mm(dq, mid_ref[own, :])
        now = later
    gv = mm_tn(dv_ref[...].astype(BF), mid_ref[...])
    g_ref[...] = adapter_scale * jnp.where(
        lax.broadcasted_iota(jnp.int32, gq.shape, 1) < edge, gq, gv
    )


def attend_back(qkv, dctx, logs, seg_wide, seg_row, mid, edge):
    rows, total = qkv.shape
    hidden = total // 3
    lanes = 2 * (hidden // HEADS)
    pairs = hidden // lanes
    column = lambda kind: pl.BlockSpec((rows, lanes), lambda p: (0, kind * pairs + p))
    return pl.pallas_call(
        functools.partial(attend_back_body, edge=edge),
        grid=(pairs,),
        in_specs=[
            column(0),
            column(1),
            column(2),
            column(0),
            pl.BlockSpec((1, 1, 2 * rows), lambda p: (p, 0, 0)),
            full(seg_wide.shape),
            full(seg_row.shape),
            full(mid.shape),
        ],
        out_specs=pl.BlockSpec((lanes, mid.shape[1]), lambda p: (p, 0)),
        out_shape=jax.ShapeDtypeStruct((hidden, mid.shape[1]), F32),
        scratch_shapes=[pltpu.VMEM((rows, lanes), F32)],
        compiler_params=params(),
        name="attend_back",
    )(qkv, qkv, qkv, dctx, logs, seg_wide, seg_row, mid)


MESH = pl.DeviceIdType.MESH


def position():
    dp, fsdp = lax.axis_index("dp"), lax.axis_index("fsdp")
    return {"x": dp, "z": fsdp // 4, "y": (fsdp // 2) % 2, "c": fsdp % 2}


def device_of(place):
    return (place["x"], (place["z"] * 2 + place["y"]) * 2 + place["c"])


def number_of(place):
    return place["x"] * 16 + (place["z"] * 2 + place["y"]) * 2 + place["c"]


def rank_device(number):
    return (number // 16, number % 16)


def greet_all(shards):
    barrier = pltpu.get_barrier_semaphore()
    me = lax.axis_index("dp") * 16 + lax.axis_index("fsdp")

    @pl.loop(1, shards)
    def _(k):
        pl.semaphore_signal(
            barrier, inc=1, device_id=rank_device((me + k) % shards), device_id_type=MESH
        )


def await_all(shards):
    pl.semaphore_wait(pltpu.get_barrier_semaphore(), shards - 1)


def direct_copy(source, target, sems, me, k, shards):
    return pltpu.make_async_remote_copy(
        src_ref=source,
        dst_ref=target,
        send_sem=sems.at[0],
        recv_sem=sems.at[1],
        device_id=rank_device((me + k) % shards),
        device_id_type=MESH,
    )


def spread(piece_of, buffer, sems, me, shards):
    @pl.loop(1, shards)
    def _(k):
        direct_copy(piece_of((me + k) % shards), buffer.at[me], sems, me, k, shards).start()


def collect(buffer, sems, me, shards):
    whole = buffer.at[pl.ds(0, shards - 1)]
    copy = direct_copy(whole, whole, sems, me, 1, shards)
    copy.wait_recv()
    copy.wait_send()


def relative_places(order):
    places = [
        {"x": dx, "z": dz, "y": dy} for dx in (0, 1) for dz in range(-3, 4) for dy in (0, 1)
    ]
    size = lambda p: abs(p["x"]) + abs(p["z"]) + abs(p["y"])
    return sorted(places, key=lambda p: (abs(p[order[-1]]), size(p), [abs(p[a]) for a in order]))


class Gather:
    def __init__(self, chunk, full_buffer, start, rows, order, sends, receives, hands, hands_got, cross=None):
        self.chunk, self.full, self.order = chunk, full_buffer, order
        self.part = pl.ds(start, rows)
        self.sends, self.receives, self.hands, self.hands_got = sends, receives, hands, hands_got
        self.cross = cross
        self.here = position()
        self.items = relative_places(order)

    def origin(self, item):
        here = self.here
        return {"x": (here["x"] + item["x"]) % 2, "z": here["z"] - item["z"], "y": (here["y"] + item["y"]) % 2, "c": here["c"]}

    def key(self, place):
        return (place["x"] * 4 + place["z"]) * 2 + place["y"]

    def outward(self, item):
        deepest = max([k for k, axis in enumerate(self.order) if item[axis]], default=-1)
        ways = []
        if deepest >= 0 and self.order[deepest] == "z":
            ways.append(("z", 1 if item["z"] > 0 else -1))
        for axis in self.order[deepest + 1 :]:
            ways += [("z", 1), ("z", -1)] if axis == "z" else [(axis, 1)]
        return ways

    def handed(self, item):
        return self.cross is None or sum(abs(step) for step in item.values()) != 1

    def copy(self, index, way, slot, item, crossing=False):
        here = self.here
        place = self.origin(item)
        number, key = number_of(place), self.key(place)
        mine = not any(item.values())
        source = self.chunk.at[self.part, :] if mine else self.full.at[number, self.part, :]
        if way is None:
            target = dict(here, c=1 - here["c"])
            sends, receives = self.hands.at[index], self.hands_got.at[key]
        else:
            axis, step = way
            target = dict(here)
            target[axis] = here["z"] + step if axis == "z" else 1 - here[axis]
            sends, receives = self.sends.at[index * 4 + slot], self.receives.at[key]
            if crossing:
                target["c"] = 1 - here["c"]
                sends, receives = self.cross.at[slot], self.hands_got.at[key]
        return pltpu.make_async_remote_copy(
            src_ref=source,
            dst_ref=self.full.at[number, self.part, :],
            send_sem=sends,
            recv_sem=receives,
            device_id=device_of(target),
            device_id_type=MESH,
        )

    def valid(self, item):
        z = self.here["z"] - item["z"]
        return (z >= 0) & (z <= 3)

    def step(self, index):
        item = self.items[index]

        @pl.when(self.valid(item))
        def _():
            if any(item.values()):
                self.arrived(index, item)
            for slot, way in enumerate(self.outward(item)):
                self.when_way(way, lambda way=way, slot=slot: self.copy(index, way, slot, item).start())
            if self.handed(item):
                self.copy(index, None, 0, item).start()
            if self.cross is not None and not any(item.values()):
                for slot, way in enumerate(self.outward(item)):
                    self.when_way(way, lambda way=way, slot=slot: self.copy(index, way, slot, item, True).start())

    def when_way(self, way, act):
        axis, step = way
        if axis == "z":
            z = self.here["z"] + step
            pl.when((z >= 0) & (z <= 3))(act)
        else:
            act()

    def arrived(self, index, item):
        place = self.origin(item)
        spot = self.full.at[number_of(place), self.part, :]
        pltpu.make_async_remote_copy(
            src_ref=spot,
            dst_ref=spot,
            send_sem=self.sends.at[index * 4],
            recv_sem=self.receives.at[self.key(place)],
            device_id=device_of(dict(self.here, c=1 - self.here["c"])),
            device_id_type=MESH,
        ).wait_recv()

    def finish(self):
        for index, item in enumerate(self.items):

            @pl.when(self.valid(item))
            def _(index=index, item=item):
                for slot, way in enumerate(self.outward(item)):
                    self.when_way(way, lambda way=way, slot=slot: self.copy(index, way, slot, item).wait_send())
                if self.cross is not None and not any(item.values()):
                    for slot, way in enumerate(self.outward(item)):
                        self.when_way(
                            way, lambda way=way, slot=slot: self.copy(index, way, slot, item, True).wait_send()
                        )
                if self.handed(item):
                    self.copy(index, None, 0, item).wait_send()
                place = dict(self.origin(item), c=1 - self.here["c"])
                spot = self.full.at[number_of(place), self.part, :]
                pltpu.make_async_remote_copy(
                    src_ref=spot,
                    dst_ref=spot,
                    send_sem=self.hands.at[index],
                    recv_sem=self.hands_got.at[self.key(place)],
                    device_id=device_of(dict(self.here, c=1 - self.here["c"])),
                    device_id_type=MESH,
                ).wait_recv()


ITEMS = 28


PICK = 64
GROUP = 16


def start_body(
    streams, shards, ids, low_ref, groups_any, fact, chunk, got, own_rows, facts, full_chunk, et_out,
    table, stage, rows, et_ref,
    row_sends, row_gets, fact_sems, own_sems, sends, receives, hands, hands_got,
):
    here = position()
    me = number_of(here)
    across = device_of(dict(here, x=1 - here["x"]))
    half, hidden = own_rows.shape
    batches = half // PICK
    fill = pltpu.make_async_copy(groups_any, table, own_sems.at[0])
    fill.start()
    greet_all(shards)
    own = [
        pltpu.make_async_copy(source, target, own_sems.at[1 + k])
        for k, (source, target) in enumerate(((fact, facts.at[me]), (chunk, full_chunk.at[me])))
    ]
    for copy in own:
        copy.start()
    await_all(shards)
    gathers = [
        Gather(
            chunk, full_chunk, start, size, order, sends.at[k], receives.at[k], hands.at[k], hands_got.at[k]
        )
        for k, (start, size, order) in enumerate(streams)
    ]
    for gather in gathers:
        gather.step(0)
    spread(lambda peer: fact, facts, fact_sems, me, shards)

    def send_rows(b):
        part = pl.ds(b * PICK, PICK)
        return pltpu.make_async_remote_copy(
            src_ref=rows.at[part, :],
            dst_ref=got.at[part, :],
            send_sem=row_sends.at[b],
            recv_sem=row_gets.at[b],
            device_id=across,
            device_id_type=MESH,
        )

    def pick(b):
        @pl.loop(0, PICK // 8)
        def _(t):
            found = [table[ids[b * PICK + t * 8 + k]] for k in range(8)]
            stage[pl.ds(pl.multiple_of(t * 8, 8), 8)] = jnp.stack(found)

        choose = (
            lax.broadcasted_iota(jnp.int32, (PICK, PICK * GROUP), 1)
            == low_ref[b * PICK : (b + 1) * PICK, :]
        )
        rows[b * PICK : (b + 1) * PICK, :] = mm(choose.astype(F32).astype(BF), flat(stage)).astype(BF)
        if b < batches:
            send_rows(b).start()

    count = et_ref.shape[1]
    first_group = (here["y"] * 2 + here["c"]) * (count // GROUP)

    def turn(k):
        block = table[pl.ds(first_group + k * (128 // GROUP), 128 // GROUP)].reshape(128, hidden)
        et_ref[:, k * 128 : (k + 1) * 128] = block.astype(F32).T.astype(BF)

    fill.wait()
    picked, turned, blocks = 0, 0, count // 128
    for index in range(1, ITEMS):
        while picked < min(2 * batches, 6 + 4 * index):
            pick(picked)
            picked += 1
        if picked == 2 * batches:
            for k in range(turned, min(turned + 3, blocks)):
                turn(k)
            turned = min(turned + 3, blocks)
        for gather in gathers:
            gather.step(index)
    for k in range(turned, blocks):
        turn(k)
    outs = [
        pltpu.make_async_copy(et_ref, et_out, own_sems.at[3]),
        pltpu.make_async_copy(rows.at[pl.ds(half, half), :], own_rows, own_sems.at[4]),
    ]
    for copy in outs:
        copy.start()
    for gather in gathers:
        gather.finish()
    collect(facts, fact_sems, me, shards)
    for b in range(batches):
        send_rows(b).wait()
    for copy in own + outs:
        copy.wait()


def vocab_rows(table, like):
    here = position()
    count = like.shape[0]
    return table.at[pl.ds(pl.multiple_of((here["y"] * 2 + here["c"]) * count, 16), count), :]


def gather_sems(streams):
    sems = pltpu.SemaphoreType.DMA
    count = len(streams)
    return [sems((count, 4 * ITEMS)), sems((count, 16)), sems((count, ITEMS)), sems((count, 16))]


def streams_of(rows, parts):
    streams, start = [], 0
    for k, (order, share) in enumerate(parts):
        size = rows - start if k == len(parts) - 1 else round(rows * share / 16) * 16
        streams.append((start, size, order))
        start += size
    return streams


def start_exchange(ids, table, fact, chunk, shards):
    anywhere = pl.BlockSpec(memory_space=pl.ANY)
    shape = jax.ShapeDtypeStruct
    sems = pltpu.SemaphoreType.DMA
    streams = streams_of(chunk.shape[0], (("xzy", 0.5), ("zxy", 0.28), ("xyz", 0.22)))
    half, hidden = ids.shape[0] // 2, table.shape[1]
    count = table.shape[0] // 4
    low = jnp.arange(ids.size, dtype=jnp.int32) % PICK * GROUP + ids % GROUP
    return pl.pallas_call(
        functools.partial(start_body, streams, shards),
        in_specs=[
            pl.BlockSpec(memory_space=pltpu.SMEM),
            pl.BlockSpec(memory_space=pltpu.VMEM),
        ]
        + [anywhere] * 3,
        out_specs=[anywhere] * 5,
        out_shape=[
            shape((half, hidden), table.dtype),
            shape((half, hidden), table.dtype),
            shape((shards, *fact.shape), fact.dtype),
            shape((shards, *chunk.shape), chunk.dtype),
            shape((hidden, count), BF),
        ],
        scratch_shapes=[
            pltpu.VMEM((table.shape[0] // GROUP, GROUP, hidden), BF),
            pltpu.VMEM((PICK, GROUP, hidden), BF),
            pltpu.VMEM((2 * half, hidden), BF),
            pltpu.VMEM((hidden, count), BF),
            sems((half // PICK,)),
            sems((half // PICK,)),
            sems((2,)),
            sems((5,)),
            *gather_sems(streams),
        ],
        compiler_params=params(collective_id=1, has_side_effects=True),
        name="start_exchange",
    )(ids // GROUP, low[:, None], table.reshape(-1, GROUP, hidden), fact, chunk)


def first_layer_body(
    streams, shards,
    own_any, got_any, first_any, other_any, chunk, code_ref, spots_ref, gain_ref, shift_ref, down_ref,
    adapt_ref, bias_ref, seg_ref, seg_row_ref,
    qkv_out, x_out, one_out, two_out, slope_out, wo_out, full_chunk, mid_ref, log_ref,
    own, got, in_slab, w, wo, up, dn, x, qkv, ctx, two, out, slope,
    load_sems, tile_sems, out_sems, cross, sends, receives, hands, hands_got,
):
    here = position()
    me = number_of(here)
    rows, hidden = x.shape
    tile = split_of(rows, 256, 16)
    tiles = rows // tile
    lanes = 2 * (hidden // HEADS)
    pairs = hidden // lanes

    rest = first_any.shape[1] - up.shape[1]
    cut = dn.shape[1] - rest

    def slab(source, target, start):
        return source.at[:, pl.ds(start, target.shape[1]), :]

    loads = [
        pltpu.make_async_copy(source, target, load_sems.at[k])
        for k, (source, target) in enumerate(
            (
                (own_any.at[pl.ds(0, rows), :], own),
                (got_any.at[pl.ds(0, rows), :], got),
                (slab(other_any, in_slab, cut), in_slab),
                (slab(first_any, up, 0), up),
                (other_any.at[:, pl.ds(0, cut), :], dn.at[:, pl.ds(0, cut), :]),
                (first_any.at[:, pl.ds(up.shape[1], rest), :], dn.at[:, pl.ds(cut, rest), :]),
                (chunk, full_chunk.at[me]),
            )
        )
    ]
    for copy in loads:
        copy.start()
    barrier = pltpu.get_barrier_semaphore()
    peers = [dict(here, c=1 - here["c"])]
    for core in (here["c"], 1 - here["c"]):
        there = dict(here, c=core)
        peers += [dict(there, x=1 - here["x"]), dict(there, y=1 - here["y"])]
        peers += [dict(there, z=flip(here["z"], k)) for k in (1, 2, 3)]
    for peer in peers:
        pl.semaphore_signal(barrier, inc=1, device_id=device_of(peer), device_id_type=MESH)
    pl.semaphore_wait(barrier, len(peers))
    gathers = [
        Gather(
            chunk, full_chunk, start, size, order, sends.at[k], receives.at[k], hands.at[k], hands_got.at[k],
            cross.at[k],
        )
        for k, (start, size, order) in enumerate(streams)
    ]
    def advance(*ranges):
        pairs_of = [(0, ranges[0]), (1, ranges[0])] + [(2, r) for r in ranges[1:]]
        for k, (first, last) in pairs_of:
            for index in range(first, last + 1):
                gathers[k].step(index)

    def at(i, plan):
        for k, ranges in plan.items():
            pl.when(i == k)(functools.partial(advance, *ranges))

    advance((0, 0), (0, 0))
    for copy in loads[:3]:
        copy.wait()
    unpack_rows(in_slab, (w, wo))

    @pl.loop(0, tiles)
    def _(i):
        part = pl.ds(pl.multiple_of(i * tile, tile), tile)
        project_body(
            own.at[part, :], got.at[part, :], code_ref.at[part, :], spots_ref, gain_ref, shift_ref, down_ref, w,
            adapt_ref, bias_ref, qkv.at[part, :], mid_ref.at[part, :], x.at[part, :],
        )

        at(i, {tiles - 3: ((1, 3), (1, 3)), tiles - 1: ((4, 5),)})

    early = [
        pltpu.make_async_copy(qkv, qkv_out, out_sems.at[0]),
        pltpu.make_async_copy(wo, wo_out, out_sems.at[1]),
    ]
    for copy in early:
        copy.start()

    @pl.loop(0, pairs)
    def _(p):
        column = lambda kind: pl.ds(pl.multiple_of((kind * pairs + p) * lanes, lanes), lanes)
        attend_body(
            qkv.at[:, column(0)], qkv.at[:, column(1)], qkv.at[:, column(2)], seg_ref, seg_row_ref,
            ctx.at[:, column(0)], log_ref.at[pl.ds(p, 1)],
        )

        at(
            p - (pairs - 6),
            {
                0: ((1, 0), (4, 11)),
                1: ((6, 7),),
                2: ((14, 15),),
                3: ((8, 9),),
                4: ((16, 17), (12, 19)),
                5: ((10, 11),),
            },
        )

    for copy in loads[3:6]:
        copy.wait()

    def tile_copies(i):
        part = pl.ds(pl.multiple_of(i * tile, tile), tile)
        turn = i % 2
        return [
            pltpu.make_async_copy(source, target.at[part, :], tile_sems.at[k, i])
            for k, (source, target) in enumerate(
                (
                    (out.at[turn], x_out),
                    (two.at[turn], two_out),
                    (slope.at[turn], slope_out),
                    (x.at[part, :], one_out),
                )
            )
        ]

    plan = {0: ((12, 13),), 1: ((18, 21), (20, 27)), 2: ((22, 25),), 3: ((26, 27),)}

    @pl.loop(0, tiles)
    def _(i):
        part = pl.ds(pl.multiple_of(i * tile, tile), tile)
        turn = i % 2

        @pl.when(i >= 2)
        def _():
            for copy in tile_copies(i - 2):
                copy.wait()

        after_body(
            ctx.at[part, :], x.at[part, :], wo, up, dn, bias_ref, gain_ref, shift_ref, out.at[turn],
            x.at[part, :], two.at[turn], slope.at[turn],
        )
        for copy in tile_copies(i):
            copy.start()
        at(i - (tiles - 4), plan)

    for gather in gathers:
        gather.finish()
    for i in (tiles - 2, tiles - 1):
        for copy in tile_copies(i):
            copy.wait()
    for copy in early + loads[6:]:
        copy.wait()


def first_layer(own, got, first, other, chunk, more, shards):
    whole = pl.BlockSpec(memory_space=pltpu.VMEM)
    anywhere = pl.BlockSpec(memory_space=pl.ANY)
    down, seg_row = more[4], more[-1]
    rows, hidden = seg_row.shape[1], own.shape[1]
    tile = split_of(rows, 256, 16)
    pairs = HEADS // 2
    units = 4 * hidden
    each = units // shards
    shape = jax.ShapeDtypeStruct
    sems = pltpu.SemaphoreType.DMA
    streams = streams_of(chunk.shape[0], (("zxy", 0.4), ("zyx", 0.4), ("xyz", 0.2)))
    return pl.pallas_call(
        functools.partial(first_layer_body, streams, shards),
        in_specs=[anywhere] * 5 + [whole] * len(more),
        out_specs=[anywhere] * 7 + [whole] * 2,
        out_shape=[
            shape((rows, 3 * hidden), BF),
            shape((rows, hidden), F32),
            shape((rows, hidden), F32),
            shape((rows, hidden), F32),
            shape((rows, units), BF),
            shape((hidden, hidden), BF),
            shape((shards, *chunk.shape), BF),
            shape((rows, down.shape[2]), BF),
            shape((pairs, 1, 2 * rows), F32),
        ],
        scratch_shapes=[
            pltpu.VMEM((rows, hidden), BF),
            pltpu.VMEM((rows, hidden), BF),
            pltpu.VMEM((shards, 4 * hidden // shards, hidden), BF),
            pltpu.VMEM((3 * hidden, hidden), BF),
            pltpu.VMEM((hidden, hidden), BF),
            pltpu.VMEM((shards, each, hidden), BF),
            pltpu.VMEM((shards, each, hidden), BF),
            pltpu.VMEM((rows, hidden), F32),
            pltpu.VMEM((rows, 3 * hidden), BF),
            pltpu.VMEM((rows, hidden), BF),
            pltpu.VMEM((2, tile, hidden), F32),
            pltpu.VMEM((2, tile, hidden), F32),
            pltpu.VMEM((2, tile, units), BF),
            sems((7,)),
            sems((4, rows // tile)),
            sems((2,)),
            sems((len(streams), 4)),
            *gather_sems(streams),
        ],
        compiler_params=params(collective_id=3, has_side_effects=True),
        name="first_layer",
    )(own, got, first, other, chunk, *more)


def adam(weight, gradient, moment_one, moment_two, fade_one, fade_two):
    moment_one = beta_first * moment_one + (1.0 - beta_first) * gradient
    moment_two = beta_second * moment_two + (1.0 - beta_second) * gradient * gradient
    one_hat = moment_one / fade_one
    two_hat = moment_two / fade_two
    weight = weight - learn_rate * (one_hat / (jnp.sqrt(two_hat) + adam_eps) + decay_rate * weight)
    return (weight, moment_one, moment_two)


BACK_TILE = 256


def finish_body(
    shards, edge,
    dout_any, one_any, two_any, slope_any, wo_any, first_any, other_any, qkv_any, gain_ref, log_ref, seg_ref,
    seg_row_ref, mid_ref, parts, late_ref, facts,
    sums_ref, dense_ref, total_ref,
    dout, one, two, slope, wo, up, dn, qkv, dctx, dv, grad, core_got, chip_sum, dense_got, grad_got, note, notes,
    tile_sems, load_sems, core_sems, dense_sems, grad_sems, note_sems,
):
    rows, hidden = dout.shape
    tile = split_of(rows, BACK_TILE, 16)
    tiles = rows // tile
    me = number_of(position())

    def tile_loads(i):
        part = pl.ds(pl.multiple_of(i * tile, tile), tile)
        return [
            pltpu.make_async_copy(source.at[part, :], target.at[part, :], tile_sems.at[k, i])
            for k, (source, target) in enumerate(
                ((two_any, two), (dout_any, dout), (slope_any, slope), (one_any, one))
            )
        ]

    here = position()
    rest = first_any.shape[1] - up.shape[1]
    cut = dn.shape[1] - rest
    chips = shards // 2
    chip, core = me // 2, here["c"]
    to_core = pltpu.make_async_remote_copy(
        src_ref=parts.at[:, 1 - core],
        dst_ref=core_got,
        send_sem=core_sems.at[0],
        recv_sem=core_sems.at[1],
        device_id=device_of(dict(here, c=1 - core)),
        device_id_type=MESH,
    )

    def to_chip(k):
        peer = (chip + k) % chips
        return pltpu.make_async_remote_copy(
            src_ref=chip_sum.at[peer],
            dst_ref=dense_got.at[chip],
            send_sem=dense_sems.at[0],
            recv_sem=dense_sems.at[1],
            device_id=rank_device(2 * peer + core),
            device_id_type=MESH,
        )

    loads = [
        pltpu.make_async_copy(source, target, load_sems.at[k])
        for k, (source, target) in enumerate(
            (
                (other_any.at[:, pl.ds(0, cut), :], dn.at[:, pl.ds(0, cut), :]),
                (first_any.at[:, pl.ds(up.shape[1], rest), :], dn.at[:, pl.ds(cut, rest), :]),
                (first_any.at[:, pl.ds(0, up.shape[1]), :], up),
                (wo_any, wo),
                (qkv_any, qkv),
            )
        )
    ]
    for copy in tile_loads(0) + loads[:4]:
        copy.start()
    for i in range(1, tiles):
        for copy in tile_loads(i):
            copy.start()
    loads[4].start()
    greet_all(shards)
    for copy in loads[:4]:
        copy.wait()

    @pl.loop(0, tiles)
    def _(i):
        for copy in tile_loads(i):
            copy.wait()
        part = pl.ds(pl.multiple_of(i * tile, tile), tile)
        after_back_body(
            dout.at[part, :], one.at[part, :], two.at[part, :], slope.at[part, :], wo, up, dn, gain_ref,
            dctx.at[part, :],
        )

        @pl.when(i == 0)
        def _():
            await_all(shards)
            to_core.start()

        @pl.when(i == 1)
        def _():
            to_core.wait_recv()

            @pl.loop(0, chips)
            def _(k):
                chip_sum[k] = (parts[k, core].astype(F32) + core_got[k].astype(F32)).astype(BF)

            dense_got[chip] = chip_sum[chip]

            @pl.loop(1, chips)
            def _(k):
                to_chip(k).start()

    loads[4].wait()
    lanes = 2 * (hidden // HEADS)
    pairs = hidden // lanes

    @pl.loop(0, pairs)
    def _(p):
        column = lambda kind: pl.ds(pl.multiple_of((kind * pairs + p) * lanes, lanes), lanes)
        attend_back_body(
            qkv.at[:, column(0)], qkv.at[:, column(1)], qkv.at[:, column(2)], dctx.at[:, column(0)],
            log_ref.at[pl.ds(p, 1)], seg_ref, seg_row_ref, mid_ref, grad.at[column(0), :], dv, edge=edge,
        )

    grad[...] = grad[...] + late_ref[...]
    each = hidden // shards
    piece = lambda peer: grad.at[pl.ds(pl.multiple_of(peer * each, each), each), :]
    grad_got[me] = piece(me)[...]
    spread(piece, grad_got, grad_sems, me, shards)
    others = chip_sum.at[pl.ds(0, chips - 1)]
    every = pltpu.make_async_remote_copy(
        src_ref=others,
        dst_ref=dense_got.at[pl.ds(0, chips - 1)],
        send_sem=dense_sems.at[0],
        recv_sem=dense_sems.at[1],
        device_id=device_of(dict(here, c=1 - core)),
        device_id_type=MESH,
    )
    every.wait_recv()
    every.wait_send()
    to_core.wait_send()
    dense = jnp.zeros((each, hidden), F32)
    for k in range(chips):
        dense = dense + dense_got[k].astype(F32)[:each, :]
    dense_ref[...] = dense
    square = jnp.sum(dense * dense, keepdims=True)
    collect(grad_got, grad_sems, me, shards)
    total = grad_got[0]
    for k in range(1, shards):
        total = total + grad_got[k]
    total_ref[...] = total
    square = square + jnp.sum(total * total, keepdims=True)
    row = lax.broadcasted_iota(jnp.int32, note.shape, 0)
    note[...] = jnp.where(row == 0, facts[...], jnp.where(row == 1, square, 0.0))
    notes[me] = note[...]
    spread(lambda peer: note, notes, note_sems, me, shards)
    collect(notes, note_sems, me, shards)
    sums = notes[0]
    for k in range(1, shards):
        sums = sums + notes[k]
    sums_ref[...] = sums


def update_body(
    sums_ref, dense_ref, total_ref, facts, head_w, head_m, head_v, adapt_w, adapt_m, adapt_v,
    loss_out, norm_out, head_w_out, head_m_out, head_v_out, adapt_w_out, adapt_m_out, adapt_v_out,
):
    norm = jnp.sqrt(sums_ref[1:2, 0:1])
    loss_out[...] = sums_ref[0:1, 0:1]
    norm_out[...] = norm
    factor = jnp.minimum(1.0, clip_limit / (norm + 1e-06))
    fades = facts[1:2, 0:1], facts[2:3, 0:1]
    new = adam(head_w[...], dense_ref[...] * factor, head_m[...], head_v[...], *fades)
    head_w_out[...], head_m_out[...], head_v_out[...] = new
    grad = (total_ref[...] * factor).T
    layers, kinds, rank, unused = adapt_w.shape
    for layer in range(layers):
        for kind in range(kinds):
            at = (layer * kinds + kind) * rank
            new = adam(
                adapt_w[layer, kind], grad[at : at + rank], adapt_m[layer, kind], adapt_v[layer, kind], *fades
            )
            adapt_w_out[layer, kind], adapt_m_out[layer, kind], adapt_v_out[layer, kind] = new


def update(sums, dense, total, facts, heads, adapts):
    whole = pl.BlockSpec(memory_space=pltpu.VMEM)
    shape = jax.ShapeDtypeStruct
    return pl.pallas_call(
        update_body,
        in_specs=[whole] * 10,
        out_specs=[whole] * 8,
        out_shape=[shape((1, 1), F32)] * 2 + [shape(a.shape, F32) for a in (*heads, *adapts)],
        compiler_params=params(),
        name="update",
    )(sums, dense, total, facts, *heads, *adapts)


def finish(back, qkv, logs, seg_wide, seg_row, mid, parts, late, facts, edge, shards):
    dout, one, two, slope, wo, first, other, gains = back
    slab = pltpu.VMEM((shards, slope.shape[1] // shards, dout.shape[1]), BF)
    parts = parts.reshape(-1, 2, *parts.shape[1:])
    rows, hidden = dout.shape
    each = hidden // shards
    whole = pl.BlockSpec(memory_space=pltpu.VMEM)
    anywhere = pl.BlockSpec(memory_space=pl.ANY)
    shape = jax.ShapeDtypeStruct
    sems = pltpu.SemaphoreType.DMA
    tiles = rows // split_of(rows, BACK_TILE, 16)
    return pl.pallas_call(
        functools.partial(finish_body, shards, edge),
        in_specs=[anywhere] * 8 + [whole] * 8,
        out_specs=[whole] * 3,
        out_shape=[
            shape((8, 128), F32),
            shape((each, hidden), F32),
            shape((each, late.shape[1]), F32),
        ],
        scratch_shapes=[
            pltpu.VMEM((rows, hidden), F32),
            pltpu.VMEM((rows, hidden), F32),
            pltpu.VMEM((rows, hidden), F32),
            pltpu.VMEM(slope.shape, BF),
            pltpu.VMEM(wo.shape, BF),
            slab,
            slab,
            pltpu.VMEM(qkv.shape, BF),
            pltpu.VMEM((rows, hidden), BF),
            pltpu.VMEM((rows, 2 * (hidden // HEADS)), F32),
            pltpu.VMEM(late.shape, F32),
            pltpu.VMEM((shards // 2, *parts.shape[2:]), BF),
            pltpu.VMEM((shards // 2, *parts.shape[2:]), BF),
            pltpu.VMEM((shards // 2, *parts.shape[2:]), BF),
            pltpu.VMEM((shards, each, late.shape[1]), F32),
            pltpu.VMEM((8, 128), F32),
            pltpu.VMEM((shards, 8, 128), F32),
            sems((4, tiles)),
            sems((5,)),
            sems((2,)),
            sems((2,)),
            sems((2,)),
            sems((2,)),
        ],
        compiler_params=params(collective_id=2, has_side_effects=True),
        name="finish",
    )(dout, one, two, slope, wo, first, other, qkv, gains, logs, seg_wide, seg_row, mid, parts, late, facts)


LOG_ROWS = 16


def flip(z, k):
    return (z % 2 + k % 2) % 2 + 2 * ((z // 2 + k // 2) % 2)


def pack_log(log_row, rows):
    high = log_row.astype(BF).astype(F32)
    middle = (log_row - high).astype(BF).astype(F32)
    low = log_row - high - middle
    row = lax.broadcasted_iota(jnp.int32, (rows, log_row.shape[1]), 0)
    return jnp.where(
        row == 0, high, jnp.where(row == 1, middle, jnp.where(row == 2, low, 0.0))
    ).astype(BF)


def unpack(block, hidden):
    logs = block[hidden : hidden + LOG_ROWS, :].astype(F32)
    return block[:hidden, :].astype(F32), jnp.sum(logs, 0, keepdims=True)


def merged(one, two):
    top = jnp.maximum(one[1], two[1])
    first, second = jnp.exp(one[1] - top), jnp.exp(two[1] - top)
    total = first + second
    inverse = 1.0 / total
    return one[0] * (first * inverse) + two[0] * (second * inverse), top + jnp.log(total)


def store_packed(ref, pair, hidden):
    ref[:hidden, :] = pair[0].astype(BF)
    ref[hidden : hidden + LOG_ROWS, :] = pack_log(pair[1], LOG_ROWS)


def head_body(
    u_ref, bias_ref, table_any, et_any, mean_ref, log_ref,
    e_ref, et_ref, bias_wide, feats, packs, handed, sums,
    loads, far_send, far_get, hand_send, hand_get, part_send, part_get, sum_send, sum_get,
):
    here = position()
    x, y, c = here["x"], here["y"], here["c"]
    labels, hidden = u_ref.shape
    sibling = device_of(dict(here, c=1 - c))

    def chip_at(k):
        return (x + k % 2) % 2, (y + k // 2) % 2

    def device_at(k):
        there = chip_at(k)
        return device_of(dict(here, x=there[0], y=there[1]))

    def slot(k, core):
        there = chip_at(k)
        return (there[0] * 2 + there[1]) * 2 + core

    fills = [
        pltpu.make_async_copy(source, target, loads.at[k])
        for k, (source, target) in enumerate(
            ((vocab_rows(table_any, e_ref), e_ref), (et_any, et_ref))
        )
    ]
    for fill in fills:
        fill.start()
    barrier = pltpu.get_barrier_semaphore()
    for target in (sibling, *[device_at(k) for k in (1, 2, 3)]):
        pl.semaphore_signal(barrier, inc=1, device_id=target, device_id_type=MESH)
    feats[slot(0, c)] = u_ref[...]
    pl.semaphore_wait(barrier, 4)

    def move(place, device, send, get):
        return pltpu.make_async_remote_copy(
            src_ref=feats.at[place],
            dst_ref=feats.at[place],
            send_sem=send,
            recv_sem=get,
            device_id=device,
            device_id_type=MESH,
        )

    def far(k):
        return move(slot(0, c), device_at(k), far_send.at[k], far_get.at[k])

    def far_here(k):
        return move(slot(k, c), device_at(k), far_send.at[k], far_get.at[k])

    def hand(k, core):
        return move(slot(k, core), sibling, hand_send.at[k], hand_get.at[k])

    for k in (1, 2, 3):
        far(k).start()
    hand(0, c).start()

    @pl.loop(0, bias_ref.shape[0])
    def _(b):
        row = jnp.broadcast_to(bias_ref[pl.ds(b, 1), :], (128, 128))
        bias_wide[pl.ds(pl.multiple_of(b * 128, 128), 128), :] = row.T

    for k in (1, 2, 3):
        far_here(k).wait_recv()
        hand(k, c).start()
    for fill in fills:
        fill.wait()
    count = e_ref.shape[0]
    steps = 4

    def target_of(s):
        return (s + 1) % steps

    def hand_part(s):
        return pltpu.make_async_remote_copy(
            src_ref=packs.at[s, 1 - c],
            dst_ref=handed.at[s],
            send_sem=part_send.at[s],
            recv_sem=part_get.at[s],
            device_id=sibling,
            device_id_type=MESH,
        )

    def sum_part(s):
        return pltpu.make_async_remote_copy(
            src_ref=packs.at[s, c],
            dst_ref=sums.at[s],
            send_sem=sum_send.at[s],
            recv_sem=sum_get.at[s],
            device_id=device_at(target_of(s)),
            device_id_type=MESH,
        )

    def together(s):
        hand_part(s).wait_recv()
        return merged(unpack(packs[s, c], hidden), unpack(handed[s], hidden))

    def settle(s):
        store_packed(packs.at[s, c], together(s), hidden)
        sum_part(s).start()

    @pl.loop(0, steps)
    def _(s):
        k = target_of(s)
        hand(k, 1 - c).wait_recv()
        u = feats[pl.ds(slot(k, 0), 2)].reshape(2 * labels, hidden)
        top = total = mean = None

        def scored(start):
            part = slice(start, min(start + 1280, count))
            bias = bias_wide[part, :]
            return mm_nt(e_ref[part, :], u) + jnp.concatenate([bias, bias], 1)

        @pl.when(s > 0)
        def _():
            settle(s - 1)

        logits = scored(0)
        for start in range(0, count, 1280):
            part = slice(start, min(start + 1280, count))
            later = scored(start + 1280) if start + 1280 < count else None
            high = jnp.max(logits, 0, keepdims=True)
            new = high if top is None else jnp.maximum(top, high)
            grown = jnp.exp(logits - new)
            part_sums = jnp.sum(grown, 0, keepdims=True)
            product = mm(et_ref[:, part], grown.astype(BF))
            if top is None:
                total, mean = part_sums, product
            else:
                shrink = jnp.exp(top - new)
                total, mean = total * shrink + part_sums, mean * shrink + product
            top = new
            logits = later
        mean = mean * (1.0 / total)
        logs = top + jnp.log(total)
        for core in range(2):
            half = slice(core * labels, (core + 1) * labels)
            packs[s, core, :hidden, :] = mean[:, half].astype(BF)
            packs[s, core, hidden : hidden + LOG_ROWS, :] = pack_log(logs[:, half], LOG_ROWS)
        hand_part(s).start()

    total = together(steps - 1)
    for s in range(steps - 1):
        sum_part(s).wait_recv()
        total = merged(total, unpack(sums[s], hidden))
    mean_ref[...] = total[0]
    log_ref[...] = total[1]
    for k in (1, 2, 3):
        far(k).wait_send()
    for k in range(4):
        hand(k, c).wait_send()
    for s in range(steps):
        hand_part(s).wait_send()
    for s in range(steps - 1):
        sum_part(s).wait_send()


def head(u, bias, table, et):
    labels, hidden = u.shape
    whole = pl.BlockSpec(memory_space=pltpu.VMEM)
    anywhere = pl.BlockSpec(memory_space=pl.ANY)
    shape = jax.ShapeDtypeStruct
    sems = pltpu.SemaphoreType.DMA
    block = (hidden + LOG_ROWS, labels)
    count = et.shape[1]
    return pl.pallas_call(
        head_body,
        in_specs=[whole] * 2 + [anywhere] * 2,
        out_specs=[whole] * 2,
        out_shape=[shape((hidden, labels), F32), shape((1, labels), F32)],
        scratch_shapes=[
            pltpu.VMEM((count, hidden), BF),
            pltpu.VMEM((hidden, count), BF),
            pltpu.VMEM((count, 128), F32),
            pltpu.VMEM((8, labels, hidden), BF),
            pltpu.VMEM((4, 2, *block), BF),
            pltpu.VMEM((4, *block), BF),
            pltpu.VMEM((4, *block), BF),
            sems((2,)),
        ]
        + [sems((4,))] * 8,
        compiler_params=params(collective_id=4, has_side_effects=True),
        name="head",
    )(u, bias, table, et)


def seg_positions(segments):
    index = jnp.arange(segments.shape[-1], dtype=jnp.int32)
    fresh = jnp.concatenate([jnp.ones((1,), dtype=bool), segments[1:] != segments[:-1]], -1)
    starts = lax.cummax(jnp.where(fresh, index, jnp.zeros_like(index)), axis=0)
    return index - starts


def pad_rows(matrix, multiple):
    return jnp.pad(matrix, ((0, -matrix.shape[0] % multiple), (0, 0)))


def slab_of(gathered, start, rows):
    if rows % 16 == 0 and start % rows == 0:
        return (gathered, start // rows, rows)
    part = gathered[:, start : start + rows].reshape(1, -1, gathered.shape[2])
    return (part, 0, part.shape[1])


def per_device(
    input_token_index,
    sentence_numbers,
    label_positions,
    label_target_token,
    sequence_task_index,
    task_loss_weight,
    optimizer_step_count,
    embed,
    position_embedding,
    norm_gain_vector,
    norm_bias_vector,
    attention_in_weight,
    attention_out_weight,
    feedforward_up,
    feedforward_down,
    layer_bias_vector,
    head_dense_bias,
    vocabulary_bias,
    adapter_down_matrix,
    adapter_up_matrix,
    adapter_moment_first,
    adapter_moment_second,
    head_projection,
    head_moment_first,
    head_moment_second,
):
    shards = lax.axis_size("dp") * lax.axis_size("fsdp")
    dp_index = lax.axis_index("dp")
    fsdp_index = lax.axis_index("fsdp")
    layers, unused, rank, up_part = adapter_up_matrix.shape
    hidden = embed.shape[1]
    tokens = input_token_index.shape[1]
    labels = label_positions.shape[1]
    qkv_rows = attention_in_weight.shape[2]
    out_rows = attention_out_weight.shape[2]
    ff_rows = feedforward_up.shape[2]
    head_rows = head_projection.shape[0]

    grouped = (lax.axis_size("dp"), lax.axis_size("fsdp")) == (2, 16)
    feeds = [[feedforward_up[layer].T, feedforward_down[layer]] for layer in range(layers)]
    attends = [[attention_in_weight[layer].T, attention_out_weight[layer].T] for layer in range(layers)]
    cut = ff_rows // 32 * 16
    first_chunk = jnp.concatenate([feeds[0][0], feeds[0][1][cut:]], 0)
    other_full = lax.all_gather(
        jnp.concatenate([feeds[0][1][:cut], *attends[0]], 0), BOTH, axis=0, tiled=False
    )
    last_chunk = pad_rows(
        jnp.concatenate([feeds[1][0], *attends[1], head_projection.astype(BF)], 0), 32
    )
    last_feed = feeds[1][1]

    table_rows = embed.shape[0]
    wanted = jnp.concatenate([input_token_index[0], label_target_token[0]])
    dp_count = lax.axis_size("dp")
    group_ids = lax.all_gather(wanted, "dp", axis=0, tiled=False) - dp_index * table_rows
    inside = (group_ids >= 0) & (group_ids < table_rows)
    group_ids = jnp.clip(group_ids, 0, table_rows - 1)
    mine = lax.dynamic_index_in_dim(inside, dp_index, 0, keepdims=False)

    task_range = jnp.arange(TASKS, dtype=jnp.int32)
    slice_rows = vocabulary_bias.shape[0]
    ups = adapter_up_matrix.reshape(-1)
    if grouped:
        pair_ids = jnp.concatenate(
            [
                lax.dynamic_index_in_dim(group_ids, (dp_index + shift) % 2, 0, keepdims=False)
                for shift in (1, 0)
            ]
        )
        fact = jnp.concatenate([vocabulary_bias, ups, sequence_task_index.astype(F32)])
        fact_rows = -(-fact.size // 1024) * 8
        got, own_rows, facts, first_full, own_turned = start_exchange(
            pair_ids,
            embed,
            jnp.pad(fact, (0, fact_rows * 128 - fact.size)).reshape(fact_rows, 128),
            first_chunk,
            shards,
        )
        facts, last_feed = lax.optimization_barrier((facts, last_feed))
        facts = facts.reshape(shards, -1)
        all_bias = facts[:, :slice_rows].reshape(-1)
        every_up = facts[:, slice_rows : slice_rows + ups.size]
        every_task = facts[:, slice_rows + ups.size].astype(jnp.int32)
    else:
        looked = jnp.where(
            inside.reshape(-1)[:, None], embed[group_ids.reshape(-1)], jnp.zeros((), BF)
        )
        own_rows = got = lax.psum_scatter(looked, "dp", scatter_dimension=0, tiled=True)
        all_bias = lax.all_gather(vocabulary_bias, BOTH, axis=0, tiled=True)
        every_up = lax.all_gather(ups, BOTH, axis=0, tiled=False)
        every_task = lax.all_gather(sequence_task_index, BOTH, axis=0, tiled=True)
    counts = labels * jnp.sum((every_task[:, None] == task_range[None, :]).astype(F32), 0)
    task_hot = (sequence_task_index[:, None] == task_range[None, :]).astype(F32)
    row_weight = jnp.sum(task_hot[0] * (task_loss_weight / jnp.maximum(counts, 1.0)))
    ups_full = (
        every_up.astype(BF)
        .reshape(shards, layers, 2, rank, up_part)
        .transpose(1, 2, 3, 0, 4)
        .reshape(layers, 2, rank, hidden)
    )
    blank = jnp.zeros((rank, hidden), BF)
    spare = lambda rows: jnp.zeros((rows, 3 * hidden), BF)
    adapters = jnp.stack(
        [
            jnp.concatenate(
                [
                    spare(2 * rank * layer),
                    jnp.concatenate([2 * ups_full[layer, 0], blank, blank], 1),
                    jnp.concatenate([blank, blank, 2 * ups_full[layer, 1]], 1),
                    spare(128 - 2 * rank * (layer + 1)),
                ],
                0,
            )
            for layer in range(layers)
        ]
    )
    downs = jnp.stack(
        [
            jnp.pad(
                jnp.concatenate([adapter_down_matrix[layer, 0], adapter_down_matrix[layer, 1]], 1),
                ((0, 0), (2 * rank * layer, 128 - 2 * rank * (layer + 1))),
            )
            for layer in range(layers)
        ]
    )
    segments = sentence_numbers[0]
    code = (jnp.pad(2 * seg_positions(segments), (0, labels)) + mine.astype(jnp.int32))[:, None]
    seg_real = segments.astype(F32)
    seg_wide = jnp.broadcast_to(seg_real[:, None], (tokens, 128))
    seg_row = seg_real[None, :]
    place_row = label_positions
    place_col = jnp.broadcast_to(label_positions.reshape(labels, 1), (labels, 128))

    target_bias = all_bias[label_target_token[0]]

    gains, shifts = norm_gain_vector, norm_bias_vector
    last_inputs = (place_col, place_row, seg_wide, downs, adapters, layer_bias_vector)
    in_start = ff_rows
    last_dn = lax.all_gather(last_feed, BOTH, axis=0, tiled=False)
    slabs_of = lambda up_full, dn_full: (slab_of(up_full, 0, ff_rows), slab_of(dn_full, 0, ff_rows))
    if grouped:
        more = (
            code, position_embedding, gains, shifts, downs, adapters, layer_bias_vector, seg_wide, seg_row,
        )
        qkv, x_last, one, two, slope, out_first, last_full, mid, logs = first_layer(
            own_rows, got, first_full, other_full, last_chunk, more, shards
        )
        slabs = [None, slabs_of(last_full, last_dn)]
        *saved, in_last, out_last, head_full = last_forward(
            x_last, *last_inputs, (last_full,), (in_start, in_start + qkv_rows + out_rows), *slabs[1], gains,
            shifts, head_dense_bias[None, :],
        )
        count = own_turned.shape[1]
        own_bias = lax.dynamic_slice_in_dim(
            all_bias, dp_index * table_rows + fsdp_index % 4 * count, count, 0
        ).reshape(-1, 128)
        mean_t, own_logs = head(saved[-1], own_bias, embed, own_turned)
    else:
        first_full = lax.all_gather(first_chunk, BOTH, axis=0, tiled=False)
        last_full = lax.all_gather(last_chunk, BOTH, axis=0, tiled=False)
        dn_full = jnp.concatenate([other_full[:, :cut], first_full[:, ff_rows:]], 1)
        slabs = [slabs_of(first_full[:, :ff_rows], dn_full), slabs_of(last_full, last_dn)]
        taken = lambda full_chunk, start, size: full_chunk[:, start : start + size].reshape(-1, hidden)
        in_first = taken(other_full, cut, qkv_rows)
        out_first = taken(other_full, cut + qkv_rows, out_rows)
        in_last = taken(last_full, in_start, qkv_rows)
        out_last = taken(last_full, in_start + qkv_rows, out_rows)
        head_full = taken(last_full, in_start + qkv_rows + out_rows, head_rows)
        qkv, mid, hidden_rows = project(
            own_rows, got, code, position_embedding, gains, shifts, downs, in_first, adapters, layer_bias_vector, tokens
        )
        context, logs = attend(qkv, seg_wide, seg_row)
        x_last, one, two, slope = after(
            context, hidden_rows, out_first, *slabs[0], layer_bias_vector, gains, shifts
        )
        saved = last_forward(
            x_last, *last_inputs, (in_last, out_last, head_full), None, *slabs[1], gains, shifts,
            head_dense_bias[None, :],
        )
        features = saved[-1]
        own_slice = lax.dynamic_slice_in_dim(embed, fsdp_index * slice_rows, slice_rows, 0)
        own_vocab = jnp.concatenate(
            [own_slice]
            + [
                lax.ppermute(
                    own_slice, "dp", [(k, (k + shift) % dp_count) for k in range(dp_count)]
                )
                for shift in range(1, dp_count)
            ],
            0,
        )
        own_bias = jnp.concatenate(
            [
                lax.dynamic_slice_in_dim(
                    all_bias,
                    ((dp_index - shift) % dp_count) * table_rows + fsdp_index * slice_rows,
                    slice_rows,
                    0,
                )
                for shift in range(dp_count)
            ]
        )
        bias_wide = jnp.broadcast_to(own_bias[:, None], (own_bias.shape[0], 128))
        every = lax.all_gather(features, "fsdp", axis=0, tiled=True)
        means, local_logs = vocab(every, own_vocab, own_vocab.T, bias_wide, labels)
        local_logs = local_logs.reshape(-1, labels)
        all_logs = lax.all_gather(local_logs, "fsdp", axis=0, tiled=False)
        whole_logs = jax.nn.logsumexp(all_logs, axis=0)
        scaled = (means * jnp.exp(local_logs - whole_logs)[:, None, :]).astype(BF)
        mean_t = lax.psum_scatter(scaled, "fsdp", scatter_dimension=0, tiled=True)[0].astype(F32)
        own_logs = lax.dynamic_index_in_dim(whole_logs, fsdp_index, 0, keepdims=False)
        own_logs = own_logs[None, :]

    step_as_real = optimizer_step_count[0].astype(F32)
    fades = (1.0 - beta_first**step_as_real, 1.0 - beta_second**step_as_real)
    lanes = lambda value: jnp.pad(
        jnp.broadcast_to(value, (1, value.size if value.ndim else 128)), ((0, 0), (0, 128))
    )[:, :128]
    facts = jnp.concatenate(
        [lanes(value) for value in (row_weight, *fades, target_bias)] + [jnp.zeros((4, 128), F32)]
    )
    hidden_grad, dense_gradient, late, facts = last_backward(
        mean_t, own_logs, own_rows, got, code, facts, saved, place_col, place_row, seg_wide, downs, in_last, adapters,
        out_last, *slabs[1], gains, head_full, 3 * rank, shards if grouped else None,
    )
    back = (hidden_grad, one, two, slope, out_first)
    adapts = (adapter_up_matrix, adapter_moment_first, adapter_moment_second)
    heads = (head_projection, head_moment_first, head_moment_second)
    if grouped:
        sums, dense_portion, adapter_portion = finish(
            (*back, first_full, other_full, gains), qkv, logs, seg_wide, seg_row, mid, dense_gradient, late, facts, rank, shards
        )
        loss, norm, *new = update(sums, dense_portion, adapter_portion, facts, heads, adapts)
        return (loss[0, 0], norm[0, 0], *new[3:], *new[:3])
    dctx = after_back(*back, *slabs[0], gains)
    first = attend_back(qkv, dctx, logs, seg_wide, seg_row, mid, rank)
    adapter_gradient = (first + late)[:, : 2 * rank * layers].T.reshape(layers, 2, rank, hidden)
    dense_portion = lax.psum_scatter(dense_gradient, BOTH, scatter_dimension=0, tiled=True)
    adapter_portion = lax.psum_scatter(adapter_gradient, BOTH, scatter_dimension=3, tiled=True)
    squared_entries = jnp.sum(adapter_portion * adapter_portion) + jnp.sum(dense_portion * dense_portion)
    masked_task_loss, norm_square = lax.psum((facts[0, 0], squared_entries), BOTH)
    gradient_norm = jnp.sqrt(norm_square)
    factor = jnp.minimum(1.0, clip_limit / (gradient_norm + 1e-06))
    adapter_new = adam(adapts[0], adapter_portion * factor, *adapts[1:], *fades)
    dense_new = adam(heads[0], dense_portion * factor, *heads[1:], *fades)
    return (masked_task_loss, gradient_norm, *adapter_new, *dense_new)


def solution(mesh):
    rows = P(BOTH, None)
    in_specs = (
        rows,
        rows,
        rows,
        rows,
        P(BOTH),
        P(),
        P(),
        P("dp", None),
        P(),
        P(),
        P(),
        P(None, None, BOTH),
        P(None, None, BOTH),
        P(None, None, BOTH),
        P(None, BOTH, None),
        P(),
        P(),
        P(BOTH),
        P(),
        P(None, None, None, BOTH),
        P(None, None, None, BOTH),
        P(None, None, None, BOTH),
        rows,
        rows,
        rows,
    )
    adapter = P(None, None, None, BOTH)
    out_specs = (P(), P(), adapter, adapter, adapter, rows, rows, rows)
    return jax.shard_map(
        per_device, mesh=mesh, in_specs=in_specs, out_specs=out_specs, check_vma=False
    )
```

```python
import functools

import jax
import jax.numpy as jnp
from jax import lax
from jax.experimental import pallas as pl
from jax.experimental.pallas import tpu as pltpu
from jax.sharding import PartitionSpec as P

HEADS = 12
TASKS = 4
REACH = 128

norm_eps = 1e-05
adapter_scale = 2.0
clip_limit = 0.01
learn_rate = 0.05
beta_first = 0.9
beta_second = 0.999
adam_eps = 1e-08
decay_rate = 0.01
masked_score = -1e30

BF = jnp.bfloat16
F32 = jnp.float32
BOTH = ("dp", "fsdp")
VMEM_BYTES = 60 * 1024 * 1024


def mm(a, b):
    return lax.dot_general(a, b, (((1,), (0,)), ((), ())), preferred_element_type=F32)


def mm_nt(a, b):
    return lax.dot_general(a, b, (((1,), (1,)), ((), ())), preferred_element_type=F32)


def mm_tn(a, b):
    return lax.dot_general(a, b, (((0,), (0,)), ((), ())), preferred_element_type=F32)


def layer_norm(rows_in, gain, shift):
    center = rows_in - jnp.mean(rows_in, -1, keepdims=True)
    spread = jnp.mean(center * center, -1, keepdims=True)
    return center * lax.rsqrt(spread + norm_eps) * gain + shift


def norm_back(rows_in, gain, gradient):
    center = rows_in - jnp.mean(rows_in, -1, keepdims=True)
    inverse = lax.rsqrt(jnp.mean(center * center, -1, keepdims=True) + norm_eps)
    unit = center * inverse
    scaled = gradient * gain
    return inverse * (
        scaled
        - jnp.mean(scaled, -1, keepdims=True)
        - unit * jnp.mean(scaled * unit, -1, keepdims=True)
    )


def gelu_pair(v):
    size = jnp.abs(v) * 0.7071067811865476
    base = 1.0 + 0.3275911 * size
    t = pl.reciprocal(base, approx=True)
    t = t * (2.0 - base * t)
    bell = jnp.exp(-0.5 * v * v)
    poly = t * (
        0.127414796 + t * (-0.142248368 + t * (0.7107068705 + t * (-0.7265760135 + t * 0.5307027145)))
    )
    tail = poly * bell
    phi = jnp.where(v >= 0.0, 1.0 - tail, tail)
    return v * phi, phi + v * (bell * 0.3989422804014327)


def params(**more):
    return pltpu.CompilerParams(vmem_limit_bytes=VMEM_BYTES, **more)


def full(shape):
    return pl.BlockSpec(shape, lambda *_: (0,) * len(shape))


def split_of(total, most, step):
    size = (min(most, total) // step) * step
    while size > step and total % size:
        size -= step
    return size if size and total % size == 0 else total


def pair_rows(block, width):
    first = lax.broadcasted_iota(jnp.int32, block.shape, 1) < width
    return jnp.concatenate([jnp.where(first, block, 0.0), jnp.where(first, 0.0, block)], 0).astype(BF)


def pair_join(wide, width):
    rows = wide.shape[1] // 2
    return jnp.concatenate([wide[:width, :rows], wide[width:, rows:]], 0)


def masked(scores, same):
    rows = scores.shape[1] // 2
    return jnp.concatenate(
        [
            jnp.where(same, scores[:, :rows], masked_score),
            jnp.where(same, scores[:, rows:], masked_score),
        ],
        1,
    )


def qkv_bias(bias_ref, layer, start, size):
    hidden = bias_ref.shape[1] // 8
    if start >= 2 * hidden:
        return bias_ref[layer : layer + 1, start - hidden : start - hidden + size]
    return bias_ref[layer : layer + 1, start : start + size] if start < hidden else 0.0


def norm_of(norm_refs, k):
    return norm_refs[0][k : k + 1, :], norm_refs[1][k : k + 1, :]


def project_body(
    own_ref, got_ref, code_ref, spots_ref, gain_ref, shift_ref, down_ref, w_ref, up_ref, bias_ref,
    out_ref, mid_ref, x_ref,
):
    mine = code_ref[...] % 2
    choose = (
        lax.broadcasted_iota(jnp.int32, (own_ref.shape[0], spots_ref.shape[0]), 1) == code_ref[...] // 2
    )
    summed = jnp.where(
        mine > 0, own_ref[...].astype(F32), got_ref[...].astype(F32)
    ) + mm(choose.astype(F32).astype(BF), spots_ref[...])
    x = layer_norm(summed, *norm_of((gain_ref, shift_ref), 0))
    x_ref[...] = x
    low = x.astype(BF)
    mid = mm(low, down_ref[0]).astype(BF)
    mid_ref[...] = mid
    total = w_ref.shape[0]
    step = total // 3
    for start in range(0, total, step):
        part = slice(start, start + step)
        out_ref[:, part] = (
            mm_nt(low, w_ref[part, :]) + mm(mid, up_ref[0, :, part]) + qkv_bias(bias_ref, 0, start, step)
        ).astype(BF)


def project(own, got, code, spots, gains, shifts, down, w, up, bias, rows):
    width = own.shape[1]
    tile = split_of(rows, 256, 16)
    total = w.shape[0]
    row = lambda n: pl.BlockSpec((tile, n), lambda i: (i, 0))
    return pl.pallas_call(
        project_body,
        grid=(rows // tile,),
        in_specs=[row(width), row(width), row(1)]
        + [full(a.shape) for a in (spots, gains, shifts, down, w, up, bias)],
        out_specs=[row(total), row(down.shape[2]), row(width)],
        out_shape=[
            jax.ShapeDtypeStruct((rows, total), BF),
            jax.ShapeDtypeStruct((rows, down.shape[2]), BF),
            jax.ShapeDtypeStruct((rows, width), F32),
        ],
        compiler_params=params(),
        name="project",
    )(own, got, code, spots, gains, shifts, down, w, up, bias)


def attend_body(q_ref, k_ref, v_ref, seg_ref, seg_row_ref, ctx_ref, log_ref):
    rows = q_ref.shape[0]
    width = q_ref.shape[1] // 2
    scale = width**-0.5
    turned = turn_blocks(v_ref)

    def scored(start):
        own, near = reach_of(start, rows)
        return mm_nt(k_ref[near, :], pair_rows(q_ref[own, :].astype(F32) * scale, width))

    scores = scored(0)
    for start in range(0, rows, REACH):
        own, near = reach_of(start, rows)
        later = scored(start + REACH) if start + REACH < rows else None
        same = seg_ref[near, :] == seg_row_ref[:, own]
        scores = masked(scores, same)
        top = jnp.max(scores, 0, keepdims=True)
        weights = jnp.exp(scores - top)
        total = jnp.sum(weights, 0, keepdims=True)
        context = mm(turned[:, near], weights.astype(BF)) * (1.0 / total)
        ctx_ref[own, :] = pair_join(context, width).T.astype(BF)
        log_ref[0, :, 2 * start : 2 * start + 2 * REACH] = top + jnp.log(total)
        scores = later


def reach_of(start, rows):
    return slice(start, start + REACH), slice(max(0, start - REACH), min(rows, start + 2 * REACH))


def turn_blocks(ref):
    blocks = [ref[k : k + 128, :].astype(F32).T.astype(BF) for k in range(0, ref.shape[0], 128)]
    return jnp.concatenate(blocks, 1)


def attend(qkv, seg_wide, seg_row):
    rows, total = qkv.shape
    hidden = total // 3
    lanes = 2 * (hidden // HEADS)
    pairs = hidden // lanes
    column = lambda kind: pl.BlockSpec((rows, lanes), lambda p: (0, kind * pairs + p))
    return pl.pallas_call(
        attend_body,
        grid=(pairs,),
        in_specs=[column(0), column(1), column(2), full(seg_wide.shape), full(seg_row.shape)],
        out_specs=[
            pl.BlockSpec((rows, lanes), lambda p: (0, p)),
            pl.BlockSpec((1, 1, 2 * rows), lambda p: (p, 0, 0)),
        ],
        out_shape=[
            jax.ShapeDtypeStruct((rows, hidden), BF),
            jax.ShapeDtypeStruct((pairs, 1, 2 * rows), F32),
        ],
        compiler_params=params(),
        name="attend",
    )(qkv, qkv, qkv, seg_wide, seg_row)


def flat(ref):
    whole = ref[...]
    return whole.reshape(-1, whole.shape[-1])


def rows_of(ref, start, size):
    each = ref.shape[1]
    if size % each == 0 and start % each == 0 and each % 16 == 0:
        part = ref[start // each : (start + size) // each, :, :]
        return part.reshape(size, part.shape[-1])
    return flat(ref)[start : start + size, :]


def feed_step(ref):
    units = ref.shape[0] * ref.shape[1]
    step = ref.shape[1]
    while units % (2 * step) == 0 and 2 * step <= 768 and ref.shape[0] > 1:
        step *= 2
    return units, (step if ref.shape[0] > 1 else split_of(units, 768, 128))


def later_biases(bias_ref, layer):
    hidden = bias_ref.shape[1] // 8
    row = bias_ref[layer : layer + 1, :]
    return row[:, 2 * hidden : 3 * hidden], row[:, 3 * hidden : 7 * hidden], row[:, 7 * hidden :]


def after_body(
    ctx_ref, x_ref, wo_ref, up_ref, down_ref, bias_ref, gain_ref, shift_ref,
    out_ref, one_ref, two_ref, slope_ref,
):
    bo, b1, b2 = later_biases(bias_ref, 0)
    one = x_ref[...] + (mm_nt(ctx_ref[...], wo_ref[...]) + bo)
    one_ref[...] = one
    middle = layer_norm(one, *norm_of((gain_ref, shift_ref), 1))
    low = middle.astype(BF)
    total = middle + b2
    units, step = feed_step(up_ref)
    gate = mm_nt(low, rows_of(up_ref, 0, step))
    for start in range(0, units, step):
        part = slice(start, start + step)
        later = mm_nt(low, rows_of(up_ref, start + step, step)) if start + step < units else None
        act, slope = gelu_pair(gate + b1[:, part])
        slope_ref[:, part] = slope.astype(BF)
        total = total + mm(act.astype(BF), rows_of(down_ref, start, step))
        gate = later
    two_ref[...] = total
    out_ref[...] = layer_norm(total, *norm_of((gain_ref, shift_ref), 2))


def slab_spec(slab):
    array, place, rows = slab
    return pl.BlockSpec((array.shape[0], rows, array.shape[2]), lambda *_: (0, place, 0))


def after(ctx, x, wo, up, down, bias, gains, shifts):
    rows, width = x.shape
    tile = split_of(rows, 256, 16)
    units = 4 * width
    row = lambda n: pl.BlockSpec((tile, n), lambda i: (i, 0))
    return pl.pallas_call(
        after_body,
        grid=(rows // tile,),
        in_specs=[row(width), row(width), full(wo.shape), slab_spec(up), slab_spec(down)]
        + [full(a.shape) for a in (bias, gains, shifts)],
        out_specs=[row(width), row(width), row(width), row(units)],
        out_shape=[jax.ShapeDtypeStruct((rows, width), F32)] * 3
        + [jax.ShapeDtypeStruct((rows, units), BF)],
        compiler_params=params(),
        name="after",
    )(ctx, x, wo, up[0], down[0], bias, gains, shifts)


def exact_rows(choose, matrix):
    high = matrix.astype(BF)
    rest = matrix - high.astype(F32)
    middle = rest.astype(BF)
    low = (rest - middle.astype(F32)).astype(BF)
    return mm(choose, high) + mm(choose, middle) + mm(choose, low)


def unpack_rows(slab_ref, targets):
    shards = slab_ref.shape[0]

    @pl.loop(0, shards // 2)
    def _(k):
        first, second = slab_ref[2 * k].astype(F32), slab_ref[2 * k + 1].astype(F32)
        at = 0
        for target in targets:
            each = target.shape[0] // shards
            both = jnp.concatenate([first[at : at + each], second[at : at + each]], 0)
            target[pl.ds(pl.multiple_of(2 * each * k, 2 * each), 2 * each), :] = both.astype(BF)
            at += each


def last_forward_body(
    x_ref, place_ref, place_row_ref, seg_ref, down_ref, adapt_ref, bias_ref, weights_any, up_any, dn_any,
    gain_ref, shift_ref, hbias_ref,
    kv_ref, q_ref, mid_ref, log_ref, one_ref, slope_ref, two_ref, low_ref, act_ref, hslope_ref, feat_ref, *more,
    places, starts,
):
    copies = []
    if starts is None:
        up_ref, dn_ref, ctx_ref, w_ref, wo_ref, hb_ref, sems = more
        sources = zip(weights_any, (w_ref, wo_ref, hb_ref))
    else:
        w_out, wo_out, hb_out, up_ref, dn_ref, ctx_ref, w_ref, wo_ref, hb_ref, in_slab, hb_slab, sems = more
        sources = [
            (weights_any[0].at[:, pl.ds(start, slab.shape[1]), :], slab)
            for start, slab in zip(starts, (in_slab, hb_slab))
        ]
    for source, target in sources:
        copies.append((source, target))
    early = len(copies)
    for source, target, place in ((up_any, up_ref, places[0]), (dn_any, dn_ref, places[1])):
        each = target.shape[1]
        copies.append((source.at[:, pl.ds(place * each, each), :], target))
    copies = [pltpu.make_async_copy(*ends, sems.at[k]) for k, ends in enumerate(copies)]
    for copy in copies:
        copy.start()
    for copy in copies[:early]:
        copy.wait()
    copies = copies[early:]
    if starts is not None:
        unpack_rows(in_slab, (w_ref, wo_ref))
        unpack_rows(hb_slab, (hb_ref,))
        for k, ends in enumerate(((w_ref, w_out), (wo_ref, wo_out), (hb_ref, hb_out))):
            copies.append(pltpu.make_async_copy(*ends, sems.at[4 + k]))
            copies[-1].start()
    rows, hidden = x_ref.shape
    labels = place_ref.shape[0]
    lanes = 2 * (hidden // HEADS)
    width = lanes // 2
    low = x_ref[...].astype(BF)
    mid = mm(low, down_ref[1]).astype(BF)
    mid_ref[...] = mid
    step = split_of(hidden, 768, 128)
    for start in range(hidden, 3 * hidden, step):
        part = slice(start, start + step)
        kv_ref[:, start - hidden : start - hidden + step] = (
            mm_nt(low, w_ref[part, :]) + mm(mid, adapt_ref[1, :, part]) + qkv_bias(bias_ref, 1, start, step)
        ).astype(BF)
    choose = (
        lax.broadcasted_iota(jnp.int32, (labels, rows), 1) == place_ref[...][:, 0:1]
    ).astype(F32).astype(BF)
    own = exact_rows(choose, x_ref[...])
    own_low = own.astype(BF)
    own_mid = mm(choose, mid).astype(BF)
    q_ref[...] = (
        mm_nt(own_low, w_ref[:hidden, :])
        + mm(own_mid, adapt_ref[1, :, :hidden])
        + qkv_bias(bias_ref, 1, 0, hidden)
    ).astype(BF)
    seg = seg_ref[...]
    seg_own = jnp.sum(
        jnp.where(
            lax.broadcasted_iota(jnp.int32, (rows, labels), 0) == place_row_ref[...], seg, 0.0
        ),
        0,
        keepdims=True,
    )
    same = seg == seg_own

    def scored(p):
        part = slice(p * lanes, (p + 1) * lanes)
        return mm_nt(kv_ref[:, part], pair_rows(q_ref[:, part].astype(F32) * width**-0.5, width))

    later = scored(0)
    for p in range(hidden // lanes):
        part = slice(p * lanes, (p + 1) * lanes)
        scores = masked(later, same)
        later = scored(p + 1) if (p + 1) * lanes < hidden else None
        top = jnp.max(scores, 0, keepdims=True)
        weights = jnp.exp(scores - top)
        total = jnp.sum(weights, 0, keepdims=True)
        context = mm_tn(
            kv_ref[:, hidden + p * lanes : hidden + (p + 1) * lanes], weights.astype(BF)
        ) * (1.0 / total)
        ctx_ref[:, part] = pair_join(context, width).T.astype(BF)
        log_ref[p : p + 1, :] = top + jnp.log(total)
    bo, b1, b2 = later_biases(bias_ref, 1)
    norms = (gain_ref, shift_ref)
    one = own + (mm_nt(ctx_ref[...], wo_ref[...]) + bo)
    one_ref[...] = one
    middle = layer_norm(one, *norm_of(norms, 3))
    middle_low = middle.astype(BF)
    sum_two = middle + b2
    units, step = feed_step(up_ref)
    for copy in copies:
        copy.wait()
    gate = mm_nt(middle_low, rows_of(up_ref, 0, step))
    for start in range(0, units, step):
        part = slice(start, start + step)
        later = mm_nt(middle_low, rows_of(up_ref, start + step, step)) if start + step < units else None
        act, slope = gelu_pair(gate + b1[:, part])
        gate = later
        slope_ref[:, part] = slope.astype(BF)
        sum_two = sum_two + mm(act.astype(BF), rows_of(dn_ref, start, step))
    two_ref[...] = sum_two
    out_low = layer_norm(sum_two, *norm_of(norms, 4)).astype(BF)
    low_ref[...] = out_low
    act, slope = gelu_pair(mm(out_low, hb_ref[...]) + hbias_ref[...])
    act_ref[...] = act
    hslope_ref[...] = slope
    feat_ref[...] = layer_norm(act, *norm_of(norms, 5)).astype(BF)


def slab_scratch(slab):
    array, place, rows = slab
    return pltpu.VMEM((array.shape[0], rows, array.shape[2]), BF)


def last_forward(
    x, place_col, place_row, seg_wide, down, adapt, bias, weights, starts, up, dn, gains, shifts, hbias
):
    rows, hidden = x.shape
    labels = place_col.shape[0]
    units = 4 * hidden
    whole = pl.BlockSpec(memory_space=pltpu.VMEM)
    anywhere = pl.BlockSpec(memory_space=pl.ANY)
    shape = jax.ShapeDtypeStruct
    pairs = HEADS // 2
    matrices = [(3 * hidden, hidden), (hidden, hidden), (hidden, hidden)]
    slabs = []
    if starts is not None:
        shards = weights[0].shape[0]
        slabs = [
            pltpu.VMEM((shards, 4 * hidden // shards, hidden), BF),
            pltpu.VMEM((shards, weights[0].shape[1] - starts[1], hidden), BF),
        ]

    def body(*refs):
        head, rest = refs[:7], refs[7:]
        return last_forward_body(
            *head, rest[: len(weights)], *rest[len(weights) :], places=(up[1], dn[1]), starts=starts
        )

    return pl.pallas_call(
        body,
        in_specs=[whole] * 7 + [anywhere] * (len(weights) + 2) + [whole] * 3,
        out_specs=[whole] * 11 + ([anywhere] * 3 if slabs else []),
        out_shape=[
            shape((rows, 2 * hidden), BF),
            shape((labels, hidden), BF),
            shape((rows, down.shape[2]), BF),
            shape((pairs, 2 * labels), F32),
            shape((labels, hidden), F32),
            shape((labels, units), BF),
            shape((labels, hidden), F32),
            shape((labels, hidden), BF),
            shape((labels, hidden), F32),
            shape((labels, hidden), F32),
            shape((labels, hidden), BF),
        ]
        + ([shape(m, BF) for m in matrices] if slabs else []),
        scratch_shapes=[
            slab_scratch(up),
            slab_scratch(dn),
            pltpu.VMEM((labels, hidden), BF),
            *[pltpu.VMEM(m, BF) for m in matrices],
            *slabs,
            pltpu.SemaphoreType.DMA((7,)),
        ],
        compiler_params=params(),
        name="last_forward",
    )(x, place_col, place_row, seg_wide, down, adapt, bias, *weights, up[0], dn[0], gains, shifts, hbias)


def vocab_body(u_ref, e_ref, et_ref, bias_ref, num_ref, log_ref, scores, weights):
    count = e_ref.shape[0]
    step = split_of(count, 640, 16)
    u = u_ref[...]
    rows = u.shape[0]
    labels = num_ref.shape[2]
    top = jnp.full((1, rows), -jnp.inf, F32)
    for start in range(0, count, step):
        part = slice(start, start + step)
        bias = bias_ref[part, :]
        logits = mm_nt(e_ref[part, :], u) + jnp.concatenate([bias] * (rows // bias.shape[1]), 1)
        scores[part, :] = logits
        top = jnp.maximum(top, jnp.max(logits, 0, keepdims=True))
    total = jnp.zeros((1, rows), F32)
    for start in range(0, count, step):
        part = slice(start, start + step)
        grown = jnp.exp(scores[part, :] - top)
        total = total + jnp.sum(grown, 0, keepdims=True)
        weights[part, :] = grown.astype(BF)
    mean = mm(et_ref[...], weights[...]) * (1.0 / total)
    logs = top + jnp.log(total)
    for k in range(rows // labels):
        num_ref[k, :, :] = mean[:, k * labels : (k + 1) * labels]
        log_ref[k, :, :] = logs[:, k * labels : (k + 1) * labels]


def vocab(u, e, et, bias_wide, labels):
    rows, hidden = u.shape
    count = e.shape[0]
    tile = 2 * labels
    return pl.pallas_call(
        vocab_body,
        grid=(rows // tile,),
        in_specs=[
            pl.BlockSpec((tile, hidden), lambda i: (i, 0)),
            full(e.shape),
            full(et.shape),
            full(bias_wide.shape),
        ],
        out_specs=[
            pl.BlockSpec((2, hidden, labels), lambda i: (i, 0, 0)),
            pl.BlockSpec((2, 1, labels), lambda i: (i, 0, 0)),
        ],
        out_shape=[
            jax.ShapeDtypeStruct((rows // labels, hidden, labels), F32),
            jax.ShapeDtypeStruct((rows // labels, 1, labels), F32),
        ],
        scratch_shapes=[pltpu.VMEM((count, tile), F32), pltpu.VMEM((count, tile), BF)],
        compiler_params=params(),
        name="vocab",
    )(u, e, et, bias_wide)


def last_backward_body(
    own_any, got_any, mean_ref, all_log_ref, code_ref, fact_ref, kv_ref, q_ref, mid_ref, log_ref, one_ref, slope_ref, two_ref,
    low_ref, act_ref, hslope_ref, feat_ref, place_ref, place_row_ref, seg_ref, down_ref, w_ref, adapt_ref, wo_ref,
    up_any, dn_any, gain_ref, hb_ref,
    dx_ref, gh_ref, g_ref, out_fact_ref,
    up_ref, dn_ref, dkv_ref, dq_ref, aims, sems, *, places, edge,
):
    labels = place_ref.shape[0]
    tail = pl.ds(kv_ref.shape[0], labels)
    aimed = [
        pltpu.make_async_copy(source.at[tail, :], aims.at[k], sems.at[2 + k])
        for k, source in enumerate((own_any, got_any))
    ]
    for copy in aimed:
        copy.start()
    copies = []
    for k, (source, target, place) in enumerate(
        ((up_any, up_ref, places[0]), (dn_any, dn_ref, places[1]))
    ):
        rows = target.shape[1]
        copies.append(
            pltpu.make_async_copy(
                source.at[:, pl.ds(place * rows, rows), :], target, sems.at[k]
            )
        )
        copies[-1].start()
    rows = kv_ref.shape[0]
    labels, hidden = feat_ref.shape
    lanes = 2 * (hidden // HEADS)
    width = lanes // 2
    scale = width**-0.5
    for copy in aimed:
        copy.wait()
    mine = code_ref[kv_ref.shape[0] :, :] % 2
    targets = jnp.where(mine > 0, aims[0].astype(F32), aims[1].astype(F32))
    weight = fact_ref[0:1, 0:1]
    chosen = jnp.sum(feat_ref[...].astype(F32) * targets, keepdims=True)
    loss = weight * (jnp.sum(all_log_ref[...] - fact_ref[3:4, :labels], keepdims=True) - chosen)
    out_fact_ref[...] = jnp.where(
        lax.broadcasted_iota(jnp.int32, fact_ref.shape, 0) == 0, loss, fact_ref[...]
    )
    du = weight * (mean_ref[...].T - targets)
    dact = norm_back(act_ref[...], gain_ref[5:6, :], du)
    dz = (hslope_ref[...] * dact).astype(BF)
    dense = mm_tn(low_ref[...], dz)
    if len(gh_ref.shape) == 2:
        gh_ref[...] = dense
    else:
        each = hidden // gh_ref.shape[0]
        spare = jnp.zeros((gh_ref.shape[1] - each, hidden), F32)
        for k in range(gh_ref.shape[0]):
            gh_ref[k] = jnp.concatenate([dense[k * each : (k + 1) * each, :], spare], 0).astype(BF)
    dtwo = norm_back(two_ref[...], gain_ref[4:5, :], mm_nt(dz, hb_ref[...]))
    dtwo_low = dtwo.astype(BF)
    dmiddle = dtwo
    units, step = feed_step(up_ref)
    for copy in copies:
        copy.wait()
    dact = mm_nt(dtwo_low, rows_of(dn_ref, 0, step))
    for start in range(0, units, step):
        part = slice(start, start + step)
        later = mm_nt(dtwo_low, rows_of(dn_ref, start + step, step)) if start + step < units else None
        dgate = (slope_ref[:, part].astype(F32) * dact).astype(BF)
        dmiddle = dmiddle + mm(dgate, rows_of(up_ref, start, step))
        dact = later
    done = norm_back(one_ref[...], gain_ref[3:4, :], dmiddle)
    dctx = mm(done.astype(BF), wo_ref[...]).astype(BF)
    seg = seg_ref[...]
    choose_t = lax.broadcasted_iota(jnp.int32, (rows, labels), 0) == place_row_ref[...]
    same = seg == jnp.sum(jnp.where(choose_t, seg, 0.0), 0, keepdims=True)

    def products(p):
        part = slice(p * lanes, (p + 1) * lanes)
        later = slice(hidden + p * lanes, hidden + (p + 1) * lanes)
        queries = pair_rows(q_ref[:, part].astype(F32) * scale, width)
        outs = pair_rows(dctx[:, part].astype(F32), width)
        return queries, outs, mm_nt(kv_ref[:, part], queries), mm_nt(kv_ref[:, later], outs)

    ahead = products(0)
    for p in range(hidden // lanes):
        part = slice(p * lanes, (p + 1) * lanes)
        later = slice(hidden + p * lanes, hidden + (p + 1) * lanes)
        queries, outs, scores, dweights = ahead
        ahead = products(p + 1) if (p + 1) * lanes < hidden else None
        keys = kv_ref[:, part]
        weights = jnp.exp(masked(scores, same) - log_ref[p : p + 1, :])
        inner = jnp.sum(dweights * weights, 0, keepdims=True)
        dscores = (weights * (dweights - inner)).astype(BF)
        dkv_ref[:, part] = mm(dscores, queries).astype(BF)
        dkv_ref[:, later] = mm(weights.astype(BF), outs).astype(BF)
        dq_ref[:, part] = (pair_join(mm_tn(keys, dscores), width) * scale).T.astype(BF)
    dq = dq_ref[...]
    own_mid = mm(
        (lax.broadcasted_iota(jnp.int32, (labels, rows), 1) == place_ref[...][:, 0:1]).astype(F32).astype(BF),
        mid_ref[...],
    ).astype(BF)
    g_ref[...] = adapter_scale * jnp.where(
        lax.broadcasted_iota(jnp.int32, g_ref.shape, 1) < edge,
        mm_tn(dq, own_mid),
        mm_tn(dkv_ref[:, hidden:], mid_ref[...]),
    )
    dmid_own = mm_nt(dq, adapt_ref[1, :, :hidden]).astype(BF)
    own = done + mm(dq, w_ref[:hidden, :]) + mm_nt(dmid_own, down_ref[1])
    spread = choose_t.astype(F32).astype(BF)
    own_high = own.astype(BF)
    own_rest = (own - own_high.astype(F32)).astype(BF)
    dmid = mm_nt(dkv_ref[:, hidden:], adapt_ref[1, :, 2 * hidden :]).astype(BF)
    step = split_of(hidden, 256, 128)
    for start in range(0, hidden, step):
        part = slice(start, start + step)
        dx_ref[:, part] = (
            mm(dkv_ref[...], w_ref[hidden:, part])
            + mm_nt(dmid, down_ref[1, part, :])
            + mm(spread, own_high[:, part])
            + mm(spread, own_rest[:, part])
        )


def last_backward(
    mean, logs, own, got, code, facts, saved, place_col, place_row, seg_wide, down, w, adapt, wo, up, dn, gains, hb, edge, shards
):
    kv = saved[0]
    rows = kv.shape[0]
    labels, hidden = saved[-1].shape
    whole = pl.BlockSpec(memory_space=pltpu.VMEM)
    anywhere = pl.BlockSpec(memory_space=pl.ANY)
    shape = jax.ShapeDtypeStruct
    return pl.pallas_call(
        functools.partial(last_backward_body, places=(up[1], dn[1]), edge=edge),
        in_specs=[anywhere] * 2 + [whole] * 22 + [anywhere] * 2 + [whole] * 2,
        out_specs=[whole] * 4,
        out_shape=[
            shape((rows, hidden), F32),
            shape((hidden, hidden), F32)
            if shards is None
            else shape((shards, -(-hidden // shards // 16) * 16, hidden), BF),
            shape((hidden, down.shape[2]), F32),
            shape(facts.shape, F32),
        ],
        scratch_shapes=[
            slab_scratch(up),
            slab_scratch(dn),
            pltpu.VMEM(kv.shape, BF),
            pltpu.VMEM((labels, hidden), BF),
            pltpu.VMEM((2, labels, hidden), BF),
            pltpu.SemaphoreType.DMA((4,)),
        ],
        compiler_params=params(),
        name="last_backward",
    )(own, got, mean, logs, code, facts, *saved, place_col, place_row, seg_wide, down, w, adapt, wo, up[0], dn[0], gains, hb)


def after_back_body(dout_ref, one_ref, two_ref, slope_ref, wo_ref, up_ref, down_ref, gain_ref, dctx_ref):
    dtwo = norm_back(two_ref[...], gain_ref[2:3, :], dout_ref[...])
    low = dtwo.astype(BF)
    dmiddle = dtwo
    units, step = feed_step(up_ref)
    dact = mm_nt(low, rows_of(down_ref, 0, step))
    for start in range(0, units, step):
        part = slice(start, start + step)
        later = mm_nt(low, rows_of(down_ref, start + step, step)) if start + step < units else None
        dgate = (slope_ref[:, part].astype(F32) * dact).astype(BF)
        dmiddle = dmiddle + mm(dgate, rows_of(up_ref, start, step))
        dact = later
    done = norm_back(one_ref[...], gain_ref[1:2, :], dmiddle)
    dctx_ref[...] = mm(done.astype(BF), wo_ref[...]).astype(BF)


def after_back(dout, one, two, slope, wo, up, down, norms):
    rows, width = dout.shape
    tile = split_of(rows, 256, 16)
    row = lambda n: pl.BlockSpec((tile, n), lambda i: (i, 0))
    return pl.pallas_call(
        after_back_body,
        grid=(rows // tile,),
        in_specs=[row(width), row(width), row(width), row(slope.shape[1]), full(wo.shape)]
        + [slab_spec(up), slab_spec(down), full(norms.shape)],
        out_specs=row(width),
        out_shape=jax.ShapeDtypeStruct((rows, width), BF),
        compiler_params=params(),
        name="after_back",
    )(dout, one, two, slope, wo, up[0], down[0], norms)


def attend_back_body(
    q_ref, k_ref, v_ref, dctx_ref, log_ref, seg_ref, seg_row_ref, mid_ref, g_ref, dv_ref, *, edge
):
    rows = q_ref.shape[0]
    width = q_ref.shape[1] // 2
    scale = width**-0.5
    dv_ref[...] = jnp.zeros_like(dv_ref)
    gq = jnp.zeros((2 * width, mid_ref.shape[1]), F32)
    turned = turn_blocks(k_ref)

    def products(start):
        own, near = reach_of(start, rows)
        queries = pair_rows(q_ref[own, :].astype(F32) * scale, width)
        outs = pair_rows(dctx_ref[own, :].astype(F32), width)
        return outs, mm_nt(k_ref[near, :], queries), mm_nt(v_ref[near, :], outs)

    now = products(0)
    for start in range(0, rows, REACH):
        own, near = reach_of(start, rows)
        later = products(start + REACH) if start + REACH < rows else None
        outs, scores, dweights = now
        same = seg_ref[near, :] == seg_row_ref[:, own]
        logs = log_ref[0, :, 2 * start : 2 * start + 2 * REACH]
        weights = jnp.exp(masked(scores, same) - logs)
        inner = jnp.sum(dweights * weights, 0, keepdims=True)
        dscores = (weights * (dweights - inner)).astype(BF)
        dv_ref[near, :] += mm(weights.astype(BF), outs)
        dq = (pair_join(mm(turned[:, near], dscores), width) * scale).astype(BF)
        gq = gq + mm(dq, mid_ref[own, :])
        now = later
    gv = mm_tn(dv_ref[...].astype(BF), mid_ref[...])
    g_ref[...] = adapter_scale * jnp.where(
        lax.broadcasted_iota(jnp.int32, gq.shape, 1) < edge, gq, gv
    )


def attend_back(qkv, dctx, logs, seg_wide, seg_row, mid, edge):
    rows, total = qkv.shape
    hidden = total // 3
    lanes = 2 * (hidden // HEADS)
    pairs = hidden // lanes
    column = lambda kind: pl.BlockSpec((rows, lanes), lambda p: (0, kind * pairs + p))
    return pl.pallas_call(
        functools.partial(attend_back_body, edge=edge),
        grid=(pairs,),
        in_specs=[
            column(0),
            column(1),
            column(2),
            column(0),
            pl.BlockSpec((1, 1, 2 * rows), lambda p: (p, 0, 0)),
            full(seg_wide.shape),
            full(seg_row.shape),
            full(mid.shape),
        ],
        out_specs=pl.BlockSpec((lanes, mid.shape[1]), lambda p: (p, 0)),
        out_shape=jax.ShapeDtypeStruct((hidden, mid.shape[1]), F32),
        scratch_shapes=[pltpu.VMEM((rows, lanes), F32)],
        compiler_params=params(),
        name="attend_back",
    )(qkv, qkv, qkv, dctx, logs, seg_wide, seg_row, mid)


MESH = pl.DeviceIdType.MESH


def position():
    dp, fsdp = lax.axis_index("dp"), lax.axis_index("fsdp")
    return {"x": dp, "z": fsdp // 4, "y": (fsdp // 2) % 2, "c": fsdp % 2}


def device_of(place):
    return (place["x"], (place["z"] * 2 + place["y"]) * 2 + place["c"])


def number_of(place):
    return place["x"] * 16 + (place["z"] * 2 + place["y"]) * 2 + place["c"]


def rank_device(number):
    return (number // 16, number % 16)


def greet_all(shards):
    barrier = pltpu.get_barrier_semaphore()
    me = lax.axis_index("dp") * 16 + lax.axis_index("fsdp")

    @pl.loop(1, shards)
    def _(k):
        pl.semaphore_signal(
            barrier, inc=1, device_id=rank_device((me + k) % shards), device_id_type=MESH
        )


def await_all(shards):
    pl.semaphore_wait(pltpu.get_barrier_semaphore(), shards - 1)


def direct_copy(source, target, sems, me, k, shards):
    return pltpu.make_async_remote_copy(
        src_ref=source,
        dst_ref=target,
        send_sem=sems.at[0],
        recv_sem=sems.at[1],
        device_id=rank_device((me + k) % shards),
        device_id_type=MESH,
    )


def spread(piece_of, buffer, sems, me, shards):
    @pl.loop(1, shards)
    def _(k):
        direct_copy(piece_of((me + k) % shards), buffer.at[me], sems, me, k, shards).start()


def collect(buffer, sems, me, shards):
    whole = buffer.at[pl.ds(0, shards - 1)]
    copy = direct_copy(whole, whole, sems, me, 1, shards)
    copy.wait_recv()
    copy.wait_send()


def relative_places(order):
    places = [
        {"x": dx, "z": dz, "y": dy} for dx in (0, 1) for dz in range(-3, 4) for dy in (0, 1)
    ]
    size = lambda p: abs(p["x"]) + abs(p["z"]) + abs(p["y"])
    return sorted(places, key=lambda p: (abs(p[order[-1]]), size(p), [abs(p[a]) for a in order]))


class Gather:
    def __init__(self, chunk, full_buffer, start, rows, order, sends, receives, hands, hands_got):
        self.chunk, self.full, self.order = chunk, full_buffer, order
        self.part = pl.ds(start, rows)
        self.sends, self.receives, self.hands, self.hands_got = sends, receives, hands, hands_got
        self.here = position()
        self.items = relative_places(order)

    def origin(self, item):
        here = self.here
        return {"x": (here["x"] + item["x"]) % 2, "z": here["z"] - item["z"], "y": (here["y"] + item["y"]) % 2, "c": here["c"]}

    def key(self, place):
        return (place["x"] * 4 + place["z"]) * 2 + place["y"]

    def outward(self, item):
        deepest = max([k for k, axis in enumerate(self.order) if item[axis]], default=-1)
        ways = []
        if deepest >= 0 and self.order[deepest] == "z":
            ways.append(("z", 1 if item["z"] > 0 else -1))
        for axis in self.order[deepest + 1 :]:
            ways += [("z", 1), ("z", -1)] if axis == "z" else [(axis, 1)]
        return ways

    def copy(self, index, way, slot, item):
        here = self.here
        place = self.origin(item)
        number, key = number_of(place), self.key(place)
        mine = not any(item.values())
        source = self.chunk.at[self.part, :] if mine else self.full.at[number, self.part, :]
        if way is None:
            target = dict(here, c=1 - here["c"])
            sends, receives = self.hands.at[index], self.hands_got.at[key]
        else:
            axis, step = way
            target = dict(here)
            target[axis] = here["z"] + step if axis == "z" else 1 - here[axis]
            sends, receives = self.sends.at[index * 4 + slot], self.receives.at[key]
        return pltpu.make_async_remote_copy(
            src_ref=source,
            dst_ref=self.full.at[number, self.part, :],
            send_sem=sends,
            recv_sem=receives,
            device_id=device_of(target),
            device_id_type=MESH,
        )

    def valid(self, item):
        z = self.here["z"] - item["z"]
        return (z >= 0) & (z <= 3)

    def step(self, index):
        item = self.items[index]

        @pl.when(self.valid(item))
        def _():
            if any(item.values()):
                self.arrived(index, item)
            for slot, way in enumerate(self.outward(item)):
                self.when_way(way, lambda way=way, slot=slot: self.copy(index, way, slot, item).start())
            self.copy(index, None, 0, item).start()

    def when_way(self, way, act):
        axis, step = way
        if axis == "z":
            z = self.here["z"] + step
            pl.when((z >= 0) & (z <= 3))(act)
        else:
            act()

    def arrived(self, index, item):
        place = self.origin(item)
        spot = self.full.at[number_of(place), self.part, :]
        pltpu.make_async_remote_copy(
            src_ref=spot,
            dst_ref=spot,
            send_sem=self.sends.at[index * 4],
            recv_sem=self.receives.at[self.key(place)],
            device_id=device_of(dict(self.here, c=1 - self.here["c"])),
            device_id_type=MESH,
        ).wait_recv()

    def finish(self):
        for index, item in enumerate(self.items):

            @pl.when(self.valid(item))
            def _(index=index, item=item):
                for slot, way in enumerate(self.outward(item)):
                    self.when_way(way, lambda way=way, slot=slot: self.copy(index, way, slot, item).wait_send())
                self.copy(index, None, 0, item).wait_send()
                place = dict(self.origin(item), c=1 - self.here["c"])
                spot = self.full.at[number_of(place), self.part, :]
                pltpu.make_async_remote_copy(
                    src_ref=spot,
                    dst_ref=spot,
                    send_sem=self.hands.at[index],
                    recv_sem=self.hands_got.at[self.key(place)],
                    device_id=device_of(dict(self.here, c=1 - self.here["c"])),
                    device_id_type=MESH,
                ).wait_recv()


ITEMS = 28


PICK = 64
GROUP = 16


def start_body(
    streams, shards, ids, low_ref, groups_any, fact, chunk, got, own_rows, facts, full_chunk,
    table, stage, rows,
    row_sends, row_gets, fact_sems, own_sems, sends, receives, hands, hands_got,
):
    here = position()
    me = number_of(here)
    across = device_of(dict(here, x=1 - here["x"]))
    half, hidden = own_rows.shape
    batches = half // PICK
    fill = pltpu.make_async_copy(groups_any, table, own_sems.at[0])
    fill.start()
    greet_all(shards)
    own = [
        pltpu.make_async_copy(source, target, own_sems.at[1 + k])
        for k, (source, target) in enumerate(((fact, facts.at[me]), (chunk, full_chunk.at[me])))
    ]
    for copy in own:
        copy.start()
    await_all(shards)
    gathers = [
        Gather(
            chunk, full_chunk, start, size, order, sends.at[k], receives.at[k], hands.at[k], hands_got.at[k]
        )
        for k, (start, size, order) in enumerate(streams)
    ]
    for gather in gathers:
        gather.step(0)
    spread(lambda peer: fact, facts, fact_sems, me, shards)

    def send_rows(b):
        part = pl.ds(b * PICK, PICK)
        return pltpu.make_async_remote_copy(
            src_ref=rows.at[part, :],
            dst_ref=got.at[part, :],
            send_sem=row_sends.at[b],
            recv_sem=row_gets.at[b],
            device_id=across,
            device_id_type=MESH,
        )

    def pick(b):
        @pl.loop(0, PICK // 8)
        def _(t):
            found = [table[ids[b * PICK + t * 8 + k]] for k in range(8)]
            stage[pl.ds(pl.multiple_of(t * 8, 8), 8)] = jnp.stack(found)

        choose = (
            lax.broadcasted_iota(jnp.int32, (PICK, PICK * GROUP), 1)
            == low_ref[b * PICK : (b + 1) * PICK, :]
        )
        rows[b * PICK : (b + 1) * PICK, :] = mm(choose.astype(F32).astype(BF), flat(stage)).astype(BF)
        if b < batches:
            send_rows(b).start()

    fill.wait()
    picked = 0
    for index in range(1, ITEMS):
        while picked < min(2 * batches, 6 + 4 * index):
            pick(picked)
            picked += 1
        for gather in gathers:
            gather.step(index)
    outs = [pltpu.make_async_copy(rows.at[pl.ds(half, half), :], own_rows, own_sems.at[3])]
    for copy in outs:
        copy.start()
    for gather in gathers:
        gather.finish()
    collect(facts, fact_sems, me, shards)
    for b in range(batches):
        send_rows(b).wait()
    for copy in own + outs:
        copy.wait()


def vocab_rows(table, like):
    here = position()
    count = like.shape[0]
    return table.at[pl.ds(pl.multiple_of((here["y"] * 2 + here["c"]) * count, 16), count), :]


def gather_sems(streams):
    sems = pltpu.SemaphoreType.DMA
    count = len(streams)
    return [sems((count, 4 * ITEMS)), sems((count, 16)), sems((count, ITEMS)), sems((count, 16))]


def streams_of(rows, parts):
    streams, start = [], 0
    for k, (order, share) in enumerate(parts):
        size = rows - start if k == len(parts) - 1 else round(rows * share / 16) * 16
        streams.append((start, size, order))
        start += size
    return streams


def start_exchange(ids, table, fact, chunk, shards):
    anywhere = pl.BlockSpec(memory_space=pl.ANY)
    shape = jax.ShapeDtypeStruct
    sems = pltpu.SemaphoreType.DMA
    streams = streams_of(chunk.shape[0], (("xzy", 0.5), ("zxy", 0.28), ("xyz", 0.22)))
    half, hidden = ids.shape[0] // 2, table.shape[1]
    low = jnp.arange(ids.size, dtype=jnp.int32) % PICK * GROUP + ids % GROUP
    return pl.pallas_call(
        functools.partial(start_body, streams, shards),
        in_specs=[
            pl.BlockSpec(memory_space=pltpu.SMEM),
            pl.BlockSpec(memory_space=pltpu.VMEM),
        ]
        + [anywhere] * 3,
        out_specs=[anywhere] * 4,
        out_shape=[
            shape((half, hidden), table.dtype),
            shape((half, hidden), table.dtype),
            shape((shards, *fact.shape), fact.dtype),
            shape((shards, *chunk.shape), chunk.dtype),
        ],
        scratch_shapes=[
            pltpu.VMEM((table.shape[0] // GROUP, GROUP, hidden), BF),
            pltpu.VMEM((PICK, GROUP, hidden), BF),
            pltpu.VMEM((2 * half, hidden), BF),
            sems((half // PICK,)),
            sems((half // PICK,)),
            sems((2,)),
            sems((4,)),
            *gather_sems(streams),
        ],
        compiler_params=params(collective_id=1, has_side_effects=True),
        name="start_exchange",
    )(ids // GROUP, low[:, None], table.reshape(-1, GROUP, hidden), fact, chunk)


def first_layer_body(
    streams, shards,
    own_any, got_any, first_any, other_any, chunk, table_any, code_ref, spots_ref, gain_ref, shift_ref, down_ref,
    adapt_ref, bias_ref, seg_ref, seg_row_ref,
    qkv_out, x_out, one_out, two_out, slope_out, wo_out, full_chunk, et_out, mid_ref, log_ref,
    own, got, in_slab, w, wo, up, dn, x, qkv, ctx, two, out, slope,
    e_in, et_stage, load_sems, tile_sems, out_sems, e_sems, et_sems, sends, receives, hands, hands_got,
):
    here = position()
    me = number_of(here)
    rows, hidden = x.shape
    tile = split_of(rows, 256, 16)
    tiles = rows // tile
    lanes = 2 * (hidden // HEADS)
    pairs = hidden // lanes

    rest = first_any.shape[1] - up.shape[1]
    cut = dn.shape[1] - rest

    def slab(source, target, start):
        return source.at[:, pl.ds(start, target.shape[1]), :]

    loads = [
        pltpu.make_async_copy(source, target, load_sems.at[k])
        for k, (source, target) in enumerate(
            (
                (own_any.at[pl.ds(0, rows), :], own),
                (got_any.at[pl.ds(0, rows), :], got),
                (slab(other_any, in_slab, cut), in_slab),
                (slab(first_any, up, 0), up),
                (other_any.at[:, pl.ds(0, cut), :], dn.at[:, pl.ds(0, cut), :]),
                (first_any.at[:, pl.ds(up.shape[1], rest), :], dn.at[:, pl.ds(cut, rest), :]),
                (chunk, full_chunk.at[me]),
            )
        )
    ]
    for copy in loads:
        copy.start()
    barrier = pltpu.get_barrier_semaphore()
    peers = [
        dict(here, c=1 - here["c"]),
        dict(here, x=1 - here["x"]),
        dict(here, y=1 - here["y"]),
        *[dict(here, z=flip(here["z"], k)) for k in (1, 2, 3)],
    ]
    for peer in peers:
        pl.semaphore_signal(barrier, inc=1, device_id=device_of(peer), device_id_type=MESH)
    pl.semaphore_wait(barrier, len(peers))
    gathers = [
        Gather(
            chunk, full_chunk, start, size, order, sends.at[k], receives.at[k], hands.at[k], hands_got.at[k]
        )
        for k, (start, size, order) in enumerate(streams)
    ]
    def advance(first, last):
        for index in range(first, last + 1):
            for gather in gathers:
                gather.step(index)

    def at(i, plan):
        for k, ends in plan.items():
            pl.when(i == k)(functools.partial(advance, *ends))

    advance(0, 0)

    groups = pairs + tiles
    size = e_in.shape[1]
    here_rows = (here["y"] * 2 + here["c"]) * (groups * size)
    unit = (
        (lax.broadcasted_iota(jnp.int32, (256, 256), 0) == lax.broadcasted_iota(jnp.int32, (256, 256), 1))
        .astype(F32)
        .astype(BF)
    )

    def group_in(g):
        source = table_any.at[pl.ds(pl.multiple_of(here_rows + g * size, 16), size), :]
        return pltpu.make_async_copy(source, e_in.at[g % 2], e_sems.at[g])

    def group_out(g):
        target = et_out.at[:, pl.ds(pl.multiple_of(g * size, 128), size)]
        return pltpu.make_async_copy(et_stage.at[g % 2], target, et_sems.at[g])

    def turn_group(g):
        group_in(g).wait()

        @pl.when(g >= 2)
        def _():
            group_out(g - 2).wait()

        for k in range(0, hidden, 256):
            et_stage[g % 2, k : k + 256, :] = mm_nt(unit, e_in[g % 2, :, k : k + 256]).astype(BF)
        group_out(g).start()

        @pl.when(g + 2 < groups)
        def _():
            group_in(g + 2).start()

    group_in(0).start()
    group_in(1).start()
    for copy in loads[:3]:
        copy.wait()
    unpack_rows(in_slab, (w, wo))

    @pl.loop(0, tiles)
    def _(i):
        part = pl.ds(pl.multiple_of(i * tile, tile), tile)
        project_body(
            own.at[part, :], got.at[part, :], code_ref.at[part, :], spots_ref, gain_ref, shift_ref, down_ref, w,
            adapt_ref, bias_ref, qkv.at[part, :], mid_ref.at[part, :], x.at[part, :],
        )

        at(i, {tiles - 3: (1, 3), tiles - 1: (4, 5)})

    early = [
        pltpu.make_async_copy(qkv, qkv_out, out_sems.at[0]),
        pltpu.make_async_copy(wo, wo_out, out_sems.at[1]),
    ]
    for copy in early:
        copy.start()

    @pl.loop(0, pairs)
    def _(p):
        column = lambda kind: pl.ds(pl.multiple_of((kind * pairs + p) * lanes, lanes), lanes)
        attend_body(
            qkv.at[:, column(0)], qkv.at[:, column(1)], qkv.at[:, column(2)], seg_ref, seg_row_ref,
            ctx.at[:, column(0)], log_ref.at[pl.ds(p, 1)],
        )

        turn_group(p)
        at(p - (pairs - 6), {1: (6, 7), 3: (8, 9), 5: (10, 13)})

    for copy in loads[3:6]:
        copy.wait()

    def tile_copies(i):
        part = pl.ds(pl.multiple_of(i * tile, tile), tile)
        turn = i % 2
        return [
            pltpu.make_async_copy(source, target.at[part, :], tile_sems.at[k, i])
            for k, (source, target) in enumerate(
                (
                    (out.at[turn], x_out),
                    (two.at[turn], two_out),
                    (slope.at[turn], slope_out),
                    (x.at[part, :], one_out),
                )
            )
        ]

    plan = {0: (14, 16), 1: (17, 19), 2: (20, 23), 3: (24, 27)}

    @pl.loop(0, tiles)
    def _(i):
        part = pl.ds(pl.multiple_of(i * tile, tile), tile)
        turn = i % 2

        @pl.when(i >= 2)
        def _():
            for copy in tile_copies(i - 2):
                copy.wait()

        after_body(
            ctx.at[part, :], x.at[part, :], wo, up, dn, bias_ref, gain_ref, shift_ref, out.at[turn],
            x.at[part, :], two.at[turn], slope.at[turn],
        )
        for copy in tile_copies(i):
            copy.start()
        turn_group(pairs + i)
        at(i - (tiles - 4), plan)

    for gather in gathers:
        gather.finish()
    for i in (tiles - 2, tiles - 1):
        for copy in tile_copies(i):
            copy.wait()
    for copy in early + loads[6:] + [group_out(g) for g in (groups - 2, groups - 1)]:
        copy.wait()


def first_layer(own, got, first, other, chunk, table, more, shards):
    whole = pl.BlockSpec(memory_space=pltpu.VMEM)
    anywhere = pl.BlockSpec(memory_space=pl.ANY)
    down, seg_row = more[4], more[-1]
    rows, hidden = seg_row.shape[1], own.shape[1]
    tile = split_of(rows, 256, 16)
    pairs = HEADS // 2
    units = 4 * hidden
    each = units // shards
    count, groups = table.shape[0] // 4, pairs + rows // tile
    shape = jax.ShapeDtypeStruct
    sems = pltpu.SemaphoreType.DMA
    streams = streams_of(chunk.shape[0], (("zxy", 0.4), ("zyx", 0.4), ("xyz", 0.2)))
    return pl.pallas_call(
        functools.partial(first_layer_body, streams, shards),
        in_specs=[anywhere] * 6 + [whole] * len(more),
        out_specs=[anywhere] * 8 + [whole] * 2,
        out_shape=[
            shape((rows, 3 * hidden), BF),
            shape((rows, hidden), F32),
            shape((rows, hidden), F32),
            shape((rows, hidden), F32),
            shape((rows, units), BF),
            shape((hidden, hidden), BF),
            shape((shards, *chunk.shape), BF),
            shape((hidden, count), BF),
            shape((rows, down.shape[2]), BF),
            shape((pairs, 1, 2 * rows), F32),
        ],
        scratch_shapes=[
            pltpu.VMEM((rows, hidden), BF),
            pltpu.VMEM((rows, hidden), BF),
            pltpu.VMEM((shards, 4 * hidden // shards, hidden), BF),
            pltpu.VMEM((3 * hidden, hidden), BF),
            pltpu.VMEM((hidden, hidden), BF),
            pltpu.VMEM((shards, each, hidden), BF),
            pltpu.VMEM((shards, each, hidden), BF),
            pltpu.VMEM((rows, hidden), F32),
            pltpu.VMEM((rows, 3 * hidden), BF),
            pltpu.VMEM((rows, hidden), BF),
            pltpu.VMEM((2, tile, hidden), F32),
            pltpu.VMEM((2, tile, hidden), F32),
            pltpu.VMEM((2, tile, units), BF),
            pltpu.VMEM((2, count // groups, hidden), BF),
            pltpu.VMEM((2, hidden, count // groups), BF),
            sems((7,)),
            sems((4, rows // tile)),
            sems((2,)),
            sems((groups,)),
            sems((groups,)),
            *gather_sems(streams),
        ],
        compiler_params=params(collective_id=3, has_side_effects=True),
        name="first_layer",
    )(own, got, first, other, chunk, table, *more)


def adam(weight, gradient, moment_one, moment_two, fade_one, fade_two):
    moment_one = beta_first * moment_one + (1.0 - beta_first) * gradient
    moment_two = beta_second * moment_two + (1.0 - beta_second) * gradient * gradient
    one_hat = moment_one / fade_one
    two_hat = moment_two / fade_two
    weight = weight - learn_rate * (one_hat / (jnp.sqrt(two_hat) + adam_eps) + decay_rate * weight)
    return (weight, moment_one, moment_two)


BACK_TILE = 256


def finish_body(
    shards, edge,
    dout_any, one_any, two_any, slope_any, wo_any, first_any, other_any, qkv_any, gain_ref, log_ref, seg_ref,
    seg_row_ref, mid_ref, parts, late_ref, facts,
    sums_ref, dense_ref, total_ref,
    dout, one, two, slope, wo, up, dn, qkv, dctx, dv, grad, core_got, chip_sum, dense_got, grad_got, note, notes,
    tile_sems, load_sems, core_sems, dense_sems, grad_sems, note_sems,
):
    rows, hidden = dout.shape
    tile = split_of(rows, BACK_TILE, 16)
    tiles = rows // tile
    me = number_of(position())

    def tile_loads(i):
        part = pl.ds(pl.multiple_of(i * tile, tile), tile)
        return [
            pltpu.make_async_copy(source.at[part, :], target.at[part, :], tile_sems.at[k, i])
            for k, (source, target) in enumerate(
                ((two_any, two), (dout_any, dout), (slope_any, slope), (one_any, one))
            )
        ]

    here = position()
    rest = first_any.shape[1] - up.shape[1]
    cut = dn.shape[1] - rest
    chips = shards // 2
    chip, core = me // 2, here["c"]
    to_core = pltpu.make_async_remote_copy(
        src_ref=parts.at[:, 1 - core],
        dst_ref=core_got,
        send_sem=core_sems.at[0],
        recv_sem=core_sems.at[1],
        device_id=device_of(dict(here, c=1 - core)),
        device_id_type=MESH,
    )

    def to_chip(k):
        peer = (chip + k) % chips
        return pltpu.make_async_remote_copy(
            src_ref=chip_sum.at[peer],
            dst_ref=dense_got.at[chip],
            send_sem=dense_sems.at[0],
            recv_sem=dense_sems.at[1],
            device_id=rank_device(2 * peer + core),
            device_id_type=MESH,
        )

    loads = [
        pltpu.make_async_copy(source, target, load_sems.at[k])
        for k, (source, target) in enumerate(
            (
                (other_any.at[:, pl.ds(0, cut), :], dn.at[:, pl.ds(0, cut), :]),
                (first_any.at[:, pl.ds(up.shape[1], rest), :], dn.at[:, pl.ds(cut, rest), :]),
                (first_any.at[:, pl.ds(0, up.shape[1]), :], up),
                (wo_any, wo),
                (qkv_any, qkv),
            )
        )
    ]
    for copy in tile_loads(0) + loads[:4]:
        copy.start()
    for i in range(1, tiles):
        for copy in tile_loads(i):
            copy.start()
    loads[4].start()
    greet_all(shards)
    for copy in loads[:4]:
        copy.wait()

    @pl.loop(0, tiles)
    def _(i):
        for copy in tile_loads(i):
            copy.wait()
        part = pl.ds(pl.multiple_of(i * tile, tile), tile)
        after_back_body(
            dout.at[part, :], one.at[part, :], two.at[part, :], slope.at[part, :], wo, up, dn, gain_ref,
            dctx.at[part, :],
        )

        @pl.when(i == 0)
        def _():
            await_all(shards)
            to_core.start()

        @pl.when(i == 1)
        def _():
            to_core.wait_recv()

            @pl.loop(0, chips)
            def _(k):
                chip_sum[k] = (parts[k, core].astype(F32) + core_got[k].astype(F32)).astype(BF)

            dense_got[chip] = chip_sum[chip]

            @pl.loop(1, chips)
            def _(k):
                to_chip(k).start()

    loads[4].wait()
    lanes = 2 * (hidden // HEADS)
    pairs = hidden // lanes

    @pl.loop(0, pairs)
    def _(p):
        column = lambda kind: pl.ds(pl.multiple_of((kind * pairs + p) * lanes, lanes), lanes)
        attend_back_body(
            qkv.at[:, column(0)], qkv.at[:, column(1)], qkv.at[:, column(2)], dctx.at[:, column(0)],
            log_ref.at[pl.ds(p, 1)], seg_ref, seg_row_ref, mid_ref, grad.at[column(0), :], dv, edge=edge,
        )

    grad[...] = grad[...] + late_ref[...]
    each = hidden // shards
    piece = lambda peer: grad.at[pl.ds(pl.multiple_of(peer * each, each), each), :]
    grad_got[me] = piece(me)[...]
    spread(piece, grad_got, grad_sems, me, shards)
    others = chip_sum.at[pl.ds(0, chips - 1)]
    every = pltpu.make_async_remote_copy(
        src_ref=others,
        dst_ref=dense_got.at[pl.ds(0, chips - 1)],
        send_sem=dense_sems.at[0],
        recv_sem=dense_sems.at[1],
        device_id=device_of(dict(here, c=1 - core)),
        device_id_type=MESH,
    )
    every.wait_recv()
    every.wait_send()
    to_core.wait_send()
    dense = jnp.zeros((each, hidden), F32)
    for k in range(chips):
        dense = dense + dense_got[k].astype(F32)[:each, :]
    dense_ref[...] = dense
    square = jnp.sum(dense * dense, keepdims=True)
    collect(grad_got, grad_sems, me, shards)
    total = grad_got[0]
    for k in range(1, shards):
        total = total + grad_got[k]
    total_ref[...] = total
    square = square + jnp.sum(total * total, keepdims=True)
    row = lax.broadcasted_iota(jnp.int32, note.shape, 0)
    note[...] = jnp.where(row == 0, facts[...], jnp.where(row == 1, square, 0.0))
    notes[me] = note[...]
    spread(lambda peer: note, notes, note_sems, me, shards)
    collect(notes, note_sems, me, shards)
    sums = notes[0]
    for k in range(1, shards):
        sums = sums + notes[k]
    sums_ref[...] = sums


def update_body(
    sums_ref, dense_ref, total_ref, facts, head_w, head_m, head_v, adapt_w, adapt_m, adapt_v,
    loss_out, norm_out, head_w_out, head_m_out, head_v_out, adapt_w_out, adapt_m_out, adapt_v_out,
):
    norm = jnp.sqrt(sums_ref[1:2, 0:1])
    loss_out[...] = sums_ref[0:1, 0:1]
    norm_out[...] = norm
    factor = jnp.minimum(1.0, clip_limit / (norm + 1e-06))
    fades = facts[1:2, 0:1], facts[2:3, 0:1]
    new = adam(head_w[...], dense_ref[...] * factor, head_m[...], head_v[...], *fades)
    head_w_out[...], head_m_out[...], head_v_out[...] = new
    grad = (total_ref[...] * factor).T
    layers, kinds, rank, unused = adapt_w.shape
    for layer in range(layers):
        for kind in range(kinds):
            at = (layer * kinds + kind) * rank
            new = adam(
                adapt_w[layer, kind], grad[at : at + rank], adapt_m[layer, kind], adapt_v[layer, kind], *fades
            )
            adapt_w_out[layer, kind], adapt_m_out[layer, kind], adapt_v_out[layer, kind] = new


def update(sums, dense, total, facts, heads, adapts):
    whole = pl.BlockSpec(memory_space=pltpu.VMEM)
    shape = jax.ShapeDtypeStruct
    return pl.pallas_call(
        update_body,
        in_specs=[whole] * 10,
        out_specs=[whole] * 8,
        out_shape=[shape((1, 1), F32)] * 2 + [shape(a.shape, F32) for a in (*heads, *adapts)],
        compiler_params=params(),
        name="update",
    )(sums, dense, total, facts, *heads, *adapts)


def finish(back, qkv, logs, seg_wide, seg_row, mid, parts, late, facts, edge, shards):
    dout, one, two, slope, wo, first, other, gains = back
    slab = pltpu.VMEM((shards, slope.shape[1] // shards, dout.shape[1]), BF)
    parts = parts.reshape(-1, 2, *parts.shape[1:])
    rows, hidden = dout.shape
    each = hidden // shards
    whole = pl.BlockSpec(memory_space=pltpu.VMEM)
    anywhere = pl.BlockSpec(memory_space=pl.ANY)
    shape = jax.ShapeDtypeStruct
    sems = pltpu.SemaphoreType.DMA
    tiles = rows // split_of(rows, BACK_TILE, 16)
    return pl.pallas_call(
        functools.partial(finish_body, shards, edge),
        in_specs=[anywhere] * 8 + [whole] * 8,
        out_specs=[whole] * 3,
        out_shape=[
            shape((8, 128), F32),
            shape((each, hidden), F32),
            shape((each, late.shape[1]), F32),
        ],
        scratch_shapes=[
            pltpu.VMEM((rows, hidden), F32),
            pltpu.VMEM((rows, hidden), F32),
            pltpu.VMEM((rows, hidden), F32),
            pltpu.VMEM(slope.shape, BF),
            pltpu.VMEM(wo.shape, BF),
            slab,
            slab,
            pltpu.VMEM(qkv.shape, BF),
            pltpu.VMEM((rows, hidden), BF),
            pltpu.VMEM((rows, 2 * (hidden // HEADS)), F32),
            pltpu.VMEM(late.shape, F32),
            pltpu.VMEM((shards // 2, *parts.shape[2:]), BF),
            pltpu.VMEM((shards // 2, *parts.shape[2:]), BF),
            pltpu.VMEM((shards // 2, *parts.shape[2:]), BF),
            pltpu.VMEM((shards, each, late.shape[1]), F32),
            pltpu.VMEM((8, 128), F32),
            pltpu.VMEM((shards, 8, 128), F32),
            sems((4, tiles)),
            sems((5,)),
            sems((2,)),
            sems((2,)),
            sems((2,)),
            sems((2,)),
        ],
        compiler_params=params(collective_id=2, has_side_effects=True),
        name="finish",
    )(dout, one, two, slope, wo, first, other, qkv, gains, logs, seg_wide, seg_row, mid, parts, late, facts)


LOG_ROWS = 16


def flip(z, k):
    return (z % 2 + k % 2) % 2 + 2 * ((z // 2 + k // 2) % 2)


def pack_log(log_row, rows):
    high = log_row.astype(BF).astype(F32)
    middle = (log_row - high).astype(BF).astype(F32)
    low = log_row - high - middle
    row = lax.broadcasted_iota(jnp.int32, (rows, log_row.shape[1]), 0)
    return jnp.where(
        row == 0, high, jnp.where(row == 1, middle, jnp.where(row == 2, low, 0.0))
    ).astype(BF)


def unpack(block, hidden):
    logs = block[hidden : hidden + LOG_ROWS, :].astype(F32)
    return block[:hidden, :].astype(F32), jnp.sum(logs, 0, keepdims=True)


def merged(one, two):
    top = jnp.maximum(one[1], two[1])
    first, second = jnp.exp(one[1] - top), jnp.exp(two[1] - top)
    total = first + second
    inverse = 1.0 / total
    return one[0] * (first * inverse) + two[0] * (second * inverse), top + jnp.log(total)


def store_packed(ref, pair, hidden):
    ref[:hidden, :] = pair[0].astype(BF)
    ref[hidden : hidden + LOG_ROWS, :] = pack_log(pair[1], LOG_ROWS)


def head_body(
    u_ref, bias_ref, table_any, et_any, mean_ref, log_ref,
    e_ref, et_ref, bias_wide, feats, packs, handed, sums,
    loads, far_send, far_get, hand_send, hand_get, part_send, part_get, sum_send, sum_get,
):
    here = position()
    x, y, c = here["x"], here["y"], here["c"]
    labels, hidden = u_ref.shape
    sibling = device_of(dict(here, c=1 - c))

    def chip_at(k):
        return (x + k % 2) % 2, (y + k // 2) % 2

    def device_at(k):
        there = chip_at(k)
        return device_of(dict(here, x=there[0], y=there[1]))

    def slot(k, core):
        there = chip_at(k)
        return (there[0] * 2 + there[1]) * 2 + core

    fills = [
        pltpu.make_async_copy(source, target, loads.at[k])
        for k, (source, target) in enumerate(
            ((vocab_rows(table_any, e_ref), e_ref), (et_any, et_ref))
        )
    ]
    for fill in fills:
        fill.start()
    barrier = pltpu.get_barrier_semaphore()
    for target in (sibling, *[device_at(k) for k in (1, 2, 3)]):
        pl.semaphore_signal(barrier, inc=1, device_id=target, device_id_type=MESH)
    feats[slot(0, c)] = u_ref[...]
    pl.semaphore_wait(barrier, 4)

    def move(place, device, send, get):
        return pltpu.make_async_remote_copy(
            src_ref=feats.at[place],
            dst_ref=feats.at[place],
            send_sem=send,
            recv_sem=get,
            device_id=device,
            device_id_type=MESH,
        )

    def far(k):
        return move(slot(0, c), device_at(k), far_send.at[k], far_get.at[k])

    def far_here(k):
        return move(slot(k, c), device_at(k), far_send.at[k], far_get.at[k])

    def hand(k, core):
        return move(slot(k, core), sibling, hand_send.at[k], hand_get.at[k])

    for k in (1, 2, 3):
        far(k).start()
    hand(0, c).start()

    @pl.loop(0, bias_ref.shape[0])
    def _(b):
        row = jnp.broadcast_to(bias_ref[pl.ds(b, 1), :], (128, 128))
        bias_wide[pl.ds(pl.multiple_of(b * 128, 128), 128), :] = row.T

    for k in (1, 2, 3):
        far_here(k).wait_recv()
        hand(k, c).start()
    for fill in fills:
        fill.wait()
    count = e_ref.shape[0]
    steps = 4

    def target_of(s):
        return (s + 1) % steps

    def hand_part(s):
        return pltpu.make_async_remote_copy(
            src_ref=packs.at[s, 1 - c],
            dst_ref=handed.at[s],
            send_sem=part_send.at[s],
            recv_sem=part_get.at[s],
            device_id=sibling,
            device_id_type=MESH,
        )

    def sum_part(s):
        return pltpu.make_async_remote_copy(
            src_ref=packs.at[s, c],
            dst_ref=sums.at[s],
            send_sem=sum_send.at[s],
            recv_sem=sum_get.at[s],
            device_id=device_at(target_of(s)),
            device_id_type=MESH,
        )

    def together(s):
        hand_part(s).wait_recv()
        return merged(unpack(packs[s, c], hidden), unpack(handed[s], hidden))

    def settle(s):
        store_packed(packs.at[s, c], together(s), hidden)
        sum_part(s).start()

    @pl.loop(0, steps)
    def _(s):
        k = target_of(s)
        hand(k, 1 - c).wait_recv()
        u = feats[pl.ds(slot(k, 0), 2)].reshape(2 * labels, hidden)
        top = total = mean = None

        def scored(start):
            part = slice(start, min(start + 1280, count))
            bias = bias_wide[part, :]
            return mm_nt(e_ref[part, :], u) + jnp.concatenate([bias, bias], 1)

        @pl.when(s > 0)
        def _():
            settle(s - 1)

        logits = scored(0)
        for start in range(0, count, 1280):
            part = slice(start, min(start + 1280, count))
            later = scored(start + 1280) if start + 1280 < count else None
            high = jnp.max(logits, 0, keepdims=True)
            new = high if top is None else jnp.maximum(top, high)
            grown = jnp.exp(logits - new)
            part_sums = jnp.sum(grown, 0, keepdims=True)
            product = mm(et_ref[:, part], grown.astype(BF))
            if top is None:
                total, mean = part_sums, product
            else:
                shrink = jnp.exp(top - new)
                total, mean = total * shrink + part_sums, mean * shrink + product
            top = new
            logits = later
        mean = mean * (1.0 / total)
        logs = top + jnp.log(total)
        for core in range(2):
            half = slice(core * labels, (core + 1) * labels)
            packs[s, core, :hidden, :] = mean[:, half].astype(BF)
            packs[s, core, hidden : hidden + LOG_ROWS, :] = pack_log(logs[:, half], LOG_ROWS)
        hand_part(s).start()

    total = together(steps - 1)
    for s in range(steps - 1):
        sum_part(s).wait_recv()
        total = merged(total, unpack(sums[s], hidden))
    mean_ref[...] = total[0]
    log_ref[...] = total[1]
    for k in (1, 2, 3):
        far(k).wait_send()
    for k in range(4):
        hand(k, c).wait_send()
    for s in range(steps):
        hand_part(s).wait_send()
    for s in range(steps - 1):
        sum_part(s).wait_send()


def head(u, bias, table, et):
    labels, hidden = u.shape
    whole = pl.BlockSpec(memory_space=pltpu.VMEM)
    anywhere = pl.BlockSpec(memory_space=pl.ANY)
    shape = jax.ShapeDtypeStruct
    sems = pltpu.SemaphoreType.DMA
    block = (hidden + LOG_ROWS, labels)
    count = et.shape[1]
    return pl.pallas_call(
        head_body,
        in_specs=[whole] * 2 + [anywhere] * 2,
        out_specs=[whole] * 2,
        out_shape=[shape((hidden, labels), F32), shape((1, labels), F32)],
        scratch_shapes=[
            pltpu.VMEM((count, hidden), BF),
            pltpu.VMEM((hidden, count), BF),
            pltpu.VMEM((count, 128), F32),
            pltpu.VMEM((8, labels, hidden), BF),
            pltpu.VMEM((4, 2, *block), BF),
            pltpu.VMEM((4, *block), BF),
            pltpu.VMEM((4, *block), BF),
            sems((2,)),
        ]
        + [sems((4,))] * 8,
        compiler_params=params(collective_id=4, has_side_effects=True),
        name="head",
    )(u, bias, table, et)


def seg_positions(segments):
    index = jnp.arange(segments.shape[-1], dtype=jnp.int32)
    fresh = jnp.concatenate([jnp.ones((1,), dtype=bool), segments[1:] != segments[:-1]], -1)
    starts = lax.cummax(jnp.where(fresh, index, jnp.zeros_like(index)), axis=0)
    return index - starts


def pad_rows(matrix, multiple):
    return jnp.pad(matrix, ((0, -matrix.shape[0] % multiple), (0, 0)))


def slab_of(gathered, start, rows):
    if rows % 16 == 0 and start % rows == 0:
        return (gathered, start // rows, rows)
    part = gathered[:, start : start + rows].reshape(1, -1, gathered.shape[2])
    return (part, 0, part.shape[1])


def per_device(
    input_token_index,
    sentence_numbers,
    label_positions,
    label_target_token,
    sequence_task_index,
    task_loss_weight,
    optimizer_step_count,
    embed,
    position_embedding,
    norm_gain_vector,
    norm_bias_vector,
    attention_in_weight,
    attention_out_weight,
    feedforward_up,
    feedforward_down,
    layer_bias_vector,
    head_dense_bias,
    vocabulary_bias,
    adapter_down_matrix,
    adapter_up_matrix,
    adapter_moment_first,
    adapter_moment_second,
    head_projection,
    head_moment_first,
    head_moment_second,
):
    shards = lax.axis_size("dp") * lax.axis_size("fsdp")
    dp_index = lax.axis_index("dp")
    fsdp_index = lax.axis_index("fsdp")
    layers, unused, rank, up_part = adapter_up_matrix.shape
    hidden = embed.shape[1]
    tokens = input_token_index.shape[1]
    labels = label_positions.shape[1]
    qkv_rows = attention_in_weight.shape[2]
    out_rows = attention_out_weight.shape[2]
    ff_rows = feedforward_up.shape[2]
    head_rows = head_projection.shape[0]

    grouped = (lax.axis_size("dp"), lax.axis_size("fsdp")) == (2, 16)
    feeds = [[feedforward_up[layer].T, feedforward_down[layer]] for layer in range(layers)]
    attends = [[attention_in_weight[layer].T, attention_out_weight[layer].T] for layer in range(layers)]
    cut = ff_rows // 32 * 16
    first_chunk = jnp.concatenate([feeds[0][0], feeds[0][1][cut:]], 0)
    other_full = lax.all_gather(
        jnp.concatenate([feeds[0][1][:cut], *attends[0]], 0), BOTH, axis=0, tiled=False
    )
    last_chunk = pad_rows(
        jnp.concatenate([feeds[1][0], *attends[1], head_projection.astype(BF)], 0), 32
    )
    last_feed = feeds[1][1]

    table_rows = embed.shape[0]
    wanted = jnp.concatenate([input_token_index[0], label_target_token[0]])
    dp_count = lax.axis_size("dp")
    group_ids = lax.all_gather(wanted, "dp", axis=0, tiled=False) - dp_index * table_rows
    inside = (group_ids >= 0) & (group_ids < table_rows)
    group_ids = jnp.clip(group_ids, 0, table_rows - 1)
    mine = lax.dynamic_index_in_dim(inside, dp_index, 0, keepdims=False)

    task_range = jnp.arange(TASKS, dtype=jnp.int32)
    slice_rows = vocabulary_bias.shape[0]
    ups = adapter_up_matrix.reshape(-1)
    if grouped:
        pair_ids = jnp.concatenate(
            [
                lax.dynamic_index_in_dim(group_ids, (dp_index + shift) % 2, 0, keepdims=False)
                for shift in (1, 0)
            ]
        )
        fact = jnp.concatenate([vocabulary_bias, ups, sequence_task_index.astype(F32)])
        fact_rows = -(-fact.size // 1024) * 8
        got, own_rows, facts, first_full = start_exchange(
            pair_ids,
            embed,
            jnp.pad(fact, (0, fact_rows * 128 - fact.size)).reshape(fact_rows, 128),
            first_chunk,
            shards,
        )
        facts, last_feed = lax.optimization_barrier((facts, last_feed))
        facts = facts.reshape(shards, -1)
        all_bias = facts[:, :slice_rows].reshape(-1)
        every_up = facts[:, slice_rows : slice_rows + ups.size]
        every_task = facts[:, slice_rows + ups.size].astype(jnp.int32)
    else:
        looked = jnp.where(
            inside.reshape(-1)[:, None], embed[group_ids.reshape(-1)], jnp.zeros((), BF)
        )
        own_rows = got = lax.psum_scatter(looked, "dp", scatter_dimension=0, tiled=True)
        all_bias = lax.all_gather(vocabulary_bias, BOTH, axis=0, tiled=True)
        every_up = lax.all_gather(ups, BOTH, axis=0, tiled=False)
        every_task = lax.all_gather(sequence_task_index, BOTH, axis=0, tiled=True)
    counts = labels * jnp.sum((every_task[:, None] == task_range[None, :]).astype(F32), 0)
    task_hot = (sequence_task_index[:, None] == task_range[None, :]).astype(F32)
    row_weight = jnp.sum(task_hot[0] * (task_loss_weight / jnp.maximum(counts, 1.0)))
    ups_full = (
        every_up.astype(BF)
        .reshape(shards, layers, 2, rank, up_part)
        .transpose(1, 2, 3, 0, 4)
        .reshape(layers, 2, rank, hidden)
    )
    blank = jnp.zeros((rank, hidden), BF)
    spare = lambda rows: jnp.zeros((rows, 3 * hidden), BF)
    adapters = jnp.stack(
        [
            jnp.concatenate(
                [
                    spare(2 * rank * layer),
                    jnp.concatenate([2 * ups_full[layer, 0], blank, blank], 1),
                    jnp.concatenate([blank, blank, 2 * ups_full[layer, 1]], 1),
                    spare(128 - 2 * rank * (layer + 1)),
                ],
                0,
            )
            for layer in range(layers)
        ]
    )
    downs = jnp.stack(
        [
            jnp.pad(
                jnp.concatenate([adapter_down_matrix[layer, 0], adapter_down_matrix[layer, 1]], 1),
                ((0, 0), (2 * rank * layer, 128 - 2 * rank * (layer + 1))),
            )
            for layer in range(layers)
        ]
    )
    segments = sentence_numbers[0]
    code = (jnp.pad(2 * seg_positions(segments), (0, labels)) + mine.astype(jnp.int32))[:, None]
    seg_real = segments.astype(F32)
    seg_wide = jnp.broadcast_to(seg_real[:, None], (tokens, 128))
    seg_row = seg_real[None, :]
    place_row = label_positions
    place_col = jnp.broadcast_to(label_positions.reshape(labels, 1), (labels, 128))

    target_bias = all_bias[label_target_token[0]]

    gains, shifts = norm_gain_vector, norm_bias_vector
    last_inputs = (place_col, place_row, seg_wide, downs, adapters, layer_bias_vector)
    in_start = ff_rows
    last_dn = lax.all_gather(last_feed, BOTH, axis=0, tiled=False)
    slabs_of = lambda up_full, dn_full: (slab_of(up_full, 0, ff_rows), slab_of(dn_full, 0, ff_rows))
    if grouped:
        more = (
            code, position_embedding, gains, shifts, downs, adapters, layer_bias_vector, seg_wide, seg_row,
        )
        qkv, x_last, one, two, slope, out_first, last_full, own_turned, mid, logs = first_layer(
            own_rows, got, first_full, other_full, last_chunk, embed, more, shards
        )
        slabs = [None, slabs_of(last_full, last_dn)]
        *saved, in_last, out_last, head_full = last_forward(
            x_last, *last_inputs, (last_full,), (in_start, in_start + qkv_rows + out_rows), *slabs[1], gains,
            shifts, head_dense_bias[None, :],
        )
        count = own_turned.shape[1]
        own_bias = lax.dynamic_slice_in_dim(
            all_bias, dp_index * table_rows + fsdp_index % 4 * count, count, 0
        ).reshape(-1, 128)
        mean_t, own_logs = head(saved[-1], own_bias, embed, own_turned)
    else:
        first_full = lax.all_gather(first_chunk, BOTH, axis=0, tiled=False)
        last_full = lax.all_gather(last_chunk, BOTH, axis=0, tiled=False)
        dn_full = jnp.concatenate([other_full[:, :cut], first_full[:, ff_rows:]], 1)
        slabs = [slabs_of(first_full[:, :ff_rows], dn_full), slabs_of(last_full, last_dn)]
        taken = lambda full_chunk, start, size: full_chunk[:, start : start + size].reshape(-1, hidden)
        in_first = taken(other_full, cut, qkv_rows)
        out_first = taken(other_full, cut + qkv_rows, out_rows)
        in_last = taken(last_full, in_start, qkv_rows)
        out_last = taken(last_full, in_start + qkv_rows, out_rows)
        head_full = taken(last_full, in_start + qkv_rows + out_rows, head_rows)
        qkv, mid, hidden_rows = project(
            own_rows, got, code, position_embedding, gains, shifts, downs, in_first, adapters, layer_bias_vector, tokens
        )
        context, logs = attend(qkv, seg_wide, seg_row)
        x_last, one, two, slope = after(
            context, hidden_rows, out_first, *slabs[0], layer_bias_vector, gains, shifts
        )
        saved = last_forward(
            x_last, *last_inputs, (in_last, out_last, head_full), None, *slabs[1], gains, shifts,
            head_dense_bias[None, :],
        )
        features = saved[-1]
        own_slice = lax.dynamic_slice_in_dim(embed, fsdp_index * slice_rows, slice_rows, 0)
        own_vocab = jnp.concatenate(
            [own_slice]
            + [
                lax.ppermute(
                    own_slice, "dp", [(k, (k + shift) % dp_count) for k in range(dp_count)]
                )
                for shift in range(1, dp_count)
            ],
            0,
        )
        own_bias = jnp.concatenate(
            [
                lax.dynamic_slice_in_dim(
                    all_bias,
                    ((dp_index - shift) % dp_count) * table_rows + fsdp_index * slice_rows,
                    slice_rows,
                    0,
                )
                for shift in range(dp_count)
            ]
        )
        bias_wide = jnp.broadcast_to(own_bias[:, None], (own_bias.shape[0], 128))
        every = lax.all_gather(features, "fsdp", axis=0, tiled=True)
        means, local_logs = vocab(every, own_vocab, own_vocab.T, bias_wide, labels)
        local_logs = local_logs.reshape(-1, labels)
        all_logs = lax.all_gather(local_logs, "fsdp", axis=0, tiled=False)
        whole_logs = jax.nn.logsumexp(all_logs, axis=0)
        scaled = (means * jnp.exp(local_logs - whole_logs)[:, None, :]).astype(BF)
        mean_t = lax.psum_scatter(scaled, "fsdp", scatter_dimension=0, tiled=True)[0].astype(F32)
        own_logs = lax.dynamic_index_in_dim(whole_logs, fsdp_index, 0, keepdims=False)
        own_logs = own_logs[None, :]

    step_as_real = optimizer_step_count[0].astype(F32)
    fades = (1.0 - beta_first**step_as_real, 1.0 - beta_second**step_as_real)
    lanes = lambda value: jnp.pad(
        jnp.broadcast_to(value, (1, value.size if value.ndim else 128)), ((0, 0), (0, 128))
    )[:, :128]
    facts = jnp.concatenate(
        [lanes(value) for value in (row_weight, *fades, target_bias)] + [jnp.zeros((4, 128), F32)]
    )
    hidden_grad, dense_gradient, late, facts = last_backward(
        mean_t, own_logs, own_rows, got, code, facts, saved, place_col, place_row, seg_wide, downs, in_last, adapters,
        out_last, *slabs[1], gains, head_full, 3 * rank, shards if grouped else None,
    )
    back = (hidden_grad, one, two, slope, out_first)
    adapts = (adapter_up_matrix, adapter_moment_first, adapter_moment_second)
    heads = (head_projection, head_moment_first, head_moment_second)
    if grouped:
        sums, dense_portion, adapter_portion = finish(
            (*back, first_full, other_full, gains), qkv, logs, seg_wide, seg_row, mid, dense_gradient, late, facts, rank, shards
        )
        loss, norm, *new = update(sums, dense_portion, adapter_portion, facts, heads, adapts)
        return (loss[0, 0], norm[0, 0], *new[3:], *new[:3])
    dctx = after_back(*back, *slabs[0], gains)
    first = attend_back(qkv, dctx, logs, seg_wide, seg_row, mid, rank)
    adapter_gradient = (first + late)[:, : 2 * rank * layers].T.reshape(layers, 2, rank, hidden)
    dense_portion = lax.psum_scatter(dense_gradient, BOTH, scatter_dimension=0, tiled=True)
    adapter_portion = lax.psum_scatter(adapter_gradient, BOTH, scatter_dimension=3, tiled=True)
    squared_entries = jnp.sum(adapter_portion * adapter_portion) + jnp.sum(dense_portion * dense_portion)
    masked_task_loss, norm_square = lax.psum((facts[0, 0], squared_entries), BOTH)
    gradient_norm = jnp.sqrt(norm_square)
    factor = jnp.minimum(1.0, clip_limit / (gradient_norm + 1e-06))
    adapter_new = adam(adapts[0], adapter_portion * factor, *adapts[1:], *fades)
    dense_new = adam(heads[0], dense_portion * factor, *heads[1:], *fades)
    return (masked_task_loss, gradient_norm, *adapter_new, *dense_new)


def solution(mesh):
    rows = P(BOTH, None)
    in_specs = (
        rows,
        rows,
        rows,
        rows,
        P(BOTH),
        P(),
        P(),
        P("dp", None),
        P(),
        P(),
        P(),
        P(None, None, BOTH),
        P(None, None, BOTH),
        P(None, None, BOTH),
        P(None, BOTH, None),
        P(),
        P(),
        P(BOTH),
        P(),
        P(None, None, None, BOTH),
        P(None, None, None, BOTH),
        P(None, None, None, BOTH),
        rows,
        rows,
        rows,
    )
    adapter = P(None, None, None, BOTH)
    out_specs = (P(), P(), adapter, adapter, adapter, rows, rows, rows)
    return jax.shard_map(
        per_device, mesh=mesh, in_specs=in_specs, out_specs=out_specs, check_vma=False
    )
```

```python
import functools

import jax
import jax.numpy as jnp
from jax import lax
from jax.experimental import pallas as pl
from jax.experimental.pallas import tpu as pltpu
from jax.sharding import PartitionSpec as P

HEADS = 12
TASKS = 4
REACH = 128

norm_eps = 1e-05
adapter_scale = 2.0
clip_limit = 0.01
learn_rate = 0.05
beta_first = 0.9
beta_second = 0.999
adam_eps = 1e-08
decay_rate = 0.01
masked_score = -1e30

BF = jnp.bfloat16
F32 = jnp.float32
BOTH = ("dp", "fsdp")
VMEM_BYTES = 60 * 1024 * 1024


def mm(a, b):
    return lax.dot_general(a, b, (((1,), (0,)), ((), ())), preferred_element_type=F32)


def mm_nt(a, b):
    return lax.dot_general(a, b, (((1,), (1,)), ((), ())), preferred_element_type=F32)


def mm_tn(a, b):
    return lax.dot_general(a, b, (((0,), (0,)), ((), ())), preferred_element_type=F32)


def layer_norm(rows_in, gain, shift):
    center = rows_in - jnp.mean(rows_in, -1, keepdims=True)
    spread = jnp.mean(center * center, -1, keepdims=True)
    return center * lax.rsqrt(spread + norm_eps) * gain + shift


def norm_back(rows_in, gain, gradient):
    center = rows_in - jnp.mean(rows_in, -1, keepdims=True)
    inverse = lax.rsqrt(jnp.mean(center * center, -1, keepdims=True) + norm_eps)
    unit = center * inverse
    scaled = gradient * gain
    return inverse * (
        scaled
        - jnp.mean(scaled, -1, keepdims=True)
        - unit * jnp.mean(scaled * unit, -1, keepdims=True)
    )


def gelu_pair(v):
    size = jnp.abs(v) * 0.7071067811865476
    base = 1.0 + 0.3275911 * size
    t = pl.reciprocal(base, approx=True)
    t = t * (2.0 - base * t)
    bell = jnp.exp(-0.5 * v * v)
    poly = t * (
        0.127414796 + t * (-0.142248368 + t * (0.7107068705 + t * (-0.7265760135 + t * 0.5307027145)))
    )
    tail = poly * bell
    phi = jnp.where(v >= 0.0, 1.0 - tail, tail)
    return v * phi, phi + v * (bell * 0.3989422804014327)


def params(**more):
    return pltpu.CompilerParams(vmem_limit_bytes=VMEM_BYTES, **more)


def full(shape):
    return pl.BlockSpec(shape, lambda *_: (0,) * len(shape))


def split_of(total, most, step):
    size = (min(most, total) // step) * step
    while size > step and total % size:
        size -= step
    return size if size and total % size == 0 else total


def pair_rows(block, width):
    first = lax.broadcasted_iota(jnp.int32, block.shape, 1) < width
    return jnp.concatenate([jnp.where(first, block, 0.0), jnp.where(first, 0.0, block)], 0).astype(BF)


def pair_join(wide, width):
    rows = wide.shape[1] // 2
    return jnp.concatenate([wide[:width, :rows], wide[width:, rows:]], 0)


def masked(scores, same):
    rows = scores.shape[1] // 2
    return jnp.concatenate(
        [
            jnp.where(same, scores[:, :rows], masked_score),
            jnp.where(same, scores[:, rows:], masked_score),
        ],
        1,
    )


def qkv_bias(bias_ref, layer, start, size):
    hidden = bias_ref.shape[1] // 8
    if start >= 2 * hidden:
        return bias_ref[layer : layer + 1, start - hidden : start - hidden + size]
    return bias_ref[layer : layer + 1, start : start + size] if start < hidden else 0.0


def norm_of(norm_refs, k):
    return norm_refs[0][k : k + 1, :], norm_refs[1][k : k + 1, :]


def project_body(
    own_ref, got_ref, code_ref, spots_ref, gain_ref, shift_ref, down_ref, w_ref, up_ref, bias_ref,
    out_ref, mid_ref, x_ref,
):
    mine = code_ref[...] % 2
    choose = (
        lax.broadcasted_iota(jnp.int32, (own_ref.shape[0], spots_ref.shape[0]), 1) == code_ref[...] // 2
    )
    summed = jnp.where(
        mine > 0, own_ref[...].astype(F32), got_ref[...].astype(F32)
    ) + mm(choose.astype(F32).astype(BF), spots_ref[...])
    x = layer_norm(summed, *norm_of((gain_ref, shift_ref), 0))
    x_ref[...] = x
    low = x.astype(BF)
    mid = mm(low, down_ref[0]).astype(BF)
    mid_ref[...] = mid
    total = w_ref.shape[0]
    step = total // 3
    for start in range(0, total, step):
        part = slice(start, start + step)
        out_ref[:, part] = (
            mm_nt(low, w_ref[part, :]) + mm(mid, up_ref[0, :, part]) + qkv_bias(bias_ref, 0, start, step)
        ).astype(BF)


def project(own, got, code, spots, gains, shifts, down, w, up, bias, rows):
    width = own.shape[1]
    tile = split_of(rows, 256, 16)
    total = w.shape[0]
    row = lambda n: pl.BlockSpec((tile, n), lambda i: (i, 0))
    return pl.pallas_call(
        project_body,
        grid=(rows // tile,),
        in_specs=[row(width), row(width), row(1)]
        + [full(a.shape) for a in (spots, gains, shifts, down, w, up, bias)],
        out_specs=[row(total), row(down.shape[2]), row(width)],
        out_shape=[
            jax.ShapeDtypeStruct((rows, total), BF),
            jax.ShapeDtypeStruct((rows, down.shape[2]), BF),
            jax.ShapeDtypeStruct((rows, width), F32),
        ],
        compiler_params=params(),
        name="project",
    )(own, got, code, spots, gains, shifts, down, w, up, bias)


def attend_body(q_ref, k_ref, v_ref, seg_ref, seg_row_ref, ctx_ref, log_ref):
    rows = q_ref.shape[0]
    width = q_ref.shape[1] // 2
    scale = width**-0.5
    turned = turn_blocks(v_ref)

    def scored(start):
        own, near = reach_of(start, rows)
        return mm_nt(k_ref[near, :], pair_rows(q_ref[own, :].astype(F32) * scale, width))

    scores = scored(0)
    for start in range(0, rows, REACH):
        own, near = reach_of(start, rows)
        later = scored(start + REACH) if start + REACH < rows else None
        same = seg_ref[near, :] == seg_row_ref[:, own]
        scores = masked(scores, same)
        top = jnp.max(scores, 0, keepdims=True)
        weights = jnp.exp(scores - top)
        total = jnp.sum(weights, 0, keepdims=True)
        context = mm(turned[:, near], weights.astype(BF)) * (1.0 / total)
        ctx_ref[own, :] = pair_join(context, width).T.astype(BF)
        log_ref[0, :, 2 * start : 2 * start + 2 * REACH] = top + jnp.log(total)
        scores = later


def reach_of(start, rows):
    return slice(start, start + REACH), slice(max(0, start - REACH), min(rows, start + 2 * REACH))


def turn_blocks(ref):
    blocks = [ref[k : k + 128, :].astype(F32).T.astype(BF) for k in range(0, ref.shape[0], 128)]
    return jnp.concatenate(blocks, 1)


def attend(qkv, seg_wide, seg_row):
    rows, total = qkv.shape
    hidden = total // 3
    lanes = 2 * (hidden // HEADS)
    pairs = hidden // lanes
    column = lambda kind: pl.BlockSpec((rows, lanes), lambda p: (0, kind * pairs + p))
    return pl.pallas_call(
        attend_body,
        grid=(pairs,),
        in_specs=[column(0), column(1), column(2), full(seg_wide.shape), full(seg_row.shape)],
        out_specs=[
            pl.BlockSpec((rows, lanes), lambda p: (0, p)),
            pl.BlockSpec((1, 1, 2 * rows), lambda p: (p, 0, 0)),
        ],
        out_shape=[
            jax.ShapeDtypeStruct((rows, hidden), BF),
            jax.ShapeDtypeStruct((pairs, 1, 2 * rows), F32),
        ],
        compiler_params=params(),
        name="attend",
    )(qkv, qkv, qkv, seg_wide, seg_row)


def flat(ref):
    whole = ref[...]
    return whole.reshape(-1, whole.shape[-1])


def rows_of(ref, start, size):
    each = ref.shape[1]
    if size % each == 0 and start % each == 0 and each % 16 == 0:
        part = ref[start // each : (start + size) // each, :, :]
        return part.reshape(size, part.shape[-1])
    return flat(ref)[start : start + size, :]


def feed_step(ref):
    units = ref.shape[0] * ref.shape[1]
    step = ref.shape[1]
    while units % (2 * step) == 0 and 2 * step <= 768 and ref.shape[0] > 1:
        step *= 2
    return units, (step if ref.shape[0] > 1 else split_of(units, 768, 128))


def later_biases(bias_ref, layer):
    hidden = bias_ref.shape[1] // 8
    row = bias_ref[layer : layer + 1, :]
    return row[:, 2 * hidden : 3 * hidden], row[:, 3 * hidden : 7 * hidden], row[:, 7 * hidden :]


def after_body(
    ctx_ref, x_ref, wo_ref, up_ref, down_ref, bias_ref, gain_ref, shift_ref,
    out_ref, one_ref, two_ref, slope_ref,
):
    bo, b1, b2 = later_biases(bias_ref, 0)
    one = x_ref[...] + (mm_nt(ctx_ref[...], wo_ref[...]) + bo)
    one_ref[...] = one
    middle = layer_norm(one, *norm_of((gain_ref, shift_ref), 1))
    low = middle.astype(BF)
    total = middle + b2
    units, step = feed_step(up_ref)
    gate = mm_nt(low, rows_of(up_ref, 0, step))
    for start in range(0, units, step):
        part = slice(start, start + step)
        later = mm_nt(low, rows_of(up_ref, start + step, step)) if start + step < units else None
        act, slope = gelu_pair(gate + b1[:, part])
        slope_ref[:, part] = slope.astype(BF)
        total = total + mm(act.astype(BF), rows_of(down_ref, start, step))
        gate = later
    two_ref[...] = total
    out_ref[...] = layer_norm(total, *norm_of((gain_ref, shift_ref), 2))


def slab_spec(slab):
    array, place, rows = slab
    return pl.BlockSpec((array.shape[0], rows, array.shape[2]), lambda *_: (0, place, 0))


def after(ctx, x, wo, up, down, bias, gains, shifts):
    rows, width = x.shape
    tile = split_of(rows, 256, 16)
    units = 4 * width
    row = lambda n: pl.BlockSpec((tile, n), lambda i: (i, 0))
    return pl.pallas_call(
        after_body,
        grid=(rows // tile,),
        in_specs=[row(width), row(width), full(wo.shape), slab_spec(up), slab_spec(down)]
        + [full(a.shape) for a in (bias, gains, shifts)],
        out_specs=[row(width), row(width), row(width), row(units)],
        out_shape=[jax.ShapeDtypeStruct((rows, width), F32)] * 3
        + [jax.ShapeDtypeStruct((rows, units), BF)],
        compiler_params=params(),
        name="after",
    )(ctx, x, wo, up[0], down[0], bias, gains, shifts)


def exact_rows(choose, matrix):
    high = matrix.astype(BF)
    rest = matrix - high.astype(F32)
    middle = rest.astype(BF)
    low = (rest - middle.astype(F32)).astype(BF)
    return mm(choose, high) + mm(choose, middle) + mm(choose, low)


def unpack_rows(slab_ref, targets):
    shards = slab_ref.shape[0]

    @pl.loop(0, shards // 2)
    def _(k):
        first, second = slab_ref[2 * k].astype(F32), slab_ref[2 * k + 1].astype(F32)
        at = 0
        for target in targets:
            each = target.shape[0] // shards
            both = jnp.concatenate([first[at : at + each], second[at : at + each]], 0)
            target[pl.ds(pl.multiple_of(2 * each * k, 2 * each), 2 * each), :] = both.astype(BF)
            at += each


def last_forward_body(
    x_ref, place_ref, place_row_ref, seg_ref, down_ref, adapt_ref, bias_ref, weights_any, up_any, dn_any,
    gain_ref, shift_ref, hbias_ref,
    kv_ref, q_ref, mid_ref, log_ref, one_ref, slope_ref, two_ref, low_ref, act_ref, hslope_ref, feat_ref, *more,
    places, starts,
):
    copies = []
    if starts is None:
        up_ref, dn_ref, ctx_ref, w_ref, wo_ref, hb_ref, sems = more
        sources = zip(weights_any, (w_ref, wo_ref, hb_ref))
    else:
        w_out, wo_out, hb_out, up_ref, dn_ref, ctx_ref, w_ref, wo_ref, hb_ref, in_slab, hb_slab, sems = more
        sources = [
            (weights_any[0].at[:, pl.ds(start, slab.shape[1]), :], slab)
            for start, slab in zip(starts, (in_slab, hb_slab))
        ]
    for source, target in sources:
        copies.append((source, target))
    early = len(copies)
    for source, target, place in ((up_any, up_ref, places[0]), (dn_any, dn_ref, places[1])):
        each = target.shape[1]
        copies.append((source.at[:, pl.ds(place * each, each), :], target))
    copies = [pltpu.make_async_copy(*ends, sems.at[k]) for k, ends in enumerate(copies)]
    for copy in copies:
        copy.start()
    for copy in copies[:early]:
        copy.wait()
    copies = copies[early:]
    if starts is not None:
        unpack_rows(in_slab, (w_ref, wo_ref))
        unpack_rows(hb_slab, (hb_ref,))
        for k, ends in enumerate(((w_ref, w_out), (wo_ref, wo_out), (hb_ref, hb_out))):
            copies.append(pltpu.make_async_copy(*ends, sems.at[4 + k]))
            copies[-1].start()
    rows, hidden = x_ref.shape
    labels = place_ref.shape[0]
    lanes = 2 * (hidden // HEADS)
    width = lanes // 2
    low = x_ref[...].astype(BF)
    mid = mm(low, down_ref[1]).astype(BF)
    mid_ref[...] = mid
    step = split_of(hidden, 768, 128)
    for start in range(hidden, 3 * hidden, step):
        part = slice(start, start + step)
        kv_ref[:, start - hidden : start - hidden + step] = (
            mm_nt(low, w_ref[part, :]) + mm(mid, adapt_ref[1, :, part]) + qkv_bias(bias_ref, 1, start, step)
        ).astype(BF)
    choose = (
        lax.broadcasted_iota(jnp.int32, (labels, rows), 1) == place_ref[...][:, 0:1]
    ).astype(F32).astype(BF)
    own = exact_rows(choose, x_ref[...])
    own_low = own.astype(BF)
    own_mid = mm(choose, mid).astype(BF)
    q_ref[...] = (
        mm_nt(own_low, w_ref[:hidden, :])
        + mm(own_mid, adapt_ref[1, :, :hidden])
        + qkv_bias(bias_ref, 1, 0, hidden)
    ).astype(BF)
    seg = seg_ref[...]
    seg_own = jnp.sum(
        jnp.where(
            lax.broadcasted_iota(jnp.int32, (rows, labels), 0) == place_row_ref[...], seg, 0.0
        ),
        0,
        keepdims=True,
    )
    same = seg == seg_own

    def scored(p):
        part = slice(p * lanes, (p + 1) * lanes)
        return mm_nt(kv_ref[:, part], pair_rows(q_ref[:, part].astype(F32) * width**-0.5, width))

    later = scored(0)
    for p in range(hidden // lanes):
        part = slice(p * lanes, (p + 1) * lanes)
        scores = masked(later, same)
        later = scored(p + 1) if (p + 1) * lanes < hidden else None
        top = jnp.max(scores, 0, keepdims=True)
        weights = jnp.exp(scores - top)
        total = jnp.sum(weights, 0, keepdims=True)
        context = mm_tn(
            kv_ref[:, hidden + p * lanes : hidden + (p + 1) * lanes], weights.astype(BF)
        ) * (1.0 / total)
        ctx_ref[:, part] = pair_join(context, width).T.astype(BF)
        log_ref[p : p + 1, :] = top + jnp.log(total)
    bo, b1, b2 = later_biases(bias_ref, 1)
    norms = (gain_ref, shift_ref)
    one = own + (mm_nt(ctx_ref[...], wo_ref[...]) + bo)
    one_ref[...] = one
    middle = layer_norm(one, *norm_of(norms, 3))
    middle_low = middle.astype(BF)
    sum_two = middle + b2
    units, step = feed_step(up_ref)
    for copy in copies:
        copy.wait()
    gate = mm_nt(middle_low, rows_of(up_ref, 0, step))
    for start in range(0, units, step):
        part = slice(start, start + step)
        later = mm_nt(middle_low, rows_of(up_ref, start + step, step)) if start + step < units else None
        act, slope = gelu_pair(gate + b1[:, part])
        gate = later
        slope_ref[:, part] = slope.astype(BF)
        sum_two = sum_two + mm(act.astype(BF), rows_of(dn_ref, start, step))
    two_ref[...] = sum_two
    out_low = layer_norm(sum_two, *norm_of(norms, 4)).astype(BF)
    low_ref[...] = out_low
    act, slope = gelu_pair(mm(out_low, hb_ref[...]) + hbias_ref[...])
    act_ref[...] = act
    hslope_ref[...] = slope
    feat_ref[...] = layer_norm(act, *norm_of(norms, 5)).astype(BF)


def slab_scratch(slab):
    array, place, rows = slab
    return pltpu.VMEM((array.shape[0], rows, array.shape[2]), BF)


def last_forward(
    x, place_col, place_row, seg_wide, down, adapt, bias, weights, starts, up, dn, gains, shifts, hbias
):
    rows, hidden = x.shape
    labels = place_col.shape[0]
    units = 4 * hidden
    whole = pl.BlockSpec(memory_space=pltpu.VMEM)
    anywhere = pl.BlockSpec(memory_space=pl.ANY)
    shape = jax.ShapeDtypeStruct
    pairs = HEADS // 2
    matrices = [(3 * hidden, hidden), (hidden, hidden), (hidden, hidden)]
    slabs = []
    if starts is not None:
        shards = weights[0].shape[0]
        slabs = [
            pltpu.VMEM((shards, 4 * hidden // shards, hidden), BF),
            pltpu.VMEM((shards, weights[0].shape[1] - starts[1], hidden), BF),
        ]

    def body(*refs):
        head, rest = refs[:7], refs[7:]
        return last_forward_body(
            *head, rest[: len(weights)], *rest[len(weights) :], places=(up[1], dn[1]), starts=starts
        )

    return pl.pallas_call(
        body,
        in_specs=[whole] * 7 + [anywhere] * (len(weights) + 2) + [whole] * 3,
        out_specs=[whole] * 11 + ([anywhere] * 3 if slabs else []),
        out_shape=[
            shape((rows, 2 * hidden), BF),
            shape((labels, hidden), BF),
            shape((rows, down.shape[2]), BF),
            shape((pairs, 2 * labels), F32),
            shape((labels, hidden), F32),
            shape((labels, units), BF),
            shape((labels, hidden), F32),
            shape((labels, hidden), BF),
            shape((labels, hidden), F32),
            shape((labels, hidden), F32),
            shape((labels, hidden), BF),
        ]
        + ([shape(m, BF) for m in matrices] if slabs else []),
        scratch_shapes=[
            slab_scratch(up),
            slab_scratch(dn),
            pltpu.VMEM((labels, hidden), BF),
            *[pltpu.VMEM(m, BF) for m in matrices],
            *slabs,
            pltpu.SemaphoreType.DMA((7,)),
        ],
        compiler_params=params(),
        name="last_forward",
    )(x, place_col, place_row, seg_wide, down, adapt, bias, *weights, up[0], dn[0], gains, shifts, hbias)


def vocab_body(u_ref, e_ref, et_ref, bias_ref, num_ref, log_ref, scores, weights):
    count = e_ref.shape[0]
    step = split_of(count, 640, 16)
    u = u_ref[...]
    rows = u.shape[0]
    labels = num_ref.shape[2]
    top = jnp.full((1, rows), -jnp.inf, F32)
    for start in range(0, count, step):
        part = slice(start, start + step)
        bias = bias_ref[part, :]
        logits = mm_nt(e_ref[part, :], u) + jnp.concatenate([bias] * (rows // bias.shape[1]), 1)
        scores[part, :] = logits
        top = jnp.maximum(top, jnp.max(logits, 0, keepdims=True))
    total = jnp.zeros((1, rows), F32)
    for start in range(0, count, step):
        part = slice(start, start + step)
        grown = jnp.exp(scores[part, :] - top)
        total = total + jnp.sum(grown, 0, keepdims=True)
        weights[part, :] = grown.astype(BF)
    mean = mm(et_ref[...], weights[...]) * (1.0 / total)
    logs = top + jnp.log(total)
    for k in range(rows // labels):
        num_ref[k, :, :] = mean[:, k * labels : (k + 1) * labels]
        log_ref[k, :, :] = logs[:, k * labels : (k + 1) * labels]


def vocab(u, e, et, bias_wide, labels):
    rows, hidden = u.shape
    count = e.shape[0]
    tile = 2 * labels
    return pl.pallas_call(
        vocab_body,
        grid=(rows // tile,),
        in_specs=[
            pl.BlockSpec((tile, hidden), lambda i: (i, 0)),
            full(e.shape),
            full(et.shape),
            full(bias_wide.shape),
        ],
        out_specs=[
            pl.BlockSpec((2, hidden, labels), lambda i: (i, 0, 0)),
            pl.BlockSpec((2, 1, labels), lambda i: (i, 0, 0)),
        ],
        out_shape=[
            jax.ShapeDtypeStruct((rows // labels, hidden, labels), F32),
            jax.ShapeDtypeStruct((rows // labels, 1, labels), F32),
        ],
        scratch_shapes=[pltpu.VMEM((count, tile), F32), pltpu.VMEM((count, tile), BF)],
        compiler_params=params(),
        name="vocab",
    )(u, e, et, bias_wide)


def last_backward_body(
    own_any, got_any, mean_ref, all_log_ref, code_ref, fact_ref, kv_ref, q_ref, mid_ref, log_ref, one_ref, slope_ref, two_ref,
    low_ref, act_ref, hslope_ref, feat_ref, place_ref, place_row_ref, seg_ref, down_ref, w_ref, adapt_ref, wo_ref,
    up_any, dn_any, gain_ref, hb_ref,
    dx_ref, gh_ref, g_ref, out_fact_ref,
    up_ref, dn_ref, dkv_ref, dq_ref, aims, sems, *, places, edge,
):
    labels = place_ref.shape[0]
    tail = pl.ds(kv_ref.shape[0], labels)
    aimed = [
        pltpu.make_async_copy(source.at[tail, :], aims.at[k], sems.at[2 + k])
        for k, source in enumerate((own_any, got_any))
    ]
    for copy in aimed:
        copy.start()
    copies = []
    for k, (source, target, place) in enumerate(
        ((up_any, up_ref, places[0]), (dn_any, dn_ref, places[1]))
    ):
        rows = target.shape[1]
        copies.append(
            pltpu.make_async_copy(
                source.at[:, pl.ds(place * rows, rows), :], target, sems.at[k]
            )
        )
        copies[-1].start()
    rows = kv_ref.shape[0]
    labels, hidden = feat_ref.shape
    lanes = 2 * (hidden // HEADS)
    width = lanes // 2
    scale = width**-0.5
    for copy in aimed:
        copy.wait()
    mine = code_ref[kv_ref.shape[0] :, :] % 2
    targets = jnp.where(mine > 0, aims[0].astype(F32), aims[1].astype(F32))
    weight = fact_ref[0:1, 0:1]
    chosen = jnp.sum(feat_ref[...].astype(F32) * targets, keepdims=True)
    loss = weight * (jnp.sum(all_log_ref[...] - fact_ref[3:4, :labels], keepdims=True) - chosen)
    out_fact_ref[...] = jnp.where(
        lax.broadcasted_iota(jnp.int32, fact_ref.shape, 0) == 0, loss, fact_ref[...]
    )
    du = weight * (mean_ref[...].T - targets)
    dact = norm_back(act_ref[...], gain_ref[5:6, :], du)
    dz = (hslope_ref[...] * dact).astype(BF)
    dense = mm_tn(low_ref[...], dz)
    if len(gh_ref.shape) == 2:
        gh_ref[...] = dense
    else:
        each = hidden // gh_ref.shape[0]
        spare = jnp.zeros((gh_ref.shape[1] - each, hidden), F32)
        for k in range(gh_ref.shape[0]):
            gh_ref[k] = jnp.concatenate([dense[k * each : (k + 1) * each, :], spare], 0).astype(BF)
    dtwo = norm_back(two_ref[...], gain_ref[4:5, :], mm_nt(dz, hb_ref[...]))
    dtwo_low = dtwo.astype(BF)
    dmiddle = dtwo
    units, step = feed_step(up_ref)
    for copy in copies:
        copy.wait()
    dact = mm_nt(dtwo_low, rows_of(dn_ref, 0, step))
    for start in range(0, units, step):
        part = slice(start, start + step)
        later = mm_nt(dtwo_low, rows_of(dn_ref, start + step, step)) if start + step < units else None
        dgate = (slope_ref[:, part].astype(F32) * dact).astype(BF)
        dmiddle = dmiddle + mm(dgate, rows_of(up_ref, start, step))
        dact = later
    done = norm_back(one_ref[...], gain_ref[3:4, :], dmiddle)
    dctx = mm(done.astype(BF), wo_ref[...]).astype(BF)
    seg = seg_ref[...]
    choose_t = lax.broadcasted_iota(jnp.int32, (rows, labels), 0) == place_row_ref[...]
    same = seg == jnp.sum(jnp.where(choose_t, seg, 0.0), 0, keepdims=True)

    def products(p):
        part = slice(p * lanes, (p + 1) * lanes)
        later = slice(hidden + p * lanes, hidden + (p + 1) * lanes)
        queries = pair_rows(q_ref[:, part].astype(F32) * scale, width)
        outs = pair_rows(dctx[:, part].astype(F32), width)
        return queries, outs, mm_nt(kv_ref[:, part], queries), mm_nt(kv_ref[:, later], outs)

    ahead = products(0)
    for p in range(hidden // lanes):
        part = slice(p * lanes, (p + 1) * lanes)
        later = slice(hidden + p * lanes, hidden + (p + 1) * lanes)
        queries, outs, scores, dweights = ahead
        ahead = products(p + 1) if (p + 1) * lanes < hidden else None
        keys = kv_ref[:, part]
        weights = jnp.exp(masked(scores, same) - log_ref[p : p + 1, :])
        inner = jnp.sum(dweights * weights, 0, keepdims=True)
        dscores = (weights * (dweights - inner)).astype(BF)
        dkv_ref[:, part] = mm(dscores, queries).astype(BF)
        dkv_ref[:, later] = mm(weights.astype(BF), outs).astype(BF)
        dq_ref[:, part] = (pair_join(mm_tn(keys, dscores), width) * scale).T.astype(BF)
    dq = dq_ref[...]
    own_mid = mm(
        (lax.broadcasted_iota(jnp.int32, (labels, rows), 1) == place_ref[...][:, 0:1]).astype(F32).astype(BF),
        mid_ref[...],
    ).astype(BF)
    g_ref[...] = adapter_scale * jnp.where(
        lax.broadcasted_iota(jnp.int32, g_ref.shape, 1) < edge,
        mm_tn(dq, own_mid),
        mm_tn(dkv_ref[:, hidden:], mid_ref[...]),
    )
    dmid_own = mm_nt(dq, adapt_ref[1, :, :hidden]).astype(BF)
    own = done + mm(dq, w_ref[:hidden, :]) + mm_nt(dmid_own, down_ref[1])
    spread = choose_t.astype(F32).astype(BF)
    own_high = own.astype(BF)
    own_rest = (own - own_high.astype(F32)).astype(BF)
    dmid = mm_nt(dkv_ref[:, hidden:], adapt_ref[1, :, 2 * hidden :]).astype(BF)
    step = split_of(hidden, 256, 128)
    for start in range(0, hidden, step):
        part = slice(start, start + step)
        dx_ref[:, part] = (
            mm(dkv_ref[...], w_ref[hidden:, part])
            + mm_nt(dmid, down_ref[1, part, :])
            + mm(spread, own_high[:, part])
            + mm(spread, own_rest[:, part])
        )


def last_backward(
    mean, logs, own, got, code, facts, saved, place_col, place_row, seg_wide, down, w, adapt, wo, up, dn, gains, hb, edge, shards
):
    kv = saved[0]
    rows = kv.shape[0]
    labels, hidden = saved[-1].shape
    whole = pl.BlockSpec(memory_space=pltpu.VMEM)
    anywhere = pl.BlockSpec(memory_space=pl.ANY)
    shape = jax.ShapeDtypeStruct
    return pl.pallas_call(
        functools.partial(last_backward_body, places=(up[1], dn[1]), edge=edge),
        in_specs=[anywhere] * 2 + [whole] * 22 + [anywhere] * 2 + [whole] * 2,
        out_specs=[whole] * 4,
        out_shape=[
            shape((rows, hidden), F32),
            shape((hidden, hidden), F32)
            if shards is None
            else shape((shards, -(-hidden // shards // 16) * 16, hidden), BF),
            shape((hidden, down.shape[2]), F32),
            shape(facts.shape, F32),
        ],
        scratch_shapes=[
            slab_scratch(up),
            slab_scratch(dn),
            pltpu.VMEM(kv.shape, BF),
            pltpu.VMEM((labels, hidden), BF),
            pltpu.VMEM((2, labels, hidden), BF),
            pltpu.SemaphoreType.DMA((4,)),
        ],
        compiler_params=params(),
        name="last_backward",
    )(own, got, mean, logs, code, facts, *saved, place_col, place_row, seg_wide, down, w, adapt, wo, up[0], dn[0], gains, hb)


def after_back_body(dout_ref, one_ref, two_ref, slope_ref, wo_ref, up_ref, down_ref, gain_ref, dctx_ref):
    dtwo = norm_back(two_ref[...], gain_ref[2:3, :], dout_ref[...])
    low = dtwo.astype(BF)
    dmiddle = dtwo
    units, step = feed_step(up_ref)
    dact = mm_nt(low, rows_of(down_ref, 0, step))
    for start in range(0, units, step):
        part = slice(start, start + step)
        later = mm_nt(low, rows_of(down_ref, start + step, step)) if start + step < units else None
        dgate = (slope_ref[:, part].astype(F32) * dact).astype(BF)
        dmiddle = dmiddle + mm(dgate, rows_of(up_ref, start, step))
        dact = later
    done = norm_back(one_ref[...], gain_ref[1:2, :], dmiddle)
    dctx_ref[...] = mm(done.astype(BF), wo_ref[...]).astype(BF)


def after_back(dout, one, two, slope, wo, up, down, norms):
    rows, width = dout.shape
    tile = split_of(rows, 256, 16)
    row = lambda n: pl.BlockSpec((tile, n), lambda i: (i, 0))
    return pl.pallas_call(
        after_back_body,
        grid=(rows // tile,),
        in_specs=[row(width), row(width), row(width), row(slope.shape[1]), full(wo.shape)]
        + [slab_spec(up), slab_spec(down), full(norms.shape)],
        out_specs=row(width),
        out_shape=jax.ShapeDtypeStruct((rows, width), BF),
        compiler_params=params(),
        name="after_back",
    )(dout, one, two, slope, wo, up[0], down[0], norms)


def attend_back_body(
    q_ref, k_ref, v_ref, dctx_ref, log_ref, seg_ref, seg_row_ref, mid_ref, g_ref, dv_ref, *, edge
):
    rows = q_ref.shape[0]
    width = q_ref.shape[1] // 2
    scale = width**-0.5
    dv_ref[...] = jnp.zeros_like(dv_ref)
    gq = jnp.zeros((2 * width, mid_ref.shape[1]), F32)
    turned = turn_blocks(k_ref)

    def products(start):
        own, near = reach_of(start, rows)
        queries = pair_rows(q_ref[own, :].astype(F32) * scale, width)
        outs = pair_rows(dctx_ref[own, :].astype(F32), width)
        return outs, mm_nt(k_ref[near, :], queries), mm_nt(v_ref[near, :], outs)

    now = products(0)
    for start in range(0, rows, REACH):
        own, near = reach_of(start, rows)
        later = products(start + REACH) if start + REACH < rows else None
        outs, scores, dweights = now
        same = seg_ref[near, :] == seg_row_ref[:, own]
        logs = log_ref[0, :, 2 * start : 2 * start + 2 * REACH]
        weights = jnp.exp(masked(scores, same) - logs)
        inner = jnp.sum(dweights * weights, 0, keepdims=True)
        dscores = (weights * (dweights - inner)).astype(BF)
        dv_ref[near, :] += mm(weights.astype(BF), outs)
        dq = (pair_join(mm(turned[:, near], dscores), width) * scale).astype(BF)
        gq = gq + mm(dq, mid_ref[own, :])
        now = later
    gv = mm_tn(dv_ref[...].astype(BF), mid_ref[...])
    g_ref[...] = adapter_scale * jnp.where(
        lax.broadcasted_iota(jnp.int32, gq.shape, 1) < edge, gq, gv
    )


def attend_back(qkv, dctx, logs, seg_wide, seg_row, mid, edge):
    rows, total = qkv.shape
    hidden = total // 3
    lanes = 2 * (hidden // HEADS)
    pairs = hidden // lanes
    column = lambda kind: pl.BlockSpec((rows, lanes), lambda p: (0, kind * pairs + p))
    return pl.pallas_call(
        functools.partial(attend_back_body, edge=edge),
        grid=(pairs,),
        in_specs=[
            column(0),
            column(1),
            column(2),
            column(0),
            pl.BlockSpec((1, 1, 2 * rows), lambda p: (p, 0, 0)),
            full(seg_wide.shape),
            full(seg_row.shape),
            full(mid.shape),
        ],
        out_specs=pl.BlockSpec((lanes, mid.shape[1]), lambda p: (p, 0)),
        out_shape=jax.ShapeDtypeStruct((hidden, mid.shape[1]), F32),
        scratch_shapes=[pltpu.VMEM((rows, lanes), F32)],
        compiler_params=params(),
        name="attend_back",
    )(qkv, qkv, qkv, dctx, logs, seg_wide, seg_row, mid)


MESH = pl.DeviceIdType.MESH


def position():
    dp, fsdp = lax.axis_index("dp"), lax.axis_index("fsdp")
    return {"x": dp, "z": fsdp // 4, "y": (fsdp // 2) % 2, "c": fsdp % 2}


def device_of(place):
    return (place["x"], (place["z"] * 2 + place["y"]) * 2 + place["c"])


def number_of(place):
    return place["x"] * 16 + (place["z"] * 2 + place["y"]) * 2 + place["c"]


def rank_device(number):
    return (number // 16, number % 16)


def greet_all(shards):
    barrier = pltpu.get_barrier_semaphore()
    me = lax.axis_index("dp") * 16 + lax.axis_index("fsdp")

    @pl.loop(1, shards)
    def _(k):
        pl.semaphore_signal(
            barrier, inc=1, device_id=rank_device((me + k) % shards), device_id_type=MESH
        )


def await_all(shards):
    pl.semaphore_wait(pltpu.get_barrier_semaphore(), shards - 1)


def direct_copy(source, target, sems, me, k, shards):
    return pltpu.make_async_remote_copy(
        src_ref=source,
        dst_ref=target,
        send_sem=sems.at[0],
        recv_sem=sems.at[1],
        device_id=rank_device((me + k) % shards),
        device_id_type=MESH,
    )


def spread(piece_of, buffer, sems, me, shards):
    @pl.loop(1, shards)
    def _(k):
        direct_copy(piece_of((me + k) % shards), buffer.at[me], sems, me, k, shards).start()


def collect(buffer, sems, me, shards):
    whole = buffer.at[pl.ds(0, shards - 1)]
    copy = direct_copy(whole, whole, sems, me, 1, shards)
    copy.wait_recv()
    copy.wait_send()


def relative_places(order):
    places = [
        {"x": dx, "z": dz, "y": dy} for dx in (0, 1) for dz in range(-3, 4) for dy in (0, 1)
    ]
    size = lambda p: abs(p["x"]) + abs(p["z"]) + abs(p["y"])
    return sorted(places, key=lambda p: (abs(p[order[-1]]), size(p), [abs(p[a]) for a in order]))


class Gather:
    def __init__(self, chunk, full_buffer, start, rows, order, sends, receives, hands, hands_got):
        self.chunk, self.full, self.order = chunk, full_buffer, order
        self.part = pl.ds(start, rows)
        self.sends, self.receives, self.hands, self.hands_got = sends, receives, hands, hands_got
        self.here = position()
        self.items = relative_places(order)

    def origin(self, item):
        here = self.here
        return {"x": (here["x"] + item["x"]) % 2, "z": here["z"] - item["z"], "y": (here["y"] + item["y"]) % 2, "c": here["c"]}

    def key(self, place):
        return (place["x"] * 4 + place["z"]) * 2 + place["y"]

    def outward(self, item):
        deepest = max([k for k, axis in enumerate(self.order) if item[axis]], default=-1)
        ways = []
        if deepest >= 0 and self.order[deepest] == "z":
            ways.append(("z", 1 if item["z"] > 0 else -1))
        for axis in self.order[deepest + 1 :]:
            ways += [("z", 1), ("z", -1)] if axis == "z" else [(axis, 1)]
        return ways

    def copy(self, index, way, slot, item):
        here = self.here
        place = self.origin(item)
        number, key = number_of(place), self.key(place)
        mine = not any(item.values())
        source = self.chunk.at[self.part, :] if mine else self.full.at[number, self.part, :]
        if way is None:
            target = dict(here, c=1 - here["c"])
            sends, receives = self.hands.at[index], self.hands_got.at[key]
        else:
            axis, step = way
            target = dict(here)
            target[axis] = here["z"] + step if axis == "z" else 1 - here[axis]
            sends, receives = self.sends.at[index * 4 + slot], self.receives.at[key]
        return pltpu.make_async_remote_copy(
            src_ref=source,
            dst_ref=self.full.at[number, self.part, :],
            send_sem=sends,
            recv_sem=receives,
            device_id=device_of(target),
            device_id_type=MESH,
        )

    def valid(self, item):
        z = self.here["z"] - item["z"]
        return (z >= 0) & (z <= 3)

    def step(self, index):
        item = self.items[index]

        @pl.when(self.valid(item))
        def _():
            if any(item.values()):
                self.arrived(index, item)
            for slot, way in enumerate(self.outward(item)):
                self.when_way(way, lambda way=way, slot=slot: self.copy(index, way, slot, item).start())
            self.copy(index, None, 0, item).start()

    def when_way(self, way, act):
        axis, step = way
        if axis == "z":
            z = self.here["z"] + step
            pl.when((z >= 0) & (z <= 3))(act)
        else:
            act()

    def arrived(self, index, item):
        place = self.origin(item)
        spot = self.full.at[number_of(place), self.part, :]
        pltpu.make_async_remote_copy(
            src_ref=spot,
            dst_ref=spot,
            send_sem=self.sends.at[index * 4],
            recv_sem=self.receives.at[self.key(place)],
            device_id=device_of(dict(self.here, c=1 - self.here["c"])),
            device_id_type=MESH,
        ).wait_recv()

    def finish(self):
        for index, item in enumerate(self.items):

            @pl.when(self.valid(item))
            def _(index=index, item=item):
                for slot, way in enumerate(self.outward(item)):
                    self.when_way(way, lambda way=way, slot=slot: self.copy(index, way, slot, item).wait_send())
                self.copy(index, None, 0, item).wait_send()
                place = dict(self.origin(item), c=1 - self.here["c"])
                spot = self.full.at[number_of(place), self.part, :]
                pltpu.make_async_remote_copy(
                    src_ref=spot,
                    dst_ref=spot,
                    send_sem=self.hands.at[index],
                    recv_sem=self.hands_got.at[self.key(place)],
                    device_id=device_of(dict(self.here, c=1 - self.here["c"])),
                    device_id_type=MESH,
                ).wait_recv()


ITEMS = 28


PICK = 64
GROUP = 16


def start_body(
    streams, shards, ids, low_ref, groups_any, fact, chunk, got, own_rows, facts, full_chunk,
    table, stage, rows,
    row_sends, row_gets, fact_sems, own_sems, sends, receives, hands, hands_got,
):
    here = position()
    me = number_of(here)
    across = device_of(dict(here, x=1 - here["x"]))
    half, hidden = own_rows.shape
    batches = half // PICK
    fill = pltpu.make_async_copy(groups_any, table, own_sems.at[0])
    fill.start()
    greet_all(shards)
    own = [
        pltpu.make_async_copy(source, target, own_sems.at[1 + k])
        for k, (source, target) in enumerate(((fact, facts.at[me]), (chunk, full_chunk.at[me])))
    ]
    for copy in own:
        copy.start()
    await_all(shards)
    gathers = [
        Gather(
            chunk, full_chunk, start, size, order, sends.at[k], receives.at[k], hands.at[k], hands_got.at[k]
        )
        for k, (start, size, order) in enumerate(streams)
    ]
    for gather in gathers:
        gather.step(0)
    spread(lambda peer: fact, facts, fact_sems, me, shards)

    def send_rows(b):
        part = pl.ds(b * PICK, PICK)
        return pltpu.make_async_remote_copy(
            src_ref=rows.at[part, :],
            dst_ref=got.at[part, :],
            send_sem=row_sends.at[b],
            recv_sem=row_gets.at[b],
            device_id=across,
            device_id_type=MESH,
        )

    def pick(b):
        @pl.loop(0, PICK // 8)
        def _(t):
            found = [table[ids[b * PICK + t * 8 + k]] for k in range(8)]
            stage[pl.ds(pl.multiple_of(t * 8, 8), 8)] = jnp.stack(found)

        choose = (
            lax.broadcasted_iota(jnp.int32, (PICK, PICK * GROUP), 1)
            == low_ref[b * PICK : (b + 1) * PICK, :]
        )
        rows[b * PICK : (b + 1) * PICK, :] = mm(choose.astype(F32).astype(BF), flat(stage)).astype(BF)
        if b < batches:
            send_rows(b).start()

    fill.wait()
    picked = 0
    for index in range(1, ITEMS):
        while picked < min(2 * batches, 2 + 3 * index):
            pick(picked)
            picked += 1
        for gather in gathers:
            gather.step(index)
    outs = [pltpu.make_async_copy(rows.at[pl.ds(half, half), :], own_rows, own_sems.at[3])]
    for copy in outs:
        copy.start()
    for gather in gathers:
        gather.finish()
    collect(facts, fact_sems, me, shards)
    for b in range(batches):
        send_rows(b).wait()
    for copy in own + outs:
        copy.wait()


def vocab_rows(table, like):
    here = position()
    count = like.shape[0]
    return table.at[pl.ds(pl.multiple_of((here["y"] * 2 + here["c"]) * count, 16), count), :]


def gather_sems(streams):
    sems = pltpu.SemaphoreType.DMA
    count = len(streams)
    return [sems((count, 4 * ITEMS)), sems((count, 16)), sems((count, ITEMS)), sems((count, 16))]


def streams_of(rows, parts):
    streams, start = [], 0
    for k, (order, share) in enumerate(parts):
        size = rows - start if k == len(parts) - 1 else round(rows * share / 16) * 16
        streams.append((start, size, order))
        start += size
    return streams


def start_exchange(ids, table, fact, chunk, shards):
    anywhere = pl.BlockSpec(memory_space=pl.ANY)
    shape = jax.ShapeDtypeStruct
    sems = pltpu.SemaphoreType.DMA
    streams = streams_of(chunk.shape[0], (("xzy", 0.5), ("zxy", 0.28), ("xyz", 0.22)))
    half, hidden = ids.shape[0] // 2, table.shape[1]
    low = jnp.arange(ids.size, dtype=jnp.int32) % PICK * GROUP + ids % GROUP
    return pl.pallas_call(
        functools.partial(start_body, streams, shards),
        in_specs=[
            pl.BlockSpec(memory_space=pltpu.SMEM),
            pl.BlockSpec(memory_space=pltpu.VMEM),
        ]
        + [anywhere] * 3,
        out_specs=[anywhere] * 4,
        out_shape=[
            shape((half, hidden), table.dtype),
            shape((half, hidden), table.dtype),
            shape((shards, *fact.shape), fact.dtype),
            shape((shards, *chunk.shape), chunk.dtype),
        ],
        scratch_shapes=[
            pltpu.VMEM((table.shape[0] // GROUP, GROUP, hidden), BF),
            pltpu.VMEM((PICK, GROUP, hidden), BF),
            pltpu.VMEM((2 * half, hidden), BF),
            sems((half // PICK,)),
            sems((half // PICK,)),
            sems((2,)),
            sems((4,)),
            *gather_sems(streams),
        ],
        compiler_params=params(collective_id=1, has_side_effects=True),
        name="start_exchange",
    )(ids // GROUP, low[:, None], table.reshape(-1, GROUP, hidden), fact, chunk)


def first_layer_body(
    streams, shards,
    own_any, got_any, first_any, chunk, table_any, code_ref, spots_ref, gain_ref, shift_ref, down_ref,
    adapt_ref, bias_ref, seg_ref, seg_row_ref,
    qkv_out, x_out, one_out, two_out, slope_out, wo_out, full_chunk, et_out, mid_ref, log_ref,
    own, got, in_slab, w, wo, up, dn, x, qkv, ctx, two, out, slope,
    e_in, et_stage, load_sems, tile_sems, out_sems, e_sems, et_sems, sends, receives, hands, hands_got,
):
    here = position()
    me = number_of(here)
    rows, hidden = x.shape
    tile = split_of(rows, 256, 16)
    tiles = rows // tile
    lanes = 2 * (hidden // HEADS)
    pairs = hidden // lanes

    def slab(source, target, start):
        return source.at[:, pl.ds(start, target.shape[1]), :]

    loads = [
        pltpu.make_async_copy(source, target, load_sems.at[k])
        for k, (source, target) in enumerate(
            (
                (own_any.at[pl.ds(0, rows), :], own),
                (got_any.at[pl.ds(0, rows), :], got),
                (slab(first_any, in_slab, 2 * up.shape[1]), in_slab),
                (slab(first_any, up, 0), up),
                (slab(first_any, dn, up.shape[1]), dn),
                (chunk, full_chunk.at[me]),
            )
        )
    ]
    for copy in loads:
        copy.start()
    barrier = pltpu.get_barrier_semaphore()
    peers = [
        dict(here, c=1 - here["c"]),
        dict(here, x=1 - here["x"]),
        dict(here, y=1 - here["y"]),
        *[dict(here, z=flip(here["z"], k)) for k in (1, 2, 3)],
    ]
    for peer in peers:
        pl.semaphore_signal(barrier, inc=1, device_id=device_of(peer), device_id_type=MESH)
    pl.semaphore_wait(barrier, len(peers))
    gathers = [
        Gather(
            chunk, full_chunk, start, size, order, sends.at[k], receives.at[k], hands.at[k], hands_got.at[k]
        )
        for k, (start, size, order) in enumerate(streams)
    ]
    def advance(first, last):
        for index in range(first, last + 1):
            for gather in gathers:
                gather.step(index)

    def at(i, plan):
        for k, ends in plan.items():
            pl.when(i == k)(functools.partial(advance, *ends))

    advance(0, 0)

    groups = pairs + tiles
    size = e_in.shape[1]
    here_rows = (here["y"] * 2 + here["c"]) * (groups * size)
    unit = (
        (lax.broadcasted_iota(jnp.int32, (256, 256), 0) == lax.broadcasted_iota(jnp.int32, (256, 256), 1))
        .astype(F32)
        .astype(BF)
    )

    def group_in(g):
        source = table_any.at[pl.ds(pl.multiple_of(here_rows + g * size, 16), size), :]
        return pltpu.make_async_copy(source, e_in.at[g % 2], e_sems.at[g])

    def group_out(g):
        target = et_out.at[:, pl.ds(pl.multiple_of(g * size, 128), size)]
        return pltpu.make_async_copy(et_stage.at[g % 2], target, et_sems.at[g])

    def turn_group(g):
        group_in(g).wait()

        @pl.when(g >= 2)
        def _():
            group_out(g - 2).wait()

        for k in range(0, hidden, 256):
            et_stage[g % 2, k : k + 256, :] = mm_nt(unit, e_in[g % 2, :, k : k + 256]).astype(BF)
        group_out(g).start()

        @pl.when(g + 2 < groups)
        def _():
            group_in(g + 2).start()

    group_in(0).start()
    group_in(1).start()
    for copy in loads[:3]:
        copy.wait()
    unpack_rows(in_slab, (w, wo))

    @pl.loop(0, tiles)
    def _(i):
        part = pl.ds(pl.multiple_of(i * tile, tile), tile)
        project_body(
            own.at[part, :], got.at[part, :], code_ref.at[part, :], spots_ref, gain_ref, shift_ref, down_ref, w,
            adapt_ref, bias_ref, qkv.at[part, :], mid_ref.at[part, :], x.at[part, :],
        )

        at(i, {tiles - 3: (1, 3), tiles - 1: (4, 5)})

    early = [
        pltpu.make_async_copy(qkv, qkv_out, out_sems.at[0]),
        pltpu.make_async_copy(wo, wo_out, out_sems.at[1]),
    ]
    for copy in early:
        copy.start()

    @pl.loop(0, pairs)
    def _(p):
        column = lambda kind: pl.ds(pl.multiple_of((kind * pairs + p) * lanes, lanes), lanes)
        attend_body(
            qkv.at[:, column(0)], qkv.at[:, column(1)], qkv.at[:, column(2)], seg_ref, seg_row_ref,
            ctx.at[:, column(0)], log_ref.at[pl.ds(p, 1)],
        )

        turn_group(p)
        at(p - (pairs - 6), {1: (6, 7), 3: (8, 9), 5: (10, 13)})

    for copy in loads[3:5]:
        copy.wait()

    def tile_copies(i):
        part = pl.ds(pl.multiple_of(i * tile, tile), tile)
        turn = i % 2
        return [
            pltpu.make_async_copy(source, target.at[part, :], tile_sems.at[k, i])
            for k, (source, target) in enumerate(
                (
                    (out.at[turn], x_out),
                    (two.at[turn], two_out),
                    (slope.at[turn], slope_out),
                    (x.at[part, :], one_out),
                )
            )
        ]

    plan = {0: (14, 16), 1: (17, 19), 2: (20, 23), 3: (24, 27)}

    @pl.loop(0, tiles)
    def _(i):
        part = pl.ds(pl.multiple_of(i * tile, tile), tile)
        turn = i % 2

        @pl.when(i >= 2)
        def _():
            for copy in tile_copies(i - 2):
                copy.wait()

        after_body(
            ctx.at[part, :], x.at[part, :], wo, up, dn, bias_ref, gain_ref, shift_ref, out.at[turn],
            x.at[part, :], two.at[turn], slope.at[turn],
        )
        for copy in tile_copies(i):
            copy.start()
        turn_group(pairs + i)
        at(i - (tiles - 4), plan)

    for gather in gathers:
        gather.finish()
    for i in (tiles - 2, tiles - 1):
        for copy in tile_copies(i):
            copy.wait()
    for copy in early + loads[5:] + [group_out(g) for g in (groups - 2, groups - 1)]:
        copy.wait()


def first_layer(own, got, first, chunk, table, more, shards):
    whole = pl.BlockSpec(memory_space=pltpu.VMEM)
    anywhere = pl.BlockSpec(memory_space=pl.ANY)
    down, seg_row = more[4], more[-1]
    rows, hidden = seg_row.shape[1], own.shape[1]
    tile = split_of(rows, 256, 16)
    pairs = HEADS // 2
    units = 4 * hidden
    each = units // shards
    count, groups = table.shape[0] // 4, pairs + rows // tile
    shape = jax.ShapeDtypeStruct
    sems = pltpu.SemaphoreType.DMA
    streams = streams_of(chunk.shape[0], (("zxy", 0.4), ("zyx", 0.4), ("xyz", 0.2)))
    return pl.pallas_call(
        functools.partial(first_layer_body, streams, shards),
        in_specs=[anywhere] * 5 + [whole] * len(more),
        out_specs=[anywhere] * 8 + [whole] * 2,
        out_shape=[
            shape((rows, 3 * hidden), BF),
            shape((rows, hidden), F32),
            shape((rows, hidden), F32),
            shape((rows, hidden), F32),
            shape((rows, units), BF),
            shape((hidden, hidden), BF),
            shape((shards, *chunk.shape), BF),
            shape((hidden, count), BF),
            shape((rows, down.shape[2]), BF),
            shape((pairs, 1, 2 * rows), F32),
        ],
        scratch_shapes=[
            pltpu.VMEM((rows, hidden), BF),
            pltpu.VMEM((rows, hidden), BF),
            pltpu.VMEM((shards, 4 * hidden // shards, hidden), BF),
            pltpu.VMEM((3 * hidden, hidden), BF),
            pltpu.VMEM((hidden, hidden), BF),
            pltpu.VMEM((shards, each, hidden), BF),
            pltpu.VMEM((shards, each, hidden), BF),
            pltpu.VMEM((rows, hidden), F32),
            pltpu.VMEM((rows, 3 * hidden), BF),
            pltpu.VMEM((rows, hidden), BF),
            pltpu.VMEM((2, tile, hidden), F32),
            pltpu.VMEM((2, tile, hidden), F32),
            pltpu.VMEM((2, tile, units), BF),
            pltpu.VMEM((2, count // groups, hidden), BF),
            pltpu.VMEM((2, hidden, count // groups), BF),
            sems((6,)),
            sems((4, rows // tile)),
            sems((2,)),
            sems((groups,)),
            sems((groups,)),
            *gather_sems(streams),
        ],
        compiler_params=params(collective_id=3, has_side_effects=True),
        name="first_layer",
    )(own, got, first, chunk, table, *more)


def adam(weight, gradient, moment_one, moment_two, fade_one, fade_two):
    moment_one = beta_first * moment_one + (1.0 - beta_first) * gradient
    moment_two = beta_second * moment_two + (1.0 - beta_second) * gradient * gradient
    one_hat = moment_one / fade_one
    two_hat = moment_two / fade_two
    weight = weight - learn_rate * (one_hat / (jnp.sqrt(two_hat) + adam_eps) + decay_rate * weight)
    return (weight, moment_one, moment_two)


BACK_TILE = 256


def finish_body(
    shards, edge,
    dout_any, one_any, two_any, slope_any, wo_any, first_any, qkv_any, gain_ref, log_ref, seg_ref,
    seg_row_ref, mid_ref, parts, late_ref, facts,
    sums_ref, dense_ref, total_ref,
    dout, one, two, slope, wo, up, dn, qkv, dctx, dv, grad, core_got, chip_sum, dense_got, grad_got, note, notes,
    tile_sems, load_sems, core_sems, dense_sems, grad_sems, note_sems,
):
    rows, hidden = dout.shape
    tile = split_of(rows, BACK_TILE, 16)
    tiles = rows // tile
    me = number_of(position())

    def tile_loads(i):
        part = pl.ds(pl.multiple_of(i * tile, tile), tile)
        return [
            pltpu.make_async_copy(source.at[part, :], target.at[part, :], tile_sems.at[k, i])
            for k, (source, target) in enumerate(
                ((two_any, two), (dout_any, dout), (slope_any, slope), (one_any, one))
            )
        ]

    here = position()
    chips = shards // 2
    chip, core = me // 2, here["c"]
    to_core = pltpu.make_async_remote_copy(
        src_ref=parts.at[:, 1 - core],
        dst_ref=core_got,
        send_sem=core_sems.at[0],
        recv_sem=core_sems.at[1],
        device_id=device_of(dict(here, c=1 - core)),
        device_id_type=MESH,
    )

    def to_chip(k):
        peer = (chip + k) % chips
        return pltpu.make_async_remote_copy(
            src_ref=chip_sum.at[peer],
            dst_ref=dense_got.at[chip],
            send_sem=dense_sems.at[0],
            recv_sem=dense_sems.at[1],
            device_id=rank_device(2 * peer + core),
            device_id_type=MESH,
        )

    loads = [
        pltpu.make_async_copy(source, target, load_sems.at[k])
        for k, (source, target) in enumerate(
            (
                (first_any.at[:, pl.ds(up.shape[1], dn.shape[1]), :], dn),
                (first_any.at[:, pl.ds(0, up.shape[1]), :], up),
                (wo_any, wo),
                (qkv_any, qkv),
            )
        )
    ]
    for copy in tile_loads(0) + loads[:3]:
        copy.start()
    for i in range(1, tiles):
        for copy in tile_loads(i):
            copy.start()
    loads[3].start()
    greet_all(shards)
    for copy in loads[:3]:
        copy.wait()

    @pl.loop(0, tiles)
    def _(i):
        for copy in tile_loads(i):
            copy.wait()
        part = pl.ds(pl.multiple_of(i * tile, tile), tile)
        after_back_body(
            dout.at[part, :], one.at[part, :], two.at[part, :], slope.at[part, :], wo, up, dn, gain_ref,
            dctx.at[part, :],
        )

        @pl.when(i == 0)
        def _():
            await_all(shards)
            to_core.start()

        @pl.when(i == 1)
        def _():
            to_core.wait_recv()

            @pl.loop(0, chips)
            def _(k):
                chip_sum[k] = (parts[k, core].astype(F32) + core_got[k].astype(F32)).astype(BF)

            dense_got[chip] = chip_sum[chip]

            @pl.loop(1, chips)
            def _(k):
                to_chip(k).start()

    loads[3].wait()
    lanes = 2 * (hidden // HEADS)
    pairs = hidden // lanes

    @pl.loop(0, pairs)
    def _(p):
        column = lambda kind: pl.ds(pl.multiple_of((kind * pairs + p) * lanes, lanes), lanes)
        attend_back_body(
            qkv.at[:, column(0)], qkv.at[:, column(1)], qkv.at[:, column(2)], dctx.at[:, column(0)],
            log_ref.at[pl.ds(p, 1)], seg_ref, seg_row_ref, mid_ref, grad.at[column(0), :], dv, edge=edge,
        )

    grad[...] = grad[...] + late_ref[...]
    each = hidden // shards
    piece = lambda peer: grad.at[pl.ds(pl.multiple_of(peer * each, each), each), :]
    grad_got[me] = piece(me)[...]
    spread(piece, grad_got, grad_sems, me, shards)
    others = chip_sum.at[pl.ds(0, chips - 1)]
    every = pltpu.make_async_remote_copy(
        src_ref=others,
        dst_ref=dense_got.at[pl.ds(0, chips - 1)],
        send_sem=dense_sems.at[0],
        recv_sem=dense_sems.at[1],
        device_id=device_of(dict(here, c=1 - core)),
        device_id_type=MESH,
    )
    every.wait_recv()
    every.wait_send()
    to_core.wait_send()
    dense = jnp.zeros((each, hidden), F32)
    for k in range(chips):
        dense = dense + dense_got[k].astype(F32)[:each, :]
    dense_ref[...] = dense
    square = jnp.sum(dense * dense, keepdims=True)
    collect(grad_got, grad_sems, me, shards)
    total = grad_got[0]
    for k in range(1, shards):
        total = total + grad_got[k]
    total_ref[...] = total
    square = square + jnp.sum(total * total, keepdims=True)
    row = lax.broadcasted_iota(jnp.int32, note.shape, 0)
    note[...] = jnp.where(row == 0, facts[...], jnp.where(row == 1, square, 0.0))
    notes[me] = note[...]
    spread(lambda peer: note, notes, note_sems, me, shards)
    collect(notes, note_sems, me, shards)
    sums = notes[0]
    for k in range(1, shards):
        sums = sums + notes[k]
    sums_ref[...] = sums


def update_body(
    sums_ref, dense_ref, total_ref, facts, head_w, head_m, head_v, adapt_w, adapt_m, adapt_v,
    loss_out, norm_out, head_w_out, head_m_out, head_v_out, adapt_w_out, adapt_m_out, adapt_v_out,
):
    norm = jnp.sqrt(sums_ref[1:2, 0:1])
    loss_out[...] = sums_ref[0:1, 0:1]
    norm_out[...] = norm
    factor = jnp.minimum(1.0, clip_limit / (norm + 1e-06))
    fades = facts[1:2, 0:1], facts[2:3, 0:1]
    new = adam(head_w[...], dense_ref[...] * factor, head_m[...], head_v[...], *fades)
    head_w_out[...], head_m_out[...], head_v_out[...] = new
    grad = (total_ref[...] * factor).T
    layers, kinds, rank, unused = adapt_w.shape
    for layer in range(layers):
        for kind in range(kinds):
            at = (layer * kinds + kind) * rank
            new = adam(
                adapt_w[layer, kind], grad[at : at + rank], adapt_m[layer, kind], adapt_v[layer, kind], *fades
            )
            adapt_w_out[layer, kind], adapt_m_out[layer, kind], adapt_v_out[layer, kind] = new


def update(sums, dense, total, facts, heads, adapts):
    whole = pl.BlockSpec(memory_space=pltpu.VMEM)
    shape = jax.ShapeDtypeStruct
    return pl.pallas_call(
        update_body,
        in_specs=[whole] * 10,
        out_specs=[whole] * 8,
        out_shape=[shape((1, 1), F32)] * 2 + [shape(a.shape, F32) for a in (*heads, *adapts)],
        compiler_params=params(),
        name="update",
    )(sums, dense, total, facts, *heads, *adapts)


def finish(back, qkv, logs, seg_wide, seg_row, mid, parts, late, facts, edge, shards):
    dout, one, two, slope, wo, first, gains = back
    slab = pltpu.VMEM((shards, slope.shape[1] // shards, dout.shape[1]), BF)
    parts = parts.reshape(-1, 2, *parts.shape[1:])
    rows, hidden = dout.shape
    each = hidden // shards
    whole = pl.BlockSpec(memory_space=pltpu.VMEM)
    anywhere = pl.BlockSpec(memory_space=pl.ANY)
    shape = jax.ShapeDtypeStruct
    sems = pltpu.SemaphoreType.DMA
    tiles = rows // split_of(rows, BACK_TILE, 16)
    return pl.pallas_call(
        functools.partial(finish_body, shards, edge),
        in_specs=[anywhere] * 7 + [whole] * 8,
        out_specs=[whole] * 3,
        out_shape=[
            shape((8, 128), F32),
            shape((each, hidden), F32),
            shape((each, late.shape[1]), F32),
        ],
        scratch_shapes=[
            pltpu.VMEM((rows, hidden), F32),
            pltpu.VMEM((rows, hidden), F32),
            pltpu.VMEM((rows, hidden), F32),
            pltpu.VMEM(slope.shape, BF),
            pltpu.VMEM(wo.shape, BF),
            slab,
            slab,
            pltpu.VMEM(qkv.shape, BF),
            pltpu.VMEM((rows, hidden), BF),
            pltpu.VMEM((rows, 2 * (hidden // HEADS)), F32),
            pltpu.VMEM(late.shape, F32),
            pltpu.VMEM((shards // 2, *parts.shape[2:]), BF),
            pltpu.VMEM((shards // 2, *parts.shape[2:]), BF),
            pltpu.VMEM((shards // 2, *parts.shape[2:]), BF),
            pltpu.VMEM((shards, each, late.shape[1]), F32),
            pltpu.VMEM((8, 128), F32),
            pltpu.VMEM((shards, 8, 128), F32),
            sems((4, tiles)),
            sems((4,)),
            sems((2,)),
            sems((2,)),
            sems((2,)),
            sems((2,)),
        ],
        compiler_params=params(collective_id=2, has_side_effects=True),
        name="finish",
    )(dout, one, two, slope, wo, first, qkv, gains, logs, seg_wide, seg_row, mid, parts, late, facts)


LOG_ROWS = 16


def flip(z, k):
    return (z % 2 + k % 2) % 2 + 2 * ((z // 2 + k // 2) % 2)


def pack_log(log_row, rows):
    high = log_row.astype(BF).astype(F32)
    middle = (log_row - high).astype(BF).astype(F32)
    low = log_row - high - middle
    row = lax.broadcasted_iota(jnp.int32, (rows, log_row.shape[1]), 0)
    return jnp.where(
        row == 0, high, jnp.where(row == 1, middle, jnp.where(row == 2, low, 0.0))
    ).astype(BF)


def unpack(block, hidden):
    logs = block[hidden : hidden + LOG_ROWS, :].astype(F32)
    return block[:hidden, :].astype(F32), jnp.sum(logs, 0, keepdims=True)


def merged(one, two):
    top = jnp.maximum(one[1], two[1])
    first, second = jnp.exp(one[1] - top), jnp.exp(two[1] - top)
    total = first + second
    inverse = 1.0 / total
    return one[0] * (first * inverse) + two[0] * (second * inverse), top + jnp.log(total)


def store_packed(ref, pair, hidden):
    ref[:hidden, :] = pair[0].astype(BF)
    ref[hidden : hidden + LOG_ROWS, :] = pack_log(pair[1], LOG_ROWS)


def head_body(
    u_ref, bias_ref, table_any, et_any, mean_ref, log_ref,
    e_ref, et_ref, bias_wide, feats, packs, handed, sums,
    loads, far_send, far_get, hand_send, hand_get, part_send, part_get, sum_send, sum_get,
):
    here = position()
    x, y, c = here["x"], here["y"], here["c"]
    labels, hidden = u_ref.shape
    sibling = device_of(dict(here, c=1 - c))

    def chip_at(k):
        return (x + k % 2) % 2, (y + k // 2) % 2

    def device_at(k):
        there = chip_at(k)
        return device_of(dict(here, x=there[0], y=there[1]))

    def slot(k, core):
        there = chip_at(k)
        return (there[0] * 2 + there[1]) * 2 + core

    fills = [
        pltpu.make_async_copy(source, target, loads.at[k])
        for k, (source, target) in enumerate(
            ((vocab_rows(table_any, e_ref), e_ref), (et_any, et_ref))
        )
    ]
    for fill in fills:
        fill.start()
    barrier = pltpu.get_barrier_semaphore()
    for target in (sibling, *[device_at(k) for k in (1, 2, 3)]):
        pl.semaphore_signal(barrier, inc=1, device_id=target, device_id_type=MESH)
    feats[slot(0, c)] = u_ref[...]
    pl.semaphore_wait(barrier, 4)

    def move(place, device, send, get):
        return pltpu.make_async_remote_copy(
            src_ref=feats.at[place],
            dst_ref=feats.at[place],
            send_sem=send,
            recv_sem=get,
            device_id=device,
            device_id_type=MESH,
        )

    def far(k):
        return move(slot(0, c), device_at(k), far_send.at[k], far_get.at[k])

    def far_here(k):
        return move(slot(k, c), device_at(k), far_send.at[k], far_get.at[k])

    def hand(k, core):
        return move(slot(k, core), sibling, hand_send.at[k], hand_get.at[k])

    for k in (1, 2, 3):
        far(k).start()
    hand(0, c).start()

    @pl.loop(0, bias_ref.shape[0])
    def _(b):
        row = jnp.broadcast_to(bias_ref[pl.ds(b, 1), :], (128, 128))
        bias_wide[pl.ds(pl.multiple_of(b * 128, 128), 128), :] = row.T

    for k in (1, 2, 3):
        far_here(k).wait_recv()
        hand(k, c).start()
    for fill in fills:
        fill.wait()
    count = e_ref.shape[0]
    steps = 4

    def target_of(s):
        return (s + 1) % steps

    def hand_part(s):
        return pltpu.make_async_remote_copy(
            src_ref=packs.at[s, 1 - c],
            dst_ref=handed.at[s],
            send_sem=part_send.at[s],
            recv_sem=part_get.at[s],
            device_id=sibling,
            device_id_type=MESH,
        )

    def sum_part(s):
        return pltpu.make_async_remote_copy(
            src_ref=packs.at[s, c],
            dst_ref=sums.at[s],
            send_sem=sum_send.at[s],
            recv_sem=sum_get.at[s],
            device_id=device_at(target_of(s)),
            device_id_type=MESH,
        )

    def together(s):
        hand_part(s).wait_recv()
        return merged(unpack(packs[s, c], hidden), unpack(handed[s], hidden))

    def settle(s):
        store_packed(packs.at[s, c], together(s), hidden)
        sum_part(s).start()

    @pl.loop(0, steps)
    def _(s):
        k = target_of(s)
        hand(k, 1 - c).wait_recv()
        u = feats[pl.ds(slot(k, 0), 2)].reshape(2 * labels, hidden)
        top = total = mean = None

        def scored(start):
            part = slice(start, min(start + 1280, count))
            bias = bias_wide[part, :]
            return mm_nt(e_ref[part, :], u) + jnp.concatenate([bias, bias], 1)

        @pl.when(s > 0)
        def _():
            settle(s - 1)

        logits = scored(0)
        for start in range(0, count, 1280):
            part = slice(start, min(start + 1280, count))
            later = scored(start + 1280) if start + 1280 < count else None
            high = jnp.max(logits, 0, keepdims=True)
            new = high if top is None else jnp.maximum(top, high)
            grown = jnp.exp(logits - new)
            part_sums = jnp.sum(grown, 0, keepdims=True)
            product = mm(et_ref[:, part], grown.astype(BF))
            if top is None:
                total, mean = part_sums, product
            else:
                shrink = jnp.exp(top - new)
                total, mean = total * shrink + part_sums, mean * shrink + product
            top = new
            logits = later
        mean = mean * (1.0 / total)
        logs = top + jnp.log(total)
        for core in range(2):
            half = slice(core * labels, (core + 1) * labels)
            packs[s, core, :hidden, :] = mean[:, half].astype(BF)
            packs[s, core, hidden : hidden + LOG_ROWS, :] = pack_log(logs[:, half], LOG_ROWS)
        hand_part(s).start()

    total = together(steps - 1)
    for s in range(steps - 1):
        sum_part(s).wait_recv()
        total = merged(total, unpack(sums[s], hidden))
    mean_ref[...] = total[0]
    log_ref[...] = total[1]
    for k in (1, 2, 3):
        far(k).wait_send()
    for k in range(4):
        hand(k, c).wait_send()
    for s in range(steps):
        hand_part(s).wait_send()
    for s in range(steps - 1):
        sum_part(s).wait_send()


def head(u, bias, table, et):
    labels, hidden = u.shape
    whole = pl.BlockSpec(memory_space=pltpu.VMEM)
    anywhere = pl.BlockSpec(memory_space=pl.ANY)
    shape = jax.ShapeDtypeStruct
    sems = pltpu.SemaphoreType.DMA
    block = (hidden + LOG_ROWS, labels)
    count = et.shape[1]
    return pl.pallas_call(
        head_body,
        in_specs=[whole] * 2 + [anywhere] * 2,
        out_specs=[whole] * 2,
        out_shape=[shape((hidden, labels), F32), shape((1, labels), F32)],
        scratch_shapes=[
            pltpu.VMEM((count, hidden), BF),
            pltpu.VMEM((hidden, count), BF),
            pltpu.VMEM((count, 128), F32),
            pltpu.VMEM((8, labels, hidden), BF),
            pltpu.VMEM((4, 2, *block), BF),
            pltpu.VMEM((4, *block), BF),
            pltpu.VMEM((4, *block), BF),
            sems((2,)),
        ]
        + [sems((4,))] * 8,
        compiler_params=params(collective_id=4, has_side_effects=True),
        name="head",
    )(u, bias, table, et)


def seg_positions(segments):
    index = jnp.arange(segments.shape[-1], dtype=jnp.int32)
    fresh = jnp.concatenate([jnp.ones((1,), dtype=bool), segments[1:] != segments[:-1]], -1)
    starts = lax.cummax(jnp.where(fresh, index, jnp.zeros_like(index)), axis=0)
    return index - starts


def pad_rows(matrix, multiple):
    return jnp.pad(matrix, ((0, -matrix.shape[0] % multiple), (0, 0)))


def slab_of(gathered, start, rows):
    if rows % 16 == 0 and start % rows == 0:
        return (gathered, start // rows, rows)
    part = gathered[:, start : start + rows].reshape(1, -1, gathered.shape[2])
    return (part, 0, part.shape[1])


def per_device(
    input_token_index,
    sentence_numbers,
    label_positions,
    label_target_token,
    sequence_task_index,
    task_loss_weight,
    optimizer_step_count,
    embed,
    position_embedding,
    norm_gain_vector,
    norm_bias_vector,
    attention_in_weight,
    attention_out_weight,
    feedforward_up,
    feedforward_down,
    layer_bias_vector,
    head_dense_bias,
    vocabulary_bias,
    adapter_down_matrix,
    adapter_up_matrix,
    adapter_moment_first,
    adapter_moment_second,
    head_projection,
    head_moment_first,
    head_moment_second,
):
    shards = lax.axis_size("dp") * lax.axis_size("fsdp")
    dp_index = lax.axis_index("dp")
    fsdp_index = lax.axis_index("fsdp")
    layers, unused, rank, up_part = adapter_up_matrix.shape
    hidden = embed.shape[1]
    tokens = input_token_index.shape[1]
    labels = label_positions.shape[1]
    qkv_rows = attention_in_weight.shape[2]
    out_rows = attention_out_weight.shape[2]
    ff_rows = feedforward_up.shape[2]
    head_rows = head_projection.shape[0]

    grouped = (lax.axis_size("dp"), lax.axis_size("fsdp")) == (2, 16)
    feeds = [[feedforward_up[layer].T, feedforward_down[layer]] for layer in range(layers)]
    attends = [[attention_in_weight[layer].T, attention_out_weight[layer].T] for layer in range(layers)]
    first_chunk = jnp.concatenate(feeds[0] + attends[0], 0)
    last_chunk = pad_rows(
        jnp.concatenate([feeds[1][0], *attends[1], head_projection.astype(BF)], 0), 32
    )
    last_feed = feeds[1][1]

    table_rows = embed.shape[0]
    wanted = jnp.concatenate([input_token_index[0], label_target_token[0]])
    dp_count = lax.axis_size("dp")
    group_ids = lax.all_gather(wanted, "dp", axis=0, tiled=False) - dp_index * table_rows
    inside = (group_ids >= 0) & (group_ids < table_rows)
    group_ids = jnp.clip(group_ids, 0, table_rows - 1)
    mine = lax.dynamic_index_in_dim(inside, dp_index, 0, keepdims=False)

    task_range = jnp.arange(TASKS, dtype=jnp.int32)
    slice_rows = vocabulary_bias.shape[0]
    ups = adapter_up_matrix.reshape(-1)
    if grouped:
        pair_ids = jnp.concatenate(
            [
                lax.dynamic_index_in_dim(group_ids, (dp_index + shift) % 2, 0, keepdims=False)
                for shift in (1, 0)
            ]
        )
        fact = jnp.concatenate([vocabulary_bias, ups, sequence_task_index.astype(F32)])
        fact_rows = -(-fact.size // 1024) * 8
        got, own_rows, facts, first_full = start_exchange(
            pair_ids,
            embed,
            jnp.pad(fact, (0, fact_rows * 128 - fact.size)).reshape(fact_rows, 128),
            first_chunk,
            shards,
        )
        facts, last_feed = lax.optimization_barrier((facts, last_feed))
        facts = facts.reshape(shards, -1)
        all_bias = facts[:, :slice_rows].reshape(-1)
        every_up = facts[:, slice_rows : slice_rows + ups.size]
        every_task = facts[:, slice_rows + ups.size].astype(jnp.int32)
    else:
        looked = jnp.where(
            inside.reshape(-1)[:, None], embed[group_ids.reshape(-1)], jnp.zeros((), BF)
        )
        own_rows = got = lax.psum_scatter(looked, "dp", scatter_dimension=0, tiled=True)
        all_bias = lax.all_gather(vocabulary_bias, BOTH, axis=0, tiled=True)
        every_up = lax.all_gather(ups, BOTH, axis=0, tiled=False)
        every_task = lax.all_gather(sequence_task_index, BOTH, axis=0, tiled=True)
    counts = labels * jnp.sum((every_task[:, None] == task_range[None, :]).astype(F32), 0)
    task_hot = (sequence_task_index[:, None] == task_range[None, :]).astype(F32)
    row_weight = jnp.sum(task_hot[0] * (task_loss_weight / jnp.maximum(counts, 1.0)))
    ups_full = (
        every_up.astype(BF)
        .reshape(shards, layers, 2, rank, up_part)
        .transpose(1, 2, 3, 0, 4)
        .reshape(layers, 2, rank, hidden)
    )
    blank = jnp.zeros((rank, hidden), BF)
    spare = lambda rows: jnp.zeros((rows, 3 * hidden), BF)
    adapters = jnp.stack(
        [
            jnp.concatenate(
                [
                    spare(2 * rank * layer),
                    jnp.concatenate([2 * ups_full[layer, 0], blank, blank], 1),
                    jnp.concatenate([blank, blank, 2 * ups_full[layer, 1]], 1),
                    spare(128 - 2 * rank * (layer + 1)),
                ],
                0,
            )
            for layer in range(layers)
        ]
    )
    downs = jnp.stack(
        [
            jnp.pad(
                jnp.concatenate([adapter_down_matrix[layer, 0], adapter_down_matrix[layer, 1]], 1),
                ((0, 0), (2 * rank * layer, 128 - 2 * rank * (layer + 1))),
            )
            for layer in range(layers)
        ]
    )
    segments = sentence_numbers[0]
    code = (jnp.pad(2 * seg_positions(segments), (0, labels)) + mine.astype(jnp.int32))[:, None]
    seg_real = segments.astype(F32)
    seg_wide = jnp.broadcast_to(seg_real[:, None], (tokens, 128))
    seg_row = seg_real[None, :]
    place_row = label_positions
    place_col = jnp.broadcast_to(label_positions.reshape(labels, 1), (labels, 128))

    target_bias = all_bias[label_target_token[0]]

    gains, shifts = norm_gain_vector, norm_bias_vector
    last_inputs = (place_col, place_row, seg_wide, downs, adapters, layer_bias_vector)
    in_start = ff_rows
    last_dn = lax.all_gather(last_feed, BOTH, axis=0, tiled=False)
    slabs_of = lambda up_full, dn_full: (slab_of(up_full, 0, ff_rows), slab_of(dn_full, 0, ff_rows))
    if grouped:
        more = (
            code, position_embedding, gains, shifts, downs, adapters, layer_bias_vector, seg_wide, seg_row,
        )
        qkv, x_last, one, two, slope, out_first, last_full, own_turned, mid, logs = first_layer(
            own_rows, got, first_full, last_chunk, embed, more, shards
        )
        slabs = [None, slabs_of(last_full, last_dn)]
        *saved, in_last, out_last, head_full = last_forward(
            x_last, *last_inputs, (last_full,), (in_start, in_start + qkv_rows + out_rows), *slabs[1], gains,
            shifts, head_dense_bias[None, :],
        )
        count = own_turned.shape[1]
        own_bias = lax.dynamic_slice_in_dim(
            all_bias, dp_index * table_rows + fsdp_index % 4 * count, count, 0
        ).reshape(-1, 128)
        mean_t, own_logs = head(saved[-1], own_bias, embed, own_turned)
    else:
        first_full = lax.all_gather(first_chunk, BOTH, axis=0, tiled=False)
        last_full = lax.all_gather(last_chunk, BOTH, axis=0, tiled=False)
        slabs = [
            (slab_of(first_full, 0, ff_rows), slab_of(first_full, ff_rows, ff_rows)),
            slabs_of(last_full, last_dn),
        ]
        taken = lambda full_chunk, start, size: full_chunk[:, start : start + size].reshape(-1, hidden)
        in_first = taken(first_full, 2 * ff_rows, qkv_rows)
        out_first = taken(first_full, 2 * ff_rows + qkv_rows, out_rows)
        in_last = taken(last_full, in_start, qkv_rows)
        out_last = taken(last_full, in_start + qkv_rows, out_rows)
        head_full = taken(last_full, in_start + qkv_rows + out_rows, head_rows)
        qkv, mid, hidden_rows = project(
            own_rows, got, code, position_embedding, gains, shifts, downs, in_first, adapters, layer_bias_vector, tokens
        )
        context, logs = attend(qkv, seg_wide, seg_row)
        x_last, one, two, slope = after(
            context, hidden_rows, out_first, *slabs[0], layer_bias_vector, gains, shifts
        )
        saved = last_forward(
            x_last, *last_inputs, (in_last, out_last, head_full), None, *slabs[1], gains, shifts,
            head_dense_bias[None, :],
        )
        features = saved[-1]
        own_slice = lax.dynamic_slice_in_dim(embed, fsdp_index * slice_rows, slice_rows, 0)
        own_vocab = jnp.concatenate(
            [own_slice]
            + [
                lax.ppermute(
                    own_slice, "dp", [(k, (k + shift) % dp_count) for k in range(dp_count)]
                )
                for shift in range(1, dp_count)
            ],
            0,
        )
        own_bias = jnp.concatenate(
            [
                lax.dynamic_slice_in_dim(
                    all_bias,
                    ((dp_index - shift) % dp_count) * table_rows + fsdp_index * slice_rows,
                    slice_rows,
                    0,
                )
                for shift in range(dp_count)
            ]
        )
        bias_wide = jnp.broadcast_to(own_bias[:, None], (own_bias.shape[0], 128))
        every = lax.all_gather(features, "fsdp", axis=0, tiled=True)
        means, local_logs = vocab(every, own_vocab, own_vocab.T, bias_wide, labels)
        local_logs = local_logs.reshape(-1, labels)
        all_logs = lax.all_gather(local_logs, "fsdp", axis=0, tiled=False)
        whole_logs = jax.nn.logsumexp(all_logs, axis=0)
        scaled = (means * jnp.exp(local_logs - whole_logs)[:, None, :]).astype(BF)
        mean_t = lax.psum_scatter(scaled, "fsdp", scatter_dimension=0, tiled=True)[0].astype(F32)
        own_logs = lax.dynamic_index_in_dim(whole_logs, fsdp_index, 0, keepdims=False)
        own_logs = own_logs[None, :]

    step_as_real = optimizer_step_count[0].astype(F32)
    fades = (1.0 - beta_first**step_as_real, 1.0 - beta_second**step_as_real)
    lanes = lambda value: jnp.pad(
        jnp.broadcast_to(value, (1, value.size if value.ndim else 128)), ((0, 0), (0, 128))
    )[:, :128]
    facts = jnp.concatenate(
        [lanes(value) for value in (row_weight, *fades, target_bias)] + [jnp.zeros((4, 128), F32)]
    )
    hidden_grad, dense_gradient, late, facts = last_backward(
        mean_t, own_logs, own_rows, got, code, facts, saved, place_col, place_row, seg_wide, downs, in_last, adapters,
        out_last, *slabs[1], gains, head_full, 3 * rank, shards if grouped else None,
    )
    back = (hidden_grad, one, two, slope, out_first)
    adapts = (adapter_up_matrix, adapter_moment_first, adapter_moment_second)
    heads = (head_projection, head_moment_first, head_moment_second)
    if grouped:
        sums, dense_portion, adapter_portion = finish(
            (*back, first_full, gains), qkv, logs, seg_wide, seg_row, mid, dense_gradient, late, facts, rank, shards
        )
        loss, norm, *new = update(sums, dense_portion, adapter_portion, facts, heads, adapts)
        return (loss[0, 0], norm[0, 0], *new[3:], *new[:3])
    dctx = after_back(*back, *slabs[0], gains)
    first = attend_back(qkv, dctx, logs, seg_wide, seg_row, mid, rank)
    adapter_gradient = (first + late)[:, : 2 * rank * layers].T.reshape(layers, 2, rank, hidden)
    dense_portion = lax.psum_scatter(dense_gradient, BOTH, scatter_dimension=0, tiled=True)
    adapter_portion = lax.psum_scatter(adapter_gradient, BOTH, scatter_dimension=3, tiled=True)
    squared_entries = jnp.sum(adapter_portion * adapter_portion) + jnp.sum(dense_portion * dense_portion)
    masked_task_loss, norm_square = lax.psum((facts[0, 0], squared_entries), BOTH)
    gradient_norm = jnp.sqrt(norm_square)
    factor = jnp.minimum(1.0, clip_limit / (gradient_norm + 1e-06))
    adapter_new = adam(adapts[0], adapter_portion * factor, *adapts[1:], *fades)
    dense_new = adam(heads[0], dense_portion * factor, *heads[1:], *fades)
    return (masked_task_loss, gradient_norm, *adapter_new, *dense_new)


def solution(mesh):
    rows = P(BOTH, None)
    in_specs = (
        rows,
        rows,
        rows,
        rows,
        P(BOTH),
        P(),
        P(),
        P("dp", None),
        P(),
        P(),
        P(),
        P(None, None, BOTH),
        P(None, None, BOTH),
        P(None, None, BOTH),
        P(None, BOTH, None),
        P(),
        P(),
        P(BOTH),
        P(),
        P(None, None, None, BOTH),
        P(None, None, None, BOTH),
        P(None, None, None, BOTH),
        rows,
        rows,
        rows,
    )
    adapter = P(None, None, None, BOTH)
    out_specs = (P(), P(), adapter, adapter, adapter, rows, rows, rows)
    return jax.shard_map(
        per_device, mesh=mesh, in_specs=in_specs, out_specs=out_specs, check_vma=False
    )
```

```python
import functools

import jax
import jax.numpy as jnp
from jax import lax
from jax.experimental import pallas as pl
from jax.experimental.pallas import tpu as pltpu
from jax.sharding import PartitionSpec as P

HEADS = 12
TASKS = 4
REACH = 128

norm_eps = 1e-05
adapter_scale = 2.0
clip_limit = 0.01
learn_rate = 0.05
beta_first = 0.9
beta_second = 0.999
adam_eps = 1e-08
decay_rate = 0.01
masked_score = -1e30

BF = jnp.bfloat16
F32 = jnp.float32
BOTH = ("dp", "fsdp")
VMEM_BYTES = 60 * 1024 * 1024


def mm(a, b):
    return lax.dot_general(a, b, (((1,), (0,)), ((), ())), preferred_element_type=F32)


def mm_nt(a, b):
    return lax.dot_general(a, b, (((1,), (1,)), ((), ())), preferred_element_type=F32)


def mm_tn(a, b):
    return lax.dot_general(a, b, (((0,), (0,)), ((), ())), preferred_element_type=F32)


def layer_norm(rows_in, gain, shift):
    center = rows_in - jnp.mean(rows_in, -1, keepdims=True)
    spread = jnp.mean(center * center, -1, keepdims=True)
    return center * lax.rsqrt(spread + norm_eps) * gain + shift


def norm_back(rows_in, gain, gradient):
    center = rows_in - jnp.mean(rows_in, -1, keepdims=True)
    inverse = lax.rsqrt(jnp.mean(center * center, -1, keepdims=True) + norm_eps)
    unit = center * inverse
    scaled = gradient * gain
    return inverse * (
        scaled
        - jnp.mean(scaled, -1, keepdims=True)
        - unit * jnp.mean(scaled * unit, -1, keepdims=True)
    )


def gelu_pair(v):
    size = jnp.abs(v) * 0.7071067811865476
    base = 1.0 + 0.3275911 * size
    t = pl.reciprocal(base, approx=True)
    t = t * (2.0 - base * t)
    bell = jnp.exp(-0.5 * v * v)
    poly = t * (
        0.127414796 + t * (-0.142248368 + t * (0.7107068705 + t * (-0.7265760135 + t * 0.5307027145)))
    )
    tail = poly * bell
    phi = jnp.where(v >= 0.0, 1.0 - tail, tail)
    return v * phi, phi + v * (bell * 0.3989422804014327)


def params(**more):
    return pltpu.CompilerParams(vmem_limit_bytes=VMEM_BYTES, **more)


def full(shape):
    return pl.BlockSpec(shape, lambda *_: (0,) * len(shape))


def split_of(total, most, step):
    size = (min(most, total) // step) * step
    while size > step and total % size:
        size -= step
    return size if size and total % size == 0 else total


def pair_rows(block, width):
    first = lax.broadcasted_iota(jnp.int32, block.shape, 1) < width
    return jnp.concatenate([jnp.where(first, block, 0.0), jnp.where(first, 0.0, block)], 0).astype(BF)


def pair_join(wide, width):
    rows = wide.shape[1] // 2
    return jnp.concatenate([wide[:width, :rows], wide[width:, rows:]], 0)


def masked(scores, same):
    rows = scores.shape[1] // 2
    return jnp.concatenate(
        [
            jnp.where(same, scores[:, :rows], masked_score),
            jnp.where(same, scores[:, rows:], masked_score),
        ],
        1,
    )


def qkv_bias(bias_ref, layer, start, size):
    hidden = bias_ref.shape[1] // 8
    if start >= 2 * hidden:
        return bias_ref[layer : layer + 1, start - hidden : start - hidden + size]
    return bias_ref[layer : layer + 1, start : start + size] if start < hidden else 0.0


def norm_of(norm_refs, k):
    return norm_refs[0][k : k + 1, :], norm_refs[1][k : k + 1, :]


def project_body(
    own_ref, got_ref, code_ref, spots_ref, gain_ref, shift_ref, down_ref, w_ref, up_ref, bias_ref,
    out_ref, mid_ref, x_ref,
):
    mine = code_ref[...] % 2
    choose = (
        lax.broadcasted_iota(jnp.int32, (own_ref.shape[0], spots_ref.shape[0]), 1) == code_ref[...] // 2
    )
    summed = jnp.where(
        mine > 0, own_ref[...].astype(F32), got_ref[...].astype(F32)
    ) + mm(choose.astype(F32).astype(BF), spots_ref[...])
    x = layer_norm(summed, *norm_of((gain_ref, shift_ref), 0))
    x_ref[...] = x
    low = x.astype(BF)
    mid = mm(low, down_ref[0]).astype(BF)
    mid_ref[...] = mid
    total = w_ref.shape[0]
    step = total // 3
    for start in range(0, total, step):
        part = slice(start, start + step)
        out_ref[:, part] = (
            mm_nt(low, w_ref[part, :]) + mm(mid, up_ref[0, :, part]) + qkv_bias(bias_ref, 0, start, step)
        ).astype(BF)


def project(own, got, code, spots, gains, shifts, down, w, up, bias, rows):
    width = own.shape[1]
    tile = split_of(rows, 256, 16)
    total = w.shape[0]
    row = lambda n: pl.BlockSpec((tile, n), lambda i: (i, 0))
    return pl.pallas_call(
        project_body,
        grid=(rows // tile,),
        in_specs=[row(width), row(width), row(1)]
        + [full(a.shape) for a in (spots, gains, shifts, down, w, up, bias)],
        out_specs=[row(total), row(down.shape[2]), row(width)],
        out_shape=[
            jax.ShapeDtypeStruct((rows, total), BF),
            jax.ShapeDtypeStruct((rows, down.shape[2]), BF),
            jax.ShapeDtypeStruct((rows, width), F32),
        ],
        compiler_params=params(),
        name="project",
    )(own, got, code, spots, gains, shifts, down, w, up, bias)


def attend_body(q_ref, k_ref, v_ref, seg_ref, seg_row_ref, ctx_ref, log_ref):
    rows = q_ref.shape[0]
    width = q_ref.shape[1] // 2
    scale = width**-0.5
    turned = turn_blocks(v_ref)

    def scored(start):
        own, near = reach_of(start, rows)
        return mm_nt(k_ref[near, :], pair_rows(q_ref[own, :].astype(F32) * scale, width))

    scores = scored(0)
    for start in range(0, rows, REACH):
        own, near = reach_of(start, rows)
        later = scored(start + REACH) if start + REACH < rows else None
        same = seg_ref[near, :] == seg_row_ref[:, own]
        scores = masked(scores, same)
        top = jnp.max(scores, 0, keepdims=True)
        weights = jnp.exp(scores - top)
        total = jnp.sum(weights, 0, keepdims=True)
        context = mm(turned[:, near], weights.astype(BF)) * (1.0 / total)
        ctx_ref[own, :] = pair_join(context, width).T.astype(BF)
        log_ref[0, :, 2 * start : 2 * start + 2 * REACH] = top + jnp.log(total)
        scores = later


def reach_of(start, rows):
    return slice(start, start + REACH), slice(max(0, start - REACH), min(rows, start + 2 * REACH))


def turn_blocks(ref):
    blocks = [ref[k : k + 128, :].astype(F32).T.astype(BF) for k in range(0, ref.shape[0], 128)]
    return jnp.concatenate(blocks, 1)


def attend(qkv, seg_wide, seg_row):
    rows, total = qkv.shape
    hidden = total // 3
    lanes = 2 * (hidden // HEADS)
    pairs = hidden // lanes
    column = lambda kind: pl.BlockSpec((rows, lanes), lambda p: (0, kind * pairs + p))
    return pl.pallas_call(
        attend_body,
        grid=(pairs,),
        in_specs=[column(0), column(1), column(2), full(seg_wide.shape), full(seg_row.shape)],
        out_specs=[
            pl.BlockSpec((rows, lanes), lambda p: (0, p)),
            pl.BlockSpec((1, 1, 2 * rows), lambda p: (p, 0, 0)),
        ],
        out_shape=[
            jax.ShapeDtypeStruct((rows, hidden), BF),
            jax.ShapeDtypeStruct((pairs, 1, 2 * rows), F32),
        ],
        compiler_params=params(),
        name="attend",
    )(qkv, qkv, qkv, seg_wide, seg_row)


def flat(ref):
    whole = ref[...]
    return whole.reshape(-1, whole.shape[-1])


def rows_of(ref, start, size):
    each = ref.shape[1]
    if size % each == 0 and start % each == 0 and each % 16 == 0:
        part = ref[start // each : (start + size) // each, :, :]
        return part.reshape(size, part.shape[-1])
    return flat(ref)[start : start + size, :]


def feed_step(ref):
    units = ref.shape[0] * ref.shape[1]
    step = ref.shape[1]
    while units % (2 * step) == 0 and 2 * step <= 768 and ref.shape[0] > 1:
        step *= 2
    return units, (step if ref.shape[0] > 1 else split_of(units, 768, 128))


def later_biases(bias_ref, layer):
    hidden = bias_ref.shape[1] // 8
    row = bias_ref[layer : layer + 1, :]
    return row[:, 2 * hidden : 3 * hidden], row[:, 3 * hidden : 7 * hidden], row[:, 7 * hidden :]


def after_body(
    ctx_ref, x_ref, wo_ref, up_ref, down_ref, bias_ref, gain_ref, shift_ref,
    out_ref, one_ref, two_ref, slope_ref,
):
    bo, b1, b2 = later_biases(bias_ref, 0)
    one = x_ref[...] + (mm_nt(ctx_ref[...], wo_ref[...]) + bo)
    one_ref[...] = one
    middle = layer_norm(one, *norm_of((gain_ref, shift_ref), 1))
    low = middle.astype(BF)
    total = middle + b2
    units, step = feed_step(up_ref)
    gate = mm_nt(low, rows_of(up_ref, 0, step))
    for start in range(0, units, step):
        part = slice(start, start + step)
        later = mm_nt(low, rows_of(up_ref, start + step, step)) if start + step < units else None
        act, slope = gelu_pair(gate + b1[:, part])
        slope_ref[:, part] = slope.astype(BF)
        total = total + mm(act.astype(BF), rows_of(down_ref, start, step))
        gate = later
    two_ref[...] = total
    out_ref[...] = layer_norm(total, *norm_of((gain_ref, shift_ref), 2))


def slab_spec(slab):
    array, place, rows = slab
    return pl.BlockSpec((array.shape[0], rows, array.shape[2]), lambda *_: (0, place, 0))


def after(ctx, x, wo, up, down, bias, gains, shifts):
    rows, width = x.shape
    tile = split_of(rows, 256, 16)
    units = 4 * width
    row = lambda n: pl.BlockSpec((tile, n), lambda i: (i, 0))
    return pl.pallas_call(
        after_body,
        grid=(rows // tile,),
        in_specs=[row(width), row(width), full(wo.shape), slab_spec(up), slab_spec(down)]
        + [full(a.shape) for a in (bias, gains, shifts)],
        out_specs=[row(width), row(width), row(width), row(units)],
        out_shape=[jax.ShapeDtypeStruct((rows, width), F32)] * 3
        + [jax.ShapeDtypeStruct((rows, units), BF)],
        compiler_params=params(),
        name="after",
    )(ctx, x, wo, up[0], down[0], bias, gains, shifts)


def exact_rows(choose, matrix):
    high = matrix.astype(BF)
    rest = matrix - high.astype(F32)
    middle = rest.astype(BF)
    low = (rest - middle.astype(F32)).astype(BF)
    return mm(choose, high) + mm(choose, middle) + mm(choose, low)


def unpack_rows(slab_ref, targets):
    shards = slab_ref.shape[0]

    @pl.loop(0, shards // 2)
    def _(k):
        first, second = slab_ref[2 * k].astype(F32), slab_ref[2 * k + 1].astype(F32)
        at = 0
        for target in targets:
            each = target.shape[0] // shards
            both = jnp.concatenate([first[at : at + each], second[at : at + each]], 0)
            target[pl.ds(pl.multiple_of(2 * each * k, 2 * each), 2 * each), :] = both.astype(BF)
            at += each


def last_forward_body(
    x_ref, place_ref, place_row_ref, seg_ref, down_ref, adapt_ref, bias_ref, weights_any, up_any, dn_any,
    gain_ref, shift_ref, hbias_ref,
    kv_ref, q_ref, mid_ref, log_ref, one_ref, slope_ref, two_ref, low_ref, act_ref, hslope_ref, feat_ref, *more,
    places, starts,
):
    copies = []
    if starts is None:
        up_ref, dn_ref, ctx_ref, w_ref, wo_ref, hb_ref, sems = more
        sources = zip(weights_any, (w_ref, wo_ref, hb_ref))
    else:
        w_out, wo_out, hb_out, up_ref, dn_ref, ctx_ref, w_ref, wo_ref, hb_ref, in_slab, hb_slab, sems = more
        sources = [
            (weights_any[0].at[:, pl.ds(start, slab.shape[1]), :], slab)
            for start, slab in zip(starts, (in_slab, hb_slab))
        ]
    for source, target in sources:
        copies.append((source, target))
    early = len(copies)
    for source, target, place in ((up_any, up_ref, places[0]), (dn_any, dn_ref, places[1])):
        each = target.shape[1]
        copies.append((source.at[:, pl.ds(place * each, each), :], target))
    copies = [pltpu.make_async_copy(*ends, sems.at[k]) for k, ends in enumerate(copies)]
    for copy in copies:
        copy.start()
    for copy in copies[:early]:
        copy.wait()
    copies = copies[early:]
    if starts is not None:
        unpack_rows(in_slab, (w_ref, wo_ref))
        unpack_rows(hb_slab, (hb_ref,))
        for k, ends in enumerate(((w_ref, w_out), (wo_ref, wo_out), (hb_ref, hb_out))):
            copies.append(pltpu.make_async_copy(*ends, sems.at[4 + k]))
            copies[-1].start()
    rows, hidden = x_ref.shape
    labels = place_ref.shape[0]
    lanes = 2 * (hidden // HEADS)
    width = lanes // 2
    low = x_ref[...].astype(BF)
    mid = mm(low, down_ref[1]).astype(BF)
    mid_ref[...] = mid
    step = split_of(hidden, 768, 128)
    for start in range(hidden, 3 * hidden, step):
        part = slice(start, start + step)
        kv_ref[:, start - hidden : start - hidden + step] = (
            mm_nt(low, w_ref[part, :]) + mm(mid, adapt_ref[1, :, part]) + qkv_bias(bias_ref, 1, start, step)
        ).astype(BF)
    choose = (
        lax.broadcasted_iota(jnp.int32, (labels, rows), 1) == place_ref[...][:, 0:1]
    ).astype(F32).astype(BF)
    own = exact_rows(choose, x_ref[...])
    own_low = own.astype(BF)
    own_mid = mm(choose, mid).astype(BF)
    q_ref[...] = (
        mm_nt(own_low, w_ref[:hidden, :])
        + mm(own_mid, adapt_ref[1, :, :hidden])
        + qkv_bias(bias_ref, 1, 0, hidden)
    ).astype(BF)
    seg = seg_ref[...]
    seg_own = jnp.sum(
        jnp.where(
            lax.broadcasted_iota(jnp.int32, (rows, labels), 0) == place_row_ref[...], seg, 0.0
        ),
        0,
        keepdims=True,
    )
    same = seg == seg_own

    def scored(p):
        part = slice(p * lanes, (p + 1) * lanes)
        return mm_nt(kv_ref[:, part], pair_rows(q_ref[:, part].astype(F32) * width**-0.5, width))

    later = scored(0)
    for p in range(hidden // lanes):
        part = slice(p * lanes, (p + 1) * lanes)
        scores = masked(later, same)
        later = scored(p + 1) if (p + 1) * lanes < hidden else None
        top = jnp.max(scores, 0, keepdims=True)
        weights = jnp.exp(scores - top)
        total = jnp.sum(weights, 0, keepdims=True)
        context = mm_tn(
            kv_ref[:, hidden + p * lanes : hidden + (p + 1) * lanes], weights.astype(BF)
        ) * (1.0 / total)
        ctx_ref[:, part] = pair_join(context, width).T.astype(BF)
        log_ref[p : p + 1, :] = top + jnp.log(total)
    bo, b1, b2 = later_biases(bias_ref, 1)
    norms = (gain_ref, shift_ref)
    one = own + (mm_nt(ctx_ref[...], wo_ref[...]) + bo)
    one_ref[...] = one
    middle = layer_norm(one, *norm_of(norms, 3))
    middle_low = middle.astype(BF)
    sum_two = middle + b2
    units, step = feed_step(up_ref)
    for copy in copies:
        copy.wait()
    gate = mm_nt(middle_low, rows_of(up_ref, 0, step))
    for start in range(0, units, step):
        part = slice(start, start + step)
        later = mm_nt(middle_low, rows_of(up_ref, start + step, step)) if start + step < units else None
        act, slope = gelu_pair(gate + b1[:, part])
        gate = later
        slope_ref[:, part] = slope.astype(BF)
        sum_two = sum_two + mm(act.astype(BF), rows_of(dn_ref, start, step))
    two_ref[...] = sum_two
    out_low = layer_norm(sum_two, *norm_of(norms, 4)).astype(BF)
    low_ref[...] = out_low
    act, slope = gelu_pair(mm(out_low, hb_ref[...]) + hbias_ref[...])
    act_ref[...] = act
    hslope_ref[...] = slope
    feat_ref[...] = layer_norm(act, *norm_of(norms, 5)).astype(BF)


def slab_scratch(slab):
    array, place, rows = slab
    return pltpu.VMEM((array.shape[0], rows, array.shape[2]), BF)


def last_forward(
    x, place_col, place_row, seg_wide, down, adapt, bias, weights, starts, up, dn, gains, shifts, hbias
):
    rows, hidden = x.shape
    labels = place_col.shape[0]
    units = 4 * hidden
    whole = pl.BlockSpec(memory_space=pltpu.VMEM)
    anywhere = pl.BlockSpec(memory_space=pl.ANY)
    shape = jax.ShapeDtypeStruct
    pairs = HEADS // 2
    matrices = [(3 * hidden, hidden), (hidden, hidden), (hidden, hidden)]
    slabs = []
    if starts is not None:
        shards = weights[0].shape[0]
        slabs = [
            pltpu.VMEM((shards, 4 * hidden // shards, hidden), BF),
            pltpu.VMEM((shards, weights[0].shape[1] - starts[1], hidden), BF),
        ]

    def body(*refs):
        head, rest = refs[:7], refs[7:]
        return last_forward_body(
            *head, rest[: len(weights)], *rest[len(weights) :], places=(up[1], dn[1]), starts=starts
        )

    return pl.pallas_call(
        body,
        in_specs=[whole] * 7 + [anywhere] * (len(weights) + 2) + [whole] * 3,
        out_specs=[whole] * 11 + ([anywhere] * 3 if slabs else []),
        out_shape=[
            shape((rows, 2 * hidden), BF),
            shape((labels, hidden), BF),
            shape((rows, down.shape[2]), BF),
            shape((pairs, 2 * labels), F32),
            shape((labels, hidden), F32),
            shape((labels, units), BF),
            shape((labels, hidden), F32),
            shape((labels, hidden), BF),
            shape((labels, hidden), F32),
            shape((labels, hidden), F32),
            shape((labels, hidden), BF),
        ]
        + ([shape(m, BF) for m in matrices] if slabs else []),
        scratch_shapes=[
            slab_scratch(up),
            slab_scratch(dn),
            pltpu.VMEM((labels, hidden), BF),
            *[pltpu.VMEM(m, BF) for m in matrices],
            *slabs,
            pltpu.SemaphoreType.DMA((7,)),
        ],
        compiler_params=params(),
        name="last_forward",
    )(x, place_col, place_row, seg_wide, down, adapt, bias, *weights, up[0], dn[0], gains, shifts, hbias)


def vocab_body(u_ref, e_ref, et_ref, bias_ref, num_ref, log_ref, scores, weights):
    count = e_ref.shape[0]
    step = split_of(count, 640, 16)
    u = u_ref[...]
    rows = u.shape[0]
    labels = num_ref.shape[2]
    top = jnp.full((1, rows), -jnp.inf, F32)
    for start in range(0, count, step):
        part = slice(start, start + step)
        bias = bias_ref[part, :]
        logits = mm_nt(e_ref[part, :], u) + jnp.concatenate([bias] * (rows // bias.shape[1]), 1)
        scores[part, :] = logits
        top = jnp.maximum(top, jnp.max(logits, 0, keepdims=True))
    total = jnp.zeros((1, rows), F32)
    for start in range(0, count, step):
        part = slice(start, start + step)
        grown = jnp.exp(scores[part, :] - top)
        total = total + jnp.sum(grown, 0, keepdims=True)
        weights[part, :] = grown.astype(BF)
    mean = mm(et_ref[...], weights[...]) * (1.0 / total)
    logs = top + jnp.log(total)
    for k in range(rows // labels):
        num_ref[k, :, :] = mean[:, k * labels : (k + 1) * labels]
        log_ref[k, :, :] = logs[:, k * labels : (k + 1) * labels]


def vocab(u, e, et, bias_wide, labels):
    rows, hidden = u.shape
    count = e.shape[0]
    tile = 2 * labels
    return pl.pallas_call(
        vocab_body,
        grid=(rows // tile,),
        in_specs=[
            pl.BlockSpec((tile, hidden), lambda i: (i, 0)),
            full(e.shape),
            full(et.shape),
            full(bias_wide.shape),
        ],
        out_specs=[
            pl.BlockSpec((2, hidden, labels), lambda i: (i, 0, 0)),
            pl.BlockSpec((2, 1, labels), lambda i: (i, 0, 0)),
        ],
        out_shape=[
            jax.ShapeDtypeStruct((rows // labels, hidden, labels), F32),
            jax.ShapeDtypeStruct((rows // labels, 1, labels), F32),
        ],
        scratch_shapes=[pltpu.VMEM((count, tile), F32), pltpu.VMEM((count, tile), BF)],
        compiler_params=params(),
        name="vocab",
    )(u, e, et, bias_wide)


def last_backward_body(
    own_any, got_any, mean_ref, all_log_ref, code_ref, fact_ref, kv_ref, q_ref, mid_ref, log_ref, one_ref, slope_ref, two_ref,
    low_ref, act_ref, hslope_ref, feat_ref, place_ref, place_row_ref, seg_ref, down_ref, w_ref, adapt_ref, wo_ref,
    up_any, dn_any, gain_ref, hb_ref,
    dx_ref, gh_ref, g_ref, out_fact_ref,
    up_ref, dn_ref, dkv_ref, dq_ref, aims, sems, *, places, edge,
):
    labels = place_ref.shape[0]
    tail = pl.ds(kv_ref.shape[0], labels)
    aimed = [
        pltpu.make_async_copy(source.at[tail, :], aims.at[k], sems.at[2 + k])
        for k, source in enumerate((own_any, got_any))
    ]
    for copy in aimed:
        copy.start()
    copies = []
    for k, (source, target, place) in enumerate(
        ((up_any, up_ref, places[0]), (dn_any, dn_ref, places[1]))
    ):
        rows = target.shape[1]
        copies.append(
            pltpu.make_async_copy(
                source.at[:, pl.ds(place * rows, rows), :], target, sems.at[k]
            )
        )
        copies[-1].start()
    rows = kv_ref.shape[0]
    labels, hidden = feat_ref.shape
    lanes = 2 * (hidden // HEADS)
    width = lanes // 2
    scale = width**-0.5
    for copy in aimed:
        copy.wait()
    mine = code_ref[kv_ref.shape[0] :, :] % 2
    targets = jnp.where(mine > 0, aims[0].astype(F32), aims[1].astype(F32))
    weight = fact_ref[0:1, 0:1]
    chosen = jnp.sum(feat_ref[...].astype(F32) * targets, keepdims=True)
    loss = weight * (jnp.sum(all_log_ref[...] - fact_ref[3:4, :labels], keepdims=True) - chosen)
    out_fact_ref[...] = jnp.where(
        lax.broadcasted_iota(jnp.int32, fact_ref.shape, 0) == 0, loss, fact_ref[...]
    )
    du = weight * (mean_ref[...].T - targets)
    dact = norm_back(act_ref[...], gain_ref[5:6, :], du)
    dz = (hslope_ref[...] * dact).astype(BF)
    dense = mm_tn(low_ref[...], dz)
    if len(gh_ref.shape) == 2:
        gh_ref[...] = dense
    else:
        each = hidden // gh_ref.shape[0]
        spare = jnp.zeros((gh_ref.shape[1] - each, hidden), F32)
        for k in range(gh_ref.shape[0]):
            gh_ref[k] = jnp.concatenate([dense[k * each : (k + 1) * each, :], spare], 0).astype(BF)
    dtwo = norm_back(two_ref[...], gain_ref[4:5, :], mm_nt(dz, hb_ref[...]))
    dtwo_low = dtwo.astype(BF)
    dmiddle = dtwo
    units, step = feed_step(up_ref)
    for copy in copies:
        copy.wait()
    dact = mm_nt(dtwo_low, rows_of(dn_ref, 0, step))
    for start in range(0, units, step):
        part = slice(start, start + step)
        later = mm_nt(dtwo_low, rows_of(dn_ref, start + step, step)) if start + step < units else None
        dgate = (slope_ref[:, part].astype(F32) * dact).astype(BF)
        dmiddle = dmiddle + mm(dgate, rows_of(up_ref, start, step))
        dact = later
    done = norm_back(one_ref[...], gain_ref[3:4, :], dmiddle)
    dctx = mm(done.astype(BF), wo_ref[...]).astype(BF)
    seg = seg_ref[...]
    choose_t = lax.broadcasted_iota(jnp.int32, (rows, labels), 0) == place_row_ref[...]
    same = seg == jnp.sum(jnp.where(choose_t, seg, 0.0), 0, keepdims=True)

    def products(p):
        part = slice(p * lanes, (p + 1) * lanes)
        later = slice(hidden + p * lanes, hidden + (p + 1) * lanes)
        queries = pair_rows(q_ref[:, part].astype(F32) * scale, width)
        outs = pair_rows(dctx[:, part].astype(F32), width)
        return queries, outs, mm_nt(kv_ref[:, part], queries), mm_nt(kv_ref[:, later], outs)

    ahead = products(0)
    for p in range(hidden // lanes):
        part = slice(p * lanes, (p + 1) * lanes)
        later = slice(hidden + p * lanes, hidden + (p + 1) * lanes)
        queries, outs, scores, dweights = ahead
        ahead = products(p + 1) if (p + 1) * lanes < hidden else None
        keys = kv_ref[:, part]
        weights = jnp.exp(masked(scores, same) - log_ref[p : p + 1, :])
        inner = jnp.sum(dweights * weights, 0, keepdims=True)
        dscores = (weights * (dweights - inner)).astype(BF)
        dkv_ref[:, part] = mm(dscores, queries).astype(BF)
        dkv_ref[:, later] = mm(weights.astype(BF), outs).astype(BF)
        dq_ref[:, part] = (pair_join(mm_tn(keys, dscores), width) * scale).T.astype(BF)
    dq = dq_ref[...]
    own_mid = mm(
        (lax.broadcasted_iota(jnp.int32, (labels, rows), 1) == place_ref[...][:, 0:1]).astype(F32).astype(BF),
        mid_ref[...],
    ).astype(BF)
    g_ref[...] = adapter_scale * jnp.where(
        lax.broadcasted_iota(jnp.int32, g_ref.shape, 1) < edge,
        mm_tn(dq, own_mid),
        mm_tn(dkv_ref[:, hidden:], mid_ref[...]),
    )
    dmid_own = mm_nt(dq, adapt_ref[1, :, :hidden]).astype(BF)
    own = done + mm(dq, w_ref[:hidden, :]) + mm_nt(dmid_own, down_ref[1])
    spread = choose_t.astype(F32).astype(BF)
    own_high = own.astype(BF)
    own_rest = (own - own_high.astype(F32)).astype(BF)
    dmid = mm_nt(dkv_ref[:, hidden:], adapt_ref[1, :, 2 * hidden :]).astype(BF)
    step = split_of(hidden, 256, 128)
    for start in range(0, hidden, step):
        part = slice(start, start + step)
        dx_ref[:, part] = (
            mm(dkv_ref[...], w_ref[hidden:, part])
            + mm_nt(dmid, down_ref[1, part, :])
            + mm(spread, own_high[:, part])
            + mm(spread, own_rest[:, part])
        )


def last_backward(
    mean, logs, own, got, code, facts, saved, place_col, place_row, seg_wide, down, w, adapt, wo, up, dn, gains, hb, edge, shards
):
    kv = saved[0]
    rows = kv.shape[0]
    labels, hidden = saved[-1].shape
    whole = pl.BlockSpec(memory_space=pltpu.VMEM)
    anywhere = pl.BlockSpec(memory_space=pl.ANY)
    shape = jax.ShapeDtypeStruct
    return pl.pallas_call(
        functools.partial(last_backward_body, places=(up[1], dn[1]), edge=edge),
        in_specs=[anywhere] * 2 + [whole] * 22 + [anywhere] * 2 + [whole] * 2,
        out_specs=[whole] * 4,
        out_shape=[
            shape((rows, hidden), F32),
            shape((hidden, hidden), F32)
            if shards is None
            else shape((shards, -(-hidden // shards // 16) * 16, hidden), BF),
            shape((hidden, down.shape[2]), F32),
            shape(facts.shape, F32),
        ],
        scratch_shapes=[
            slab_scratch(up),
            slab_scratch(dn),
            pltpu.VMEM(kv.shape, BF),
            pltpu.VMEM((labels, hidden), BF),
            pltpu.VMEM((2, labels, hidden), BF),
            pltpu.SemaphoreType.DMA((4,)),
        ],
        compiler_params=params(),
        name="last_backward",
    )(own, got, mean, logs, code, facts, *saved, place_col, place_row, seg_wide, down, w, adapt, wo, up[0], dn[0], gains, hb)


def after_back_body(dout_ref, one_ref, two_ref, slope_ref, wo_ref, up_ref, down_ref, gain_ref, dctx_ref):
    dtwo = norm_back(two_ref[...], gain_ref[2:3, :], dout_ref[...])
    low = dtwo.astype(BF)
    dmiddle = dtwo
    units, step = feed_step(up_ref)
    dact = mm_nt(low, rows_of(down_ref, 0, step))
    for start in range(0, units, step):
        part = slice(start, start + step)
        later = mm_nt(low, rows_of(down_ref, start + step, step)) if start + step < units else None
        dgate = (slope_ref[:, part].astype(F32) * dact).astype(BF)
        dmiddle = dmiddle + mm(dgate, rows_of(up_ref, start, step))
        dact = later
    done = norm_back(one_ref[...], gain_ref[1:2, :], dmiddle)
    dctx_ref[...] = mm(done.astype(BF), wo_ref[...]).astype(BF)


def after_back(dout, one, two, slope, wo, up, down, norms):
    rows, width = dout.shape
    tile = split_of(rows, 256, 16)
    row = lambda n: pl.BlockSpec((tile, n), lambda i: (i, 0))
    return pl.pallas_call(
        after_back_body,
        grid=(rows // tile,),
        in_specs=[row(width), row(width), row(width), row(slope.shape[1]), full(wo.shape)]
        + [slab_spec(up), slab_spec(down), full(norms.shape)],
        out_specs=row(width),
        out_shape=jax.ShapeDtypeStruct((rows, width), BF),
        compiler_params=params(),
        name="after_back",
    )(dout, one, two, slope, wo, up[0], down[0], norms)


def attend_back_body(
    q_ref, k_ref, v_ref, dctx_ref, log_ref, seg_ref, seg_row_ref, mid_ref, g_ref, dv_ref, *, edge
):
    rows = q_ref.shape[0]
    width = q_ref.shape[1] // 2
    scale = width**-0.5
    dv_ref[...] = jnp.zeros_like(dv_ref)
    gq = jnp.zeros((2 * width, mid_ref.shape[1]), F32)
    turned = turn_blocks(k_ref)

    def products(start):
        own, near = reach_of(start, rows)
        queries = pair_rows(q_ref[own, :].astype(F32) * scale, width)
        outs = pair_rows(dctx_ref[own, :].astype(F32), width)
        return outs, mm_nt(k_ref[near, :], queries), mm_nt(v_ref[near, :], outs)

    now = products(0)
    for start in range(0, rows, REACH):
        own, near = reach_of(start, rows)
        later = products(start + REACH) if start + REACH < rows else None
        outs, scores, dweights = now
        same = seg_ref[near, :] == seg_row_ref[:, own]
        logs = log_ref[0, :, 2 * start : 2 * start + 2 * REACH]
        weights = jnp.exp(masked(scores, same) - logs)
        inner = jnp.sum(dweights * weights, 0, keepdims=True)
        dscores = (weights * (dweights - inner)).astype(BF)
        dv_ref[near, :] += mm(weights.astype(BF), outs)
        dq = (pair_join(mm(turned[:, near], dscores), width) * scale).astype(BF)
        gq = gq + mm(dq, mid_ref[own, :])
        now = later
    gv = mm_tn(dv_ref[...].astype(BF), mid_ref[...])
    g_ref[...] = adapter_scale * jnp.where(
        lax.broadcasted_iota(jnp.int32, gq.shape, 1) < edge, gq, gv
    )


def attend_back(qkv, dctx, logs, seg_wide, seg_row, mid, edge):
    rows, total = qkv.shape
    hidden = total // 3
    lanes = 2 * (hidden // HEADS)
    pairs = hidden // lanes
    column = lambda kind: pl.BlockSpec((rows, lanes), lambda p: (0, kind * pairs + p))
    return pl.pallas_call(
        functools.partial(attend_back_body, edge=edge),
        grid=(pairs,),
        in_specs=[
            column(0),
            column(1),
            column(2),
            column(0),
            pl.BlockSpec((1, 1, 2 * rows), lambda p: (p, 0, 0)),
            full(seg_wide.shape),
            full(seg_row.shape),
            full(mid.shape),
        ],
        out_specs=pl.BlockSpec((lanes, mid.shape[1]), lambda p: (p, 0)),
        out_shape=jax.ShapeDtypeStruct((hidden, mid.shape[1]), F32),
        scratch_shapes=[pltpu.VMEM((rows, lanes), F32)],
        compiler_params=params(),
        name="attend_back",
    )(qkv, qkv, qkv, dctx, logs, seg_wide, seg_row, mid)


MESH = pl.DeviceIdType.MESH


def position():
    dp, fsdp = lax.axis_index("dp"), lax.axis_index("fsdp")
    return {"x": dp, "z": fsdp // 4, "y": (fsdp // 2) % 2, "c": fsdp % 2}


def device_of(place):
    return (place["x"], (place["z"] * 2 + place["y"]) * 2 + place["c"])


def number_of(place):
    return place["x"] * 16 + (place["z"] * 2 + place["y"]) * 2 + place["c"]


def rank_device(number):
    return (number // 16, number % 16)


def greet_all(shards):
    barrier = pltpu.get_barrier_semaphore()
    me = lax.axis_index("dp") * 16 + lax.axis_index("fsdp")

    @pl.loop(1, shards)
    def _(k):
        pl.semaphore_signal(
            barrier, inc=1, device_id=rank_device((me + k) % shards), device_id_type=MESH
        )


def await_all(shards):
    pl.semaphore_wait(pltpu.get_barrier_semaphore(), shards - 1)


def direct_copy(source, target, sems, me, k, shards):
    return pltpu.make_async_remote_copy(
        src_ref=source,
        dst_ref=target,
        send_sem=sems.at[0],
        recv_sem=sems.at[1],
        device_id=rank_device((me + k) % shards),
        device_id_type=MESH,
    )


def spread(piece_of, buffer, sems, me, shards):
    @pl.loop(1, shards)
    def _(k):
        direct_copy(piece_of((me + k) % shards), buffer.at[me], sems, me, k, shards).start()


def collect(buffer, sems, me, shards):
    whole = buffer.at[pl.ds(0, shards - 1)]
    copy = direct_copy(whole, whole, sems, me, 1, shards)
    copy.wait_recv()
    copy.wait_send()


def relative_places(order):
    places = [
        {"x": dx, "z": dz, "y": dy} for dx in (0, 1) for dz in range(-3, 4) for dy in (0, 1)
    ]
    size = lambda p: abs(p["x"]) + abs(p["z"]) + abs(p["y"])
    return sorted(places, key=lambda p: (abs(p[order[-1]]), size(p), [abs(p[a]) for a in order]))


class Gather:
    def __init__(self, chunk, full_buffer, start, rows, order, sends, receives, hands, hands_got):
        self.chunk, self.full, self.order = chunk, full_buffer, order
        self.part = pl.ds(start, rows)
        self.sends, self.receives, self.hands, self.hands_got = sends, receives, hands, hands_got
        self.here = position()
        self.items = relative_places(order)

    def origin(self, item):
        here = self.here
        return {"x": (here["x"] + item["x"]) % 2, "z": here["z"] - item["z"], "y": (here["y"] + item["y"]) % 2, "c": here["c"]}

    def key(self, place):
        return (place["x"] * 4 + place["z"]) * 2 + place["y"]

    def outward(self, item):
        deepest = max([k for k, axis in enumerate(self.order) if item[axis]], default=-1)
        ways = []
        if deepest >= 0 and self.order[deepest] == "z":
            ways.append(("z", 1 if item["z"] > 0 else -1))
        for axis in self.order[deepest + 1 :]:
            ways += [("z", 1), ("z", -1)] if axis == "z" else [(axis, 1)]
        return ways

    def copy(self, index, way, slot, item):
        here = self.here
        place = self.origin(item)
        number, key = number_of(place), self.key(place)
        mine = not any(item.values())
        source = self.chunk.at[self.part, :] if mine else self.full.at[number, self.part, :]
        if way is None:
            target = dict(here, c=1 - here["c"])
            sends, receives = self.hands.at[index], self.hands_got.at[key]
        else:
            axis, step = way
            target = dict(here)
            target[axis] = here["z"] + step if axis == "z" else 1 - here[axis]
            sends, receives = self.sends.at[index * 4 + slot], self.receives.at[key]
        return pltpu.make_async_remote_copy(
            src_ref=source,
            dst_ref=self.full.at[number, self.part, :],
            send_sem=sends,
            recv_sem=receives,
            device_id=device_of(target),
            device_id_type=MESH,
        )

    def valid(self, item):
        z = self.here["z"] - item["z"]
        return (z >= 0) & (z <= 3)

    def step(self, index):
        item = self.items[index]

        @pl.when(self.valid(item))
        def _():
            if any(item.values()):
                self.arrived(index, item)
            for slot, way in enumerate(self.outward(item)):
                self.when_way(way, lambda way=way, slot=slot: self.copy(index, way, slot, item).start())
            self.copy(index, None, 0, item).start()

    def when_way(self, way, act):
        axis, step = way
        if axis == "z":
            z = self.here["z"] + step
            pl.when((z >= 0) & (z <= 3))(act)
        else:
            act()

    def arrived(self, index, item):
        place = self.origin(item)
        spot = self.full.at[number_of(place), self.part, :]
        pltpu.make_async_remote_copy(
            src_ref=spot,
            dst_ref=spot,
            send_sem=self.sends.at[index * 4],
            recv_sem=self.receives.at[self.key(place)],
            device_id=device_of(dict(self.here, c=1 - self.here["c"])),
            device_id_type=MESH,
        ).wait_recv()

    def finish(self):
        for index, item in enumerate(self.items):

            @pl.when(self.valid(item))
            def _(index=index, item=item):
                for slot, way in enumerate(self.outward(item)):
                    self.when_way(way, lambda way=way, slot=slot: self.copy(index, way, slot, item).wait_send())
                self.copy(index, None, 0, item).wait_send()
                place = dict(self.origin(item), c=1 - self.here["c"])
                spot = self.full.at[number_of(place), self.part, :]
                pltpu.make_async_remote_copy(
                    src_ref=spot,
                    dst_ref=spot,
                    send_sem=self.hands.at[index],
                    recv_sem=self.hands_got.at[self.key(place)],
                    device_id=device_of(dict(self.here, c=1 - self.here["c"])),
                    device_id_type=MESH,
                ).wait_recv()


ITEMS = 28


PICK = 64
GROUP = 16


def start_body(
    streams, shards, ids, low_ref, groups_any, fact, chunk, got, own_rows, facts, full_chunk,
    table, stage, rows,
    row_sends, row_gets, fact_sems, own_sems, sends, receives, hands, hands_got,
):
    here = position()
    me = number_of(here)
    across = device_of(dict(here, x=1 - here["x"]))
    half, hidden = own_rows.shape
    batches = half // PICK
    fill = pltpu.make_async_copy(groups_any, table, own_sems.at[0])
    fill.start()
    greet_all(shards)
    own = [
        pltpu.make_async_copy(source, target, own_sems.at[1 + k])
        for k, (source, target) in enumerate(((fact, facts.at[me]), (chunk, full_chunk.at[me])))
    ]
    for copy in own:
        copy.start()
    await_all(shards)
    gathers = [
        Gather(
            chunk, full_chunk, start, size, order, sends.at[k], receives.at[k], hands.at[k], hands_got.at[k]
        )
        for k, (start, size, order) in enumerate(streams)
    ]
    for gather in gathers:
        gather.step(0)
    spread(lambda peer: fact, facts, fact_sems, me, shards)

    def send_rows(b):
        part = pl.ds(b * PICK, PICK)
        return pltpu.make_async_remote_copy(
            src_ref=rows.at[part, :],
            dst_ref=got.at[part, :],
            send_sem=row_sends.at[b],
            recv_sem=row_gets.at[b],
            device_id=across,
            device_id_type=MESH,
        )

    def pick(b):
        @pl.loop(0, PICK // 8)
        def _(t):
            found = [table[ids[b * PICK + t * 8 + k]] for k in range(8)]
            stage[pl.ds(pl.multiple_of(t * 8, 8), 8)] = jnp.stack(found)

        choose = (
            lax.broadcasted_iota(jnp.int32, (PICK, PICK * GROUP), 1)
            == low_ref[b * PICK : (b + 1) * PICK, :]
        )
        rows[b * PICK : (b + 1) * PICK, :] = mm(choose.astype(F32).astype(BF), flat(stage)).astype(BF)
        if b < batches:
            send_rows(b).start()

    fill.wait()
    picked = 0
    for index in range(1, ITEMS):
        while picked < min(2 * batches, 2 + 3 * index):
            pick(picked)
            picked += 1
        for gather in gathers:
            gather.step(index)
    outs = [pltpu.make_async_copy(rows.at[pl.ds(half, half), :], own_rows, own_sems.at[3])]
    for copy in outs:
        copy.start()
    for gather in gathers:
        gather.finish()
    collect(facts, fact_sems, me, shards)
    for b in range(batches):
        send_rows(b).wait()
    for copy in own + outs:
        copy.wait()


def vocab_rows(table, like):
    here = position()
    count = like.shape[0]
    return table.at[pl.ds(pl.multiple_of((here["y"] * 2 + here["c"]) * count, 16), count), :]


def gather_sems(streams):
    sems = pltpu.SemaphoreType.DMA
    count = len(streams)
    return [sems((count, 4 * ITEMS)), sems((count, 16)), sems((count, ITEMS)), sems((count, 16))]


def streams_of(rows, parts):
    streams, start = [], 0
    for k, (order, share) in enumerate(parts):
        size = rows - start if k == len(parts) - 1 else round(rows * share / 16) * 16
        streams.append((start, size, order))
        start += size
    return streams


def start_exchange(ids, table, fact, chunk, shards):
    anywhere = pl.BlockSpec(memory_space=pl.ANY)
    shape = jax.ShapeDtypeStruct
    sems = pltpu.SemaphoreType.DMA
    streams = streams_of(chunk.shape[0], (("xzy", 0.5), ("zxy", 0.28), ("xyz", 0.22)))
    half, hidden = ids.shape[0] // 2, table.shape[1]
    low = jnp.arange(ids.size, dtype=jnp.int32) % PICK * GROUP + ids % GROUP
    return pl.pallas_call(
        functools.partial(start_body, streams, shards),
        in_specs=[
            pl.BlockSpec(memory_space=pltpu.SMEM),
            pl.BlockSpec(memory_space=pltpu.VMEM),
        ]
        + [anywhere] * 3,
        out_specs=[anywhere] * 4,
        out_shape=[
            shape((half, hidden), table.dtype),
            shape((half, hidden), table.dtype),
            shape((shards, *fact.shape), fact.dtype),
            shape((shards, *chunk.shape), chunk.dtype),
        ],
        scratch_shapes=[
            pltpu.VMEM((table.shape[0] // GROUP, GROUP, hidden), BF),
            pltpu.VMEM((PICK, GROUP, hidden), BF),
            pltpu.VMEM((2 * half, hidden), BF),
            sems((half // PICK,)),
            sems((half // PICK,)),
            sems((2,)),
            sems((4,)),
            *gather_sems(streams),
        ],
        compiler_params=params(collective_id=1, has_side_effects=True),
        name="start_exchange",
    )(ids // GROUP, low[:, None], table.reshape(-1, GROUP, hidden), fact, chunk)


def first_layer_body(
    streams, shards,
    own_any, got_any, first_any, chunk, table_any, code_ref, spots_ref, gain_ref, shift_ref, down_ref,
    adapt_ref, bias_ref, seg_ref, seg_row_ref,
    qkv_out, x_out, one_out, two_out, slope_out, wo_out, full_chunk, et_out, mid_ref, log_ref,
    own, got, in_slab, w, wo, up, dn, x, qkv, ctx, two, out, slope,
    e_in, et_stage, load_sems, tile_sems, out_sems, e_sems, et_sems, sends, receives, hands, hands_got,
):
    here = position()
    me = number_of(here)
    rows, hidden = x.shape
    tile = split_of(rows, 256, 16)
    tiles = rows // tile
    lanes = 2 * (hidden // HEADS)
    pairs = hidden // lanes

    def slab(source, target, start):
        return source.at[:, pl.ds(start, target.shape[1]), :]

    loads = [
        pltpu.make_async_copy(source, target, load_sems.at[k])
        for k, (source, target) in enumerate(
            (
                (own_any.at[pl.ds(0, rows), :], own),
                (got_any.at[pl.ds(0, rows), :], got),
                (slab(first_any, in_slab, 2 * up.shape[1]), in_slab),
                (slab(first_any, up, 0), up),
                (slab(first_any, dn, up.shape[1]), dn),
                (chunk, full_chunk.at[me]),
            )
        )
    ]
    for copy in loads:
        copy.start()
    barrier = pltpu.get_barrier_semaphore()
    peers = [
        dict(here, c=1 - here["c"]),
        dict(here, x=1 - here["x"]),
        dict(here, y=1 - here["y"]),
        *[dict(here, z=flip(here["z"], k)) for k in (1, 2, 3)],
    ]
    for peer in peers:
        pl.semaphore_signal(barrier, inc=1, device_id=device_of(peer), device_id_type=MESH)
    pl.semaphore_wait(barrier, len(peers))
    gathers = [
        Gather(
            chunk, full_chunk, start, size, order, sends.at[k], receives.at[k], hands.at[k], hands_got.at[k]
        )
        for k, (start, size, order) in enumerate(streams)
    ]
    def advance(first, last):
        for index in range(first, last + 1):
            for gather in gathers:
                gather.step(index)

    def at(i, plan):
        for k, ends in plan.items():
            pl.when(i == k)(functools.partial(advance, *ends))

    advance(0, 0)

    groups = pairs + tiles
    size = e_in.shape[1]
    here_rows = (here["y"] * 2 + here["c"]) * (groups * size)
    unit = (
        (lax.broadcasted_iota(jnp.int32, (256, 256), 0) == lax.broadcasted_iota(jnp.int32, (256, 256), 1))
        .astype(F32)
        .astype(BF)
    )

    def group_in(g):
        source = table_any.at[pl.ds(pl.multiple_of(here_rows + g * size, 16), size), :]
        return pltpu.make_async_copy(source, e_in.at[g % 2], e_sems.at[g])

    def group_out(g):
        target = et_out.at[:, pl.ds(pl.multiple_of(g * size, 128), size)]
        return pltpu.make_async_copy(et_stage.at[g % 2], target, et_sems.at[g])

    def turn_group(g):
        group_in(g).wait()

        @pl.when(g >= 2)
        def _():
            group_out(g - 2).wait()

        for k in range(0, hidden, 256):
            et_stage[g % 2, k : k + 256, :] = mm_nt(unit, e_in[g % 2, :, k : k + 256]).astype(BF)
        group_out(g).start()

        @pl.when(g + 2 < groups)
        def _():
            group_in(g + 2).start()

    group_in(0).start()
    group_in(1).start()
    for copy in loads[:3]:
        copy.wait()
    unpack_rows(in_slab, (w, wo))

    @pl.loop(0, tiles)
    def _(i):
        part = pl.ds(pl.multiple_of(i * tile, tile), tile)
        project_body(
            own.at[part, :], got.at[part, :], code_ref.at[part, :], spots_ref, gain_ref, shift_ref, down_ref, w,
            adapt_ref, bias_ref, qkv.at[part, :], mid_ref.at[part, :], x.at[part, :],
        )

        at(i, {tiles - 3: (1, 3), tiles - 1: (4, 5)})

    early = [
        pltpu.make_async_copy(qkv, qkv_out, out_sems.at[0]),
        pltpu.make_async_copy(wo, wo_out, out_sems.at[1]),
    ]
    for copy in early:
        copy.start()

    @pl.loop(0, pairs)
    def _(p):
        column = lambda kind: pl.ds(pl.multiple_of((kind * pairs + p) * lanes, lanes), lanes)
        attend_body(
            qkv.at[:, column(0)], qkv.at[:, column(1)], qkv.at[:, column(2)], seg_ref, seg_row_ref,
            ctx.at[:, column(0)], log_ref.at[pl.ds(p, 1)],
        )

        turn_group(p)
        at(p - (pairs - 6), {1: (6, 7), 3: (8, 9), 5: (10, 13)})

    for copy in loads[3:5]:
        copy.wait()

    def tile_copies(i):
        part = pl.ds(pl.multiple_of(i * tile, tile), tile)
        turn = i % 2
        return [
            pltpu.make_async_copy(source, target.at[part, :], tile_sems.at[k, i])
            for k, (source, target) in enumerate(
                (
                    (out.at[turn], x_out),
                    (two.at[turn], two_out),
                    (slope.at[turn], slope_out),
                    (x.at[part, :], one_out),
                )
            )
        ]

    plan = {0: (14, 16), 1: (17, 19), 2: (20, 23), 3: (24, 27)}

    @pl.loop(0, tiles)
    def _(i):
        part = pl.ds(pl.multiple_of(i * tile, tile), tile)
        turn = i % 2

        @pl.when(i >= 2)
        def _():
            for copy in tile_copies(i - 2):
                copy.wait()

        after_body(
            ctx.at[part, :], x.at[part, :], wo, up, dn, bias_ref, gain_ref, shift_ref, out.at[turn],
            x.at[part, :], two.at[turn], slope.at[turn],
        )
        for copy in tile_copies(i):
            copy.start()
        turn_group(pairs + i)
        at(i - (tiles - 4), plan)

    for gather in gathers:
        gather.finish()
    for i in (tiles - 2, tiles - 1):
        for copy in tile_copies(i):
            copy.wait()
    for copy in early + loads[5:] + [group_out(g) for g in (groups - 2, groups - 1)]:
        copy.wait()


def first_layer(own, got, first, chunk, table, more, shards):
    whole = pl.BlockSpec(memory_space=pltpu.VMEM)
    anywhere = pl.BlockSpec(memory_space=pl.ANY)
    down, seg_row = more[4], more[-1]
    rows, hidden = seg_row.shape[1], own.shape[1]
    tile = split_of(rows, 256, 16)
    pairs = HEADS // 2
    units = 4 * hidden
    each = units // shards
    count, groups = table.shape[0] // 4, pairs + rows // tile
    shape = jax.ShapeDtypeStruct
    sems = pltpu.SemaphoreType.DMA
    streams = streams_of(chunk.shape[0], (("zxy", 0.4), ("zyx", 0.4), ("xyz", 0.2)))
    return pl.pallas_call(
        functools.partial(first_layer_body, streams, shards),
        in_specs=[anywhere] * 5 + [whole] * len(more),
        out_specs=[anywhere] * 8 + [whole] * 2,
        out_shape=[
            shape((rows, 3 * hidden), BF),
            shape((rows, hidden), F32),
            shape((rows, hidden), F32),
            shape((rows, hidden), F32),
            shape((rows, units), BF),
            shape((hidden, hidden), BF),
            shape((shards, *chunk.shape), BF),
            shape((hidden, count), BF),
            shape((rows, down.shape[2]), BF),
            shape((pairs, 1, 2 * rows), F32),
        ],
        scratch_shapes=[
            pltpu.VMEM((rows, hidden), BF),
            pltpu.VMEM((rows, hidden), BF),
            pltpu.VMEM((shards, 4 * hidden // shards, hidden), BF),
            pltpu.VMEM((3 * hidden, hidden), BF),
            pltpu.VMEM((hidden, hidden), BF),
            pltpu.VMEM((shards, each, hidden), BF),
            pltpu.VMEM((shards, each, hidden), BF),
            pltpu.VMEM((rows, hidden), F32),
            pltpu.VMEM((rows, 3 * hidden), BF),
            pltpu.VMEM((rows, hidden), BF),
            pltpu.VMEM((2, tile, hidden), F32),
            pltpu.VMEM((2, tile, hidden), F32),
            pltpu.VMEM((2, tile, units), BF),
            pltpu.VMEM((2, count // groups, hidden), BF),
            pltpu.VMEM((2, hidden, count // groups), BF),
            sems((6,)),
            sems((4, rows // tile)),
            sems((2,)),
            sems((groups,)),
            sems((groups,)),
            *gather_sems(streams),
        ],
        compiler_params=params(collective_id=3, has_side_effects=True),
        name="first_layer",
    )(own, got, first, chunk, table, *more)


def adam(weight, gradient, moment_one, moment_two, fade_one, fade_two):
    moment_one = beta_first * moment_one + (1.0 - beta_first) * gradient
    moment_two = beta_second * moment_two + (1.0 - beta_second) * gradient * gradient
    one_hat = moment_one / fade_one
    two_hat = moment_two / fade_two
    weight = weight - learn_rate * (one_hat / (jnp.sqrt(two_hat) + adam_eps) + decay_rate * weight)
    return (weight, moment_one, moment_two)


BACK_TILE = 256


def finish_body(
    shards, edge,
    dout_any, one_any, two_any, slope_any, wo_any, first_any, qkv_any, gain_ref, log_ref, seg_ref,
    seg_row_ref, mid_ref, parts, late_ref, facts,
    sums_ref, dense_ref, total_ref,
    dout, one, two, slope, wo, up, dn, qkv, dctx, dv, grad, core_got, chip_sum, dense_got, grad_got, note, notes,
    tile_sems, load_sems, core_sems, dense_sems, grad_sems, note_sems,
):
    rows, hidden = dout.shape
    tile = split_of(rows, BACK_TILE, 16)
    tiles = rows // tile
    me = number_of(position())

    def tile_loads(i):
        part = pl.ds(pl.multiple_of(i * tile, tile), tile)
        return [
            pltpu.make_async_copy(source.at[part, :], target.at[part, :], tile_sems.at[k, i])
            for k, (source, target) in enumerate(
                ((two_any, two), (dout_any, dout), (slope_any, slope), (one_any, one))
            )
        ]

    here = position()
    chips = shards // 2
    chip, core = me // 2, here["c"]
    to_core = pltpu.make_async_remote_copy(
        src_ref=parts.at[:, 1 - core],
        dst_ref=core_got,
        send_sem=core_sems.at[0],
        recv_sem=core_sems.at[1],
        device_id=device_of(dict(here, c=1 - core)),
        device_id_type=MESH,
    )

    def to_chip(k):
        peer = (chip + k) % chips
        return pltpu.make_async_remote_copy(
            src_ref=chip_sum.at[peer],
            dst_ref=dense_got.at[chip],
            send_sem=dense_sems.at[0],
            recv_sem=dense_sems.at[1],
            device_id=rank_device(2 * peer + core),
            device_id_type=MESH,
        )

    loads = [
        pltpu.make_async_copy(source, target, load_sems.at[k])
        for k, (source, target) in enumerate(
            (
                (first_any.at[:, pl.ds(up.shape[1], dn.shape[1]), :], dn),
                (first_any.at[:, pl.ds(0, up.shape[1]), :], up),
                (wo_any, wo),
                (qkv_any, qkv),
            )
        )
    ]
    for copy in tile_loads(0) + loads[:3]:
        copy.start()
    for i in range(1, tiles):
        for copy in tile_loads(i):
            copy.start()
    loads[3].start()
    greet_all(shards)
    for copy in loads[:3]:
        copy.wait()

    @pl.loop(0, tiles)
    def _(i):
        for copy in tile_loads(i):
            copy.wait()
        part = pl.ds(pl.multiple_of(i * tile, tile), tile)
        after_back_body(
            dout.at[part, :], one.at[part, :], two.at[part, :], slope.at[part, :], wo, up, dn, gain_ref,
            dctx.at[part, :],
        )

        @pl.when(i == 0)
        def _():
            await_all(shards)
            to_core.start()

        @pl.when(i == 1)
        def _():
            to_core.wait_recv()

            @pl.loop(0, chips)
            def _(k):
                chip_sum[k] = (parts[k, core].astype(F32) + core_got[k].astype(F32)).astype(BF)

            dense_got[chip] = chip_sum[chip]

            @pl.loop(1, chips)
            def _(k):
                to_chip(k).start()

    loads[3].wait()
    lanes = 2 * (hidden // HEADS)
    pairs = hidden // lanes

    @pl.loop(0, pairs)
    def _(p):
        column = lambda kind: pl.ds(pl.multiple_of((kind * pairs + p) * lanes, lanes), lanes)
        attend_back_body(
            qkv.at[:, column(0)], qkv.at[:, column(1)], qkv.at[:, column(2)], dctx.at[:, column(0)],
            log_ref.at[pl.ds(p, 1)], seg_ref, seg_row_ref, mid_ref, grad.at[column(0), :], dv, edge=edge,
        )

    grad[...] = grad[...] + late_ref[...]
    each = hidden // shards
    piece = lambda peer: grad.at[pl.ds(pl.multiple_of(peer * each, each), each), :]
    grad_got[me] = piece(me)[...]
    spread(piece, grad_got, grad_sems, me, shards)
    others = chip_sum.at[pl.ds(0, chips - 1)]
    every = pltpu.make_async_remote_copy(
        src_ref=others,
        dst_ref=dense_got.at[pl.ds(0, chips - 1)],
        send_sem=dense_sems.at[0],
        recv_sem=dense_sems.at[1],
        device_id=device_of(dict(here, c=1 - core)),
        device_id_type=MESH,
    )
    every.wait_recv()
    every.wait_send()
    to_core.wait_send()
    dense = jnp.zeros((each, hidden), F32)
    for k in range(chips):
        dense = dense + dense_got[k].astype(F32)[:each, :]
    dense_ref[...] = dense
    square = jnp.sum(dense * dense, keepdims=True)
    collect(grad_got, grad_sems, me, shards)
    total = grad_got[0]
    for k in range(1, shards):
        total = total + grad_got[k]
    total_ref[...] = total
    square = square + jnp.sum(total * total, keepdims=True)
    row = lax.broadcasted_iota(jnp.int32, note.shape, 0)
    note[...] = jnp.where(row == 0, facts[...], jnp.where(row == 1, square, 0.0))
    notes[me] = note[...]
    spread(lambda peer: note, notes, note_sems, me, shards)
    collect(notes, note_sems, me, shards)
    sums = notes[0]
    for k in range(1, shards):
        sums = sums + notes[k]
    sums_ref[...] = sums


def update_body(
    sums_ref, dense_ref, total_ref, facts, head_w, head_m, head_v, adapt_w, adapt_m, adapt_v,
    loss_out, norm_out, head_w_out, head_m_out, head_v_out, adapt_w_out, adapt_m_out, adapt_v_out,
):
    norm = jnp.sqrt(sums_ref[1:2, 0:1])
    loss_out[...] = sums_ref[0:1, 0:1]
    norm_out[...] = norm
    factor = jnp.minimum(1.0, clip_limit / (norm + 1e-06))
    fades = facts[1:2, 0:1], facts[2:3, 0:1]
    new = adam(head_w[...], dense_ref[...] * factor, head_m[...], head_v[...], *fades)
    head_w_out[...], head_m_out[...], head_v_out[...] = new
    grad = (total_ref[...] * factor).T
    layers, kinds, rank, unused = adapt_w.shape
    for layer in range(layers):
        for kind in range(kinds):
            at = (layer * kinds + kind) * rank
            new = adam(
                adapt_w[layer, kind], grad[at : at + rank], adapt_m[layer, kind], adapt_v[layer, kind], *fades
            )
            adapt_w_out[layer, kind], adapt_m_out[layer, kind], adapt_v_out[layer, kind] = new


def update(sums, dense, total, facts, heads, adapts):
    whole = pl.BlockSpec(memory_space=pltpu.VMEM)
    shape = jax.ShapeDtypeStruct
    return pl.pallas_call(
        update_body,
        in_specs=[whole] * 10,
        out_specs=[whole] * 8,
        out_shape=[shape((1, 1), F32)] * 2 + [shape(a.shape, F32) for a in (*heads, *adapts)],
        compiler_params=params(),
        name="update",
    )(sums, dense, total, facts, *heads, *adapts)


def finish(back, qkv, logs, seg_wide, seg_row, mid, parts, late, facts, edge, shards):
    dout, one, two, slope, wo, first, gains = back
    slab = pltpu.VMEM((shards, slope.shape[1] // shards, dout.shape[1]), BF)
    parts = parts.reshape(-1, 2, *parts.shape[1:])
    rows, hidden = dout.shape
    each = hidden // shards
    whole = pl.BlockSpec(memory_space=pltpu.VMEM)
    anywhere = pl.BlockSpec(memory_space=pl.ANY)
    shape = jax.ShapeDtypeStruct
    sems = pltpu.SemaphoreType.DMA
    tiles = rows // split_of(rows, BACK_TILE, 16)
    return pl.pallas_call(
        functools.partial(finish_body, shards, edge),
        in_specs=[anywhere] * 7 + [whole] * 8,
        out_specs=[whole] * 3,
        out_shape=[
            shape((8, 128), F32),
            shape((each, hidden), F32),
            shape((each, late.shape[1]), F32),
        ],
        scratch_shapes=[
            pltpu.VMEM((rows, hidden), F32),
            pltpu.VMEM((rows, hidden), F32),
            pltpu.VMEM((rows, hidden), F32),
            pltpu.VMEM(slope.shape, BF),
            pltpu.VMEM(wo.shape, BF),
            slab,
            slab,
            pltpu.VMEM(qkv.shape, BF),
            pltpu.VMEM((rows, hidden), BF),
            pltpu.VMEM((rows, 2 * (hidden // HEADS)), F32),
            pltpu.VMEM(late.shape, F32),
            pltpu.VMEM((shards // 2, *parts.shape[2:]), BF),
            pltpu.VMEM((shards // 2, *parts.shape[2:]), BF),
            pltpu.VMEM((shards // 2, *parts.shape[2:]), BF),
            pltpu.VMEM((shards, each, late.shape[1]), F32),
            pltpu.VMEM((8, 128), F32),
            pltpu.VMEM((shards, 8, 128), F32),
            sems((4, tiles)),
            sems((4,)),
            sems((2,)),
            sems((2,)),
            sems((2,)),
            sems((2,)),
        ],
        compiler_params=params(collective_id=2, has_side_effects=True),
        name="finish",
    )(dout, one, two, slope, wo, first, qkv, gains, logs, seg_wide, seg_row, mid, parts, late, facts)


LOG_ROWS = 16


def flip(z, k):
    return (z % 2 + k % 2) % 2 + 2 * ((z // 2 + k // 2) % 2)


def pack_log(log_row, rows):
    high = log_row.astype(BF).astype(F32)
    middle = (log_row - high).astype(BF).astype(F32)
    low = log_row - high - middle
    row = lax.broadcasted_iota(jnp.int32, (rows, log_row.shape[1]), 0)
    return jnp.where(
        row == 0, high, jnp.where(row == 1, middle, jnp.where(row == 2, low, 0.0))
    ).astype(BF)


def unpack(block, hidden):
    logs = block[hidden : hidden + LOG_ROWS, :].astype(F32)
    return block[:hidden, :].astype(F32), jnp.sum(logs, 0, keepdims=True)


def merged(one, two):
    top = jnp.maximum(one[1], two[1])
    first, second = jnp.exp(one[1] - top), jnp.exp(two[1] - top)
    total = first + second
    inverse = 1.0 / total
    return one[0] * (first * inverse) + two[0] * (second * inverse), top + jnp.log(total)


def store_packed(ref, pair, hidden):
    ref[:hidden, :] = pair[0].astype(BF)
    ref[hidden : hidden + LOG_ROWS, :] = pack_log(pair[1], LOG_ROWS)


def head_body(
    u_ref, bias_ref, table_any, et_any, mean_ref, log_ref,
    e_ref, et_ref, bias_wide, feats, packs, handed, sums,
    loads, far_send, far_get, hand_send, hand_get, part_send, part_get, sum_send, sum_get,
):
    here = position()
    x, y, c = here["x"], here["y"], here["c"]
    labels, hidden = u_ref.shape
    sibling = device_of(dict(here, c=1 - c))

    def chip_at(k):
        return (x + k % 2) % 2, (y + k // 2) % 2

    def device_at(k):
        there = chip_at(k)
        return device_of(dict(here, x=there[0], y=there[1]))

    def slot(k, core):
        there = chip_at(k)
        return (there[0] * 2 + there[1]) * 2 + core

    fills = [
        pltpu.make_async_copy(source, target, loads.at[k])
        for k, (source, target) in enumerate(
            ((vocab_rows(table_any, e_ref), e_ref), (et_any, et_ref))
        )
    ]
    for fill in fills:
        fill.start()
    barrier = pltpu.get_barrier_semaphore()
    for target in (sibling, *[device_at(k) for k in (1, 2, 3)]):
        pl.semaphore_signal(barrier, inc=1, device_id=target, device_id_type=MESH)
    feats[slot(0, c)] = u_ref[...]
    pl.semaphore_wait(barrier, 4)

    def move(place, device, send, get):
        return pltpu.make_async_remote_copy(
            src_ref=feats.at[place],
            dst_ref=feats.at[place],
            send_sem=send,
            recv_sem=get,
            device_id=device,
            device_id_type=MESH,
        )

    def far(k):
        return move(slot(0, c), device_at(k), far_send.at[k], far_get.at[k])

    def far_here(k):
        return move(slot(k, c), device_at(k), far_send.at[k], far_get.at[k])

    def hand(k, core):
        return move(slot(k, core), sibling, hand_send.at[k], hand_get.at[k])

    for k in (1, 2, 3):
        far(k).start()
    hand(0, c).start()

    @pl.loop(0, bias_ref.shape[0])
    def _(b):
        row = jnp.broadcast_to(bias_ref[pl.ds(b, 1), :], (128, 128))
        bias_wide[pl.ds(pl.multiple_of(b * 128, 128), 128), :] = row.T

    for k in (1, 2, 3):
        far_here(k).wait_recv()
        hand(k, c).start()
    for fill in fills:
        fill.wait()
    count = e_ref.shape[0]
    steps = 4

    def target_of(s):
        return (s + 1) % steps

    def hand_part(s):
        return pltpu.make_async_remote_copy(
            src_ref=packs.at[s, 1 - c],
            dst_ref=handed.at[s],
            send_sem=part_send.at[s],
            recv_sem=part_get.at[s],
            device_id=sibling,
            device_id_type=MESH,
        )

    def sum_part(s):
        return pltpu.make_async_remote_copy(
            src_ref=packs.at[s, c],
            dst_ref=sums.at[s],
            send_sem=sum_send.at[s],
            recv_sem=sum_get.at[s],
            device_id=device_at(target_of(s)),
            device_id_type=MESH,
        )

    def together(s):
        hand_part(s).wait_recv()
        return merged(unpack(packs[s, c], hidden), unpack(handed[s], hidden))

    def settle(s):
        store_packed(packs.at[s, c], together(s), hidden)
        sum_part(s).start()

    @pl.loop(0, steps)
    def _(s):
        k = target_of(s)
        hand(k, 1 - c).wait_recv()
        u = feats[pl.ds(slot(k, 0), 2)].reshape(2 * labels, hidden)
        top = total = mean = None

        def scored(start):
            part = slice(start, min(start + 1280, count))
            bias = bias_wide[part, :]
            return mm_nt(e_ref[part, :], u) + jnp.concatenate([bias, bias], 1)

        @pl.when(s > 0)
        def _():
            settle(s - 1)

        logits = scored(0)
        for start in range(0, count, 1280):
            part = slice(start, min(start + 1280, count))
            later = scored(start + 1280) if start + 1280 < count else None
            high = jnp.max(logits, 0, keepdims=True)
            new = high if top is None else jnp.maximum(top, high)
            grown = jnp.exp(logits - new)
            part_sums = jnp.sum(grown, 0, keepdims=True)
            product = mm(et_ref[:, part], grown.astype(BF))
            if top is None:
                total, mean = part_sums, product
            else:
                shrink = jnp.exp(top - new)
                total, mean = total * shrink + part_sums, mean * shrink + product
            top = new
            logits = later
        mean = mean * (1.0 / total)
        logs = top + jnp.log(total)
        for core in range(2):
            half = slice(core * labels, (core + 1) * labels)
            packs[s, core, :hidden, :] = mean[:, half].astype(BF)
            packs[s, core, hidden : hidden + LOG_ROWS, :] = pack_log(logs[:, half], LOG_ROWS)
        hand_part(s).start()

    total = together(steps - 1)
    for s in range(steps - 1):
        sum_part(s).wait_recv()
        total = merged(total, unpack(sums[s], hidden))
    mean_ref[...] = total[0]
    log_ref[...] = total[1]
    for k in (1, 2, 3):
        far(k).wait_send()
    for k in range(4):
        hand(k, c).wait_send()
    for s in range(steps):
        hand_part(s).wait_send()
    for s in range(steps - 1):
        sum_part(s).wait_send()


def head(u, bias, table, et):
    labels, hidden = u.shape
    whole = pl.BlockSpec(memory_space=pltpu.VMEM)
    anywhere = pl.BlockSpec(memory_space=pl.ANY)
    shape = jax.ShapeDtypeStruct
    sems = pltpu.SemaphoreType.DMA
    block = (hidden + LOG_ROWS, labels)
    count = et.shape[1]
    return pl.pallas_call(
        head_body,
        in_specs=[whole] * 2 + [anywhere] * 2,
        out_specs=[whole] * 2,
        out_shape=[shape((hidden, labels), F32), shape((1, labels), F32)],
        scratch_shapes=[
            pltpu.VMEM((count, hidden), BF),
            pltpu.VMEM((hidden, count), BF),
            pltpu.VMEM((count, 128), F32),
            pltpu.VMEM((8, labels, hidden), BF),
            pltpu.VMEM((4, 2, *block), BF),
            pltpu.VMEM((4, *block), BF),
            pltpu.VMEM((4, *block), BF),
            sems((2,)),
        ]
        + [sems((4,))] * 8,
        compiler_params=params(collective_id=4, has_side_effects=True),
        name="head",
    )(u, bias, table, et)


def seg_positions(segments):
    index = jnp.arange(segments.shape[-1], dtype=jnp.int32)
    fresh = jnp.concatenate([jnp.ones((1,), dtype=bool), segments[1:] != segments[:-1]], -1)
    starts = lax.cummax(jnp.where(fresh, index, jnp.zeros_like(index)), axis=0)
    return index - starts


def pad_rows(matrix, multiple):
    return jnp.pad(matrix, ((0, -matrix.shape[0] % multiple), (0, 0)))


def slab_of(gathered, start, rows):
    if rows % 16 == 0 and start % rows == 0:
        return (gathered, start // rows, rows)
    part = gathered[:, start : start + rows].reshape(1, -1, gathered.shape[2])
    return (part, 0, part.shape[1])


def per_device(
    input_token_index,
    sentence_numbers,
    label_positions,
    label_target_token,
    sequence_task_index,
    task_loss_weight,
    optimizer_step_count,
    embed,
    position_embedding,
    norm_gain_vector,
    norm_bias_vector,
    attention_in_weight,
    attention_out_weight,
    feedforward_up,
    feedforward_down,
    layer_bias_vector,
    head_dense_bias,
    vocabulary_bias,
    adapter_down_matrix,
    adapter_up_matrix,
    adapter_moment_first,
    adapter_moment_second,
    head_projection,
    head_moment_first,
    head_moment_second,
):
    shards = lax.axis_size("dp") * lax.axis_size("fsdp")
    dp_index = lax.axis_index("dp")
    fsdp_index = lax.axis_index("fsdp")
    layers, unused, rank, up_part = adapter_up_matrix.shape
    hidden = embed.shape[1]
    tokens = input_token_index.shape[1]
    labels = label_positions.shape[1]
    qkv_rows = attention_in_weight.shape[2]
    out_rows = attention_out_weight.shape[2]
    ff_rows = feedforward_up.shape[2]
    head_rows = head_projection.shape[0]

    grouped = (lax.axis_size("dp"), lax.axis_size("fsdp")) == (2, 16)
    feeds = [[feedforward_up[layer].T, feedforward_down[layer]] for layer in range(layers)]
    attends = [[attention_in_weight[layer].T, attention_out_weight[layer].T] for layer in range(layers)]
    first_chunk = jnp.concatenate(feeds[0] + attends[0], 0)
    last_chunk = pad_rows(
        jnp.concatenate(feeds[1] + attends[1] + [head_projection.astype(BF)], 0), 32
    )

    table_rows = embed.shape[0]
    wanted = jnp.concatenate([input_token_index[0], label_target_token[0]])
    dp_count = lax.axis_size("dp")
    group_ids = lax.all_gather(wanted, "dp", axis=0, tiled=False) - dp_index * table_rows
    inside = (group_ids >= 0) & (group_ids < table_rows)
    group_ids = jnp.clip(group_ids, 0, table_rows - 1)
    mine = lax.dynamic_index_in_dim(inside, dp_index, 0, keepdims=False)

    task_range = jnp.arange(TASKS, dtype=jnp.int32)
    slice_rows = vocabulary_bias.shape[0]
    ups = adapter_up_matrix.reshape(-1)
    if grouped:
        pair_ids = jnp.concatenate(
            [
                lax.dynamic_index_in_dim(group_ids, (dp_index + shift) % 2, 0, keepdims=False)
                for shift in (1, 0)
            ]
        )
        fact = jnp.concatenate([vocabulary_bias, ups, sequence_task_index.astype(F32)])
        fact_rows = -(-fact.size // 1024) * 8
        got, own_rows, facts, first_full = start_exchange(
            pair_ids,
            embed,
            jnp.pad(fact, (0, fact_rows * 128 - fact.size)).reshape(fact_rows, 128),
            first_chunk,
            shards,
        )
        facts = facts.reshape(shards, -1)
        all_bias = facts[:, :slice_rows].reshape(-1)
        every_up = facts[:, slice_rows : slice_rows + ups.size]
        every_task = facts[:, slice_rows + ups.size].astype(jnp.int32)
    else:
        looked = jnp.where(
            inside.reshape(-1)[:, None], embed[group_ids.reshape(-1)], jnp.zeros((), BF)
        )
        own_rows = got = lax.psum_scatter(looked, "dp", scatter_dimension=0, tiled=True)
        all_bias = lax.all_gather(vocabulary_bias, BOTH, axis=0, tiled=True)
        every_up = lax.all_gather(ups, BOTH, axis=0, tiled=False)
        every_task = lax.all_gather(sequence_task_index, BOTH, axis=0, tiled=True)
    counts = labels * jnp.sum((every_task[:, None] == task_range[None, :]).astype(F32), 0)
    task_hot = (sequence_task_index[:, None] == task_range[None, :]).astype(F32)
    row_weight = jnp.sum(task_hot[0] * (task_loss_weight / jnp.maximum(counts, 1.0)))
    ups_full = (
        every_up.astype(BF)
        .reshape(shards, layers, 2, rank, up_part)
        .transpose(1, 2, 3, 0, 4)
        .reshape(layers, 2, rank, hidden)
    )
    blank = jnp.zeros((rank, hidden), BF)
    spare = lambda rows: jnp.zeros((rows, 3 * hidden), BF)
    adapters = jnp.stack(
        [
            jnp.concatenate(
                [
                    spare(2 * rank * layer),
                    jnp.concatenate([2 * ups_full[layer, 0], blank, blank], 1),
                    jnp.concatenate([blank, blank, 2 * ups_full[layer, 1]], 1),
                    spare(128 - 2 * rank * (layer + 1)),
                ],
                0,
            )
            for layer in range(layers)
        ]
    )
    downs = jnp.stack(
        [
            jnp.pad(
                jnp.concatenate([adapter_down_matrix[layer, 0], adapter_down_matrix[layer, 1]], 1),
                ((0, 0), (2 * rank * layer, 128 - 2 * rank * (layer + 1))),
            )
            for layer in range(layers)
        ]
    )
    segments = sentence_numbers[0]
    code = (jnp.pad(2 * seg_positions(segments), (0, labels)) + mine.astype(jnp.int32))[:, None]
    seg_real = segments.astype(F32)
    seg_wide = jnp.broadcast_to(seg_real[:, None], (tokens, 128))
    seg_row = seg_real[None, :]
    place_row = label_positions
    place_col = jnp.broadcast_to(label_positions.reshape(labels, 1), (labels, 128))

    target_bias = all_bias[label_target_token[0]]

    gains, shifts = norm_gain_vector, norm_bias_vector
    last_inputs = (place_col, place_row, seg_wide, downs, adapters, layer_bias_vector)
    in_start = 2 * ff_rows
    slabs_of = lambda full_chunk: (slab_of(full_chunk, 0, ff_rows), slab_of(full_chunk, ff_rows, ff_rows))
    if grouped:
        more = (
            code, position_embedding, gains, shifts, downs, adapters, layer_bias_vector, seg_wide, seg_row,
        )
        qkv, x_last, one, two, slope, out_first, last_full, own_turned, mid, logs = first_layer(
            own_rows, got, first_full, last_chunk, embed, more, shards
        )
        slabs = [None, slabs_of(last_full)]
        *saved, in_last, out_last, head_full = last_forward(
            x_last, *last_inputs, (last_full,), (in_start, in_start + qkv_rows + out_rows), *slabs[1], gains,
            shifts, head_dense_bias[None, :],
        )
        count = own_turned.shape[1]
        own_bias = lax.dynamic_slice_in_dim(
            all_bias, dp_index * table_rows + fsdp_index % 4 * count, count, 0
        ).reshape(-1, 128)
        mean_t, own_logs = head(saved[-1], own_bias, embed, own_turned)
    else:
        first_full = lax.all_gather(first_chunk, BOTH, axis=0, tiled=False)
        last_full = lax.all_gather(last_chunk, BOTH, axis=0, tiled=False)
        slabs = [slabs_of(first_full), slabs_of(last_full)]
        taken = lambda full_chunk, start, size: full_chunk[:, start : start + size].reshape(-1, hidden)
        in_first = taken(first_full, 2 * ff_rows, qkv_rows)
        out_first = taken(first_full, 2 * ff_rows + qkv_rows, out_rows)
        in_last = taken(last_full, in_start, qkv_rows)
        out_last = taken(last_full, in_start + qkv_rows, out_rows)
        head_full = taken(last_full, in_start + qkv_rows + out_rows, head_rows)
        qkv, mid, hidden_rows = project(
            own_rows, got, code, position_embedding, gains, shifts, downs, in_first, adapters, layer_bias_vector, tokens
        )
        context, logs = attend(qkv, seg_wide, seg_row)
        x_last, one, two, slope = after(
            context, hidden_rows, out_first, *slabs[0], layer_bias_vector, gains, shifts
        )
        saved = last_forward(
            x_last, *last_inputs, (in_last, out_last, head_full), None, *slabs[1], gains, shifts,
            head_dense_bias[None, :],
        )
        features = saved[-1]
        own_slice = lax.dynamic_slice_in_dim(embed, fsdp_index * slice_rows, slice_rows, 0)
        own_vocab = jnp.concatenate(
            [own_slice]
            + [
                lax.ppermute(
                    own_slice, "dp", [(k, (k + shift) % dp_count) for k in range(dp_count)]
                )
                for shift in range(1, dp_count)
            ],
            0,
        )
        own_bias = jnp.concatenate(
            [
                lax.dynamic_slice_in_dim(
                    all_bias,
                    ((dp_index - shift) % dp_count) * table_rows + fsdp_index * slice_rows,
                    slice_rows,
                    0,
                )
                for shift in range(dp_count)
            ]
        )
        bias_wide = jnp.broadcast_to(own_bias[:, None], (own_bias.shape[0], 128))
        every = lax.all_gather(features, "fsdp", axis=0, tiled=True)
        means, local_logs = vocab(every, own_vocab, own_vocab.T, bias_wide, labels)
        local_logs = local_logs.reshape(-1, labels)
        all_logs = lax.all_gather(local_logs, "fsdp", axis=0, tiled=False)
        whole_logs = jax.nn.logsumexp(all_logs, axis=0)
        scaled = (means * jnp.exp(local_logs - whole_logs)[:, None, :]).astype(BF)
        mean_t = lax.psum_scatter(scaled, "fsdp", scatter_dimension=0, tiled=True)[0].astype(F32)
        own_logs = lax.dynamic_index_in_dim(whole_logs, fsdp_index, 0, keepdims=False)
        own_logs = own_logs[None, :]

    step_as_real = optimizer_step_count[0].astype(F32)
    fades = (1.0 - beta_first**step_as_real, 1.0 - beta_second**step_as_real)
    lanes = lambda value: jnp.pad(
        jnp.broadcast_to(value, (1, value.size if value.ndim else 128)), ((0, 0), (0, 128))
    )[:, :128]
    facts = jnp.concatenate(
        [lanes(value) for value in (row_weight, *fades, target_bias)] + [jnp.zeros((4, 128), F32)]
    )
    hidden_grad, dense_gradient, late, facts = last_backward(
        mean_t, own_logs, own_rows, got, code, facts, saved, place_col, place_row, seg_wide, downs, in_last, adapters,
        out_last, *slabs[1], gains, head_full, 3 * rank, shards if grouped else None,
    )
    back = (hidden_grad, one, two, slope, out_first)
    adapts = (adapter_up_matrix, adapter_moment_first, adapter_moment_second)
    heads = (head_projection, head_moment_first, head_moment_second)
    if grouped:
        sums, dense_portion, adapter_portion = finish(
            (*back, first_full, gains), qkv, logs, seg_wide, seg_row, mid, dense_gradient, late, facts, rank, shards
        )
        loss, norm, *new = update(sums, dense_portion, adapter_portion, facts, heads, adapts)
        return (loss[0, 0], norm[0, 0], *new[3:], *new[:3])
    dctx = after_back(*back, *slabs[0], gains)
    first = attend_back(qkv, dctx, logs, seg_wide, seg_row, mid, rank)
    adapter_gradient = (first + late)[:, : 2 * rank * layers].T.reshape(layers, 2, rank, hidden)
    dense_portion = lax.psum_scatter(dense_gradient, BOTH, scatter_dimension=0, tiled=True)
    adapter_portion = lax.psum_scatter(adapter_gradient, BOTH, scatter_dimension=3, tiled=True)
    squared_entries = jnp.sum(adapter_portion * adapter_portion) + jnp.sum(dense_portion * dense_portion)
    masked_task_loss, norm_square = lax.psum((facts[0, 0], squared_entries), BOTH)
    gradient_norm = jnp.sqrt(norm_square)
    factor = jnp.minimum(1.0, clip_limit / (gradient_norm + 1e-06))
    adapter_new = adam(adapts[0], adapter_portion * factor, *adapts[1:], *fades)
    dense_new = adam(heads[0], dense_portion * factor, *heads[1:], *fades)
    return (masked_task_loss, gradient_norm, *adapter_new, *dense_new)


def solution(mesh):
    rows = P(BOTH, None)
    in_specs = (
        rows,
        rows,
        rows,
        rows,
        P(BOTH),
        P(),
        P(),
        P("dp", None),
        P(),
        P(),
        P(),
        P(None, None, BOTH),
        P(None, None, BOTH),
        P(None, None, BOTH),
        P(None, BOTH, None),
        P(),
        P(),
        P(BOTH),
        P(),
        P(None, None, None, BOTH),
        P(None, None, None, BOTH),
        P(None, None, None, BOTH),
        rows,
        rows,
        rows,
    )
    adapter = P(None, None, None, BOTH)
    out_specs = (P(), P(), adapter, adapter, adapter, rows, rows, rows)
    return jax.shard_map(
        per_device, mesh=mesh, in_specs=in_specs, out_specs=out_specs, check_vma=False
    )
```
